32 devices in a mesh: dp: 16 (over z, y, core), mp: 2 (over x).
Axes of the slice: x: 2, y: 2, z: 4, core: 2. Of those that a mesh axis runs over, the one named last changes fastest.
Arguments:
- image_latents: bfloat16 [1024, 16, 16, 256], P('dp', None, None, 'mp'), may hold values from -6 to 6
- image_heights: int32 [1024], P('dp'), may hold values from 4 to 16, as said below
- code_index: int32 [1024, 16, 16], P('dp'), may hold values from 0 to 511
- kernel_three: bfloat16 [9, 256, 256], P(None, None, 'mp'), may hold values from -0.125 to 0.125
- bias_three: bfloat16 [256], P('mp'), may hold values from -3 to 3
- weight_mix: bfloat16 [256, 256], P('mp'), may hold values from -0.375 to 0.375
- bias_mix: bfloat16 [256], P('mp'), may hold values from -3 to 3
- weight_project: bfloat16 [256, 64], P('mp'), may hold values from -0.375 to 0.375
- bias_project: bfloat16 [64], replicated, may hold values from -3 to 3
- codebook: bfloat16 [512, 64], replicated, may hold values from -6 to 6
- weight_decode: bfloat16 [64, 256], P(None, 'mp'), may hold values from -0.75 to 0.75
- bias_decode: bfloat16 [256], P('mp'), may hold values from -3 to 3
- out_grad: bfloat16 [1024, 16, 16, 256], P('dp', None, None, 'mp'), may hold values from -6 to 6
Outputs:
- decoded: bfloat16 [1024, 16, 16, 256], P('dp', None, None, 'mp')
- latents_grad: bfloat16 [1024, 16, 16, 256], P('dp', None, None, 'mp')
- kernel_grad: float32 [9, 256, 256], P(None, None, 'mp')
- bias_three_grad: float32 [256], P('mp')
- mix_grad: float32 [256, 256], P('mp')
- bias_mix_grad: float32 [256], P('mp')
- project_grad: float32 [256, 64], P('mp')
- bias_project_grad: float32 [64], replicated
- codebook_grad: float32 [512, 64], replicated
- decode_grad: float32 [64, 256], P(None, 'mp')
- bias_decode_grad: float32 [256], P('mp')
The draws below stay inside these ranges and needn't reach their ends.
Inputs may be any that keep to these rules, and one draw needn't show every extreme that they name: `image_heights`: at least one image has all 16 rows live and one has 4.
All inputs are finite; a program needn't handle non-finite values.
Results may differ from the reference program's by a relative error of at most 0.0054.
Values may be sent and summed in bfloat16 or wider, within the bound.
No kernel may reach another device: no remote copies, remote signals or barrier semaphores. Data moves between devices by JAX's collectives and lax.ppermute only.
A program may use at most 320 MiB of HBM per device.

```python
import math
import jax
import jax.numpy as jnp
from jax import lax

CH = 256
EMBED = 64
CODES = 512
SIDE = 16
IMAGES = 1024


def draw_image_heights(key, part):
    key = jax.random.fold_in(key, 5)
    heights = jax.random.randint(key, (IMAGES,), SIDE // 4, SIDE + 1, dtype=jnp.int32)
    return heights.at[0].set(SIDE).at[IMAGES - 1].set(SIDE // 4)


def with_ends(entries, stream_key, low, largest):
    place = [jax.random.randint(jax.random.fold_in(stream_key, axis), (), 0, length) for axis, length in enumerate(entries.shape)]
    main_axis = entries.shape.index(max(entries.shape))
    neighbour = place[:main_axis] + [(place[main_axis] + 1) % entries.shape[main_axis]] + place[main_axis + 1:]
    return entries.at[tuple(place)].set(low).at[tuple(neighbour)].set(largest)


def block_scale(own_key, extent, shards, low, high):
    def one(position, blocks):
        steps = jax.random.uniform(jax.random.fold_in(jax.random.fold_in(own_key, 6), position), (blocks,), jnp.float32, low / len(shards), high / len(shards))
        return jnp.repeat(jnp.exp(steps), extent[position] // blocks).reshape((-1,) + (1,) * (len(extent) - position - 1))

    factor_of = one(*shards[0])
    for cut in shards[1:]:
        factor_of = factor_of * one(*cut)
    return factor_of


def scatter_about(rng, dims, width, bound, pieces=(), kind=jnp.bfloat16):
    values = jax.random.normal(rng, dims, jnp.float32) * width
    if len(pieces) > 0:
        values = block_scale(rng, dims, pieces, -0.22, 0.18) * values
    return jnp.clip(values, min=-bound, max=bound).astype(kind)


def setup_inputs(seed: int = 0) -> dict:
    key_of = jax.random.split(jax.random.key(seed), 14)
    return {
        "image_latents": scatter_about(key_of[0], (IMAGES, SIDE, SIDE, CH), 1.0, 6.0, ((0, 16), (3, 2))),
        "image_heights": draw_image_heights(jax.random.fold_in(key_of[13], 71), 0),
        "code_index": with_ends(jax.random.randint(key_of[2], (IMAGES, SIDE, SIDE), 0, CODES), jax.random.fold_in(key_of[2], 1), 0, CODES - 1).astype(jnp.int32),
        "kernel_three": scatter_about(key_of[3], (9, CH, CH), (9 * CH) ** -0.5, 0.125, ((2, 2),)),
        "bias_three": scatter_about(key_of[4], (CH,), 0.5, 3.0, ((0, 2),)),
        "weight_mix": scatter_about(key_of[5], (CH, CH), CH ** -0.5, 0.375, ((0, 2),)),
        "bias_mix": scatter_about(key_of[6], (CH,), 0.5, 3.0, ((0, 2),)),
        "weight_project": scatter_about(key_of[7], (CH, EMBED), CH ** -0.5, 0.375, ((0, 2),)),
        "bias_project": scatter_about(key_of[8], (EMBED,), 0.5, 3.0),
        "codebook": scatter_about(key_of[9], (CODES, EMBED), 1.0, 6.0),
        "weight_decode": scatter_about(key_of[10], (EMBED, CH), EMBED ** -0.5, 0.75, ((1, 2),)),
        "bias_decode": scatter_about(key_of[11], (CH,), 0.5, 3.0, ((0, 2),)),
        "out_grad": scatter_about(key_of[12], (IMAGES, SIDE, SIDE, CH), 1.0, 6.0, ((0, 16), (3, 2))),
    }


@jax.custom_vjp
def low(v):
    return lax.optimization_barrier(v.astype(jnp.bfloat16)).astype(jnp.float32)

@jax.custom_vjp
def low_back(v):
    return v

def low_keep(v):
    return (low(v), None)

def low_pass(kept, grad):
    return (grad,)

def back_keep(v):
    return (v, None)

def back_low(kept, grad):
    return (low(grad),)
low.defvjp(low_keep, low_pass)
low_back.defvjp(back_keep, back_low)
HIGH = lax.Precision.HIGHEST
commit_weight = 0.25

def conv_three(active, kernel):
    side = active.shape[1]
    padded = jnp.pad(active, ((0, 0), (1, 1), (1, 1), (0, 0)))
    total = jnp.zeros(active.shape[:3] + (kernel.shape[2],), jnp.float32)
    for offset in range(9):
        window = padded[:, offset // 3:offset // 3 + side, offset % 3:offset % 3 + side, :]
        total = total + jnp.einsum('bhwc,cd->bhwd', window, kernel[offset], precision=HIGH)
    return total

def reference(image_latents, image_heights, code_index, kernel_three, bias_three, weight_mix, bias_mix, weight_project, bias_project, codebook, weight_decode, bias_decode, out_grad):
    images = image_latents.shape[0]
    side = image_latents.shape[1]
    group = math.gcd(images, 16)
    blocks = images // group
    weights = tuple((w.astype(jnp.float32) for w in (kernel_three, bias_three, weight_mix, bias_mix, weight_project, bias_project, codebook, weight_decode, bias_decode)))

    def one_block(carry, block):
        latent_in, heights, code_rows, cotangent = block
        latent_in = latent_in.astype(jnp.float32)
        cotangent = cotangent.astype(jnp.float32)
        rows = jnp.arange(side, dtype=jnp.int32)
        row_mask = (rows[None, :] < heights[:, None]).astype(jnp.float32)[:, :, None, None]
        kernel, bias_one, mix, bias_two, project, bias_proj, book, decode_w, decode_b = weights

        def encode(latent_in, kernel, bias_one, mix, bias_two, project, bias_proj):
            active = low(jax.nn.gelu(latent_in) * row_mask)
            first = low_back(conv_three(active, kernel) + bias_one)
            second = low(jax.nn.gelu(first))
            mixed = low_back(jnp.einsum('bhwc,cd->bhwd', second, mix, precision=HIGH) + bias_two)
            block_out = latent_in + mixed
            latent = jnp.einsum('bhwc,ce->bhwe', low(block_out), project, precision=HIGH) + bias_proj
            return low_back(latent)
        latent, encode_back = jax.vjp(encode, latent_in, kernel, bias_one, mix, bias_two, project, bias_proj)
        chosen = jnp.take(book, code_rows, axis=0)

        def decode(quantized, decode_w, decode_b):
            return (jnp.einsum('bhwe,ec->bhwc', low(quantized), decode_w, precision=HIGH) + decode_b) * row_mask
        decoded, decode_back = jax.vjp(decode, chosen, decode_w, decode_b)
        quant_grad, decode_w_grad, decode_b_grad = decode_back(cotangent)

        def commit(latent):
            return commit_weight * jnp.sum(row_mask * (latent - chosen) ** 2)
        unit = jnp.ones((), jnp.float32)
        commit_grad = jax.vjp(commit, latent)[1](unit)[0]

        def book_loss(book):
            return jnp.sum(row_mask * (latent - jnp.take(book, code_rows, axis=0)) ** 2)
        book_grad = jax.vjp(book_loss, book)[1](unit)[0]
        grads = encode_back(quant_grad + commit_grad)
        new_terms = grads[1:] + (book_grad, decode_w_grad, decode_b_grad)
        carry = tuple((c + t for c, t in zip(carry, new_terms)))
        return (carry, (decoded.astype(jnp.bfloat16), grads[0].astype(jnp.bfloat16)))
    start = tuple((jnp.zeros(w.shape, jnp.float32) for w in weights))
    stacked = (image_latents.reshape((blocks, group) + image_latents.shape[1:]), image_heights.reshape(blocks, group), code_index.reshape((blocks, group) + code_index.shape[1:]), out_grad.reshape((blocks, group) + out_grad.shape[1:]))
    totals, outputs = lax.scan(one_block, start, stacked)
    decoded = outputs[0].reshape(image_latents.shape)
    latents_grad = outputs[1].reshape(image_latents.shape)
    kernel_grad, bias_three_grad, mix_grad, bias_mix_grad, project_grad, bias_project_grad, codebook_grad, decode_grad, bias_decode_grad = totals
    return (decoded, latents_grad, kernel_grad, bias_three_grad, mix_grad, bias_mix_grad, project_grad, bias_project_grad, codebook_grad, decode_grad, bias_decode_grad)
```

```python
import functools

import jax
import jax.numpy as jnp
from jax import lax
from jax.experimental import pallas as pl
from jax.experimental.pallas import tpu as pltpu
from jax.sharding import PartitionSpec as P

SIDE = 16
HALF = 128
LEAD = 16
BLOCK = 32
SENTINEL = 512.0
GELU_SCALE = 0.7978845608028654
GELU_CUBE = 0.044715
COMMIT = 0.25
F32 = jnp.float32
BF16 = jnp.bfloat16
ANY = pl.BlockSpec(memory_space=pl.ANY)
SMEM = pl.BlockSpec(memory_space=pltpu.SMEM)
VMEM = pl.BlockSpec(memory_space=pltpu.VMEM)
MIB = 1 << 20

NT = (((1,), (1,)), ((), ()))
TN = (((0,), (0,)), ((), ()))
NN = (((1,), (0,)), ((), ()))


def dot(a, b, dims=NN):
    return lax.dot_general(a, b, dims, preferred_element_type=F32)


def shape(dims, kind):
    return jax.ShapeDtypeStruct(dims, kind)


def params(mib):
    return pltpu.CompilerParams(vmem_limit_bytes=mib * MIB)


def cost(flops, moved, slow=0):
    return pl.CostEstimate(flops=flops, bytes_accessed=moved, transcendentals=slow)


class Plan:
    def __init__(self, images):
        self.images = images
        longest = images * SIDE // 2 + SIDE // 2
        chunk = 64
        self.chunks = [chunk] * (-(-longest // chunk))
        self.starts = [sum(self.chunks[:k]) for k in range(len(self.chunks))]
        self.total = sum(self.chunks)
        self.packed = LEAD + longest + self.total + LEAD
        self.in_step = [c // 4 + 2 for c in self.chunks]
        self.rows = []
        for c in self.chunks:
            most = 1 + c + 15 + c // 4 + 1
            self.rows.append(-(-most // BLOCK) * BLOCK)


def meta_size(plan):
    return plan.images + len(plan.chunks) + 1 + 4


def plan_rows(plan, heights, place, meta):
    images = plan.images
    base = images + len(plan.chunks) + 1

    def total_of(b, acc):
        return acc + heights[b]

    total = lax.fori_loop(0, images, total_of, jnp.int32(0))

    def split_of(b, state):
        acc, best, split, cut = state
        acc = acc + heights[b]
        worst = jnp.maximum(acc, total - acc)
        better = worst < best
        return (acc, jnp.where(better, worst, best), jnp.where(better, b + 1, split), jnp.where(better, acc, cut))

    _, _, split, cut = lax.fori_loop(0, images, split_of, (jnp.int32(0), jnp.int32(1 << 20), jnp.int32(0), jnp.int32(0)))
    mine = place[0]
    own_first = jnp.where(mine == 0, 0, split)
    own_last = jnp.where(mine == 0, split, images)
    own_row = jnp.where(mine == 0, 0, cut)
    send_row = jnp.where(mine == 0, cut, 0)
    for k in range(len(plan.chunks) + 1):
        meta[images + k] = own_first
    ends = [plan.starts[k] + plan.chunks[k] for k in range(len(plan.chunks))]

    def place_of(b, acc):
        meta[b] = acc - own_row
        acc = acc + heights[b]
        end = acc - own_row
        inside = jnp.logical_and(b >= own_first, b < own_last)
        step = jnp.int32(0)
        for k in range(len(plan.chunks) - 1):
            step = step + (end > ends[k]).astype(jnp.int32)

        @pl.when(inside)
        def _():
            meta[images + 1 + step] = b + 1

        return acc

    lax.fori_loop(0, images, place_of, jnp.int32(0))
    for k in range(len(plan.chunks)):
        meta[images + k + 1] = jnp.maximum(meta[images + k + 1], meta[images + k])
    meta[base] = own_row
    meta[base + 1] = send_row
    meta[base + 2] = own_first
    meta[base + 3] = own_last


def pack_rows(plan, meta, source, packed, piece, count):
    base = plan.images + len(plan.chunks) + 1

    def one(i, carry):
        b = piece * count + i
        row = meta[b] + meta[base] + LEAD
        packed[pl.ds(row, SIDE)] = source[b]
        return carry

    lax.fori_loop(0, count, one, 0)


def pack_latents(plan, heights, place, x_hbm, meta, own, *rest):
    n = len(plan.chunks)
    sends, (x_in, packed, sem_in, sem_out) = rest[:n], rest[n:]
    pieces = 8
    count = plan.images // pieces
    fetch = []
    for p in range(pieces):
        part = pl.ds(p * count, count)
        fetch.append(pltpu.make_async_copy(x_hbm.at[part], x_in.at[part], sem_in.at[p]))
        fetch[-1].start()
    plan_rows(plan, heights, place, meta)
    base = plan.images + n + 1
    for p in range(pieces):
        fetch[p].wait()
        pack_rows(plan, meta, x_in, packed, p, count)
    copies = []
    for k in range(n):
        part = pl.ds(LEAD + meta[base + 1] + plan.starts[k], plan.chunks[k])
        copies.append(pltpu.make_async_copy(packed.at[part], sends[k], sem_out.at[k]))
        copies[-1].start()
    copies.append(pltpu.make_async_copy(packed.at[pl.ds(meta[base], LEAD + plan.total)], own, sem_out.at[n]))
    copies[-1].start()
    for copy in copies:
        copy.wait()


def pack_code_grads(plan, meta, og_hbm, decode_w, own, *rest):
    n = len(plan.chunks)
    sends, (og_in, packed, sem_in) = rest[:n], rest[n:]
    pieces = 8
    count = plan.images // pieces
    fetch = []
    for p in range(pieces):
        part = pl.ds(p * count, count)
        fetch.append(pltpu.make_async_copy(og_hbm.at[part], og_in.at[part], sem_in.at[p]))
        fetch[-1].start()
    base = plan.images + n + 1
    w = decode_w[...]
    blank = jnp.zeros_like(w)
    upper = jnp.concatenate([w, blank], axis=0)
    lower = jnp.concatenate([blank, w], axis=0)
    for p in range(pieces):
        fetch[p].wait()
        pack_rows(plan, meta, og_in, packed, p, count)
    for k in range(n):
        half = plan.chunks[k] // 2
        for which in range(2):
            row = LEAD + meta[base + 1 - which] + plan.starts[k]
            a = packed[pl.ds(row, half)].reshape(half * SIDE, HALF)
            b = packed[pl.ds(row + half, half)].reshape(half * SIDE, HALF)
            both = dot(a, upper, NT) + dot(b, lower, NT)
            both = both.reshape(half, SIDE, HALF)
            if which == 0:
                sends[k][...] = both.astype(BF16)
            else:
                own[pl.ds(plan.starts[k] // 2, half)] = both


def decode_images(plan, steps, heights, codes, code_columns, og, codebook, decode_w, decode_b, decoded, chosen, grads, table, sums):
    step = pl.program_id(0)
    group = plan.images // steps

    @pl.when(step == 0)
    def _():
        book = codebook[...]
        full = dot(book, decode_w[...]) + decode_b[...].astype(F32)
        table[...] = jnp.concatenate([full.astype(BF16), book, book], axis=1)
        sums[...] = jnp.zeros_like(sums)

    spots = SIDE * SIDE
    codes_n = codebook.shape[0]
    lane = lax.broadcasted_iota(jnp.int32, (spots, codes_n), 1)
    sub = lax.broadcasted_iota(jnp.int32, (codes_n, spots), 0)
    spot = lax.broadcasted_iota(jnp.int32, (spots, HALF), 0)
    for i in range(group):
        live = heights[step * group + i] * SIDE
        hot = (code_columns[0, :, i : i + 1] == lane).astype(F32).astype(BF16)
        both = dot(hot, table[...])
        alive = spot < live
        decoded[i] = jnp.where(alive, both[:, :HALF], 0.0).astype(BF16).reshape(SIDE, SIDE, HALF)
        chosen[i] = both[:, HALF:].astype(BF16).reshape(SIDE, SIDE, HALF)
        hot_t = (codes[i : i + 1, :] == sub).astype(F32).astype(BF16)
        cot = og[i].reshape(spots, HALF).astype(F32)
        cot = jnp.where(alive, cot, 0.0).astype(BF16)
        sums[...] += dot(hot_t, cot)

    @pl.when(step == steps - 1)
    def _():
        total = sums[...]
        w = lax.dot_general(codebook[...].astype(F32), total, TN, precision=lax.Precision.HIGHEST, preferred_element_type=F32)
        bias = jnp.sum(total, axis=0, keepdims=True)
        embed = w.shape[0]
        grads[0:embed] = w
        grads[embed : embed + 8] = jnp.broadcast_to(bias, (8, HALF))


def gelu_parts(v):
    square = v * v
    t = jnp.tanh(v * (GELU_SCALE + (GELU_SCALE * GELU_CUBE) * square))
    half = 0.5 + 0.5 * t
    slope = half + (0.5 * v) * (1.0 - t * t) * (GELU_SCALE + (3.0 * GELU_SCALE * GELU_CUBE) * square)
    return v * half, slope


def main_step(plan, k, *refs):
    first_step = k == 0
    last_step = k == len(plan.chunks) - 1
    refs = list(refs)

    def take(count):
        got = refs[:count]
        del refs[:count]
        return got

    meta, heights, x_own, x_far, q_own, q_far, chosen_hbm, codes = take(8)
    kernel, kernel_t, mix, project, bias = take(5)
    if not first_step:
        x_past, q_past, carry_own, carry_far = take(4)
        past_accs = take(5)
    win_own, win_far, next_own, next_far = take(4)
    kernel_acc, mix_acc, project_acc, book_acc, bias_acc = take(5)
    xo, xf, qo, qf, qd, ch_in, xc_o, xc_f, qc, chc, act3, slope_x, grad3, block_g, diffs, lg_o, lg_f, out_o, out_f, sems = refs

    chunk, start = plan.chunks[k], plan.starts[k]
    images, in_step, rows = plan.images, plan.in_step[k], plan.rows[k]
    half = chunk // 2
    spots = BLOCK * SIDE
    low = meta[images + k]
    high = meta[images + k + 1]
    fetch_at = jnp.minimum(low, images - in_step)

    copies = [
        (x_own.at[pl.ds(start, LEAD + chunk)], xo.at[pl.ds(0, LEAD + chunk)]),
        (x_far, xf.at[pl.ds(LEAD, chunk)]),
        (q_own.at[pl.ds(start // 2, half)], qo.at[pl.ds(LEAD, half)]),
        (q_far, qf.at[pl.ds(LEAD, half)]),
        (chosen_hbm.at[pl.ds(fetch_at, in_step)], ch_in),
    ]
    if not first_step:
        past = plan.chunks[k - 1]
        copies += [
            (x_past.at[pl.ds(past - LEAD, LEAD)], xf.at[pl.ds(0, LEAD)]),
            (q_own.at[pl.ds(start // 2 - LEAD, LEAD)], qo.at[pl.ds(0, LEAD)]),
            (q_past.at[pl.ds(past // 2 - LEAD, LEAD)], qf.at[pl.ds(0, LEAD)]),
        ]
        accs = (mix_acc, project_acc, book_acc, bias_acc, kernel_acc)
        copies += list(zip(past_accs[1:] + past_accs[:1], accs))
    started = []
    for i, (source, target) in enumerate(copies):
        started.append(pltpu.make_async_copy(source, target, sems.at[i]))
        started[-1].start()
    started, later = started[:8], started[8:]

    if first_step:
        for acc in (kernel_acc, mix_acc, project_acc, book_acc, bias_acc):
            acc[...] = jnp.zeros(acc.shape, F32)
        out_o[0:LEAD] = jnp.zeros((LEAD, SIDE, HALF), BF16)
        out_f[0:LEAD] = jnp.zeros((LEAD, SIDE, HALF), BF16)
    else:
        out_o[0:LEAD] = carry_own[...]
        out_f[0:LEAD] = carry_far[...]

    blank = jnp.zeros((SIDE, SIDE, HALF), BF16)
    blank_f = jnp.zeros((SIDE, SIDE, HALF), F32)
    no_code = jnp.full((SIDE, SIDE, HALF), SENTINEL, BF16)
    for r in range(0, rows, SIDE):
        part = pl.ds(r, SIDE)
        xc_o[part] = blank
        xc_f[part] = blank
        qc[part] = blank_f
        chc[part] = no_code
    for copy in started:
        copy.wait()

    lane3 = lax.broadcasted_iota(jnp.int32, (1, SIDE, HALF), 2) < HALF // 2

    def spread(r0, count):
        both = (qo[pl.ds(r0, count)] + qf[pl.ds(r0, count)].astype(F32)).reshape(count * SIDE, HALF)
        turned = pltpu.roll(both, HALF // 2, 1).reshape(count, SIDE, HALF)
        both = both.reshape(count, SIDE, HALF)
        return jnp.where(lane3, both, turned), jnp.where(lane3, turned, both)

    upper, lower = spread(LEAD, half)
    qd[pl.ds(LEAD, half)] = upper
    qd[pl.ds(LEAD + half, half)] = lower
    if not first_step:
        _, lower = spread(0, LEAD)
        qd[0:LEAD] = lower

    def place(b, dst):
        src = meta[b] - start + LEAD
        xc_o[pl.ds(dst, SIDE)] = xo[pl.ds(src, SIDE)]
        xc_f[pl.ds(dst, SIDE)] = xf[pl.ds(src, SIDE)]
        qc[pl.ds(dst, SIDE)] = qd[pl.ds(src, SIDE)]
        chc[pl.ds(dst, SIDE)] = ch_in[b - fetch_at]
        end = dst + heights[b]
        xc_o[pl.ds(end, SIDE)] = blank
        xc_f[pl.ds(end, SIDE)] = blank
        qc[pl.ds(end, SIDE)] = blank_f
        chc[pl.ds(end, SIDE)] = no_code
        return end + 1

    used = lax.fori_loop(low, high, place, jnp.int32(1))
    blocks = jnp.where(high > low, (used + (BLOCK - 1)) // BLOCK, 0)

    column = lax.rem(lax.broadcasted_iota(jnp.int32, (spots, 1), 0), SIDE)
    not_first = column != 0
    not_last = column != SIDE - 1

    def shifted(value):
        back = jnp.where(not_first, pltpu.roll(value, 1, 0), 0.0)
        ahead = jnp.where(not_last, pltpu.roll(value, spots - 1, 0), 0.0)
        return back, ahead

    edge = jnp.zeros((SIDE, 3 * 2 * HALF), BF16)
    act3[0:SIDE] = edge
    grad3[0:SIDE] = edge
    beyond = pl.multiple_of((blocks * BLOCK + 1) * SIDE, SIDE)
    act3[pl.ds(beyond, SIDE)] = edge
    grad3[pl.ds(beyond, SIDE)] = edge
    diffs[pl.ds(blocks * BLOCK, SIDE)] = blank

    def read_x(r0):
        o = xc_o[pl.ds(r0, BLOCK)].reshape(spots, HALF)
        f = xc_f[pl.ds(r0, BLOCK)].reshape(spots, HALF)
        return jnp.concatenate([o, f], axis=1).astype(F32)

    def at(row, count=BLOCK):
        return pl.ds(pl.multiple_of(row * SIDE, SIDE), count * SIDE)

    def activate(j, carry):
        r0 = j * BLOCK
        value, slope = gelu_parts(read_x(r0))
        slope_x[at(r0), :] = slope
        back, ahead = shifted(value)
        act3[at(r0 + 1), 0 : 2 * HALF] = back.astype(BF16)
        act3[at(r0 + 1), 2 * HALF : 4 * HALF] = value.astype(BF16)
        act3[at(r0 + 1), 4 * HALF : 6 * HALF] = ahead.astype(BF16)
        return carry

    lax.fori_loop(0, blocks, activate, 0)
    for copy in later[:4]:
        copy.wait()

    bias_first = bias[0:1, :].astype(F32)
    bias_mix = bias[1:2, :].astype(F32)
    bias_code = bias[2:3, 0:HALF].astype(F32)
    lane = lax.broadcasted_iota(jnp.int32, (1, HALF), 1) < HALF // 2
    hb = BLOCK // 2
    hs = hb * SIDE

    def sum_rows(value):
        return jnp.sum(value.reshape(value.shape[0] // 8, 8, value.shape[1]), axis=0)

    def middle(j, carry):
        r0 = j * BLOCK
        pre = dot(act3[at(r0), :], kernel[0]) + dot(act3[at(r0 + 1), :], kernel[1]) + dot(act3[at(r0 + 2), :], kernel[2])
        value, slope = gelu_parts(pre + bias_first)
        second = value.astype(BF16)
        mixed = dot(second, mix[...]) + bias_mix
        block_low = (read_x(r0) + mixed).astype(BF16)
        latent = dot(block_low[:hs], project[0]) + dot(block_low[hs:], project[1]) + bias_code
        ch = jnp.where(lane3, chc[pl.ds(r0, hb)].astype(F32), chc[pl.ds(r0 + hb, hb)].astype(F32)).reshape(hs, HALF)
        q = jnp.where(lane3, qc[pl.ds(r0, hb)], qc[pl.ds(r0 + hb, hb)]).reshape(hs, HALF)
        live = ch < 0.5 * SENTINEL
        diff = jnp.where(live, latent - ch, 0.0)
        code_grad = jnp.where(live, q + (2.0 * COMMIT) * diff, 0.0)
        grad_low = code_grad.astype(BF16)
        block = jnp.concatenate([dot(grad_low, project[0], NT), dot(grad_low, project[1], NT)], axis=0)
        block_g[at(r0), :] = block
        mixed_grad = block.astype(BF16)
        first_grad = slope * dot(mixed_grad, mix[...], NT)
        back, ahead = shifted(first_grad)
        first_low = first_grad.astype(BF16)
        grad3[at(r0 + 1), 0 : 2 * HALF] = ahead.astype(BF16)
        grad3[at(r0 + 1), 2 * HALF : 4 * HALF] = first_low
        grad3[at(r0 + 1), 4 * HALF : 6 * HALF] = back.astype(BF16)
        mix_acc[...] += dot(second, mixed_grad, TN)
        project_acc[...] += jnp.where(lane, dot(block_low[:hs], grad_low, TN), dot(block_low[hs:], grad_low, TN))
        bias_acc[0:8] += sum_rows(first_low.astype(F32))
        bias_acc[8:16] += sum_rows(mixed_grad.astype(F32))
        bias_acc[16:24, 0:HALF] += sum_rows(grad_low.astype(F32))
        big = diff.astype(BF16).astype(F32)
        small = diff - big
        turned = pltpu.roll(small, HALF // 2, 1)
        diffs[pl.ds(r0, hb)] = jnp.where(lane, big, turned).astype(BF16).reshape(hb, SIDE, HALF)
        turned = pltpu.roll(big, HALF // 2, 1)
        diffs[pl.ds(r0 + hb, hb)] = jnp.where(lane, turned, small).astype(BF16).reshape(hb, SIDE, HALF)
        return carry

    lax.fori_loop(0, blocks, middle, 0)
    for copy in later[4:]:
        copy.wait()

    def finish(j, carry):
        r0 = j * BLOCK
        active = act3[at(r0 + 1), 2 * HALF : 4 * HALF]
        grad = None
        for i in range(3):
            window = grad3[at(r0 + 2 - i), :]
            term = dot(window, kernel_t[i])
            grad = term if grad is None else grad + term
            kernel_acc[:, i * 6 * HALF : (i + 1) * 6 * HALF] += dot(active, window, TN)
        out = (block_g[at(r0), :] + slope_x[at(r0), :] * grad).astype(BF16)
        lg_o[pl.ds(r0, BLOCK)] = out[:, :HALF].reshape(BLOCK, SIDE, HALF)
        lg_f[pl.ds(r0, BLOCK)] = out[:, HALF:].reshape(BLOCK, SIDE, HALF)
        return carry

    lax.fori_loop(0, blocks, finish, 0)

    codes_n = book_acc.shape[0]
    code_of = lax.broadcasted_iota(jnp.int32, (codes_n, SIDE * SIDE), 0)
    spot = lax.broadcasted_iota(jnp.int32, (1, SIDE * SIDE), 1)

    def collect(b, src):
        dst = meta[b] - start + LEAD
        out_o[pl.ds(dst, SIDE)] = lg_o[pl.ds(src, SIDE)]
        out_f[pl.ds(dst, SIDE)] = lg_f[pl.ds(src, SIDE)]
        row = jnp.where(spot < heights[b] * SIDE, codes[pl.ds(b, 1), :], -1)
        hot = (row == code_of).astype(F32).astype(BF16)
        book_acc[...] += dot(hot, diffs[pl.ds(src, SIDE)].reshape(SIDE * SIDE, HALF))
        return src + heights[b] + 1

    lax.fori_loop(low, high, collect, jnp.int32(1))
    size = win_own.shape[0]
    win_own[...] = out_o[0:size]
    win_far[...] = out_f[0:size]
    next_own[...] = out_o[chunk : chunk + LEAD]
    next_far[...] = out_f[chunk : chunk + LEAD]


def gather_grads(plan, place, kernel_acc, mix_acc, project_acc, book_acc, bias_acc, decode_acc, own, far):
    swap = place[0] == 1

    def lanes(value):
        return value[:, :HALF], value[:, HALF:]

    def order(first, second):
        return jnp.where(swap, second, first), jnp.where(swap, first, second)

    row = 0
    for tap in range(9):
        block = kernel_acc[:, tap * 2 * HALF : (tap + 1) * 2 * HALF]
        mine, theirs = lanes(block)
        a, b = order(mine[:HALF], mine[HALF:])
        own[row : row + HALF] = a
        own[row + HALF : row + 2 * HALF] = b
        a, b = order(theirs[:HALF], theirs[HALF:])
        far[row : row + HALF] = a
        far[row + HALF : row + 2 * HALF] = b
        row += 2 * HALF
    for target, part in ((own, mix_acc[:HALF]), (far, mix_acc[HALF:])):
        a, b = order(*lanes(part))
        target[row : row + HALF] = a
        target[row + HALF : row + 2 * HALF] = b
    row += 2 * HALF
    side = HALF // 2
    lane = lax.broadcasted_iota(jnp.int32, (1, HALF), 1) < side
    for target, part in ((own, project_acc[:HALF]), (far, project_acc[HALF:])):
        part = part + pltpu.roll(part, side, 1)
        target[row : row + side] = jnp.where(lane, part[:side], part[side:])
    row += side
    book = book_acc[...]
    book = -2.0 * (book + pltpu.roll(book, side, 1))
    n = book.shape[0] // 2
    book = jnp.where(lane, book[:n], book[n:])
    own[row : row + n] = book
    far[row : row + n] = book
    row += n
    sums = [jnp.sum(bias_acc[8 * i : 8 * i + 8], axis=0, keepdims=True) for i in range(3)]
    code = sums[2][:, :HALF]
    code = code + pltpu.roll(code, side, 1)
    which = lax.broadcasted_iota(jnp.int32, (8, HALF), 0)
    for target, first in ((own, 0), (far, HALF)):
        part = jnp.where(which == 0, sums[0][:, first : first + HALF], sums[1][:, first : first + HALF])
        target[row : row + 8] = jnp.where(which == 2, code, part)
    row += 8
    size = decode_acc.shape[0]
    own[row : row + size] = decode_acc[...]
    far[row : row + size] = jnp.zeros((size, HALF), F32)


def restore_rows(plan, meta, heights, *refs):
    n = len(plan.chunks)
    own, far, out = refs[:n], refs[n : 2 * n], refs[2 * n]
    stage_own, stage_far, sems = refs[2 * n + 1 :]
    copies = []
    for k in range(n):
        size = own[k].shape[0]
        for i, (source, target) in enumerate(((own[k], stage_own), (far[k], stage_far))):
            copies.append(pltpu.make_async_copy(source, target.at[pl.ds(plan.starts[k], size)], sems.at[i, k]))
            copies[-1].start()
    for copy in copies:
        copy.wait()
    base = plan.images + n + 1
    own_row, send_row = meta[base], meta[base + 1]
    first, last = meta[base + 2], meta[base + 3]
    row_of = lax.broadcasted_iota(jnp.int32, (SIDE, 1, 1), 0)

    def own_image(b, carry):
        rows = stage_own[pl.ds(meta[b] + LEAD, SIDE)]
        out[b] = jnp.where(row_of < heights[b], rows, jnp.zeros_like(rows))
        return carry

    def far_image(b, carry):
        rows = stage_far[pl.ds(meta[b] + own_row - send_row + LEAD, SIDE)]
        out[b] = jnp.where(row_of < heights[b], rows, jnp.zeros_like(rows))
        return carry

    lax.fori_loop(first, last, own_image, 0)
    lax.fori_loop(0, first, far_image, 0)
    lax.fori_loop(last, plan.images, far_image, 0)


def trade(value):
    return lax.ppermute(value, "mp", [(0, 1), (1, 0)])


def run_main(plan, k, meta, heights, streams, weights, state):
    chunk, rows, in_step = plan.chunks[k], plan.rows[k], plan.in_step[k]
    last = k == len(plan.chunks) - 1
    x_own, x_far, q_own, q_far, chosen, codes = streams
    codebook_rows = 512
    args = [meta, heights, x_own, x_far[k], q_own, q_far[k], chosen, codes, *weights]
    specs = [SMEM, SMEM, ANY, ANY, ANY, ANY, ANY, VMEM] + [VMEM] * len(weights)
    alias = {}
    if state is not None:
        args += [x_far[k - 1], q_far[k - 1], *state]
        specs += [ANY, ANY, VMEM, VMEM] + [ANY] * 5
        for i in range(5):
            alias[len(args) - 5 + i] = 4 + i
    size = chunk + LEAD if last else chunk
    tile = (SIDE, HALF)
    outs = [shape((size,) + tile, BF16)] * 2 + [shape((LEAD,) + tile, BF16)] * 2
    outs += [shape((2 * HALF, 18 * HALF), F32), shape((2 * HALF, 2 * HALF), F32), shape((2 * HALF, HALF), F32)]
    outs += [shape((codebook_rows, HALF), F32), shape((24, 2 * HALF), F32)]
    half = chunk // 2
    scratch = [
        pltpu.VMEM((LEAD + chunk + SIDE,) + tile, BF16),
        pltpu.VMEM((LEAD + chunk + SIDE,) + tile, BF16),
        pltpu.VMEM((LEAD + half,) + tile, F32),
        pltpu.VMEM((LEAD + half,) + tile, BF16),
        pltpu.VMEM((LEAD + chunk + SIDE,) + tile, F32),
        pltpu.VMEM((in_step, SIDE) + tile, BF16),
        pltpu.VMEM((rows + 2 * SIDE,) + tile, BF16),
        pltpu.VMEM((rows + 2 * SIDE,) + tile, BF16),
        pltpu.VMEM((rows + 2 * SIDE,) + tile, F32),
        pltpu.VMEM((rows + 2 * SIDE,) + tile, BF16),
        pltpu.VMEM(((rows + 2) * SIDE, 6 * HALF), BF16),
        pltpu.VMEM((rows * SIDE, 2 * HALF), F32),
        pltpu.VMEM(((rows + 2) * SIDE, 6 * HALF), BF16),
        pltpu.VMEM((rows * SIDE, 2 * HALF), F32),
        pltpu.VMEM((rows + 2 * SIDE,) + tile, BF16),
        pltpu.VMEM((rows + 2 * SIDE,) + tile, BF16),
        pltpu.VMEM((rows + 2 * SIDE,) + tile, BF16),
        pltpu.VMEM((LEAD + chunk + 2 * SIDE,) + tile, BF16),
        pltpu.VMEM((LEAD + chunk + 2 * SIDE,) + tile, BF16),
        pltpu.SemaphoreType.DMA((13,)),
    ]
    spots = chunk * SIDE
    return pl.pallas_call(
        functools.partial(main_step, plan, k),
        out_shape=outs,
        in_specs=specs,
        out_specs=[VMEM] * len(outs),
        scratch_shapes=scratch,
        input_output_aliases=alias,
        compiler_params=params(52),
        cost_estimate=cost(60 * 65536 * spots, 8 * MIB, 2 * 256 * spots),
        name=f"main_{k}",
    )(*args)


def local(
    image_latents,
    image_heights,
    code_index,
    kernel_three,
    bias_three,
    weight_mix,
    bias_mix,
    weight_project,
    bias_project,
    codebook,
    weight_decode,
    bias_decode,
    out_grad,
):
    images = image_latents.shape[0]
    plan = Plan(images)
    n = len(plan.chunks)
    tile = (SIDE, HALF)
    where = lax.axis_index("mp").astype(jnp.int32)
    place = where.reshape(1)
    swap = where == 1

    packed = pl.pallas_call(
        functools.partial(pack_latents, plan),
        out_shape=[shape((meta_size(plan),), jnp.int32), shape((LEAD + plan.total,) + tile, BF16)]
        + [shape((c,) + tile, BF16) for c in plan.chunks],
        in_specs=[SMEM, SMEM, ANY],
        out_specs=[SMEM, ANY] + [ANY] * n,
        scratch_shapes=[
            pltpu.VMEM((images, SIDE) + tile, BF16),
            pltpu.VMEM((plan.packed + SIDE,) + tile, BF16),
            pltpu.SemaphoreType.DMA((8,)),
            pltpu.SemaphoreType.DMA((n + 1,)),
        ],
        compiler_params=params(40),
        cost_estimate=cost(0, 12 * MIB),
        name="pack_latents",
    )(image_heights, place, image_latents)
    meta, x_own, x_send = packed[0], packed[1], packed[2:]

    packed = pl.pallas_call(
        functools.partial(pack_code_grads, plan),
        out_shape=[shape((plan.total // 2,) + tile, F32)] + [shape((c // 2,) + tile, BF16) for c in plan.chunks],
        in_specs=[SMEM, ANY, VMEM],
        out_specs=[VMEM] + [VMEM] * n,
        scratch_shapes=[
            pltpu.VMEM((images, SIDE) + tile, BF16),
            pltpu.VMEM((plan.packed + SIDE,) + tile, BF16),
            pltpu.SemaphoreType.DMA((8,)),
        ],
        compiler_params=params(40),
        cost_estimate=cost(2 * 2 * plan.total * SIDE * 256 * 128, 10 * MIB),
        name="pack_code_grads",
    )(meta, out_grad, weight_decode)
    q_own, q_send = packed[0], packed[1:]

    x_far = [trade(x_send[k]) for k in range(n)]
    q_far = [trade(q_send[k]) for k in range(n)]

    def own_first(value, axis):
        a, b = jnp.split(value, 2, axis)
        return jnp.where(swap, jnp.concatenate([b, a], axis), value)

    far_kernel, far_mix, far_project = trade(kernel_three), trade(weight_mix), trade(weight_project)
    far_bias = trade(jnp.stack([bias_three, bias_mix]))
    kernel = own_first(jnp.concatenate([kernel_three, far_kernel], axis=2), 1)
    kernel_fwd = kernel.reshape(3, 3 * 256, 256)
    kernel_bwd = kernel.transpose(0, 2, 1).reshape(3, 3 * 256, 256)
    mix = own_first(jnp.concatenate([weight_mix, far_mix], axis=0), 1)
    project = jnp.concatenate([weight_project, far_project], axis=0)
    blank = jnp.zeros_like(project)
    project = jnp.stack([jnp.concatenate([project, blank], 1), jnp.concatenate([blank, project], 1)])
    twice = jnp.concatenate([bias_project, bias_project])
    bias = jnp.concatenate(
        [jnp.concatenate([jnp.stack([bias_three, bias_mix]), far_bias], 1), jnp.concatenate([twice, twice])[None]], 0
    )
    weights = (kernel_fwd, kernel_bwd, mix, project, bias)

    groups = 8
    group = images // groups
    codes = code_index.reshape(images, SIDE * SIDE)
    code_columns = codes.T.reshape(SIDE * SIDE, groups, group).transpose(1, 0, 2)
    book_rows, embed = codebook.shape
    whole = lambda dims: pl.BlockSpec(dims, lambda g: (0,) * len(dims))
    four = pl.BlockSpec((group, SIDE) + tile, lambda g: (g, 0, 0, 0))
    decoded, chosen, decode_acc = pl.pallas_call(
        functools.partial(decode_images, plan, groups),
        grid=(groups,),
        out_shape=[shape((images, SIDE) + tile, BF16)] * 2 + [shape((embed + 8, HALF), F32)],
        in_specs=[
            SMEM,
            pl.BlockSpec((group, SIDE * SIDE), lambda g: (g, 0)),
            pl.BlockSpec((1, SIDE * SIDE, group), lambda g: (g, 0, 0)),
            four,
            whole((book_rows, embed)),
            whole((embed, HALF)),
            whole((1, HALF)),
        ],
        out_specs=[four, four, whole((embed + 8, HALF))],
        scratch_shapes=[pltpu.VMEM((book_rows, 2 * HALF), BF16), pltpu.VMEM((book_rows, HALF), F32)],
        compiler_params=params(32),
        cost_estimate=cost(2 * images * 256 * 512 * 512, 14 * MIB),
        name="decode_images",
    )(image_heights, codes, code_columns, out_grad, codebook, weight_decode, bias_decode.reshape(1, HALF))

    streams = (x_own, x_far, q_own, q_far, chosen, codes)
    state = None
    win_own, win_far = [], []
    for k in range(n):
        outs = run_main(plan, k, meta, image_heights, streams, weights, state)
        win_own.append(outs[0])
        win_far.append(trade(outs[1]))
        state = outs[2:]
    accs = state[2:]

    latents_grad = pl.pallas_call(
        functools.partial(restore_rows, plan),
        out_shape=shape((images, SIDE) + tile, BF16),
        in_specs=[SMEM, SMEM] + [ANY] * (2 * n),
        out_specs=VMEM,
        scratch_shapes=[
            pltpu.VMEM((plan.total + LEAD + SIDE,) + tile, BF16),
            pltpu.VMEM((plan.total + LEAD + SIDE,) + tile, BF16),
            pltpu.SemaphoreType.DMA((2, n)),
        ],
        compiler_params=params(40),
        cost_estimate=cost(0, 10 * MIB),
        name="restore_rows",
    )(meta, image_heights, *win_own, *win_far)

    rows = 9 * 256 + 256 + 64 + book_rows // 2 + 8 + embed + 8
    own, far = pl.pallas_call(
        functools.partial(gather_grads, plan),
        out_shape=[shape((rows, HALF), F32)] * 2,
        in_specs=[SMEM] + [VMEM] * 6,
        out_specs=[VMEM, VMEM],
        compiler_params=params(40),
        cost_estimate=cost(0, 8 * MIB),
        name="gather_grads",
    )(place, *accs, decode_acc)
    total = lax.psum(own + trade(far), "dp")

    row = 9 * 256
    kernel_grad = total[:row].reshape(9, 256, HALF)
    mix_grad = jnp.concatenate([total[row : row + HALF], total[row + HALF : row + 256]], axis=1)
    row += 256
    project_grad = jnp.concatenate([total[row : row + 64, :64], total[row : row + 64, 64:]], axis=0)
    row += 64
    codebook_grad = jnp.concatenate([total[row : row + book_rows // 2, :64], total[row : row + book_rows // 2, 64:]], axis=0)
    row += book_rows // 2
    bias_three_grad, bias_mix_grad, bias_project_grad = total[row], total[row + 1], total[row + 2, :64]
    row += 8
    decode_grad = total[row : row + embed]
    bias_decode_grad = total[row + embed]
    return (
        decoded,
        latents_grad,
        kernel_grad,
        bias_three_grad,
        mix_grad,
        bias_mix_grad,
        project_grad,
        bias_project_grad,
        codebook_grad,
        decode_grad,
        bias_decode_grad,
    )


def solution(mesh):
    tile = P("dp", None, None, "mp")
    placed = (
        tile,
        P("dp"),
        P("dp", None, None),
        P(None, None, "mp"),
        P("mp"),
        P("mp", None),
        P("mp"),
        P("mp", None),
        P(),
        P(),
        P(None, "mp"),
        P("mp"),
        tile,
    )
    outs = (
        tile,
        tile,
        P(None, None, "mp"),
        P("mp"),
        P("mp", None),
        P("mp"),
        P("mp", None),
        P(),
        P(),
        P(None, "mp"),
        P("mp"),
    )
    return jax.shard_map(local, mesh=mesh, in_specs=placed, out_specs=outs, check_vma=False)
```

```python
import functools

import jax
import jax.numpy as jnp
from jax import lax
from jax.experimental import pallas as pl
from jax.experimental.pallas import tpu as pltpu
from jax.sharding import PartitionSpec as P

SIDE = 16
HALF = 128
LEAD = 16
BLOCK = 32
SENTINEL = 512.0
GELU_SCALE = 0.7978845608028654
GELU_CUBE = 0.044715
COMMIT = 0.25
F32 = jnp.float32
BF16 = jnp.bfloat16
ANY = pl.BlockSpec(memory_space=pl.ANY)
SMEM = pl.BlockSpec(memory_space=pltpu.SMEM)
VMEM = pl.BlockSpec(memory_space=pltpu.VMEM)
MIB = 1 << 20

NT = (((1,), (1,)), ((), ()))
TN = (((0,), (0,)), ((), ()))
NN = (((1,), (0,)), ((), ()))


def dot(a, b, dims=NN):
    return lax.dot_general(a, b, dims, preferred_element_type=F32)


def shape(dims, kind):
    return jax.ShapeDtypeStruct(dims, kind)


def params(mib):
    return pltpu.CompilerParams(vmem_limit_bytes=mib * MIB)


def cost(flops, moved, slow=0):
    return pl.CostEstimate(flops=flops, bytes_accessed=moved, transcendentals=slow)


class Plan:
    def __init__(self, images):
        self.images = images
        longest = images * SIDE // 2 + SIDE // 2
        part = images // 4
        self.chunks = [5 * part, 9 * part, 10 * part]
        self.usual = len(self.chunks)
        rest = longest - sum(self.chunks)
        self.chunks.append(rest)
        self.starts = [sum(self.chunks[:k]) for k in range(len(self.chunks))]
        self.total = sum(self.chunks)
        self.packed = -(-(LEAD + longest + self.total + LEAD) // SIDE) * SIDE
        self.in_step = [c // 4 + 2 for c in self.chunks]
        self.rows = []
        for c in self.chunks:
            most = 1 + c + 15 + c // 4 + 1
            self.rows.append(-(-most // BLOCK) * BLOCK)
        self.covered = sum(self.chunks[: self.usual])


def meta_size(plan):
    return plan.images + len(plan.chunks) + 1 + 5


def plan_rows(plan, heights, place, meta):
    images = plan.images
    base = images + len(plan.chunks) + 1

    def total_of(b, acc):
        return acc + heights[b]

    total = lax.fori_loop(0, images, total_of, jnp.int32(0))

    def split_of(b, state):
        acc, best, split, cut = state
        acc = acc + heights[b]
        worst = jnp.maximum(acc, total - acc)
        better = worst < best
        return (acc, jnp.where(better, worst, best), jnp.where(better, b + 1, split), jnp.where(better, acc, cut))

    _, _, split, cut = lax.fori_loop(0, images, split_of, (jnp.int32(0), jnp.int32(1 << 20), jnp.int32(0), jnp.int32(0)))
    mine = place[0]
    own_first = jnp.where(mine == 0, 0, split)
    own_last = jnp.where(mine == 0, split, images)
    own_row = jnp.where(mine == 0, 0, cut)
    send_row = jnp.where(mine == 0, cut, 0)
    for k in range(len(plan.chunks) + 1):
        meta[images + k] = own_first
    ends = [plan.starts[k] + plan.chunks[k] for k in range(len(plan.chunks))]

    def place_of(b, acc):
        meta[b] = acc - own_row
        acc = acc + heights[b]
        end = acc - own_row
        inside = jnp.logical_and(b >= own_first, b < own_last)
        step = jnp.int32(0)
        for k in range(len(plan.chunks) - 1):
            step = step + (end > ends[k]).astype(jnp.int32)

        @pl.when(inside)
        def _():
            meta[images + 1 + step] = b + 1

        return acc

    lax.fori_loop(0, images, place_of, jnp.int32(0))
    for k in range(len(plan.chunks)):
        meta[images + k + 1] = jnp.maximum(meta[images + k + 1], meta[images + k])
    meta[base] = own_row
    meta[base + 1] = send_row
    meta[base + 2] = own_first
    meta[base + 3] = own_last
    meta[base + 4] = jnp.maximum(cut, total - cut)


def pack_rows(plan, meta, source, packed, piece, count):
    base = plan.images + len(plan.chunks) + 1

    def one(i, carry):
        b = piece * count + i
        row = meta[b] + meta[base] + LEAD
        packed[pl.ds(row, SIDE)] = source[b]
        return carry

    lax.fori_loop(0, count, one, 0)


def pack_latents(plan, heights, place, x_hbm, mix, project, bias_first, bias_mix, meta, own, small, *rest):
    n = len(plan.chunks)
    sends, (x_in, packed, sem_in, sem_out) = rest[:n], rest[n:]
    pieces = 8
    count = plan.images // pieces
    fetch = []
    for p in range(pieces):
        part = pl.ds(p * count, count)
        fetch.append(pltpu.make_async_copy(x_hbm.at[part], x_in.at[part], sem_in.at[p]))
        fetch[-1].start()
    plan_rows(plan, heights, place, meta)
    small[0:HALF] = mix[:, :HALF]
    small[HALF : 2 * HALF] = mix[:, HALF:]
    small[2 * HALF : 3 * HALF] = jnp.concatenate([project[...], jnp.zeros_like(project)], axis=1)
    which = lax.broadcasted_iota(jnp.int32, (SIDE, HALF), 0)
    first, second = bias_first[...].astype(F32), bias_mix[...].astype(F32)
    small[3 * HALF : 3 * HALF + SIDE] = jnp.where(which == 0, first, jnp.where(which == 1, second, 0.0)).astype(BF16)
    base = plan.images + n + 1
    for p in range(pieces):
        fetch[p].wait()
        pack_rows(plan, meta, x_in, packed, p, count)
    copies = []
    for k in range(n):
        part = pl.ds(LEAD + meta[base + 1] + plan.starts[k], plan.chunks[k])
        copies.append(pltpu.make_async_copy(packed.at[part], sends[k], sem_out.at[k]))
        copies[-1].start()
    copies.append(pltpu.make_async_copy(packed.at[pl.ds(meta[base], LEAD + plan.total)], own, sem_out.at[n]))
    copies[-1].start()
    for copy in copies:
        copy.wait()


def pack_code_grads(plan, meta, og_hbm, decode_w, own, *rest):
    n = len(plan.chunks)
    sends, (og_in, packed, sem_in) = rest[:n], rest[n:]
    pieces = 8
    count = plan.images // pieces
    fetch = []
    for p in range(pieces):
        part = pl.ds(p * count, count)
        fetch.append(pltpu.make_async_copy(og_hbm.at[part], og_in.at[part], sem_in.at[p]))
        fetch[-1].start()
    base = plan.images + n + 1

    def clear(i, carry):
        packed[pl.ds(i * SIDE, SIDE)] = jnp.zeros((SIDE, SIDE, HALF), BF16)
        return carry

    lax.fori_loop(0, packed.shape[0] // SIDE, clear, 0)
    w = decode_w[...]
    blank = jnp.zeros_like(w)
    upper = jnp.concatenate([w, blank], axis=0)
    lower = jnp.concatenate([blank, w], axis=0)
    for p in range(pieces):
        fetch[p].wait()
        pack_rows(plan, meta, og_in, packed, p, count)
    for k in range(n):
        half = plan.chunks[k] // 2
        for which in range(2):
            row = LEAD + meta[base + 1 - which] + plan.starts[k]
            a = packed[pl.ds(row, half)].reshape(half * SIDE, HALF)
            b = packed[pl.ds(row + half, half)].reshape(half * SIDE, HALF)
            both = dot(a, upper, NT) + dot(b, lower, NT)
            both = both.reshape(half, SIDE, HALF)
            if which == 0:
                sends[k][...] = both.astype(BF16)
            else:
                own[pl.ds(plan.starts[k] // 2, half)] = both


def prepare_weights(place, kernel, far_kernel, small, far_small, bias_code, forward, backward, mix, project, bias):
    first = pl.multiple_of(place[0] * HALF, HALF)
    order = (first, HALF - first)
    for tap in range(9):
        i, j = tap // 3, tap % 3
        for d, source in enumerate((kernel, far_kernel)):
            for c in range(2):
                tile = source[tap, pl.ds(order[c], HALF), :]
                row = j * 2 * HALF
                forward[i, row + c * HALF : row + (c + 1) * HALF, d * HALF : (d + 1) * HALF] = tile
                backward[i, row + d * HALF : row + (d + 1) * HALF, c * HALF : (c + 1) * HALF] = tile.T
    blank = jnp.zeros((HALF, HALF // 2), BF16)
    for d, source in enumerate((small, far_small)):
        rows = pl.ds(d * HALF, HALF)
        for c in range(2):
            mix[rows, c * HALF : (c + 1) * HALF] = source[pl.ds(order[c], HALF), :]
        part = source[2 * HALF : 3 * HALF, : HALF // 2]
        project[0, rows, :] = jnp.concatenate([part, blank], axis=1)
        project[1, rows, :] = jnp.concatenate([blank, part], axis=1)
        bias[0:8, d * HALF : (d + 1) * HALF] = source[3 * HALF : 3 * HALF + SIDE, :].astype(F32)[0:8]
    code = bias_code[...].astype(F32)
    code = jnp.concatenate([code, code], axis=1)
    bias[8:16, :] = jnp.broadcast_to(jnp.concatenate([code, code], axis=1), (8, 2 * HALF))


def decode_images(plan, steps, heights, codes, og, codebook, decode_w, decode_b, decoded, chosen, grads, table, sums):
    step = pl.program_id(0)
    group = plan.images // steps

    @pl.when(step == 0)
    def _():
        book = codebook[...]
        full = dot(book, decode_w[...]) + decode_b[...].astype(F32)
        table[...] = jnp.concatenate([full.astype(BF16), book, book], axis=1)
        sums[...] = jnp.zeros_like(sums)

    spots = SIDE * SIDE
    codes_n = codebook.shape[0]
    lane = lax.broadcasted_iota(jnp.int32, (spots, codes_n), 1)
    sub = lax.broadcasted_iota(jnp.int32, (codes_n, spots), 0)
    spot = lax.broadcasted_iota(jnp.int32, (spots, HALF), 0)
    code_columns = codes[...].astype(F32).T.astype(jnp.int32)
    for i in range(group):
        live = heights[step * group + i] * SIDE
        hot = (code_columns[:, i : i + 1] == lane).astype(F32).astype(BF16)
        both = dot(hot, table[...])
        alive = spot < live
        decoded[i] = jnp.where(alive, both[:, :HALF], 0.0).astype(BF16).reshape(SIDE, SIDE, HALF)
        chosen[i] = both[:, HALF:].astype(BF16).reshape(SIDE, SIDE, HALF)
        hot_t = (codes[i : i + 1, :] == sub).astype(F32).astype(BF16)
        cot = og[i].reshape(spots, HALF).astype(F32)
        cot = jnp.where(alive, cot, 0.0).astype(BF16)
        sums[...] += dot(hot_t, cot)

    @pl.when(step == steps - 1)
    def _():
        total = sums[...]
        w = lax.dot_general(codebook[...].astype(F32), total, TN, precision=lax.Precision.HIGHEST, preferred_element_type=F32)
        bias = jnp.sum(total, axis=0, keepdims=True)
        embed = w.shape[0]
        grads[0:embed] = w
        grads[embed : embed + 8] = jnp.broadcast_to(bias, (8, HALF))


def gelu_parts(v):
    square = v * v
    t = jnp.tanh(v * (GELU_SCALE + (GELU_SCALE * GELU_CUBE) * square))
    half = 0.5 + 0.5 * t
    slope = half + (0.5 * v) * (1.0 - t * t) * (GELU_SCALE + (3.0 * GELU_SCALE * GELU_CUBE) * square)
    return v * half, slope


def main_step(plan, k, *refs):
    first_step = k == 0
    fresh = k in (0, plan.usual)
    refs = list(refs)

    def take(count):
        got = refs[:count]
        del refs[:count]
        return got

    meta, heights, x_own, x_far, q_own, q_far, chosen_hbm, codes = take(8)
    kernel, kernel_t, mix, project, bias = take(5)
    if not first_step:
        x_past, q_past, carry_own, carry_far = take(4)
    if not fresh:
        past_accs = take(5)
    win_own, win_far, next_own, next_far = take(4)
    kernel_acc, mix_acc, project_acc, book_acc, bias_acc = take(5)
    xo, xf, qo, qf, qd, ch_in, xc_o, xc_f, qc, chc, act3, slope_x, grad3, block_g, diffs, lg_o, lg_f, out_o, out_f, sems = refs

    chunk, start = plan.chunks[k], plan.starts[k]
    images, in_step, rows = plan.images, plan.in_step[k], plan.rows[k]
    half = chunk // 2
    spots = BLOCK * SIDE
    low = meta[images + k]
    high = meta[images + k + 1]
    fetch_at = jnp.minimum(low, images - in_step)

    copies = [
        (x_own.at[pl.ds(start, LEAD + chunk)], xo.at[pl.ds(0, LEAD + chunk)]),
        (x_far, xf.at[pl.ds(LEAD, chunk)]),
        (q_own.at[pl.ds(start // 2, half)], qo.at[pl.ds(LEAD, half)]),
        (q_far, qf.at[pl.ds(LEAD, half)]),
        (chosen_hbm.at[pl.ds(fetch_at, in_step)], ch_in),
    ]
    if not first_step:
        past = plan.chunks[k - 1]
        copies += [
            (x_past.at[pl.ds(past - LEAD, LEAD)], xf.at[pl.ds(0, LEAD)]),
            (q_own.at[pl.ds(start // 2 - LEAD, LEAD)], qo.at[pl.ds(0, LEAD)]),
            (q_past.at[pl.ds(past // 2 - LEAD, LEAD)], qf.at[pl.ds(0, LEAD)]),
        ]
    accs = (mix_acc, project_acc, book_acc, bias_acc, kernel_acc)
    early = len(copies)
    if not fresh:
        copies += list(zip(past_accs[1:] + past_accs[:1], accs))
    started = []
    for i, (source, target) in enumerate(copies):
        started.append(pltpu.make_async_copy(source, target, sems.at[i]))
        started[-1].start()
    started, later = started[:early], started[early:]

    if fresh:
        for acc in accs:
            acc[...] = jnp.zeros(acc.shape, F32)
    if first_step:
        out_o[0:LEAD] = jnp.zeros((LEAD, SIDE, HALF), BF16)
        out_f[0:LEAD] = jnp.zeros((LEAD, SIDE, HALF), BF16)
    else:
        out_o[0:LEAD] = carry_own[...]
        out_f[0:LEAD] = carry_far[...]

    blank = jnp.zeros((SIDE, SIDE, HALF), BF16)
    blank_f = jnp.zeros((SIDE, SIDE, HALF), F32)
    no_code = jnp.full((SIDE, SIDE, HALF), SENTINEL, BF16)
    for r in range(0, rows, SIDE):
        part = pl.ds(r, SIDE)
        xc_o[part] = blank
        xc_f[part] = blank
        qc[part] = blank_f
        chc[part] = no_code
    for copy in started:
        copy.wait()

    lane3 = lax.broadcasted_iota(jnp.int32, (1, SIDE, HALF), 2) < HALF // 2

    def spread(r0, count):
        both = (qo[pl.ds(r0, count)] + qf[pl.ds(r0, count)].astype(F32)).reshape(count * SIDE, HALF)
        turned = pltpu.roll(both, HALF // 2, 1).reshape(count, SIDE, HALF)
        both = both.reshape(count, SIDE, HALF)
        return jnp.where(lane3, both, turned), jnp.where(lane3, turned, both)

    upper, lower = spread(LEAD, half)
    qd[pl.ds(LEAD, half)] = upper
    qd[pl.ds(LEAD + half, half)] = lower
    if not first_step:
        _, lower = spread(0, LEAD)
        qd[0:LEAD] = lower

    def place(b, dst):
        src = meta[b] - start + LEAD
        xc_o[pl.ds(dst, SIDE)] = xo[pl.ds(src, SIDE)]
        xc_f[pl.ds(dst, SIDE)] = xf[pl.ds(src, SIDE)]
        qc[pl.ds(dst, SIDE)] = qd[pl.ds(src, SIDE)]
        chc[pl.ds(dst, SIDE)] = ch_in[b - fetch_at]
        end = dst + heights[b]
        xc_o[pl.ds(end, SIDE)] = blank
        xc_f[pl.ds(end, SIDE)] = blank
        qc[pl.ds(end, SIDE)] = blank_f
        chc[pl.ds(end, SIDE)] = no_code
        return end + 1

    used = lax.fori_loop(low, high, place, jnp.int32(1))
    blocks = jnp.where(high > low, (used + (BLOCK - 1)) // BLOCK, 0)

    column = lax.rem(lax.broadcasted_iota(jnp.int32, (spots, 1), 0), SIDE)
    not_first = column != 0
    not_last = column != SIDE - 1

    def shifted(value):
        back = jnp.where(not_first, pltpu.roll(value, 1, 0), 0.0)
        ahead = jnp.where(not_last, pltpu.roll(value, spots - 1, 0), 0.0)
        return back, ahead

    edge = jnp.zeros((SIDE, 3 * 2 * HALF), BF16)
    act3[0:SIDE] = edge
    grad3[0:SIDE] = edge
    beyond = pl.multiple_of((blocks * BLOCK + 1) * SIDE, SIDE)
    act3[pl.ds(beyond, SIDE)] = edge
    grad3[pl.ds(beyond, SIDE)] = edge
    diffs[pl.ds(blocks * BLOCK, SIDE)] = blank

    def read_x(r0):
        o = xc_o[pl.ds(r0, BLOCK)].reshape(spots, HALF)
        f = xc_f[pl.ds(r0, BLOCK)].reshape(spots, HALF)
        return jnp.concatenate([o, f], axis=1).astype(F32)

    def at(row, count=BLOCK):
        return pl.ds(pl.multiple_of(row * SIDE, SIDE), count * SIDE)

    def activate(j, carry):
        r0 = j * BLOCK
        value, slope = gelu_parts(read_x(r0))
        slope_x[at(r0), :] = slope
        back, ahead = shifted(value)
        act3[at(r0 + 1), 0 : 2 * HALF] = back.astype(BF16)
        act3[at(r0 + 1), 2 * HALF : 4 * HALF] = value.astype(BF16)
        act3[at(r0 + 1), 4 * HALF : 6 * HALF] = ahead.astype(BF16)
        return carry

    lax.fori_loop(0, blocks, activate, 0)
    for copy in later[:4]:
        copy.wait()

    bias_first = bias[0:1, :]
    bias_mix = bias[1:2, :]
    bias_code = bias[8:9, 0:HALF]
    lane = lax.broadcasted_iota(jnp.int32, (1, HALF), 1) < HALF // 2
    hb = BLOCK // 2
    hs = hb * SIDE

    def sum_rows(value):
        return jnp.sum(value.reshape(value.shape[0] // 8, 8, value.shape[1]), axis=0)

    def middle(j, carry):
        r0 = j * BLOCK
        pre = dot(act3[at(r0), :], kernel[0]) + dot(act3[at(r0 + 1), :], kernel[1]) + dot(act3[at(r0 + 2), :], kernel[2])
        value, slope = gelu_parts(pre + bias_first)
        second = value.astype(BF16)
        mixed = dot(second, mix[...]) + bias_mix
        block_low = (read_x(r0) + mixed).astype(BF16)
        latent = dot(block_low[:hs], project[0]) + dot(block_low[hs:], project[1]) + bias_code
        ch = jnp.where(lane3, chc[pl.ds(r0, hb)].astype(F32), chc[pl.ds(r0 + hb, hb)].astype(F32)).reshape(hs, HALF)
        q = jnp.where(lane3, qc[pl.ds(r0, hb)], qc[pl.ds(r0 + hb, hb)]).reshape(hs, HALF)
        live = ch < 0.5 * SENTINEL
        diff = jnp.where(live, latent - ch, 0.0)
        code_grad = jnp.where(live, q + (2.0 * COMMIT) * diff, 0.0)
        grad_low = code_grad.astype(BF16)
        block = jnp.concatenate([dot(grad_low, project[0], NT), dot(grad_low, project[1], NT)], axis=0)
        block_g[at(r0), :] = block
        mixed_grad = block.astype(BF16)
        first_grad = slope * dot(mixed_grad, mix[...], NT)
        back, ahead = shifted(first_grad)
        first_low = first_grad.astype(BF16)
        grad3[at(r0 + 1), 0 : 2 * HALF] = ahead.astype(BF16)
        grad3[at(r0 + 1), 2 * HALF : 4 * HALF] = first_low
        grad3[at(r0 + 1), 4 * HALF : 6 * HALF] = back.astype(BF16)
        mix_acc[...] += dot(second, mixed_grad, TN)
        project_acc[...] += jnp.where(lane, dot(block_low[:hs], grad_low, TN), dot(block_low[hs:], grad_low, TN))
        bias_acc[0:8] += sum_rows(first_low.astype(F32))
        bias_acc[8:16] += sum_rows(mixed_grad.astype(F32))
        bias_acc[16:24, 0:HALF] += sum_rows(grad_low.astype(F32))
        big = diff.astype(BF16).astype(F32)
        small = diff - big
        turned = pltpu.roll(small, HALF // 2, 1)
        diffs[pl.ds(r0, hb)] = jnp.where(lane, big, turned).astype(BF16).reshape(hb, SIDE, HALF)
        turned = pltpu.roll(big, HALF // 2, 1)
        diffs[pl.ds(r0 + hb, hb)] = jnp.where(lane, turned, small).astype(BF16).reshape(hb, SIDE, HALF)
        return carry

    lax.fori_loop(0, blocks, middle, 0)
    for copy in later[4:]:
        copy.wait()

    def finish(j, carry):
        r0 = j * BLOCK
        active = act3[at(r0 + 1), 2 * HALF : 4 * HALF]
        grad = None
        for i in range(3):
            window = grad3[at(r0 + 2 - i), :]
            term = dot(window, kernel_t[i])
            grad = term if grad is None else grad + term
            kernel_acc[:, i * 6 * HALF : (i + 1) * 6 * HALF] += dot(active, window, TN)
        out = (block_g[at(r0), :] + slope_x[at(r0), :] * grad).astype(BF16)
        lg_o[pl.ds(r0, BLOCK)] = out[:, :HALF].reshape(BLOCK, SIDE, HALF)
        lg_f[pl.ds(r0, BLOCK)] = out[:, HALF:].reshape(BLOCK, SIDE, HALF)
        return carry

    lax.fori_loop(0, blocks, finish, 0)

    codes_n = book_acc.shape[0]
    code_of = lax.broadcasted_iota(jnp.int32, (codes_n, SIDE * SIDE), 0)
    spot = lax.broadcasted_iota(jnp.int32, (1, SIDE * SIDE), 1)

    def collect(b, src):
        dst = meta[b] - start + LEAD
        out_o[pl.ds(dst, SIDE)] = lg_o[pl.ds(src, SIDE)]
        out_f[pl.ds(dst, SIDE)] = lg_f[pl.ds(src, SIDE)]
        row = jnp.where(spot < heights[b] * SIDE, codes[pl.ds(b, 1), :], -1)
        hot = (row == code_of).astype(F32).astype(BF16)
        book_acc[...] += dot(hot, diffs[pl.ds(src, SIDE)].reshape(SIDE * SIDE, HALF))
        return src + heights[b] + 1

    lax.fori_loop(low, high, collect, jnp.int32(1))
    size = win_own.shape[0]
    win_own[...] = out_o[0:size]
    win_far[...] = out_f[0:size]
    next_own[...] = out_o[chunk : chunk + LEAD]
    next_far[...] = out_f[chunk : chunk + LEAD]


class Layout:
    def __init__(self, devices, book_rows, embed):
        self.mix = 9 * 2 * HALF
        self.project = self.mix + 2 * HALF
        self.book = self.project + HALF // 2
        self.bias = self.book + book_rows // 2
        self.decode = self.bias + 8
        used = self.decode + embed + 8
        self.devices = devices
        self.piece = -(-used // (devices * SIDE)) * SIDE
        self.rows = self.piece * devices
        self.half = self.rows // 2
        self.used = used


def lay_out(layout, swap, kernel_acc, mix_acc, project_acc, book_acc, bias_acc, decode_acc, own, far):
    def lanes(value):
        return value[:, :HALF], value[:, HALF:]

    def order(first, second):
        return jnp.where(swap, second, first), jnp.where(swap, first, second)

    row = 0
    for tap in range(9):
        block = kernel_acc[:, tap * 2 * HALF : (tap + 1) * 2 * HALF]
        mine, theirs = lanes(block)
        a, b = order(mine[:HALF], mine[HALF:])
        own[row : row + HALF] = a
        own[row + HALF : row + 2 * HALF] = b
        a, b = order(theirs[:HALF], theirs[HALF:])
        far[row : row + HALF] = a
        far[row + HALF : row + 2 * HALF] = b
        row += 2 * HALF
    row = layout.mix
    for target, part in ((own, mix_acc[:HALF]), (far, mix_acc[HALF:])):
        a, b = order(*lanes(part))
        target[row : row + HALF] = a
        target[row + HALF : row + 2 * HALF] = b
    row = layout.project
    side = HALF // 2
    lane = lax.broadcasted_iota(jnp.int32, (1, HALF), 1) < side
    for target, part in ((own, project_acc[:HALF]), (far, project_acc[HALF:])):
        part = part + pltpu.roll(part, side, 1)
        target[row : row + side] = jnp.where(lane, part[:side], part[side:])
    row = layout.book
    book = book_acc[...]
    book = -2.0 * (book + pltpu.roll(book, side, 1))
    n = book.shape[0] // 2
    book = jnp.where(lane, book[:n], book[n:])
    own[row : row + n] = book
    far[row : row + n] = book
    row = layout.bias
    sums = [jnp.sum(bias_acc[8 * i : 8 * i + 8], axis=0, keepdims=True) for i in range(3)]
    code = sums[2][:, :HALF]
    code = code + pltpu.roll(code, side, 1)
    which = lax.broadcasted_iota(jnp.int32, (8, HALF), 0)
    for target, first in ((own, 0), (far, HALF)):
        part = jnp.where(which == 0, sums[0][:, first : first + HALF], sums[1][:, first : first + HALF])
        target[row : row + 8] = jnp.where(which == 2, code, jnp.where(which < 2, part, 0.0))
    row = layout.decode
    rest = layout.rows - row
    own[row:] = jnp.zeros((rest, HALF), F32)
    far[row:] = jnp.zeros((rest, HALF), F32)
    if decode_acc is not None:
        own[row : row + decode_acc.shape[0]] = decode_acc[...]


def gather_plain(layout, place, *refs):
    lay_out(layout, place[0] == 1, *refs[:5], None, *refs[5:])


def gather_grads(plan, layout, place, meta, *refs):
    accs, (keep_own, keep_far, send, own, far) = refs[:6], refs[6:]
    lay_out(layout, place[0] == 1, *accs, own, far)
    base = plan.images + len(plan.chunks) + 1
    over = (meta[base + 4] > plan.covered).astype(F32)
    which = lax.broadcasted_iota(jnp.int32, (8, HALF), 0)
    row = layout.bias
    own[row : row + 8] = jnp.where(which == 3, over, own[row : row + 8])
    half = layout.half
    mine = pl.ds(pl.multiple_of(place[1] * half, SIDE), half)
    other = pl.ds(pl.multiple_of((1 - place[1]) * half, SIDE), half)
    keep_own[...] = own[mine, :]
    keep_far[...] = far[mine, :]
    send[0] = own[other, :].astype(BF16)
    send[1] = far[other, :].astype(BF16)


def add_far(keep_far, came, out):
    out[...] = (keep_far[...] + came[1].astype(F32)).astype(BF16)


def add_own(keep_own, came, came_far, out):
    total = keep_own[...] + came[0].astype(F32) + came_far[...].astype(F32)
    out[...] = total.astype(BF16).reshape(out.shape)


def add_pieces(pieces, out):
    total = pieces[0].astype(F32)
    for i in range(1, pieces.shape[0]):
        total = total + pieces[i].astype(F32)
    out[...] = jnp.broadcast_to(total.astype(BF16)[None], out.shape)


def write_grads(layout, place, mine, theirs, kernel, first_bias, mix, mix_bias, project, project_bias, book, decode, decode_bias, whole):
    half = layout.half
    whole[pl.ds(pl.multiple_of(place[1] * half, SIDE), half), :] = mine[...].astype(F32)
    whole[pl.ds(pl.multiple_of((1 - place[1]) * half, SIDE), half), :] = theirs[...].astype(F32)
    split_grads(layout, whole, kernel, first_bias, mix, mix_bias, project, project_bias, book, decode, decode_bias)


def split_grads(layout, whole, kernel, first_bias, mix, mix_bias, project, project_bias, book, decode, decode_bias):
    for tap in range(9):
        kernel[tap] = whole[tap * 2 * HALF : (tap + 1) * 2 * HALF]
    row = layout.mix
    mix[:, :HALF] = whole[row : row + HALF]
    mix[:, HALF:] = whole[row + HALF : row + 2 * HALF]
    side = HALF // 2
    for row, target in ((layout.project, project), (layout.book, book)):
        n = target.shape[0] // 2
        part = whole[row : row + n]
        target[:n] = part[:, :side]
        target[n:] = part[:, side:]
    row = layout.bias
    first_bias[...] = whole[row : row + 1]
    mix_bias[...] = whole[row + 1 : row + 2]
    project_bias[...] = whole[row + 2 : row + 3, :side]
    row = layout.decode
    n = decode.shape[0]
    decode[...] = whole[row : row + n]
    decode_bias[...] = whole[row + n : row + n + 1]


def split_again(layout, total, extra, *refs):
    whole = refs[-1]
    whole[...] = total[...].astype(F32) + extra[...]
    split_grads(layout, whole, *refs[:-1])


def restore_rows(plan, n, meta, heights, *refs):
    own, far, out = refs[:n], refs[n : 2 * n], refs[2 * n]
    stage_own, stage_far, sems = refs[2 * n + 1 :]
    copies = []
    for k in range(n):
        size = plan.chunks[k] + (LEAD if k == n - 1 else 0)
        for i, (source, target) in enumerate(((own[k], stage_own), (far[k], stage_far))):
            from_rows = source.at[pl.ds(0, size)]
            copies.append(pltpu.make_async_copy(from_rows, target.at[pl.ds(plan.starts[k], size)], sems.at[i, k]))
            copies[-1].start()
    for copy in copies:
        copy.wait()
    base = plan.images + len(plan.chunks) + 1
    own_row, send_row = meta[base], meta[base + 1]
    first, last = meta[base + 2], meta[base + 3]
    row_of = lax.broadcasted_iota(jnp.int32, (SIDE, 1, 1), 0)

    def own_image(b, carry):
        rows = stage_own[pl.ds(meta[b] + LEAD, SIDE)]
        out[b] = jnp.where(row_of < heights[b], rows, jnp.zeros_like(rows))
        return carry

    def far_image(b, carry):
        rows = stage_far[pl.ds(meta[b] + own_row - send_row + LEAD, SIDE)]
        out[b] = jnp.where(row_of < heights[b], rows, jnp.zeros_like(rows))
        return carry

    lax.fori_loop(first, last, own_image, 0)
    lax.fori_loop(0, first, far_image, 0)
    lax.fori_loop(last, plan.images, far_image, 0)


def trade(value):
    return lax.ppermute(value, "mp", [(0, 1), (1, 0)])


def run_main(plan, k, meta, heights, streams, weights, state):
    chunk, rows, in_step = plan.chunks[k], plan.rows[k], plan.in_step[k]
    last = k >= plan.usual - 1
    x_own, x_far, q_own, q_far, chosen, codes = streams
    codebook_rows = 512
    args = [meta, heights, x_own, x_far[k], q_own, q_far[k], chosen, codes, *weights]
    specs = [SMEM, SMEM, ANY, ANY, ANY, ANY, ANY, VMEM] + [VMEM] * len(weights)
    alias = {}
    if state is not None:
        args += [x_far[k - 1], q_far[k - 1], *state]
        specs += [ANY, ANY, VMEM, VMEM] + [ANY] * (len(state) - 2)
        for i in range(len(state) - 2):
            alias[len(args) - 5 + i] = 4 + i
    size = chunk + LEAD if last else chunk
    tile = (SIDE, HALF)
    outs = [shape((size,) + tile, BF16)] * 2 + [shape((LEAD,) + tile, BF16)] * 2
    outs += [shape((2 * HALF, 18 * HALF), F32), shape((2 * HALF, 2 * HALF), F32), shape((2 * HALF, HALF), F32)]
    outs += [shape((codebook_rows, HALF), F32), shape((24, 2 * HALF), F32)]
    half = chunk // 2
    scratch = [
        pltpu.VMEM((LEAD + chunk + SIDE,) + tile, BF16),
        pltpu.VMEM((LEAD + chunk + SIDE,) + tile, BF16),
        pltpu.VMEM((LEAD + half,) + tile, F32),
        pltpu.VMEM((LEAD + half,) + tile, BF16),
        pltpu.VMEM((LEAD + chunk + SIDE,) + tile, F32),
        pltpu.VMEM((in_step, SIDE) + tile, BF16),
        pltpu.VMEM((rows + 2 * SIDE,) + tile, BF16),
        pltpu.VMEM((rows + 2 * SIDE,) + tile, BF16),
        pltpu.VMEM((rows + 2 * SIDE,) + tile, F32),
        pltpu.VMEM((rows + 2 * SIDE,) + tile, BF16),
        pltpu.VMEM(((rows + 2) * SIDE, 6 * HALF), BF16),
        pltpu.VMEM((rows * SIDE, 2 * HALF), F32),
        pltpu.VMEM(((rows + 2) * SIDE, 6 * HALF), BF16),
        pltpu.VMEM((rows * SIDE, 2 * HALF), F32),
        pltpu.VMEM((rows + 2 * SIDE,) + tile, BF16),
        pltpu.VMEM((rows + 2 * SIDE,) + tile, BF16),
        pltpu.VMEM((rows + 2 * SIDE,) + tile, BF16),
        pltpu.VMEM((LEAD + chunk + 2 * SIDE,) + tile, BF16),
        pltpu.VMEM((LEAD + chunk + 2 * SIDE,) + tile, BF16),
        pltpu.SemaphoreType.DMA((13,)),
    ]
    spots = chunk * SIDE
    return pl.pallas_call(
        functools.partial(main_step, plan, k),
        out_shape=outs,
        in_specs=specs,
        out_specs=[VMEM] * len(outs),
        scratch_shapes=scratch,
        input_output_aliases=alias,
        compiler_params=params(58),
        cost_estimate=cost(60 * 65536 * spots, 8 * MIB, 2 * 256 * spots),
        name=f"main_{k}",
    )(*args)


def local(
    image_latents,
    image_heights,
    code_index,
    kernel_three,
    bias_three,
    weight_mix,
    bias_mix,
    weight_project,
    bias_project,
    codebook,
    weight_decode,
    bias_decode,
    out_grad,
):
    images = image_latents.shape[0]
    plan = Plan(images)
    n = len(plan.chunks)
    tile = (SIDE, HALF)
    where = lax.axis_index("mp").astype(jnp.int32)
    place = where.reshape(1)

    packed = pl.pallas_call(
        functools.partial(pack_latents, plan),
        out_shape=[
            shape((meta_size(plan),), jnp.int32),
            shape((LEAD + plan.total,) + tile, BF16),
            shape((3 * HALF + SIDE, HALF), BF16),
        ]
        + [shape((c,) + tile, BF16) for c in plan.chunks],
        in_specs=[SMEM, SMEM, ANY] + [VMEM] * 4,
        out_specs=[SMEM, ANY, VMEM] + [ANY] * n,
        scratch_shapes=[
            pltpu.VMEM((images, SIDE) + tile, BF16),
            pltpu.VMEM((plan.packed + SIDE,) + tile, BF16),
            pltpu.SemaphoreType.DMA((8,)),
            pltpu.SemaphoreType.DMA((n + 1,)),
        ],
        compiler_params=params(40),
        cost_estimate=cost(0, 12 * MIB),
        name="pack_latents",
    )(image_heights, place, image_latents, weight_mix, weight_project, bias_three.reshape(1, HALF), bias_mix.reshape(1, HALF))
    meta, x_own, small, x_send = packed[0], packed[1], packed[2], packed[3:]

    packed = pl.pallas_call(
        functools.partial(pack_code_grads, plan),
        out_shape=[shape((plan.total // 2,) + tile, F32)] + [shape((c // 2,) + tile, BF16) for c in plan.chunks],
        in_specs=[SMEM, ANY, VMEM],
        out_specs=[VMEM] + [VMEM] * n,
        scratch_shapes=[
            pltpu.VMEM((images, SIDE) + tile, BF16),
            pltpu.VMEM((plan.packed + SIDE,) + tile, BF16),
            pltpu.SemaphoreType.DMA((8,)),
        ],
        compiler_params=params(40),
        cost_estimate=cost(2 * 2 * plan.total * SIDE * 256 * 128, 10 * MIB),
        name="pack_code_grads",
    )(meta, out_grad, weight_decode)
    q_own, q_send = packed[0], packed[1:]

    far_kernel = trade(kernel_three)
    far_small = trade(small)
    usual = plan.usual
    x_far, q_far = [], []
    for k in range(usual):
        x_far.append(trade(x_send[k]))
        q_far.append(trade(q_send[k]))

    weights = pl.pallas_call(
        prepare_weights,
        out_shape=[
            shape((3, 6 * HALF, 2 * HALF), BF16),
            shape((3, 6 * HALF, 2 * HALF), BF16),
            shape((2 * HALF, 2 * HALF), BF16),
            shape((2, 2 * HALF, HALF), BF16),
            shape((SIDE, 2 * HALF), F32),
        ],
        in_specs=[SMEM] + [VMEM] * 5,
        out_specs=[VMEM] * 5,
        compiler_params=params(16),
        cost_estimate=cost(0, 5 * MIB),
        name="prepare_weights",
    )(place, kernel_three, far_kernel, small, far_small, bias_project.reshape(1, -1))

    groups = 8
    group = images // groups
    codes = code_index.reshape(images, SIDE * SIDE)
    book_rows, embed = codebook.shape
    whole = lambda dims: pl.BlockSpec(dims, lambda g: (0,) * len(dims))
    four = pl.BlockSpec((group, SIDE) + tile, lambda g: (g, 0, 0, 0))
    decoded, chosen, decode_acc = pl.pallas_call(
        functools.partial(decode_images, plan, groups),
        grid=(groups,),
        out_shape=[shape((images, SIDE) + tile, BF16)] * 2 + [shape((embed + 8, HALF), F32)],
        in_specs=[
            SMEM,
            pl.BlockSpec((group, SIDE * SIDE), lambda g: (g, 0)),
            four,
            whole((book_rows, embed)),
            whole((embed, HALF)),
            whole((1, HALF)),
        ],
        out_specs=[four, four, whole((embed + 8, HALF))],
        scratch_shapes=[pltpu.VMEM((book_rows, 2 * HALF), BF16), pltpu.VMEM((book_rows, HALF), F32)],
        compiler_params=params(32),
        cost_estimate=cost(2 * images * 256 * 512 * 512, 14 * MIB),
        name="decode_images",
    )(image_heights, codes, out_grad, codebook, weight_decode, bias_decode.reshape(1, HALF))

    streams = (x_own, x_far, q_own, q_far, chosen, codes)
    state = None
    win_own, win_far = [], []
    for k in range(usual):
        outs = run_main(plan, k, meta, image_heights, streams, weights, state)
        win_own.append(outs[0])
        win_far.append(trade(outs[1]))
        state = outs[2:]
    carry, accs = state[:2], state[2:]

    def restore(own, far):
        count = len(own)
        return pl.pallas_call(
            functools.partial(restore_rows, plan, count),
            out_shape=shape((images, SIDE) + tile, BF16),
            in_specs=[SMEM, SMEM] + [ANY] * (2 * count),
            out_specs=VMEM,
            scratch_shapes=[
                pltpu.VMEM((plan.total + LEAD + SIDE,) + tile, BF16),
                pltpu.VMEM((plan.total + LEAD + SIDE,) + tile, BF16),
                pltpu.SemaphoreType.DMA((2, count)),
            ],
            compiler_params=params(40),
            cost_estimate=cost(0, 10 * MIB),
            name="restore_rows",
        )(meta, image_heights, *own, *far)

    latents_grad = restore(win_own, win_far)

    devices = lax.axis_size("dp")
    layout = Layout(devices, book_rows, embed)
    half, piece, chips = layout.half, layout.piece, devices // 2
    core = lax.rem(lax.axis_index("dp").astype(jnp.int32), 2)
    spot = jnp.stack([where, core])
    keep_own, keep_far, send = pl.pallas_call(
        functools.partial(gather_grads, plan, layout),
        out_shape=[shape((half, HALF), F32)] * 2 + [shape((2, half, HALF), BF16)],
        in_specs=[SMEM, SMEM] + [VMEM] * 6,
        out_specs=[VMEM] * 3,
        scratch_shapes=[pltpu.VMEM((layout.rows, HALF), F32)] * 2,
        compiler_params=params(40),
        cost_estimate=cost(0, 8 * MIB),
        name="gather_grads",
    )(spot, meta, *accs, decode_acc)
    across = [(i, i ^ 1) for i in range(devices)]

    def step(body, out, name, *args):
        return pl.pallas_call(
            body,
            out_shape=out,
            in_specs=[VMEM] * len(args),
            out_specs=VMEM,
            compiler_params=params(24),
            cost_estimate=cost(0, 2 * MIB),
            name=name,
        )(*args)

    came = lax.ppermute(send, "dp", across)
    far = step(add_far, shape((half, HALF), BF16), "add_far", keep_far, came)
    came_far = trade(far)
    mine = step(add_own, shape((chips, piece, HALF), BF16), "add_own", keep_own, came, came_far)
    groups = [[i for i in range(devices) if i % 2 == c] for c in range(2)]
    mine = lax.all_to_all(mine, "dp", 0, 0, axis_index_groups=groups, tiled=True)
    mine = step(add_pieces, shape((chips, piece, HALF), BF16), "add_pieces", mine)
    mine = lax.all_to_all(mine, "dp", 0, 0, axis_index_groups=groups, tiled=True)
    mine = mine.reshape(half, HALF)
    theirs = lax.ppermute(mine, "dp", across)

    grads_out = [
        shape((9, 2 * HALF, HALF), F32),
        shape((1, HALF), F32),
        shape((HALF, 2 * HALF), F32),
        shape((1, HALF), F32),
        shape((HALF, embed), F32),
        shape((1, embed), F32),
        shape((book_rows, embed), F32),
        shape((embed, HALF), F32),
        shape((1, HALF), F32),
    ]
    whole = pltpu.VMEM((layout.rows, HALF), F32)

    def usual_end(latents_grad):
        grads = pl.pallas_call(
            functools.partial(write_grads, layout),
            out_shape=grads_out,
            in_specs=[SMEM, VMEM, VMEM],
            out_specs=[VMEM] * 9,
            scratch_shapes=[whole],
            compiler_params=params(24),
            cost_estimate=cost(0, 4 * MIB),
            name="write_grads",
        )(spot, mine, theirs)
        return (latents_grad, *grads)

    def longer_end(latents_grad):
        last_x, last_q = trade(x_send[usual]), trade(q_send[usual])
        streams = (x_own, x_far + [last_x], q_own, q_far + [last_q], chosen, codes)
        outs = run_main(plan, usual, meta, image_heights, streams, weights, carry)
        latents_grad = restore(win_own + [outs[0]], win_far + [trade(outs[1])])
        own, far = pl.pallas_call(
            functools.partial(gather_plain, layout),
            out_shape=[shape((layout.rows, HALF), F32)] * 2,
            in_specs=[SMEM] + [VMEM] * 5,
            out_specs=[VMEM] * 2,
            compiler_params=params(40),
            name="gather_plain",
        )(spot, *outs[4:])
        extra = lax.psum(own + trade(far), "dp")
        first, second = jnp.where(core == 0, mine, theirs), jnp.where(core == 0, theirs, mine)
        grads = pl.pallas_call(
            functools.partial(split_again, layout),
            out_shape=grads_out,
            in_specs=[VMEM, VMEM],
            out_specs=[VMEM] * 9,
            scratch_shapes=[whole],
            compiler_params=params(24),
            name="split_again",
        )(jnp.concatenate([first, second]), extra)
        return (latents_grad, *grads)

    flag = layout.bias + 3
    holder = flag // half
    flags = jnp.where(core == holder, mine[flag - holder * half, 0], theirs[flag - holder * half, 0])
    ends = lax.cond(flags.astype(F32) > 0.5, longer_end, usual_end, latents_grad)
    latents_grad, kernel_grad, first_bias, mix_grad, mix_bias, project_grad, project_bias, book, decode, decode_bias = ends
    return (
        decoded,
        latents_grad,
        kernel_grad,
        first_bias.reshape(HALF),
        mix_grad,
        mix_bias.reshape(HALF),
        project_grad,
        project_bias.reshape(embed),
        book,
        decode,
        decode_bias.reshape(HALF),
    )


def solution(mesh):
    tile = P("dp", None, None, "mp")
    placed = (
        tile,
        P("dp"),
        P("dp", None, None),
        P(None, None, "mp"),
        P("mp"),
        P("mp", None),
        P("mp"),
        P("mp", None),
        P(),
        P(),
        P(None, "mp"),
        P("mp"),
        tile,
    )
    outs = (
        tile,
        tile,
        P(None, None, "mp"),
        P("mp"),
        P("mp", None),
        P("mp"),
        P("mp", None),
        P(),
        P(),
        P(None, "mp"),
        P("mp"),
    )
    return jax.shard_map(local, mesh=mesh, in_specs=placed, out_specs=outs, check_vma=False)
```

```python
import functools

import jax
import jax.numpy as jnp
from jax import lax
from jax.experimental import pallas as pl
from jax.experimental.pallas import tpu as pltpu
from jax.sharding import PartitionSpec as P

SIDE = 16
HALF = 128
LEAD = 16
BLOCK = 32
TILE = 32
SENTINEL = 512.0
GELU_SCALE = 0.7978845608028654
GELU_CUBE = 0.044715
COMMIT = 0.25
F32 = jnp.float32
BF16 = jnp.bfloat16
ANY = pl.BlockSpec(memory_space=pl.ANY)
SMEM = pl.BlockSpec(memory_space=pltpu.SMEM)
VMEM = pl.BlockSpec(memory_space=pltpu.VMEM)
MIB = 1 << 20

NT = (((1,), (1,)), ((), ()))
TN = (((0,), (0,)), ((), ()))
NN = (((1,), (0,)), ((), ()))


def dot(a, b, dims=NN):
    return lax.dot_general(a, b, dims, preferred_element_type=F32)


def one_hot_columns(codes, code_of):
    return jnp.where(code_of == codes.astype(jnp.int16), jnp.bfloat16(1), jnp.bfloat16(0))


def numbers(count, width):
    return lax.broadcasted_iota(jnp.int32, (count, width), 0).astype(jnp.int16)


def shape(dims, kind):
    return jax.ShapeDtypeStruct(dims, kind)


def params(mib):
    return pltpu.CompilerParams(vmem_limit_bytes=mib * MIB)


def cost(flops, moved, slow=0):
    return pl.CostEstimate(flops=flops, bytes_accessed=moved, transcendentals=slow)


class Plan:
    def __init__(self, images):
        self.images = images
        longest = images * SIDE // 2 + SIDE // 2
        part = images // 4
        self.chunks = [5 * part, 9 * part, 10 * part]
        self.usual = len(self.chunks)
        rest = longest - sum(self.chunks)
        self.chunks.append(rest)
        self.starts = [sum(self.chunks[:k]) for k in range(len(self.chunks))]
        self.total = sum(self.chunks)
        self.packed = -(-(LEAD + longest + self.total + LEAD) // SIDE) * SIDE
        self.rows = []
        for c in self.chunks:
            most = 1 + c + 15 + c // 4 + 1
            self.rows.append(-(-most // BLOCK) * BLOCK)
        self.covered = sum(self.chunks[: self.usual])


def meta_size(plan):
    return plan.images + len(plan.chunks) + 1 + 5


def plan_rows(plan, heights, place, meta):
    images = plan.images
    base = images + len(plan.chunks) + 1

    def total_of(b, acc):
        return acc + heights[b]

    total = lax.fori_loop(0, images, total_of, jnp.int32(0))

    def split_of(b, state):
        acc, best, split, cut = state
        acc = acc + heights[b]
        worst = jnp.maximum(acc, total - acc)
        better = worst < best
        return (acc, jnp.where(better, worst, best), jnp.where(better, b + 1, split), jnp.where(better, acc, cut))

    _, _, split, cut = lax.fori_loop(0, images, split_of, (jnp.int32(0), jnp.int32(1 << 20), jnp.int32(0), jnp.int32(0)))
    mine = place[0]
    own_first = jnp.where(mine == 0, 0, split)
    own_last = jnp.where(mine == 0, split, images)
    own_row = jnp.where(mine == 0, 0, cut)
    send_row = jnp.where(mine == 0, cut, 0)
    for k in range(len(plan.chunks) + 1):
        meta[images + k] = own_first
    ends = [plan.starts[k] + plan.chunks[k] for k in range(len(plan.chunks))]

    def place_of(b, acc):
        meta[b] = acc - own_row
        acc = acc + heights[b]
        end = acc - own_row
        inside = jnp.logical_and(b >= own_first, b < own_last)
        step = jnp.int32(0)
        for k in range(len(plan.chunks) - 1):
            step = step + (end > ends[k]).astype(jnp.int32)

        @pl.when(inside)
        def _():
            meta[images + 1 + step] = b + 1

        return acc

    lax.fori_loop(0, images, place_of, jnp.int32(0))
    for k in range(len(plan.chunks)):
        meta[images + k + 1] = jnp.maximum(meta[images + k + 1], meta[images + k])
    meta[base] = own_row
    meta[base + 1] = send_row
    meta[base + 2] = own_first
    meta[base + 3] = own_last
    meta[base + 4] = jnp.maximum(cut, total - cut)


def pack_rows(plan, meta, source, packed, piece, count):
    base = plan.images + len(plan.chunks) + 1

    def one(i, carry):
        b = piece * count + i
        row = meta[b] + meta[base] + LEAD
        packed[pl.ds(row, SIDE)] = source[b]
        return carry

    lax.fori_loop(0, count, one, 0)


def pack_latents(plan, heights, place, x_hbm, meta, own, *rest):
    n = len(plan.chunks)
    sends, (x_in, packed, sem_in, sem_out) = rest[:n], rest[n:]
    pieces = 8
    count = plan.images // pieces
    fetch = []
    for p in range(pieces):
        part = pl.ds(p * count, count)
        fetch.append(pltpu.make_async_copy(x_hbm.at[part], x_in.at[part], sem_in.at[p]))
        fetch[-1].start()
    plan_rows(plan, heights, place, meta)
    base = plan.images + n + 1
    for p in range(pieces):
        fetch[p].wait()
        pack_rows(plan, meta, x_in, packed, p, count)
    copies = []
    for k in range(n):
        part = pl.ds(LEAD + meta[base + 1] + plan.starts[k], plan.chunks[k])
        copies.append(pltpu.make_async_copy(packed.at[part], sends[k], sem_out.at[k]))
        copies[-1].start()
    copies.append(pltpu.make_async_copy(packed.at[pl.ds(meta[base], LEAD + plan.total)], own, sem_out.at[n]))
    copies[-1].start()
    for copy in copies:
        copy.wait()


def pack_code_grads(plan, meta, og_hbm, decode_w, weight_mix, project_t, bias_first, bias_mix, own, small, *rest):
    n = len(plan.chunks)
    sends, (og_in, packed, sem_in) = rest[:n], rest[n:]
    pieces = 8
    count = plan.images // pieces
    fetch = []
    for p in range(pieces):
        part = pl.ds(p * count, count)
        fetch.append(pltpu.make_async_copy(og_hbm.at[part], og_in.at[part], sem_in.at[p]))
        fetch[-1].start()
    base = plan.images + n + 1

    def clear(i, carry):
        packed[pl.ds(i * SIDE, SIDE)] = jnp.zeros((SIDE, SIDE, HALF), BF16)
        return carry

    lax.fori_loop(0, packed.shape[0] // SIDE, clear, 0)
    side = HALF // 2
    small[0:HALF] = weight_mix[:, :HALF]
    small[HALF : 2 * HALF] = weight_mix[:, HALF:]
    small[2 * HALF : 2 * HALF + side] = project_t[...]
    which = lax.broadcasted_iota(jnp.int32, (SIDE, HALF), 0)
    first, second = bias_first[...].astype(F32), bias_mix[...].astype(F32)
    first = jnp.where(which == 0, first, jnp.where(which == 1, second, 0.0))
    small[2 * HALF + side : 2 * HALF + side + SIDE] = first.astype(BF16)
    w = decode_w[...]
    blank = jnp.zeros_like(w)
    upper = jnp.concatenate([w, blank], axis=0)
    lower = jnp.concatenate([blank, w], axis=0)
    for p in range(pieces):
        fetch[p].wait()
        pack_rows(plan, meta, og_in, packed, p, count)
    for k in range(n):
        half = plan.chunks[k] // 2
        for which in range(2):
            row = LEAD + meta[base + 1 - which] + plan.starts[k]
            a = packed[pl.ds(row, half)].reshape(half * SIDE, HALF)
            b = packed[pl.ds(row + half, half)].reshape(half * SIDE, HALF)
            both = dot(a, upper, NT) + dot(b, lower, NT)
            both = both.reshape(half, SIDE, HALF)
            if which == 0:
                sends[k][...] = both.astype(BF16)
            else:
                own[pl.ds(plan.starts[k] // 2, half)] = both


def prepare_weights(place, kernel, far_kernel, small, far_small, bias_code, codebook_t, forward, backward, mix, project, bias, book):
    first = pl.multiple_of(place[0] * HALF, HALF)
    order = (first, HALF - first)
    for tap in range(9):
        for d, source in enumerate((kernel, far_kernel)):
            for c in range(2):
                tile = source[tap, pl.ds(order[c], HALF), :]
                row = tap * 2 * HALF
                forward[row + c * HALF : row + (c + 1) * HALF, d * HALF : (d + 1) * HALF] = tile
                backward[row + d * HALF : row + (d + 1) * HALF, c * HALF : (c + 1) * HALF] = tile.T
    blank = jnp.zeros((HALF, HALF // 2), BF16)
    for d, source in enumerate((small, far_small)):
        rows = pl.ds(d * HALF, HALF)
        for c in range(2):
            mix[rows, c * HALF : (c + 1) * HALF] = source[pl.ds(order[c], HALF), :]
        part = source[2 * HALF : 2 * HALF + HALF // 2, :].T
        project[0, rows, :] = jnp.concatenate([part, blank], axis=1)
        project[1, rows, :] = jnp.concatenate([blank, part], axis=1)
        bias[0:8, d * HALF : (d + 1) * HALF] = source[2 * HALF + HALF // 2 : 2 * HALF + HALF // 2 + SIDE, :].astype(F32)[0:8]
    code = bias_code[...].astype(F32)
    code = jnp.concatenate([code, code], axis=1)
    bias[8:16, :] = jnp.broadcast_to(jnp.concatenate([code, code], axis=1), (8, 2 * HALF))
    book[...] = jnp.concatenate([codebook_t[...], codebook_t[...]], axis=0)


def sum_codes(plan, steps, heights, codes, og, codebook_t, grads, hot, cots, sums):
    step = pl.program_id(0)
    group = plan.images // steps

    @pl.when(step == 0)
    def _():
        sums[...] = jnp.zeros_like(sums)

    spots = SIDE * SIDE
    code_of = numbers(codebook_t.shape[1], spots)
    spot = lax.broadcasted_iota(jnp.int32, (spots, 1), 0)
    for i in range(group):
        live = heights[step * group + i] * SIDE
        hot[:, i * spots : (i + 1) * spots] = one_hot_columns(codes[i : i + 1, :], code_of)
        cot = og[i].reshape(spots, HALF).astype(F32)
        cots[i * spots : (i + 1) * spots] = jnp.where(spot < live, cot, 0.0).astype(BF16)
    sums[...] += dot(hot[...], cots[...])

    @pl.when(step == steps - 1)
    def _():
        total = sums[...]
        book = codebook_t[...].astype(F32)
        w = lax.dot_general(book, total, NN, precision=lax.Precision.HIGHEST, preferred_element_type=F32)
        bias = jnp.sum(total, axis=0, keepdims=True)
        embed = w.shape[0]
        grads[0:embed] = w
        grads[embed : embed + 8] = jnp.broadcast_to(bias, (8, HALF))


def decode_images(plan, steps, heights, codes, codebook_t, decode_w, decode_b, _, decoded, table):
    step = pl.program_id(0)
    group = plan.images // steps

    @pl.when(step == 0)
    def _():
        full = dot(codebook_t[...], decode_w[...], TN) + decode_b[...].astype(F32)
        table[...] = full.T.astype(BF16)

    spots = SIDE * SIDE
    code_of = numbers(codebook_t.shape[1], spots)
    spot = lax.broadcasted_iota(jnp.int32, (spots, 1), 0)
    for i in range(group):
        live = heights[step * group + i] * SIDE
        out = dot(table[...], one_hot_columns(codes[i : i + 1, :], code_of)).T
        decoded[i] = jnp.where(spot < live, out, 0.0).astype(BF16).reshape(SIDE, SIDE, HALF)


def gelu_parts(v):
    square = v * v
    t = jnp.tanh(v * (GELU_SCALE + (GELU_SCALE * GELU_CUBE) * square))
    half = 0.5 + 0.5 * t
    slope = half + (0.5 * v) * (1.0 - t * t) * (GELU_SCALE + (3.0 * GELU_SCALE * GELU_CUBE) * square)
    return v * half, slope


def main_step(plan, k, waits, *refs):
    first_step = k == 0
    fresh = k in (0, plan.usual)
    refs = list(refs[waits:])

    def take(count):
        got = refs[:count]
        del refs[:count]
        return got

    meta, heights, x_own, x_far, q_own, q_far, codes = take(7)
    kernel, kernel_t, mix, project, bias, book = take(6)
    if not first_step:
        x_past, q_past, carry_own, carry_far = take(4)
    if not fresh:
        past_accs = take(5)
    win_own, win_far, next_own, next_far = take(4)
    kernel_acc, mix_acc, project_acc, book_acc, bias_acc = take(5)
    xo, xf, qo, qf, qd, xc_o, xc_f, qc, chc, act3, slope_x, grad3, block_g, diffs, lg_o, lg_f, out_o, out_f = refs[:18]
    second_s, slope_s, low_s, mixed_s, code_s, sems = refs[18:]

    chunk, start = plan.chunks[k], plan.starts[k]
    images, rows = plan.images, plan.rows[k]
    half = chunk // 2
    spots = BLOCK * SIDE
    low = meta[images + k]
    high = meta[images + k + 1]

    copies = [
        (x_own.at[pl.ds(start, LEAD + chunk)], xo.at[pl.ds(0, LEAD + chunk)]),
        (x_far, xf.at[pl.ds(LEAD, chunk)]),
        (q_own.at[pl.ds(start // 2, half)], qo.at[pl.ds(LEAD, half)]),
        (q_far, qf.at[pl.ds(LEAD, half)]),
    ]
    if not first_step:
        past = plan.chunks[k - 1]
        copies += [
            (x_past.at[pl.ds(past - LEAD, LEAD)], xf.at[pl.ds(0, LEAD)]),
            (q_own.at[pl.ds(start // 2 - LEAD, LEAD)], qo.at[pl.ds(0, LEAD)]),
            (q_past.at[pl.ds(past // 2 - LEAD, LEAD)], qf.at[pl.ds(0, LEAD)]),
        ]
    accs = (mix_acc, project_acc, book_acc, bias_acc, kernel_acc)
    early = len(copies)
    if not fresh:
        copies += list(zip(past_accs[1:] + past_accs[:1], accs))
    started = []
    for i, (source, target) in enumerate(copies):
        started.append(pltpu.make_async_copy(source, target, sems.at[i]))
        started[-1].start()
    started, later = started[:early], started[early:]

    if fresh:
        for acc in accs:
            acc[...] = jnp.zeros(acc.shape, F32)
    if first_step:
        out_o[0:LEAD] = jnp.zeros((LEAD, SIDE, HALF), BF16)
        out_f[0:LEAD] = jnp.zeros((LEAD, SIDE, HALF), BF16)
    else:
        out_o[0:LEAD] = carry_own[...]
        out_f[0:LEAD] = carry_far[...]

    blank = jnp.zeros((SIDE, SIDE, HALF), BF16)
    blank_f = jnp.zeros((SIDE, SIDE, HALF), F32)
    no_code = jnp.full((SIDE, SIDE, HALF), SENTINEL, BF16)
    for r in range(0, rows, SIDE):
        part = pl.ds(r, SIDE)
        xc_o[part] = blank
        xc_f[part] = blank
        qc[part] = blank_f
        chc[part] = no_code
    for copy in started:
        copy.wait()

    lane3 = lax.broadcasted_iota(jnp.int32, (1, SIDE, HALF), 2) < HALF // 2

    def spread(r0, count):
        both = (qo[pl.ds(r0, count)] + qf[pl.ds(r0, count)].astype(F32)).reshape(count * SIDE, HALF)
        turned = pltpu.roll(both, HALF // 2, 1).reshape(count, SIDE, HALF)
        both = both.reshape(count, SIDE, HALF)
        return jnp.where(lane3, both, turned), jnp.where(lane3, turned, both)

    upper, lower = spread(LEAD, half)
    qd[pl.ds(LEAD, half)] = upper
    qd[pl.ds(LEAD + half, half)] = lower
    if not first_step:
        _, lower = spread(0, LEAD)
        qd[0:LEAD] = lower

    codes_n = book_acc.shape[0]
    code_of = numbers(codes_n, SIDE * SIDE)

    def place(b, dst):
        src = meta[b] - start + LEAD
        xc_o[pl.ds(dst, SIDE)] = xo[pl.ds(src, SIDE)]
        xc_f[pl.ds(dst, SIDE)] = xf[pl.ds(src, SIDE)]
        qc[pl.ds(dst, SIDE)] = qd[pl.ds(src, SIDE)]
        found = dot(book[...], one_hot_columns(codes[pl.ds(b, 1), :], code_of)).T
        chc[pl.ds(dst, SIDE)] = found.astype(BF16).reshape(SIDE, SIDE, HALF)
        end = dst + heights[b]
        xc_o[pl.ds(end, SIDE)] = blank
        xc_f[pl.ds(end, SIDE)] = blank
        qc[pl.ds(end, SIDE)] = blank_f
        chc[pl.ds(end, SIDE)] = no_code
        return end + 1

    used = lax.fori_loop(low, high, place, jnp.int32(1))
    blocks = jnp.where(high > low, (used + (BLOCK - 1)) // BLOCK, 0)

    column = lax.rem(lax.broadcasted_iota(jnp.int32, (TILE, 1), 0), SIDE)
    not_first = column != 0
    not_last = column != SIDE - 1

    def shifted(value):
        back = jnp.where(not_first, pltpu.roll(value, 1, 0), 0.0)
        ahead = jnp.where(not_last, pltpu.roll(value, TILE - 1, 0), 0.0)
        return back.astype(BF16), ahead.astype(BF16)

    edge = jnp.zeros((SIDE, 3 * 2 * HALF), BF16)
    act3[0:SIDE] = edge
    grad3[0:SIDE] = edge
    beyond = pl.multiple_of((blocks * BLOCK + 1) * SIDE, SIDE)
    act3[pl.ds(beyond, SIDE)] = edge
    grad3[pl.ds(beyond, SIDE)] = edge
    diffs[pl.ds(blocks * BLOCK, SIDE)] = blank

    tiles = range(0, spots, TILE)

    def read_x(r0, t):
        part = pl.ds(r0 + t // SIDE, TILE // SIDE)
        o = xc_o[part].reshape(TILE, HALF)
        f = xc_f[part].reshape(TILE, HALF)
        return jnp.concatenate([o, f], axis=1).astype(F32)

    def at(row, count=BLOCK):
        return pl.ds(pl.multiple_of(row * SIDE, SIDE), count * SIDE)

    def tile_at(row, t):
        return pl.ds(pl.multiple_of(row * SIDE, SIDE) + t, TILE)

    def activate(j, carry):
        r0 = j * BLOCK
        for t in tiles:
            value, slope = gelu_parts(read_x(r0, t))
            slope_x[tile_at(r0, t), :] = slope
            back, ahead = shifted(value)
            act3[tile_at(r0 + 1, t), 0 : 2 * HALF] = back
            act3[tile_at(r0 + 1, t), 2 * HALF : 4 * HALF] = value.astype(BF16)
            act3[tile_at(r0 + 1, t), 4 * HALF : 6 * HALF] = ahead
        return carry

    lax.fori_loop(0, blocks, activate, 0)
    for copy in later[:4]:
        copy.wait()

    bias_first = bias[0:1, :]
    bias_mix = bias[1:2, :]
    bias_code = bias[8:9, 0:HALF]
    lane = lax.broadcasted_iota(jnp.int32, (1, HALF), 1) < HALF // 2
    hb = BLOCK // 2
    hs = hb * SIDE

    def add_rows(total, value):
        value = value.astype(F32)
        for i in range(0, value.shape[0], 8):
            part = value[i : i + 8]
            total = part if total is None else total + part
        return total

    half_tiles = range(0, hs, TILE)

    def middle(j, carry):
        r0 = j * BLOCK
        window = jnp.concatenate([act3[at(r0 + i), :] for i in range(3)], axis=1)
        pre = dot(window, kernel[...])
        for t in tiles:
            value, slope = gelu_parts(pre[t : t + TILE] + bias_first)
            second_s[t : t + TILE] = value.astype(BF16)
            slope_s[t : t + TILE] = slope
        mixed = dot(second_s[...], mix[...])
        for t in tiles:
            low_s[t : t + TILE] = (read_x(r0, t) + mixed[t : t + TILE] + bias_mix).astype(BF16)
        latent = dot(low_s[0:hs], project[0]) + dot(low_s[hs:], project[1])
        total = None
        for t in half_tiles:
            first = pl.ds(r0 + t // SIDE, TILE // SIDE)
            other = pl.ds(r0 + hb + t // SIDE, TILE // SIDE)
            ch = jnp.where(lane3, chc[first].astype(F32), chc[other].astype(F32)).reshape(TILE, HALF)
            q = jnp.where(lane3, qc[first], qc[other]).reshape(TILE, HALF)
            live = ch < 0.5 * SENTINEL
            diff = jnp.where(live, latent[t : t + TILE] + bias_code - ch, 0.0)
            code_grad = jnp.where(live, q + (2.0 * COMMIT) * diff, 0.0).astype(BF16)
            code_s[t : t + TILE] = code_grad
            total = add_rows(total, code_grad)
            big = diff.astype(BF16).astype(F32)
            small = diff - big
            turned = pltpu.roll(small, HALF // 2, 1)
            diffs[first] = jnp.where(lane, big, turned).astype(BF16).reshape(TILE // SIDE, SIDE, HALF)
            turned = pltpu.roll(big, HALF // 2, 1)
            diffs[other] = jnp.where(lane, turned, small).astype(BF16).reshape(TILE // SIDE, SIDE, HALF)
        bias_acc[16:24, 0:HALF] += total
        total = None
        for half_block in range(2):
            block = dot(code_s[...], project[half_block], NT)
            for t in half_tiles:
                part = block[t : t + TILE]
                spot_of = t + half_block * hs
                block_g[tile_at(r0, spot_of), :] = part
                mixed_grad = part.astype(BF16)
                mixed_s[spot_of : spot_of + TILE] = mixed_grad
                total = add_rows(total, mixed_grad)
        bias_acc[8:16] += total
        second_grad = dot(mixed_s[...], mix[...], NT)
        total = None
        for t in tiles:
            first_grad = slope_s[t : t + TILE] * second_grad[t : t + TILE]
            back, ahead = shifted(first_grad)
            first_low = first_grad.astype(BF16)
            grad3[tile_at(r0 + 1, t), 0 : 2 * HALF] = ahead
            grad3[tile_at(r0 + 1, t), 2 * HALF : 4 * HALF] = first_low
            grad3[tile_at(r0 + 1, t), 4 * HALF : 6 * HALF] = back
            total = add_rows(total, first_low)
        bias_acc[0:8] += total
        mix_acc[...] += dot(second_s[...], mixed_s[...], TN)
        project_acc[...] += jnp.where(lane, dot(low_s[0:hs], code_s[...], TN), dot(low_s[hs:], code_s[...], TN))
        return carry

    lax.fori_loop(0, blocks, middle, 0)
    for copy in later[4:]:
        copy.wait()

    def finish(j, carry):
        r0 = j * BLOCK
        active = act3[at(r0 + 1), 2 * HALF : 4 * HALF].T
        for i in range(3):
            kernel_acc[:, i * 6 * HALF : (i + 1) * 6 * HALF] += dot(active, grad3[at(r0 + 2 - i), :])
        window = jnp.concatenate([grad3[at(r0 + 2 - i), :] for i in range(3)], axis=1)
        grad = dot(window, kernel_t[...])
        for t in tiles:
            out = block_g[tile_at(r0, t), :] + slope_x[tile_at(r0, t), :] * grad[t : t + TILE]
            out = out.astype(BF16)
            part = pl.ds(r0 + t // SIDE, TILE // SIDE)
            lg_o[part] = out[:, :HALF].reshape(TILE // SIDE, SIDE, HALF)
            lg_f[part] = out[:, HALF:].reshape(TILE // SIDE, SIDE, HALF)
        return carry

    lax.fori_loop(0, blocks, finish, 0)

    spot = lax.broadcasted_iota(jnp.int32, (1, SIDE * SIDE), 1)

    def collect(b, src):
        dst = meta[b] - start + LEAD
        out_o[pl.ds(dst, SIDE)] = lg_o[pl.ds(src, SIDE)]
        out_f[pl.ds(dst, SIDE)] = lg_f[pl.ds(src, SIDE)]
        row = jnp.where(spot < heights[b] * SIDE, codes[pl.ds(b, 1), :], -1)
        hot = one_hot_columns(row, code_of)
        book_acc[...] += dot(hot, diffs[pl.ds(src, SIDE)].reshape(SIDE * SIDE, HALF))
        return src + heights[b] + 1

    lax.fori_loop(low, high, collect, jnp.int32(1))
    size = win_own.shape[0]
    win_own[...] = out_o[0:size]
    win_far[...] = out_f[0:size]
    next_own[...] = out_o[chunk : chunk + LEAD]
    next_far[...] = out_f[chunk : chunk + LEAD]


class Layout:
    def __init__(self, devices, book_rows, embed):
        self.mix = 9 * 2 * HALF
        self.project = self.mix + 2 * HALF
        self.book = self.project + HALF // 2
        self.bias = self.book + book_rows // 2
        self.decode = self.bias + 8
        used = self.decode + embed + 8
        self.devices = devices
        self.piece = -(-used // (devices * SIDE)) * SIDE
        self.rows = self.piece * devices
        self.half = self.rows // 2
        self.used = used


def lay_out(layout, swap, kernel_acc, mix_acc, project_acc, book_acc, bias_acc, decode_acc, own, far):
    def lanes(value):
        return value[:, :HALF], value[:, HALF:]

    def order(first, second):
        return jnp.where(swap, second, first), jnp.where(swap, first, second)

    row = 0
    for tap in range(9):
        block = kernel_acc[:, tap * 2 * HALF : (tap + 1) * 2 * HALF]
        mine, theirs = lanes(block)
        a, b = order(mine[:HALF], mine[HALF:])
        own[row : row + HALF] = a
        own[row + HALF : row + 2 * HALF] = b
        a, b = order(theirs[:HALF], theirs[HALF:])
        far[row : row + HALF] = a
        far[row + HALF : row + 2 * HALF] = b
        row += 2 * HALF
    row = layout.mix
    for target, part in ((own, mix_acc[:HALF]), (far, mix_acc[HALF:])):
        a, b = order(*lanes(part))
        target[row : row + HALF] = a
        target[row + HALF : row + 2 * HALF] = b
    row = layout.project
    side = HALF // 2
    for target, part in ((own, project_acc[:HALF]), (far, project_acc[HALF:])):
        part = part + pltpu.roll(part, side, 1)
        target[row : row + side] = part.T[:side]
    row = layout.book
    book = book_acc[...]
    book = -2.0 * (book + pltpu.roll(book, side, 1))
    book = book.T[:side]
    for c in range(book.shape[1] // HALF):
        part = book[:, c * HALF : (c + 1) * HALF]
        own[row + c * side : row + (c + 1) * side] = part
        far[row + c * side : row + (c + 1) * side] = part
    row = layout.bias
    sums = [jnp.sum(bias_acc[8 * i : 8 * i + 8], axis=0, keepdims=True) for i in range(3)]
    code = sums[2][:, :HALF]
    code = code + pltpu.roll(code, side, 1)
    which = lax.broadcasted_iota(jnp.int32, (8, HALF), 0)
    for target, first in ((own, 0), (far, HALF)):
        part = jnp.where(which == 0, sums[0][:, first : first + HALF], sums[1][:, first : first + HALF])
        target[row : row + 8] = jnp.where(which == 2, code, jnp.where(which < 2, part, 0.0))
    row = layout.decode
    rest = layout.rows - row
    own[row:] = jnp.zeros((rest, HALF), F32)
    far[row:] = jnp.zeros((rest, HALF), F32)
    if decode_acc is not None:
        own[row : row + decode_acc.shape[0]] = decode_acc[...]


def gather_plain(layout, place, *refs):
    lay_out(layout, place[0] == 1, *refs[:5], None, *refs[5:])


def gather_grads(plan, layout, place, meta, *refs):
    refs = refs[:6] + refs[7:]
    accs, (keep_own, keep_far, send, own, far) = refs[:6], refs[6:]
    lay_out(layout, place[0] == 1, *accs, own, far)
    base = plan.images + len(plan.chunks) + 1
    over = (meta[base + 4] > plan.covered).astype(F32)
    which = lax.broadcasted_iota(jnp.int32, (8, HALF), 0)
    row = layout.bias
    own[row : row + 8] = jnp.where(which == 3, over, own[row : row + 8])
    half = layout.half
    mine = pl.ds(pl.multiple_of(place[1] * half, SIDE), half)
    other = pl.ds(pl.multiple_of((1 - place[1]) * half, SIDE), half)
    keep_own[...] = own[mine, :]
    keep_far[...] = far[mine, :]
    send[0] = own[other, :].astype(BF16)
    send[1] = far[other, :].astype(BF16)


def add_far(keep_far, came, out):
    out[...] = (keep_far[...] + came[1].astype(F32)).astype(BF16)


def add_own(keep_own, came, came_far, out):
    total = keep_own[...] + came[0].astype(F32) + came_far[...].astype(F32)
    out[...] = total.astype(BF16).reshape(out.shape)


def add_pieces(pieces, _, out):
    total = pieces[0].astype(F32)
    for i in range(1, pieces.shape[0]):
        total = total + pieces[i].astype(F32)
    out[...] = jnp.broadcast_to(total.astype(BF16)[None], out.shape)


def write_grads(layout, place, mine, theirs, kernel, first_bias, mix, mix_bias, project, project_bias, book, decode, decode_bias, whole):
    half = layout.half
    whole[pl.ds(pl.multiple_of(place[1] * half, SIDE), half), :] = mine[...].astype(F32)
    whole[pl.ds(pl.multiple_of((1 - place[1]) * half, SIDE), half), :] = theirs[...].astype(F32)
    split_grads(layout, whole, kernel, first_bias, mix, mix_bias, project, project_bias, book, decode, decode_bias)


def split_grads(layout, whole, kernel, first_bias, mix, mix_bias, project, project_bias, book, decode, decode_bias):
    for tap in range(9):
        kernel[tap] = whole[tap * 2 * HALF : (tap + 1) * 2 * HALF]
    row = layout.mix
    mix[:, :HALF] = whole[row : row + HALF]
    mix[:, HALF:] = whole[row + HALF : row + 2 * HALF]
    side = HALF // 2
    for row, target in ((layout.project, project), (layout.book, book)):
        for c in range(target.shape[1] // HALF):
            target[:, c * HALF : (c + 1) * HALF] = whole[row + c * side : row + (c + 1) * side]
    row = layout.bias
    first_bias[...] = whole[row : row + 1]
    mix_bias[...] = whole[row + 1 : row + 2]
    project_bias[...] = whole[row + 2 : row + 3, :side]
    row = layout.decode
    n = decode.shape[0]
    decode[...] = whole[row : row + n]
    decode_bias[...] = whole[row + n : row + n + 1]


def split_again(layout, total, extra, *refs):
    whole = refs[-1]
    whole[...] = total[...].astype(F32) + extra[...]
    split_grads(layout, whole, *refs[:-1])


def restore_rows(plan, n, meta, heights, *refs):
    own, far, out = refs[:n], refs[n : 2 * n], refs[2 * n]
    stage_own, stage_far, sems = refs[2 * n + 1 :]
    copies = []
    for k in range(n):
        size = plan.chunks[k] + (LEAD if k == n - 1 else 0)
        for i, (source, target) in enumerate(((own[k], stage_own), (far[k], stage_far))):
            from_rows = source.at[pl.ds(0, size)]
            copies.append(pltpu.make_async_copy(from_rows, target.at[pl.ds(plan.starts[k], size)], sems.at[i, k]))
            copies[-1].start()
    for copy in copies:
        copy.wait()
    base = plan.images + len(plan.chunks) + 1
    own_row, send_row = meta[base], meta[base + 1]
    first, last = meta[base + 2], meta[base + 3]
    row_of = lax.broadcasted_iota(jnp.int32, (SIDE, 1, 1), 0)

    def own_image(b, carry):
        rows = stage_own[pl.ds(meta[b] + LEAD, SIDE)]
        out[b] = jnp.where(row_of < heights[b], rows, jnp.zeros_like(rows))
        return carry

    def far_image(b, carry):
        rows = stage_far[pl.ds(meta[b] + own_row - send_row + LEAD, SIDE)]
        out[b] = jnp.where(row_of < heights[b], rows, jnp.zeros_like(rows))
        return carry

    lax.fori_loop(first, last, own_image, 0)
    lax.fori_loop(0, first, far_image, 0)
    lax.fori_loop(last, plan.images, far_image, 0)


def trade(value):
    return lax.ppermute(value, "mp", [(0, 1), (1, 0)])


def run_main(plan, k, meta, heights, streams, weights, state, waits=()):
    chunk, rows = plan.chunks[k], plan.rows[k]
    last = k >= plan.usual - 1
    x_own, x_far, q_own, q_far, codes = streams
    codebook_rows = weights[-1].shape[1]
    args = [*waits, meta, heights, x_own, x_far[k], q_own, q_far[k], codes, *weights]
    specs = [ANY] * len(waits) + [SMEM, SMEM, ANY, ANY, ANY, ANY, VMEM] + [VMEM] * len(weights)
    alias = {}
    if state is not None:
        args += [x_far[k - 1], q_far[k - 1], *state]
        specs += [ANY, ANY, VMEM, VMEM] + [ANY] * (len(state) - 2)
        for i in range(len(state) - 2):
            alias[len(args) - 5 + i] = 4 + i
    size = chunk + LEAD if last else chunk
    tile = (SIDE, HALF)
    outs = [shape((size,) + tile, BF16)] * 2 + [shape((LEAD,) + tile, BF16)] * 2
    outs += [shape((2 * HALF, 18 * HALF), F32), shape((2 * HALF, 2 * HALF), F32), shape((2 * HALF, HALF), F32)]
    outs += [shape((codebook_rows, HALF), F32), shape((24, 2 * HALF), F32)]
    half = chunk // 2
    scratch = [
        pltpu.VMEM((LEAD + chunk + SIDE,) + tile, BF16),
        pltpu.VMEM((LEAD + chunk + SIDE,) + tile, BF16),
        pltpu.VMEM((LEAD + half,) + tile, F32),
        pltpu.VMEM((LEAD + half,) + tile, BF16),
        pltpu.VMEM((LEAD + chunk + SIDE,) + tile, F32),
        pltpu.VMEM((rows + 2 * SIDE,) + tile, BF16),
        pltpu.VMEM((rows + 2 * SIDE,) + tile, BF16),
        pltpu.VMEM((rows + 2 * SIDE,) + tile, F32),
        pltpu.VMEM((rows + 2 * SIDE,) + tile, BF16),
        pltpu.VMEM(((rows + 2) * SIDE, 6 * HALF), BF16),
        pltpu.VMEM((rows * SIDE, 2 * HALF), F32),
        pltpu.VMEM(((rows + 2) * SIDE, 6 * HALF), BF16),
        pltpu.VMEM((rows * SIDE, 2 * HALF), F32),
        pltpu.VMEM((rows + 2 * SIDE,) + tile, BF16),
        pltpu.VMEM((rows + 2 * SIDE,) + tile, BF16),
        pltpu.VMEM((rows + 2 * SIDE,) + tile, BF16),
        pltpu.VMEM((LEAD + chunk + 2 * SIDE,) + tile, BF16),
        pltpu.VMEM((LEAD + chunk + 2 * SIDE,) + tile, BF16),
        pltpu.VMEM((BLOCK * SIDE, 2 * HALF), BF16),
        pltpu.VMEM((BLOCK * SIDE, 2 * HALF), F32),
        pltpu.VMEM((BLOCK * SIDE, 2 * HALF), BF16),
        pltpu.VMEM((BLOCK * SIDE, 2 * HALF), BF16),
        pltpu.VMEM((BLOCK * SIDE // 2, HALF), BF16),
        pltpu.SemaphoreType.DMA((13,)),
    ]
    spots = chunk * SIDE
    return pl.pallas_call(
        functools.partial(main_step, plan, k, len(waits)),
        out_shape=outs,
        in_specs=specs,
        out_specs=[VMEM] * len(outs),
        scratch_shapes=scratch,
        input_output_aliases=alias,
        compiler_params=params(58),
        cost_estimate=cost(60 * 65536 * spots, 8 * MIB, 2 * 256 * spots),
        name=f"main_{k}",
    )(*args)


def local(
    image_latents,
    image_heights,
    code_index,
    kernel_three,
    bias_three,
    weight_mix,
    bias_mix,
    weight_project,
    bias_project,
    codebook,
    weight_decode,
    bias_decode,
    out_grad,
):
    images = image_latents.shape[0]
    plan = Plan(images)
    n = len(plan.chunks)
    tile = (SIDE, HALF)
    where = lax.axis_index("mp").astype(jnp.int32)
    place = where.reshape(1)

    packed = pl.pallas_call(
        functools.partial(pack_latents, plan),
        out_shape=[
            shape((meta_size(plan),), jnp.int32),
            shape((LEAD + plan.total,) + tile, BF16),
        ]
        + [shape((c,) + tile, BF16) for c in plan.chunks],
        in_specs=[SMEM, SMEM, ANY],
        out_specs=[SMEM, ANY] + [ANY] * n,
        scratch_shapes=[
            pltpu.VMEM((images, SIDE) + tile, BF16),
            pltpu.VMEM((plan.packed + SIDE,) + tile, BF16),
            pltpu.SemaphoreType.DMA((8,)),
            pltpu.SemaphoreType.DMA((n + 1,)),
        ],
        compiler_params=params(40),
        cost_estimate=cost(0, 12 * MIB),
        name="pack_latents",
    )(image_heights, place, image_latents)
    meta, x_own, x_send = packed[0], packed[1], packed[2:]

    packed = pl.pallas_call(
        functools.partial(pack_code_grads, plan),
        out_shape=[shape((plan.total // 2,) + tile, F32), shape((2 * HALF + HALF // 2 + SIDE, HALF), BF16)]
        + [shape((c // 2,) + tile, BF16) for c in plan.chunks],
        in_specs=[SMEM, ANY] + [VMEM] * 5,
        out_specs=[VMEM] * (n + 2),
        scratch_shapes=[
            pltpu.VMEM((images, SIDE) + tile, BF16),
            pltpu.VMEM((plan.packed + SIDE,) + tile, BF16),
            pltpu.SemaphoreType.DMA((8,)),
        ],
        compiler_params=params(40),
        cost_estimate=cost(2 * 2 * plan.total * SIDE * 256 * 128, 10 * MIB),
        name="pack_code_grads",
    )(meta, out_grad, weight_decode, weight_mix, weight_project.T, bias_three.reshape(1, HALF), bias_mix.reshape(1, HALF))
    q_own, small, q_send = packed[0], packed[1], packed[2:]

    book_rows, embed = codebook.shape
    codebook_t = codebook.T
    far_kernel = trade(kernel_three)
    far_small = trade(small)
    usual = plan.usual
    x_far, q_far = [], []
    for k in range(usual):
        x_far.append(trade(x_send[k]))
        q_far.append(trade(q_send[k]))

    weights = pl.pallas_call(
        prepare_weights,
        out_shape=[
            shape((18 * HALF, 2 * HALF), BF16),
            shape((18 * HALF, 2 * HALF), BF16),
            shape((2 * HALF, 2 * HALF), BF16),
            shape((2, 2 * HALF, HALF), BF16),
            shape((SIDE, 2 * HALF), F32),
            shape((HALF, book_rows), BF16),
        ],
        in_specs=[SMEM] + [VMEM] * 6,
        out_specs=[VMEM] * 6,
        compiler_params=params(16),
        cost_estimate=cost(0, 5 * MIB),
        name="prepare_weights",
    )(place, kernel_three, far_kernel, small, far_small, bias_project.reshape(1, -1), codebook_t)

    groups = 8
    group = images // groups
    codes = code_index.reshape(images, SIDE * SIDE)
    whole = lambda dims: pl.BlockSpec(dims, lambda g: (0,) * len(dims))
    four = pl.BlockSpec((group, SIDE) + tile, lambda g: (g, 0, 0, 0))
    row = pl.BlockSpec((group, SIDE * SIDE), lambda g: (g, 0))
    decode_acc = pl.pallas_call(
        functools.partial(sum_codes, plan, groups),
        grid=(groups,),
        out_shape=shape((embed + 8, HALF), F32),
        in_specs=[SMEM, row, four, whole((embed, book_rows))],
        out_specs=whole((embed + 8, HALF)),
        scratch_shapes=[
            pltpu.VMEM((book_rows, group * SIDE * SIDE), BF16),
            pltpu.VMEM((group * SIDE * SIDE, HALF), BF16),
            pltpu.VMEM((book_rows, HALF), F32),
        ],
        compiler_params=params(32),
        cost_estimate=cost(images * 256 * 512 * 256, 5 * MIB),
        name="sum_codes",
    )(image_heights, codes, out_grad, codebook_t)

    def decode(after):
        return pl.pallas_call(
            functools.partial(decode_images, plan, groups),
            grid=(groups,),
            out_shape=shape((images, SIDE) + tile, BF16),
            in_specs=[SMEM, row, whole((embed, book_rows)), whole((embed, HALF)), whole((1, HALF)), ANY],
            out_specs=four,
            scratch_shapes=[pltpu.VMEM((HALF, book_rows), BF16)],
            compiler_params=params(32),
            cost_estimate=cost(images * 256 * 512 * 256, 5 * MIB),
            name="decode_images",
        )(image_heights, codes, codebook_t, weight_decode, bias_decode.reshape(1, HALF), after)

    streams = (x_own, x_far, q_own, q_far, codes)
    state = None
    win_own, win_far = [], []
    for k in range(usual):
        outs = run_main(plan, k, meta, image_heights, streams, weights, state, win_far[: k - 1] if k > 1 else ())
        win_own.append(outs[0])
        win_far.append(trade(outs[1]))
        state = outs[2:]
    carry, accs = state[:2], state[2:]

    def restore(own, far):
        count = len(own)
        return pl.pallas_call(
            functools.partial(restore_rows, plan, count),
            out_shape=shape((images, SIDE) + tile, BF16),
            in_specs=[SMEM, SMEM] + [ANY] * (2 * count),
            out_specs=VMEM,
            scratch_shapes=[
                pltpu.VMEM((plan.total + LEAD + SIDE,) + tile, BF16),
                pltpu.VMEM((plan.total + LEAD + SIDE,) + tile, BF16),
                pltpu.SemaphoreType.DMA((2, count)),
            ],
            compiler_params=params(40),
            cost_estimate=cost(0, 10 * MIB),
            name="restore_rows",
        )(meta, image_heights, *own, *far)

    latents_grad = restore(win_own, win_far)

    devices = lax.axis_size("dp")
    layout = Layout(devices, book_rows, embed)
    half, piece, chips = layout.half, layout.piece, devices // 2
    core = lax.rem(lax.axis_index("dp").astype(jnp.int32), 2)
    spot = jnp.stack([where, core])
    keep_own, keep_far, send = pl.pallas_call(
        functools.partial(gather_grads, plan, layout),
        out_shape=[shape((half, HALF), F32)] * 2 + [shape((2, half, HALF), BF16)],
        in_specs=[SMEM, SMEM] + [VMEM] * 6 + [ANY],
        out_specs=[VMEM] * 3,
        scratch_shapes=[pltpu.VMEM((layout.rows, HALF), F32)] * 2,
        compiler_params=params(40),
        cost_estimate=cost(0, 8 * MIB),
        name="gather_grads",
    )(spot, meta, *accs, decode_acc, win_far[usual - 2])
    decoded = decode(send)
    across = [(i, i ^ 1) for i in range(devices)]

    def step(body, out, name, *args, waits=()):
        specs = [VMEM] * len(args) + [ANY] * len(waits)
        args = (*args, *waits)
        return pl.pallas_call(
            body,
            out_shape=out,
            in_specs=specs,
            out_specs=VMEM,
            compiler_params=params(24),
            cost_estimate=cost(0, 2 * MIB),
            name=name,
        )(*args)

    came = lax.ppermute(send, "dp", across)
    far = step(add_far, shape((half, HALF), BF16), "add_far", keep_far, came)
    came_far = trade(far)
    mine = step(add_own, shape((chips, piece, HALF), BF16), "add_own", keep_own, came, came_far)
    groups = [[i for i in range(devices) if i % 2 == c] for c in range(2)]
    mine = lax.all_to_all(mine, "dp", 0, 0, axis_index_groups=groups, tiled=True)
    mine = step(add_pieces, shape((chips, piece, HALF), BF16), "add_pieces", mine, waits=win_far[usual - 1 :])
    mine = lax.all_to_all(mine, "dp", 0, 0, axis_index_groups=groups, tiled=True)
    mine = mine.reshape(half, HALF)
    theirs = lax.ppermute(mine, "dp", across)

    grads_out = [
        shape((9, 2 * HALF, HALF), F32),
        shape((1, HALF), F32),
        shape((HALF, 2 * HALF), F32),
        shape((1, HALF), F32),
        shape((embed, HALF), F32),
        shape((1, embed), F32),
        shape((embed, book_rows), F32),
        shape((embed, HALF), F32),
        shape((1, HALF), F32),
    ]
    whole = pltpu.VMEM((layout.rows, HALF), F32)

    def usual_end(latents_grad):
        grads = pl.pallas_call(
            functools.partial(write_grads, layout),
            out_shape=grads_out,
            in_specs=[SMEM, VMEM, VMEM],
            out_specs=[VMEM] * 9,
            scratch_shapes=[whole],
            compiler_params=params(24),
            cost_estimate=cost(0, 4 * MIB),
            name="write_grads",
        )(spot, mine, theirs)
        return (latents_grad, *grads)

    def longer_end(latents_grad):
        last_x, last_q = trade(x_send[usual]), trade(q_send[usual])
        streams = (x_own, x_far + [last_x], q_own, q_far + [last_q], codes)
        outs = run_main(plan, usual, meta, image_heights, streams, weights, carry)
        latents_grad = restore(win_own + [outs[0]], win_far + [trade(outs[1])])
        own, far = pl.pallas_call(
            functools.partial(gather_plain, layout),
            out_shape=[shape((layout.rows, HALF), F32)] * 2,
            in_specs=[SMEM] + [VMEM] * 5,
            out_specs=[VMEM] * 2,
            compiler_params=params(40),
            name="gather_plain",
        )(spot, *outs[4:])
        extra = lax.psum(own + trade(far), "dp")
        first, second = jnp.where(core == 0, mine, theirs), jnp.where(core == 0, theirs, mine)
        grads = pl.pallas_call(
            functools.partial(split_again, layout),
            out_shape=grads_out,
            in_specs=[VMEM, VMEM],
            out_specs=[VMEM] * 9,
            scratch_shapes=[whole],
            compiler_params=params(24),
            name="split_again",
        )(jnp.concatenate([first, second]), extra)
        return (latents_grad, *grads)

    flag = layout.bias + 3
    holder = flag // half
    flags = jnp.where(core == holder, mine[flag - holder * half, 0], theirs[flag - holder * half, 0])
    ends = lax.cond(flags.astype(F32) > 0.5, longer_end, usual_end, latents_grad)
    latents_grad, kernel_grad, first_bias, mix_grad, mix_bias, project_grad, project_bias, book, decode, decode_bias = ends
    return (
        decoded,
        latents_grad,
        kernel_grad,
        first_bias.reshape(HALF),
        mix_grad,
        mix_bias.reshape(HALF),
        project_grad.T,
        project_bias.reshape(embed),
        book.T,
        decode,
        decode_bias.reshape(HALF),
    )


def solution(mesh):
    tile = P("dp", None, None, "mp")
    placed = (
        tile,
        P("dp"),
        P("dp", None, None),
        P(None, None, "mp"),
        P("mp"),
        P("mp", None),
        P("mp"),
        P("mp", None),
        P(),
        P(),
        P(None, "mp"),
        P("mp"),
        tile,
    )
    outs = (
        tile,
        tile,
        P(None, None, "mp"),
        P("mp"),
        P("mp", None),
        P("mp"),
        P("mp", None),
        P(),
        P(),
        P(None, "mp"),
        P("mp"),
    )
    return jax.shard_map(local, mesh=mesh, in_specs=placed, out_specs=outs, check_vma=False)
```

```python
import functools

import jax
import jax.numpy as jnp
from jax import lax
from jax.experimental import pallas as pl
from jax.experimental.pallas import tpu as pltpu
from jax.sharding import PartitionSpec as P

SIDE = 16
HALF = 128
LEAD = 16
BLOCK = 32
TILE = 32
MARK = 1e9
GELU_SCALE = 0.7978845608028654
GELU_CUBE = 0.044715
COMMIT = 0.25
F32 = jnp.float32
BF16 = jnp.bfloat16
ANY = pl.BlockSpec(memory_space=pl.ANY)
SMEM = pl.BlockSpec(memory_space=pltpu.SMEM)
HBM = pl.BlockSpec(memory_space=pltpu.HBM)
VMEM = pl.BlockSpec(memory_space=pltpu.VMEM)
MIB = 1 << 20

NT = (((1,), (1,)), ((), ()))
TN = (((0,), (0,)), ((), ()))
NN = (((1,), (0,)), ((), ()))


def dot(a, b, dims=NN):
    return lax.dot_general(a, b, dims, preferred_element_type=F32)


def one_hot_columns(codes, code_of):
    return jnp.where(code_of == codes.astype(jnp.int16), jnp.bfloat16(1), jnp.bfloat16(0))


def numbers(count, width):
    return lax.broadcasted_iota(jnp.int32, (count, width), 0).astype(jnp.int16)


def shape(dims, kind):
    return jax.ShapeDtypeStruct(dims, kind)


def params(mib):
    return pltpu.CompilerParams(vmem_limit_bytes=mib * MIB)


def cost(flops, moved, slow=0):
    return pl.CostEstimate(flops=flops, bytes_accessed=moved, transcendentals=slow)


class Plan:
    def __init__(self, images):
        self.images = images
        longest = images * SIDE // 2 + SIDE // 2
        part = images // 4
        self.chunks = [5 * part, 9 * part, 10 * part]
        self.usual = len(self.chunks)
        rest = longest - sum(self.chunks)
        self.chunks.append(rest)
        self.starts = [sum(self.chunks[:k]) for k in range(len(self.chunks))]
        self.total = sum(self.chunks)
        self.packed = -(-(LEAD + longest + self.total + LEAD) // SIDE) * SIDE
        self.rows = []
        for c in self.chunks:
            most = 1 + c + 15 + c // 4 + 1
            self.rows.append(-(-most // BLOCK) * BLOCK)
        self.covered = sum(self.chunks[: self.usual])


def meta_size(plan):
    return plan.images + len(plan.chunks) + 1 + 5


def plan_rows(plan, heights, place, meta):
    images = plan.images
    base = images + len(plan.chunks) + 1

    def total_of(b, acc):
        return acc + heights[b]

    total = lax.fori_loop(0, images, total_of, jnp.int32(0))

    def split_of(b, state):
        acc, best, split, cut = state
        acc = acc + heights[b]
        worst = jnp.maximum(acc, total - acc)
        better = worst < best
        return (acc, jnp.where(better, worst, best), jnp.where(better, b + 1, split), jnp.where(better, acc, cut))

    _, _, split, cut = lax.fori_loop(0, images, split_of, (jnp.int32(0), jnp.int32(1 << 20), jnp.int32(0), jnp.int32(0)))
    mine = place[0]
    own_first = jnp.where(mine == 0, 0, split)
    own_last = jnp.where(mine == 0, split, images)
    own_row = jnp.where(mine == 0, 0, cut)
    send_row = jnp.where(mine == 0, cut, 0)
    for k in range(len(plan.chunks) + 1):
        meta[images + k] = own_first
    ends = [plan.starts[k] + plan.chunks[k] for k in range(len(plan.chunks))]

    def place_of(b, acc):
        meta[b] = acc - own_row
        acc = acc + heights[b]
        end = acc - own_row
        inside = jnp.logical_and(b >= own_first, b < own_last)
        step = jnp.int32(0)
        for k in range(len(plan.chunks) - 1):
            step = step + (end > ends[k]).astype(jnp.int32)

        @pl.when(inside)
        def _():
            meta[images + 1 + step] = b + 1

        return acc

    lax.fori_loop(0, images, place_of, jnp.int32(0))
    for k in range(len(plan.chunks)):
        meta[images + k + 1] = jnp.maximum(meta[images + k + 1], meta[images + k])
    meta[base] = own_row
    meta[base + 1] = send_row
    meta[base + 2] = own_first
    meta[base + 3] = own_last
    meta[base + 4] = jnp.maximum(cut, total - cut)


def pack_rows(plan, meta, source, packed, piece, count):
    base = plan.images + len(plan.chunks) + 1

    def one(i, carry):
        b = piece * count + i
        row = meta[b] + meta[base] + LEAD
        packed[pl.ds(row, SIDE)] = source[b]
        return carry

    lax.fori_loop(0, count, one, 0)


def pack_latents(plan, heights, place, x_hbm, meta, own, *rest):
    n = len(plan.chunks)
    sends, (x_in, packed, sem_in, sem_out) = rest[:n], rest[n:]
    pieces = 8
    count = plan.images // pieces
    fetch = []
    for p in range(pieces):
        part = pl.ds(p * count, count)
        fetch.append(pltpu.make_async_copy(x_hbm.at[part], x_in.at[part], sem_in.at[p]))
        fetch[-1].start()
    plan_rows(plan, heights, place, meta)
    base = plan.images + n + 1
    for p in range(pieces):
        fetch[p].wait()
        pack_rows(plan, meta, x_in, packed, p, count)
    copies = []
    for k in range(n):
        part = pl.ds(LEAD + meta[base + 1] + plan.starts[k], plan.chunks[k])
        copies.append(pltpu.make_async_copy(packed.at[part], sends[k], sem_out.at[k]))
        copies[-1].start()
    copies.append(pltpu.make_async_copy(packed.at[pl.ds(meta[base], LEAD + plan.total)], own, sem_out.at[n]))
    copies[-1].start()
    for copy in copies:
        copy.wait()


def pack_code_grads(plan, meta, og_hbm, *rest):
    n = len(plan.chunks)
    sources, (own, small), rest = rest[:5], rest[5:7], rest[7:]
    sends, rest = rest[:n], rest[n:]
    og_in, packed, sem_in, sem_small = rest[:4]
    held = rest[4:]
    small_fetch = []
    for i in range(5):
        small_fetch.append(pltpu.make_async_copy(sources[i], held[i], sem_small.at[i]))
        small_fetch[-1].start()
    decode_w, weight_mix, project_t, bias_first, bias_mix = held
    pieces = 8
    count = plan.images // pieces
    fetch = []
    for p in range(pieces):
        part = pl.ds(p * count, count)
        fetch.append(pltpu.make_async_copy(og_hbm.at[part], og_in.at[part], sem_in.at[p]))
        fetch[-1].start()
    base = plan.images + n + 1

    def clear(i, carry):
        packed[pl.ds(i * SIDE, SIDE)] = jnp.zeros((SIDE, SIDE, HALF), BF16)
        return carry

    lax.fori_loop(0, packed.shape[0] // SIDE, clear, 0)
    for copy in small_fetch:
        copy.wait()
    side = HALF // 2
    small[0:HALF] = weight_mix[:, :HALF]
    small[HALF : 2 * HALF] = weight_mix[:, HALF:]
    small[2 * HALF : 2 * HALF + side] = project_t[...]
    which = lax.broadcasted_iota(jnp.int32, (SIDE, HALF), 0)
    first, second = bias_first[...].astype(F32), bias_mix[...].astype(F32)
    first = jnp.where(which == 0, first, jnp.where(which == 1, second, 0.0))
    small[2 * HALF + side : 2 * HALF + side + SIDE] = first.astype(BF16)
    w = decode_w[...]
    blank = jnp.zeros_like(w)
    upper = jnp.concatenate([w, blank], axis=0)
    lower = jnp.concatenate([blank, w], axis=0)
    for p in range(pieces):
        fetch[p].wait()
        pack_rows(plan, meta, og_in, packed, p, count)
    for k in range(n):
        half = plan.chunks[k] // 2
        for which in range(2):
            row = LEAD + meta[base + 1 - which] + plan.starts[k]
            a = packed[pl.ds(row, half)].reshape(half * SIDE, HALF)
            b = packed[pl.ds(row + half, half)].reshape(half * SIDE, HALF)
            both = dot(a, upper, NT) + dot(b, lower, NT)
            both = both.reshape(half, SIDE, HALF)
            if which == 0:
                sends[k][...] = both.astype(BF16)
            else:
                own[pl.ds(plan.starts[k] // 2, half)] = both


def prepare_weights(place, kernel, far_kernel, small, far_small, bias_code, codebook_t, forward, backward, mix, project, bias, book):
    first = pl.multiple_of(place[0] * HALF, HALF)
    order = (first, HALF - first)
    for tap in range(9):
        for d, source in enumerate((kernel, far_kernel)):
            for c in range(2):
                tile = source[tap, pl.ds(order[c], HALF), :]
                row = tap * 2 * HALF
                forward[row + c * HALF : row + (c + 1) * HALF, d * HALF : (d + 1) * HALF] = tile
                backward[row + d * HALF : row + (d + 1) * HALF, c * HALF : (c + 1) * HALF] = tile.T
    blank = jnp.zeros((HALF, HALF // 2), BF16)
    for d, source in enumerate((small, far_small)):
        rows = pl.ds(d * HALF, HALF)
        for c in range(2):
            mix[rows, c * HALF : (c + 1) * HALF] = source[pl.ds(order[c], HALF), :]
        part = source[2 * HALF : 2 * HALF + HALF // 2, :].T
        project[0, rows, :] = jnp.concatenate([part, blank], axis=1)
        project[1, rows, :] = jnp.concatenate([blank, part], axis=1)
        bias[0:8, d * HALF : (d + 1) * HALF] = source[2 * HALF + HALF // 2 : 2 * HALF + HALF // 2 + SIDE, :].astype(F32)[0:8]
    code = bias_code[...].astype(F32)
    code = jnp.concatenate([code, code], axis=1)
    bias[8:16, :] = jnp.broadcast_to(jnp.concatenate([code, code], axis=1), (8, 2 * HALF))
    book[...] = jnp.concatenate([codebook_t[...], codebook_t[...]], axis=0)


def sum_codes(plan, steps, heights, codes, og, codebook_t, grads, hot, cots, sums):
    step = pl.program_id(0)
    group = plan.images // steps

    @pl.when(step == 0)
    def _():
        sums[...] = jnp.zeros_like(sums)

    spots = SIDE * SIDE
    code_of = numbers(codebook_t.shape[1], spots)
    spot = lax.broadcasted_iota(jnp.int32, (spots, 1), 0)
    for i in range(group):
        live = heights[step * group + i] * SIDE
        hot[:, i * spots : (i + 1) * spots] = one_hot_columns(codes[i : i + 1, :], code_of)
        cot = og[i].reshape(spots, HALF).astype(F32)
        cots[i * spots : (i + 1) * spots] = jnp.where(spot < live, cot, 0.0).astype(BF16)
    sums[...] += dot(hot[...], cots[...])

    @pl.when(step == steps - 1)
    def _():
        total = sums[...]
        book = codebook_t[...].astype(F32)
        w = lax.dot_general(book, total, NN, precision=lax.Precision.HIGHEST, preferred_element_type=F32)
        bias = jnp.sum(total, axis=0, keepdims=True)
        embed = w.shape[0]
        grads[0:embed] = w
        grads[embed : embed + 8] = jnp.broadcast_to(bias, (8, HALF))


def decode_images(plan, steps, heights, codes, codebook_t, decode_w, decode_b, _, decoded, table):
    step = pl.program_id(0)
    group = plan.images // steps

    @pl.when(step == 0)
    def _():
        full = dot(codebook_t[...], decode_w[...], TN) + decode_b[...].astype(F32)
        table[...] = full.T.astype(BF16)

    spots = SIDE * SIDE
    code_of = numbers(codebook_t.shape[1], spots)
    spot = lax.broadcasted_iota(jnp.int32, (spots, 1), 0)
    for i in range(group):
        live = heights[step * group + i] * SIDE
        out = dot(table[...], one_hot_columns(codes[i : i + 1, :], code_of)).T
        decoded[i] = jnp.where(spot < live, out, 0.0).astype(BF16).reshape(SIDE, SIDE, HALF)


def gelu_parts(v):
    square = v * v
    t = jnp.tanh(v * (GELU_SCALE + (GELU_SCALE * GELU_CUBE) * square))
    half = 0.5 + 0.5 * t
    slope = half + (0.5 * v) * (1.0 - t * t) * (GELU_SCALE + (3.0 * GELU_SCALE * GELU_CUBE) * square)
    return v * half, slope


def main_step(plan, layout, k, waits, *refs):
    first_step = k == 0
    fresh = k in (0, plan.usual)
    final = k == plan.usual - 1
    refs = list(refs[waits:])

    def take(count):
        got = refs[:count]
        del refs[:count]
        return got

    if final:
        place, decode_acc = take(2)
    meta, heights, x_own, x_far, q_own, q_far, codes = take(7)
    kernel, kernel_t, mix, project, bias, book = take(6)
    if not first_step:
        x_past, q_past, carry_own, carry_far = take(4)
    if not fresh:
        past_accs = take(5)
    win_own, win_far, next_own, next_far = take(4)
    if final:
        laid_out = take(3)
    kernel_acc, mix_acc, project_acc, book_acc, bias_acc = take(5)
    if final:
        laid_out += take(2)
    xo, xf, qo, qf, qd, xc_o, xc_f, qc, code_rows, act3, slope_x, grad3, block_g, lg_o, lg_f, out_o, out_f = take(17)
    second_s, slope_s, low_s, mixed_s, code_s, hot_s, found_s, diff_s, sems = refs

    chunk, start = plan.chunks[k], plan.starts[k]
    images, rows = plan.images, plan.rows[k]
    half = chunk // 2
    spots = BLOCK * SIDE
    low = meta[images + k]
    high = meta[images + k + 1]

    copies = [
        (x_own.at[pl.ds(start, LEAD + chunk)], xo.at[pl.ds(0, LEAD + chunk)]),
        (x_far, xf.at[pl.ds(LEAD, chunk)]),
        (q_own.at[pl.ds(start // 2, half)], qo.at[pl.ds(LEAD, half)]),
        (q_far, qf.at[pl.ds(LEAD, half)]),
    ]
    if not first_step:
        past = plan.chunks[k - 1]
        copies += [
            (x_past.at[pl.ds(past - LEAD, LEAD)], xf.at[pl.ds(0, LEAD)]),
            (q_own.at[pl.ds(start // 2 - LEAD, LEAD)], qo.at[pl.ds(0, LEAD)]),
            (q_past.at[pl.ds(past // 2 - LEAD, LEAD)], qf.at[pl.ds(0, LEAD)]),
        ]
    accs = (mix_acc, project_acc, book_acc, bias_acc, kernel_acc)
    early = len(copies)
    if not fresh:
        copies += list(zip(past_accs[1:] + past_accs[:1], accs))
    started = []
    for i, (source, target) in enumerate(copies):
        started.append(pltpu.make_async_copy(source, target, sems.at[i]))
        started[-1].start()
    started, later = started[:early], started[early:]

    if fresh:
        for acc in accs:
            acc[...] = jnp.zeros(acc.shape, F32)
    if first_step:
        out_o[0:LEAD] = jnp.zeros((LEAD, SIDE, HALF), BF16)
        out_f[0:LEAD] = jnp.zeros((LEAD, SIDE, HALF), BF16)
    else:
        out_o[0:LEAD] = carry_own[...]
        out_f[0:LEAD] = carry_far[...]

    blank = jnp.zeros((SIDE, SIDE, HALF), BF16)
    no_row = jnp.full((SIDE, SIDE, HALF), MARK, F32)
    code_rows[...] = jnp.full(code_rows.shape, -1, jnp.int32)
    for r in range(0, rows, SIDE):
        part = pl.ds(r, SIDE)
        xc_o[part] = blank
        xc_f[part] = blank
        qc[part] = no_row
    for copy in started:
        copy.wait()

    lane3 = lax.broadcasted_iota(jnp.int32, (1, SIDE, HALF), 2) < HALF // 2

    def spread(r0, count):
        both = (qo[pl.ds(r0, count)] + qf[pl.ds(r0, count)].astype(F32)).reshape(count * SIDE, HALF)
        turned = pltpu.roll(both, HALF // 2, 1).reshape(count, SIDE, HALF)
        both = both.reshape(count, SIDE, HALF)
        return jnp.where(lane3, both, turned), jnp.where(lane3, turned, both)

    upper, lower = spread(LEAD, half)
    qd[pl.ds(LEAD, half)] = upper
    qd[pl.ds(LEAD + half, half)] = lower
    if not first_step:
        _, lower = spread(0, LEAD)
        qd[0:LEAD] = lower

    spot = lax.broadcasted_iota(jnp.int32, (1, SIDE * SIDE), 1)
    lane128 = lax.broadcasted_iota(jnp.int32, (1, HALF), 1)
    per_row = HALF // SIDE

    def put(b, dst):
        src = meta[b] - start + LEAD
        xc_o[pl.ds(dst, SIDE)] = xo[pl.ds(src, SIDE)]
        xc_f[pl.ds(dst, SIDE)] = xf[pl.ds(src, SIDE)]
        qc[pl.ds(dst, SIDE)] = qd[pl.ds(src, SIDE)]
        end = dst + heights[b]
        xc_o[pl.ds(end, SIDE)] = blank
        xc_f[pl.ds(end, SIDE)] = blank
        qc[pl.ds(end, SIDE)] = no_row
        row = jnp.where(spot < heights[b] * SIDE, codes[pl.ds(b, 1), :], -1)
        turn = lax.rem(dst, per_row) * SIDE
        upper = pltpu.roll(row[:, :HALF], turn, 1)
        lower = pltpu.roll(row[:, HALF:], turn, 1)
        inside = lane128 >= turn
        pieces = (jnp.where(inside, upper, -1), jnp.where(inside, lower, upper), jnp.where(inside, -1, lower))
        for i, piece in enumerate(pieces):
            target = pl.ds(dst // per_row + i, 1)
            code_rows[target, :] = jnp.where(piece < 0, code_rows[target, :], piece)
        return end + 1

    used = lax.fori_loop(low, high, put, jnp.int32(1))
    blocks = jnp.where(high > low, (used + (BLOCK - 1)) // BLOCK, 0)

    column = lax.rem(lax.broadcasted_iota(jnp.int32, (TILE, 1), 0), SIDE)
    not_first = column != 0
    not_last = column != SIDE - 1

    def shifted(value):
        back = jnp.where(not_first, pltpu.roll(value, 1, 0), 0.0)
        ahead = jnp.where(not_last, pltpu.roll(value, TILE - 1, 0), 0.0)
        return back.astype(BF16), ahead.astype(BF16)

    edge = jnp.zeros((SIDE, 3 * 2 * HALF), BF16)
    act3[0:SIDE] = edge
    grad3[0:SIDE] = edge
    beyond = pl.multiple_of((blocks * BLOCK + 1) * SIDE, SIDE)
    act3[pl.ds(beyond, SIDE)] = edge
    grad3[pl.ds(beyond, SIDE)] = edge

    tiles = range(0, spots, TILE)

    def read_x(r0, t):
        part = pl.ds(r0 + t // SIDE, TILE // SIDE)
        o = xc_o[part].reshape(TILE, HALF)
        f = xc_f[part].reshape(TILE, HALF)
        return jnp.concatenate([o, f], axis=1).astype(F32)

    def at(row, count=BLOCK):
        return pl.ds(pl.multiple_of(row * SIDE, SIDE), count * SIDE)

    def tile_at(row, t):
        return pl.ds(pl.multiple_of(row * SIDE, SIDE) + t, TILE)

    def activate(j, carry):
        r0 = j * BLOCK
        for t in tiles:
            value, slope = gelu_parts(read_x(r0, t))
            slope_x[tile_at(r0, t), :] = slope
            back, ahead = shifted(value)
            act3[tile_at(r0 + 1, t), 0 : 2 * HALF] = back
            act3[tile_at(r0 + 1, t), 2 * HALF : 4 * HALF] = value.astype(BF16)
            act3[tile_at(r0 + 1, t), 4 * HALF : 6 * HALF] = ahead
        return carry

    lax.fori_loop(0, blocks, activate, 0)
    for copy in later[:4]:
        copy.wait()

    bias_first = bias[0:1, :]
    bias_mix = bias[1:2, :]
    bias_code = bias[8:9, 0:HALF]
    lane = lax.broadcasted_iota(jnp.int32, (1, HALF), 1) < HALF // 2
    hb = BLOCK // 2
    hs = hb * SIDE

    def add_rows(total, value):
        value = value.astype(F32)
        for i in range(0, value.shape[0], 8):
            part = value[i : i + 8]
            total = part if total is None else total + part
        return total

    half_tiles = range(0, hs, TILE)
    code_of = numbers(book_acc.shape[0], HALF)
    halves = (0, hs)

    def middle(j, carry):
        r0 = j * BLOCK
        for i in range(BLOCK // per_row):
            row = code_rows[pl.ds(j * (BLOCK // per_row) + i, 1), :]
            hot_s[:, i * HALF : (i + 1) * HALF] = one_hot_columns(row, code_of)
        for h in halves:
            found_s[h : h + hs] = dot(book[...], hot_s[:, h : h + hs]).astype(BF16).T
        pre = []
        for h in halves:
            window = jnp.concatenate([act3[at(r0 + i + h // SIDE, hb), :] for i in range(3)], axis=1)
            pre.append(dot(window, kernel[...]))
        for h, part in zip(halves, pre):
            for t in half_tiles:
                value, slope = gelu_parts(part[t : t + TILE] + bias_first)
                second_s[h + t : h + t + TILE] = value.astype(BF16)
                slope_s[h + t : h + t + TILE] = slope
        mixed = [dot(second_s[h : h + hs], mix[...]) for h in halves]
        for h, part in zip(halves, mixed):
            for t in half_tiles:
                low_s[h + t : h + t + TILE] = (read_x(r0, h + t) + part[t : t + TILE] + bias_mix).astype(BF16)
        latents = [dot(low_s[h : h + hs], project[i]) for i, h in enumerate(halves)]
        total = None
        for t in half_tiles:
            first = pl.ds(r0 + t // SIDE, TILE // SIDE)
            other = pl.ds(r0 + hb + t // SIDE, TILE // SIDE)
            ch = jnp.where(lane, found_s[t : t + TILE].astype(F32), found_s[hs + t : hs + t + TILE].astype(F32))
            q = jnp.where(lane3, qc[first], qc[other]).reshape(TILE, HALF)
            live = q < 0.5 * MARK
            latent = latents[0][t : t + TILE] + latents[1][t : t + TILE] + bias_code
            diff = jnp.where(live, latent - ch, 0.0)
            code_grad = jnp.where(live, q + (2.0 * COMMIT) * diff, 0.0).astype(BF16)
            code_s[t : t + TILE] = code_grad
            total = add_rows(total, code_grad)
            big = diff.astype(BF16).astype(F32)
            small = diff - big
            turned = pltpu.roll(small, HALF // 2, 1)
            diff_s[t : t + TILE] = jnp.where(lane, big, turned).astype(BF16)
            turned = pltpu.roll(big, HALF // 2, 1)
            diff_s[hs + t : hs + t + TILE] = jnp.where(lane, turned, small).astype(BF16)
        bias_acc[16:24, 0:HALF] += total
        total = None
        blocks_g = [dot(code_s[...], project[i], NT) for i in range(2)]
        for h, part in zip(halves, blocks_g):
            for t in half_tiles:
                block_g[tile_at(r0, h + t), :] = part[t : t + TILE]
                mixed_grad = part[t : t + TILE].astype(BF16)
                mixed_s[h + t : h + t + TILE] = mixed_grad
                total = add_rows(total, mixed_grad)
        bias_acc[8:16] += total
        second_grad = [dot(mixed_s[h : h + hs], mix[...], NT) for h in halves]
        total = None
        for h, part in zip(halves, second_grad):
            for t in half_tiles:
                first_grad = slope_s[h + t : h + t + TILE] * part[t : t + TILE]
                back, ahead = shifted(first_grad)
                first_low = first_grad.astype(BF16)
                grad3[tile_at(r0 + 1, h + t), 0 : 2 * HALF] = ahead
                grad3[tile_at(r0 + 1, h + t), 2 * HALF : 4 * HALF] = first_low
                grad3[tile_at(r0 + 1, h + t), 4 * HALF : 6 * HALF] = back
                total = add_rows(total, first_low)
        bias_acc[0:8] += total
        book_acc[...] += dot(hot_s[...], diff_s[...])
        mix_acc[...] += dot(second_s[...], mixed_s[...], TN)
        project_acc[...] += jnp.where(lane, dot(low_s[0:hs], code_s[...], TN), dot(low_s[hs:], code_s[...], TN))
        return carry

    lax.fori_loop(0, blocks, middle, 0)
    for copy in later[4:]:
        copy.wait()

    def finish(j, carry):
        r0 = j * BLOCK
        active = act3[at(r0 + 1), 2 * HALF : 4 * HALF].T
        for i in range(3):
            kernel_acc[:, i * 6 * HALF : (i + 1) * 6 * HALF] += dot(active, grad3[at(r0 + 2 - i), :])
        grads = []
        for h in halves:
            window = jnp.concatenate([grad3[at(r0 + 2 - i + h // SIDE, hb), :] for i in range(3)], axis=1)
            grads.append(dot(window, kernel_t[...]))
        for h, grad in zip(halves, grads):
            for t in half_tiles:
                here = tile_at(r0, h + t)
                out = (block_g[here, :] + slope_x[here, :] * grad[t : t + TILE]).astype(BF16)
                part = pl.ds(r0 + (h + t) // SIDE, TILE // SIDE)
                lg_o[part] = out[:, :HALF].reshape(TILE // SIDE, SIDE, HALF)
                lg_f[part] = out[:, HALF:].reshape(TILE // SIDE, SIDE, HALF)
        return carry

    lax.fori_loop(0, blocks, finish, 0)

    def collect(b, src):
        dst = meta[b] - start + LEAD
        out_o[pl.ds(dst, SIDE)] = lg_o[pl.ds(src, SIDE)]
        out_f[pl.ds(dst, SIDE)] = lg_f[pl.ds(src, SIDE)]
        return src + heights[b] + 1

    lax.fori_loop(low, high, collect, jnp.int32(1))
    size = win_own.shape[0]
    win_own[...] = out_o[0:size]
    win_far[...] = out_f[0:size]
    next_own[...] = out_o[chunk : chunk + LEAD]
    next_far[...] = out_f[chunk : chunk + LEAD]
    if final:
        sums = (kernel_acc, mix_acc, project_acc, book_acc, bias_acc, decode_acc)
        gather_grads(plan, layout, place, meta, sums, *laid_out)


class Layout:
    def __init__(self, devices, book_rows, embed):
        self.mix = 9 * 2 * HALF
        self.project = self.mix + 2 * HALF
        self.book = self.project + HALF // 2
        self.bias = self.book + book_rows // 2
        self.decode = self.bias + 8
        used = self.decode + embed + 8
        self.devices = devices
        self.piece = -(-used // (devices * SIDE)) * SIDE
        self.rows = self.piece * devices
        self.half = self.rows // 2
        self.used = used


def lay_out(layout, swap, kernel_acc, mix_acc, project_acc, book_acc, bias_acc, decode_acc, own, far):
    def lanes(value):
        return value[:, :HALF], value[:, HALF:]

    def order(first, second):
        return jnp.where(swap, second, first), jnp.where(swap, first, second)

    row = 0
    for tap in range(9):
        block = kernel_acc[:, tap * 2 * HALF : (tap + 1) * 2 * HALF]
        mine, theirs = lanes(block)
        a, b = order(mine[:HALF], mine[HALF:])
        own[row : row + HALF] = a
        own[row + HALF : row + 2 * HALF] = b
        a, b = order(theirs[:HALF], theirs[HALF:])
        far[row : row + HALF] = a
        far[row + HALF : row + 2 * HALF] = b
        row += 2 * HALF
    row = layout.mix
    for target, part in ((own, mix_acc[:HALF]), (far, mix_acc[HALF:])):
        a, b = order(*lanes(part))
        target[row : row + HALF] = a
        target[row + HALF : row + 2 * HALF] = b
    row = layout.project
    side = HALF // 2
    for target, part in ((own, project_acc[:HALF]), (far, project_acc[HALF:])):
        part = part + pltpu.roll(part, side, 1)
        target[row : row + side] = part.T[:side]
    row = layout.book
    book = book_acc[...]
    book = -2.0 * (book + pltpu.roll(book, side, 1))
    book = book.T[:side]
    for c in range(book.shape[1] // HALF):
        part = book[:, c * HALF : (c + 1) * HALF]
        own[row + c * side : row + (c + 1) * side] = part
        far[row + c * side : row + (c + 1) * side] = part
    row = layout.bias
    sums = [jnp.sum(bias_acc[8 * i : 8 * i + 8], axis=0, keepdims=True) for i in range(3)]
    code = sums[2][:, :HALF]
    code = code + pltpu.roll(code, side, 1)
    which = lax.broadcasted_iota(jnp.int32, (8, HALF), 0)
    for target, first in ((own, 0), (far, HALF)):
        part = jnp.where(which == 0, sums[0][:, first : first + HALF], sums[1][:, first : first + HALF])
        target[row : row + 8] = jnp.where(which == 2, code, jnp.where(which < 2, part, 0.0))
    row = layout.decode
    rest = layout.rows - row
    own[row:] = jnp.zeros((rest, HALF), F32)
    far[row:] = jnp.zeros((rest, HALF), F32)
    if decode_acc is not None:
        own[row : row + decode_acc.shape[0]] = decode_acc[...]


def gather_plain(layout, place, *refs):
    lay_out(layout, place[0] == 1, *refs[:5], None, *refs[5:])


def gather_grads(plan, layout, place, meta, accs, keep_own, keep_far, send, own, far):
    lay_out(layout, place[0] == 1, *accs, own, far)
    base = plan.images + len(plan.chunks) + 1
    over = (meta[base + 4] > plan.covered).astype(F32)
    which = lax.broadcasted_iota(jnp.int32, (8, HALF), 0)
    row = layout.bias
    own[row : row + 8] = jnp.where(which == 3, over, own[row : row + 8])
    half = layout.half
    mine = pl.ds(pl.multiple_of(place[1] * half, SIDE), half)
    other = pl.ds(pl.multiple_of((1 - place[1]) * half, SIDE), half)
    keep_own[...] = own[mine, :]
    keep_far[...] = far[mine, :]
    send[0] = own[other, :].astype(BF16)
    send[1] = far[other, :].astype(BF16)


def hold(value, _, out):
    pass


def add_far(keep_far, came, out):
    out[...] = (keep_far[...] + came[1].astype(F32)).astype(BF16)


def add_own(keep_own, came, came_far, out):
    total = keep_own[...] + came[0].astype(F32) + came_far[...].astype(F32)
    out[...] = total.astype(BF16).reshape(out.shape)


def add_pieces(pieces, *rest):
    out = rest[-1]
    total = pieces[0].astype(F32)
    for i in range(1, pieces.shape[0]):
        total = total + pieces[i].astype(F32)
    out[...] = jnp.broadcast_to(total.astype(BF16)[None], out.shape)


def write_grads(layout, place, mine, theirs, kernel, first_bias, mix, mix_bias, project, project_bias, book, decode, decode_bias, whole):
    half = layout.half
    whole[pl.ds(pl.multiple_of(place[1] * half, SIDE), half), :] = mine[...].astype(F32)
    whole[pl.ds(pl.multiple_of((1 - place[1]) * half, SIDE), half), :] = theirs[...].astype(F32)
    split_grads(layout, whole, kernel, first_bias, mix, mix_bias, project, project_bias, book, decode, decode_bias)


def split_grads(layout, whole, kernel, first_bias, mix, mix_bias, project, project_bias, book, decode, decode_bias):
    for tap in range(9):
        kernel[tap] = whole[tap * 2 * HALF : (tap + 1) * 2 * HALF]
    row = layout.mix
    mix[:, :HALF] = whole[row : row + HALF]
    mix[:, HALF:] = whole[row + HALF : row + 2 * HALF]
    side = HALF // 2
    for row, target in ((layout.project, project), (layout.book, book)):
        for c in range(target.shape[1] // HALF):
            target[:, c * HALF : (c + 1) * HALF] = whole[row + c * side : row + (c + 1) * side]
    row = layout.bias
    first_bias[...] = whole[row : row + 1]
    mix_bias[...] = whole[row + 1 : row + 2]
    project_bias[...] = whole[row + 2 : row + 3, :side]
    row = layout.decode
    n = decode.shape[0]
    decode[...] = whole[row : row + n]
    decode_bias[...] = whole[row + n : row + n + 1]


def split_again(layout, total, extra, *refs):
    whole = refs[-1]
    whole[...] = total[...].astype(F32) + extra[...]
    split_grads(layout, whole, *refs[:-1])


def restore_rows(plan, n, waits, *refs):
    meta, heights, *refs = refs[waits:]
    own, far, out = refs[:n], refs[n : 2 * n], refs[2 * n]
    stage_own, stage_far, sems = refs[2 * n + 1 :]
    copies = []
    for k in range(n):
        size = plan.chunks[k] + (LEAD if k == n - 1 else 0)
        for i, (source, target) in enumerate(((own[k], stage_own), (far[k], stage_far))):
            from_rows = source.at[pl.ds(0, size)]
            copies.append(pltpu.make_async_copy(from_rows, target.at[pl.ds(plan.starts[k], size)], sems.at[i, k]))
            copies[-1].start()
    for copy in copies:
        copy.wait()
    base = plan.images + len(plan.chunks) + 1
    own_row, send_row = meta[base], meta[base + 1]
    first, last = meta[base + 2], meta[base + 3]
    row_of = lax.broadcasted_iota(jnp.int32, (SIDE, 1, 1), 0)

    def own_image(b, carry):
        rows = stage_own[pl.ds(meta[b] + LEAD, SIDE)]
        out[b] = jnp.where(row_of < heights[b], rows, jnp.zeros_like(rows))
        return carry

    def far_image(b, carry):
        rows = stage_far[pl.ds(meta[b] + own_row - send_row + LEAD, SIDE)]
        out[b] = jnp.where(row_of < heights[b], rows, jnp.zeros_like(rows))
        return carry

    lax.fori_loop(first, last, own_image, 0)
    lax.fori_loop(0, first, far_image, 0)
    lax.fori_loop(last, plan.images, far_image, 0)


def trade(value):
    return lax.ppermute(value, "mp", [(0, 1), (1, 0)])


def run_main(plan, layout, k, meta, heights, streams, weights, state, waits=(), ending=()):
    chunk, rows = plan.chunks[k], plan.rows[k]
    last = k >= plan.usual - 1
    final = k == plan.usual - 1
    x_own, x_far, q_own, q_far, codes = streams
    book_rows = weights[-1].shape[1]
    args = [*waits, *ending, meta, heights, x_own, x_far[k], q_own, q_far[k], codes, *weights]
    specs = [ANY] * len(waits) + ([SMEM, VMEM] if final else [])
    specs += [SMEM, SMEM, ANY, ANY, ANY, ANY, VMEM] + [VMEM] * len(weights)
    alias = {}
    if state is not None:
        args += [x_far[k - 1], q_far[k - 1], *state]
        specs += [ANY, ANY, VMEM, VMEM] + [ANY] * (len(state) - 2)
        if not final:
            for i in range(len(state) - 2):
                alias[len(args) - 5 + i] = 4 + i
    size = chunk + LEAD if last else chunk
    tile = (SIDE, HALF)
    outs = [shape((size,) + tile, BF16)] * 2 + [shape((LEAD,) + tile, BF16)] * 2
    sums = [(2 * HALF, 18 * HALF), (2 * HALF, 2 * HALF), (2 * HALF, HALF), (book_rows, HALF), (24, 2 * HALF)]
    scratch = []
    if final:
        outs += [shape((layout.half, HALF), F32)] * 2 + [shape((2, layout.half, HALF), BF16)]
        scratch += [pltpu.VMEM(dims, F32) for dims in sums]
        scratch += [pltpu.VMEM((layout.rows, HALF), F32)] * 2
    else:
        outs += [shape(dims, F32) for dims in sums]
    half = chunk // 2
    spots = BLOCK * SIDE
    scratch += [
        pltpu.VMEM((LEAD + chunk + SIDE,) + tile, BF16),
        pltpu.VMEM((LEAD + chunk + SIDE,) + tile, BF16),
        pltpu.VMEM((LEAD + half,) + tile, F32),
        pltpu.VMEM((LEAD + half,) + tile, BF16),
        pltpu.VMEM((LEAD + chunk + SIDE,) + tile, F32),
        pltpu.VMEM((rows + 2 * SIDE,) + tile, BF16),
        pltpu.VMEM((rows + 2 * SIDE,) + tile, BF16),
        pltpu.VMEM((rows + 2 * SIDE,) + tile, F32),
        pltpu.VMEM((-(-(rows * SIDE // HALF + 4) // 8) * 8, HALF), jnp.int32),
        pltpu.VMEM(((rows + 2) * SIDE, 6 * HALF), BF16),
        pltpu.VMEM((rows * SIDE, 2 * HALF), F32),
        pltpu.VMEM(((rows + 2) * SIDE, 6 * HALF), BF16),
        pltpu.VMEM((rows * SIDE, 2 * HALF), F32),
        pltpu.VMEM((rows + 2 * SIDE,) + tile, BF16),
        pltpu.VMEM((rows + 2 * SIDE,) + tile, BF16),
        pltpu.VMEM((LEAD + chunk + 2 * SIDE,) + tile, BF16),
        pltpu.VMEM((LEAD + chunk + 2 * SIDE,) + tile, BF16),
        pltpu.VMEM((spots, 2 * HALF), BF16),
        pltpu.VMEM((spots, 2 * HALF), F32),
        pltpu.VMEM((spots, 2 * HALF), BF16),
        pltpu.VMEM((spots, 2 * HALF), BF16),
        pltpu.VMEM((spots // 2, HALF), BF16),
        pltpu.VMEM((book_rows, spots), BF16),
        pltpu.VMEM((spots, HALF), BF16),
        pltpu.VMEM((spots, HALF), BF16),
        pltpu.SemaphoreType.DMA((13,)),
    ]
    spots = chunk * SIDE
    return pl.pallas_call(
        functools.partial(main_step, plan, layout, k, len(waits)),
        out_shape=outs,
        in_specs=specs,
        out_specs=[VMEM] * len(outs),
        scratch_shapes=scratch,
        input_output_aliases=alias,
        compiler_params=params(58),
        cost_estimate=cost(60 * 65536 * spots, 8 * MIB, 2 * 256 * spots),
        name=f"main_{k}",
    )(*args)


def local(
    image_latents,
    image_heights,
    code_index,
    kernel_three,
    bias_three,
    weight_mix,
    bias_mix,
    weight_project,
    bias_project,
    codebook,
    weight_decode,
    bias_decode,
    out_grad,
):
    images = image_latents.shape[0]
    plan = Plan(images)
    n = len(plan.chunks)
    tile = (SIDE, HALF)
    where = lax.axis_index("mp").astype(jnp.int32)
    core = lax.rem(lax.axis_index("dp").astype(jnp.int32), 2)
    spot = place = jnp.stack([where, core])

    packed = pl.pallas_call(
        functools.partial(pack_latents, plan),
        out_shape=[
            shape((meta_size(plan),), jnp.int32),
            shape((LEAD + plan.total,) + tile, BF16),
        ]
        + [shape((c,) + tile, BF16) for c in plan.chunks],
        in_specs=[SMEM, SMEM, HBM],
        out_specs=[SMEM, ANY] + [ANY] * n,
        scratch_shapes=[
            pltpu.VMEM((images, SIDE) + tile, BF16),
            pltpu.VMEM((plan.packed + SIDE,) + tile, BF16),
            pltpu.SemaphoreType.DMA((8,)),
            pltpu.SemaphoreType.DMA((n + 1,)),
        ],
        compiler_params=params(40),
        cost_estimate=cost(0, 12 * MIB),
        name="pack_latents",
    )(image_heights, place, image_latents)
    meta, x_own, x_send = packed[0], packed[1], packed[2:]

    packed = pl.pallas_call(
        functools.partial(pack_code_grads, plan),
        out_shape=[shape((plan.total // 2,) + tile, F32), shape((2 * HALF + HALF // 2 + SIDE, HALF), BF16)]
        + [shape((c // 2,) + tile, BF16) for c in plan.chunks],
        in_specs=[SMEM] + [HBM] * 6,
        out_specs=[VMEM] * (n + 2),
        scratch_shapes=[
            pltpu.VMEM((images, SIDE) + tile, BF16),
            pltpu.VMEM((plan.packed + SIDE,) + tile, BF16),
            pltpu.SemaphoreType.DMA((8,)),
            pltpu.SemaphoreType.DMA((5,)),
            pltpu.VMEM(weight_decode.shape, BF16),
            pltpu.VMEM(weight_mix.shape, BF16),
            pltpu.VMEM(weight_project.shape[::-1], BF16),
            pltpu.VMEM((1, HALF), BF16),
            pltpu.VMEM((1, HALF), BF16),
        ],
        compiler_params=params(40),
        cost_estimate=cost(2 * 2 * plan.total * SIDE * 256 * 128, 10 * MIB),
        name="pack_code_grads",
    )(meta, out_grad, weight_decode, weight_mix, weight_project.T, bias_three.reshape(1, HALF), bias_mix.reshape(1, HALF))
    q_own, small, q_send = packed[0], packed[1], packed[2:]

    book_rows, embed = codebook.shape
    codebook_t = codebook.T
    far_kernel = trade(kernel_three)
    far_small = trade(small)
    usual = plan.usual
    x_far, q_far = [], []
    for k in range(usual):
        x_far.append(trade(x_send[k]))
        q_far.append(trade(q_send[k]))

    weights = pl.pallas_call(
        prepare_weights,
        out_shape=[
            shape((18 * HALF, 2 * HALF), BF16),
            shape((18 * HALF, 2 * HALF), BF16),
            shape((2 * HALF, 2 * HALF), BF16),
            shape((2, 2 * HALF, HALF), BF16),
            shape((SIDE, 2 * HALF), F32),
            shape((HALF, book_rows), BF16),
        ],
        in_specs=[SMEM] + [VMEM] * 6,
        out_specs=[VMEM] * 6,
        compiler_params=params(16),
        cost_estimate=cost(0, 5 * MIB),
        name="prepare_weights",
    )(place, kernel_three, far_kernel, small, far_small, bias_project.reshape(1, -1), codebook_t)

    groups = 8
    group = images // groups
    codes = code_index.reshape(images, SIDE * SIDE)
    whole = lambda dims: pl.BlockSpec(dims, lambda g: (0,) * len(dims))
    four = pl.BlockSpec((group, SIDE) + tile, lambda g: (g, 0, 0, 0))
    row = pl.BlockSpec((group, SIDE * SIDE), lambda g: (g, 0))
    decode_acc = pl.pallas_call(
        functools.partial(sum_codes, plan, groups),
        grid=(groups,),
        out_shape=shape((embed + 8, HALF), F32),
        in_specs=[SMEM, row, four, whole((embed, book_rows))],
        out_specs=whole((embed + 8, HALF)),
        scratch_shapes=[
            pltpu.VMEM((book_rows, group * SIDE * SIDE), BF16),
            pltpu.VMEM((group * SIDE * SIDE, HALF), BF16),
            pltpu.VMEM((book_rows, HALF), F32),
        ],
        compiler_params=params(32),
        cost_estimate=cost(images * 256 * 512 * 256, 5 * MIB),
        name="sum_codes",
    )(image_heights, codes, out_grad, codebook_t)

    def decode(after):
        return pl.pallas_call(
            functools.partial(decode_images, plan, groups),
            grid=(groups,),
            out_shape=shape((images, SIDE) + tile, BF16),
            in_specs=[SMEM, row, whole((embed, book_rows)), whole((embed, HALF)), whole((1, HALF)), ANY],
            out_specs=four,
            scratch_shapes=[pltpu.VMEM((HALF, book_rows), BF16)],
            compiler_params=params(32),
            cost_estimate=cost(images * 256 * 512 * 256, 5 * MIB),
            name="decode_images",
        )(image_heights, codes, codebook_t, weight_decode, bias_decode.reshape(1, HALF), after)

    devices = lax.axis_size("dp")
    layout = Layout(devices, book_rows, embed)
    half, piece, chips = layout.half, layout.piece, devices // 2
    streams = (x_own, x_far, q_own, q_far, codes)
    state = None
    win_own, win_far = [], []
    for k in range(usual):
        waits = win_far[k - 2 : k - 1] if k > 1 else []
        ending = (spot, decode_acc) if k == usual - 1 else ()
        outs = run_main(plan, layout, k, meta, image_heights, streams, weights, state, waits, ending)
        win_own.append(outs[0])
        win_far.append(trade(outs[1]))
        state = outs[2:]
    carry, (keep_own, keep_far, send) = state[:2], state[2:]

    def restore(own, far, waits=()):
        count = len(own)
        return pl.pallas_call(
            functools.partial(restore_rows, plan, count, len(waits)),
            out_shape=shape((images, SIDE) + tile, BF16),
            in_specs=[ANY] * len(waits) + [SMEM, SMEM] + [ANY] * (2 * count),
            out_specs=VMEM,
            scratch_shapes=[
                pltpu.VMEM((plan.total + LEAD + SIDE,) + tile, BF16),
                pltpu.VMEM((plan.total + LEAD + SIDE,) + tile, BF16),
                pltpu.SemaphoreType.DMA((2, count)),
            ],
            compiler_params=params(40),
            cost_estimate=cost(0, 10 * MIB),
            name="restore_rows",
        )(*waits, meta, image_heights, *own, *far)

    across = [(i, i ^ 1) for i in range(devices)]

    def step(body, out, name, *args, waits=()):
        specs = [VMEM] * len(args) + [ANY] * len(waits)
        args = (*args, *waits)
        return pl.pallas_call(
            body,
            out_shape=out,
            in_specs=specs,
            out_specs=VMEM,
            compiler_params=params(24),
            cost_estimate=cost(0, 2 * MIB),
            name=name,
        )(*args)

    send = pl.pallas_call(
        hold,
        out_shape=shape(send.shape, BF16),
        in_specs=[ANY, ANY],
        out_specs=ANY,
        input_output_aliases={0: 0},
        name="hold",
    )(send, win_far[usual - 2])
    came = lax.ppermute(send, "dp", across)
    far = step(add_far, shape((half, HALF), BF16), "add_far", keep_far, came)
    came_far = trade(far)
    mine = step(add_own, shape((chips, piece, HALF), BF16), "add_own", keep_own, came, came_far)
    cores = [[i for i in range(devices) if i % 2 == c] for c in range(2)]
    decoded = decode(mine)
    mine = lax.all_to_all(mine, "dp", 0, 0, axis_index_groups=cores, tiled=True)
    mine = step(add_pieces, shape((chips, piece, HALF), BF16), "add_pieces", mine, waits=[win_far[usual - 1], decoded])
    latents_grad = restore(win_own, win_far, [mine])
    mine = lax.all_to_all(mine, "dp", 0, 0, axis_index_groups=cores, tiled=True)
    mine = mine.reshape(half, HALF)
    theirs = lax.ppermute(mine, "dp", across)

    grads_out = [
        shape((9, 2 * HALF, HALF), F32),
        shape((1, HALF), F32),
        shape((HALF, 2 * HALF), F32),
        shape((1, HALF), F32),
        shape((embed, HALF), F32),
        shape((1, embed), F32),
        shape((embed, book_rows), F32),
        shape((embed, HALF), F32),
        shape((1, HALF), F32),
    ]
    whole = pltpu.VMEM((layout.rows, HALF), F32)

    def usual_end(latents_grad):
        grads = pl.pallas_call(
            functools.partial(write_grads, layout),
            out_shape=grads_out,
            in_specs=[SMEM, VMEM, VMEM],
            out_specs=[VMEM] * 9,
            scratch_shapes=[whole],
            compiler_params=params(24),
            cost_estimate=cost(0, 4 * MIB),
            name="write_grads",
        )(spot, mine, theirs)
        return (latents_grad, *grads)

    def longer_end(latents_grad):
        last_x, last_q = trade(x_send[usual]), trade(q_send[usual])
        streams = (x_own, x_far + [last_x], q_own, q_far + [last_q], codes)
        outs = run_main(plan, layout, usual, meta, image_heights, streams, weights, carry)
        latents_grad = restore(win_own + [outs[0]], win_far + [trade(outs[1])])
        own, far = pl.pallas_call(
            functools.partial(gather_plain, layout),
            out_shape=[shape((layout.rows, HALF), F32)] * 2,
            in_specs=[SMEM] + [VMEM] * 5,
            out_specs=[VMEM] * 2,
            compiler_params=params(40),
            name="gather_plain",
        )(spot, *outs[4:])
        extra = lax.psum(own + trade(far), "dp")
        first, second = jnp.where(core == 0, mine, theirs), jnp.where(core == 0, theirs, mine)
        grads = pl.pallas_call(
            functools.partial(split_again, layout),
            out_shape=grads_out,
            in_specs=[VMEM, VMEM],
            out_specs=[VMEM] * 9,
            scratch_shapes=[whole],
            compiler_params=params(24),
            name="split_again",
        )(jnp.concatenate([first, second]), extra)
        return (latents_grad, *grads)

    flag = layout.bias + 3
    holder = flag // half
    flags = jnp.where(core == holder, mine[flag - holder * half, 0], theirs[flag - holder * half, 0])
    ends = lax.cond(flags.astype(F32) > 0.5, longer_end, usual_end, latents_grad)
    latents_grad, kernel_grad, first_bias, mix_grad, mix_bias, project_grad, project_bias, book, decode, decode_bias = ends
    return (
        decoded,
        latents_grad,
        kernel_grad,
        first_bias.reshape(HALF),
        mix_grad,
        mix_bias.reshape(HALF),
        project_grad.T,
        project_bias.reshape(embed),
        book.T,
        decode,
        decode_bias.reshape(HALF),
    )


def solution(mesh):
    tile = P("dp", None, None, "mp")
    placed = (
        tile,
        P("dp"),
        P("dp", None, None),
        P(None, None, "mp"),
        P("mp"),
        P("mp", None),
        P("mp"),
        P("mp", None),
        P(),
        P(),
        P(None, "mp"),
        P("mp"),
        tile,
    )
    outs = (
        tile,
        tile,
        P(None, None, "mp"),
        P("mp"),
        P("mp", None),
        P("mp"),
        P("mp", None),
        P(),
        P(),
        P(None, "mp"),
        P("mp"),
    )
    return jax.shard_map(local, mesh=mesh, in_specs=placed, out_specs=outs, check_vma=False)
```

```python
import functools

import jax
import jax.numpy as jnp
from jax import lax
from jax.experimental import pallas as pl
from jax.experimental.pallas import tpu as pltpu
from jax.sharding import PartitionSpec as P

SIDE = 16
HALF = 128
LEAD = 16
BLOCK = 32
TILE = 32
MARK = 1e9
GELU_SCALE = 0.7978845608028654
GELU_CUBE = 0.044715
COMMIT = 0.25
F32 = jnp.float32
BF16 = jnp.bfloat16
ANY = pl.BlockSpec(memory_space=pl.ANY)
SMEM = pl.BlockSpec(memory_space=pltpu.SMEM)
HBM = pl.BlockSpec(memory_space=pltpu.HBM)
VMEM = pl.BlockSpec(memory_space=pltpu.VMEM)
MIB = 1 << 20

NT = (((1,), (1,)), ((), ()))
TN = (((0,), (0,)), ((), ()))
NN = (((1,), (0,)), ((), ()))


def dot(a, b, dims=NN):
    return lax.dot_general(a, b, dims, preferred_element_type=F32)


def one_hot_columns(codes, code_of):
    return jnp.where(code_of == codes.astype(jnp.int16), jnp.bfloat16(1), jnp.bfloat16(0))


def numbers(count, width):
    return lax.broadcasted_iota(jnp.int32, (count, width), 0).astype(jnp.int16)


def shape(dims, kind):
    return jax.ShapeDtypeStruct(dims, kind)


def params(mib):
    return pltpu.CompilerParams(vmem_limit_bytes=mib * MIB)


def cost(flops, moved, slow=0):
    return pl.CostEstimate(flops=flops, bytes_accessed=moved, transcendentals=slow)


class Plan:
    def __init__(self, images):
        self.images = images
        longest = images * SIDE // 2 + SIDE // 2
        part = images // 8
        self.chunks = [10 * part, 17 * part, 21 * part]
        self.usual = len(self.chunks)
        rest = longest - sum(self.chunks)
        self.chunks.append(rest)
        self.starts = [sum(self.chunks[:k]) for k in range(len(self.chunks))]
        self.total = sum(self.chunks)
        self.packed = -(-(LEAD + longest + self.total + LEAD) // SIDE) * SIDE
        self.rows = []
        for c in self.chunks:
            most = 1 + c + 15 + c // 4 + 1
            self.rows.append(-(-most // BLOCK) * BLOCK)
        self.covered = sum(self.chunks[: self.usual])


def meta_size(plan):
    return plan.images + len(plan.chunks) + 1 + 5


def plan_rows(plan, heights, place, meta):
    images = plan.images
    base = images + len(plan.chunks) + 1

    def total_of(b, acc):
        return acc + heights[b]

    total = lax.fori_loop(0, images, total_of, jnp.int32(0))

    def split_of(b, state):
        acc, best, split, cut = state
        acc = acc + heights[b]
        worst = jnp.maximum(acc, total - acc)
        better = worst < best
        return (acc, jnp.where(better, worst, best), jnp.where(better, b + 1, split), jnp.where(better, acc, cut))

    _, _, split, cut = lax.fori_loop(0, images, split_of, (jnp.int32(0), jnp.int32(1 << 20), jnp.int32(0), jnp.int32(0)))
    mine = place[0]
    own_first = jnp.where(mine == 0, 0, split)
    own_last = jnp.where(mine == 0, split, images)
    own_row = jnp.where(mine == 0, 0, cut)
    send_row = jnp.where(mine == 0, cut, 0)
    for k in range(len(plan.chunks) + 1):
        meta[images + k] = own_first
    ends = [plan.starts[k] + plan.chunks[k] for k in range(len(plan.chunks))]

    def place_of(b, acc):
        meta[b] = acc - own_row
        acc = acc + heights[b]
        end = acc - own_row
        inside = jnp.logical_and(b >= own_first, b < own_last)
        step = jnp.int32(0)
        for k in range(len(plan.chunks) - 1):
            step = step + (end > ends[k]).astype(jnp.int32)

        @pl.when(inside)
        def _():
            meta[images + 1 + step] = b + 1

        return acc

    lax.fori_loop(0, images, place_of, jnp.int32(0))
    for k in range(len(plan.chunks)):
        meta[images + k + 1] = jnp.maximum(meta[images + k + 1], meta[images + k])
    meta[base] = own_row
    meta[base + 1] = send_row
    meta[base + 2] = own_first
    meta[base + 3] = own_last
    meta[base + 4] = jnp.maximum(cut, total - cut)


def pack_rows(plan, meta, source, packed, piece, count):
    base = plan.images + len(plan.chunks) + 1

    def one(i, carry):
        b = piece * count + i
        row = meta[b] + meta[base] + LEAD
        packed[pl.ds(row, SIDE)] = source[b]
        return carry

    lax.fori_loop(0, count, one, 0)


def pack_latents(plan, heights, place, x_hbm, meta, own, *rest):
    n = len(plan.chunks)
    sends, (x_in, packed, sem_in, sem_out) = rest[:n], rest[n:]
    pieces = 8
    count = plan.images // pieces
    fetch = []
    for p in range(pieces):
        part = pl.ds(p * count, count)
        fetch.append(pltpu.make_async_copy(x_hbm.at[part], x_in.at[part], sem_in.at[p]))
        fetch[-1].start()
    plan_rows(plan, heights, place, meta)
    base = plan.images + n + 1
    for p in range(pieces):
        fetch[p].wait()
        pack_rows(plan, meta, x_in, packed, p, count)
    copies = []
    for k in range(n):
        part = pl.ds(LEAD + meta[base + 1] + plan.starts[k], plan.chunks[k])
        copies.append(pltpu.make_async_copy(packed.at[part], sends[k], sem_out.at[k]))
        copies[-1].start()
    copies.append(pltpu.make_async_copy(packed.at[pl.ds(meta[base], LEAD + plan.total)], own, sem_out.at[n]))
    copies[-1].start()
    for copy in copies:
        copy.wait()


def pack_code_grads(plan, meta, og_hbm, *rest):
    n = len(plan.chunks)
    sources, (own, small), rest = rest[:5], rest[5:7], rest[7:]
    sends, rest = rest[:n], rest[n:]
    og_in, packed, sem_in, sem_small = rest[:4]
    held = rest[4:]
    small_fetch = []
    for i in range(5):
        small_fetch.append(pltpu.make_async_copy(sources[i], held[i], sem_small.at[i]))
        small_fetch[-1].start()
    decode_w, weight_mix, project_t, bias_first, bias_mix = held
    pieces = 8
    count = plan.images // pieces
    fetch = []
    for p in range(pieces):
        part = pl.ds(p * count, count)
        fetch.append(pltpu.make_async_copy(og_hbm.at[part], og_in.at[part], sem_in.at[p]))
        fetch[-1].start()
    base = plan.images + n + 1

    def clear(i, carry):
        packed[pl.ds(i * SIDE, SIDE)] = jnp.zeros((SIDE, SIDE, HALF), BF16)
        return carry

    lax.fori_loop(0, packed.shape[0] // SIDE, clear, 0)
    for copy in small_fetch:
        copy.wait()
    side = HALF // 2
    small[0:HALF] = weight_mix[:, :HALF]
    small[HALF : 2 * HALF] = weight_mix[:, HALF:]
    small[2 * HALF : 2 * HALF + side] = project_t[...]
    which = lax.broadcasted_iota(jnp.int32, (SIDE, HALF), 0)
    first, second = bias_first[...].astype(F32), bias_mix[...].astype(F32)
    first = jnp.where(which == 0, first, jnp.where(which == 1, second, 0.0))
    small[2 * HALF + side : 2 * HALF + side + SIDE] = first.astype(BF16)
    w = decode_w[...]
    blank = jnp.zeros_like(w)
    upper = jnp.concatenate([w, blank], axis=0)
    lower = jnp.concatenate([blank, w], axis=0)
    for p in range(pieces):
        fetch[p].wait()
        pack_rows(plan, meta, og_in, packed, p, count)
    for k in range(n):
        half = plan.chunks[k] // 2
        for which in range(2):
            row = LEAD + meta[base + 1 - which] + plan.starts[k]
            a = packed[pl.ds(row, half)].reshape(half * SIDE, HALF)
            b = packed[pl.ds(row + half, half)].reshape(half * SIDE, HALF)
            both = dot(a, upper, NT) + dot(b, lower, NT)
            both = both.reshape(half, SIDE, HALF)
            if which == 0:
                sends[k][...] = both.astype(BF16)
            else:
                own[pl.ds(plan.starts[k] // 2, half)] = both


def prepare_weights(place, kernel, far_kernel, small, far_small, bias_code, codebook_t, forward, backward, mix, project, bias, book):
    first = pl.multiple_of(place[0] * HALF, HALF)
    order = (first, HALF - first)
    for tap in range(9):
        for d, source in enumerate((kernel, far_kernel)):
            for c in range(2):
                tile = source[tap, pl.ds(order[c], HALF), :]
                row = tap * 2 * HALF
                forward[row + c * HALF : row + (c + 1) * HALF, d * HALF : (d + 1) * HALF] = tile
                backward[row + d * HALF : row + (d + 1) * HALF, c * HALF : (c + 1) * HALF] = tile.T
    blank = jnp.zeros((HALF, HALF // 2), BF16)
    for d, source in enumerate((small, far_small)):
        rows = pl.ds(d * HALF, HALF)
        for c in range(2):
            mix[rows, c * HALF : (c + 1) * HALF] = source[pl.ds(order[c], HALF), :]
        part = source[2 * HALF : 2 * HALF + HALF // 2, :].T
        project[0, rows, :] = jnp.concatenate([part, blank], axis=1)
        project[1, rows, :] = jnp.concatenate([blank, part], axis=1)
        bias[0:8, d * HALF : (d + 1) * HALF] = source[2 * HALF + HALF // 2 : 2 * HALF + HALF // 2 + SIDE, :].astype(F32)[0:8]
    code = bias_code[...].astype(F32)
    code = jnp.concatenate([code, code], axis=1)
    bias[8:16, :] = jnp.broadcast_to(jnp.concatenate([code, code], axis=1), (8, 2 * HALF))
    book[...] = jnp.concatenate([codebook_t[...], codebook_t[...]], axis=0)


def sum_codes(plan, steps, heights, codes, og, codebook_t, grads, hot, cots, sums):
    step = pl.program_id(0)
    group = plan.images // steps

    @pl.when(step == 0)
    def _():
        sums[...] = jnp.zeros_like(sums)

    spots = SIDE * SIDE
    code_of = numbers(codebook_t.shape[1], spots)
    spot = lax.broadcasted_iota(jnp.int32, (spots, 1), 0)
    for i in range(group):
        live = heights[step * group + i] * SIDE
        hot[:, i * spots : (i + 1) * spots] = one_hot_columns(codes[i : i + 1, :], code_of)
        cot = og[i].reshape(spots, HALF).astype(F32)
        cots[i * spots : (i + 1) * spots] = jnp.where(spot < live, cot, 0.0).astype(BF16)
    half = sums.shape[0] // 2
    for h in (0, half):
        sums[h : h + half] += dot(hot[h : h + half], cots[...])

    @pl.when(step == steps - 1)
    def _():
        total = sums[...]
        book = codebook_t[...].astype(F32)
        w = lax.dot_general(book, total, NN, precision=lax.Precision.HIGHEST, preferred_element_type=F32)
        bias = jnp.sum(total, axis=0, keepdims=True)
        embed = w.shape[0]
        grads[0:embed] = w
        grads[embed : embed + 8] = jnp.broadcast_to(bias, (8, HALF))


def decode_images(plan, steps, heights, codes, codebook_t, decode_w, decode_b, _, decoded, table):
    step = pl.program_id(0)
    group = plan.images // steps

    @pl.when(step == 0)
    def _():
        full = dot(codebook_t[...], decode_w[...], TN) + decode_b[...].astype(F32)
        table[...] = full.T.astype(BF16)

    spots = SIDE * SIDE
    code_of = numbers(codebook_t.shape[1], spots)
    spot = lax.broadcasted_iota(jnp.int32, (spots, 1), 0)
    for i in range(group):
        live = heights[step * group + i] * SIDE
        out = dot(table[...], one_hot_columns(codes[i : i + 1, :], code_of)).T
        decoded[i] = jnp.where(spot < live, out, 0.0).astype(BF16).reshape(SIDE, SIDE, HALF)


def gelu_parts(v):
    square = v * v
    t = jnp.tanh(v * (GELU_SCALE + (GELU_SCALE * GELU_CUBE) * square))
    half = 0.5 + 0.5 * t
    slope = half + (0.5 * v) * (1.0 - t * t) * (GELU_SCALE + (3.0 * GELU_SCALE * GELU_CUBE) * square)
    return v * half, slope


def main_step(plan, layout, k, waits, *refs):
    first_step = k == 0
    fresh = k in (0, plan.usual)
    final = k == plan.usual - 1
    refs = list(refs[waits:])

    def take(count):
        got = refs[:count]
        del refs[:count]
        return got

    if final:
        place, decode_acc = take(2)
    meta, heights, x_own, x_far, q_own, q_far, codes = take(7)
    kernel_hbm, kernel_t_hbm, mix, project, bias, book = take(6)
    if not first_step:
        x_past, q_past, carry_own, carry_far = take(4)
    if not fresh:
        past_accs = take(5)
    win_own, win_far, next_own, next_far = take(4)
    if final:
        laid_out = take(3)
    if not final:
        sums_out = take(5)
    kernel_acc, mix_acc, project_acc, book_acc, bias_acc = take(5)
    if final:
        laid_out += take(2)
    kernel, kernel_t, weight_sems = take(3)
    xo, xf, qo, qf, qd, xc_o, xc_f, qc, code_rows, act3, slope_x, grad3, block_g, lg_o, lg_f, out_o, out_f = take(17)
    second_s, slope_s, low_s, mixed_s, code_s, hot_s, found_s, diff_s, sems = refs

    chunk, start = plan.chunks[k], plan.starts[k]
    images, rows = plan.images, plan.rows[k]
    half = chunk // 2
    spots = BLOCK * SIDE
    low = meta[images + k]
    high = meta[images + k + 1]

    copies = [
        (x_own.at[pl.ds(start, LEAD + chunk)], xo.at[pl.ds(0, LEAD + chunk)]),
        (x_far, xf.at[pl.ds(LEAD, chunk)]),
        (q_own.at[pl.ds(start // 2, half)], qo.at[pl.ds(LEAD, half)]),
        (q_far, qf.at[pl.ds(LEAD, half)]),
    ]
    if not first_step:
        past = plan.chunks[k - 1]
        copies += [
            (x_past.at[pl.ds(past - LEAD, LEAD)], xf.at[pl.ds(0, LEAD)]),
            (q_own.at[pl.ds(start // 2 - LEAD, LEAD)], qo.at[pl.ds(0, LEAD)]),
            (q_past.at[pl.ds(past // 2 - LEAD, LEAD)], qf.at[pl.ds(0, LEAD)]),
        ]
    accs = (mix_acc, project_acc, book_acc, bias_acc, kernel_acc)
    early = len(copies)
    if not fresh:
        copies += list(zip(past_accs[1:] + past_accs[:1], accs))
    weight_copies = []
    for i, (source, target) in enumerate(((kernel_hbm, kernel), (kernel_t_hbm, kernel_t))):
        weight_copies.append(pltpu.make_async_copy(source, target, weight_sems.at[i]))
    started = []
    for i, (source, target) in enumerate(copies):
        started.append(pltpu.make_async_copy(source, target, sems.at[i]))
        started[-1].start()
    for copy in weight_copies:
        copy.start()
    started, later = started[:early], started[early:]

    if fresh:
        for acc in accs:
            acc[...] = jnp.zeros(acc.shape, F32)
    if first_step:
        out_o[0:LEAD] = jnp.zeros((LEAD, SIDE, HALF), BF16)
        out_f[0:LEAD] = jnp.zeros((LEAD, SIDE, HALF), BF16)
    else:
        out_o[0:LEAD] = carry_own[...]
        out_f[0:LEAD] = carry_far[...]

    blank = jnp.zeros((SIDE, SIDE, HALF), BF16)
    no_row = jnp.full((SIDE, SIDE, HALF), MARK, F32)
    code_rows[...] = jnp.full(code_rows.shape, -1, jnp.int32)
    for r in range(0, rows + 2 * BLOCK, SIDE):
        part = pl.ds(r, SIDE)
        xc_o[part] = blank
        xc_f[part] = blank
        if r < rows:
            qc[part] = no_row
    for copy in started:
        copy.wait()

    lane3 = lax.broadcasted_iota(jnp.int32, (1, SIDE, HALF), 2) < HALF // 2

    def spread(r0, count):
        both = (qo[pl.ds(r0, count)] + qf[pl.ds(r0, count)].astype(F32)).reshape(count * SIDE, HALF)
        turned = pltpu.roll(both, HALF // 2, 1).reshape(count, SIDE, HALF)
        both = both.reshape(count, SIDE, HALF)
        return jnp.where(lane3, both, turned), jnp.where(lane3, turned, both)

    upper, lower = spread(LEAD, half)
    qd[pl.ds(LEAD, half)] = upper
    qd[pl.ds(LEAD + half, half)] = lower
    if not first_step:
        _, lower = spread(0, LEAD)
        qd[0:LEAD] = lower

    spot = lax.broadcasted_iota(jnp.int32, (1, SIDE * SIDE), 1)
    lane128 = lax.broadcasted_iota(jnp.int32, (1, HALF), 1)
    per_row = HALF // SIDE

    def put(b, dst):
        src = meta[b] - start + LEAD
        xc_o[pl.ds(dst, SIDE)] = xo[pl.ds(src, SIDE)]
        xc_f[pl.ds(dst, SIDE)] = xf[pl.ds(src, SIDE)]
        qc[pl.ds(dst, SIDE)] = qd[pl.ds(src, SIDE)]
        end = dst + heights[b]
        xc_o[pl.ds(end, SIDE)] = blank
        xc_f[pl.ds(end, SIDE)] = blank
        qc[pl.ds(end, SIDE)] = no_row
        row = jnp.where(spot < heights[b] * SIDE, codes[pl.ds(b, 1), :], -1)
        turn = lax.rem(dst, per_row) * SIDE
        upper = pltpu.roll(row[:, :HALF], turn, 1)
        lower = pltpu.roll(row[:, HALF:], turn, 1)
        inside = lane128 >= turn
        pieces = (jnp.where(inside, upper, -1), jnp.where(inside, lower, upper), jnp.where(inside, -1, lower))
        for i, piece in enumerate(pieces):
            target = pl.ds(dst // per_row + i, 1)
            code_rows[target, :] = jnp.where(piece < 0, code_rows[target, :], piece)
        return end + 1

    used = lax.fori_loop(low, high, put, jnp.int32(1))
    blocks = jnp.where(high > low, (used + (BLOCK - 1)) // BLOCK, 0)

    column = lax.rem(lax.broadcasted_iota(jnp.int32, (TILE, 1), 0), SIDE)
    not_first = column != 0
    not_last = column != SIDE - 1

    def shifted(value):
        back = jnp.where(not_first, pltpu.roll(value, 1, 0), 0.0)
        ahead = jnp.where(not_last, pltpu.roll(value, TILE - 1, 0), 0.0)
        return back.astype(BF16), ahead.astype(BF16)

    edge = jnp.zeros((SIDE, 3 * 2 * HALF), BF16)
    act3[0:SIDE] = edge
    grad3[0:SIDE] = edge
    beyond = pl.multiple_of((blocks * BLOCK + 1) * SIDE, SIDE)
    grad3[pl.ds(beyond, SIDE)] = edge

    tiles = range(0, spots, TILE)

    def read_x(r0, t):
        part = pl.ds(r0 + t // SIDE, TILE // SIDE)
        o = xc_o[part].reshape(TILE, HALF)
        f = xc_f[part].reshape(TILE, HALF)
        return jnp.concatenate([o, f], axis=1).astype(F32)

    def at(row, count=BLOCK):
        return pl.ds(pl.multiple_of(row * SIDE, SIDE), count * SIDE)

    def tile_at(row, t):
        return pl.ds(pl.multiple_of(row * SIDE, SIDE) + t, TILE)

    def activate(j, carry):
        r0 = j * BLOCK
        for t in tiles:
            value, slope = gelu_parts(read_x(r0, t))
            slope_x[tile_at(r0, t), :] = slope
            back, ahead = shifted(value)
            act3[tile_at(r0 + 1, t), 0 : 2 * HALF] = back
            act3[tile_at(r0 + 1, t), 2 * HALF : 4 * HALF] = value.astype(BF16)
            act3[tile_at(r0 + 1, t), 4 * HALF : 6 * HALF] = ahead
        return carry

    lax.fori_loop(0, 2, activate, 0)
    for copy in later:
        copy.wait()
    for copy in weight_copies:
        copy.wait()

    bias_first = bias[0:1, :]
    bias_mix = bias[1:2, :]
    bias_code = bias[8:9, 0:HALF]
    lane = lax.broadcasted_iota(jnp.int32, (1, HALF), 1) < HALF // 2
    hb = BLOCK // 2
    hs = hb * SIDE

    def add_rows(total, value):
        value = value.astype(F32)
        for i in range(0, value.shape[0], 8):
            part = value[i : i + 8]
            total = part if total is None else total + part
        return total

    half_tiles = range(0, hs, TILE)
    code_of = numbers(book_acc.shape[0], HALF)
    halves = (0, hs)

    def middle(j, carry):
        r0 = j * BLOCK
        for i in range(BLOCK // per_row):
            row = code_rows[pl.ds(j * (BLOCK // per_row) + i, 1), :]
            hot_s[:, i * HALF : (i + 1) * HALF] = one_hot_columns(row, code_of)
        for h in halves:
            found_s[h : h + hs] = dot(book[...], hot_s[:, h : h + hs]).astype(BF16).T
        pre = []
        for h in halves:
            window = jnp.concatenate([act3[at(r0 + i + h // SIDE, hb), :] for i in range(3)], axis=1)
            pre.append(dot(window, kernel[...]))
        for h, part in zip(halves, pre):
            for t in half_tiles:
                value, slope = gelu_parts(part[t : t + TILE] + bias_first)
                second_s[h + t : h + t + TILE] = value.astype(BF16)
                slope_s[h + t : h + t + TILE] = slope
        mixed = [dot(second_s[h : h + hs], mix[...]) for h in halves]
        for h, part in zip(halves, mixed):
            for t in half_tiles:
                low_s[h + t : h + t + TILE] = (read_x(r0, h + t) + part[t : t + TILE] + bias_mix).astype(BF16)
        latents = [dot(low_s[h : h + hs], project[i]) for i, h in enumerate(halves)]
        total = None
        for t in half_tiles:
            first = pl.ds(r0 + t // SIDE, TILE // SIDE)
            other = pl.ds(r0 + hb + t // SIDE, TILE // SIDE)
            ch = jnp.where(lane, found_s[t : t + TILE].astype(F32), found_s[hs + t : hs + t + TILE].astype(F32))
            q = jnp.where(lane3, qc[first], qc[other]).reshape(TILE, HALF)
            live = q < 0.5 * MARK
            latent = latents[0][t : t + TILE] + latents[1][t : t + TILE] + bias_code
            diff = jnp.where(live, latent - ch, 0.0)
            code_grad = jnp.where(live, q + (2.0 * COMMIT) * diff, 0.0).astype(BF16)
            code_s[t : t + TILE] = code_grad
            total = add_rows(total, code_grad)
            big = diff.astype(BF16).astype(F32)
            small = diff - big
            turned = pltpu.roll(small, HALF // 2, 1)
            diff_s[t : t + TILE] = jnp.where(lane, big, turned).astype(BF16)
            turned = pltpu.roll(big, HALF // 2, 1)
            diff_s[hs + t : hs + t + TILE] = jnp.where(lane, turned, small).astype(BF16)
        bias_acc[16:24, 0:HALF] += total
        total = None
        blocks_g = [dot(code_s[...], project[i], NT) for i in range(2)]
        for h, part in zip(halves, blocks_g):
            for t in half_tiles:
                block_g[tile_at(r0, h + t), :] = part[t : t + TILE]
                mixed_grad = part[t : t + TILE].astype(BF16)
                mixed_s[h + t : h + t + TILE] = mixed_grad
                total = add_rows(total, mixed_grad)
        bias_acc[8:16] += total
        second_grad = [dot(mixed_s[h : h + hs], mix[...], NT) for h in halves]
        total = None
        for h, part in zip(halves, second_grad):
            for t in half_tiles:
                first_grad = slope_s[h + t : h + t + TILE] * part[t : t + TILE]
                back, ahead = shifted(first_grad)
                first_low = first_grad.astype(BF16)
                grad3[tile_at(r0 + 1, h + t), 0 : 2 * HALF] = ahead
                grad3[tile_at(r0 + 1, h + t), 2 * HALF : 4 * HALF] = first_low
                grad3[tile_at(r0 + 1, h + t), 4 * HALF : 6 * HALF] = back
                total = add_rows(total, first_low)
        bias_acc[0:8] += total
        book_acc[...] += dot(hot_s[...], diff_s[...])
        mix_acc[...] += dot(second_s[...], mixed_s[...], TN)
        project_acc[...] += jnp.where(lane, dot(low_s[0:hs], code_s[...], TN), dot(low_s[hs:], code_s[...], TN))
        return carry

    def finish(j, carry):
        r0 = j * BLOCK
        active = act3[at(r0 + 1), 2 * HALF : 4 * HALF].T
        for i in range(3):
            kernel_acc[:, i * 6 * HALF : (i + 1) * 6 * HALF] += dot(active, grad3[at(r0 + 2 - i), :])
        grads = []
        for h in halves:
            window = jnp.concatenate([grad3[at(r0 + 2 - i + h // SIDE, hb), :] for i in range(3)], axis=1)
            grads.append(dot(window, kernel_t[...]))
        for h, grad in zip(halves, grads):
            for t in half_tiles:
                here = tile_at(r0, h + t)
                out = (block_g[here, :] + slope_x[here, :] * grad[t : t + TILE]).astype(BF16)
                part = pl.ds(r0 + (h + t) // SIDE, TILE // SIDE)
                lg_o[part] = out[:, :HALF].reshape(TILE // SIDE, SIDE, HALF)
                lg_f[part] = out[:, HALF:].reshape(TILE // SIDE, SIDE, HALF)
        return carry

    def opening(j, carry):
        middle(j, carry)
        return activate(j + 2, carry)

    def steady(j, carry):
        finish(j - 2, carry)
        middle(j, carry)
        return activate(j + 2, carry)

    lax.fori_loop(0, jnp.minimum(blocks, 2), opening, 0)
    lax.fori_loop(2, blocks, steady, 0)
    lax.fori_loop(jnp.maximum(blocks - 2, 0), blocks, finish, 0)
    leaving = []
    if not final:
        leaving += list(zip((kernel_acc, mix_acc, project_acc, book_acc, bias_acc), sums_out))
        for i, (source, target) in enumerate(leaving):
            leaving[i] = pltpu.make_async_copy(source, target, sems.at[i])
            leaving[i].start()

    def collect(b, src):
        dst = meta[b] - start + LEAD
        out_o[pl.ds(dst, SIDE)] = lg_o[pl.ds(src, SIDE)]
        out_f[pl.ds(dst, SIDE)] = lg_f[pl.ds(src, SIDE)]
        return src + heights[b] + 1

    lax.fori_loop(low, high, collect, jnp.int32(1))
    size = win_own.shape[0]
    windows = (
        (out_o.at[pl.ds(0, size)], win_own),
        (out_f.at[pl.ds(0, size)], win_far),
        (out_o.at[pl.ds(chunk, LEAD)], next_own),
        (out_f.at[pl.ds(chunk, LEAD)], next_far),
    )
    for i, (source, target) in enumerate(windows):
        leaving.append(pltpu.make_async_copy(source, target, sems.at[5 + i]))
        leaving[-1].start()
    if final:
        sums = (kernel_acc, mix_acc, project_acc, book_acc, bias_acc, decode_acc)
        gather_grads(plan, layout, place, meta, sums, *laid_out)
    for copy in leaving:
        copy.wait()


class Layout:
    def __init__(self, devices, book_rows, embed):
        self.mix = 9 * 2 * HALF
        self.project = self.mix + 2 * HALF
        self.book = self.project + HALF // 2
        self.bias = self.book + book_rows // 2
        self.decode = self.bias + 8
        used = self.decode + embed + 8
        self.devices = devices
        self.piece = -(-used // (devices * SIDE)) * SIDE
        self.rows = self.piece * devices
        self.half = self.rows // 2
        self.used = used


def lay_out(layout, swap, kernel_acc, mix_acc, project_acc, book_acc, bias_acc, decode_acc, own, far):
    def lanes(value):
        return value[:, :HALF], value[:, HALF:]

    def order(first, second):
        return jnp.where(swap, second, first), jnp.where(swap, first, second)

    row = 0
    for tap in range(9):
        block = kernel_acc[:, tap * 2 * HALF : (tap + 1) * 2 * HALF]
        mine, theirs = lanes(block)
        a, b = order(mine[:HALF], mine[HALF:])
        own[row : row + HALF] = a
        own[row + HALF : row + 2 * HALF] = b
        a, b = order(theirs[:HALF], theirs[HALF:])
        far[row : row + HALF] = a
        far[row + HALF : row + 2 * HALF] = b
        row += 2 * HALF
    row = layout.mix
    for target, part in ((own, mix_acc[:HALF]), (far, mix_acc[HALF:])):
        a, b = order(*lanes(part))
        target[row : row + HALF] = a
        target[row + HALF : row + 2 * HALF] = b
    row = layout.project
    side = HALF // 2
    for target, part in ((own, project_acc[:HALF]), (far, project_acc[HALF:])):
        part = part + pltpu.roll(part, side, 1)
        target[row : row + side] = part.T[:side]
    row = layout.book
    book = book_acc[...]
    book = -2.0 * (book + pltpu.roll(book, side, 1))
    book = book.T[:side]
    for c in range(book.shape[1] // HALF):
        part = book[:, c * HALF : (c + 1) * HALF]
        own[row + c * side : row + (c + 1) * side] = part
        far[row + c * side : row + (c + 1) * side] = part
    row = layout.bias
    sums = [jnp.sum(bias_acc[8 * i : 8 * i + 8], axis=0, keepdims=True) for i in range(3)]
    code = sums[2][:, :HALF]
    code = code + pltpu.roll(code, side, 1)
    which = lax.broadcasted_iota(jnp.int32, (8, HALF), 0)
    for target, first in ((own, 0), (far, HALF)):
        part = jnp.where(which == 0, sums[0][:, first : first + HALF], sums[1][:, first : first + HALF])
        target[row : row + 8] = jnp.where(which == 2, code, jnp.where(which < 2, part, 0.0))
    row = layout.decode
    rest = layout.rows - row
    own[row:] = jnp.zeros((rest, HALF), F32)
    far[row:] = jnp.zeros((rest, HALF), F32)
    if decode_acc is not None:
        own[row : row + decode_acc.shape[0]] = decode_acc[...]


def gather_plain(layout, place, *refs):
    lay_out(layout, place[0] == 1, *refs[:5], None, *refs[5:])


def gather_grads(plan, layout, place, meta, accs, keep_own, keep_far, send, own, far):
    lay_out(layout, place[0] == 1, *accs, own, far)
    base = plan.images + len(plan.chunks) + 1
    over = (meta[base + 4] > plan.covered).astype(F32)
    which = lax.broadcasted_iota(jnp.int32, (8, HALF), 0)
    row = layout.bias
    own[row : row + 8] = jnp.where(which == 3, over, own[row : row + 8])
    half = layout.half
    mine = pl.ds(pl.multiple_of(place[1] * half, SIDE), half)
    other = pl.ds(pl.multiple_of((1 - place[1]) * half, SIDE), half)
    keep_own[...] = own[mine, :]
    keep_far[...] = far[mine, :]
    send[0] = own[other, :].astype(BF16)
    send[1] = far[other, :].astype(BF16)


def hold(value, _, out):
    pass


def add_far(keep_far, came, out):
    out[...] = (keep_far[...] + came[1].astype(F32)).astype(BF16)


def add_own(keep_own, came, came_far, out):
    total = keep_own[...] + came[0].astype(F32) + came_far[...].astype(F32)
    out[...] = total.astype(BF16).reshape(out.shape)


def add_pieces(pieces, *rest):
    out = rest[-1]
    total = pieces[0].astype(F32)
    for i in range(1, pieces.shape[0]):
        total = total + pieces[i].astype(F32)
    out[...] = jnp.broadcast_to(total.astype(BF16)[None], out.shape)


def write_grads(layout, place, mine, theirs, kernel, first_bias, mix, mix_bias, project, project_bias, book, decode, decode_bias, whole):
    half = layout.half
    whole[pl.ds(pl.multiple_of(place[1] * half, SIDE), half), :] = mine[...].astype(F32)
    whole[pl.ds(pl.multiple_of((1 - place[1]) * half, SIDE), half), :] = theirs[...].astype(F32)
    split_grads(layout, whole, kernel, first_bias, mix, mix_bias, project, project_bias, book, decode, decode_bias)


def split_grads(layout, whole, kernel, first_bias, mix, mix_bias, project, project_bias, book, decode, decode_bias):
    for tap in range(9):
        kernel[tap] = whole[tap * 2 * HALF : (tap + 1) * 2 * HALF]
    row = layout.mix
    mix[:, :HALF] = whole[row : row + HALF]
    mix[:, HALF:] = whole[row + HALF : row + 2 * HALF]
    side = HALF // 2
    for row, target in ((layout.project, project), (layout.book, book)):
        for c in range(target.shape[1] // HALF):
            target[:, c * HALF : (c + 1) * HALF] = whole[row + c * side : row + (c + 1) * side]
    row = layout.bias
    first_bias[...] = whole[row : row + 1]
    mix_bias[...] = whole[row + 1 : row + 2]
    project_bias[...] = whole[row + 2 : row + 3, :side]
    row = layout.decode
    n = decode.shape[0]
    decode[...] = whole[row : row + n]
    decode_bias[...] = whole[row + n : row + n + 1]


def split_again(layout, total, extra, *refs):
    whole = refs[-1]
    whole[...] = total[...].astype(F32) + extra[...]
    split_grads(layout, whole, *refs[:-1])


def restore_rows(plan, n, waits, *refs):
    meta, heights, *refs = refs[waits:]
    own, far, out = refs[:n], refs[n : 2 * n], refs[2 * n]
    stage_own, stage_far, sems = refs[2 * n + 1 :]
    copies = []
    for k in range(n):
        size = plan.chunks[k] + (LEAD if k == n - 1 else 0)
        for i, (source, target) in enumerate(((own[k], stage_own), (far[k], stage_far))):
            from_rows = source.at[pl.ds(0, size)]
            copies.append(pltpu.make_async_copy(from_rows, target.at[pl.ds(plan.starts[k], size)], sems.at[i, k]))
            copies[-1].start()
    for copy in copies:
        copy.wait()
    base = plan.images + len(plan.chunks) + 1
    own_row, send_row = meta[base], meta[base + 1]
    first, last = meta[base + 2], meta[base + 3]
    row_of = lax.broadcasted_iota(jnp.int32, (SIDE, 1, 1), 0)

    def own_image(b, carry):
        rows = stage_own[pl.ds(meta[b] + LEAD, SIDE)]
        out[b] = jnp.where(row_of < heights[b], rows, jnp.zeros_like(rows))
        return carry

    def far_image(b, carry):
        rows = stage_far[pl.ds(meta[b] + own_row - send_row + LEAD, SIDE)]
        out[b] = jnp.where(row_of < heights[b], rows, jnp.zeros_like(rows))
        return carry

    lax.fori_loop(first, last, own_image, 0)
    lax.fori_loop(0, first, far_image, 0)
    lax.fori_loop(last, plan.images, far_image, 0)


def trade(value):
    return lax.ppermute(value, "mp", [(0, 1), (1, 0)])


def run_main(plan, layout, k, meta, heights, streams, weights, state, waits=(), ending=()):
    chunk, rows = plan.chunks[k], plan.rows[k]
    last = k >= plan.usual - 1
    final = k == plan.usual - 1
    x_own, x_far, q_own, q_far, codes = streams
    book_rows = weights[-1].shape[1]
    args = [*waits, *ending, meta, heights, x_own, x_far[k], q_own, q_far[k], codes, *weights]
    specs = [ANY] * len(waits) + ([SMEM, VMEM] if final else [])
    specs += [SMEM, SMEM, ANY, ANY, ANY, ANY, VMEM, ANY, ANY] + [VMEM] * (len(weights) - 2)
    alias = {}
    if state is not None:
        args += [x_far[k - 1], q_far[k - 1], *state]
        specs += [ANY, ANY, VMEM, VMEM] + [ANY] * (len(state) - 2)
        if not final:
            for i in range(len(state) - 2):
                alias[len(args) - 5 + i] = 4 + i
    size = chunk + LEAD if last else chunk
    tile = (SIDE, HALF)
    outs = [shape((size,) + tile, BF16)] * 2 + [shape((LEAD,) + tile, BF16)] * 2
    sums = [(2 * HALF, 18 * HALF), (2 * HALF, 2 * HALF), (2 * HALF, HALF), (book_rows, HALF), (24, 2 * HALF)]
    scratch = [pltpu.VMEM(dims, F32) for dims in sums]
    out_specs = [ANY] * 4
    if final:
        outs += [shape((layout.half, HALF), F32)] * 2 + [shape((2, layout.half, HALF), BF16)]
        out_specs += [VMEM] * 3
        scratch += [pltpu.VMEM((layout.rows, HALF), F32)] * 2
    else:
        outs += [shape(dims, F32) for dims in sums]
        out_specs += [ANY] * 5
    scratch += [pltpu.VMEM((18 * HALF, 2 * HALF), BF16)] * 2 + [pltpu.SemaphoreType.DMA((2,))]
    half = chunk // 2
    spots = BLOCK * SIDE
    scratch += [
        pltpu.VMEM((LEAD + chunk + SIDE,) + tile, BF16),
        pltpu.VMEM((LEAD + chunk + SIDE,) + tile, BF16),
        pltpu.VMEM((LEAD + half,) + tile, F32),
        pltpu.VMEM((LEAD + half,) + tile, BF16),
        pltpu.VMEM((LEAD + chunk + SIDE,) + tile, F32),
        pltpu.VMEM((rows + 2 * BLOCK + SIDE,) + tile, BF16),
        pltpu.VMEM((rows + 2 * BLOCK + SIDE,) + tile, BF16),
        pltpu.VMEM((rows + 2 * SIDE,) + tile, F32),
        pltpu.VMEM((-(-(rows * SIDE // HALF + 4) // 8) * 8, HALF), jnp.int32),
        pltpu.VMEM(((rows + 2 * BLOCK + 2) * SIDE, 6 * HALF), BF16),
        pltpu.VMEM(((rows + 2 * BLOCK) * SIDE, 2 * HALF), F32),
        pltpu.VMEM(((rows + 2) * SIDE, 6 * HALF), BF16),
        pltpu.VMEM((rows * SIDE, 2 * HALF), F32),
        pltpu.VMEM((rows + 2 * SIDE,) + tile, BF16),
        pltpu.VMEM((rows + 2 * SIDE,) + tile, BF16),
        pltpu.VMEM((LEAD + chunk + 2 * SIDE,) + tile, BF16),
        pltpu.VMEM((LEAD + chunk + 2 * SIDE,) + tile, BF16),
        pltpu.VMEM((spots, 2 * HALF), BF16),
        pltpu.VMEM((spots, 2 * HALF), F32),
        pltpu.VMEM((spots, 2 * HALF), BF16),
        pltpu.VMEM((spots, 2 * HALF), BF16),
        pltpu.VMEM((spots // 2, HALF), BF16),
        pltpu.VMEM((book_rows, spots), BF16),
        pltpu.VMEM((spots, HALF), BF16),
        pltpu.VMEM((spots, HALF), BF16),
        pltpu.SemaphoreType.DMA((13,)),
    ]
    spots = chunk * SIDE
    return pl.pallas_call(
        functools.partial(main_step, plan, layout, k, len(waits)),
        out_shape=outs,
        in_specs=specs,
        out_specs=out_specs,
        scratch_shapes=scratch,
        input_output_aliases=alias,
        compiler_params=params(58),
        cost_estimate=cost(60 * 65536 * spots, 8 * MIB, 2 * 256 * spots),
        name=f"main_{k}",
    )(*args)


def local(
    image_latents,
    image_heights,
    code_index,
    kernel_three,
    bias_three,
    weight_mix,
    bias_mix,
    weight_project,
    bias_project,
    codebook,
    weight_decode,
    bias_decode,
    out_grad,
):
    images = image_latents.shape[0]
    plan = Plan(images)
    n = len(plan.chunks)
    tile = (SIDE, HALF)
    where = lax.axis_index("mp").astype(jnp.int32)
    core = lax.rem(lax.axis_index("dp").astype(jnp.int32), 2)
    spot = place = jnp.stack([where, core])

    packed = pl.pallas_call(
        functools.partial(pack_latents, plan),
        out_shape=[
            shape((meta_size(plan),), jnp.int32),
            shape((LEAD + plan.total,) + tile, BF16),
        ]
        + [shape((c,) + tile, BF16) for c in plan.chunks],
        in_specs=[SMEM, SMEM, HBM],
        out_specs=[SMEM, ANY] + [ANY] * n,
        scratch_shapes=[
            pltpu.VMEM((images, SIDE) + tile, BF16),
            pltpu.VMEM((plan.packed + SIDE,) + tile, BF16),
            pltpu.SemaphoreType.DMA((8,)),
            pltpu.SemaphoreType.DMA((n + 1,)),
        ],
        compiler_params=params(60),
        cost_estimate=cost(0, 12 * MIB),
        name="pack_latents",
    )(image_heights, place, image_latents)
    meta, x_own, x_send = packed[0], packed[1], packed[2:]

    packed = pl.pallas_call(
        functools.partial(pack_code_grads, plan),
        out_shape=[shape((plan.total // 2,) + tile, F32), shape((2 * HALF + HALF // 2 + SIDE, HALF), BF16)]
        + [shape((c // 2,) + tile, BF16) for c in plan.chunks],
        in_specs=[SMEM] + [HBM] * 6,
        out_specs=[VMEM] * (n + 2),
        scratch_shapes=[
            pltpu.VMEM((images, SIDE) + tile, BF16),
            pltpu.VMEM((plan.packed + SIDE,) + tile, BF16),
            pltpu.SemaphoreType.DMA((8,)),
            pltpu.SemaphoreType.DMA((5,)),
            pltpu.VMEM(weight_decode.shape, BF16),
            pltpu.VMEM(weight_mix.shape, BF16),
            pltpu.VMEM(weight_project.shape[::-1], BF16),
            pltpu.VMEM((1, HALF), BF16),
            pltpu.VMEM((1, HALF), BF16),
        ],
        compiler_params=params(60),
        cost_estimate=cost(2 * 2 * plan.total * SIDE * 256 * 128, 10 * MIB),
        name="pack_code_grads",
    )(meta, out_grad, weight_decode, weight_mix, weight_project.T, bias_three.reshape(1, HALF), bias_mix.reshape(1, HALF))
    q_own, small, q_send = packed[0], packed[1], packed[2:]

    book_rows, embed = codebook.shape
    codebook_t = codebook.T
    far_kernel = trade(kernel_three)
    far_small = trade(small)
    usual = plan.usual
    x_far, q_far = [], []
    for k in range(usual):
        x_far.append(trade(x_send[k]))
        q_far.append(trade(q_send[k]))

    weights = pl.pallas_call(
        prepare_weights,
        out_shape=[
            shape((18 * HALF, 2 * HALF), BF16),
            shape((18 * HALF, 2 * HALF), BF16),
            shape((2 * HALF, 2 * HALF), BF16),
            shape((2, 2 * HALF, HALF), BF16),
            shape((SIDE, 2 * HALF), F32),
            shape((HALF, book_rows), BF16),
        ],
        in_specs=[SMEM] + [VMEM] * 6,
        out_specs=[VMEM] * 6,
        compiler_params=params(16),
        cost_estimate=cost(0, 5 * MIB),
        name="prepare_weights",
    )(place, kernel_three, far_kernel, small, far_small, bias_project.reshape(1, -1), codebook_t)

    groups = 8
    group = images // groups
    codes = code_index.reshape(images, SIDE * SIDE)
    whole = lambda dims: pl.BlockSpec(dims, lambda g: (0,) * len(dims))
    four = pl.BlockSpec((group, SIDE) + tile, lambda g: (g, 0, 0, 0))
    row = pl.BlockSpec((group, SIDE * SIDE), lambda g: (g, 0))
    decode_acc = pl.pallas_call(
        functools.partial(sum_codes, plan, groups),
        grid=(groups,),
        out_shape=shape((embed + 8, HALF), F32),
        in_specs=[SMEM, row, four, whole((embed, book_rows))],
        out_specs=whole((embed + 8, HALF)),
        scratch_shapes=[
            pltpu.VMEM((book_rows, group * SIDE * SIDE), BF16),
            pltpu.VMEM((group * SIDE * SIDE, HALF), BF16),
            pltpu.VMEM((book_rows, HALF), F32),
        ],
        compiler_params=params(60),
        cost_estimate=cost(images * 256 * 512 * 256, 5 * MIB),
        name="sum_codes",
    )(image_heights, codes, out_grad, codebook_t)

    def decode(after):
        return pl.pallas_call(
            functools.partial(decode_images, plan, groups),
            grid=(groups,),
            out_shape=shape((images, SIDE) + tile, BF16),
            in_specs=[SMEM, row, whole((embed, book_rows)), whole((embed, HALF)), whole((1, HALF)), ANY],
            out_specs=four,
            scratch_shapes=[pltpu.VMEM((HALF, book_rows), BF16)],
            compiler_params=params(32),
            cost_estimate=cost(images * 256 * 512 * 256, 5 * MIB),
            name="decode_images",
        )(image_heights, codes, codebook_t, weight_decode, bias_decode.reshape(1, HALF), after)

    devices = lax.axis_size("dp")
    layout = Layout(devices, book_rows, embed)
    half, piece, chips = layout.half, layout.piece, devices // 2
    streams = (x_own, x_far, q_own, q_far, codes)
    state = None
    win_own, win_far = [], []
    for k in range(usual):
        waits = win_far[k - 2 : k - 1] if k > 1 else []
        ending = (spot, decode_acc) if k == usual - 1 else ()
        outs = run_main(plan, layout, k, meta, image_heights, streams, weights, state, waits, ending)
        win_own.append(outs[0])
        if k < usual - 1:
            win_far.append(trade(outs[1]))
        state = outs[2:]
    last_window = outs[1]
    carry, (keep_own, keep_far, send) = state[:2], state[2:]

    def restore(own, far, waits=()):
        count = len(own)
        return pl.pallas_call(
            functools.partial(restore_rows, plan, count, len(waits)),
            out_shape=shape((images, SIDE) + tile, BF16),
            in_specs=[ANY] * len(waits) + [SMEM, SMEM] + [ANY] * (2 * count),
            out_specs=VMEM,
            scratch_shapes=[
                pltpu.VMEM((plan.total + LEAD + SIDE,) + tile, BF16),
                pltpu.VMEM((plan.total + LEAD + SIDE,) + tile, BF16),
                pltpu.SemaphoreType.DMA((2, count)),
            ],
            compiler_params=params(60),
            cost_estimate=cost(0, 10 * MIB),
            name="restore_rows",
        )(*waits, meta, image_heights, *own, *far)

    across = [(i, i ^ 1) for i in range(devices)]

    def step(body, out, name, *args, waits=()):
        specs = [VMEM] * len(args) + [ANY] * len(waits)
        args = (*args, *waits)
        return pl.pallas_call(
            body,
            out_shape=out,
            in_specs=specs,
            out_specs=VMEM,
            compiler_params=params(24),
            cost_estimate=cost(0, 2 * MIB),
            name=name,
        )(*args)

    def held(value, other):
        return pl.pallas_call(
            hold,
            out_shape=shape(value.shape, value.dtype),
            in_specs=[ANY, ANY],
            out_specs=ANY,
            input_output_aliases={0: 0},
            name="hold",
        )(value, other)

    send = held(send, win_far[usual - 2])
    came = lax.ppermute(send, "dp", across)
    far = step(add_far, shape((half, HALF), BF16), "add_far", keep_far, came)
    came_far = trade(far)
    win_far.append(trade(held(last_window, came_far)))
    mine = step(add_own, shape((chips, piece, HALF), BF16), "add_own", keep_own, came, came_far)
    cores = [[i for i in range(devices) if i % 2 == c] for c in range(2)]
    decoded = decode(mine)
    mine = lax.all_to_all(mine, "dp", 0, 0, axis_index_groups=cores, tiled=True)
    mine = step(add_pieces, shape((chips, piece, HALF), BF16), "add_pieces", mine, waits=[win_far[usual - 1], decoded])
    latents_grad = restore(win_own, win_far, [mine])
    mine = lax.all_to_all(mine, "dp", 0, 0, axis_index_groups=cores, tiled=True)
    mine = held(mine, latents_grad).reshape(half, HALF)
    theirs = lax.ppermute(mine, "dp", across)

    grads_out = [
        shape((9, 2 * HALF, HALF), F32),
        shape((1, HALF), F32),
        shape((HALF, 2 * HALF), F32),
        shape((1, HALF), F32),
        shape((embed, HALF), F32),
        shape((1, embed), F32),
        shape((embed, book_rows), F32),
        shape((embed, HALF), F32),
        shape((1, HALF), F32),
    ]
    whole = pltpu.VMEM((layout.rows, HALF), F32)

    def usual_end(latents_grad):
        grads = pl.pallas_call(
            functools.partial(write_grads, layout),
            out_shape=grads_out,
            in_specs=[SMEM, VMEM, VMEM],
            out_specs=[VMEM] * 9,
            scratch_shapes=[whole],
            compiler_params=params(24),
            cost_estimate=cost(0, 4 * MIB),
            name="write_grads",
        )(spot, mine, theirs)
        return (latents_grad, *grads)

    def longer_end(latents_grad):
        last_x, last_q = trade(x_send[usual]), trade(q_send[usual])
        streams = (x_own, x_far + [last_x], q_own, q_far + [last_q], codes)
        outs = run_main(plan, layout, usual, meta, image_heights, streams, weights, carry)
        latents_grad = restore(win_own + [outs[0]], win_far + [trade(outs[1])])
        own, far = pl.pallas_call(
            functools.partial(gather_plain, layout),
            out_shape=[shape((layout.rows, HALF), F32)] * 2,
            in_specs=[SMEM] + [VMEM] * 5,
            out_specs=[VMEM] * 2,
            compiler_params=params(40),
            name="gather_plain",
        )(spot, *outs[4:])
        extra = lax.psum(own + trade(far), "dp")
        first, second = jnp.where(core == 0, mine, theirs), jnp.where(core == 0, theirs, mine)
        grads = pl.pallas_call(
            functools.partial(split_again, layout),
            out_shape=grads_out,
            in_specs=[VMEM, VMEM],
            out_specs=[VMEM] * 9,
            scratch_shapes=[whole],
            compiler_params=params(24),
            name="split_again",
        )(jnp.concatenate([first, second]), extra)
        return (latents_grad, *grads)

    flag = layout.bias + 3
    holder = flag // half
    flags = jnp.where(core == holder, mine[flag - holder * half, 0], theirs[flag - holder * half, 0])
    ends = lax.cond(flags.astype(F32) > 0.5, longer_end, usual_end, latents_grad)
    latents_grad, kernel_grad, first_bias, mix_grad, mix_bias, project_grad, project_bias, book, decode, decode_bias = ends
    return (
        decoded,
        latents_grad,
        kernel_grad,
        first_bias.reshape(HALF),
        mix_grad,
        mix_bias.reshape(HALF),
        project_grad.T,
        project_bias.reshape(embed),
        book.T,
        decode,
        decode_bias.reshape(HALF),
    )


def solution(mesh):
    tile = P("dp", None, None, "mp")
    placed = (
        tile,
        P("dp"),
        P("dp", None, None),
        P(None, None, "mp"),
        P("mp"),
        P("mp", None),
        P("mp"),
        P("mp", None),
        P(),
        P(),
        P(None, "mp"),
        P("mp"),
        tile,
    )
    outs = (
        tile,
        tile,
        P(None, None, "mp"),
        P("mp"),
        P("mp", None),
        P("mp"),
        P("mp", None),
        P(),
        P(),
        P(None, "mp"),
        P("mp"),
    )
    return jax.shard_map(local, mesh=mesh, in_specs=placed, out_specs=outs, check_vma=False)
```

```python
import functools

import jax
import jax.numpy as jnp
from jax import lax
from jax.experimental import pallas as pl
from jax.experimental.pallas import tpu as pltpu
from jax.sharding import PartitionSpec as P

SIDE = 16
HALF = 128
LEAD = 16
BLOCK = 32
TILE = 32
MARK = 1e9
GELU_SCALE = 0.7978845608028654
GELU_CUBE = 0.044715
COMMIT = 0.25
F32 = jnp.float32
BF16 = jnp.bfloat16
ANY = pl.BlockSpec(memory_space=pl.ANY)
SMEM = pl.BlockSpec(memory_space=pltpu.SMEM)
HBM = pl.BlockSpec(memory_space=pltpu.HBM)
VMEM = pl.BlockSpec(memory_space=pltpu.VMEM)
MIB = 1 << 20

NT = (((1,), (1,)), ((), ()))
TN = (((0,), (0,)), ((), ()))
NN = (((1,), (0,)), ((), ()))


def dot(a, b, dims=NN):
    return lax.dot_general(a, b, dims, preferred_element_type=F32)


def one_hot_columns(codes, code_of):
    return jnp.where(code_of == codes.astype(jnp.int16), jnp.bfloat16(1), jnp.bfloat16(0))


def numbers(count, width):
    return lax.broadcasted_iota(jnp.int32, (count, width), 0).astype(jnp.int16)


def shape(dims, kind):
    return jax.ShapeDtypeStruct(dims, kind)


def params(mib):
    return pltpu.CompilerParams(vmem_limit_bytes=mib * MIB)


def cost(flops, moved, slow=0):
    return pl.CostEstimate(flops=flops, bytes_accessed=moved, transcendentals=slow)


class Plan:
    def __init__(self, images):
        self.images = images
        longest = images * SIDE // 2 + SIDE // 2
        part = images // 8
        self.chunks = [19 * part, 29 * part]
        self.usual = len(self.chunks)
        rest = longest - sum(self.chunks)
        self.chunks.append(rest)
        self.starts = [sum(self.chunks[:k]) for k in range(len(self.chunks))]
        self.total = sum(self.chunks)
        self.packed = -(-(LEAD + longest + self.total + LEAD) // SIDE) * SIDE
        self.rows, self.block = [], []
        for k, c in enumerate(self.chunks):
            block = BLOCK if k < self.usual else SIDE
            most = 1 + c + 15 + c // 4 + 1
            self.rows.append(-(-most // block) * block)
            self.block.append(block)
        self.live = -(-(LEAD + images * SIDE) // BLOCK) * BLOCK
        self.packed = max(self.packed, self.live)
        self.covered = sum(self.chunks[: self.usual])


def meta_size(plan):
    return plan.images + len(plan.chunks) + 1 + 6


def plan_rows(plan, heights, place, meta):
    images = plan.images
    base = images + len(plan.chunks) + 1

    def total_of(b, acc):
        return acc + heights[b]

    total = lax.fori_loop(0, images, total_of, jnp.int32(0))

    def split_of(b, state):
        acc, best, split, cut = state
        acc = acc + heights[b]
        worst = jnp.maximum(acc, total - acc)
        better = worst < best
        return (acc, jnp.where(better, worst, best), jnp.where(better, b + 1, split), jnp.where(better, acc, cut))

    _, _, split, cut = lax.fori_loop(0, images, split_of, (jnp.int32(0), jnp.int32(1 << 20), jnp.int32(0), jnp.int32(0)))
    mine = place[0]
    own_first = jnp.where(mine == 0, 0, split)
    own_last = jnp.where(mine == 0, split, images)
    own_row = jnp.where(mine == 0, 0, cut)
    send_row = jnp.where(mine == 0, cut, 0)
    for k in range(len(plan.chunks) + 1):
        meta[images + k] = own_first
    ends = [plan.starts[k] + plan.chunks[k] for k in range(len(plan.chunks))]

    def place_of(b, acc):
        meta[b] = acc - own_row
        acc = acc + heights[b]
        end = acc - own_row
        inside = jnp.logical_and(b >= own_first, b < own_last)
        step = jnp.int32(0)
        for k in range(len(plan.chunks) - 1):
            step = step + (end > ends[k]).astype(jnp.int32)

        @pl.when(inside)
        def _():
            meta[images + 1 + step] = b + 1

        return acc

    lax.fori_loop(0, images, place_of, jnp.int32(0))
    for k in range(len(plan.chunks)):
        meta[images + k + 1] = jnp.maximum(meta[images + k + 1], meta[images + k])
    meta[base] = own_row
    meta[base + 1] = send_row
    meta[base + 2] = own_first
    meta[base + 3] = own_last
    meta[base + 4] = jnp.maximum(cut, total - cut)
    meta[base + 5] = total


def pack_rows(plan, meta, source, packed, piece, count):
    base = plan.images + len(plan.chunks) + 1

    def one(i, carry):
        b = piece * count + i
        row = meta[b] + meta[base] + LEAD
        packed[pl.ds(row, SIDE)] = source[b]
        return carry

    lax.fori_loop(0, count, one, 0)


def pack_latents(plan, heights, place, x_hbm, meta, own, *rest):
    n = len(plan.chunks)
    sends, (x_in, packed, sem_in, sem_out) = rest[:n], rest[n:]
    pieces = 8
    count = plan.images // pieces
    fetch = []
    for p in range(pieces):
        part = pl.ds(p * count, count)
        fetch.append(pltpu.make_async_copy(x_hbm.at[part], x_in.at[part], sem_in.at[p]))
        fetch[-1].start()
    plan_rows(plan, heights, place, meta)
    base = plan.images + n + 1
    for p in range(pieces):
        fetch[p].wait()
        pack_rows(plan, meta, x_in, packed, p, count)
    copies = []
    for k in range(n):
        part = pl.ds(LEAD + meta[base + 1] + plan.starts[k], plan.chunks[k])
        copies.append(pltpu.make_async_copy(packed.at[part], sends[k], sem_out.at[k]))
        copies[-1].start()
    copies.append(pltpu.make_async_copy(packed.at[pl.ds(meta[base], LEAD + plan.total)], own, sem_out.at[n]))
    copies[-1].start()
    for copy in copies:
        copy.wait()


def pack_code_grads(plan, meta, og_hbm, *rest):
    n = len(plan.chunks)
    sources, (own, small, rows_out), rest = rest[:5], rest[5:8], rest[8:]
    sends, rest = rest[:n], rest[n:]
    og_in, packed, sem_in, sem_small = rest[:4]
    held = rest[4:]
    small_fetch = []
    for i in range(5):
        small_fetch.append(pltpu.make_async_copy(sources[i], held[i], sem_small.at[i]))
        small_fetch[-1].start()
    decode_w, weight_mix, project_t, bias_first, bias_mix = held
    pieces = 8
    count = plan.images // pieces
    fetch = []
    for p in range(pieces):
        part = pl.ds(p * count, count)
        fetch.append(pltpu.make_async_copy(og_hbm.at[part], og_in.at[part], sem_in.at[p]))
        fetch[-1].start()
    base = plan.images + n + 1

    def clear(i, carry):
        packed[pl.ds(i * SIDE, SIDE)] = jnp.zeros((SIDE, SIDE, HALF), BF16)
        return carry

    lax.fori_loop(0, packed.shape[0] // SIDE, clear, 0)
    for copy in small_fetch:
        copy.wait()
    side = HALF // 2
    small[0:HALF] = weight_mix[:, :HALF]
    small[HALF : 2 * HALF] = weight_mix[:, HALF:]
    small[2 * HALF : 2 * HALF + side] = project_t[...]
    which = lax.broadcasted_iota(jnp.int32, (SIDE, HALF), 0)
    first, second = bias_first[...].astype(F32), bias_mix[...].astype(F32)
    first = jnp.where(which == 0, first, jnp.where(which == 1, second, 0.0))
    small[2 * HALF + side : 2 * HALF + side + SIDE] = first.astype(BF16)
    w = decode_w[...]
    blank = jnp.zeros_like(w)
    upper = jnp.concatenate([w, blank], axis=0)
    lower = jnp.concatenate([blank, w], axis=0)
    for p in range(pieces):
        fetch[p].wait()
        pack_rows(plan, meta, og_in, packed, p, count)
    leaving = pltpu.make_async_copy(packed.at[pl.ds(0, rows_out.shape[0])], rows_out, sem_small.at[5])
    leaving.start()
    for k in range(n):
        half = plan.chunks[k] // 2
        for which in range(2):
            row = LEAD + meta[base + 1 - which] + plan.starts[k]
            a = packed[pl.ds(row, half)].reshape(half * SIDE, HALF)
            b = packed[pl.ds(row + half, half)].reshape(half * SIDE, HALF)
            both = dot(a, upper, NT) + dot(b, lower, NT)
            both = both.reshape(half, SIDE, HALF)
            if which == 0:
                sends[k][...] = both.astype(BF16)
            else:
                own[pl.ds(plan.starts[k] // 2, half)] = both
    leaving.wait()


def prepare_weights(place, kernel, far_kernel, small, far_small, bias_code, codebook_t, forward, backward, mix, project, bias, book):
    first = pl.multiple_of(place[0] * HALF, HALF)
    order = (first, HALF - first)
    for tap in range(9):
        for d, source in enumerate((kernel, far_kernel)):
            for c in range(2):
                tile = source[tap, pl.ds(order[c], HALF), :]
                row = tap * 2 * HALF
                forward[row + c * HALF : row + (c + 1) * HALF, d * HALF : (d + 1) * HALF] = tile
                backward[row + d * HALF : row + (d + 1) * HALF, c * HALF : (c + 1) * HALF] = tile.T
    blank = jnp.zeros((HALF, HALF // 2), BF16)
    for d, source in enumerate((small, far_small)):
        rows = pl.ds(d * HALF, HALF)
        for c in range(2):
            mix[rows, c * HALF : (c + 1) * HALF] = source[pl.ds(order[c], HALF), :]
        part = source[2 * HALF : 2 * HALF + HALF // 2, :].T
        project[0, rows, :] = jnp.concatenate([part, blank], axis=1)
        project[1, rows, :] = jnp.concatenate([blank, part], axis=1)
        bias[0:8, d * HALF : (d + 1) * HALF] = source[2 * HALF + HALF // 2 : 2 * HALF + HALF // 2 + SIDE, :].astype(F32)[0:8]
    code = bias_code[...].astype(F32)
    code = jnp.concatenate([code, code], axis=1)
    bias[8:16, :] = jnp.broadcast_to(jnp.concatenate([code, code], axis=1), (8, 2 * HALF))
    book[...] = jnp.concatenate([codebook_t[...], codebook_t[...]], axis=0)


def sum_codes(plan, meta, heights, codes, rows_hbm, codebook_t, grads, rows, code_rows, hot, sums, sem):
    fetch = pltpu.make_async_copy(rows_hbm, rows, sem)
    fetch.start()
    sums[...] = jnp.zeros_like(sums)
    code_rows[...] = jnp.full(code_rows.shape, -1, jnp.int32)
    base = plan.images + len(plan.chunks) + 1

    def put(b, carry):
        put_codes(code_rows, codes, b, heights[b], meta[b] + meta[base] + LEAD)
        return carry

    lax.fori_loop(0, plan.images, put, 0)
    fetch.wait()
    code_of = numbers(codebook_t.shape[1], HALF)
    spots = BLOCK * SIDE
    per_block = spots // HALF
    half = sums.shape[0] // 2

    def add(j, carry):
        cot = rows[pl.ds(j * BLOCK, BLOCK)].reshape(spots, HALF)
        for i in range(per_block):
            hot[:, i * HALF : (i + 1) * HALF] = one_hot_columns(code_rows[pl.ds(j * per_block + i, 1), :], code_of)
        for h in (0, half):
            sums[h : h + half] += dot(hot[h : h + half], cot)
        return carry

    lax.fori_loop(0, (LEAD + meta[base + 5] + BLOCK - 1) // BLOCK, add, 0)
    total = sums[...]
    book = codebook_t[...].astype(F32)
    w = lax.dot_general(book, total, NN, precision=lax.Precision.HIGHEST, preferred_element_type=F32)
    bias = jnp.sum(total, axis=0, keepdims=True)
    embed = w.shape[0]
    grads[0:embed] = w
    grads[embed : embed + 8] = jnp.broadcast_to(bias, (8, HALF))


def decode_images(plan, steps, heights, codes, codebook_t, decode_w, decode_b, _, decoded, token, table):
    step = pl.program_id(0)
    token[...] = jnp.zeros_like(token)
    group = plan.images // steps

    @pl.when(step == 0)
    def _():
        full = dot(codebook_t[...], decode_w[...], TN) + decode_b[...].astype(F32)
        table[...] = full.T.astype(BF16)

    spots = SIDE * SIDE
    code_of = numbers(codebook_t.shape[1], spots)
    spot = lax.broadcasted_iota(jnp.int32, (spots, 1), 0)
    for i in range(group):
        live = heights[step * group + i] * SIDE
        out = dot(table[...], one_hot_columns(codes[i : i + 1, :], code_of)).T
        decoded[i] = jnp.where(spot < live, out, 0.0).astype(BF16).reshape(SIDE, SIDE, HALF)


def put_codes(code_rows, codes, b, height, dst):
    spot = lax.broadcasted_iota(jnp.int32, (1, SIDE * SIDE), 1)
    lane = lax.broadcasted_iota(jnp.int32, (1, HALF), 1)
    per_row = HALF // SIDE
    row = jnp.where(spot < height * SIDE, codes[pl.ds(b, 1), :], -1)
    turn = lax.rem(dst, per_row) * SIDE
    upper = pltpu.roll(row[:, :HALF], turn, 1)
    lower = pltpu.roll(row[:, HALF:], turn, 1)
    inside = lane >= turn
    pieces = (jnp.where(inside, upper, -1), jnp.where(inside, lower, upper), jnp.where(inside, -1, lower))
    for i, piece in enumerate(pieces):
        target = pl.ds(dst // per_row + i, 1)
        code_rows[target, :] = jnp.where(piece < 0, code_rows[target, :], piece)


def gelu_parts(v):
    square = v * v
    t = jnp.tanh(v * (GELU_SCALE + (GELU_SCALE * GELU_CUBE) * square))
    half = 0.5 + 0.5 * t
    slope = half + (0.5 * v) * (1.0 - t * t) * (GELU_SCALE + (3.0 * GELU_SCALE * GELU_CUBE) * square)
    return v * half, slope


def main_step(plan, layout, k, waits, *refs):
    first_step = k == 0
    fresh = k in (0, plan.usual)
    final = k == plan.usual - 1
    refs = list(refs[waits:])

    def take(count):
        got = refs[:count]
        del refs[:count]
        return got

    if final:
        place, decode_acc = take(2)
    meta, heights, x_own, x_far, q_own, q_far, codes = take(7)
    kernel_hbm, kernel_t_hbm, mix, project, bias, book = take(6)
    if not first_step:
        x_past, q_past, carry_own, carry_far = take(4)
    if not fresh:
        past_accs = take(5)
    win_own, win_far, next_own, next_far = take(4)
    if final:
        laid_out = take(3)
    if not final:
        sums_out = take(5)
    kernel_acc, mix_acc, project_acc, book_acc, bias_acc = take(5)
    if final:
        laid_out += take(2)
    kernel, kernel_t, weight_sems = take(3)
    xo, xf, qo, qf, qd, xc_o, xc_f, qc, code_rows, act3, slope_x, grad3, block_g, out_o, out_f = take(15)
    second_s, slope_s, low_s, mixed_s, code_s, hot_s, found_s, diff_s, sems = refs

    chunk, start = plan.chunks[k], plan.starts[k]
    images, rows, block = plan.images, plan.rows[k], plan.block[k]
    half = chunk // 2
    spots = block * SIDE
    low = meta[images + k]
    high = meta[images + k + 1]

    copies = [
        (x_own.at[pl.ds(start, LEAD + chunk)], xo.at[pl.ds(0, LEAD + chunk)]),
        (x_far, xf.at[pl.ds(LEAD, chunk)]),
        (q_own.at[pl.ds(start // 2, half)], qo.at[pl.ds(LEAD, half)]),
        (q_far, qf.at[pl.ds(LEAD, half)]),
    ]
    if not first_step:
        past = plan.chunks[k - 1]
        copies += [
            (x_past.at[pl.ds(past - LEAD, LEAD)], xf.at[pl.ds(0, LEAD)]),
            (q_own.at[pl.ds(start // 2 - LEAD, LEAD)], qo.at[pl.ds(0, LEAD)]),
            (q_past.at[pl.ds(past // 2 - LEAD, LEAD)], qf.at[pl.ds(0, LEAD)]),
        ]
    accs = (mix_acc, project_acc, book_acc, bias_acc, kernel_acc)
    early = len(copies)
    if not fresh:
        copies += list(zip(past_accs[1:] + past_accs[:1], accs))
    weight_copies = []
    for i, (source, target) in enumerate(((kernel_hbm, kernel), (kernel_t_hbm, kernel_t))):
        weight_copies.append(pltpu.make_async_copy(source, target, weight_sems.at[i]))
    started = []
    for i, (source, target) in enumerate(copies):
        started.append(pltpu.make_async_copy(source, target, sems.at[i]))
        started[-1].start()
    for copy in weight_copies:
        copy.start()
    started, later = started[:early], started[early:]

    if fresh:
        for acc in accs:
            acc[...] = jnp.zeros(acc.shape, F32)
    if first_step:
        out_o[0:LEAD] = jnp.zeros((LEAD, SIDE, HALF), BF16)
        out_f[0:LEAD] = jnp.zeros((LEAD, SIDE, HALF), BF16)
    else:
        out_o[0:LEAD] = carry_own[...]
        out_f[0:LEAD] = carry_far[...]

    blank = jnp.zeros((SIDE, SIDE, HALF), BF16)
    no_row = jnp.full((SIDE, SIDE, HALF), MARK, F32)
    code_rows[...] = jnp.full(code_rows.shape, -1, jnp.int32)
    for r in range(0, rows + 2 * block, SIDE):
        part = pl.ds(r, SIDE)
        xc_o[part] = blank
        xc_f[part] = blank
        if r < rows:
            qc[part] = no_row
    for copy in started:
        copy.wait()

    lane3 = lax.broadcasted_iota(jnp.int32, (1, SIDE, HALF), 2) < HALF // 2

    def spread(r0, count):
        both = (qo[pl.ds(r0, count)] + qf[pl.ds(r0, count)].astype(F32)).reshape(count * SIDE, HALF)
        turned = pltpu.roll(both, HALF // 2, 1).reshape(count, SIDE, HALF)
        both = both.reshape(count, SIDE, HALF)
        return jnp.where(lane3, both, turned), jnp.where(lane3, turned, both)

    upper, lower = spread(LEAD, half)
    qd[pl.ds(LEAD, half)] = upper
    qd[pl.ds(LEAD + half, half)] = lower
    if not first_step:
        _, lower = spread(0, LEAD)
        qd[0:LEAD] = lower

    per_row = HALF // SIDE

    def put(b, dst):
        src = meta[b] - start + LEAD
        xc_o[pl.ds(dst, SIDE)] = xo[pl.ds(src, SIDE)]
        xc_f[pl.ds(dst, SIDE)] = xf[pl.ds(src, SIDE)]
        qc[pl.ds(dst, SIDE)] = qd[pl.ds(src, SIDE)]
        end = dst + heights[b]
        xc_o[pl.ds(end, SIDE)] = blank
        xc_f[pl.ds(end, SIDE)] = blank
        qc[pl.ds(end, SIDE)] = no_row
        put_codes(code_rows, codes, b, heights[b], dst)
        return end + 1

    used = lax.fori_loop(low, high, put, jnp.int32(1))
    blocks = jnp.where(high > low, (used + (block - 1)) // block, 0)

    column = lax.rem(lax.broadcasted_iota(jnp.int32, (TILE, 1), 0), SIDE)
    not_first = column != 0
    not_last = column != SIDE - 1

    def shifted(value):
        back = jnp.where(not_first, pltpu.roll(value, 1, 0), 0.0)
        ahead = jnp.where(not_last, pltpu.roll(value, TILE - 1, 0), 0.0)
        return back.astype(BF16), ahead.astype(BF16)

    edge = jnp.zeros((SIDE, 3 * 2 * HALF), BF16)
    act3[0:SIDE] = edge
    grad3[0:SIDE] = edge
    beyond = pl.multiple_of((blocks * block + 1) * SIDE, SIDE)
    grad3[pl.ds(beyond, SIDE)] = edge

    tiles = range(0, spots, TILE)

    def read_x(r0, t):
        part = pl.ds(r0 + t // SIDE, TILE // SIDE)
        o = xc_o[part].reshape(TILE, HALF)
        f = xc_f[part].reshape(TILE, HALF)
        return jnp.concatenate([o, f], axis=1).astype(F32)

    def at(row, count=block):
        return pl.ds(pl.multiple_of(row * SIDE, SIDE), count * SIDE)

    def tile_at(row, t):
        return pl.ds(pl.multiple_of(row * SIDE, SIDE) + t, TILE)

    def activate(j, carry):
        r0 = j * block
        for t in tiles:
            value, slope = gelu_parts(read_x(r0, t))
            slope_x[tile_at(r0, t), :] = slope
            back, ahead = shifted(value)
            act3[tile_at(r0 + 1, t), 0 : 2 * HALF] = back
            act3[tile_at(r0 + 1, t), 2 * HALF : 4 * HALF] = value.astype(BF16)
            act3[tile_at(r0 + 1, t), 4 * HALF : 6 * HALF] = ahead
        return carry

    fused = k < plan.usual
    lax.fori_loop(0, 2 if fused else blocks + 1, activate, 0)
    for copy in later:
        copy.wait()
    for copy in weight_copies:
        copy.wait()

    bias_first = bias[0:1, :]
    bias_mix = bias[1:2, :]
    bias_code = bias[8:9, 0:HALF]
    lane = lax.broadcasted_iota(jnp.int32, (1, HALF), 1) < HALF // 2
    hb = block // 2
    hs = hb * SIDE

    def add_rows(total, value):
        value = value.astype(F32)
        for i in range(0, value.shape[0], 8):
            part = value[i : i + 8]
            total = part if total is None else total + part
        return total

    half_tiles = range(0, hs, TILE)
    code_of = numbers(book_acc.shape[0], HALF)
    halves = (0, hs)

    def middle(j, carry):
        r0 = j * block
        for i in range(block // per_row):
            row = code_rows[pl.ds(j * (block // per_row) + i, 1), :]
            hot_s[:, i * HALF : (i + 1) * HALF] = one_hot_columns(row, code_of)
        for h in halves:
            found_s[h : h + hs] = dot(book[...], hot_s[:, h : h + hs]).astype(BF16).T
        pre = []
        for h in halves:
            window = jnp.concatenate([act3[at(r0 + i + h // SIDE, hb), :] for i in range(3)], axis=1)
            pre.append(dot(window, kernel[...]))
        for h, part in zip(halves, pre):
            for t in half_tiles:
                value, slope = gelu_parts(part[t : t + TILE] + bias_first)
                second_s[h + t : h + t + TILE] = value.astype(BF16)
                slope_s[h + t : h + t + TILE] = slope
        mixed = [dot(second_s[h : h + hs], mix[...]) for h in halves]
        for h, part in zip(halves, mixed):
            for t in half_tiles:
                low_s[h + t : h + t + TILE] = (read_x(r0, h + t) + part[t : t + TILE] + bias_mix).astype(BF16)
        latents = [dot(low_s[h : h + hs], project[i]) for i, h in enumerate(halves)]
        total = None
        for t in half_tiles:
            first = pl.ds(r0 + t // SIDE, TILE // SIDE)
            other = pl.ds(r0 + hb + t // SIDE, TILE // SIDE)
            ch = jnp.where(lane, found_s[t : t + TILE].astype(F32), found_s[hs + t : hs + t + TILE].astype(F32))
            q = jnp.where(lane3, qc[first], qc[other]).reshape(TILE, HALF)
            live = q < 0.5 * MARK
            latent = latents[0][t : t + TILE] + latents[1][t : t + TILE] + bias_code
            diff = jnp.where(live, latent - ch, 0.0)
            code_grad = jnp.where(live, q + (2.0 * COMMIT) * diff, 0.0).astype(BF16)
            code_s[t : t + TILE] = code_grad
            total = add_rows(total, code_grad)
            big = diff.astype(BF16).astype(F32)
            small = diff - big
            turned = pltpu.roll(small, HALF // 2, 1)
            diff_s[t : t + TILE] = jnp.where(lane, big, turned).astype(BF16)
            turned = pltpu.roll(big, HALF // 2, 1)
            diff_s[hs + t : hs + t + TILE] = jnp.where(lane, turned, small).astype(BF16)
        bias_acc[16:24, 0:HALF] += total
        total = None
        blocks_g = [dot(code_s[...], project[i], NT) for i in range(2)]
        for h, part in zip(halves, blocks_g):
            for t in half_tiles:
                block_g[tile_at(r0, h + t), :] = part[t : t + TILE]
                mixed_grad = part[t : t + TILE].astype(BF16)
                mixed_s[h + t : h + t + TILE] = mixed_grad
                total = add_rows(total, mixed_grad)
        bias_acc[8:16] += total
        second_grad = [dot(mixed_s[h : h + hs], mix[...], NT) for h in halves]
        total = None
        for h, part in zip(halves, second_grad):
            for t in half_tiles:
                first_grad = slope_s[h + t : h + t + TILE] * part[t : t + TILE]
                back, ahead = shifted(first_grad)
                first_low = first_grad.astype(BF16)
                grad3[tile_at(r0 + 1, h + t), 0 : 2 * HALF] = ahead
                grad3[tile_at(r0 + 1, h + t), 2 * HALF : 4 * HALF] = first_low
                grad3[tile_at(r0 + 1, h + t), 4 * HALF : 6 * HALF] = back
                total = add_rows(total, first_low)
        bias_acc[0:8] += total
        book_acc[...] += dot(hot_s[...], diff_s[...])
        mix_acc[...] += dot(second_s[...], mixed_s[...], TN)
        project_acc[...] += jnp.where(lane, dot(low_s[0:hs], code_s[...], TN), dot(low_s[hs:], code_s[...], TN))
        return carry

    def finish(j, carry):
        r0 = j * block
        active = act3[at(r0 + 1), 2 * HALF : 4 * HALF].T
        for i in range(3):
            kernel_acc[:, i * 6 * HALF : (i + 1) * 6 * HALF] += dot(active, grad3[at(r0 + 2 - i), :])
        grads = []
        for h in halves:
            window = jnp.concatenate([grad3[at(r0 + 2 - i + h // SIDE, hb), :] for i in range(3)], axis=1)
            grads.append(dot(window, kernel_t[...]))
        for h, grad in zip(halves, grads):
            for t in half_tiles:
                here = tile_at(r0, h + t)
                out = (block_g[here, :] + slope_x[here, :] * grad[t : t + TILE]).astype(BF16)
                part = pl.ds(r0 + (h + t) // SIDE, TILE // SIDE)
                xc_o[part] = out[:, :HALF].reshape(TILE // SIDE, SIDE, HALF)
                xc_f[part] = out[:, HALF:].reshape(TILE // SIDE, SIDE, HALF)
        return carry

    def opening(j, carry):
        middle(j, carry)
        return activate(j + 2, carry)

    def steady(j, carry):
        finish(j - 2, carry)
        middle(j, carry)
        return activate(j + 2, carry)

    if fused:
        lax.fori_loop(0, jnp.minimum(blocks, 2), opening, 0)
        lax.fori_loop(2, blocks, steady, 0)
        lax.fori_loop(jnp.maximum(blocks - 2, 0), blocks, finish, 0)
    else:
        lax.fori_loop(0, blocks, middle, 0)
        lax.fori_loop(0, blocks, finish, 0)
    leaving = []
    if not final:
        leaving += list(zip((kernel_acc, mix_acc, project_acc, book_acc, bias_acc), sums_out))
        for i, (source, target) in enumerate(leaving):
            leaving[i] = pltpu.make_async_copy(source, target, sems.at[i])
            leaving[i].start()

    def collect(b, src):
        dst = meta[b] - start + LEAD
        out_o[pl.ds(dst, SIDE)] = xc_o[pl.ds(src, SIDE)]
        out_f[pl.ds(dst, SIDE)] = xc_f[pl.ds(src, SIDE)]
        return src + heights[b] + 1

    lax.fori_loop(low, high, collect, jnp.int32(1))
    size = win_own.shape[0]
    windows = (
        (out_o.at[pl.ds(0, size)], win_own),
        (out_f.at[pl.ds(0, size)], win_far),
        (out_o.at[pl.ds(chunk, LEAD)], next_own),
        (out_f.at[pl.ds(chunk, LEAD)], next_far),
    )
    for i, (source, target) in enumerate(windows):
        leaving.append(pltpu.make_async_copy(source, target, sems.at[5 + i]))
        leaving[-1].start()
    if final:
        sums = (kernel_acc, mix_acc, project_acc, book_acc, bias_acc, decode_acc)
        leaving += gather_grads(plan, layout, place, meta, sums, *laid_out, sems)
    for copy in leaving:
        copy.wait()


class Layout:
    def __init__(self, devices, book_rows, embed):
        self.mix = 9 * 2 * HALF
        self.project = self.mix + 2 * HALF
        self.book = self.project + HALF // 2
        self.bias = self.book + book_rows // 2
        self.decode = self.bias + 8
        used = self.decode + embed + 8
        self.devices = devices
        self.piece = -(-used // (devices * SIDE)) * SIDE
        self.rows = self.piece * devices
        self.half = self.rows // 2
        self.used = used


def lay_out(layout, swap, kernel_acc, mix_acc, project_acc, book_acc, bias_acc, decode_acc, own, far):
    def lanes(value):
        return value[:, :HALF], value[:, HALF:]

    def order(first, second):
        return jnp.where(swap, second, first), jnp.where(swap, first, second)

    row = 0
    for tap in range(9):
        block = kernel_acc[:, tap * 2 * HALF : (tap + 1) * 2 * HALF]
        mine, theirs = lanes(block)
        a, b = order(mine[:HALF], mine[HALF:])
        own[row : row + HALF] = a
        own[row + HALF : row + 2 * HALF] = b
        a, b = order(theirs[:HALF], theirs[HALF:])
        far[row : row + HALF] = a
        far[row + HALF : row + 2 * HALF] = b
        row += 2 * HALF
    row = layout.mix
    for target, part in ((own, mix_acc[:HALF]), (far, mix_acc[HALF:])):
        a, b = order(*lanes(part))
        target[row : row + HALF] = a
        target[row + HALF : row + 2 * HALF] = b
    row = layout.project
    side = HALF // 2
    for target, part in ((own, project_acc[:HALF]), (far, project_acc[HALF:])):
        part = part + pltpu.roll(part, side, 1)
        target[row : row + side] = part.T[:side]
    row = layout.book
    book = book_acc[...]
    book = -2.0 * (book + pltpu.roll(book, side, 1))
    book = book.T[:side]
    for c in range(book.shape[1] // HALF):
        part = book[:, c * HALF : (c + 1) * HALF]
        own[row + c * side : row + (c + 1) * side] = part
        far[row + c * side : row + (c + 1) * side] = part
    row = layout.bias
    sums = [jnp.sum(bias_acc[8 * i : 8 * i + 8], axis=0, keepdims=True) for i in range(3)]
    code = sums[2][:, :HALF]
    code = code + pltpu.roll(code, side, 1)
    which = lax.broadcasted_iota(jnp.int32, (8, HALF), 0)
    for target, first in ((own, 0), (far, HALF)):
        part = jnp.where(which == 0, sums[0][:, first : first + HALF], sums[1][:, first : first + HALF])
        target[row : row + 8] = jnp.where(which == 2, code, jnp.where(which < 2, part, 0.0))
    row = layout.decode
    rest = layout.rows - row
    own[row:] = jnp.zeros((rest, HALF), F32)
    far[row:] = jnp.zeros((rest, HALF), F32)
    if decode_acc is not None:
        own[row : row + decode_acc.shape[0]] = decode_acc[...]


def gather_plain(layout, place, *refs):
    lay_out(layout, place[0] == 1, *refs[:5], None, *refs[5:])


def gather_grads(plan, layout, place, meta, accs, keep_own, keep_far, send, own, far, sems):
    lay_out(layout, place[0] == 1, *accs, own, far)
    base = plan.images + len(plan.chunks) + 1
    over = (meta[base + 4] > plan.covered).astype(F32)
    which = lax.broadcasted_iota(jnp.int32, (8, HALF), 0)
    row = layout.bias
    own[row : row + 8] = jnp.where(which == 3, over, own[row : row + 8])
    half = layout.half
    mine = pl.ds(pl.multiple_of(place[1] * half, SIDE), half)
    other = pl.ds(pl.multiple_of((1 - place[1]) * half, SIDE), half)
    kept = []
    for i, (source, target) in enumerate(((own, keep_own), (far, keep_far))):
        kept.append(pltpu.make_async_copy(source.at[mine, :], target, sems.at[9 + i]))
        kept[-1].start()
    send[0] = own[other, :].astype(BF16)
    send[1] = far[other, :].astype(BF16)
    return kept


def hold(value, _, out):
    pass


def add_far(keep_far, came, out):
    out[...] = (keep_far[...] + came[1].astype(F32)).astype(BF16)


def add_own(keep_own, came, came_far, out, token):
    token[...] = jnp.zeros_like(token)
    total = keep_own[...] + came[0].astype(F32) + came_far[...].astype(F32)
    out[...] = total.astype(BF16).reshape(out.shape)


def add_pieces(pieces, *rest):
    out = rest[-1]
    total = pieces[0].astype(F32)
    for i in range(1, pieces.shape[0]):
        total = total + pieces[i].astype(F32)
    out[...] = jnp.broadcast_to(total.astype(BF16)[None], out.shape)


def write_grads(layout, place, mine, theirs, kernel, first_bias, mix, mix_bias, project, project_bias, book, decode, decode_bias, whole):
    half = layout.half
    whole[pl.ds(pl.multiple_of(place[1] * half, SIDE), half), :] = mine[...].astype(F32)
    whole[pl.ds(pl.multiple_of((1 - place[1]) * half, SIDE), half), :] = theirs[...].astype(F32)
    split_grads(layout, whole, kernel, first_bias, mix, mix_bias, project, project_bias, book, decode, decode_bias)


def split_grads(layout, whole, kernel, first_bias, mix, mix_bias, project, project_bias, book, decode, decode_bias):
    for tap in range(9):
        kernel[tap] = whole[tap * 2 * HALF : (tap + 1) * 2 * HALF]
    row = layout.mix
    mix[:, :HALF] = whole[row : row + HALF]
    mix[:, HALF:] = whole[row + HALF : row + 2 * HALF]
    side = HALF // 2
    for row, target in ((layout.project, project), (layout.book, book)):
        for c in range(target.shape[1] // HALF):
            target[:, c * HALF : (c + 1) * HALF] = whole[row + c * side : row + (c + 1) * side]
    row = layout.bias
    first_bias[...] = whole[row : row + 1]
    mix_bias[...] = whole[row + 1 : row + 2]
    project_bias[...] = whole[row + 2 : row + 3, :side]
    row = layout.decode
    n = decode.shape[0]
    decode[...] = whole[row : row + n]
    decode_bias[...] = whole[row + n : row + n + 1]


def split_again(layout, total, extra, *refs):
    whole = refs[-1]
    whole[...] = total[...].astype(F32) + extra[...]
    split_grads(layout, whole, *refs[:-1])


def restore_rows(plan, n, waits, *refs):
    meta, heights, *refs = refs[waits:]
    own, far, out, token = refs[:n], refs[n : 2 * n], refs[2 * n], refs[2 * n + 1]
    token[...] = jnp.zeros_like(token)
    stage_own, stage_far, sems = refs[2 * n + 2 :]
    copies = []
    for k in range(n):
        size = plan.chunks[k] + (LEAD if k == n - 1 else 0)
        for i, (source, target) in enumerate(((own[k], stage_own), (far[k], stage_far))):
            from_rows = source.at[pl.ds(0, size)]
            copies.append(pltpu.make_async_copy(from_rows, target.at[pl.ds(plan.starts[k], size)], sems.at[i, k]))
            copies[-1].start()
    for copy in copies:
        copy.wait()
    base = plan.images + len(plan.chunks) + 1
    own_row, send_row = meta[base], meta[base + 1]
    first, last = meta[base + 2], meta[base + 3]
    row_of = lax.broadcasted_iota(jnp.int32, (SIDE, 1, 1), 0)

    def own_image(b, carry):
        rows = stage_own[pl.ds(meta[b] + LEAD, SIDE)]
        out[b] = jnp.where(row_of < heights[b], rows, jnp.zeros_like(rows))
        return carry

    def far_image(b, carry):
        rows = stage_far[pl.ds(meta[b] + own_row - send_row + LEAD, SIDE)]
        out[b] = jnp.where(row_of < heights[b], rows, jnp.zeros_like(rows))
        return carry

    lax.fori_loop(first, last, own_image, 0)
    lax.fori_loop(0, first, far_image, 0)
    lax.fori_loop(last, plan.images, far_image, 0)


def trade(value):
    return lax.ppermute(value, "mp", [(0, 1), (1, 0)])


def run_main(plan, layout, k, meta, heights, streams, weights, state, waits=(), ending=()):
    chunk, rows, block = plan.chunks[k], plan.rows[k], plan.block[k]
    last = k >= plan.usual - 1
    final = k == plan.usual - 1
    x_own, x_far, q_own, q_far, codes = streams
    book_rows = weights[-1].shape[1]
    args = [*waits, *ending, meta, heights, x_own, x_far[k], q_own, q_far[k], codes, *weights]
    specs = [ANY] * len(waits) + ([SMEM, VMEM] if final else [])
    specs += [SMEM, SMEM, ANY, ANY, ANY, ANY, VMEM, ANY, ANY] + [VMEM] * (len(weights) - 2)
    alias = {}
    if state is not None:
        args += [x_far[k - 1], q_far[k - 1], *state]
        specs += [ANY, ANY, VMEM, VMEM] + [ANY] * (len(state) - 2)
        if not final:
            for i in range(len(state) - 2):
                alias[len(args) - 5 + i] = 4 + i
    size = chunk + LEAD if last else chunk
    tile = (SIDE, HALF)
    outs = [shape((size,) + tile, BF16)] * 2 + [shape((LEAD,) + tile, BF16)] * 2
    sums = [(2 * HALF, 18 * HALF), (2 * HALF, 2 * HALF), (2 * HALF, HALF), (book_rows, HALF), (24, 2 * HALF)]
    scratch = [pltpu.VMEM(dims, F32) for dims in sums]
    out_specs = [ANY] * 4
    if final:
        outs += [shape((layout.half, HALF), F32)] * 2 + [shape((2, layout.half, HALF), BF16)]
        out_specs += [ANY, ANY, VMEM]
        scratch += [pltpu.VMEM((layout.rows, HALF), F32)] * 2
    else:
        outs += [shape(dims, F32) for dims in sums]
        out_specs += [ANY] * 5
    scratch += [pltpu.VMEM((18 * HALF, 2 * HALF), BF16)] * 2 + [pltpu.SemaphoreType.DMA((2,))]
    half = chunk // 2
    spots = block * SIDE
    scratch += [
        pltpu.VMEM((LEAD + chunk + SIDE,) + tile, BF16),
        pltpu.VMEM((LEAD + chunk + SIDE,) + tile, BF16),
        pltpu.VMEM((LEAD + half,) + tile, F32),
        pltpu.VMEM((LEAD + half,) + tile, BF16),
        pltpu.VMEM((LEAD + chunk + SIDE,) + tile, F32),
        pltpu.VMEM((rows + 2 * block + SIDE,) + tile, BF16),
        pltpu.VMEM((rows + 2 * block + SIDE,) + tile, BF16),
        pltpu.VMEM((rows + 2 * SIDE,) + tile, F32),
        pltpu.VMEM((-(-(rows * SIDE // HALF + 4) // 8) * 8, HALF), jnp.int32),
        pltpu.VMEM(((rows + 2 * block + 2) * SIDE, 6 * HALF), BF16),
        pltpu.VMEM(((rows + 2 * block) * SIDE, 2 * HALF), F32),
        pltpu.VMEM(((rows + 2) * SIDE, 6 * HALF), BF16),
        pltpu.VMEM((rows * SIDE, 2 * HALF), F32),
        pltpu.VMEM((LEAD + chunk + 2 * SIDE,) + tile, BF16),
        pltpu.VMEM((LEAD + chunk + 2 * SIDE,) + tile, BF16),
        pltpu.VMEM((spots, 2 * HALF), BF16),
        pltpu.VMEM((spots, 2 * HALF), F32),
        pltpu.VMEM((spots, 2 * HALF), BF16),
        pltpu.VMEM((spots, 2 * HALF), BF16),
        pltpu.VMEM((spots // 2, HALF), BF16),
        pltpu.VMEM((book_rows, spots), BF16),
        pltpu.VMEM((spots, HALF), BF16),
        pltpu.VMEM((spots, HALF), BF16),
        pltpu.SemaphoreType.DMA((13,)),
    ]
    spots = chunk * SIDE
    return pl.pallas_call(
        functools.partial(main_step, plan, layout, k, len(waits)),
        out_shape=outs,
        in_specs=specs,
        out_specs=out_specs,
        scratch_shapes=scratch,
        input_output_aliases=alias,
        compiler_params=params(58),
        cost_estimate=cost(60 * 65536 * spots, 8 * MIB, 2 * 256 * spots),
        name=f"main_{k}",
    )(*args)


def local(
    image_latents,
    image_heights,
    code_index,
    kernel_three,
    bias_three,
    weight_mix,
    bias_mix,
    weight_project,
    bias_project,
    codebook,
    weight_decode,
    bias_decode,
    out_grad,
):
    images = image_latents.shape[0]
    plan = Plan(images)
    n = len(plan.chunks)
    tile = (SIDE, HALF)
    where = lax.axis_index("mp").astype(jnp.int32)
    core = lax.rem(lax.axis_index("dp").astype(jnp.int32), 2)
    spot = place = jnp.stack([where, core])

    packed = pl.pallas_call(
        functools.partial(pack_latents, plan),
        out_shape=[
            shape((meta_size(plan),), jnp.int32),
            shape((LEAD + plan.total,) + tile, BF16),
        ]
        + [shape((c,) + tile, BF16) for c in plan.chunks],
        in_specs=[SMEM, SMEM, HBM],
        out_specs=[SMEM, ANY] + [ANY] * n,
        scratch_shapes=[
            pltpu.VMEM((images, SIDE) + tile, BF16),
            pltpu.VMEM((plan.packed + SIDE,) + tile, BF16),
            pltpu.SemaphoreType.DMA((8,)),
            pltpu.SemaphoreType.DMA((n + 1,)),
        ],
        compiler_params=params(60),
        cost_estimate=cost(0, 12 * MIB),
        name="pack_latents",
    )(image_heights, place, image_latents)
    meta, x_own, x_send = packed[0], packed[1], packed[2:]

    packed = pl.pallas_call(
        functools.partial(pack_code_grads, plan),
        out_shape=[shape((plan.total // 2,) + tile, F32), shape((2 * HALF + HALF // 2 + SIDE, HALF), BF16)]
        + [shape((plan.live,) + tile, BF16)]
        + [shape((c // 2,) + tile, BF16) for c in plan.chunks],
        in_specs=[SMEM] + [HBM] * 6,
        out_specs=[VMEM, VMEM, ANY] + [VMEM] * n,
        scratch_shapes=[
            pltpu.VMEM((images, SIDE) + tile, BF16),
            pltpu.VMEM((plan.packed + SIDE,) + tile, BF16),
            pltpu.SemaphoreType.DMA((8,)),
            pltpu.SemaphoreType.DMA((6,)),
            pltpu.VMEM(weight_decode.shape, BF16),
            pltpu.VMEM(weight_mix.shape, BF16),
            pltpu.VMEM(weight_project.shape[::-1], BF16),
            pltpu.VMEM((1, HALF), BF16),
            pltpu.VMEM((1, HALF), BF16),
        ],
        compiler_params=params(60),
        cost_estimate=cost(2 * 2 * plan.total * SIDE * 256 * 128, 10 * MIB),
        name="pack_code_grads",
    )(meta, out_grad, weight_decode, weight_mix, weight_project.T, bias_three.reshape(1, HALF), bias_mix.reshape(1, HALF))
    q_own, small, live_rows, q_send = packed[0], packed[1], packed[2], packed[3:]

    book_rows, embed = codebook.shape
    codebook_t = codebook.T
    far_kernel = trade(kernel_three)
    far_small = trade(small)
    usual = plan.usual
    x_far, q_far = [], []
    for k in range(usual):
        x_far.append(trade(x_send[k]))
        q_far.append(trade(q_send[k]))

    weights = pl.pallas_call(
        prepare_weights,
        out_shape=[
            shape((18 * HALF, 2 * HALF), BF16),
            shape((18 * HALF, 2 * HALF), BF16),
            shape((2 * HALF, 2 * HALF), BF16),
            shape((2, 2 * HALF, HALF), BF16),
            shape((SIDE, 2 * HALF), F32),
            shape((HALF, book_rows), BF16),
        ],
        in_specs=[SMEM] + [VMEM] * 6,
        out_specs=[VMEM] * 6,
        compiler_params=params(16),
        cost_estimate=cost(0, 5 * MIB),
        name="prepare_weights",
    )(place, kernel_three, far_kernel, small, far_small, bias_project.reshape(1, -1), codebook_t)

    groups = 8
    group = images // groups
    codes = code_index.reshape(images, SIDE * SIDE)
    whole = lambda dims: pl.BlockSpec(dims, lambda g: (0,) * len(dims))
    four = pl.BlockSpec((group, SIDE) + tile, lambda g: (g, 0, 0, 0))
    row = pl.BlockSpec((group, SIDE * SIDE), lambda g: (g, 0))
    decode_acc = pl.pallas_call(
        functools.partial(sum_codes, plan),
        out_shape=shape((embed + 8, HALF), F32),
        in_specs=[SMEM, SMEM, VMEM, ANY, VMEM],
        out_specs=VMEM,
        scratch_shapes=[
            pltpu.VMEM((plan.live,) + tile, BF16),
            pltpu.VMEM((plan.live // 8 + 8, HALF), jnp.int32),
            pltpu.VMEM((book_rows, BLOCK * SIDE), BF16),
            pltpu.VMEM((book_rows, HALF), F32),
            pltpu.SemaphoreType.DMA,
        ],
        compiler_params=params(40),
        cost_estimate=cost(images * 256 * 512 * 256, 5 * MIB),
        name="sum_codes",
    )(meta, image_heights, codes, live_rows, codebook_t)

    def decode(after):
        return pl.pallas_call(
            functools.partial(decode_images, plan, groups),
            grid=(groups,),
            out_shape=[shape((images, SIDE) + tile, BF16), shape((8, HALF), F32)],
            in_specs=[SMEM, row, whole((embed, book_rows)), whole((embed, HALF)), whole((1, HALF)), ANY],
            out_specs=[four, whole((8, HALF))],
            scratch_shapes=[pltpu.VMEM((HALF, book_rows), BF16)],
            compiler_params=params(32),
            cost_estimate=cost(images * 256 * 512 * 256, 5 * MIB),
            name="decode_images",
        )(image_heights, codes, codebook_t, weight_decode, bias_decode.reshape(1, HALF), after)

    devices = lax.axis_size("dp")
    layout = Layout(devices, book_rows, embed)
    half, piece, chips = layout.half, layout.piece, devices // 2
    streams = (x_own, x_far, q_own, q_far, codes)
    state = None
    win_own, win_far = [], []
    for k in range(usual):
        waits = win_far[k - 2 : k - 1] if k > 1 else []
        ending = (spot, decode_acc) if k == usual - 1 else ()
        outs = run_main(plan, layout, k, meta, image_heights, streams, weights, state, waits, ending)
        win_own.append(outs[0])
        if k < usual - 1:
            win_far.append(trade(outs[1]))
        state = outs[2:]
    last_window = outs[1]
    carry, (keep_own, keep_far, send) = state[:2], state[2:]

    def restore(own, far, waits=()):
        count = len(own)
        return pl.pallas_call(
            functools.partial(restore_rows, plan, count, len(waits)),
            out_shape=[shape((images, SIDE) + tile, BF16), shape((8, HALF), F32)],
            in_specs=[ANY] * len(waits) + [SMEM, SMEM] + [ANY] * (2 * count),
            out_specs=[VMEM, VMEM],
            scratch_shapes=[
                pltpu.VMEM((plan.total + LEAD + SIDE,) + tile, BF16),
                pltpu.VMEM((plan.total + LEAD + SIDE,) + tile, BF16),
                pltpu.SemaphoreType.DMA((2, count)),
            ],
            compiler_params=params(60),
            cost_estimate=cost(0, 10 * MIB),
            name="restore_rows",
        )(*waits, meta, image_heights, *own, *far)

    across = [(i, i ^ 1) for i in range(devices)]

    def step(body, out, name, *args, waits=()):
        specs = [VMEM] * len(args) + [ANY] * len(waits)
        args = (*args, *waits)
        return pl.pallas_call(
            body,
            out_shape=out,
            in_specs=specs,
            out_specs=[VMEM] * len(out) if isinstance(out, list) else VMEM,
            compiler_params=params(24),
            cost_estimate=cost(0, 2 * MIB),
            name=name,
        )(*args)

    def held(value, other):
        return pl.pallas_call(
            hold,
            out_shape=shape(value.shape, value.dtype),
            in_specs=[ANY, ANY],
            out_specs=ANY,
            input_output_aliases={0: 0},
            name="hold",
        )(value, other)

    send = held(send, win_far[usual - 2])
    came = lax.ppermute(send, "dp", across)
    far = step(add_far, shape((half, HALF), BF16), "add_far", keep_far, came)
    came_far = trade(far)
    parts = [shape((chips, piece, HALF), BF16), shape((8, HALF), F32)]
    mine, token = step(add_own, parts, "add_own", keep_own, came, came_far)
    win_far.append(trade(held(last_window, token)))
    cores = [[i for i in range(devices) if i % 2 == c] for c in range(2)]
    decoded, token = decode(token)
    mine = lax.all_to_all(mine, "dp", 0, 0, axis_index_groups=cores, tiled=True)
    mine = step(add_pieces, shape((chips, piece, HALF), BF16), "add_pieces", mine, waits=[token])
    latents_grad, token = restore(win_own, win_far, [mine])
    mine = lax.all_to_all(mine, "dp", 0, 0, axis_index_groups=cores, tiled=True)
    mine = held(mine, token).reshape(half, HALF)
    theirs = lax.ppermute(mine, "dp", across)

    grads_out = [
        shape((9, 2 * HALF, HALF), F32),
        shape((1, HALF), F32),
        shape((HALF, 2 * HALF), F32),
        shape((1, HALF), F32),
        shape((embed, HALF), F32),
        shape((1, embed), F32),
        shape((embed, book_rows), F32),
        shape((embed, HALF), F32),
        shape((1, HALF), F32),
    ]
    whole = pltpu.VMEM((layout.rows, HALF), F32)

    def usual_end(latents_grad):
        grads = pl.pallas_call(
            functools.partial(write_grads, layout),
            out_shape=grads_out,
            in_specs=[SMEM, VMEM, VMEM],
            out_specs=[VMEM] * 9,
            scratch_shapes=[whole],
            compiler_params=params(24),
            cost_estimate=cost(0, 4 * MIB),
            name="write_grads",
        )(spot, mine, theirs)
        return (latents_grad, *grads)

    def longer_end(latents_grad):
        last_x, last_q = trade(x_send[usual]), trade(q_send[usual])
        streams = (x_own, x_far + [last_x], q_own, q_far + [last_q], codes)
        outs = run_main(plan, layout, usual, meta, image_heights, streams, weights, carry)
        latents_grad, _ = restore(win_own + [outs[0]], win_far + [trade(outs[1])])
        own, far = pl.pallas_call(
            functools.partial(gather_plain, layout),
            out_shape=[shape((layout.rows, HALF), F32)] * 2,
            in_specs=[SMEM] + [VMEM] * 5,
            out_specs=[VMEM] * 2,
            compiler_params=params(40),
            name="gather_plain",
        )(spot, *outs[4:])
        extra = lax.psum(own + trade(far), "dp")
        first, second = jnp.where(core == 0, mine, theirs), jnp.where(core == 0, theirs, mine)
        grads = pl.pallas_call(
            functools.partial(split_again, layout),
            out_shape=grads_out,
            in_specs=[VMEM, VMEM],
            out_specs=[VMEM] * 9,
            scratch_shapes=[whole],
            compiler_params=params(24),
            name="split_again",
        )(jnp.concatenate([first, second]), extra)
        return (latents_grad, *grads)

    flag = layout.bias + 3
    holder = flag // half
    flags = jnp.where(core == holder, mine[flag - holder * half, 0], theirs[flag - holder * half, 0])
    ends = lax.cond(flags.astype(F32) > 0.5, longer_end, usual_end, latents_grad)
    latents_grad, kernel_grad, first_bias, mix_grad, mix_bias, project_grad, project_bias, book, decode, decode_bias = ends
    return (
        decoded,
        latents_grad,
        kernel_grad,
        first_bias.reshape(HALF),
        mix_grad,
        mix_bias.reshape(HALF),
        project_grad.T,
        project_bias.reshape(embed),
        book.T,
        decode,
        decode_bias.reshape(HALF),
    )


def solution(mesh):
    tile = P("dp", None, None, "mp")
    placed = (
        tile,
        P("dp"),
        P("dp", None, None),
        P(None, None, "mp"),
        P("mp"),
        P("mp", None),
        P("mp"),
        P("mp", None),
        P(),
        P(),
        P(None, "mp"),
        P("mp"),
        tile,
    )
    outs = (
        tile,
        tile,
        P(None, None, "mp"),
        P("mp"),
        P("mp", None),
        P("mp"),
        P("mp", None),
        P(),
        P(),
        P(None, "mp"),
        P("mp"),
    )
    return jax.shard_map(local, mesh=mesh, in_specs=placed, out_specs=outs, check_vma=False)
```

```python
import functools

import jax
import jax.numpy as jnp
from jax import lax
from jax.experimental import pallas as pl
from jax.experimental.pallas import tpu as pltpu
from jax.sharding import PartitionSpec as P

SIDE = 16
HALF = 128
LEAD = 16
BLOCK = 32
TILE = 32
MARK = 1e9
GELU_SCALE = 0.7978845608028654
GELU_CUBE = 0.044715
COMMIT = 0.25
F32 = jnp.float32
BF16 = jnp.bfloat16
ANY = pl.BlockSpec(memory_space=pl.ANY)
SMEM = pl.BlockSpec(memory_space=pltpu.SMEM)
HBM = pl.BlockSpec(memory_space=pltpu.HBM)
VMEM = pl.BlockSpec(memory_space=pltpu.VMEM)
MIB = 1 << 20

NT = (((1,), (1,)), ((), ()))
TN = (((0,), (0,)), ((), ()))
NN = (((1,), (0,)), ((), ()))


def dot(a, b, dims=NN):
    return lax.dot_general(a, b, dims, preferred_element_type=F32)


def one_hot_columns(codes, code_of):
    return jnp.where(code_of == codes.astype(jnp.int16), jnp.bfloat16(1), jnp.bfloat16(0))


def numbers(count, width):
    return lax.broadcasted_iota(jnp.int32, (count, width), 0).astype(jnp.int16)


def shape(dims, kind):
    return jax.ShapeDtypeStruct(dims, kind)


def params(mib):
    return pltpu.CompilerParams(vmem_limit_bytes=mib * MIB)


def cost(flops, moved, slow=0):
    return pl.CostEstimate(flops=flops, bytes_accessed=moved, transcendentals=slow)


class Plan:
    def __init__(self, images):
        self.images = images
        longest = images * SIDE // 2 + SIDE // 2
        part = images // 8
        self.chunks = [19 * part, 29 * part]
        self.usual = len(self.chunks)
        rest = longest - sum(self.chunks)
        self.chunks.append(rest)
        self.starts = [sum(self.chunks[:k]) for k in range(len(self.chunks))]
        self.total = sum(self.chunks)
        self.packed = -(-(LEAD + longest + self.total + LEAD) // SIDE) * SIDE
        self.rows, self.block = [], []
        for k, c in enumerate(self.chunks):
            block = BLOCK if k < self.usual else SIDE
            most = 1 + c + 15 + c // 4 + 1
            self.rows.append(-(-most // block) * block)
            self.block.append(block)
        self.covered = sum(self.chunks[: self.usual])


def meta_size(plan):
    return plan.images + len(plan.chunks) + 1 + 5


def plan_rows(plan, heights, place, meta):
    images = plan.images
    base = images + len(plan.chunks) + 1

    def total_of(b, acc):
        return acc + heights[b]

    total = lax.fori_loop(0, images, total_of, jnp.int32(0))

    def split_of(b, state):
        acc, best, split, cut = state
        acc = acc + heights[b]
        worst = jnp.maximum(acc, total - acc)
        better = worst < best
        return (acc, jnp.where(better, worst, best), jnp.where(better, b + 1, split), jnp.where(better, acc, cut))

    _, _, split, cut = lax.fori_loop(0, images, split_of, (jnp.int32(0), jnp.int32(1 << 20), jnp.int32(0), jnp.int32(0)))
    mine = place[0]
    own_first = jnp.where(mine == 0, 0, split)
    own_last = jnp.where(mine == 0, split, images)
    own_row = jnp.where(mine == 0, 0, cut)
    send_row = jnp.where(mine == 0, cut, 0)
    for k in range(len(plan.chunks) + 1):
        meta[images + k] = own_first
    ends = [plan.starts[k] + plan.chunks[k] for k in range(len(plan.chunks))]

    def place_of(b, acc):
        meta[b] = acc - own_row
        acc = acc + heights[b]
        end = acc - own_row
        inside = jnp.logical_and(b >= own_first, b < own_last)
        step = jnp.int32(0)
        for k in range(len(plan.chunks) - 1):
            step = step + (end > ends[k]).astype(jnp.int32)

        @pl.when(inside)
        def _():
            meta[images + 1 + step] = b + 1

        return acc

    lax.fori_loop(0, images, place_of, jnp.int32(0))
    for k in range(len(plan.chunks)):
        meta[images + k + 1] = jnp.maximum(meta[images + k + 1], meta[images + k])
    meta[base] = own_row
    meta[base + 1] = send_row
    meta[base + 2] = own_first
    meta[base + 3] = own_last
    meta[base + 4] = jnp.maximum(cut, total - cut)


def pack_rows(plan, meta, source, packed, piece, count):
    base = plan.images + len(plan.chunks) + 1

    def one(i, carry):
        b = piece * count + i
        row = meta[b] + meta[base] + LEAD
        packed[pl.ds(row, SIDE)] = source[b]
        return carry

    lax.fori_loop(0, count, one, 0)


def pack_latents(plan, heights, place, x_hbm, meta, own, *rest):
    n = len(plan.chunks)
    sends, (x_in, packed, sem_in, sem_out) = rest[:n], rest[n:]
    pieces = 8
    count = plan.images // pieces
    fetch = []
    for p in range(pieces):
        part = pl.ds(p * count, count)
        fetch.append(pltpu.make_async_copy(x_hbm.at[part], x_in.at[part], sem_in.at[p]))
        fetch[-1].start()
    plan_rows(plan, heights, place, meta)
    base = plan.images + n + 1
    for p in range(pieces):
        fetch[p].wait()
        pack_rows(plan, meta, x_in, packed, p, count)
    copies = []
    for k in range(n):
        part = pl.ds(LEAD + meta[base + 1] + plan.starts[k], plan.chunks[k])
        copies.append(pltpu.make_async_copy(packed.at[part], sends[k], sem_out.at[k]))
        copies[-1].start()
    copies.append(pltpu.make_async_copy(packed.at[pl.ds(meta[base], LEAD + plan.total)], own, sem_out.at[n]))
    copies[-1].start()
    for copy in copies:
        copy.wait()


def pack_code_grads(plan, meta, og_hbm, *rest):
    n = len(plan.chunks)
    sources, (own, small), rest = rest[:5], rest[6:8], rest[8:]
    sends, rest = rest[:n], rest[n:]
    og_in, packed, sem_in, sem_small = rest[:4]
    held = rest[4:]
    small_fetch = []
    for i in range(5):
        small_fetch.append(pltpu.make_async_copy(sources[i], held[i], sem_small.at[i]))
        small_fetch[-1].start()
    decode_w, weight_mix, project_t, bias_first, bias_mix = held
    pieces = 8
    count = plan.images // pieces
    fetch = []
    for p in range(pieces):
        part = pl.ds(p * count, count)
        fetch.append(pltpu.make_async_copy(og_hbm.at[part], og_in.at[part], sem_in.at[p]))
        fetch[-1].start()
    base = plan.images + n + 1

    def clear(i, carry):
        packed[pl.ds(i * SIDE, SIDE)] = jnp.zeros((SIDE, SIDE, HALF), BF16)
        return carry

    lax.fori_loop(0, packed.shape[0] // SIDE, clear, 0)
    for copy in small_fetch:
        copy.wait()
    side = HALF // 2
    small[0:HALF] = weight_mix[:, :HALF]
    small[HALF : 2 * HALF] = weight_mix[:, HALF:]
    small[2 * HALF : 2 * HALF + side] = project_t[...]
    which = lax.broadcasted_iota(jnp.int32, (SIDE, HALF), 0)
    first, second = bias_first[...].astype(F32), bias_mix[...].astype(F32)
    first = jnp.where(which == 0, first, jnp.where(which == 1, second, 0.0))
    small[2 * HALF + side : 2 * HALF + side + SIDE] = first.astype(BF16)
    w = decode_w[...]
    blank = jnp.zeros_like(w)
    upper = jnp.concatenate([w, blank], axis=0)
    lower = jnp.concatenate([blank, w], axis=0)
    for p in range(pieces):
        fetch[p].wait()
        pack_rows(plan, meta, og_in, packed, p, count)
    for k in range(n):
        half = plan.chunks[k] // 2
        for which in range(2):
            row = LEAD + meta[base + 1 - which] + plan.starts[k]
            a = packed[pl.ds(row, half)].reshape(half * SIDE, HALF)
            b = packed[pl.ds(row + half, half)].reshape(half * SIDE, HALF)
            both = dot(a, upper, NT) + dot(b, lower, NT)
            both = both.reshape(half, SIDE, HALF)
            if which == 0:
                sends[k][...] = both.astype(BF16)
            else:
                own[pl.ds(plan.starts[k] // 2, half)] = both


def prepare_weights(place, own_hbm, far_hbm, small, far_small, bias_code, codebook_t, *refs):
    forward, backward, mix, project, bias, book, kernel, far_kernel, sems = refs
    copies = []
    for i, (source, target) in enumerate(((own_hbm, kernel), (far_hbm, far_kernel))):
        copies.append(pltpu.make_async_copy(source, target, sems.at[i]))
        copies[-1].start()
    for copy in copies:
        copy.wait()
    first = pl.multiple_of(place[0] * HALF, HALF)
    order = (first, HALF - first)
    for tap in range(9):
        for d, source in enumerate((kernel, far_kernel)):
            for c in range(2):
                tile = source[tap, pl.ds(order[c], HALF), :]
                row = tap * 2 * HALF
                forward[row + c * HALF : row + (c + 1) * HALF, d * HALF : (d + 1) * HALF] = tile
                backward[row + d * HALF : row + (d + 1) * HALF, c * HALF : (c + 1) * HALF] = tile.T
    blank = jnp.zeros((HALF, HALF // 2), BF16)
    for d, source in enumerate((small, far_small)):
        rows = pl.ds(d * HALF, HALF)
        for c in range(2):
            mix[rows, c * HALF : (c + 1) * HALF] = source[pl.ds(order[c], HALF), :]
        part = source[2 * HALF : 2 * HALF + HALF // 2, :].T
        project[0, rows, :] = jnp.concatenate([part, blank], axis=1)
        project[1, rows, :] = jnp.concatenate([blank, part], axis=1)
        bias[0:8, d * HALF : (d + 1) * HALF] = source[2 * HALF + HALF // 2 : 2 * HALF + HALF // 2 + SIDE, :].astype(F32)[0:8]
    code = bias_code[...].astype(F32)
    code = jnp.concatenate([code, code], axis=1)
    bias[8:16, :] = jnp.broadcast_to(jnp.concatenate([code, code], axis=1), (8, 2 * HALF))
    book[...] = jnp.concatenate([codebook_t[...], codebook_t[...]], axis=0)


def sum_codes(first, group, heights, codes, og, codebook_t, _, grads, hot, cots, sums):
    step = pl.program_id(0)

    @pl.when(step == 0)
    def _():
        sums[...] = jnp.zeros_like(sums)

    spots = SIDE * SIDE
    code_of = numbers(codebook_t.shape[1], spots)
    spot = lax.broadcasted_iota(jnp.int32, (spots, 1), 0)
    for i in range(group):
        live = heights[(first + step) * group + i] * SIDE
        hot[:, i * spots : (i + 1) * spots] = one_hot_columns(codes[i : i + 1, :], code_of)
        cot = og[i].reshape(spots, HALF).astype(F32)
        cots[i * spots : (i + 1) * spots] = jnp.where(spot < live, cot, 0.0).astype(BF16)
    half = sums.shape[0] // 2
    for h in (0, half):
        sums[h : h + half] += dot(hot[h : h + half], cots[...])

    @pl.when(step == pl.num_programs(0) - 1)
    def _():
        total = sums[...]
        book = codebook_t[...].astype(F32)
        w = lax.dot_general(book, total, NN, precision=lax.Precision.HIGHEST, preferred_element_type=F32)
        bias = jnp.sum(total, axis=0, keepdims=True)
        embed = w.shape[0]
        grads[0:embed] = w
        grads[embed : embed + 8] = jnp.broadcast_to(bias, (8, HALF))


def decode_images(plan, steps, heights, codes, codebook_t, decode_w, decode_b, _, decoded, token, table):
    step = pl.program_id(0)
    token[...] = jnp.zeros_like(token)
    group = plan.images // steps

    @pl.when(step == 0)
    def _():
        full = dot(codebook_t[...], decode_w[...], TN) + decode_b[...].astype(F32)
        table[...] = full.T.astype(BF16)

    spots = SIDE * SIDE
    code_of = numbers(codebook_t.shape[1], spots)
    spot = lax.broadcasted_iota(jnp.int32, (spots, 1), 0)
    for i in range(group):
        live = heights[step * group + i] * SIDE
        out = dot(table[...], one_hot_columns(codes[i : i + 1, :], code_of)).T
        decoded[i] = jnp.where(spot < live, out, 0.0).astype(BF16).reshape(SIDE, SIDE, HALF)


def put_codes(code_rows, codes, b, height, dst):
    spot = lax.broadcasted_iota(jnp.int32, (1, SIDE * SIDE), 1)
    lane = lax.broadcasted_iota(jnp.int32, (1, HALF), 1)
    per_row = HALF // SIDE
    row = jnp.where(spot < height * SIDE, codes[pl.ds(b, 1), :], -1)
    turn = lax.rem(dst, per_row) * SIDE
    upper = pltpu.roll(row[:, :HALF], turn, 1)
    lower = pltpu.roll(row[:, HALF:], turn, 1)
    inside = lane >= turn
    pieces = (jnp.where(inside, upper, -1), jnp.where(inside, lower, upper), jnp.where(inside, -1, lower))
    for i, piece in enumerate(pieces):
        target = pl.ds(dst // per_row + i, 1)
        code_rows[target, :] = jnp.where(piece < 0, code_rows[target, :], piece)


def gelu_parts(v):
    square = v * v
    t = jnp.tanh(v * (GELU_SCALE + (GELU_SCALE * GELU_CUBE) * square))
    half = 0.5 + 0.5 * t
    slope = half + (0.5 * v) * (1.0 - t * t) * (GELU_SCALE + (3.0 * GELU_SCALE * GELU_CUBE) * square)
    return v * half, slope


def main_step(plan, layout, k, waits, *refs):
    first_step = k == 0
    fresh = k in (0, plan.usual)
    final = k == plan.usual - 1
    refs = list(refs[waits:])

    def take(count):
        got = refs[:count]
        del refs[:count]
        return got

    if final:
        place, decode_acc = take(2)
    meta, heights, x_own, x_far, q_own, q_far, codes = take(7)
    kernel_hbm, kernel_t_hbm, mix, project, bias, book = take(6)
    if not first_step:
        x_past, q_past, carry_own, carry_far = take(4)
    if not fresh:
        past_accs = take(5)
    win_own, win_far, next_own, next_far = take(4)
    if final:
        laid_out = take(3)
    if not final:
        sums_out = take(5)
    kernel_acc, mix_acc, project_acc, book_acc, bias_acc = take(5)
    kernel, kernel_t, weight_sems = take(3)
    xo, xf, qo, qf, qd, xc_o, xc_f, qc, code_rows, act3, slope_x, grad3, block_g = take(13)
    second_s, slope_s, low_s, mixed_s, code_s, hot_s, found_s, diff_s, sems = refs

    chunk, start = plan.chunks[k], plan.starts[k]
    images, rows, block = plan.images, plan.rows[k], plan.block[k]
    half = chunk // 2
    spots = block * SIDE
    low = meta[images + k]
    high = meta[images + k + 1]

    copies = [
        (x_own.at[pl.ds(start, LEAD + chunk)], xo.at[pl.ds(0, LEAD + chunk)]),
        (x_far, xf.at[pl.ds(LEAD, chunk)]),
        (q_own.at[pl.ds(start // 2, half)], qo.at[pl.ds(LEAD, half)]),
        (q_far, qf.at[pl.ds(LEAD, half)]),
    ]
    if not first_step:
        past = plan.chunks[k - 1]
        copies += [
            (x_past.at[pl.ds(past - LEAD, LEAD)], xf.at[pl.ds(0, LEAD)]),
            (q_own.at[pl.ds(start // 2 - LEAD, LEAD)], qo.at[pl.ds(0, LEAD)]),
            (q_past.at[pl.ds(past // 2 - LEAD, LEAD)], qf.at[pl.ds(0, LEAD)]),
        ]
    accs = (mix_acc, project_acc, book_acc, bias_acc, kernel_acc)
    early = len(copies)
    if not fresh:
        copies += list(zip(past_accs[1:] + past_accs[:1], accs))
    weight_copies = []
    for i, (source, target) in enumerate(((kernel_hbm, kernel), (kernel_t_hbm, kernel_t))):
        weight_copies.append(pltpu.make_async_copy(source, target, weight_sems.at[i]))
    started = []
    for i, (source, target) in enumerate(copies):
        started.append(pltpu.make_async_copy(source, target, sems.at[i]))
        started[-1].start()
    for copy in weight_copies:
        copy.start()
    started, later = started[:early], started[early:]

    if fresh:
        for acc in accs:
            acc[...] = jnp.zeros(acc.shape, F32)

    blank = jnp.zeros((SIDE, SIDE, HALF), BF16)
    no_row = jnp.full((SIDE, SIDE, HALF), MARK, F32)
    code_rows[...] = jnp.full(code_rows.shape, -1, jnp.int32)
    for r in range(0, rows + 2 * block, SIDE):
        part = pl.ds(r, SIDE)
        xc_o[part] = blank
        xc_f[part] = blank
        if r < rows:
            qc[part] = no_row
    for copy in started:
        copy.wait()

    lane3 = lax.broadcasted_iota(jnp.int32, (1, SIDE, HALF), 2) < HALF // 2

    def spread(r0, count):
        both = (qo[pl.ds(r0, count)] + qf[pl.ds(r0, count)].astype(F32)).reshape(count * SIDE, HALF)
        turned = pltpu.roll(both, HALF // 2, 1).reshape(count, SIDE, HALF)
        both = both.reshape(count, SIDE, HALF)
        return jnp.where(lane3, both, turned), jnp.where(lane3, turned, both)

    upper, lower = spread(LEAD, half)
    qd[pl.ds(LEAD, half)] = upper
    qd[pl.ds(LEAD + half, half)] = lower
    if not first_step:
        _, lower = spread(0, LEAD)
        qd[0:LEAD] = lower

    per_row = HALF // SIDE

    def put(b, dst):
        src = meta[b] - start + LEAD
        xc_o[pl.ds(dst, SIDE)] = xo[pl.ds(src, SIDE)]
        xc_f[pl.ds(dst, SIDE)] = xf[pl.ds(src, SIDE)]
        qc[pl.ds(dst, SIDE)] = qd[pl.ds(src, SIDE)]
        end = dst + heights[b]
        xc_o[pl.ds(end, SIDE)] = blank
        xc_f[pl.ds(end, SIDE)] = blank
        qc[pl.ds(end, SIDE)] = no_row
        put_codes(code_rows, codes, b, heights[b], dst)
        return end + 1

    used = lax.fori_loop(low, high, put, jnp.int32(1))
    blocks = jnp.where(high > low, (used + (block - 1)) // block, 0)

    column = lax.rem(lax.broadcasted_iota(jnp.int32, (TILE, 1), 0), SIDE)
    not_first = column != 0
    not_last = column != SIDE - 1

    def shifted(value):
        back = jnp.where(not_first, pltpu.roll(value, 1, 0), 0.0)
        ahead = jnp.where(not_last, pltpu.roll(value, TILE - 1, 0), 0.0)
        return back.astype(BF16), ahead.astype(BF16)

    edge = jnp.zeros((SIDE, 3 * 2 * HALF), BF16)
    act3[0:SIDE] = edge
    grad3[0:SIDE] = edge
    beyond = pl.multiple_of((blocks * block + 1) * SIDE, SIDE)
    grad3[pl.ds(beyond, SIDE)] = edge

    tiles = range(0, spots, TILE)

    def read_x(r0, t):
        part = pl.ds(r0 + t // SIDE, TILE // SIDE)
        o = xc_o[part].reshape(TILE, HALF)
        f = xc_f[part].reshape(TILE, HALF)
        return jnp.concatenate([o, f], axis=1).astype(F32)

    def at(row, count=block):
        return pl.ds(pl.multiple_of(row * SIDE, SIDE), count * SIDE)

    def tile_at(row, t):
        return pl.ds(pl.multiple_of(row * SIDE, SIDE) + t, TILE)

    def activate(j, carry):
        r0 = j * block
        for t in tiles:
            value, slope = gelu_parts(read_x(r0, t))
            slope_x[tile_at(r0, t), :] = slope
            back, ahead = shifted(value)
            act3[tile_at(r0 + 1, t), 0 : 2 * HALF] = back
            act3[tile_at(r0 + 1, t), 2 * HALF : 4 * HALF] = value.astype(BF16)
            act3[tile_at(r0 + 1, t), 4 * HALF : 6 * HALF] = ahead
        return carry

    fused = k < plan.usual
    lax.fori_loop(0, 2 if fused else blocks + 1, activate, 0)
    for copy in later:
        copy.wait()
    for copy in weight_copies:
        copy.wait()

    bias_first = bias[0:1, :]
    bias_mix = bias[1:2, :]
    bias_code = bias[8:9, 0:HALF]
    lane = lax.broadcasted_iota(jnp.int32, (1, HALF), 1) < HALF // 2
    hb = block // 2
    hs = hb * SIDE

    def add_rows(total, value):
        value = value.astype(F32)
        for i in range(0, value.shape[0], 8):
            part = value[i : i + 8]
            total = part if total is None else total + part
        return total

    half_tiles = range(0, hs, TILE)
    code_of = numbers(book_acc.shape[0], HALF)
    halves = (0, hs)

    def middle(j, carry):
        r0 = j * block
        for i in range(block // per_row):
            row = code_rows[pl.ds(j * (block // per_row) + i, 1), :]
            hot_s[:, i * HALF : (i + 1) * HALF] = one_hot_columns(row, code_of)
        for h in halves:
            found_s[h : h + hs] = dot(book[...], hot_s[:, h : h + hs]).astype(BF16).T
        pre = []
        for h in halves:
            window = jnp.concatenate([act3[at(r0 + i + h // SIDE, hb), :] for i in range(3)], axis=1)
            pre.append(dot(window, kernel[...]))
        for h, part in zip(halves, pre):
            for t in half_tiles:
                value, slope = gelu_parts(part[t : t + TILE] + bias_first)
                second_s[h + t : h + t + TILE] = value.astype(BF16)
                slope_s[h + t : h + t + TILE] = slope
        mixed = [dot(second_s[h : h + hs], mix[...]) for h in halves]
        for h, part in zip(halves, mixed):
            for t in half_tiles:
                low_s[h + t : h + t + TILE] = (read_x(r0, h + t) + part[t : t + TILE] + bias_mix).astype(BF16)
        latents = [dot(low_s[h : h + hs], project[i]) for i, h in enumerate(halves)]
        total = None
        for t in half_tiles:
            first = pl.ds(r0 + t // SIDE, TILE // SIDE)
            other = pl.ds(r0 + hb + t // SIDE, TILE // SIDE)
            ch = jnp.where(lane, found_s[t : t + TILE].astype(F32), found_s[hs + t : hs + t + TILE].astype(F32))
            q = jnp.where(lane3, qc[first], qc[other]).reshape(TILE, HALF)
            live = q < 0.5 * MARK
            latent = latents[0][t : t + TILE] + latents[1][t : t + TILE] + bias_code
            diff = jnp.where(live, latent - ch, 0.0)
            code_grad = jnp.where(live, q + (2.0 * COMMIT) * diff, 0.0).astype(BF16)
            code_s[t : t + TILE] = code_grad
            total = add_rows(total, code_grad)
            big = diff.astype(BF16).astype(F32)
            small = diff - big
            turned = pltpu.roll(small, HALF // 2, 1)
            diff_s[t : t + TILE] = jnp.where(lane, big, turned).astype(BF16)
            turned = pltpu.roll(big, HALF // 2, 1)
            diff_s[hs + t : hs + t + TILE] = jnp.where(lane, turned, small).astype(BF16)
        bias_acc[16:24, 0:HALF] += total
        total = None
        blocks_g = [dot(code_s[...], project[i], NT) for i in range(2)]
        for h, part in zip(halves, blocks_g):
            for t in half_tiles:
                block_g[tile_at(r0, h + t), :] = part[t : t + TILE]
                mixed_grad = part[t : t + TILE].astype(BF16)
                mixed_s[h + t : h + t + TILE] = mixed_grad
                total = add_rows(total, mixed_grad)
        bias_acc[8:16] += total
        second_grad = [dot(mixed_s[h : h + hs], mix[...], NT) for h in halves]
        total = None
        for h, part in zip(halves, second_grad):
            for t in half_tiles:
                first_grad = slope_s[h + t : h + t + TILE] * part[t : t + TILE]
                back, ahead = shifted(first_grad)
                first_low = first_grad.astype(BF16)
                grad3[tile_at(r0 + 1, h + t), 0 : 2 * HALF] = ahead
                grad3[tile_at(r0 + 1, h + t), 2 * HALF : 4 * HALF] = first_low
                grad3[tile_at(r0 + 1, h + t), 4 * HALF : 6 * HALF] = back
                total = add_rows(total, first_low)
        bias_acc[0:8] += total
        book_acc[...] += dot(hot_s[...], diff_s[...])
        mix_acc[...] += dot(second_s[...], mixed_s[...], TN)
        project_acc[...] += jnp.where(lane, dot(low_s[0:hs], code_s[...], TN), dot(low_s[hs:], code_s[...], TN))
        return carry

    def finish(j, carry):
        r0 = j * block
        active = act3[at(r0 + 1), 2 * HALF : 4 * HALF].T
        for i in range(3):
            kernel_acc[:, i * 6 * HALF : (i + 1) * 6 * HALF] += dot(active, grad3[at(r0 + 2 - i), :])
        grads = []
        for h in halves:
            window = jnp.concatenate([grad3[at(r0 + 2 - i + h // SIDE, hb), :] for i in range(3)], axis=1)
            grads.append(dot(window, kernel_t[...]))
        for h, grad in zip(halves, grads):
            for t in half_tiles:
                here = tile_at(r0, h + t)
                out = (block_g[here, :] + slope_x[here, :] * grad[t : t + TILE]).astype(BF16)
                part = pl.ds(r0 + (h + t) // SIDE, TILE // SIDE)
                xc_o[part] = out[:, :HALF].reshape(TILE // SIDE, SIDE, HALF)
                xc_f[part] = out[:, HALF:].reshape(TILE // SIDE, SIDE, HALF)
        return carry

    def opening(j, carry):
        middle(j, carry)
        return activate(j + 2, carry)

    def steady(j, carry):
        finish(j - 2, carry)
        middle(j, carry)
        return activate(j + 2, carry)

    if fused:
        lax.fori_loop(0, jnp.minimum(blocks, 2), opening, 0)
        lax.fori_loop(2, blocks, steady, 0)
        lax.fori_loop(jnp.maximum(blocks - 2, 0), blocks, finish, 0)
    else:
        lax.fori_loop(0, blocks, middle, 0)
        lax.fori_loop(0, blocks, finish, 0)
    leaving = []
    if not final:
        leaving += list(zip((kernel_acc, mix_acc, project_acc, book_acc, bias_acc), sums_out))
        for i, (source, target) in enumerate(leaving):
            leaving[i] = pltpu.make_async_copy(source, target, sems.at[i])
            leaving[i].start()

    out_o, out_f = xo, xf
    if first_step:
        out_o[0:LEAD] = blank
        out_f[0:LEAD] = blank
    else:
        out_o[0:LEAD] = carry_own[...]
        out_f[0:LEAD] = carry_far[...]

    def collect(b, src):
        dst = meta[b] - start + LEAD
        out_o[pl.ds(dst, SIDE)] = xc_o[pl.ds(src, SIDE)]
        out_f[pl.ds(dst, SIDE)] = xc_f[pl.ds(src, SIDE)]
        return src + heights[b] + 1

    lax.fori_loop(low, high, collect, jnp.int32(1))
    size = win_own.shape[0]
    windows = (
        (out_o.at[pl.ds(0, size)], win_own),
        (out_f.at[pl.ds(0, size)], win_far),
        (out_o.at[pl.ds(chunk, LEAD)], next_own),
        (out_f.at[pl.ds(chunk, LEAD)], next_far),
    )
    for i, (source, target) in enumerate(windows):
        leaving.append(pltpu.make_async_copy(source, target, sems.at[5 + i]))
        leaving[-1].start()
    if final:
        sums = (kernel_acc, mix_acc, project_acc, book_acc, bias_acc, decode_acc)
        laid_out += [slope_x.at[pl.ds(0, layout.rows), pl.ds(i * HALF, HALF)] for i in range(2)]
        leaving += gather_grads(plan, layout, place, meta, sums, *laid_out, sems)
    for copy in leaving:
        copy.wait()


class Layout:
    def __init__(self, devices, book_rows, embed):
        self.mix = 9 * 2 * HALF
        self.project = self.mix + 2 * HALF
        self.book = self.project + HALF // 2
        self.bias = self.book + book_rows // 2
        self.decode = self.bias + 8
        used = self.decode + embed + 8
        self.devices = devices
        self.piece = -(-used // (devices * SIDE)) * SIDE
        self.rows = self.piece * devices
        self.half = self.rows // 2
        self.used = used


def lay_out(layout, swap, kernel_acc, mix_acc, project_acc, book_acc, bias_acc, decode_acc, own, far):
    def lanes(value):
        return value[:, :HALF], value[:, HALF:]

    def order(first, second):
        return jnp.where(swap, second, first), jnp.where(swap, first, second)

    row = 0
    for tap in range(9):
        block = kernel_acc[:, tap * 2 * HALF : (tap + 1) * 2 * HALF]
        mine, theirs = lanes(block)
        a, b = order(mine[:HALF], mine[HALF:])
        own[row : row + HALF] = a
        own[row + HALF : row + 2 * HALF] = b
        a, b = order(theirs[:HALF], theirs[HALF:])
        far[row : row + HALF] = a
        far[row + HALF : row + 2 * HALF] = b
        row += 2 * HALF
    row = layout.mix
    for target, part in ((own, mix_acc[:HALF]), (far, mix_acc[HALF:])):
        a, b = order(*lanes(part))
        target[row : row + HALF] = a
        target[row + HALF : row + 2 * HALF] = b
    row = layout.project
    side = HALF // 2
    for target, part in ((own, project_acc[:HALF]), (far, project_acc[HALF:])):
        part = part + pltpu.roll(part, side, 1)
        target[row : row + side] = part.T[:side]
    row = layout.book
    book = book_acc[...]
    book = -2.0 * (book + pltpu.roll(book, side, 1))
    book = book.T[:side]
    for c in range(book.shape[1] // HALF):
        part = book[:, c * HALF : (c + 1) * HALF]
        own[row + c * side : row + (c + 1) * side] = part
        far[row + c * side : row + (c + 1) * side] = part
    row = layout.bias
    sums = [jnp.sum(bias_acc[8 * i : 8 * i + 8], axis=0, keepdims=True) for i in range(3)]
    code = sums[2][:, :HALF]
    code = code + pltpu.roll(code, side, 1)
    which = lax.broadcasted_iota(jnp.int32, (8, HALF), 0)
    for target, first in ((own, 0), (far, HALF)):
        part = jnp.where(which == 0, sums[0][:, first : first + HALF], sums[1][:, first : first + HALF])
        target[row : row + 8] = jnp.where(which == 2, code, jnp.where(which < 2, part, 0.0))
    row = layout.decode
    rest = layout.rows - row
    own[row:] = jnp.zeros((rest, HALF), F32)
    far[row:] = jnp.zeros((rest, HALF), F32)
    if decode_acc is not None:
        own[row : row + decode_acc.shape[0]] = decode_acc[...]


def gather_plain(layout, place, *refs):
    lay_out(layout, place[0] == 1, *refs[:5], None, *refs[5:])


def gather_grads(plan, layout, place, meta, accs, keep_own, keep_far, send, own, far, sems):
    lay_out(layout, place[0] == 1, *accs, own, far)
    base = plan.images + len(plan.chunks) + 1
    over = (meta[base + 4] > plan.covered).astype(F32)
    which = lax.broadcasted_iota(jnp.int32, (8, HALF), 0)
    row = layout.bias
    own[row : row + 8] = jnp.where(which == 3, over, own[row : row + 8])
    half = layout.half
    mine = pl.ds(pl.multiple_of(place[1] * half, SIDE), half)
    other = pl.ds(pl.multiple_of((1 - place[1]) * half, SIDE), half)
    kept = []
    for i, (source, target) in enumerate(((own, keep_own), (far, keep_far))):
        kept.append(pltpu.make_async_copy(source.at[mine, :], target, sems.at[9 + i]))
        kept[-1].start()
    send[0] = own[other, :].astype(BF16)
    send[1] = far[other, :].astype(BF16)
    return kept


def hold(value, _, out):
    pass


def add_core(place, keep_own, keep_far, came, out, token):
    token[...] = jnp.zeros_like(token)
    mine = place[0]
    chips, piece = out.shape[0] // 2, out.shape[1]
    for c in range(chips):
        rows = pl.ds(c * piece, piece)
        out[2 * c + mine] = (keep_own[rows] + came[0, rows].astype(F32)).astype(BF16)
        out[2 * c + 1 - mine] = (keep_far[rows] + came[1, rows].astype(F32)).astype(BF16)


def add_pieces(pieces, *rest):
    out = rest[-1]
    total = pieces[0].astype(F32)
    for i in range(1, pieces.shape[0]):
        total = total + pieces[i].astype(F32)
    out[...] = jnp.broadcast_to(total.astype(BF16)[None], out.shape)


def write_grads(layout, place, mine, theirs, kernel, first_bias, mix, mix_bias, project, project_bias, book, decode, decode_bias, whole):
    half = layout.half
    whole[pl.ds(pl.multiple_of(place[1] * half, SIDE), half), :] = mine[...].astype(F32)
    whole[pl.ds(pl.multiple_of((1 - place[1]) * half, SIDE), half), :] = theirs[...].astype(F32)
    split_grads(layout, whole, kernel, first_bias, mix, mix_bias, project, project_bias, book, decode, decode_bias)


def split_grads(layout, whole, kernel, first_bias, mix, mix_bias, project, project_bias, book, decode, decode_bias):
    for tap in range(9):
        kernel[tap] = whole[tap * 2 * HALF : (tap + 1) * 2 * HALF]
    row = layout.mix
    mix[:, :HALF] = whole[row : row + HALF]
    mix[:, HALF:] = whole[row + HALF : row + 2 * HALF]
    side = HALF // 2
    for row, target in ((layout.project, project), (layout.book, book)):
        for c in range(target.shape[1] // HALF):
            target[:, c * HALF : (c + 1) * HALF] = whole[row + c * side : row + (c + 1) * side]
    row = layout.bias
    first_bias[...] = whole[row : row + 1]
    mix_bias[...] = whole[row + 1 : row + 2]
    project_bias[...] = whole[row + 2 : row + 3, :side]
    row = layout.decode
    n = decode.shape[0]
    decode[...] = whole[row : row + n]
    decode_bias[...] = whole[row + n : row + n + 1]


def split_again(layout, total, extra, *refs):
    whole = refs[-1]
    whole[...] = total[...].astype(F32) + extra[...]
    split_grads(layout, whole, *refs[:-1])


def restore_rows(plan, n, waits, *refs):
    meta, heights, *refs = refs[waits:]
    own, far, out, token = refs[:n], refs[n : 2 * n], refs[2 * n], refs[2 * n + 1]
    token[...] = jnp.zeros_like(token)
    stage_own, stage_far, sems = refs[2 * n + 2 :]
    copies = []
    for k in range(n):
        size = plan.chunks[k] + (LEAD if k == n - 1 else 0)
        for i, (source, target) in enumerate(((own[k], stage_own), (far[k], stage_far))):
            from_rows = source.at[pl.ds(0, size)]
            copies.append(pltpu.make_async_copy(from_rows, target.at[pl.ds(plan.starts[k], size)], sems.at[i, k]))
            copies[-1].start()
    for copy in copies:
        copy.wait()
    base = plan.images + len(plan.chunks) + 1
    own_row, send_row = meta[base], meta[base + 1]
    first, last = meta[base + 2], meta[base + 3]
    row_of = lax.broadcasted_iota(jnp.int32, (SIDE, 1, 1), 0)

    def own_image(b, carry):
        rows = stage_own[pl.ds(meta[b] + LEAD, SIDE)]
        out[b] = jnp.where(row_of < heights[b], rows, jnp.zeros_like(rows))
        return carry

    def far_image(b, carry):
        rows = stage_far[pl.ds(meta[b] + own_row - send_row + LEAD, SIDE)]
        out[b] = jnp.where(row_of < heights[b], rows, jnp.zeros_like(rows))
        return carry

    lax.fori_loop(first, last, own_image, 0)
    lax.fori_loop(0, first, far_image, 0)
    lax.fori_loop(last, plan.images, far_image, 0)


def trade(value):
    return lax.ppermute(value, "mp", [(0, 1), (1, 0)])


def held(value, other):
    return pl.pallas_call(
        hold,
        out_shape=shape(value.shape, value.dtype),
        in_specs=[ANY, ANY],
        out_specs=ANY,
        input_output_aliases={0: 0},
        compiler_params=params(60),
        name="hold",
    )(value, other)


def run_main(plan, layout, k, meta, heights, streams, weights, state, waits=(), ending=()):
    chunk, rows, block = plan.chunks[k], plan.rows[k], plan.block[k]
    last = k >= plan.usual - 1
    final = k == plan.usual - 1
    x_own, x_far, q_own, q_far, codes = streams
    book_rows = weights[-1].shape[1]
    args = [*waits, *ending, meta, heights, x_own, x_far[k], q_own, q_far[k], codes, *weights]
    specs = [ANY] * len(waits) + ([SMEM, VMEM] if final else [])
    specs += [SMEM, SMEM, ANY, ANY, ANY, ANY, VMEM, ANY, ANY] + [VMEM] * (len(weights) - 2)
    alias = {}
    if state is not None:
        args += [x_far[k - 1], q_far[k - 1], *state]
        specs += [ANY, ANY, VMEM, VMEM] + [ANY] * (len(state) - 2)
        if not final:
            for i in range(len(state) - 2):
                alias[len(args) - 5 + i] = 4 + i
    size = chunk + LEAD if last else chunk
    tile = (SIDE, HALF)
    outs = [shape((size,) + tile, BF16)] * 2 + [shape((LEAD,) + tile, BF16)] * 2
    sums = [(2 * HALF, 18 * HALF), (2 * HALF, 2 * HALF), (2 * HALF, HALF), (book_rows, HALF), (24, 2 * HALF)]
    scratch = [pltpu.VMEM(dims, F32) for dims in sums]
    out_specs = [ANY] * 4
    if final:
        outs += [shape((layout.half, HALF), F32)] * 2 + [shape((2, layout.half, HALF), BF16)]
        out_specs += [ANY, ANY, VMEM]
    else:
        outs += [shape(dims, F32) for dims in sums]
        out_specs += [ANY] * 5
    scratch += [pltpu.VMEM((18 * HALF, 2 * HALF), BF16)] * 2 + [pltpu.SemaphoreType.DMA((2,))]
    half = chunk // 2
    spots = block * SIDE
    scratch += [
        pltpu.VMEM((LEAD + chunk + 2 * SIDE,) + tile, BF16),
        pltpu.VMEM((LEAD + chunk + 2 * SIDE,) + tile, BF16),
        pltpu.VMEM((LEAD + half,) + tile, F32),
        pltpu.VMEM((LEAD + half,) + tile, BF16),
        pltpu.VMEM((LEAD + chunk + SIDE,) + tile, F32),
        pltpu.VMEM((rows + 2 * block + SIDE,) + tile, BF16),
        pltpu.VMEM((rows + 2 * block + SIDE,) + tile, BF16),
        pltpu.VMEM((rows + 2 * SIDE,) + tile, F32),
        pltpu.VMEM((-(-(rows * SIDE // HALF + 4) // 8) * 8, HALF), jnp.int32),
        pltpu.VMEM(((rows + 2 * block + 2) * SIDE, 6 * HALF), BF16),
        pltpu.VMEM(((rows + 2 * block) * SIDE, 2 * HALF), F32),
        pltpu.VMEM(((rows + 2) * SIDE, 6 * HALF), BF16),
        pltpu.VMEM((rows * SIDE, 2 * HALF), F32),
        pltpu.VMEM((spots, 2 * HALF), BF16),
        pltpu.VMEM((spots, 2 * HALF), F32),
        pltpu.VMEM((spots, 2 * HALF), BF16),
        pltpu.VMEM((spots, 2 * HALF), BF16),
        pltpu.VMEM((spots // 2, HALF), BF16),
        pltpu.VMEM((book_rows, spots), BF16),
        pltpu.VMEM((spots, HALF), BF16),
        pltpu.VMEM((spots, HALF), BF16),
        pltpu.SemaphoreType.DMA((13,)),
    ]
    spots = chunk * SIDE
    return pl.pallas_call(
        functools.partial(main_step, plan, layout, k, len(waits)),
        out_shape=outs,
        in_specs=specs,
        out_specs=out_specs,
        scratch_shapes=scratch,
        input_output_aliases=alias,
        compiler_params=params(58),
        cost_estimate=cost(60 * 65536 * spots, 8 * MIB, 2 * 256 * spots),
        name=f"main_{k}",
    )(*args)


def local(
    image_latents,
    image_heights,
    code_index,
    kernel_three,
    bias_three,
    weight_mix,
    bias_mix,
    weight_project,
    bias_project,
    codebook,
    weight_decode,
    bias_decode,
    out_grad,
):
    images = image_latents.shape[0]
    plan = Plan(images)
    n = len(plan.chunks)
    tile = (SIDE, HALF)
    where = lax.axis_index("mp").astype(jnp.int32)
    core = lax.rem(lax.axis_index("dp").astype(jnp.int32), 2)
    spot = place = jnp.stack([where, core])

    packed = pl.pallas_call(
        functools.partial(pack_latents, plan),
        out_shape=[
            shape((meta_size(plan),), jnp.int32),
            shape((LEAD + plan.total,) + tile, BF16),
        ]
        + [shape((c,) + tile, BF16) for c in plan.chunks],
        in_specs=[SMEM, SMEM, HBM],
        out_specs=[SMEM, ANY] + [ANY] * n,
        scratch_shapes=[
            pltpu.VMEM((images, SIDE) + tile, BF16),
            pltpu.VMEM((plan.packed + SIDE,) + tile, BF16),
            pltpu.SemaphoreType.DMA((8,)),
            pltpu.SemaphoreType.DMA((n + 1,)),
        ],
        compiler_params=params(60),
        cost_estimate=cost(0, 12 * MIB),
        name="pack_latents",
    )(image_heights, place, image_latents)
    meta, x_own, x_send = packed[0], packed[1], packed[2:]

    far_kernel = trade(kernel_three)
    packed = pl.pallas_call(
        functools.partial(pack_code_grads, plan),
        out_shape=[shape((plan.total // 2,) + tile, F32), shape((2 * HALF + HALF // 2 + SIDE, HALF), BF16)]
        + [shape((c // 2,) + tile, BF16) for c in plan.chunks],
        in_specs=[SMEM] + [HBM] * 6 + [ANY],
        out_specs=[VMEM] * (n + 2),
        scratch_shapes=[
            pltpu.VMEM((images, SIDE) + tile, BF16),
            pltpu.VMEM((plan.packed + SIDE,) + tile, BF16),
            pltpu.SemaphoreType.DMA((8,)),
            pltpu.SemaphoreType.DMA((5,)),
            pltpu.VMEM(weight_decode.shape, BF16),
            pltpu.VMEM(weight_mix.shape, BF16),
            pltpu.VMEM(weight_project.shape[::-1], BF16),
            pltpu.VMEM((1, HALF), BF16),
            pltpu.VMEM((1, HALF), BF16),
        ],
        compiler_params=params(60),
        cost_estimate=cost(2 * 2 * plan.total * SIDE * 256 * 128, 10 * MIB),
        name="pack_code_grads",
    )(meta, out_grad, weight_decode, weight_mix, weight_project.T, bias_three.reshape(1, HALF), bias_mix.reshape(1, HALF), far_kernel)
    q_own, small, q_send = packed[0], packed[1], packed[2:]

    book_rows, embed = codebook.shape
    codebook_t = codebook.T
    far_small = trade(small)
    usual = plan.usual
    x_far, q_far = [], []
    x_far.append(trade(x_send[0]))
    q_far.append(trade(q_send[0]))

    weights = pl.pallas_call(
        prepare_weights,
        out_shape=[
            shape((18 * HALF, 2 * HALF), BF16),
            shape((18 * HALF, 2 * HALF), BF16),
            shape((2 * HALF, 2 * HALF), BF16),
            shape((2, 2 * HALF, HALF), BF16),
            shape((SIDE, 2 * HALF), F32),
            shape((HALF, book_rows), BF16),
        ],
        in_specs=[SMEM, HBM, HBM] + [VMEM] * 4,
        out_specs=[VMEM] * 6,
        scratch_shapes=[pltpu.VMEM(kernel_three.shape, BF16)] * 2 + [pltpu.SemaphoreType.DMA((2,))],
        compiler_params=params(60),
        cost_estimate=cost(0, 5 * MIB),
        name="prepare_weights",
    )(place, kernel_three, far_kernel, small, far_small, bias_project.reshape(1, -1), codebook_t)

    groups = 8
    group = images // groups
    codes = code_index.reshape(images, SIDE * SIDE)
    whole = lambda dims: pl.BlockSpec(dims, lambda g: (0,) * len(dims))
    four = pl.BlockSpec((group, SIDE) + tile, lambda g: (g, 0, 0, 0))
    row = pl.BlockSpec((group, SIDE * SIDE), lambda g: (g, 0))
    def code_sums(first, steps):
        return pl.pallas_call(
            functools.partial(sum_codes, first, group),
            grid=(steps,),
            out_shape=shape((embed + 8, HALF), F32),
            in_specs=[
                SMEM,
                pl.BlockSpec((group, SIDE * SIDE), lambda g: (g + first, 0)),
                pl.BlockSpec((group, SIDE) + tile, lambda g: (g + first, 0, 0, 0)),
                whole((embed, book_rows)),
                ANY,
            ],
            out_specs=whole((embed + 8, HALF)),
            scratch_shapes=[
                pltpu.VMEM((book_rows, group * SIDE * SIDE), BF16),
                pltpu.VMEM((group * SIDE * SIDE, HALF), BF16),
                pltpu.VMEM((book_rows, HALF), F32),
            ],
            compiler_params=params(60),
            cost_estimate=cost(steps * group * 256 * 512 * 256, steps * group * 65536),
            name=f"sum_codes_{first}",
        )(image_heights, codes, out_grad, codebook_t, small)

    decode_acc = code_sums(0, groups)
    for k in range(1, usual):
        x_far.append(trade(held(x_send[k], decode_acc)))
        q_far.append(trade(held(q_send[k], decode_acc)))

    def decode(after):
        return pl.pallas_call(
            functools.partial(decode_images, plan, groups),
            grid=(groups,),
            out_shape=[shape((images, SIDE) + tile, BF16), shape((8, HALF), F32)],
            in_specs=[SMEM, row, whole((embed, book_rows)), whole((embed, HALF)), whole((1, HALF)), ANY],
            out_specs=[four, whole((8, HALF))],
            scratch_shapes=[pltpu.VMEM((HALF, book_rows), BF16)],
            compiler_params=params(32),
            cost_estimate=cost(images * 256 * 512 * 256, 5 * MIB),
            name="decode_images",
        )(image_heights, codes, codebook_t, weight_decode, bias_decode.reshape(1, HALF), after)

    devices = lax.axis_size("dp")
    layout = Layout(devices, book_rows, embed)
    half, piece, chips = layout.half, layout.piece, devices // 2
    streams = (x_own, x_far, q_own, q_far, codes)
    state = None
    win_own, win_far = [], []
    for k in range(usual):
        waits = win_far[k - 2 : k - 1] if k > 1 else []
        ending = (spot, decode_acc) if k == usual - 1 else ()
        outs = run_main(plan, layout, k, meta, image_heights, streams, weights, state, waits, ending)
        win_own.append(outs[0])
        if k < usual - 1:
            win_far.append(trade(outs[1]))
        state = outs[2:]
    last_window = outs[1]
    carry, (keep_own, keep_far, send) = state[:2], state[2:]

    def restore(own, far, waits=()):
        count = len(own)
        return pl.pallas_call(
            functools.partial(restore_rows, plan, count, len(waits)),
            out_shape=[shape((images, SIDE) + tile, BF16), shape((8, HALF), F32)],
            in_specs=[ANY] * len(waits) + [SMEM, SMEM] + [ANY] * (2 * count),
            out_specs=[VMEM, VMEM],
            scratch_shapes=[
                pltpu.VMEM((plan.total + LEAD + SIDE,) + tile, BF16),
                pltpu.VMEM((plan.total + LEAD + SIDE,) + tile, BF16),
                pltpu.SemaphoreType.DMA((2, count)),
            ],
            compiler_params=params(60),
            cost_estimate=cost(0, 10 * MIB),
            name="restore_rows",
        )(*waits, meta, image_heights, *own, *far)

    across = [(i, i ^ 1) for i in range(devices)]

    def step(body, out, name, *args, waits=()):
        specs = [VMEM] * len(args) + [ANY] * len(waits)
        args = (*args, *waits)
        return pl.pallas_call(
            body,
            out_shape=out,
            in_specs=specs,
            out_specs=[VMEM] * len(out) if isinstance(out, list) else VMEM,
            compiler_params=params(24),
            cost_estimate=cost(0, 2 * MIB),
            name=name,
        )(*args)

    send = held(send, win_far[usual - 2])
    came = lax.ppermute(send, "dp", across)
    win_far.append(trade(last_window))
    mine, token = pl.pallas_call(
        add_core,
        out_shape=[shape((2 * chips, piece, HALF), BF16), shape((8, HALF), F32)],
        in_specs=[SMEM] + [VMEM] * 3,
        out_specs=[VMEM, VMEM],
        compiler_params=params(24),
        cost_estimate=cost(0, 4 * MIB),
        name="add_core",
    )(spot, keep_own, keep_far, came)
    both = [[2 * i + j for i in range(devices) if i % 2 == c for j in range(2)] for c in range(2)]
    cores = [[i for i in range(devices) if i % 2 == c] for c in range(2)]
    decoded, token = decode(token)
    mine = lax.all_to_all(mine, ("dp", "mp"), 0, 0, axis_index_groups=both, tiled=True)
    mine = step(add_pieces, shape((chips, piece, HALF), BF16), "add_pieces", mine, waits=[token])
    latents_grad, token = restore(win_own, win_far, [mine])
    mine = lax.all_to_all(mine, "dp", 0, 0, axis_index_groups=cores, tiled=True)
    mine = held(mine, token).reshape(half, HALF)
    theirs = lax.ppermute(mine, "dp", across)

    grads_out = [
        shape((9, 2 * HALF, HALF), F32),
        shape((1, HALF), F32),
        shape((HALF, 2 * HALF), F32),
        shape((1, HALF), F32),
        shape((embed, HALF), F32),
        shape((1, embed), F32),
        shape((embed, book_rows), F32),
        shape((embed, HALF), F32),
        shape((1, HALF), F32),
    ]
    whole = pltpu.VMEM((layout.rows, HALF), F32)

    def usual_end(latents_grad):
        grads = pl.pallas_call(
            functools.partial(write_grads, layout),
            out_shape=grads_out,
            in_specs=[SMEM, VMEM, VMEM],
            out_specs=[VMEM] * 9,
            scratch_shapes=[whole],
            compiler_params=params(24),
            cost_estimate=cost(0, 4 * MIB),
            name="write_grads",
        )(spot, mine, theirs)
        return (latents_grad, *grads)

    def longer_end(latents_grad):
        last_x, last_q = trade(x_send[usual]), trade(q_send[usual])
        streams = (x_own, x_far + [last_x], q_own, q_far + [last_q], codes)
        outs = run_main(plan, layout, usual, meta, image_heights, streams, weights, carry)
        latents_grad, _ = restore(win_own + [outs[0]], win_far + [trade(outs[1])])
        own, far = pl.pallas_call(
            functools.partial(gather_plain, layout),
            out_shape=[shape((layout.rows, HALF), F32)] * 2,
            in_specs=[SMEM] + [VMEM] * 5,
            out_specs=[VMEM] * 2,
            compiler_params=params(40),
            name="gather_plain",
        )(spot, *outs[4:])
        extra = lax.psum(own + trade(far), "dp")
        first, second = jnp.where(core == 0, mine, theirs), jnp.where(core == 0, theirs, mine)
        grads = pl.pallas_call(
            functools.partial(split_again, layout),
            out_shape=grads_out,
            in_specs=[VMEM, VMEM],
            out_specs=[VMEM] * 9,
            scratch_shapes=[whole],
            compiler_params=params(24),
            name="split_again",
        )(jnp.concatenate([first, second]), extra)
        return (latents_grad, *grads)

    flag = layout.bias + 3
    holder = flag // half
    flags = jnp.where(core == holder, mine[flag - holder * half, 0], theirs[flag - holder * half, 0])
    ends = lax.cond(flags.astype(F32) > 0.5, longer_end, usual_end, latents_grad)
    latents_grad, kernel_grad, first_bias, mix_grad, mix_bias, project_grad, project_bias, book, decode, decode_bias = ends
    return (
        decoded,
        latents_grad,
        kernel_grad,
        first_bias.reshape(HALF),
        mix_grad,
        mix_bias.reshape(HALF),
        project_grad.T,
        project_bias.reshape(embed),
        book.T,
        decode,
        decode_bias.reshape(HALF),
    )


def solution(mesh):
    tile = P("dp", None, None, "mp")
    placed = (
        tile,
        P("dp"),
        P("dp", None, None),
        P(None, None, "mp"),
        P("mp"),
        P("mp", None),
        P("mp"),
        P("mp", None),
        P(),
        P(),
        P(None, "mp"),
        P("mp"),
        tile,
    )
    outs = (
        tile,
        tile,
        P(None, None, "mp"),
        P("mp"),
        P("mp", None),
        P("mp"),
        P("mp", None),
        P(),
        P(),
        P(None, "mp"),
        P("mp"),
    )
    return jax.shard_map(local, mesh=mesh, in_specs=placed, out_specs=outs, check_vma=False)
```

```python
import functools

import jax
import jax.numpy as jnp
from jax import lax
from jax.experimental import pallas as pl
from jax.experimental.pallas import tpu as pltpu
from jax.sharding import PartitionSpec as P

SIDE = 16
HALF = 128
LEAD = 16
BLOCK = 32
TILE = 32
MARK = 1e9
GELU_SCALE = 0.7978845608028654
GELU_CUBE = 0.044715
COMMIT = 0.25
F32 = jnp.float32
BF16 = jnp.bfloat16
ANY = pl.BlockSpec(memory_space=pl.ANY)
SMEM = pl.BlockSpec(memory_space=pltpu.SMEM)
HBM = pl.BlockSpec(memory_space=pltpu.HBM)
VMEM = pl.BlockSpec(memory_space=pltpu.VMEM)
MIB = 1 << 20

NT = (((1,), (1,)), ((), ()))
TN = (((0,), (0,)), ((), ()))
NN = (((1,), (0,)), ((), ()))


def dot(a, b, dims=NN):
    return lax.dot_general(a, b, dims, preferred_element_type=F32)


def one_hot_columns(codes, code_of):
    return jnp.where(code_of == codes.astype(jnp.int16), jnp.bfloat16(1), jnp.bfloat16(0))


def numbers(count, width):
    return lax.broadcasted_iota(jnp.int32, (count, width), 0).astype(jnp.int16)


def shape(dims, kind):
    return jax.ShapeDtypeStruct(dims, kind)


def params(mib):
    return pltpu.CompilerParams(vmem_limit_bytes=mib * MIB)


def cost(flops, moved, slow=0):
    return pl.CostEstimate(flops=flops, bytes_accessed=moved, transcendentals=slow)


class Plan:
    def __init__(self, images):
        self.images = images
        longest = images * SIDE // 2 + SIDE // 2
        part = images // 8
        self.chunks = [19 * part, 29 * part]
        self.usual = len(self.chunks)
        rest = longest - sum(self.chunks)
        self.chunks.append(rest)
        self.starts = [sum(self.chunks[:k]) for k in range(len(self.chunks))]
        self.total = sum(self.chunks)
        self.packed = -(-(LEAD + longest + self.total + LEAD) // SIDE) * SIDE
        self.rows, self.block = [], []
        for k, c in enumerate(self.chunks):
            block = BLOCK if k < self.usual else SIDE
            most = 1 + c + 15 + c // 4 + 1
            self.rows.append(-(-most // block) * block)
            self.block.append(block)
        self.covered = sum(self.chunks[: self.usual])


def meta_size(plan):
    return plan.images + len(plan.chunks) + 1 + 5


def plan_rows(plan, heights, place, meta):
    images = plan.images
    base = images + len(plan.chunks) + 1

    def total_of(b, acc):
        return acc + heights[b]

    total = lax.fori_loop(0, images, total_of, jnp.int32(0))

    def split_of(b, state):
        acc, best, split, cut = state
        acc = acc + heights[b]
        worst = jnp.maximum(acc, total - acc)
        better = worst < best
        return (acc, jnp.where(better, worst, best), jnp.where(better, b + 1, split), jnp.where(better, acc, cut))

    _, _, split, cut = lax.fori_loop(0, images, split_of, (jnp.int32(0), jnp.int32(1 << 20), jnp.int32(0), jnp.int32(0)))
    mine = place[0]
    own_first = jnp.where(mine == 0, 0, split)
    own_last = jnp.where(mine == 0, split, images)
    own_row = jnp.where(mine == 0, 0, cut)
    send_row = jnp.where(mine == 0, cut, 0)
    for k in range(len(plan.chunks) + 1):
        meta[images + k] = own_first
    ends = [plan.starts[k] + plan.chunks[k] for k in range(len(plan.chunks))]

    def place_of(b, acc):
        meta[b] = acc - own_row
        acc = acc + heights[b]
        end = acc - own_row
        inside = jnp.logical_and(b >= own_first, b < own_last)
        step = jnp.int32(0)
        for k in range(len(plan.chunks) - 1):
            step = step + (end > ends[k]).astype(jnp.int32)

        @pl.when(inside)
        def _():
            meta[images + 1 + step] = b + 1

        return acc

    lax.fori_loop(0, images, place_of, jnp.int32(0))
    for k in range(len(plan.chunks)):
        meta[images + k + 1] = jnp.maximum(meta[images + k + 1], meta[images + k])
    meta[base] = own_row
    meta[base + 1] = send_row
    meta[base + 2] = own_first
    meta[base + 3] = own_last
    meta[base + 4] = jnp.maximum(cut, total - cut)


def pack_rows(plan, meta, source, packed, piece, count):
    base = plan.images + len(plan.chunks) + 1

    def one(i, carry):
        b = piece * count + i
        row = meta[b] + meta[base] + LEAD
        packed[pl.ds(row, SIDE)] = source[b]
        return carry

    lax.fori_loop(0, count, one, 0)


def pack_latents(plan, heights, place, x_hbm, meta, own, *rest):
    n = len(plan.chunks)
    sends, (x_in, packed, sem_in, sem_out) = rest[:n], rest[n:]
    pieces = 8
    count = plan.images // pieces
    fetch = []
    for p in range(pieces):
        part = pl.ds(p * count, count)
        fetch.append(pltpu.make_async_copy(x_hbm.at[part], x_in.at[part], sem_in.at[p]))
        fetch[-1].start()
    plan_rows(plan, heights, place, meta)
    base = plan.images + n + 1
    for p in range(pieces):
        fetch[p].wait()
        pack_rows(plan, meta, x_in, packed, p, count)
    copies = []
    for k in range(n):
        part = pl.ds(LEAD + meta[base + 1] + plan.starts[k], plan.chunks[k])
        copies.append(pltpu.make_async_copy(packed.at[part], sends[k], sem_out.at[k]))
        copies[-1].start()
    copies.append(pltpu.make_async_copy(packed.at[pl.ds(meta[base], LEAD + plan.total)], own, sem_out.at[n]))
    copies[-1].start()
    for copy in copies:
        copy.wait()


def pack_code_grads(plan, meta, og_hbm, *rest):
    n = len(plan.chunks)
    sources, (own, small), rest = rest[:5], rest[6:8], rest[8:]
    sends, rest = rest[:n], rest[n:]
    og_in, packed, sem_in, sem_small = rest[:4]
    held = rest[4:]
    small_fetch = []
    for i in range(5):
        small_fetch.append(pltpu.make_async_copy(sources[i], held[i], sem_small.at[i]))
        small_fetch[-1].start()
    decode_w, weight_mix, project_t, bias_first, bias_mix = held
    pieces = 8
    count = plan.images // pieces
    fetch = []
    for p in range(pieces):
        part = pl.ds(p * count, count)
        fetch.append(pltpu.make_async_copy(og_hbm.at[part], og_in.at[part], sem_in.at[p]))
        fetch[-1].start()
    base = plan.images + n + 1

    def clear(i, carry):
        packed[pl.ds(i * SIDE, SIDE)] = jnp.zeros((SIDE, SIDE, HALF), BF16)
        return carry

    lax.fori_loop(0, packed.shape[0] // SIDE, clear, 0)
    for copy in small_fetch:
        copy.wait()
    side = HALF // 2
    small[0:HALF] = weight_mix[:, :HALF]
    small[HALF : 2 * HALF] = weight_mix[:, HALF:]
    small[2 * HALF : 2 * HALF + side] = project_t[...]
    which = lax.broadcasted_iota(jnp.int32, (SIDE, HALF), 0)
    first, second = bias_first[...].astype(F32), bias_mix[...].astype(F32)
    first = jnp.where(which == 0, first, jnp.where(which == 1, second, 0.0))
    small[2 * HALF + side : 2 * HALF + side + SIDE] = first.astype(BF16)
    w = decode_w[...]
    blank = jnp.zeros_like(w)
    upper = jnp.concatenate([w, blank], axis=0)
    lower = jnp.concatenate([blank, w], axis=0)
    for p in range(pieces):
        fetch[p].wait()
        pack_rows(plan, meta, og_in, packed, p, count)
    for k in range(n):
        half = plan.chunks[k] // 2
        for which in range(2):
            row = LEAD + meta[base + 1 - which] + plan.starts[k]
            a = packed[pl.ds(row, half)].reshape(half * SIDE, HALF)
            b = packed[pl.ds(row + half, half)].reshape(half * SIDE, HALF)
            both = dot(a, upper, NT) + dot(b, lower, NT)
            both = both.reshape(half, SIDE, HALF)
            if which == 0:
                sends[k][...] = both.astype(BF16)
            else:
                own[pl.ds(plan.starts[k] // 2, half)] = both


def prepare_weights(place, own_hbm, far_hbm, small, far_small, bias_code, codebook_t, *refs):
    forward, backward, mix, project, bias, book, kernel, far_kernel, sems = refs
    copies = []
    for i, (source, target) in enumerate(((own_hbm, kernel), (far_hbm, far_kernel))):
        copies.append(pltpu.make_async_copy(source, target, sems.at[i]))
        copies[-1].start()
    for copy in copies:
        copy.wait()
    first = pl.multiple_of(place[0] * HALF, HALF)
    order = (first, HALF - first)
    for tap in range(9):
        for d, source in enumerate((kernel, far_kernel)):
            for c in range(2):
                tile = source[tap, pl.ds(order[c], HALF), :]
                row = tap * 2 * HALF
                forward[row + c * HALF : row + (c + 1) * HALF, d * HALF : (d + 1) * HALF] = tile
                backward[row + d * HALF : row + (d + 1) * HALF, c * HALF : (c + 1) * HALF] = tile.T
    blank = jnp.zeros((HALF, HALF // 2), BF16)
    for d, source in enumerate((small, far_small)):
        rows = pl.ds(d * HALF, HALF)
        for c in range(2):
            mix[rows, c * HALF : (c + 1) * HALF] = source[pl.ds(order[c], HALF), :]
        part = source[2 * HALF : 2 * HALF + HALF // 2, :].T
        project[0, rows, :] = jnp.concatenate([part, blank], axis=1)
        project[1, rows, :] = jnp.concatenate([blank, part], axis=1)
        bias[0:8, d * HALF : (d + 1) * HALF] = source[2 * HALF + HALF // 2 : 2 * HALF + HALF // 2 + SIDE, :].astype(F32)[0:8]
    code = bias_code[...].astype(F32)
    code = jnp.concatenate([code, code], axis=1)
    bias[8:16, :] = jnp.broadcast_to(jnp.concatenate([code, code], axis=1), (8, 2 * HALF))
    book[...] = jnp.concatenate([codebook_t[...], codebook_t[...]], axis=0)


def sum_codes(first, group, heights, codes, og, codebook_t, _, __, grads, hot, cots, sums):
    step = pl.program_id(0)

    @pl.when(step == 0)
    def _():
        sums[...] = jnp.zeros_like(sums)

    spots = SIDE * SIDE
    code_of = numbers(codebook_t.shape[1], spots)
    spot = lax.broadcasted_iota(jnp.int32, (spots, 1), 0)
    for i in range(group):
        live = heights[(first + step) * group + i] * SIDE
        hot[:, i * spots : (i + 1) * spots] = one_hot_columns(codes[i : i + 1, :], code_of)
        cot = og[i].reshape(spots, HALF).astype(F32)
        cots[i * spots : (i + 1) * spots] = jnp.where(spot < live, cot, 0.0).astype(BF16)
    half = sums.shape[0] // 2
    for h in (0, half):
        sums[h : h + half] += dot(hot[h : h + half], cots[...])

    @pl.when(step == pl.num_programs(0) - 1)
    def _():
        total = sums[...]
        book = codebook_t[...].astype(F32)
        w = lax.dot_general(book, total, NN, precision=lax.Precision.HIGHEST, preferred_element_type=F32)
        bias = jnp.sum(total, axis=0, keepdims=True)
        embed = w.shape[0]
        grads[0:embed] = w
        grads[embed : embed + 8] = jnp.broadcast_to(bias, (8, HALF))


def decode_images(plan, steps, heights, codes, codebook_t, decode_w, decode_b, _, decoded, token, table):
    step = pl.program_id(0)
    token[...] = jnp.zeros_like(token)
    group = plan.images // steps

    @pl.when(step == 0)
    def _():
        full = dot(codebook_t[...], decode_w[...], TN) + decode_b[...].astype(F32)
        table[...] = full.T.astype(BF16)

    spots = SIDE * SIDE
    code_of = numbers(codebook_t.shape[1], spots)
    spot = lax.broadcasted_iota(jnp.int32, (spots, 1), 0)
    for i in range(group):
        live = heights[step * group + i] * SIDE
        out = dot(table[...], one_hot_columns(codes[i : i + 1, :], code_of)).T
        decoded[i] = jnp.where(spot < live, out, 0.0).astype(BF16).reshape(SIDE, SIDE, HALF)


def put_codes(code_rows, codes, b, height, dst):
    spot = lax.broadcasted_iota(jnp.int32, (1, SIDE * SIDE), 1)
    lane = lax.broadcasted_iota(jnp.int32, (1, HALF), 1)
    per_row = HALF // SIDE
    row = jnp.where(spot < height * SIDE, codes[pl.ds(b, 1), :], -1)
    turn = lax.rem(dst, per_row) * SIDE
    upper = pltpu.roll(row[:, :HALF], turn, 1)
    lower = pltpu.roll(row[:, HALF:], turn, 1)
    inside = lane >= turn
    pieces = (jnp.where(inside, upper, -1), jnp.where(inside, lower, upper), jnp.where(inside, -1, lower))
    for i, piece in enumerate(pieces):
        target = pl.ds(dst // per_row + i, 1)
        code_rows[target, :] = jnp.where(piece < 0, code_rows[target, :], piece)


def gelu_parts(v):
    square = v * v
    t = jnp.tanh(v * (GELU_SCALE + (GELU_SCALE * GELU_CUBE) * square))
    half = 0.5 + 0.5 * t
    slope = half + (0.5 * v) * (1.0 - t * t) * (GELU_SCALE + (3.0 * GELU_SCALE * GELU_CUBE) * square)
    return v * half, slope


def main_step(plan, layout, k, waits, *refs):
    first_step = k == 0
    fresh = k in (0, plan.usual)
    final = k == plan.usual - 1
    refs = list(refs[waits:])

    def take(count):
        got = refs[:count]
        del refs[:count]
        return got

    if final:
        place, decode_acc = take(2)
    meta, heights, x_own, x_far, q_own, q_far, codes = take(7)
    kernel_hbm, kernel_t_hbm, mix, project, bias, book = take(6)
    if not first_step:
        x_past, q_past, carry_own, carry_far = take(4)
    if not fresh:
        past_accs = take(5)
    win_own, win_far, next_own, next_far = take(4)
    if final:
        laid_out = take(3)
    if not final:
        sums_out = take(5)
    kernel_acc, mix_acc, project_acc, book_acc, bias_acc = take(5)
    kernel, kernel_t, weight_sems = take(3)
    xo, xf, qo, qf, qd, xc_o, xc_f, qc, code_rows, act3, slope_x, grad3, block_g = take(13)
    second_s, slope_s, low_s, mixed_s, code_s, hot_s, found_s, diff_s, sems = refs

    chunk, start = plan.chunks[k], plan.starts[k]
    images, rows, block = plan.images, plan.rows[k], plan.block[k]
    half = chunk // 2
    spots = block * SIDE
    low = meta[images + k]
    high = meta[images + k + 1]

    copies = [
        (x_own.at[pl.ds(start, LEAD + chunk)], xo.at[pl.ds(0, LEAD + chunk)]),
        (x_far, xf.at[pl.ds(LEAD, chunk)]),
        (q_own.at[pl.ds(start // 2, half)], qo.at[pl.ds(LEAD, half)]),
        (q_far, qf.at[pl.ds(LEAD, half)]),
    ]
    if not first_step:
        past = plan.chunks[k - 1]
        copies += [
            (x_past.at[pl.ds(past - LEAD, LEAD)], xf.at[pl.ds(0, LEAD)]),
            (q_own.at[pl.ds(start // 2 - LEAD, LEAD)], qo.at[pl.ds(0, LEAD)]),
            (q_past.at[pl.ds(past // 2 - LEAD, LEAD)], qf.at[pl.ds(0, LEAD)]),
        ]
    accs = (mix_acc, project_acc, book_acc, bias_acc, kernel_acc)
    early = len(copies)
    if not fresh:
        copies += list(zip(past_accs[1:] + past_accs[:1], accs))
    weight_copies = []
    for i, (source, target) in enumerate(((kernel_hbm, kernel), (kernel_t_hbm, kernel_t))):
        weight_copies.append(pltpu.make_async_copy(source, target, weight_sems.at[i]))
    started = []
    for i, (source, target) in enumerate(copies):
        started.append(pltpu.make_async_copy(source, target, sems.at[i]))
        started[-1].start()
    for copy in weight_copies:
        copy.start()
    started, later = started[:early], started[early:]

    if fresh:
        for acc in accs:
            acc[...] = jnp.zeros(acc.shape, F32)

    blank = jnp.zeros((SIDE, SIDE, HALF), BF16)
    no_row = jnp.full((SIDE, SIDE, HALF), MARK, F32)
    code_rows[...] = jnp.full(code_rows.shape, -1, jnp.int32)
    for r in range(0, rows + 2 * block, SIDE):
        part = pl.ds(r, SIDE)
        xc_o[part] = blank
        xc_f[part] = blank
        if r < rows:
            qc[part] = no_row
    for copy in started:
        copy.wait()

    lane3 = lax.broadcasted_iota(jnp.int32, (1, SIDE, HALF), 2) < HALF // 2

    def spread(r0, count):
        both = (qo[pl.ds(r0, count)] + qf[pl.ds(r0, count)].astype(F32)).reshape(count * SIDE, HALF)
        turned = pltpu.roll(both, HALF // 2, 1).reshape(count, SIDE, HALF)
        both = both.reshape(count, SIDE, HALF)
        return jnp.where(lane3, both, turned), jnp.where(lane3, turned, both)

    upper, lower = spread(LEAD, half)
    qd[pl.ds(LEAD, half)] = upper
    qd[pl.ds(LEAD + half, half)] = lower
    if not first_step:
        _, lower = spread(0, LEAD)
        qd[0:LEAD] = lower

    per_row = HALF // SIDE

    def put(b, dst):
        src = meta[b] - start + LEAD
        xc_o[pl.ds(dst, SIDE)] = xo[pl.ds(src, SIDE)]
        xc_f[pl.ds(dst, SIDE)] = xf[pl.ds(src, SIDE)]
        qc[pl.ds(dst, SIDE)] = qd[pl.ds(src, SIDE)]
        end = dst + heights[b]
        xc_o[pl.ds(end, SIDE)] = blank
        xc_f[pl.ds(end, SIDE)] = blank
        qc[pl.ds(end, SIDE)] = no_row
        put_codes(code_rows, codes, b, heights[b], dst)
        return end + 1

    used = lax.fori_loop(low, high, put, jnp.int32(1))
    blocks = jnp.where(high > low, (used + (block - 1)) // block, 0)

    column = lax.rem(lax.broadcasted_iota(jnp.int32, (TILE, 1), 0), SIDE)
    not_first = column != 0
    not_last = column != SIDE - 1

    def shifted(value):
        back = jnp.where(not_first, pltpu.roll(value, 1, 0), 0.0)
        ahead = jnp.where(not_last, pltpu.roll(value, TILE - 1, 0), 0.0)
        return back.astype(BF16), ahead.astype(BF16)

    edge = jnp.zeros((SIDE, 3 * 2 * HALF), BF16)
    act3[0:SIDE] = edge
    grad3[0:SIDE] = edge
    beyond = pl.multiple_of((blocks * block + 1) * SIDE, SIDE)
    grad3[pl.ds(beyond, SIDE)] = edge

    tiles = range(0, spots, TILE)

    def read_x(r0, t):
        part = pl.ds(r0 + t // SIDE, TILE // SIDE)
        o = xc_o[part].reshape(TILE, HALF)
        f = xc_f[part].reshape(TILE, HALF)
        return jnp.concatenate([o, f], axis=1).astype(F32)

    def at(row, count=block):
        return pl.ds(pl.multiple_of(row * SIDE, SIDE), count * SIDE)

    def tile_at(row, t):
        return pl.ds(pl.multiple_of(row * SIDE, SIDE) + t, TILE)

    def activate(j, carry):
        r0 = j * block
        for t in tiles:
            value, slope = gelu_parts(read_x(r0, t))
            slope_x[tile_at(r0, t), :] = slope
            back, ahead = shifted(value)
            act3[tile_at(r0 + 1, t), 0 : 2 * HALF] = back
            act3[tile_at(r0 + 1, t), 2 * HALF : 4 * HALF] = value.astype(BF16)
            act3[tile_at(r0 + 1, t), 4 * HALF : 6 * HALF] = ahead
        return carry

    fused = k < plan.usual
    lax.fori_loop(0, 2 if fused else blocks + 1, activate, 0)
    for copy in later:
        copy.wait()
    for copy in weight_copies:
        copy.wait()

    bias_first = bias[0:1, :]
    bias_mix = bias[1:2, :]
    bias_code = bias[8:9, 0:HALF]
    lane = lax.broadcasted_iota(jnp.int32, (1, HALF), 1) < HALF // 2
    hb = block // 2
    hs = hb * SIDE

    def add_rows(total, value):
        value = value.astype(F32)
        for i in range(0, value.shape[0], 8):
            part = value[i : i + 8]
            total = part if total is None else total + part
        return total

    half_tiles = range(0, hs, TILE)
    code_of = numbers(book_acc.shape[0], HALF)
    halves = (0, hs)

    def middle(j, carry):
        r0 = j * block
        for i in range(block // per_row):
            row = code_rows[pl.ds(j * (block // per_row) + i, 1), :]
            hot_s[:, i * HALF : (i + 1) * HALF] = one_hot_columns(row, code_of)
        for h in halves:
            found_s[h : h + hs] = dot(book[...], hot_s[:, h : h + hs]).astype(BF16).T
        pre = []
        for h in halves:
            window = jnp.concatenate([act3[at(r0 + i + h // SIDE, hb), :] for i in range(3)], axis=1)
            pre.append(dot(window, kernel[...]))
        for h, part in zip(halves, pre):
            for t in half_tiles:
                value, slope = gelu_parts(part[t : t + TILE] + bias_first)
                second_s[h + t : h + t + TILE] = value.astype(BF16)
                slope_s[h + t : h + t + TILE] = slope
        mixed = [dot(second_s[h : h + hs], mix[...]) for h in halves]
        for h, part in zip(halves, mixed):
            for t in half_tiles:
                low_s[h + t : h + t + TILE] = (read_x(r0, h + t) + part[t : t + TILE] + bias_mix).astype(BF16)
        latents = [dot(low_s[h : h + hs], project[i]) for i, h in enumerate(halves)]
        total = None
        for t in half_tiles:
            first = pl.ds(r0 + t // SIDE, TILE // SIDE)
            other = pl.ds(r0 + hb + t // SIDE, TILE // SIDE)
            ch = jnp.where(lane, found_s[t : t + TILE].astype(F32), found_s[hs + t : hs + t + TILE].astype(F32))
            q = jnp.where(lane3, qc[first], qc[other]).reshape(TILE, HALF)
            live = q < 0.5 * MARK
            latent = latents[0][t : t + TILE] + latents[1][t : t + TILE] + bias_code
            diff = jnp.where(live, latent - ch, 0.0)
            code_grad = jnp.where(live, q + (2.0 * COMMIT) * diff, 0.0).astype(BF16)
            code_s[t : t + TILE] = code_grad
            total = add_rows(total, code_grad)
            big = diff.astype(BF16).astype(F32)
            small = diff - big
            turned = pltpu.roll(small, HALF // 2, 1)
            diff_s[t : t + TILE] = jnp.where(lane, big, turned).astype(BF16)
            turned = pltpu.roll(big, HALF // 2, 1)
            diff_s[hs + t : hs + t + TILE] = jnp.where(lane, turned, small).astype(BF16)
        bias_acc[16:24, 0:HALF] += total
        total = None
        blocks_g = [dot(code_s[...], project[i], NT) for i in range(2)]
        for h, part in zip(halves, blocks_g):
            for t in half_tiles:
                block_g[tile_at(r0, h + t), :] = part[t : t + TILE]
                mixed_grad = part[t : t + TILE].astype(BF16)
                mixed_s[h + t : h + t + TILE] = mixed_grad
                total = add_rows(total, mixed_grad)
        bias_acc[8:16] += total
        second_grad = [dot(mixed_s[h : h + hs], mix[...], NT) for h in halves]
        total = None
        for h, part in zip(halves, second_grad):
            for t in half_tiles:
                first_grad = slope_s[h + t : h + t + TILE] * part[t : t + TILE]
                back, ahead = shifted(first_grad)
                first_low = first_grad.astype(BF16)
                grad3[tile_at(r0 + 1, h + t), 0 : 2 * HALF] = ahead
                grad3[tile_at(r0 + 1, h + t), 2 * HALF : 4 * HALF] = first_low
                grad3[tile_at(r0 + 1, h + t), 4 * HALF : 6 * HALF] = back
                total = add_rows(total, first_low)
        bias_acc[0:8] += total
        book_acc[...] += dot(hot_s[...], diff_s[...])
        mix_acc[...] += dot(second_s[...], mixed_s[...], TN)
        project_acc[...] += jnp.where(lane, dot(low_s[0:hs], code_s[...], TN), dot(low_s[hs:], code_s[...], TN))
        return carry

    def finish(j, carry):
        r0 = j * block
        active = act3[at(r0 + 1), 2 * HALF : 4 * HALF].T
        for i in range(3):
            kernel_acc[:, i * 6 * HALF : (i + 1) * 6 * HALF] += dot(active, grad3[at(r0 + 2 - i), :])
        grads = []
        for h in halves:
            window = jnp.concatenate([grad3[at(r0 + 2 - i + h // SIDE, hb), :] for i in range(3)], axis=1)
            grads.append(dot(window, kernel_t[...]))
        for h, grad in zip(halves, grads):
            for t in half_tiles:
                here = tile_at(r0, h + t)
                out = (block_g[here, :] + slope_x[here, :] * grad[t : t + TILE]).astype(BF16)
                part = pl.ds(r0 + (h + t) // SIDE, TILE // SIDE)
                xc_o[part] = out[:, :HALF].reshape(TILE // SIDE, SIDE, HALF)
                xc_f[part] = out[:, HALF:].reshape(TILE // SIDE, SIDE, HALF)
        return carry

    def opening(j, carry):
        middle(j, carry)
        return activate(j + 2, carry)

    def steady(j, carry):
        finish(j - 2, carry)
        middle(j, carry)
        return activate(j + 2, carry)

    if fused:
        lax.fori_loop(0, jnp.minimum(blocks, 2), opening, 0)
        lax.fori_loop(2, blocks, steady, 0)
        lax.fori_loop(jnp.maximum(blocks - 2, 0), blocks, finish, 0)
    else:
        lax.fori_loop(0, blocks, middle, 0)
        lax.fori_loop(0, blocks, finish, 0)
    leaving = []
    if not final:
        leaving += list(zip((kernel_acc, mix_acc, project_acc, book_acc, bias_acc), sums_out))
        for i, (source, target) in enumerate(leaving):
            leaving[i] = pltpu.make_async_copy(source, target, sems.at[i])
            leaving[i].start()

    out_o, out_f = xo, xf
    if first_step:
        out_o[0:LEAD] = blank
        out_f[0:LEAD] = blank
    else:
        out_o[0:LEAD] = carry_own[...]
        out_f[0:LEAD] = carry_far[...]

    def collect(b, src):
        dst = meta[b] - start + LEAD
        out_o[pl.ds(dst, SIDE)] = xc_o[pl.ds(src, SIDE)]
        out_f[pl.ds(dst, SIDE)] = xc_f[pl.ds(src, SIDE)]
        return src + heights[b] + 1

    lax.fori_loop(low, high, collect, jnp.int32(1))
    size = win_own.shape[0]
    windows = (
        (out_o.at[pl.ds(0, size)], win_own),
        (out_f.at[pl.ds(0, size)], win_far),
        (out_o.at[pl.ds(chunk, LEAD)], next_own),
        (out_f.at[pl.ds(chunk, LEAD)], next_far),
    )
    for i, (source, target) in enumerate(windows):
        leaving.append(pltpu.make_async_copy(source, target, sems.at[5 + i]))
        leaving[-1].start()
    if final:
        sums = (kernel_acc, mix_acc, project_acc, book_acc, bias_acc, decode_acc)
        laid_out += [slope_x.at[pl.ds(0, layout.rows), pl.ds(i * HALF, HALF)] for i in range(2)]
        leaving += gather_grads(plan, layout, place, meta, sums, *laid_out, sems)
    for copy in leaving:
        copy.wait()


class Layout:
    def __init__(self, devices, book_rows, embed):
        self.mix = 9 * 2 * HALF
        self.project = self.mix + 2 * HALF
        self.book = self.project + HALF // 2
        self.bias = self.book + book_rows // 2
        self.decode = self.bias + 8
        used = self.decode + embed + 8
        self.devices = devices
        self.piece = -(-used // (devices * SIDE)) * SIDE
        self.rows = self.piece * devices
        self.half = self.rows // 2
        self.used = used


def lay_out(layout, swap, kernel_acc, mix_acc, project_acc, book_acc, bias_acc, decode_acc, own, far):
    def lanes(value):
        return value[:, :HALF], value[:, HALF:]

    def order(first, second):
        return jnp.where(swap, second, first), jnp.where(swap, first, second)

    row = 0
    for tap in range(9):
        block = kernel_acc[:, tap * 2 * HALF : (tap + 1) * 2 * HALF]
        mine, theirs = lanes(block)
        a, b = order(mine[:HALF], mine[HALF:])
        own[row : row + HALF] = a
        own[row + HALF : row + 2 * HALF] = b
        a, b = order(theirs[:HALF], theirs[HALF:])
        far[row : row + HALF] = a
        far[row + HALF : row + 2 * HALF] = b
        row += 2 * HALF
    row = layout.mix
    for target, part in ((own, mix_acc[:HALF]), (far, mix_acc[HALF:])):
        a, b = order(*lanes(part))
        target[row : row + HALF] = a
        target[row + HALF : row + 2 * HALF] = b
    row = layout.project
    side = HALF // 2
    for target, part in ((own, project_acc[:HALF]), (far, project_acc[HALF:])):
        part = part + pltpu.roll(part, side, 1)
        target[row : row + side] = part.T[:side]
    row = layout.book
    book = book_acc[...]
    book = -2.0 * (book + pltpu.roll(book, side, 1))
    book = book.T[:side]
    for c in range(book.shape[1] // HALF):
        part = book[:, c * HALF : (c + 1) * HALF]
        own[row + c * side : row + (c + 1) * side] = part
        far[row + c * side : row + (c + 1) * side] = part
    row = layout.bias
    sums = [jnp.sum(bias_acc[8 * i : 8 * i + 8], axis=0, keepdims=True) for i in range(3)]
    code = sums[2][:, :HALF]
    code = code + pltpu.roll(code, side, 1)
    which = lax.broadcasted_iota(jnp.int32, (8, HALF), 0)
    for target, first in ((own, 0), (far, HALF)):
        part = jnp.where(which == 0, sums[0][:, first : first + HALF], sums[1][:, first : first + HALF])
        target[row : row + 8] = jnp.where(which == 2, code, jnp.where(which < 2, part, 0.0))
    row = layout.decode
    rest = layout.rows - row
    own[row:] = jnp.zeros((rest, HALF), F32)
    far[row:] = jnp.zeros((rest, HALF), F32)
    if decode_acc is not None:
        own[row : row + decode_acc.shape[0]] = decode_acc[...]


def gather_plain(layout, place, *refs):
    lay_out(layout, place[0] == 1, *refs[:5], None, *refs[5:])


def gather_grads(plan, layout, place, meta, accs, keep_own, keep_far, send, own, far, sems):
    lay_out(layout, place[0] == 1, *accs, own, far)
    base = plan.images + len(plan.chunks) + 1
    over = (meta[base + 4] > plan.covered).astype(F32)
    which = lax.broadcasted_iota(jnp.int32, (8, HALF), 0)
    row = layout.bias
    own[row : row + 8] = jnp.where(which == 3, over, own[row : row + 8])
    half = layout.half
    mine = pl.ds(pl.multiple_of(place[1] * half, SIDE), half)
    other = pl.ds(pl.multiple_of((1 - place[1]) * half, SIDE), half)
    kept = []
    for i, (source, target) in enumerate(((own, keep_own), (far, keep_far))):
        kept.append(pltpu.make_async_copy(source.at[mine, :], target, sems.at[9 + i]))
        kept[-1].start()
    send[0] = own[other, :].astype(BF16)
    send[1] = far[other, :].astype(BF16)
    return kept


def hold(value, _, out):
    pass


def add_core(place, keep_own, keep_far, came, out, token):
    token[...] = jnp.zeros_like(token)
    mine = place[0]
    chips, piece = out.shape[0] // 2, out.shape[1]
    for c in range(chips):
        rows = pl.ds(c * piece, piece)
        out[2 * c + mine] = (keep_own[rows] + came[0, rows].astype(F32)).astype(BF16)
        out[2 * c + 1 - mine] = (keep_far[rows] + came[1, rows].astype(F32)).astype(BF16)


def add_pieces(pieces, *rest):
    out = rest[-1]
    total = pieces[0].astype(F32)
    for i in range(1, pieces.shape[0]):
        total = total + pieces[i].astype(F32)
    out[...] = jnp.broadcast_to(total.astype(BF16)[None], out.shape)


def write_grads(layout, place, mine, theirs, kernel, first_bias, mix, mix_bias, project, project_bias, book, decode, decode_bias, whole):
    half = layout.half
    whole[pl.ds(pl.multiple_of(place[1] * half, SIDE), half), :] = mine[...].astype(F32)
    whole[pl.ds(pl.multiple_of((1 - place[1]) * half, SIDE), half), :] = theirs[...].astype(F32)
    split_grads(layout, whole, kernel, first_bias, mix, mix_bias, project, project_bias, book, decode, decode_bias)


def split_grads(layout, whole, kernel, first_bias, mix, mix_bias, project, project_bias, book, decode, decode_bias):
    for tap in range(9):
        kernel[tap] = whole[tap * 2 * HALF : (tap + 1) * 2 * HALF]
    row = layout.mix
    mix[:, :HALF] = whole[row : row + HALF]
    mix[:, HALF:] = whole[row + HALF : row + 2 * HALF]
    side = HALF // 2
    for row, target in ((layout.project, project), (layout.book, book)):
        for c in range(target.shape[1] // HALF):
            target[:, c * HALF : (c + 1) * HALF] = whole[row + c * side : row + (c + 1) * side]
    row = layout.bias
    first_bias[...] = whole[row : row + 1]
    mix_bias[...] = whole[row + 1 : row + 2]
    project_bias[...] = whole[row + 2 : row + 3, :side]
    row = layout.decode
    n = decode.shape[0]
    decode[...] = whole[row : row + n]
    decode_bias[...] = whole[row + n : row + n + 1]


def split_again(layout, total, extra, *refs):
    whole = refs[-1]
    whole[...] = total[...].astype(F32) + extra[...]
    split_grads(layout, whole, *refs[:-1])


def restore_rows(plan, n, waits, *refs):
    meta, heights, *refs = refs[waits:]
    own, far, out, token = refs[:n], refs[n : 2 * n], refs[2 * n], refs[2 * n + 1]
    token[...] = jnp.zeros_like(token)
    stage_own, stage_far, sems = refs[2 * n + 2 :]
    copies = []
    for k in range(n):
        size = plan.chunks[k] + (LEAD if k == n - 1 else 0)
        for i, (source, target) in enumerate(((own[k], stage_own), (far[k], stage_far))):
            from_rows = source.at[pl.ds(0, size)]
            copies.append(pltpu.make_async_copy(from_rows, target.at[pl.ds(plan.starts[k], size)], sems.at[i, k]))
            copies[-1].start()
    for copy in copies:
        copy.wait()
    base = plan.images + len(plan.chunks) + 1
    own_row, send_row = meta[base], meta[base + 1]
    first, last = meta[base + 2], meta[base + 3]
    row_of = lax.broadcasted_iota(jnp.int32, (SIDE, 1, 1), 0)

    def own_image(b, carry):
        rows = stage_own[pl.ds(meta[b] + LEAD, SIDE)]
        out[b] = jnp.where(row_of < heights[b], rows, jnp.zeros_like(rows))
        return carry

    def far_image(b, carry):
        rows = stage_far[pl.ds(meta[b] + own_row - send_row + LEAD, SIDE)]
        out[b] = jnp.where(row_of < heights[b], rows, jnp.zeros_like(rows))
        return carry

    lax.fori_loop(first, last, own_image, 0)
    lax.fori_loop(0, first, far_image, 0)
    lax.fori_loop(last, plan.images, far_image, 0)


def trade(value):
    return lax.ppermute(value, "mp", [(0, 1), (1, 0)])


def held(value, other):
    return pl.pallas_call(
        hold,
        out_shape=shape(value.shape, value.dtype),
        in_specs=[ANY, ANY],
        out_specs=ANY,
        input_output_aliases={0: 0},
        compiler_params=params(60),
        name="hold",
    )(value, other)


def run_main(plan, layout, k, meta, heights, streams, weights, state, waits=(), ending=()):
    chunk, rows, block = plan.chunks[k], plan.rows[k], plan.block[k]
    last = k >= plan.usual - 1
    final = k == plan.usual - 1
    x_own, x_far, q_own, q_far, codes = streams
    book_rows = weights[-1].shape[1]
    args = [*waits, *ending, meta, heights, x_own, x_far[k], q_own, q_far[k], codes, *weights]
    specs = [ANY] * len(waits) + ([SMEM, VMEM] if final else [])
    specs += [SMEM, SMEM, ANY, ANY, ANY, ANY, VMEM, ANY, ANY] + [VMEM] * (len(weights) - 2)
    alias = {}
    if state is not None:
        args += [x_far[k - 1], q_far[k - 1], *state]
        specs += [ANY, ANY, VMEM, VMEM] + [ANY] * (len(state) - 2)
        if not final:
            for i in range(len(state) - 2):
                alias[len(args) - 5 + i] = 4 + i
    size = chunk + LEAD if last else chunk
    tile = (SIDE, HALF)
    outs = [shape((size,) + tile, BF16)] * 2 + [shape((LEAD,) + tile, BF16)] * 2
    sums = [(2 * HALF, 18 * HALF), (2 * HALF, 2 * HALF), (2 * HALF, HALF), (book_rows, HALF), (24, 2 * HALF)]
    scratch = [pltpu.VMEM(dims, F32) for dims in sums]
    out_specs = [ANY] * 4
    if final:
        outs += [shape((layout.half, HALF), F32)] * 2 + [shape((2, layout.half, HALF), BF16)]
        out_specs += [ANY, ANY, VMEM]
    else:
        outs += [shape(dims, F32) for dims in sums]
        out_specs += [ANY] * 5
    scratch += [pltpu.VMEM((18 * HALF, 2 * HALF), BF16)] * 2 + [pltpu.SemaphoreType.DMA((2,))]
    half = chunk // 2
    spots = block * SIDE
    scratch += [
        pltpu.VMEM((LEAD + chunk + 2 * SIDE,) + tile, BF16),
        pltpu.VMEM((LEAD + chunk + 2 * SIDE,) + tile, BF16),
        pltpu.VMEM((LEAD + half,) + tile, F32),
        pltpu.VMEM((LEAD + half,) + tile, BF16),
        pltpu.VMEM((LEAD + chunk + SIDE,) + tile, F32),
        pltpu.VMEM((rows + 2 * block + SIDE,) + tile, BF16),
        pltpu.VMEM((rows + 2 * block + SIDE,) + tile, BF16),
        pltpu.VMEM((rows + 2 * SIDE,) + tile, F32),
        pltpu.VMEM((-(-(rows * SIDE // HALF + 4) // 8) * 8, HALF), jnp.int32),
        pltpu.VMEM(((rows + 2 * block + 2) * SIDE, 6 * HALF), BF16),
        pltpu.VMEM(((rows + 2 * block) * SIDE, 2 * HALF), F32),
        pltpu.VMEM(((rows + 2) * SIDE, 6 * HALF), BF16),
        pltpu.VMEM((rows * SIDE, 2 * HALF), F32),
        pltpu.VMEM((spots, 2 * HALF), BF16),
        pltpu.VMEM((spots, 2 * HALF), F32),
        pltpu.VMEM((spots, 2 * HALF), BF16),
        pltpu.VMEM((spots, 2 * HALF), BF16),
        pltpu.VMEM((spots // 2, HALF), BF16),
        pltpu.VMEM((book_rows, spots), BF16),
        pltpu.VMEM((spots, HALF), BF16),
        pltpu.VMEM((spots, HALF), BF16),
        pltpu.SemaphoreType.DMA((13,)),
    ]
    spots = chunk * SIDE
    return pl.pallas_call(
        functools.partial(main_step, plan, layout, k, len(waits)),
        out_shape=outs,
        in_specs=specs,
        out_specs=out_specs,
        scratch_shapes=scratch,
        input_output_aliases=alias,
        compiler_params=params(58),
        cost_estimate=cost(60 * 65536 * spots, 8 * MIB, 2 * 256 * spots),
        name=f"main_{k}",
    )(*args)


def local(
    image_latents,
    image_heights,
    code_index,
    kernel_three,
    bias_three,
    weight_mix,
    bias_mix,
    weight_project,
    bias_project,
    codebook,
    weight_decode,
    bias_decode,
    out_grad,
):
    images = image_latents.shape[0]
    plan = Plan(images)
    n = len(plan.chunks)
    tile = (SIDE, HALF)
    where = lax.axis_index("mp").astype(jnp.int32)
    core = lax.rem(lax.axis_index("dp").astype(jnp.int32), 2)
    spot = place = jnp.stack([where, core])

    packed = pl.pallas_call(
        functools.partial(pack_latents, plan),
        out_shape=[
            shape((meta_size(plan),), jnp.int32),
            shape((LEAD + plan.total,) + tile, BF16),
        ]
        + [shape((c,) + tile, BF16) for c in plan.chunks],
        in_specs=[SMEM, SMEM, HBM],
        out_specs=[SMEM, ANY] + [ANY] * n,
        scratch_shapes=[
            pltpu.VMEM((images, SIDE) + tile, BF16),
            pltpu.VMEM((plan.packed + SIDE,) + tile, BF16),
            pltpu.SemaphoreType.DMA((8,)),
            pltpu.SemaphoreType.DMA((n + 1,)),
        ],
        compiler_params=params(60),
        cost_estimate=cost(0, 12 * MIB),
        name="pack_latents",
    )(image_heights, place, image_latents)
    meta, x_own, x_send = packed[0], packed[1], packed[2:]

    far_kernel = trade(kernel_three)
    packed = pl.pallas_call(
        functools.partial(pack_code_grads, plan),
        out_shape=[shape((plan.total // 2,) + tile, F32), shape((2 * HALF + HALF // 2 + SIDE, HALF), BF16)]
        + [shape((c // 2,) + tile, BF16) for c in plan.chunks],
        in_specs=[SMEM] + [HBM] * 6 + [SMEM],
        out_specs=[VMEM] * (n + 2),
        scratch_shapes=[
            pltpu.VMEM((images, SIDE) + tile, BF16),
            pltpu.VMEM((plan.packed + SIDE,) + tile, BF16),
            pltpu.SemaphoreType.DMA((8,)),
            pltpu.SemaphoreType.DMA((5,)),
            pltpu.VMEM(weight_decode.shape, BF16),
            pltpu.VMEM(weight_mix.shape, BF16),
            pltpu.VMEM(weight_project.shape[::-1], BF16),
            pltpu.VMEM((1, HALF), BF16),
            pltpu.VMEM((1, HALF), BF16),
        ],
        compiler_params=params(60),
        cost_estimate=cost(2 * 2 * plan.total * SIDE * 256 * 128, 10 * MIB),
        name="pack_code_grads",
    )(meta, out_grad, weight_decode, weight_mix, weight_project.T, bias_three.reshape(1, HALF), bias_mix.reshape(1, HALF), meta)
    q_own, small, q_send = packed[0], packed[1], packed[2:]

    book_rows, embed = codebook.shape
    codebook_t = codebook.T
    far_small = trade(small)
    usual = plan.usual
    x_far, q_far = [], []
    x_far.append(trade(x_send[0]))
    q_far.append(trade(q_send[0]))

    weights = pl.pallas_call(
        prepare_weights,
        out_shape=[
            shape((18 * HALF, 2 * HALF), BF16),
            shape((18 * HALF, 2 * HALF), BF16),
            shape((2 * HALF, 2 * HALF), BF16),
            shape((2, 2 * HALF, HALF), BF16),
            shape((SIDE, 2 * HALF), F32),
            shape((HALF, book_rows), BF16),
        ],
        in_specs=[SMEM, HBM, HBM] + [VMEM] * 4,
        out_specs=[VMEM] * 6,
        scratch_shapes=[pltpu.VMEM(kernel_three.shape, BF16)] * 2 + [pltpu.SemaphoreType.DMA((2,))],
        compiler_params=params(60),
        cost_estimate=cost(0, 5 * MIB),
        name="prepare_weights",
    )(place, kernel_three, far_kernel, small, far_small, bias_project.reshape(1, -1), codebook_t)

    groups = 8
    group = images // groups
    codes = code_index.reshape(images, SIDE * SIDE)
    whole = lambda dims: pl.BlockSpec(dims, lambda g: (0,) * len(dims))
    four = pl.BlockSpec((group, SIDE) + tile, lambda g: (g, 0, 0, 0))
    row = pl.BlockSpec((group, SIDE * SIDE), lambda g: (g, 0))
    def code_sums(first, steps):
        return pl.pallas_call(
            functools.partial(sum_codes, first, group),
            grid=(steps,),
            out_shape=shape((embed + 8, HALF), F32),
            in_specs=[
                SMEM,
                pl.BlockSpec((group, SIDE * SIDE), lambda g: (g + first, 0)),
                pl.BlockSpec((group, SIDE) + tile, lambda g: (g + first, 0, 0, 0)),
                whole((embed, book_rows)),
                ANY,
                ANY,
            ],
            out_specs=whole((embed + 8, HALF)),
            scratch_shapes=[
                pltpu.VMEM((book_rows, group * SIDE * SIDE), BF16),
                pltpu.VMEM((group * SIDE * SIDE, HALF), BF16),
                pltpu.VMEM((book_rows, HALF), F32),
            ],
            compiler_params=params(60),
            cost_estimate=cost(steps * group * 256 * 512 * 256, steps * group * 65536),
            name=f"sum_codes_{first}",
        )(image_heights, codes, out_grad, codebook_t, small, far_kernel)

    decode_acc = code_sums(0, groups)
    for k in range(1, usual):
        x_far.append(trade(held(x_send[k], decode_acc)))
        q_far.append(trade(held(q_send[k], decode_acc)))

    def decode(after):
        return pl.pallas_call(
            functools.partial(decode_images, plan, groups),
            grid=(groups,),
            out_shape=[shape((images, SIDE) + tile, BF16), shape((8, HALF), F32)],
            in_specs=[SMEM, row, whole((embed, book_rows)), whole((embed, HALF)), whole((1, HALF)), ANY],
            out_specs=[four, whole((8, HALF))],
            scratch_shapes=[pltpu.VMEM((HALF, book_rows), BF16)],
            compiler_params=params(32),
            cost_estimate=cost(images * 256 * 512 * 256, 5 * MIB),
            name="decode_images",
        )(image_heights, codes, codebook_t, weight_decode, bias_decode.reshape(1, HALF), after)

    devices = lax.axis_size("dp")
    layout = Layout(devices, book_rows, embed)
    half, piece, chips = layout.half, layout.piece, devices // 2
    streams = (x_own, x_far, q_own, q_far, codes)
    state = None
    win_own, win_far = [], []
    for k in range(usual):
        waits = win_far[k - 2 : k - 1] if k > 1 else []
        ending = (spot, decode_acc) if k == usual - 1 else ()
        outs = run_main(plan, layout, k, meta, image_heights, streams, weights, state, waits, ending)
        win_own.append(outs[0])
        if k < usual - 1:
            win_far.append(trade(outs[1]))
        state = outs[2:]
    last_window = outs[1]
    carry, (keep_own, keep_far, send) = state[:2], state[2:]

    def restore(own, far, waits=()):
        count = len(own)
        return pl.pallas_call(
            functools.partial(restore_rows, plan, count, len(waits)),
            out_shape=[shape((images, SIDE) + tile, BF16), shape((8, HALF), F32)],
            in_specs=[ANY] * len(waits) + [SMEM, SMEM] + [ANY] * (2 * count),
            out_specs=[VMEM, VMEM],
            scratch_shapes=[
                pltpu.VMEM((plan.total + LEAD + SIDE,) + tile, BF16),
                pltpu.VMEM((plan.total + LEAD + SIDE,) + tile, BF16),
                pltpu.SemaphoreType.DMA((2, count)),
            ],
            compiler_params=params(60),
            cost_estimate=cost(0, 10 * MIB),
            name="restore_rows",
        )(*waits, meta, image_heights, *own, *far)

    across = [(i, i ^ 1) for i in range(devices)]

    def step(body, out, name, *args, waits=()):
        specs = [VMEM] * len(args) + [ANY] * len(waits)
        args = (*args, *waits)
        return pl.pallas_call(
            body,
            out_shape=out,
            in_specs=specs,
            out_specs=[VMEM] * len(out) if isinstance(out, list) else VMEM,
            compiler_params=params(24),
            cost_estimate=cost(0, 2 * MIB),
            name=name,
        )(*args)

    send = held(send, win_far[usual - 2])
    came = lax.ppermute(send, "dp", across)
    win_far.append(trade(last_window))
    mine, token = pl.pallas_call(
        add_core,
        out_shape=[shape((2 * chips, piece, HALF), BF16), shape((8, HALF), F32)],
        in_specs=[SMEM] + [VMEM] * 3,
        out_specs=[VMEM, VMEM],
        compiler_params=params(24),
        cost_estimate=cost(0, 4 * MIB),
        name="add_core",
    )(spot, keep_own, keep_far, came)
    both = [[2 * i + j for i in range(devices) if i % 2 == c for j in range(2)] for c in range(2)]
    cores = [[i for i in range(devices) if i % 2 == c] for c in range(2)]
    decoded, token = decode(token)
    latents_grad, token = restore(win_own, win_far, [token])
    mine = lax.all_to_all(mine, ("dp", "mp"), 0, 0, axis_index_groups=both, tiled=True)
    mine = step(add_pieces, shape((chips, piece, HALF), BF16), "add_pieces", mine, waits=[token])
    mine = lax.all_to_all(mine, "dp", 0, 0, axis_index_groups=cores, tiled=True)
    mine = mine.reshape(half, HALF)
    theirs = lax.ppermute(mine, "dp", across)

    grads_out = [
        shape((9, 2 * HALF, HALF), F32),
        shape((1, HALF), F32),
        shape((HALF, 2 * HALF), F32),
        shape((1, HALF), F32),
        shape((embed, HALF), F32),
        shape((1, embed), F32),
        shape((embed, book_rows), F32),
        shape((embed, HALF), F32),
        shape((1, HALF), F32),
    ]
    whole = pltpu.VMEM((layout.rows, HALF), F32)

    def usual_end(latents_grad):
        grads = pl.pallas_call(
            functools.partial(write_grads, layout),
            out_shape=grads_out,
            in_specs=[SMEM, VMEM, VMEM],
            out_specs=[VMEM] * 9,
            scratch_shapes=[whole],
            compiler_params=params(24),
            cost_estimate=cost(0, 4 * MIB),
            name="write_grads",
        )(spot, mine, theirs)
        return (latents_grad, *grads)

    def longer_end(latents_grad):
        last_x, last_q = trade(x_send[usual]), trade(q_send[usual])
        streams = (x_own, x_far + [last_x], q_own, q_far + [last_q], codes)
        outs = run_main(plan, layout, usual, meta, image_heights, streams, weights, carry)
        latents_grad, _ = restore(win_own + [outs[0]], win_far + [trade(outs[1])])
        own, far = pl.pallas_call(
            functools.partial(gather_plain, layout),
            out_shape=[shape((layout.rows, HALF), F32)] * 2,
            in_specs=[SMEM] + [VMEM] * 5,
            out_specs=[VMEM] * 2,
            compiler_params=params(40),
            name="gather_plain",
        )(spot, *outs[4:])
        extra = lax.psum(own + trade(far), "dp")
        first, second = jnp.where(core == 0, mine, theirs), jnp.where(core == 0, theirs, mine)
        grads = pl.pallas_call(
            functools.partial(split_again, layout),
            out_shape=grads_out,
            in_specs=[VMEM, VMEM],
            out_specs=[VMEM] * 9,
            scratch_shapes=[whole],
            compiler_params=params(24),
            name="split_again",
        )(jnp.concatenate([first, second]), extra)
        return (latents_grad, *grads)

    flag = layout.bias + 3
    holder = flag // half
    flags = jnp.where(core == holder, mine[flag - holder * half, 0], theirs[flag - holder * half, 0])
    ends = lax.cond(flags.astype(F32) > 0.5, longer_end, usual_end, latents_grad)
    latents_grad, kernel_grad, first_bias, mix_grad, mix_bias, project_grad, project_bias, book, decode, decode_bias = ends
    return (
        decoded,
        latents_grad,
        kernel_grad,
        first_bias.reshape(HALF),
        mix_grad,
        mix_bias.reshape(HALF),
        project_grad.T,
        project_bias.reshape(embed),
        book.T,
        decode,
        decode_bias.reshape(HALF),
    )


def solution(mesh):
    tile = P("dp", None, None, "mp")
    placed = (
        tile,
        P("dp"),
        P("dp", None, None),
        P(None, None, "mp"),
        P("mp"),
        P("mp", None),
        P("mp"),
        P("mp", None),
        P(),
        P(),
        P(None, "mp"),
        P("mp"),
        tile,
    )
    outs = (
        tile,
        tile,
        P(None, None, "mp"),
        P("mp"),
        P("mp", None),
        P("mp"),
        P("mp", None),
        P(),
        P(),
        P(None, "mp"),
        P("mp"),
    )
    return jax.shard_map(local, mesh=mesh, in_specs=placed, out_specs=outs, check_vma=False)
```

```python
import functools

import jax
import jax.numpy as jnp
from jax import lax
from jax.experimental import pallas as pl
from jax.experimental.pallas import tpu as pltpu
from jax.sharding import PartitionSpec as P

SIDE = 16
HALF = 128
LEAD = 16
BLOCK = 32
TILE = 32
MARK = 1e9
GELU_SCALE = 0.7978845608028654
GELU_CUBE = 0.044715
COMMIT = 0.25
F32 = jnp.float32
BF16 = jnp.bfloat16
ANY = pl.BlockSpec(memory_space=pl.ANY)
SMEM = pl.BlockSpec(memory_space=pltpu.SMEM)
HBM = pl.BlockSpec(memory_space=pltpu.HBM)
VMEM = pl.BlockSpec(memory_space=pltpu.VMEM)
MIB = 1 << 20

NT = (((1,), (1,)), ((), ()))
TN = (((0,), (0,)), ((), ()))
NN = (((1,), (0,)), ((), ()))


def dot(a, b, dims=NN):
    return lax.dot_general(a, b, dims, preferred_element_type=F32)


def one_hot_columns(codes, code_of):
    return jnp.where(code_of == codes.astype(jnp.int16), jnp.bfloat16(1), jnp.bfloat16(0))


def numbers(count, width):
    return lax.broadcasted_iota(jnp.int32, (count, width), 0).astype(jnp.int16)


def shape(dims, kind):
    return jax.ShapeDtypeStruct(dims, kind)


def params(mib):
    return pltpu.CompilerParams(vmem_limit_bytes=mib * MIB)


def cost(flops, moved, slow=0):
    return pl.CostEstimate(flops=flops, bytes_accessed=moved, transcendentals=slow)


class Plan:
    def __init__(self, images):
        self.images = images
        longest = images * SIDE // 2 + SIDE // 2
        part = images // 8
        self.chunks = [16 * part, 32 * part]
        self.usual = len(self.chunks)
        rest = longest - sum(self.chunks)
        self.chunks.append(rest)
        self.starts = [sum(self.chunks[:k]) for k in range(len(self.chunks))]
        self.total = sum(self.chunks)
        self.packed = -(-(LEAD + longest + self.total + LEAD) // SIDE) * SIDE
        self.rows, self.block = [], []
        for k, c in enumerate(self.chunks):
            block = BLOCK if k < self.usual else SIDE
            most = 1 + c + 15 + c // 4 + 1
            self.rows.append(-(-most // block) * block)
            self.block.append(block)
        self.covered = sum(self.chunks[: self.usual])


def meta_size(plan):
    return plan.images + len(plan.chunks) + 1 + 5


def plan_rows(plan, heights, place, meta):
    images = plan.images
    base = images + len(plan.chunks) + 1

    def total_of(b, acc):
        return acc + heights[b]

    total = lax.fori_loop(0, images, total_of, jnp.int32(0))

    def split_of(b, state):
        acc, best, split, cut = state
        acc = acc + heights[b]
        worst = jnp.maximum(acc, total - acc)
        better = worst < best
        return (acc, jnp.where(better, worst, best), jnp.where(better, b + 1, split), jnp.where(better, acc, cut))

    _, _, split, cut = lax.fori_loop(0, images, split_of, (jnp.int32(0), jnp.int32(1 << 20), jnp.int32(0), jnp.int32(0)))
    mine = place[0]
    own_first = jnp.where(mine == 0, 0, split)
    own_last = jnp.where(mine == 0, split, images)
    own_row = jnp.where(mine == 0, 0, cut)
    send_row = jnp.where(mine == 0, cut, 0)
    for k in range(len(plan.chunks) + 1):
        meta[images + k] = own_first
    ends = [plan.starts[k] + plan.chunks[k] for k in range(len(plan.chunks))]

    def place_of(b, acc):
        meta[b] = acc - own_row
        acc = acc + heights[b]
        end = acc - own_row
        inside = jnp.logical_and(b >= own_first, b < own_last)
        step = jnp.int32(0)
        for k in range(len(plan.chunks) - 1):
            step = step + (end > ends[k]).astype(jnp.int32)

        @pl.when(inside)
        def _():
            meta[images + 1 + step] = b + 1

        return acc

    lax.fori_loop(0, images, place_of, jnp.int32(0))
    for k in range(len(plan.chunks)):
        meta[images + k + 1] = jnp.maximum(meta[images + k + 1], meta[images + k])
    meta[base] = own_row
    meta[base + 1] = send_row
    meta[base + 2] = own_first
    meta[base + 3] = own_last
    meta[base + 4] = jnp.maximum(cut, total - cut)


def pack_rows(plan, meta, source, packed, piece, count):
    base = plan.images + len(plan.chunks) + 1

    def one(i, carry):
        b = piece * count + i
        row = meta[b] + meta[base] + LEAD
        packed[pl.ds(row, SIDE)] = source[b]
        return carry

    lax.fori_loop(0, count, one, 0)


def pack_latents(plan, heights, place, x_hbm, meta, own, *rest):
    n = len(plan.chunks)
    sends, (x_in, packed, sem_in, sem_out) = rest[:n], rest[n:]
    pieces = 8
    count = plan.images // pieces
    fetch = []
    for p in range(pieces):
        part = pl.ds(p * count, count)
        fetch.append(pltpu.make_async_copy(x_hbm.at[part], x_in.at[part], sem_in.at[p]))
        fetch[-1].start()
    plan_rows(plan, heights, place, meta)
    base = plan.images + n + 1
    for p in range(pieces):
        fetch[p].wait()
        pack_rows(plan, meta, x_in, packed, p, count)
    copies = []
    for k in range(n):
        part = pl.ds(LEAD + meta[base + 1] + plan.starts[k], plan.chunks[k])
        copies.append(pltpu.make_async_copy(packed.at[part], sends[k], sem_out.at[k]))
        copies[-1].start()
    copies.append(pltpu.make_async_copy(packed.at[pl.ds(meta[base], LEAD + plan.total)], own, sem_out.at[n]))
    copies[-1].start()
    for copy in copies:
        copy.wait()


def pack_code_grads(plan, meta, og_hbm, *rest):
    n = len(plan.chunks)
    sources, (own, small), rest = rest[:5], rest[6:8], rest[8:]
    sends, rest = rest[:n], rest[n:]
    og_in, packed, sem_in, sem_small = rest[:4]
    held = rest[4:]
    small_fetch = []
    for i in range(5):
        small_fetch.append(pltpu.make_async_copy(sources[i], held[i], sem_small.at[i]))
        small_fetch[-1].start()
    decode_w, weight_mix, project_t, bias_first, bias_mix = held
    pieces = 8
    count = plan.images // pieces
    fetch = []
    for p in range(pieces):
        part = pl.ds(p * count, count)
        fetch.append(pltpu.make_async_copy(og_hbm.at[part], og_in.at[part], sem_in.at[p]))
        fetch[-1].start()
    base = plan.images + n + 1

    def clear(i, carry):
        packed[pl.ds(i * SIDE, SIDE)] = jnp.zeros((SIDE, SIDE, HALF), BF16)
        return carry

    lax.fori_loop(0, packed.shape[0] // SIDE, clear, 0)
    for copy in small_fetch:
        copy.wait()
    side = HALF // 2
    small[0:HALF] = weight_mix[:, :HALF]
    small[HALF : 2 * HALF] = weight_mix[:, HALF:]
    small[2 * HALF : 2 * HALF + side] = project_t[...]
    which = lax.broadcasted_iota(jnp.int32, (SIDE, HALF), 0)
    first, second = bias_first[...].astype(F32), bias_mix[...].astype(F32)
    first = jnp.where(which == 0, first, jnp.where(which == 1, second, 0.0))
    small[2 * HALF + side : 2 * HALF + side + SIDE] = first.astype(BF16)
    w = decode_w[...]
    blank = jnp.zeros_like(w)
    upper = jnp.concatenate([w, blank], axis=0)
    lower = jnp.concatenate([blank, w], axis=0)
    for p in range(pieces):
        fetch[p].wait()
        pack_rows(plan, meta, og_in, packed, p, count)
    for k in range(n):
        half = plan.chunks[k] // 2
        for which in range(2):
            row = LEAD + meta[base + 1 - which] + plan.starts[k]
            a = packed[pl.ds(row, half)].reshape(half * SIDE, HALF)
            b = packed[pl.ds(row + half, half)].reshape(half * SIDE, HALF)
            both = dot(a, upper, NT) + dot(b, lower, NT)
            both = both.reshape(half, SIDE, HALF)
            if which == 0:
                sends[k][...] = both.astype(BF16)
            else:
                own[pl.ds(plan.starts[k] // 2, half)] = both


def prepare_weights(place, own_hbm, far_hbm, small, far_small, bias_code, codebook_t, *refs):
    forward, backward, mix, project, bias, book, kernel, far_kernel, sems = refs
    copies = []
    for i, (source, target) in enumerate(((own_hbm, kernel), (far_hbm, far_kernel))):
        copies.append(pltpu.make_async_copy(source, target, sems.at[i]))
        copies[-1].start()
    for copy in copies:
        copy.wait()
    first = pl.multiple_of(place[0] * HALF, HALF)
    order = (first, HALF - first)
    for tap in range(9):
        for d, source in enumerate((kernel, far_kernel)):
            for c in range(2):
                tile = source[tap, pl.ds(order[c], HALF), :]
                row = tap * 2 * HALF
                forward[row + c * HALF : row + (c + 1) * HALF, d * HALF : (d + 1) * HALF] = tile
                backward[row + d * HALF : row + (d + 1) * HALF, c * HALF : (c + 1) * HALF] = tile.T
    blank = jnp.zeros((HALF, HALF // 2), BF16)
    for d, source in enumerate((small, far_small)):
        rows = pl.ds(d * HALF, HALF)
        for c in range(2):
            mix[rows, c * HALF : (c + 1) * HALF] = source[pl.ds(order[c], HALF), :]
        part = source[2 * HALF : 2 * HALF + HALF // 2, :].T
        project[0, rows, :] = jnp.concatenate([part, blank], axis=1)
        project[1, rows, :] = jnp.concatenate([blank, part], axis=1)
        bias[0:8, d * HALF : (d + 1) * HALF] = source[2 * HALF + HALF // 2 : 2 * HALF + HALF // 2 + SIDE, :].astype(F32)[0:8]
    code = bias_code[...].astype(F32)
    code = jnp.concatenate([code, code], axis=1)
    bias[8:16, :] = jnp.broadcast_to(jnp.concatenate([code, code], axis=1), (8, 2 * HALF))
    book[...] = jnp.concatenate([codebook_t[...], codebook_t[...]], axis=0)


def sum_codes(first, group, heights, codes, og, codebook_t, _, __, grads, hot, cots, sums):
    step = pl.program_id(0)

    @pl.when(step == 0)
    def _():
        sums[...] = jnp.zeros_like(sums)

    spots = SIDE * SIDE
    code_of = numbers(codebook_t.shape[1], spots)
    spot = lax.broadcasted_iota(jnp.int32, (spots, 1), 0)
    for i in range(group):
        live = heights[(first + step) * group + i] * SIDE
        hot[:, i * spots : (i + 1) * spots] = one_hot_columns(codes[i : i + 1, :], code_of)
        cot = og[i].reshape(spots, HALF).astype(F32)
        cots[i * spots : (i + 1) * spots] = jnp.where(spot < live, cot, 0.0).astype(BF16)
    half = sums.shape[0] // 2
    for h in (0, half):
        sums[h : h + half] += dot(hot[h : h + half], cots[...])

    @pl.when(step == pl.num_programs(0) - 1)
    def _():
        total = sums[...]
        book = codebook_t[...].astype(F32)
        w = lax.dot_general(book, total, NN, precision=lax.Precision.HIGHEST, preferred_element_type=F32)
        bias = jnp.sum(total, axis=0, keepdims=True)
        embed = w.shape[0]
        grads[0:embed] = w
        grads[embed : embed + 8] = jnp.broadcast_to(bias, (8, HALF))


def decode_images(plan, steps, heights, codes, codebook_t, decode_w, decode_b, _, decoded, token, table):
    step = pl.program_id(0)
    token[...] = jnp.zeros_like(token)
    group = plan.images // steps

    @pl.when(step == 0)
    def _():
        full = dot(codebook_t[...], decode_w[...], TN) + decode_b[...].astype(F32)
        table[...] = full.T.astype(BF16)

    spots = SIDE * SIDE
    code_of = numbers(codebook_t.shape[1], spots)
    spot = lax.broadcasted_iota(jnp.int32, (spots, 1), 0)
    for i in range(group):
        live = heights[step * group + i] * SIDE
        out = dot(table[...], one_hot_columns(codes[i : i + 1, :], code_of)).T
        decoded[i] = jnp.where(spot < live, out, 0.0).astype(BF16).reshape(SIDE, SIDE, HALF)


def put_codes(code_rows, codes, b, height, dst):
    spot = lax.broadcasted_iota(jnp.int32, (1, SIDE * SIDE), 1)
    lane = lax.broadcasted_iota(jnp.int32, (1, HALF), 1)
    per_row = HALF // SIDE
    row = jnp.where(spot < height * SIDE, codes[pl.ds(b, 1), :], -1)
    turn = lax.rem(dst, per_row) * SIDE
    upper = pltpu.roll(row[:, :HALF], turn, 1)
    lower = pltpu.roll(row[:, HALF:], turn, 1)
    inside = lane >= turn
    pieces = (jnp.where(inside, upper, -1), jnp.where(inside, lower, upper), jnp.where(inside, -1, lower))
    for i, piece in enumerate(pieces):
        target = pl.ds(dst // per_row + i, 1)
        code_rows[target, :] = jnp.where(piece < 0, code_rows[target, :], piece)


def gelu_parts(v):
    square = v * v
    t = jnp.tanh(v * (GELU_SCALE + (GELU_SCALE * GELU_CUBE) * square))
    half = 0.5 + 0.5 * t
    slope = half + (0.5 * v) * (1.0 - t * t) * (GELU_SCALE + (3.0 * GELU_SCALE * GELU_CUBE) * square)
    return v * half, slope


def main_step(plan, layout, k, waits, *refs):
    first_step = k == 0
    fresh = k in (0, plan.usual)
    final = k == plan.usual - 1
    refs = list(refs[waits:])

    def take(count):
        got = refs[:count]
        del refs[:count]
        return got

    if final:
        place, decode_acc = take(2)
    meta, heights, x_own, x_far, q_own, q_far, codes = take(7)
    kernel_hbm, kernel_t_hbm, mix, project, bias, book = take(6)
    if not first_step:
        x_past, q_past, carry_own, carry_far = take(4)
    if not fresh:
        past_accs = take(5)
    win_own, win_far, next_own, next_far = take(4)
    if final:
        laid_out = take(3)
    if not final:
        sums_out = take(5)
    kernel_acc, mix_acc, project_acc, book_acc, bias_acc = take(5)
    kernel, kernel_t, weight_sems = take(3)
    xo, xf, qo, qf, qd, xc_o, xc_f, qc, code_rows, act3, slope_x, grad3, block_g = take(13)
    second_s, slope_s, low_s, mixed_s, code_s, hot_s, found_s, diff_s, sems = refs

    chunk, start = plan.chunks[k], plan.starts[k]
    images, rows, block = plan.images, plan.rows[k], plan.block[k]
    half = chunk // 2
    spots = block * SIDE
    low = meta[images + k]
    high = meta[images + k + 1]

    copies = [
        (x_own.at[pl.ds(start, LEAD + chunk)], xo.at[pl.ds(0, LEAD + chunk)]),
        (x_far, xf.at[pl.ds(LEAD, chunk)]),
        (q_own.at[pl.ds(start // 2, half)], qo.at[pl.ds(LEAD, half)]),
        (q_far, qf.at[pl.ds(LEAD, half)]),
    ]
    if not first_step:
        past = plan.chunks[k - 1]
        copies += [
            (x_past.at[pl.ds(past - LEAD, LEAD)], xf.at[pl.ds(0, LEAD)]),
            (q_own.at[pl.ds(start // 2 - LEAD, LEAD)], qo.at[pl.ds(0, LEAD)]),
            (q_past.at[pl.ds(past // 2 - LEAD, LEAD)], qf.at[pl.ds(0, LEAD)]),
        ]
    accs = (mix_acc, project_acc, book_acc, bias_acc, kernel_acc)
    early = len(copies)
    if not fresh:
        copies += list(zip(past_accs[1:] + past_accs[:1], accs))
    weight_copies = []
    for i, (source, target) in enumerate(((kernel_hbm, kernel), (kernel_t_hbm, kernel_t))):
        weight_copies.append(pltpu.make_async_copy(source, target, weight_sems.at[i]))
    started = []
    for i, (source, target) in enumerate(copies):
        started.append(pltpu.make_async_copy(source, target, sems.at[i]))
        started[-1].start()
    for copy in weight_copies:
        copy.start()
    started, later = started[:early], started[early:]

    if fresh:
        for acc in accs:
            acc[...] = jnp.zeros(acc.shape, F32)

    blank = jnp.zeros((SIDE, SIDE, HALF), BF16)
    no_row = jnp.full((SIDE, SIDE, HALF), MARK, F32)
    code_rows[...] = jnp.full(code_rows.shape, -1, jnp.int32)
    for r in range(0, rows + 2 * block, SIDE):
        part = pl.ds(r, SIDE)
        xc_o[part] = blank
        xc_f[part] = blank
        if r < rows:
            qc[part] = no_row
    for copy in started:
        copy.wait()

    lane3 = lax.broadcasted_iota(jnp.int32, (1, SIDE, HALF), 2) < HALF // 2

    def spread(r0, count):
        both = (qo[pl.ds(r0, count)] + qf[pl.ds(r0, count)].astype(F32)).reshape(count * SIDE, HALF)
        turned = pltpu.roll(both, HALF // 2, 1).reshape(count, SIDE, HALF)
        both = both.reshape(count, SIDE, HALF)
        return jnp.where(lane3, both, turned), jnp.where(lane3, turned, both)

    upper, lower = spread(LEAD, half)
    qd[pl.ds(LEAD, half)] = upper
    qd[pl.ds(LEAD + half, half)] = lower
    if not first_step:
        _, lower = spread(0, LEAD)
        qd[0:LEAD] = lower

    per_row = HALF // SIDE

    def put(b, dst):
        src = meta[b] - start + LEAD
        xc_o[pl.ds(dst, SIDE)] = xo[pl.ds(src, SIDE)]
        xc_f[pl.ds(dst, SIDE)] = xf[pl.ds(src, SIDE)]
        qc[pl.ds(dst, SIDE)] = qd[pl.ds(src, SIDE)]
        end = dst + heights[b]
        xc_o[pl.ds(end, SIDE)] = blank
        xc_f[pl.ds(end, SIDE)] = blank
        qc[pl.ds(end, SIDE)] = no_row
        put_codes(code_rows, codes, b, heights[b], dst)
        return end + 1

    used = lax.fori_loop(low, high, put, jnp.int32(1))
    blocks = jnp.where(high > low, (used + (block - 1)) // block, 0)

    column = lax.rem(lax.broadcasted_iota(jnp.int32, (TILE, 1), 0), SIDE)
    not_first = column != 0
    not_last = column != SIDE - 1

    def shifted(value):
        back = jnp.where(not_first, pltpu.roll(value, 1, 0), 0.0)
        ahead = jnp.where(not_last, pltpu.roll(value, TILE - 1, 0), 0.0)
        return back.astype(BF16), ahead.astype(BF16)

    edge = jnp.zeros((SIDE, 3 * 2 * HALF), BF16)
    act3[0:SIDE] = edge
    grad3[0:SIDE] = edge
    beyond = pl.multiple_of((blocks * block + 1) * SIDE, SIDE)
    grad3[pl.ds(beyond, SIDE)] = edge

    tiles = range(0, spots, TILE)

    def read_x(r0, t):
        part = pl.ds(r0 + t // SIDE, TILE // SIDE)
        o = xc_o[part].reshape(TILE, HALF)
        f = xc_f[part].reshape(TILE, HALF)
        return jnp.concatenate([o, f], axis=1).astype(F32)

    def at(row, count=block):
        return pl.ds(pl.multiple_of(row * SIDE, SIDE), count * SIDE)

    def tile_at(row, t):
        return pl.ds(pl.multiple_of(row * SIDE, SIDE) + t, TILE)

    def activate(j, carry):
        r0 = j * block
        for t in tiles:
            value, slope = gelu_parts(read_x(r0, t))
            slope_x[tile_at(r0, t), :] = slope
            back, ahead = shifted(value)
            act3[tile_at(r0 + 1, t), 0 : 2 * HALF] = back
            act3[tile_at(r0 + 1, t), 2 * HALF : 4 * HALF] = value.astype(BF16)
            act3[tile_at(r0 + 1, t), 4 * HALF : 6 * HALF] = ahead
        return carry

    fused = k < plan.usual
    lax.fori_loop(0, 2 if fused else blocks + 1, activate, 0)
    for copy in later:
        copy.wait()
    for copy in weight_copies:
        copy.wait()

    bias_first = bias[0:1, :]
    bias_mix = bias[1:2, :]
    bias_code = bias[8:9, 0:HALF]
    lane = lax.broadcasted_iota(jnp.int32, (1, HALF), 1) < HALF // 2
    hb = block // 2
    hs = hb * SIDE

    def add_rows(total, value):
        value = value.astype(F32)
        for i in range(0, value.shape[0], 8):
            part = value[i : i + 8]
            total = part if total is None else total + part
        return total

    half_tiles = range(0, hs, TILE)
    code_of = numbers(book_acc.shape[0], HALF)
    halves = (0, hs)

    def middle(j, carry):
        r0 = j * block
        for i in range(block // per_row):
            row = code_rows[pl.ds(j * (block // per_row) + i, 1), :]
            hot_s[:, i * HALF : (i + 1) * HALF] = one_hot_columns(row, code_of)
        for h in halves:
            found_s[h : h + hs] = dot(book[...], hot_s[:, h : h + hs]).astype(BF16).T
        pre = []
        for h in halves:
            window = jnp.concatenate([act3[at(r0 + i + h // SIDE, hb), :] for i in range(3)], axis=1)
            pre.append(dot(window, kernel[...]))
        for h, part in zip(halves, pre):
            for t in half_tiles:
                value, slope = gelu_parts(part[t : t + TILE] + bias_first)
                second_s[h + t : h + t + TILE] = value.astype(BF16)
                slope_s[h + t : h + t + TILE] = slope
        mixed = [dot(second_s[h : h + hs], mix[...]) for h in halves]
        for h, part in zip(halves, mixed):
            for t in half_tiles:
                low_s[h + t : h + t + TILE] = (read_x(r0, h + t) + part[t : t + TILE] + bias_mix).astype(BF16)
        latents = [dot(low_s[h : h + hs], project[i]) for i, h in enumerate(halves)]
        total = None
        for t in half_tiles:
            first = pl.ds(r0 + t // SIDE, TILE // SIDE)
            other = pl.ds(r0 + hb + t // SIDE, TILE // SIDE)
            ch = jnp.where(lane, found_s[t : t + TILE].astype(F32), found_s[hs + t : hs + t + TILE].astype(F32))
            q = jnp.where(lane3, qc[first], qc[other]).reshape(TILE, HALF)
            live = q < 0.5 * MARK
            latent = latents[0][t : t + TILE] + latents[1][t : t + TILE] + bias_code
            diff = jnp.where(live, latent - ch, 0.0)
            code_grad = jnp.where(live, q + (2.0 * COMMIT) * diff, 0.0).astype(BF16)
            code_s[t : t + TILE] = code_grad
            total = add_rows(total, code_grad)
            big = diff.astype(BF16).astype(F32)
            small = diff - big
            turned = pltpu.roll(small, HALF // 2, 1)
            diff_s[t : t + TILE] = jnp.where(lane, big, turned).astype(BF16)
            turned = pltpu.roll(big, HALF // 2, 1)
            diff_s[hs + t : hs + t + TILE] = jnp.where(lane, turned, small).astype(BF16)
        bias_acc[16:24, 0:HALF] += total
        total = None
        blocks_g = [dot(code_s[...], project[i], NT) for i in range(2)]
        for h, part in zip(halves, blocks_g):
            for t in half_tiles:
                block_g[tile_at(r0, h + t), :] = part[t : t + TILE]
                mixed_grad = part[t : t + TILE].astype(BF16)
                mixed_s[h + t : h + t + TILE] = mixed_grad
                total = add_rows(total, mixed_grad)
        bias_acc[8:16] += total
        second_grad = [dot(mixed_s[h : h + hs], mix[...], NT) for h in halves]
        total = None
        for h, part in zip(halves, second_grad):
            for t in half_tiles:
                first_grad = slope_s[h + t : h + t + TILE] * part[t : t + TILE]
                back, ahead = shifted(first_grad)
                first_low = first_grad.astype(BF16)
                grad3[tile_at(r0 + 1, h + t), 0 : 2 * HALF] = ahead
                grad3[tile_at(r0 + 1, h + t), 2 * HALF : 4 * HALF] = first_low
                grad3[tile_at(r0 + 1, h + t), 4 * HALF : 6 * HALF] = back
                total = add_rows(total, first_low)
        bias_acc[0:8] += total
        book_acc[...] += dot(hot_s[...], diff_s[...])
        mix_acc[...] += dot(second_s[...], mixed_s[...], TN)
        project_acc[...] += jnp.where(lane, dot(low_s[0:hs], code_s[...], TN), dot(low_s[hs:], code_s[...], TN))
        return carry

    def finish(j, carry):
        r0 = j * block
        active = act3[at(r0 + 1), 2 * HALF : 4 * HALF].T
        for i in range(3):
            kernel_acc[:, i * 6 * HALF : (i + 1) * 6 * HALF] += dot(active, grad3[at(r0 + 2 - i), :])
        grads = []
        for h in halves:
            window = jnp.concatenate([grad3[at(r0 + 2 - i + h // SIDE, hb), :] for i in range(3)], axis=1)
            grads.append(dot(window, kernel_t[...]))
        for h, grad in zip(halves, grads):
            for t in half_tiles:
                here = tile_at(r0, h + t)
                out = (block_g[here, :] + slope_x[here, :] * grad[t : t + TILE]).astype(BF16)
                part = pl.ds(r0 + (h + t) // SIDE, TILE // SIDE)
                xc_o[part] = out[:, :HALF].reshape(TILE // SIDE, SIDE, HALF)
                xc_f[part] = out[:, HALF:].reshape(TILE // SIDE, SIDE, HALF)
        return carry

    def opening(j, carry):
        middle(j, carry)
        return activate(j + 2, carry)

    def steady(j, carry):
        finish(j - 2, carry)
        middle(j, carry)
        return activate(j + 2, carry)

    if fused:
        lax.fori_loop(0, jnp.minimum(blocks, 2), opening, 0)
        lax.fori_loop(2, blocks, steady, 0)
        lax.fori_loop(jnp.maximum(blocks - 2, 0), blocks, finish, 0)
    else:
        lax.fori_loop(0, blocks, middle, 0)
        lax.fori_loop(0, blocks, finish, 0)
    leaving = []
    if not final:
        leaving += list(zip((kernel_acc, mix_acc, project_acc, book_acc, bias_acc), sums_out))
        for i, (source, target) in enumerate(leaving):
            leaving[i] = pltpu.make_async_copy(source, target, sems.at[i])
            leaving[i].start()

    out_o, out_f = xo, xf
    if first_step:
        out_o[0:LEAD] = blank
        out_f[0:LEAD] = blank
    else:
        out_o[0:LEAD] = carry_own[...]
        out_f[0:LEAD] = carry_far[...]

    def collect(b, src):
        dst = meta[b] - start + LEAD
        out_o[pl.ds(dst, SIDE)] = xc_o[pl.ds(src, SIDE)]
        out_f[pl.ds(dst, SIDE)] = xc_f[pl.ds(src, SIDE)]
        return src + heights[b] + 1

    lax.fori_loop(low, high, collect, jnp.int32(1))
    size = win_own.shape[0]
    windows = (
        (out_o.at[pl.ds(0, size)], win_own),
        (out_f.at[pl.ds(0, size)], win_far),
        (out_o.at[pl.ds(chunk, LEAD)], next_own),
        (out_f.at[pl.ds(chunk, LEAD)], next_far),
    )
    for i, (source, target) in enumerate(windows):
        leaving.append(pltpu.make_async_copy(source, target, sems.at[5 + i]))
        leaving[-1].start()
    if final:
        sums = (kernel_acc, mix_acc, project_acc, book_acc, bias_acc, decode_acc)
        laid_out += [slope_x.at[pl.ds(0, layout.rows), pl.ds(i * HALF, HALF)] for i in range(2)]
        leaving += gather_grads(plan, layout, place, meta, sums, *laid_out, sems)
    for copy in leaving:
        copy.wait()


class Layout:
    def __init__(self, devices, book_rows, embed):
        self.mix = 9 * 2 * HALF
        self.project = self.mix + 2 * HALF
        self.book = self.project + HALF // 2
        self.bias = self.book + book_rows // 2
        self.decode = self.bias + 8
        used = self.decode + embed + 8
        self.devices = devices
        self.piece = -(-used // (devices * SIDE)) * SIDE
        self.rows = self.piece * devices
        self.half = self.rows // 2
        self.used = used


def lay_out(layout, swap, kernel_acc, mix_acc, project_acc, book_acc, bias_acc, decode_acc, own, far):
    def lanes(value):
        return value[:, :HALF], value[:, HALF:]

    def order(first, second):
        return jnp.where(swap, second, first), jnp.where(swap, first, second)

    row = 0
    for tap in range(9):
        block = kernel_acc[:, tap * 2 * HALF : (tap + 1) * 2 * HALF]
        mine, theirs = lanes(block)
        a, b = order(mine[:HALF], mine[HALF:])
        own[row : row + HALF] = a
        own[row + HALF : row + 2 * HALF] = b
        a, b = order(theirs[:HALF], theirs[HALF:])
        far[row : row + HALF] = a
        far[row + HALF : row + 2 * HALF] = b
        row += 2 * HALF
    row = layout.mix
    for target, part in ((own, mix_acc[:HALF]), (far, mix_acc[HALF:])):
        a, b = order(*lanes(part))
        target[row : row + HALF] = a
        target[row + HALF : row + 2 * HALF] = b
    row = layout.project
    side = HALF // 2
    for target, part in ((own, project_acc[:HALF]), (far, project_acc[HALF:])):
        part = part + pltpu.roll(part, side, 1)
        target[row : row + side] = part.T[:side]
    row = layout.book
    book = book_acc[...]
    book = -2.0 * (book + pltpu.roll(book, side, 1))
    book = book.T[:side]
    for c in range(book.shape[1] // HALF):
        part = book[:, c * HALF : (c + 1) * HALF]
        own[row + c * side : row + (c + 1) * side] = part
        far[row + c * side : row + (c + 1) * side] = part
    row = layout.bias
    sums = [jnp.sum(bias_acc[8 * i : 8 * i + 8], axis=0, keepdims=True) for i in range(3)]
    code = sums[2][:, :HALF]
    code = code + pltpu.roll(code, side, 1)
    which = lax.broadcasted_iota(jnp.int32, (8, HALF), 0)
    for target, first in ((own, 0), (far, HALF)):
        part = jnp.where(which == 0, sums[0][:, first : first + HALF], sums[1][:, first : first + HALF])
        target[row : row + 8] = jnp.where(which == 2, code, jnp.where(which < 2, part, 0.0))
    row = layout.decode
    rest = layout.rows - row
    own[row:] = jnp.zeros((rest, HALF), F32)
    far[row:] = jnp.zeros((rest, HALF), F32)
    if decode_acc is not None:
        own[row : row + decode_acc.shape[0]] = decode_acc[...]


def gather_plain(layout, place, *refs):
    lay_out(layout, place[0] == 1, *refs[:5], None, *refs[5:])


def gather_grads(plan, layout, place, meta, accs, keep_own, keep_far, send, own, far, sems):
    lay_out(layout, place[0] == 1, *accs, own, far)
    base = plan.images + len(plan.chunks) + 1
    over = (meta[base + 4] > plan.covered).astype(F32)
    which = lax.broadcasted_iota(jnp.int32, (8, HALF), 0)
    row = layout.bias
    own[row : row + 8] = jnp.where(which == 3, over, own[row : row + 8])
    half = layout.half
    mine = pl.ds(pl.multiple_of(place[1] * half, SIDE), half)
    other = pl.ds(pl.multiple_of((1 - place[1]) * half, SIDE), half)
    kept = []
    for i, (source, target) in enumerate(((own, keep_own), (far, keep_far))):
        kept.append(pltpu.make_async_copy(source.at[mine, :], target, sems.at[9 + i]))
        kept[-1].start()
    send[0] = own[other, :].astype(BF16)
    send[1] = far[other, :].astype(BF16)
    return kept


def hold(*refs):
    pass


def add_core(place, keep_own, keep_far, came, out, token):
    token[...] = jnp.zeros_like(token)
    mine = place[0]
    chips, piece = out.shape[0] // 2, out.shape[1]
    for c in range(chips):
        rows = pl.ds(c * piece, piece)
        out[2 * c + mine] = (keep_own[rows] + came[0, rows].astype(F32)).astype(BF16)
        out[2 * c + 1 - mine] = (keep_far[rows] + came[1, rows].astype(F32)).astype(BF16)


def add_pieces(pieces, *rest):
    out = rest[-1]
    total = pieces[0].astype(F32)
    for i in range(1, pieces.shape[0]):
        total = total + pieces[i].astype(F32)
    out[...] = jnp.broadcast_to(total.astype(BF16)[None], out.shape)


def write_grads(layout, place, mine, theirs, kernel, first_bias, mix, mix_bias, project, project_bias, book, decode, decode_bias, whole):
    half = layout.half
    whole[pl.ds(pl.multiple_of(place[1] * half, SIDE), half), :] = mine[...].astype(F32)
    whole[pl.ds(pl.multiple_of((1 - place[1]) * half, SIDE), half), :] = theirs[...].astype(F32)
    split_grads(layout, whole, kernel, first_bias, mix, mix_bias, project, project_bias, book, decode, decode_bias)


def split_grads(layout, whole, kernel, first_bias, mix, mix_bias, project, project_bias, book, decode, decode_bias):
    for tap in range(9):
        kernel[tap] = whole[tap * 2 * HALF : (tap + 1) * 2 * HALF]
    row = layout.mix
    mix[:, :HALF] = whole[row : row + HALF]
    mix[:, HALF:] = whole[row + HALF : row + 2 * HALF]
    side = HALF // 2
    for row, target in ((layout.project, project), (layout.book, book)):
        for c in range(target.shape[1] // HALF):
            target[:, c * HALF : (c + 1) * HALF] = whole[row + c * side : row + (c + 1) * side]
    row = layout.bias
    first_bias[...] = whole[row : row + 1]
    mix_bias[...] = whole[row + 1 : row + 2]
    project_bias[...] = whole[row + 2 : row + 3, :side]
    row = layout.decode
    n = decode.shape[0]
    decode[...] = whole[row : row + n]
    decode_bias[...] = whole[row + n : row + n + 1]


def split_again(layout, total, extra, *refs):
    whole = refs[-1]
    whole[...] = total[...].astype(F32) + extra[...]
    split_grads(layout, whole, *refs[:-1])


def restore_rows(plan, n, waits, *refs):
    meta, heights, *refs = refs[waits:]
    own, far, out, token = refs[:n], refs[n : 2 * n], refs[2 * n], refs[2 * n + 1]
    token[...] = jnp.zeros_like(token)
    stage_own, stage_far, sems = refs[2 * n + 2 :]
    copies = []
    for k in range(n):
        size = plan.chunks[k] + (LEAD if k == n - 1 else 0)
        for i, (source, target) in enumerate(((own[k], stage_own), (far[k], stage_far))):
            from_rows = source.at[pl.ds(0, size)]
            copies.append(pltpu.make_async_copy(from_rows, target.at[pl.ds(plan.starts[k], size)], sems.at[i, k]))
            copies[-1].start()
    for copy in copies:
        copy.wait()
    base = plan.images + len(plan.chunks) + 1
    own_row, send_row = meta[base], meta[base + 1]
    first, last = meta[base + 2], meta[base + 3]
    row_of = lax.broadcasted_iota(jnp.int32, (SIDE, 1, 1), 0)

    def own_image(b, carry):
        rows = stage_own[pl.ds(meta[b] + LEAD, SIDE)]
        out[b] = jnp.where(row_of < heights[b], rows, jnp.zeros_like(rows))
        return carry

    def far_image(b, carry):
        rows = stage_far[pl.ds(meta[b] + own_row - send_row + LEAD, SIDE)]
        out[b] = jnp.where(row_of < heights[b], rows, jnp.zeros_like(rows))
        return carry

    lax.fori_loop(first, last, own_image, 0)
    lax.fori_loop(0, first, far_image, 0)
    lax.fori_loop(last, plan.images, far_image, 0)


def trade(value):
    return lax.ppermute(value, "mp", [(0, 1), (1, 0)])


def held(value, *others):
    return pl.pallas_call(
        hold,
        out_shape=shape(value.shape, value.dtype),
        in_specs=[ANY] * (1 + len(others)),
        out_specs=ANY,
        input_output_aliases={0: 0},
        compiler_params=params(60),
        name="hold",
    )(value, *others)


def run_main(plan, layout, k, meta, heights, streams, weights, state, waits=(), ending=()):
    chunk, rows, block = plan.chunks[k], plan.rows[k], plan.block[k]
    last = k >= plan.usual - 1
    final = k == plan.usual - 1
    x_own, x_far, q_own, q_far, codes = streams
    book_rows = weights[-1].shape[1]
    args = [*waits, *ending, meta, heights, x_own, x_far[k], q_own, q_far[k], codes, *weights]
    specs = [ANY] * len(waits) + ([SMEM, VMEM] if final else [])
    specs += [SMEM, SMEM, ANY, ANY, ANY, ANY, VMEM, ANY, ANY] + [VMEM] * (len(weights) - 2)
    alias = {}
    if state is not None:
        args += [x_far[k - 1], q_far[k - 1], *state]
        specs += [ANY, ANY, VMEM, VMEM] + [ANY] * (len(state) - 2)
        if not final:
            for i in range(len(state) - 2):
                alias[len(args) - 5 + i] = 4 + i
    size = chunk + LEAD if last else chunk
    tile = (SIDE, HALF)
    outs = [shape((size,) + tile, BF16)] * 2 + [shape((LEAD,) + tile, BF16)] * 2
    sums = [(2 * HALF, 18 * HALF), (2 * HALF, 2 * HALF), (2 * HALF, HALF), (book_rows, HALF), (24, 2 * HALF)]
    scratch = [pltpu.VMEM(dims, F32) for dims in sums]
    out_specs = [ANY] * 4
    if final:
        outs += [shape((layout.half, HALF), F32)] * 2 + [shape((2, layout.half, HALF), BF16)]
        out_specs += [ANY, ANY, VMEM]
    else:
        outs += [shape(dims, F32) for dims in sums]
        out_specs += [ANY] * 5
    scratch += [pltpu.VMEM((18 * HALF, 2 * HALF), BF16)] * 2 + [pltpu.SemaphoreType.DMA((2,))]
    half = chunk // 2
    spots = block * SIDE
    scratch += [
        pltpu.VMEM((LEAD + chunk + 2 * SIDE,) + tile, BF16),
        pltpu.VMEM((LEAD + chunk + 2 * SIDE,) + tile, BF16),
        pltpu.VMEM((LEAD + half,) + tile, F32),
        pltpu.VMEM((LEAD + half,) + tile, BF16),
        pltpu.VMEM((LEAD + chunk + SIDE,) + tile, F32),
        pltpu.VMEM((rows + 2 * block + SIDE,) + tile, BF16),
        pltpu.VMEM((rows + 2 * block + SIDE,) + tile, BF16),
        pltpu.VMEM((rows + 2 * SIDE,) + tile, F32),
        pltpu.VMEM((-(-(rows * SIDE // HALF + 4) // 8) * 8, HALF), jnp.int32),
        pltpu.VMEM(((rows + 2 * block + 2) * SIDE, 6 * HALF), BF16),
        pltpu.VMEM(((rows + 2 * block) * SIDE, 2 * HALF), F32),
        pltpu.VMEM(((rows + 2) * SIDE, 6 * HALF), BF16),
        pltpu.VMEM((rows * SIDE, 2 * HALF), F32),
        pltpu.VMEM((spots, 2 * HALF), BF16),
        pltpu.VMEM((spots, 2 * HALF), F32),
        pltpu.VMEM((spots, 2 * HALF), BF16),
        pltpu.VMEM((spots, 2 * HALF), BF16),
        pltpu.VMEM((spots // 2, HALF), BF16),
        pltpu.VMEM((book_rows, spots), BF16),
        pltpu.VMEM((spots, HALF), BF16),
        pltpu.VMEM((spots, HALF), BF16),
        pltpu.SemaphoreType.DMA((13,)),
    ]
    spots = chunk * SIDE
    return pl.pallas_call(
        functools.partial(main_step, plan, layout, k, len(waits)),
        out_shape=outs,
        in_specs=specs,
        out_specs=out_specs,
        scratch_shapes=scratch,
        input_output_aliases=alias,
        compiler_params=params(58),
        cost_estimate=cost(60 * 65536 * spots, 8 * MIB, 2 * 256 * spots),
        name=f"main_{k}",
    )(*args)


def local(
    image_latents,
    image_heights,
    code_index,
    kernel_three,
    bias_three,
    weight_mix,
    bias_mix,
    weight_project,
    bias_project,
    codebook,
    weight_decode,
    bias_decode,
    out_grad,
):
    images = image_latents.shape[0]
    plan = Plan(images)
    n = len(plan.chunks)
    tile = (SIDE, HALF)
    where = lax.axis_index("mp").astype(jnp.int32)
    core = lax.rem(lax.axis_index("dp").astype(jnp.int32), 2)
    spot = place = jnp.stack([where, core])

    packed = pl.pallas_call(
        functools.partial(pack_latents, plan),
        out_shape=[
            shape((meta_size(plan),), jnp.int32),
            shape((LEAD + plan.total,) + tile, BF16),
        ]
        + [shape((c,) + tile, BF16) for c in plan.chunks],
        in_specs=[SMEM, SMEM, HBM],
        out_specs=[SMEM, ANY] + [ANY] * n,
        scratch_shapes=[
            pltpu.VMEM((images, SIDE) + tile, BF16),
            pltpu.VMEM((plan.packed + SIDE,) + tile, BF16),
            pltpu.SemaphoreType.DMA((8,)),
            pltpu.SemaphoreType.DMA((n + 1,)),
        ],
        compiler_params=params(60),
        cost_estimate=cost(0, 12 * MIB),
        name="pack_latents",
    )(image_heights, place, image_latents)
    meta, x_own, x_send = packed[0], packed[1], packed[2:]

    far_kernel = trade(kernel_three)
    packed = pl.pallas_call(
        functools.partial(pack_code_grads, plan),
        out_shape=[shape((plan.total // 2,) + tile, F32), shape((2 * HALF + HALF // 2 + SIDE, HALF), BF16)]
        + [shape((c // 2,) + tile, BF16) for c in plan.chunks],
        in_specs=[SMEM] + [HBM] * 6 + [SMEM],
        out_specs=[VMEM] * (n + 2),
        scratch_shapes=[
            pltpu.VMEM((images, SIDE) + tile, BF16),
            pltpu.VMEM((plan.packed + SIDE,) + tile, BF16),
            pltpu.SemaphoreType.DMA((8,)),
            pltpu.SemaphoreType.DMA((5,)),
            pltpu.VMEM(weight_decode.shape, BF16),
            pltpu.VMEM(weight_mix.shape, BF16),
            pltpu.VMEM(weight_project.shape[::-1], BF16),
            pltpu.VMEM((1, HALF), BF16),
            pltpu.VMEM((1, HALF), BF16),
        ],
        compiler_params=params(60),
        cost_estimate=cost(2 * 2 * plan.total * SIDE * 256 * 128, 10 * MIB),
        name="pack_code_grads",
    )(meta, out_grad, weight_decode, weight_mix, weight_project.T, bias_three.reshape(1, HALF), bias_mix.reshape(1, HALF), meta)
    q_own, small, q_send = packed[0], packed[1], packed[2:]

    book_rows, embed = codebook.shape
    codebook_t = codebook.T
    far_small = trade(small)
    usual = plan.usual
    x_far, q_far = [], []
    x_far.append(trade(x_send[0]))
    q_far.append(trade(q_send[0]))

    weights = pl.pallas_call(
        prepare_weights,
        out_shape=[
            shape((18 * HALF, 2 * HALF), BF16),
            shape((18 * HALF, 2 * HALF), BF16),
            shape((2 * HALF, 2 * HALF), BF16),
            shape((2, 2 * HALF, HALF), BF16),
            shape((SIDE, 2 * HALF), F32),
            shape((HALF, book_rows), BF16),
        ],
        in_specs=[SMEM, HBM, HBM] + [VMEM] * 4,
        out_specs=[VMEM] * 6,
        scratch_shapes=[pltpu.VMEM(kernel_three.shape, BF16)] * 2 + [pltpu.SemaphoreType.DMA((2,))],
        compiler_params=params(60),
        cost_estimate=cost(0, 5 * MIB),
        name="prepare_weights",
    )(place, kernel_three, far_kernel, small, far_small, bias_project.reshape(1, -1), codebook_t)

    groups = 8
    group = images // groups
    codes = code_index.reshape(images, SIDE * SIDE)
    whole = lambda dims: pl.BlockSpec(dims, lambda g: (0,) * len(dims))
    four = pl.BlockSpec((group, SIDE) + tile, lambda g: (g, 0, 0, 0))
    row = pl.BlockSpec((group, SIDE * SIDE), lambda g: (g, 0))
    def code_sums(first, steps):
        return pl.pallas_call(
            functools.partial(sum_codes, first, group),
            grid=(steps,),
            out_shape=shape((embed + 8, HALF), F32),
            in_specs=[
                SMEM,
                pl.BlockSpec((group, SIDE * SIDE), lambda g: (g + first, 0)),
                pl.BlockSpec((group, SIDE) + tile, lambda g: (g + first, 0, 0, 0)),
                whole((embed, book_rows)),
                ANY,
                ANY,
            ],
            out_specs=whole((embed + 8, HALF)),
            scratch_shapes=[
                pltpu.VMEM((book_rows, group * SIDE * SIDE), BF16),
                pltpu.VMEM((group * SIDE * SIDE, HALF), BF16),
                pltpu.VMEM((book_rows, HALF), F32),
            ],
            compiler_params=params(60),
            cost_estimate=cost(steps * group * 256 * 512 * 256, steps * group * 65536),
            name=f"sum_codes_{first}",
        )(image_heights, codes, out_grad, codebook_t, small, far_kernel)

    def decode(after):
        return pl.pallas_call(
            functools.partial(decode_images, plan, groups),
            grid=(groups,),
            out_shape=[shape((images, SIDE) + tile, BF16), shape((8, HALF), F32)],
            in_specs=[SMEM, row, whole((embed, book_rows)), whole((embed, HALF)), whole((1, HALF)), ANY],
            out_specs=[four, whole((8, HALF))],
            scratch_shapes=[pltpu.VMEM((HALF, book_rows), BF16)],
            compiler_params=params(32),
            cost_estimate=cost(images * 256 * 512 * 256, 5 * MIB),
            name="decode_images",
        )(image_heights, codes, codebook_t, weight_decode, bias_decode.reshape(1, HALF), after)

    decode_acc = code_sums(0, groups)
    decoded, token = decode(decode_acc)
    for k in range(1, usual):
        x_far.append(trade(held(x_send[k], token, far_small, x_far[0], q_far[0])))
        q_far.append(trade(held(q_send[k], token, far_small, x_far[0], q_far[0])))

    devices = lax.axis_size("dp")
    layout = Layout(devices, book_rows, embed)
    half, piece, chips = layout.half, layout.piece, devices // 2
    streams = (x_own, x_far, q_own, q_far, codes)
    state = None
    win_own, win_far = [], []
    for k in range(usual):
        waits = win_far[k - 2 : k - 1] if k > 1 else []
        ending = (spot, decode_acc) if k == usual - 1 else ()
        outs = run_main(plan, layout, k, meta, image_heights, streams, weights, state, waits, ending)
        win_own.append(outs[0])
        if k < usual - 1:
            win_far.append(trade(outs[1]))
        state = outs[2:]
    last_window = outs[1]
    carry, (keep_own, keep_far, send) = state[:2], state[2:]

    def restore(own, far, waits=()):
        count = len(own)
        return pl.pallas_call(
            functools.partial(restore_rows, plan, count, len(waits)),
            out_shape=[shape((images, SIDE) + tile, BF16), shape((8, HALF), F32)],
            in_specs=[ANY] * len(waits) + [SMEM, SMEM] + [ANY] * (2 * count),
            out_specs=[VMEM, VMEM],
            scratch_shapes=[
                pltpu.VMEM((plan.total + LEAD + SIDE,) + tile, BF16),
                pltpu.VMEM((plan.total + LEAD + SIDE,) + tile, BF16),
                pltpu.SemaphoreType.DMA((2, count)),
            ],
            compiler_params=params(60),
            cost_estimate=cost(0, 10 * MIB),
            name="restore_rows",
        )(*waits, meta, image_heights, *own, *far)

    across = [(i, i ^ 1) for i in range(devices)]

    def step(body, out, name, *args, waits=()):
        specs = [VMEM] * len(args) + [ANY] * len(waits)
        args = (*args, *waits)
        return pl.pallas_call(
            body,
            out_shape=out,
            in_specs=specs,
            out_specs=[VMEM] * len(out) if isinstance(out, list) else VMEM,
            compiler_params=params(24),
            cost_estimate=cost(0, 2 * MIB),
            name=name,
        )(*args)

    send = held(send, win_far[usual - 2])
    came = lax.ppermute(send, "dp", across)
    win_far.append(trade(last_window))
    mine, token = pl.pallas_call(
        add_core,
        out_shape=[shape((2 * chips, piece, HALF), BF16), shape((8, HALF), F32)],
        in_specs=[SMEM] + [VMEM] * 3,
        out_specs=[VMEM, VMEM],
        compiler_params=params(24),
        cost_estimate=cost(0, 4 * MIB),
        name="add_core",
    )(spot, keep_own, keep_far, came)
    both = [[2 * i + j for i in range(devices) if i % 2 == c for j in range(2)] for c in range(2)]
    cores = [[i for i in range(devices) if i % 2 == c] for c in range(2)]
    mine = lax.all_to_all(mine, ("dp", "mp"), 0, 0, axis_index_groups=both, tiled=True)
    mine = step(add_pieces, shape((chips, piece, HALF), BF16), "add_pieces", mine, waits=[win_far[usual - 1]])
    latents_grad, token = restore(win_own, win_far, [mine])
    mine = lax.all_to_all(mine, "dp", 0, 0, axis_index_groups=cores, tiled=True)
    mine = held(mine, token).reshape(half, HALF)
    theirs = lax.ppermute(mine, "dp", across)

    grads_out = [
        shape((9, 2 * HALF, HALF), F32),
        shape((1, HALF), F32),
        shape((HALF, 2 * HALF), F32),
        shape((1, HALF), F32),
        shape((embed, HALF), F32),
        shape((1, embed), F32),
        shape((embed, book_rows), F32),
        shape((embed, HALF), F32),
        shape((1, HALF), F32),
    ]
    whole = pltpu.VMEM((layout.rows, HALF), F32)

    def usual_end(latents_grad):
        grads = pl.pallas_call(
            functools.partial(write_grads, layout),
            out_shape=grads_out,
            in_specs=[SMEM, VMEM, VMEM],
            out_specs=[VMEM] * 9,
            scratch_shapes=[whole],
            compiler_params=params(24),
            cost_estimate=cost(0, 4 * MIB),
            name="write_grads",
        )(spot, mine, theirs)
        return (latents_grad, *grads)

    def longer_end(latents_grad):
        last_x, last_q = trade(x_send[usual]), trade(q_send[usual])
        streams = (x_own, x_far + [last_x], q_own, q_far + [last_q], codes)
        outs = run_main(plan, layout, usual, meta, image_heights, streams, weights, carry)
        latents_grad, _ = restore(win_own + [outs[0]], win_far + [trade(outs[1])])
        own, far = pl.pallas_call(
            functools.partial(gather_plain, layout),
            out_shape=[shape((layout.rows, HALF), F32)] * 2,
            in_specs=[SMEM] + [VMEM] * 5,
            out_specs=[VMEM] * 2,
            compiler_params=params(40),
            name="gather_plain",
        )(spot, *outs[4:])
        extra = lax.psum(own + trade(far), "dp")
        first, second = jnp.where(core == 0, mine, theirs), jnp.where(core == 0, theirs, mine)
        grads = pl.pallas_call(
            functools.partial(split_again, layout),
            out_shape=grads_out,
            in_specs=[VMEM, VMEM],
            out_specs=[VMEM] * 9,
            scratch_shapes=[whole],
            compiler_params=params(24),
            name="split_again",
        )(jnp.concatenate([first, second]), extra)
        return (latents_grad, *grads)

    flag = layout.bias + 3
    holder = flag // half
    flags = jnp.where(core == holder, mine[flag - holder * half, 0], theirs[flag - holder * half, 0])
    ends = lax.cond(flags.astype(F32) > 0.5, longer_end, usual_end, latents_grad)
    latents_grad, kernel_grad, first_bias, mix_grad, mix_bias, project_grad, project_bias, book, decode, decode_bias = ends
    return (
        decoded,
        latents_grad,
        kernel_grad,
        first_bias.reshape(HALF),
        mix_grad,
        mix_bias.reshape(HALF),
        project_grad.T,
        project_bias.reshape(embed),
        book.T,
        decode,
        decode_bias.reshape(HALF),
    )


def solution(mesh):
    tile = P("dp", None, None, "mp")
    placed = (
        tile,
        P("dp"),
        P("dp", None, None),
        P(None, None, "mp"),
        P("mp"),
        P("mp", None),
        P("mp"),
        P("mp", None),
        P(),
        P(),
        P(None, "mp"),
        P("mp"),
        tile,
    )
    outs = (
        tile,
        tile,
        P(None, None, "mp"),
        P("mp"),
        P("mp", None),
        P("mp"),
        P("mp", None),
        P(),
        P(),
        P(None, "mp"),
        P("mp"),
    )
    return jax.shard_map(local, mesh=mesh, in_specs=placed, out_specs=outs, check_vma=False)
```

```python
import functools

import jax
import jax.numpy as jnp
from jax import lax
from jax.experimental import pallas as pl
from jax.experimental.pallas import tpu as pltpu
from jax.sharding import PartitionSpec as P

SIDE = 16
HALF = 128
LEAD = 16
BLOCK = 32
TILE = 32
MARK = 1e9
GELU_SCALE = 0.7978845608028654
GELU_CUBE = 0.044715
COMMIT = 0.25
F32 = jnp.float32
BF16 = jnp.bfloat16
ANY = pl.BlockSpec(memory_space=pl.ANY)
SMEM = pl.BlockSpec(memory_space=pltpu.SMEM)
HBM = pl.BlockSpec(memory_space=pltpu.HBM)
VMEM = pl.BlockSpec(memory_space=pltpu.VMEM)
MIB = 1 << 20

NT = (((1,), (1,)), ((), ()))
TN = (((0,), (0,)), ((), ()))
NN = (((1,), (0,)), ((), ()))


def dot(a, b, dims=NN):
    return lax.dot_general(a, b, dims, preferred_element_type=F32)


def one_hot_columns(codes, code_of):
    return jnp.where(code_of == codes.astype(jnp.int16), jnp.bfloat16(1), jnp.bfloat16(0))


def numbers(count, width):
    return lax.broadcasted_iota(jnp.int32, (count, width), 0).astype(jnp.int16)


def shape(dims, kind):
    return jax.ShapeDtypeStruct(dims, kind)


def params(mib):
    return pltpu.CompilerParams(vmem_limit_bytes=mib * MIB)


def cost(flops, moved, slow=0):
    return pl.CostEstimate(flops=flops, bytes_accessed=moved, transcendentals=slow)


class Plan:
    def __init__(self, images):
        self.images = images
        longest = images * SIDE // 2 + SIDE // 2
        part = images // 8
        self.chunks = [19 * part, 29 * part]
        self.usual = len(self.chunks)
        rest = longest - sum(self.chunks)
        self.chunks.append(rest)
        self.starts = [sum(self.chunks[:k]) for k in range(len(self.chunks))]
        self.total = sum(self.chunks)
        self.packed = -(-(LEAD + longest + self.total + LEAD) // SIDE) * SIDE
        self.rows, self.block = [], []
        for k, c in enumerate(self.chunks):
            block = BLOCK if k < self.usual else SIDE
            most = 1 + c + 15 + c // 4 + 1
            self.rows.append(-(-most // block) * block)
            self.block.append(block)
        self.covered = sum(self.chunks[: self.usual])


def meta_size(plan):
    return plan.images + len(plan.chunks) + 1 + 5


def plan_rows(plan, heights, place, meta):
    images = plan.images
    base = images + len(plan.chunks) + 1

    def total_of(b, acc):
        return acc + heights[b]

    total = lax.fori_loop(0, images, total_of, jnp.int32(0))

    def split_of(b, state):
        acc, best, split, cut = state
        acc = acc + heights[b]
        worst = jnp.maximum(acc, total - acc)
        better = worst < best
        return (acc, jnp.where(better, worst, best), jnp.where(better, b + 1, split), jnp.where(better, acc, cut))

    _, _, split, cut = lax.fori_loop(0, images, split_of, (jnp.int32(0), jnp.int32(1 << 20), jnp.int32(0), jnp.int32(0)))
    mine = place[0]
    own_first = jnp.where(mine == 0, 0, split)
    own_last = jnp.where(mine == 0, split, images)
    own_row = jnp.where(mine == 0, 0, cut)
    send_row = jnp.where(mine == 0, cut, 0)
    for k in range(len(plan.chunks) + 1):
        meta[images + k] = own_first
    ends = [plan.starts[k] + plan.chunks[k] for k in range(len(plan.chunks))]

    def place_of(b, acc):
        meta[b] = acc - own_row
        acc = acc + heights[b]
        end = acc - own_row
        inside = jnp.logical_and(b >= own_first, b < own_last)
        step = jnp.int32(0)
        for k in range(len(plan.chunks) - 1):
            step = step + (end > ends[k]).astype(jnp.int32)

        @pl.when(inside)
        def _():
            meta[images + 1 + step] = b + 1

        return acc

    lax.fori_loop(0, images, place_of, jnp.int32(0))
    for k in range(len(plan.chunks)):
        meta[images + k + 1] = jnp.maximum(meta[images + k + 1], meta[images + k])
    meta[base] = own_row
    meta[base + 1] = send_row
    meta[base + 2] = own_first
    meta[base + 3] = own_last
    meta[base + 4] = jnp.maximum(cut, total - cut)


def pack_rows(plan, meta, source, packed, piece, count):
    base = plan.images + len(plan.chunks) + 1

    def one(i, carry):
        b = piece * count + i
        row = meta[b] + meta[base] + LEAD
        packed[pl.ds(row, SIDE)] = source[b]
        return carry

    lax.fori_loop(0, count, one, 0)


def pack_latents(plan, heights, place, x_hbm, meta, own, *rest):
    n = len(plan.chunks)
    sends, (x_in, packed, sem_in, sem_out) = rest[:n], rest[n:]
    pieces = 8
    count = plan.images // pieces
    fetch = []
    for p in range(pieces):
        part = pl.ds(p * count, count)
        fetch.append(pltpu.make_async_copy(x_hbm.at[part], x_in.at[part], sem_in.at[p]))
        fetch[-1].start()
    plan_rows(plan, heights, place, meta)
    base = plan.images + n + 1
    for p in range(pieces):
        fetch[p].wait()
        pack_rows(plan, meta, x_in, packed, p, count)
    copies = []
    for k in range(n):
        part = pl.ds(LEAD + meta[base + 1] + plan.starts[k], plan.chunks[k])
        copies.append(pltpu.make_async_copy(packed.at[part], sends[k], sem_out.at[k]))
        copies[-1].start()
    copies.append(pltpu.make_async_copy(packed.at[pl.ds(meta[base], LEAD + plan.total)], own, sem_out.at[n]))
    copies[-1].start()
    for copy in copies:
        copy.wait()


def pack_code_grads(plan, meta, og_hbm, *rest):
    n = len(plan.chunks)
    sources, (own, small), rest = rest[:5], rest[6:8], rest[8:]
    sends, rest = rest[:n], rest[n:]
    og_in, packed, sem_in, sem_small = rest[:4]
    held = rest[4:]
    small_fetch = []
    for i in range(5):
        small_fetch.append(pltpu.make_async_copy(sources[i], held[i], sem_small.at[i]))
        small_fetch[-1].start()
    decode_w, weight_mix, project_t, bias_first, bias_mix = held
    pieces = 8
    count = plan.images // pieces
    fetch = []
    for p in range(pieces):
        part = pl.ds(p * count, count)
        fetch.append(pltpu.make_async_copy(og_hbm.at[part], og_in.at[part], sem_in.at[p]))
        fetch[-1].start()
    base = plan.images + n + 1

    def clear(i, carry):
        packed[pl.ds(i * SIDE, SIDE)] = jnp.zeros((SIDE, SIDE, HALF), BF16)
        return carry

    lax.fori_loop(0, packed.shape[0] // SIDE, clear, 0)
    for copy in small_fetch:
        copy.wait()
    side = HALF // 2
    small[0:HALF] = weight_mix[:, :HALF]
    small[HALF : 2 * HALF] = weight_mix[:, HALF:]
    small[2 * HALF : 2 * HALF + side] = project_t[...]
    which = lax.broadcasted_iota(jnp.int32, (SIDE, HALF), 0)
    first, second = bias_first[...].astype(F32), bias_mix[...].astype(F32)
    first = jnp.where(which == 0, first, jnp.where(which == 1, second, 0.0))
    small[2 * HALF + side : 2 * HALF + side + SIDE] = first.astype(BF16)
    w = decode_w[...]
    blank = jnp.zeros_like(w)
    upper = jnp.concatenate([w, blank], axis=0)
    lower = jnp.concatenate([blank, w], axis=0)
    for p in range(pieces):
        fetch[p].wait()
        pack_rows(plan, meta, og_in, packed, p, count)
    for k in range(n):
        half = plan.chunks[k] // 2
        for which in range(2):
            row = LEAD + meta[base + 1 - which] + plan.starts[k]
            a = packed[pl.ds(row, half)].reshape(half * SIDE, HALF)
            b = packed[pl.ds(row + half, half)].reshape(half * SIDE, HALF)
            both = dot(a, upper, NT) + dot(b, lower, NT)
            both = both.reshape(half, SIDE, HALF)
            if which == 0:
                sends[k][...] = both.astype(BF16)
            else:
                own[pl.ds(plan.starts[k] // 2, half)] = both


def prepare_weights(place, own_hbm, far_hbm, small, far_small, bias_code, codebook_t, *refs):
    forward, backward, mix, project, bias, book, kernel, far_kernel, sems = refs
    copies = []
    for i, (source, target) in enumerate(((own_hbm, kernel), (far_hbm, far_kernel))):
        copies.append(pltpu.make_async_copy(source, target, sems.at[i]))
        copies[-1].start()
    for copy in copies:
        copy.wait()
    first = pl.multiple_of(place[0] * HALF, HALF)
    order = (first, HALF - first)
    for tap in range(9):
        for d, source in enumerate((kernel, far_kernel)):
            for c in range(2):
                tile = source[tap, pl.ds(order[c], HALF), :]
                row = tap * 2 * HALF
                forward[row + c * HALF : row + (c + 1) * HALF, d * HALF : (d + 1) * HALF] = tile
                backward[row + d * HALF : row + (d + 1) * HALF, c * HALF : (c + 1) * HALF] = tile.T
    blank = jnp.zeros((HALF, HALF // 2), BF16)
    for d, source in enumerate((small, far_small)):
        rows = pl.ds(d * HALF, HALF)
        for c in range(2):
            mix[rows, c * HALF : (c + 1) * HALF] = source[pl.ds(order[c], HALF), :]
        part = source[2 * HALF : 2 * HALF + HALF // 2, :].T
        project[0, rows, :] = jnp.concatenate([part, blank], axis=1)
        project[1, rows, :] = jnp.concatenate([blank, part], axis=1)
        bias[0:8, d * HALF : (d + 1) * HALF] = source[2 * HALF + HALF // 2 : 2 * HALF + HALF // 2 + SIDE, :].astype(F32)[0:8]
    code = bias_code[...].astype(F32)
    code = jnp.concatenate([code, code], axis=1)
    bias[8:16, :] = jnp.broadcast_to(jnp.concatenate([code, code], axis=1), (8, 2 * HALF))
    book[...] = jnp.concatenate([codebook_t[...], codebook_t[...]], axis=0)


def sum_codes(first, group, heights, codes, og, codebook_t, _, __, grads, hot, cots, sums):
    step = pl.program_id(0)

    @pl.when(step == 0)
    def _():
        sums[...] = jnp.zeros_like(sums)

    spots = SIDE * SIDE
    code_of = numbers(codebook_t.shape[1], spots)
    spot = lax.broadcasted_iota(jnp.int32, (spots, 1), 0)
    for i in range(group):
        live = heights[(first + step) * group + i] * SIDE
        hot[:, i * spots : (i + 1) * spots] = one_hot_columns(codes[i : i + 1, :], code_of)
        cot = og[i].reshape(spots, HALF).astype(F32)
        cots[i * spots : (i + 1) * spots] = jnp.where(spot < live, cot, 0.0).astype(BF16)
    half = sums.shape[0] // 2
    for h in (0, half):
        sums[h : h + half] += dot(hot[h : h + half], cots[...])

    @pl.when(step == pl.num_programs(0) - 1)
    def _():
        total = sums[...]
        book = codebook_t[...].astype(F32)
        w = lax.dot_general(book, total, NN, precision=lax.Precision.HIGHEST, preferred_element_type=F32)
        bias = jnp.sum(total, axis=0, keepdims=True)
        embed = w.shape[0]
        grads[0:embed] = w
        grads[embed : embed + 8] = jnp.broadcast_to(bias, (8, HALF))


def decode_images(plan, steps, heights, codes, codebook_t, decode_w, decode_b, _, decoded, token, table):
    step = pl.program_id(0)
    token[...] = jnp.zeros_like(token)
    group = plan.images // steps

    @pl.when(step == 0)
    def _():
        full = dot(codebook_t[...], decode_w[...], TN) + decode_b[...].astype(F32)
        table[...] = full.T.astype(BF16)

    spots = SIDE * SIDE
    code_of = numbers(codebook_t.shape[1], spots)
    spot = lax.broadcasted_iota(jnp.int32, (spots, 1), 0)
    for i in range(group):
        live = heights[step * group + i] * SIDE
        out = dot(table[...], one_hot_columns(codes[i : i + 1, :], code_of)).T
        decoded[i] = jnp.where(spot < live, out, 0.0).astype(BF16).reshape(SIDE, SIDE, HALF)


def put_codes(code_rows, codes, b, height, dst):
    spot = lax.broadcasted_iota(jnp.int32, (1, SIDE * SIDE), 1)
    lane = lax.broadcasted_iota(jnp.int32, (1, HALF), 1)
    per_row = HALF // SIDE
    row = jnp.where(spot < height * SIDE, codes[pl.ds(b, 1), :], -1)
    turn = lax.rem(dst, per_row) * SIDE
    upper = pltpu.roll(row[:, :HALF], turn, 1)
    lower = pltpu.roll(row[:, HALF:], turn, 1)
    inside = lane >= turn
    pieces = (jnp.where(inside, upper, -1), jnp.where(inside, lower, upper), jnp.where(inside, -1, lower))
    for i, piece in enumerate(pieces):
        target = pl.ds(dst // per_row + i, 1)
        code_rows[target, :] = jnp.where(piece < 0, code_rows[target, :], piece)


def gelu_parts(v):
    square = v * v
    t = jnp.tanh(v * (GELU_SCALE + (GELU_SCALE * GELU_CUBE) * square))
    half = 0.5 + 0.5 * t
    slope = half + (0.5 * v) * (1.0 - t * t) * (GELU_SCALE + (3.0 * GELU_SCALE * GELU_CUBE) * square)
    return v * half, slope


def main_step(plan, layout, k, waits, *refs):
    first_step = k == 0
    fresh = k in (0, plan.usual)
    final = k == plan.usual - 1
    refs = list(refs[waits:])

    def take(count):
        got = refs[:count]
        del refs[:count]
        return got

    if final:
        place, decode_acc = take(2)
    meta, heights, x_own, x_far, q_own, q_far, codes = take(7)
    kernel_hbm, kernel_t_hbm, mix, project, bias, book = take(6)
    if not first_step:
        x_past, q_past, carry_own, carry_far = take(4)
    if not fresh:
        past_accs = take(5)
    win_own, win_far, next_own, next_far = take(4)
    if final:
        laid_out = take(3)
    if not final:
        sums_out = take(5)
    kernel_acc, mix_acc, project_acc, book_acc, bias_acc = take(5)
    kernel, kernel_t, weight_sems = take(3)
    xo, xf, qo, qf, qd, xc_o, xc_f, qc, code_rows, act3, slope_x, grad3, block_g = take(13)
    second_s, slope_s, low_s, mixed_s, code_s, hot_s, found_s, diff_s, sems = refs

    chunk, start = plan.chunks[k], plan.starts[k]
    images, rows, block = plan.images, plan.rows[k], plan.block[k]
    half = chunk // 2
    spots = block * SIDE
    low = meta[images + k]
    high = meta[images + k + 1]

    copies = [
        (x_own.at[pl.ds(start, LEAD + chunk)], xo.at[pl.ds(0, LEAD + chunk)]),
        (x_far, xf.at[pl.ds(LEAD, chunk)]),
        (q_own.at[pl.ds(start // 2, half)], qo.at[pl.ds(LEAD, half)]),
        (q_far, qf.at[pl.ds(LEAD, half)]),
    ]
    if not first_step:
        past = plan.chunks[k - 1]
        copies += [
            (x_past.at[pl.ds(past - LEAD, LEAD)], xf.at[pl.ds(0, LEAD)]),
            (q_own.at[pl.ds(start // 2 - LEAD, LEAD)], qo.at[pl.ds(0, LEAD)]),
            (q_past.at[pl.ds(past // 2 - LEAD, LEAD)], qf.at[pl.ds(0, LEAD)]),
        ]
    accs = (mix_acc, project_acc, book_acc, bias_acc, kernel_acc)
    early = len(copies)
    if not fresh:
        copies += list(zip(past_accs[1:] + past_accs[:1], accs))
    weight_copies = []
    for i, (source, target) in enumerate(((kernel_hbm, kernel), (kernel_t_hbm, kernel_t))):
        weight_copies.append(pltpu.make_async_copy(source, target, weight_sems.at[i]))
    started = []
    for i, (source, target) in enumerate(copies):
        started.append(pltpu.make_async_copy(source, target, sems.at[i]))
        started[-1].start()
    for copy in weight_copies:
        copy.start()
    started, later = started[:early], started[early:]

    if fresh:
        for acc in accs:
            acc[...] = jnp.zeros(acc.shape, F32)

    blank = jnp.zeros((SIDE, SIDE, HALF), BF16)
    no_row = jnp.full((SIDE, SIDE, HALF), MARK, F32)
    code_rows[...] = jnp.full(code_rows.shape, -1, jnp.int32)
    for r in range(0, rows + 2 * block, SIDE):
        part = pl.ds(r, SIDE)
        xc_o[part] = blank
        xc_f[part] = blank
        if r < rows:
            qc[part] = no_row
    for copy in started:
        copy.wait()

    lane3 = lax.broadcasted_iota(jnp.int32, (1, SIDE, HALF), 2) < HALF // 2

    def spread(r0, count):
        both = (qo[pl.ds(r0, count)] + qf[pl.ds(r0, count)].astype(F32)).reshape(count * SIDE, HALF)
        turned = pltpu.roll(both, HALF // 2, 1).reshape(count, SIDE, HALF)
        both = both.reshape(count, SIDE, HALF)
        return jnp.where(lane3, both, turned), jnp.where(lane3, turned, both)

    upper, lower = spread(LEAD, half)
    qd[pl.ds(LEAD, half)] = upper
    qd[pl.ds(LEAD + half, half)] = lower
    if not first_step:
        _, lower = spread(0, LEAD)
        qd[0:LEAD] = lower

    per_row = HALF // SIDE

    def put(b, dst):
        src = meta[b] - start + LEAD
        xc_o[pl.ds(dst, SIDE)] = xo[pl.ds(src, SIDE)]
        xc_f[pl.ds(dst, SIDE)] = xf[pl.ds(src, SIDE)]
        qc[pl.ds(dst, SIDE)] = qd[pl.ds(src, SIDE)]
        end = dst + heights[b]
        xc_o[pl.ds(end, SIDE)] = blank
        xc_f[pl.ds(end, SIDE)] = blank
        qc[pl.ds(end, SIDE)] = no_row
        put_codes(code_rows, codes, b, heights[b], dst)
        return end + 1

    used = lax.fori_loop(low, high, put, jnp.int32(1))
    blocks = jnp.where(high > low, (used + (block - 1)) // block, 0)

    column = lax.rem(lax.broadcasted_iota(jnp.int32, (TILE, 1), 0), SIDE)
    not_first = column != 0
    not_last = column != SIDE - 1

    def shifted(value):
        back = jnp.where(not_first, pltpu.roll(value, 1, 0), 0.0)
        ahead = jnp.where(not_last, pltpu.roll(value, TILE - 1, 0), 0.0)
        return back.astype(BF16), ahead.astype(BF16)

    edge = jnp.zeros((SIDE, 3 * 2 * HALF), BF16)
    act3[0:SIDE] = edge
    grad3[0:SIDE] = edge
    beyond = pl.multiple_of((blocks * block + 1) * SIDE, SIDE)
    grad3[pl.ds(beyond, SIDE)] = edge

    tiles = range(0, spots, TILE)

    def read_x(r0, t):
        part = pl.ds(r0 + t // SIDE, TILE // SIDE)
        o = xc_o[part].reshape(TILE, HALF)
        f = xc_f[part].reshape(TILE, HALF)
        return jnp.concatenate([o, f], axis=1).astype(F32)

    def at(row, count=block):
        return pl.ds(pl.multiple_of(row * SIDE, SIDE), count * SIDE)

    def tile_at(row, t):
        return pl.ds(pl.multiple_of(row * SIDE, SIDE) + t, TILE)

    def activate(j, carry):
        r0 = j * block
        for t in tiles:
            value, slope = gelu_parts(read_x(r0, t))
            slope_x[tile_at(r0, t), :] = slope
            back, ahead = shifted(value)
            act3[tile_at(r0 + 1, t), 0 : 2 * HALF] = back
            act3[tile_at(r0 + 1, t), 2 * HALF : 4 * HALF] = value.astype(BF16)
            act3[tile_at(r0 + 1, t), 4 * HALF : 6 * HALF] = ahead
        return carry

    fused = k < plan.usual
    lax.fori_loop(0, 2 if fused else blocks + 1, activate, 0)
    for copy in later:
        copy.wait()
    for copy in weight_copies:
        copy.wait()

    bias_first = bias[0:1, :]
    bias_mix = bias[1:2, :]
    bias_code = bias[8:9, 0:HALF]
    lane = lax.broadcasted_iota(jnp.int32, (1, HALF), 1) < HALF // 2
    hb = block // 2
    hs = hb * SIDE

    def add_rows(total, value):
        value = value.astype(F32)
        for i in range(0, value.shape[0], 8):
            part = value[i : i + 8]
            total = part if total is None else total + part
        return total

    half_tiles = range(0, hs, TILE)
    code_of = numbers(book_acc.shape[0], HALF)
    halves = (0, hs)

    def middle(j, carry):
        r0 = j * block
        for i in range(block // per_row):
            row = code_rows[pl.ds(j * (block // per_row) + i, 1), :]
            hot_s[:, i * HALF : (i + 1) * HALF] = one_hot_columns(row, code_of)
        for h in halves:
            found_s[h : h + hs] = dot(book[...], hot_s[:, h : h + hs]).astype(BF16).T
        pre = []
        for h in halves:
            window = jnp.concatenate([act3[at(r0 + i + h // SIDE, hb), :] for i in range(3)], axis=1)
            pre.append(dot(window, kernel[...]))
        for h, part in zip(halves, pre):
            for t in half_tiles:
                value, slope = gelu_parts(part[t : t + TILE] + bias_first)
                second_s[h + t : h + t + TILE] = value.astype(BF16)
                slope_s[h + t : h + t + TILE] = slope
        mixed = [dot(second_s[h : h + hs], mix[...]) for h in halves]
        for h, part in zip(halves, mixed):
            for t in half_tiles:
                low_s[h + t : h + t + TILE] = (read_x(r0, h + t) + part[t : t + TILE] + bias_mix).astype(BF16)
        latents = [dot(low_s[h : h + hs], project[i]) for i, h in enumerate(halves)]
        total = None
        for t in half_tiles:
            first = pl.ds(r0 + t // SIDE, TILE // SIDE)
            other = pl.ds(r0 + hb + t // SIDE, TILE // SIDE)
            ch = jnp.where(lane, found_s[t : t + TILE].astype(F32), found_s[hs + t : hs + t + TILE].astype(F32))
            q = jnp.where(lane3, qc[first], qc[other]).reshape(TILE, HALF)
            live = q < 0.5 * MARK
            latent = latents[0][t : t + TILE] + latents[1][t : t + TILE] + bias_code
            diff = jnp.where(live, latent - ch, 0.0)
            code_grad = jnp.where(live, q + (2.0 * COMMIT) * diff, 0.0).astype(BF16)
            code_s[t : t + TILE] = code_grad
            total = add_rows(total, code_grad)
            big = diff.astype(BF16).astype(F32)
            small = diff - big
            turned = pltpu.roll(small, HALF // 2, 1)
            diff_s[t : t + TILE] = jnp.where(lane, big, turned).astype(BF16)
            turned = pltpu.roll(big, HALF // 2, 1)
            diff_s[hs + t : hs + t + TILE] = jnp.where(lane, turned, small).astype(BF16)
        bias_acc[16:24, 0:HALF] += total
        total = None
        blocks_g = [dot(code_s[...], project[i], NT) for i in range(2)]
        for h, part in zip(halves, blocks_g):
            for t in half_tiles:
                block_g[tile_at(r0, h + t), :] = part[t : t + TILE]
                mixed_grad = part[t : t + TILE].astype(BF16)
                mixed_s[h + t : h + t + TILE] = mixed_grad
                total = add_rows(total, mixed_grad)
        bias_acc[8:16] += total
        second_grad = [dot(mixed_s[h : h + hs], mix[...], NT) for h in halves]
        total = None
        for h, part in zip(halves, second_grad):
            for t in half_tiles:
                first_grad = slope_s[h + t : h + t + TILE] * part[t : t + TILE]
                back, ahead = shifted(first_grad)
                first_low = first_grad.astype(BF16)
                grad3[tile_at(r0 + 1, h + t), 0 : 2 * HALF] = ahead
                grad3[tile_at(r0 + 1, h + t), 2 * HALF : 4 * HALF] = first_low
                grad3[tile_at(r0 + 1, h + t), 4 * HALF : 6 * HALF] = back
                total = add_rows(total, first_low)
        bias_acc[0:8] += total
        book_acc[...] += dot(hot_s[...], diff_s[...])
        mix_acc[...] += dot(second_s[...], mixed_s[...], TN)
        project_acc[...] += jnp.where(lane, dot(low_s[0:hs], code_s[...], TN), dot(low_s[hs:], code_s[...], TN))
        return carry

    def finish(j, carry):
        r0 = j * block
        active = act3[at(r0 + 1), 2 * HALF : 4 * HALF].T
        for i in range(3):
            kernel_acc[:, i * 6 * HALF : (i + 1) * 6 * HALF] += dot(active, grad3[at(r0 + 2 - i), :])
        grads = []
        for h in halves:
            window = jnp.concatenate([grad3[at(r0 + 2 - i + h // SIDE, hb), :] for i in range(3)], axis=1)
            grads.append(dot(window, kernel_t[...]))
        for h, grad in zip(halves, grads):
            for t in half_tiles:
                here = tile_at(r0, h + t)
                out = (block_g[here, :] + slope_x[here, :] * grad[t : t + TILE]).astype(BF16)
                part = pl.ds(r0 + (h + t) // SIDE, TILE // SIDE)
                xc_o[part] = out[:, :HALF].reshape(TILE // SIDE, SIDE, HALF)
                xc_f[part] = out[:, HALF:].reshape(TILE // SIDE, SIDE, HALF)
        return carry

    def opening(j, carry):
        middle(j, carry)
        return activate(j + 2, carry)

    def steady(j, carry):
        finish(j - 2, carry)
        middle(j, carry)
        return activate(j + 2, carry)

    if fused:
        lax.fori_loop(0, jnp.minimum(blocks, 2), opening, 0)
        lax.fori_loop(2, blocks, steady, 0)
        lax.fori_loop(jnp.maximum(blocks - 2, 0), blocks, finish, 0)
    else:
        lax.fori_loop(0, blocks, middle, 0)
        lax.fori_loop(0, blocks, finish, 0)
    leaving = []
    if not final:
        leaving += list(zip((kernel_acc, mix_acc, project_acc, book_acc, bias_acc), sums_out))
        for i, (source, target) in enumerate(leaving):
            leaving[i] = pltpu.make_async_copy(source, target, sems.at[i])
            leaving[i].start()

    out_o, out_f = xo, xf
    if first_step:
        out_o[0:LEAD] = blank
        out_f[0:LEAD] = blank
    else:
        out_o[0:LEAD] = carry_own[...]
        out_f[0:LEAD] = carry_far[...]

    def collect(b, src):
        dst = meta[b] - start + LEAD
        out_o[pl.ds(dst, SIDE)] = xc_o[pl.ds(src, SIDE)]
        out_f[pl.ds(dst, SIDE)] = xc_f[pl.ds(src, SIDE)]
        return src + heights[b] + 1

    lax.fori_loop(low, high, collect, jnp.int32(1))
    size = win_own.shape[0]
    windows = (
        (out_o.at[pl.ds(0, size)], win_own),
        (out_f.at[pl.ds(0, size)], win_far),
        (out_o.at[pl.ds(chunk, LEAD)], next_own),
        (out_f.at[pl.ds(chunk, LEAD)], next_far),
    )
    for i, (source, target) in enumerate(windows):
        leaving.append(pltpu.make_async_copy(source, target, sems.at[5 + i]))
        leaving[-1].start()
    if final:
        sums = (kernel_acc, mix_acc, project_acc, book_acc, bias_acc, decode_acc)
        laid_out += [slope_x.at[pl.ds(0, layout.rows), pl.ds(i * HALF, HALF)] for i in range(2)]
        leaving += gather_grads(plan, layout, place, meta, sums, *laid_out, sems)
    for copy in leaving:
        copy.wait()


class Layout:
    def __init__(self, devices, book_rows, embed):
        self.mix = 9 * 2 * HALF
        self.project = self.mix + 2 * HALF
        self.book = self.project + HALF // 2
        self.bias = self.book + book_rows // 2
        self.decode = self.bias + 8
        used = self.decode + embed + 8
        self.devices = devices
        self.piece = -(-used // (devices * SIDE)) * SIDE
        self.rows = self.piece * devices
        self.half = self.rows // 2
        self.used = used


def lay_out(layout, swap, kernel_acc, mix_acc, project_acc, book_acc, bias_acc, decode_acc, own, far):
    def lanes(value):
        return value[:, :HALF], value[:, HALF:]

    def order(first, second):
        return jnp.where(swap, second, first), jnp.where(swap, first, second)

    row = 0
    for tap in range(9):
        block = kernel_acc[:, tap * 2 * HALF : (tap + 1) * 2 * HALF]
        mine, theirs = lanes(block)
        a, b = order(mine[:HALF], mine[HALF:])
        own[row : row + HALF] = a
        own[row + HALF : row + 2 * HALF] = b
        a, b = order(theirs[:HALF], theirs[HALF:])
        far[row : row + HALF] = a
        far[row + HALF : row + 2 * HALF] = b
        row += 2 * HALF
    row = layout.mix
    for target, part in ((own, mix_acc[:HALF]), (far, mix_acc[HALF:])):
        a, b = order(*lanes(part))
        target[row : row + HALF] = a
        target[row + HALF : row + 2 * HALF] = b
    row = layout.project
    side = HALF // 2
    for target, part in ((own, project_acc[:HALF]), (far, project_acc[HALF:])):
        part = part + pltpu.roll(part, side, 1)
        target[row : row + side] = part.T[:side]
    row = layout.book
    book = book_acc[...]
    book = -2.0 * (book + pltpu.roll(book, side, 1))
    book = book.T[:side]
    for c in range(book.shape[1] // HALF):
        part = book[:, c * HALF : (c + 1) * HALF]
        own[row + c * side : row + (c + 1) * side] = part
        far[row + c * side : row + (c + 1) * side] = part
    row = layout.bias
    sums = [jnp.sum(bias_acc[8 * i : 8 * i + 8], axis=0, keepdims=True) for i in range(3)]
    code = sums[2][:, :HALF]
    code = code + pltpu.roll(code, side, 1)
    which = lax.broadcasted_iota(jnp.int32, (8, HALF), 0)
    for target, first in ((own, 0), (far, HALF)):
        part = jnp.where(which == 0, sums[0][:, first : first + HALF], sums[1][:, first : first + HALF])
        target[row : row + 8] = jnp.where(which == 2, code, jnp.where(which < 2, part, 0.0))
    row = layout.decode
    rest = layout.rows - row
    own[row:] = jnp.zeros((rest, HALF), F32)
    far[row:] = jnp.zeros((rest, HALF), F32)
    if decode_acc is not None:
        own[row : row + decode_acc.shape[0]] = decode_acc[...]


def gather_plain(layout, place, *refs):
    lay_out(layout, place[0] == 1, *refs[:5], None, *refs[5:])


def gather_grads(plan, layout, place, meta, accs, keep_own, keep_far, send, own, far, sems):
    lay_out(layout, place[0] == 1, *accs, own, far)
    base = plan.images + len(plan.chunks) + 1
    over = (meta[base + 4] > plan.covered).astype(F32)
    which = lax.broadcasted_iota(jnp.int32, (8, HALF), 0)
    row = layout.bias
    own[row : row + 8] = jnp.where(which == 3, over, own[row : row + 8])
    half = layout.half
    mine = pl.ds(pl.multiple_of(place[1] * half, SIDE), half)
    other = pl.ds(pl.multiple_of((1 - place[1]) * half, SIDE), half)
    kept = []
    for i, (source, target) in enumerate(((own, keep_own), (far, keep_far))):
        kept.append(pltpu.make_async_copy(source.at[mine, :], target, sems.at[9 + i]))
        kept[-1].start()
    send[0] = own[other, :].astype(BF16)
    send[1] = far[other, :].astype(BF16)
    return kept


def hold(*refs):
    pass


def add_core(keep_own, keep_far, came, out, token):
    token[...] = jnp.zeros_like(token)
    chips, piece = out.shape[0], out.shape[1] // 2
    for c in range(chips):
        rows = pl.ds(c * piece, piece)
        out[c, 0:piece] = (keep_own[rows] + came[0, rows].astype(F32)).astype(BF16)
        out[c, piece:] = (keep_far[rows] + came[1, rows].astype(F32)).astype(BF16)


def add_pieces(pieces, _, own, far):
    total = pieces[0].astype(F32)
    for i in range(1, pieces.shape[0]):
        total = total + pieces[i].astype(F32)
    half = own.shape[0]
    own[...] = total[:half]
    far[...] = total[half:].astype(BF16)


def add_last(own, came, out):
    total = (own[...] + came[...].astype(F32)).astype(BF16)
    out[...] = jnp.broadcast_to(total[None], out.shape)


def write_grads(layout, place, mine, theirs, kernel, first_bias, mix, mix_bias, project, project_bias, book, decode, decode_bias, whole):
    half = layout.half
    whole[pl.ds(pl.multiple_of(place[1] * half, SIDE), half), :] = mine[...].astype(F32)
    whole[pl.ds(pl.multiple_of((1 - place[1]) * half, SIDE), half), :] = theirs[...].astype(F32)
    split_grads(layout, whole, kernel, first_bias, mix, mix_bias, project, project_bias, book, decode, decode_bias)


def split_grads(layout, whole, kernel, first_bias, mix, mix_bias, project, project_bias, book, decode, decode_bias):
    for tap in range(9):
        kernel[tap] = whole[tap * 2 * HALF : (tap + 1) * 2 * HALF]
    row = layout.mix
    mix[:, :HALF] = whole[row : row + HALF]
    mix[:, HALF:] = whole[row + HALF : row + 2 * HALF]
    side = HALF // 2
    for row, target in ((layout.project, project), (layout.book, book)):
        for c in range(target.shape[1] // HALF):
            target[:, c * HALF : (c + 1) * HALF] = whole[row + c * side : row + (c + 1) * side]
    row = layout.bias
    first_bias[...] = whole[row : row + 1]
    mix_bias[...] = whole[row + 1 : row + 2]
    project_bias[...] = whole[row + 2 : row + 3, :side]
    row = layout.decode
    n = decode.shape[0]
    decode[...] = whole[row : row + n]
    decode_bias[...] = whole[row + n : row + n + 1]


def split_again(layout, total, extra, *refs):
    whole = refs[-1]
    whole[...] = total[...].astype(F32) + extra[...]
    split_grads(layout, whole, *refs[:-1])


def restore_rows(plan, n, waits, *refs):
    meta, heights, *refs = refs[waits:]
    own, far, out, token = refs[:n], refs[n : 2 * n], refs[2 * n], refs[2 * n + 1]
    token[...] = jnp.zeros_like(token)
    stage_own, stage_far, sems = refs[2 * n + 2 :]
    copies = []
    for k in range(n):
        size = plan.chunks[k] + (LEAD if k == n - 1 else 0)
        for i, (source, target) in enumerate(((own[k], stage_own), (far[k], stage_far))):
            from_rows = source.at[pl.ds(0, size)]
            copies.append(pltpu.make_async_copy(from_rows, target.at[pl.ds(plan.starts[k], size)], sems.at[i, k]))
            copies[-1].start()
    for copy in copies:
        copy.wait()
    base = plan.images + len(plan.chunks) + 1
    own_row, send_row = meta[base], meta[base + 1]
    first, last = meta[base + 2], meta[base + 3]
    row_of = lax.broadcasted_iota(jnp.int32, (SIDE, 1, 1), 0)

    def own_image(b, carry):
        rows = stage_own[pl.ds(meta[b] + LEAD, SIDE)]
        out[b] = jnp.where(row_of < heights[b], rows, jnp.zeros_like(rows))
        return carry

    def far_image(b, carry):
        rows = stage_far[pl.ds(meta[b] + own_row - send_row + LEAD, SIDE)]
        out[b] = jnp.where(row_of < heights[b], rows, jnp.zeros_like(rows))
        return carry

    lax.fori_loop(first, last, own_image, 0)
    lax.fori_loop(0, first, far_image, 0)
    lax.fori_loop(last, plan.images, far_image, 0)


def trade(value):
    return lax.ppermute(value, "mp", [(0, 1), (1, 0)])


def held(value, *others):
    return pl.pallas_call(
        hold,
        out_shape=shape(value.shape, value.dtype),
        in_specs=[ANY] * (1 + len(others)),
        out_specs=ANY,
        input_output_aliases={0: 0},
        compiler_params=params(60),
        name="hold",
    )(value, *others)


def run_main(plan, layout, k, meta, heights, streams, weights, state, waits=(), ending=()):
    chunk, rows, block = plan.chunks[k], plan.rows[k], plan.block[k]
    last = k >= plan.usual - 1
    final = k == plan.usual - 1
    x_own, x_far, q_own, q_far, codes = streams
    book_rows = weights[-1].shape[1]
    args = [*waits, *ending, meta, heights, x_own, x_far[k], q_own, q_far[k], codes, *weights]
    specs = [ANY] * len(waits) + ([SMEM, VMEM] if final else [])
    specs += [SMEM, SMEM, ANY, ANY, ANY, ANY, VMEM, ANY, ANY] + [VMEM] * (len(weights) - 2)
    alias = {}
    if state is not None:
        args += [x_far[k - 1], q_far[k - 1], *state]
        specs += [ANY, ANY, VMEM, VMEM] + [ANY] * (len(state) - 2)
        if not final:
            for i in range(len(state) - 2):
                alias[len(args) - 5 + i] = 4 + i
    size = chunk + LEAD if last else chunk
    tile = (SIDE, HALF)
    outs = [shape((size,) + tile, BF16)] * 2 + [shape((LEAD,) + tile, BF16)] * 2
    sums = [(2 * HALF, 18 * HALF), (2 * HALF, 2 * HALF), (2 * HALF, HALF), (book_rows, HALF), (24, 2 * HALF)]
    scratch = [pltpu.VMEM(dims, F32) for dims in sums]
    out_specs = [ANY] * 4
    if final:
        outs += [shape((layout.half, HALF), F32)] * 2 + [shape((2, layout.half, HALF), BF16)]
        out_specs += [ANY, ANY, VMEM]
    else:
        outs += [shape(dims, F32) for dims in sums]
        out_specs += [ANY] * 5
    scratch += [pltpu.VMEM((18 * HALF, 2 * HALF), BF16)] * 2 + [pltpu.SemaphoreType.DMA((2,))]
    half = chunk // 2
    spots = block * SIDE
    scratch += [
        pltpu.VMEM((LEAD + chunk + 2 * SIDE,) + tile, BF16),
        pltpu.VMEM((LEAD + chunk + 2 * SIDE,) + tile, BF16),
        pltpu.VMEM((LEAD + half,) + tile, F32),
        pltpu.VMEM((LEAD + half,) + tile, BF16),
        pltpu.VMEM((LEAD + chunk + SIDE,) + tile, F32),
        pltpu.VMEM((rows + 2 * block + SIDE,) + tile, BF16),
        pltpu.VMEM((rows + 2 * block + SIDE,) + tile, BF16),
        pltpu.VMEM((rows + 2 * SIDE,) + tile, F32),
        pltpu.VMEM((-(-(rows * SIDE // HALF + 4) // 8) * 8, HALF), jnp.int32),
        pltpu.VMEM(((rows + 2 * block + 2) * SIDE, 6 * HALF), BF16),
        pltpu.VMEM(((rows + 2 * block) * SIDE, 2 * HALF), F32),
        pltpu.VMEM(((rows + 2) * SIDE, 6 * HALF), BF16),
        pltpu.VMEM((rows * SIDE, 2 * HALF), F32),
        pltpu.VMEM((spots, 2 * HALF), BF16),
        pltpu.VMEM((spots, 2 * HALF), F32),
        pltpu.VMEM((spots, 2 * HALF), BF16),
        pltpu.VMEM((spots, 2 * HALF), BF16),
        pltpu.VMEM((spots // 2, HALF), BF16),
        pltpu.VMEM((book_rows, spots), BF16),
        pltpu.VMEM((spots, HALF), BF16),
        pltpu.VMEM((spots, HALF), BF16),
        pltpu.SemaphoreType.DMA((13,)),
    ]
    spots = chunk * SIDE
    return pl.pallas_call(
        functools.partial(main_step, plan, layout, k, len(waits)),
        out_shape=outs,
        in_specs=specs,
        out_specs=out_specs,
        scratch_shapes=scratch,
        input_output_aliases=alias,
        compiler_params=params(58),
        cost_estimate=cost(60 * 65536 * spots, 8 * MIB, 2 * 256 * spots),
        name=f"main_{k}",
    )(*args)


def local(
    image_latents,
    image_heights,
    code_index,
    kernel_three,
    bias_three,
    weight_mix,
    bias_mix,
    weight_project,
    bias_project,
    codebook,
    weight_decode,
    bias_decode,
    out_grad,
):
    images = image_latents.shape[0]
    plan = Plan(images)
    n = len(plan.chunks)
    tile = (SIDE, HALF)
    where = lax.axis_index("mp").astype(jnp.int32)
    core = lax.rem(lax.axis_index("dp").astype(jnp.int32), 2)
    spot = place = jnp.stack([where, core])

    packed = pl.pallas_call(
        functools.partial(pack_latents, plan),
        out_shape=[
            shape((meta_size(plan),), jnp.int32),
            shape((LEAD + plan.total,) + tile, BF16),
        ]
        + [shape((c,) + tile, BF16) for c in plan.chunks],
        in_specs=[SMEM, SMEM, HBM],
        out_specs=[SMEM, ANY] + [ANY] * n,
        scratch_shapes=[
            pltpu.VMEM((images, SIDE) + tile, BF16),
            pltpu.VMEM((plan.packed + SIDE,) + tile, BF16),
            pltpu.SemaphoreType.DMA((8,)),
            pltpu.SemaphoreType.DMA((n + 1,)),
        ],
        compiler_params=params(60),
        cost_estimate=cost(0, 12 * MIB),
        name="pack_latents",
    )(image_heights, place, image_latents)
    meta, x_own, x_send = packed[0], packed[1], packed[2:]

    far_kernel = trade(kernel_three)
    packed = pl.pallas_call(
        functools.partial(pack_code_grads, plan),
        out_shape=[shape((plan.total // 2,) + tile, F32), shape((2 * HALF + HALF // 2 + SIDE, HALF), BF16)]
        + [shape((c // 2,) + tile, BF16) for c in plan.chunks],
        in_specs=[SMEM] + [HBM] * 6 + [SMEM],
        out_specs=[VMEM] * (n + 2),
        scratch_shapes=[
            pltpu.VMEM((images, SIDE) + tile, BF16),
            pltpu.VMEM((plan.packed + SIDE,) + tile, BF16),
            pltpu.SemaphoreType.DMA((8,)),
            pltpu.SemaphoreType.DMA((5,)),
            pltpu.VMEM(weight_decode.shape, BF16),
            pltpu.VMEM(weight_mix.shape, BF16),
            pltpu.VMEM(weight_project.shape[::-1], BF16),
            pltpu.VMEM((1, HALF), BF16),
            pltpu.VMEM((1, HALF), BF16),
        ],
        compiler_params=params(60),
        cost_estimate=cost(2 * 2 * plan.total * SIDE * 256 * 128, 10 * MIB),
        name="pack_code_grads",
    )(meta, out_grad, weight_decode, weight_mix, weight_project.T, bias_three.reshape(1, HALF), bias_mix.reshape(1, HALF), meta)
    q_own, small, q_send = packed[0], packed[1], packed[2:]

    book_rows, embed = codebook.shape
    codebook_t = codebook.T
    far_small = trade(small)
    usual = plan.usual
    x_far, q_far = [], []
    x_far.append(trade(x_send[0]))
    q_far.append(trade(q_send[0]))

    weights = pl.pallas_call(
        prepare_weights,
        out_shape=[
            shape((18 * HALF, 2 * HALF), BF16),
            shape((18 * HALF, 2 * HALF), BF16),
            shape((2 * HALF, 2 * HALF), BF16),
            shape((2, 2 * HALF, HALF), BF16),
            shape((SIDE, 2 * HALF), F32),
            shape((HALF, book_rows), BF16),
        ],
        in_specs=[SMEM, HBM, HBM] + [VMEM] * 4,
        out_specs=[VMEM] * 6,
        scratch_shapes=[pltpu.VMEM(kernel_three.shape, BF16)] * 2 + [pltpu.SemaphoreType.DMA((2,))],
        compiler_params=params(20),
        cost_estimate=cost(0, 5 * MIB),
        name="prepare_weights",
    )(place, kernel_three, far_kernel, small, far_small, bias_project.reshape(1, -1), codebook_t)

    groups = 8
    group = images // groups
    codes = code_index.reshape(images, SIDE * SIDE)
    whole = lambda dims: pl.BlockSpec(dims, lambda g: (0,) * len(dims))
    four = pl.BlockSpec((group, SIDE) + tile, lambda g: (g, 0, 0, 0))
    row = pl.BlockSpec((group, SIDE * SIDE), lambda g: (g, 0))
    def code_sums(first, steps):
        return pl.pallas_call(
            functools.partial(sum_codes, first, group),
            grid=(steps,),
            out_shape=shape((embed + 8, HALF), F32),
            in_specs=[
                SMEM,
                pl.BlockSpec((group, SIDE * SIDE), lambda g: (g + first, 0)),
                pl.BlockSpec((group, SIDE) + tile, lambda g: (g + first, 0, 0, 0)),
                whole((embed, book_rows)),
                ANY,
                ANY,
            ],
            out_specs=whole((embed + 8, HALF)),
            scratch_shapes=[
                pltpu.VMEM((book_rows, group * SIDE * SIDE), BF16),
                pltpu.VMEM((group * SIDE * SIDE, HALF), BF16),
                pltpu.VMEM((book_rows, HALF), F32),
            ],
            compiler_params=params(60),
            cost_estimate=cost(steps * group * 256 * 512 * 256, steps * group * 65536),
            name=f"sum_codes_{first}",
        )(image_heights, codes, out_grad, codebook_t, small, far_kernel)

    def decode(after):
        return pl.pallas_call(
            functools.partial(decode_images, plan, groups),
            grid=(groups,),
            out_shape=[shape((images, SIDE) + tile, BF16), shape((8, HALF), F32)],
            in_specs=[SMEM, row, whole((embed, book_rows)), whole((embed, HALF)), whole((1, HALF)), ANY],
            out_specs=[four, whole((8, HALF))],
            scratch_shapes=[pltpu.VMEM((HALF, book_rows), BF16)],
            compiler_params=params(32),
            cost_estimate=cost(images * 256 * 512 * 256, 5 * MIB),
            name="decode_images",
        )(image_heights, codes, codebook_t, weight_decode, bias_decode.reshape(1, HALF), after)

    decode_acc = code_sums(0, groups)
    for k in range(1, usual):
        x_far.append(trade(held(x_send[k], decode_acc, far_small, x_far[0], q_far[0])))
        q_far.append(trade(held(q_send[k], decode_acc, far_small, x_far[0], q_far[0])))

    devices = lax.axis_size("dp")
    layout = Layout(devices, book_rows, embed)
    half, piece, chips = layout.half, layout.piece, devices // 2
    streams = (x_own, x_far, q_own, q_far, codes)
    state = None
    win_own, win_far = [], []
    for k in range(usual):
        waits = win_far[k - 2 : k - 1] if k > 1 else []
        ending = (spot, decode_acc) if k == usual - 1 else ()
        outs = run_main(plan, layout, k, meta, image_heights, streams, weights, state, waits, ending)
        win_own.append(outs[0])
        if k < usual - 1:
            win_far.append(trade(outs[1]))
        state = outs[2:]
    last_window = outs[1]
    carry, (keep_own, keep_far, send) = state[:2], state[2:]

    def restore(own, far, waits=()):
        count = len(own)
        return pl.pallas_call(
            functools.partial(restore_rows, plan, count, len(waits)),
            out_shape=[shape((images, SIDE) + tile, BF16), shape((8, HALF), F32)],
            in_specs=[ANY] * len(waits) + [SMEM, SMEM] + [ANY] * (2 * count),
            out_specs=[VMEM, VMEM],
            scratch_shapes=[
                pltpu.VMEM((plan.total + LEAD + SIDE,) + tile, BF16),
                pltpu.VMEM((plan.total + LEAD + SIDE,) + tile, BF16),
                pltpu.SemaphoreType.DMA((2, count)),
            ],
            compiler_params=params(60),
            cost_estimate=cost(0, 10 * MIB),
            name="restore_rows",
        )(*waits, meta, image_heights, *own, *far)

    across = [(i, i ^ 1) for i in range(devices)]

    def step(body, out, name, *args, waits=()):
        specs = [VMEM] * len(args) + [ANY] * len(waits)
        args = (*args, *waits)
        return pl.pallas_call(
            body,
            out_shape=out,
            in_specs=specs,
            out_specs=[VMEM] * len(out) if isinstance(out, list) else VMEM,
            compiler_params=params(24),
            cost_estimate=cost(0, 2 * MIB),
            name=name,
        )(*args)

    send = held(send, win_far[usual - 2])
    came = lax.ppermute(send, "dp", across)
    win_far.append(trade(last_window))
    parts = [shape((chips, 2 * piece, HALF), BF16), shape((8, HALF), F32)]
    mine, token = step(add_core, parts, "add_core", keep_own, keep_far, came)
    decoded, token = decode(token)
    cores = [[i for i in range(devices) if i % 2 == c] for c in range(2)]
    mine = lax.all_to_all(mine, "dp", 0, 0, axis_index_groups=cores, tiled=True)
    parts = [shape((piece, HALF), F32), shape((piece, HALF), BF16)]
    own_piece, far_piece = step(add_pieces, parts, "add_pieces", mine, waits=[token])
    came = trade(far_piece)
    mine = step(add_last, shape((chips, piece, HALF), BF16), "add_last", own_piece, came)
    latents_grad, token = restore(win_own, win_far, [own_piece])
    mine = lax.all_to_all(mine, "dp", 0, 0, axis_index_groups=cores, tiled=True)
    mine = held(mine, token).reshape(half, HALF)
    theirs = lax.ppermute(mine, "dp", across)

    grads_out = [
        shape((9, 2 * HALF, HALF), F32),
        shape((1, HALF), F32),
        shape((HALF, 2 * HALF), F32),
        shape((1, HALF), F32),
        shape((embed, HALF), F32),
        shape((1, embed), F32),
        shape((embed, book_rows), F32),
        shape((embed, HALF), F32),
        shape((1, HALF), F32),
    ]
    whole = pltpu.VMEM((layout.rows, HALF), F32)

    def usual_end(latents_grad):
        grads = pl.pallas_call(
            functools.partial(write_grads, layout),
            out_shape=grads_out,
            in_specs=[SMEM, VMEM, VMEM],
            out_specs=[VMEM] * 9,
            scratch_shapes=[whole],
            compiler_params=params(24),
            cost_estimate=cost(0, 4 * MIB),
            name="write_grads",
        )(spot, mine, theirs)
        return (latents_grad, *grads)

    def longer_end(latents_grad):
        last_x, last_q = trade(x_send[usual]), trade(q_send[usual])
        streams = (x_own, x_far + [last_x], q_own, q_far + [last_q], codes)
        outs = run_main(plan, layout, usual, meta, image_heights, streams, weights, carry)
        latents_grad, _ = restore(win_own + [outs[0]], win_far + [trade(outs[1])])
        own, far = pl.pallas_call(
            functools.partial(gather_plain, layout),
            out_shape=[shape((layout.rows, HALF), F32)] * 2,
            in_specs=[SMEM] + [VMEM] * 5,
            out_specs=[VMEM] * 2,
            compiler_params=params(40),
            name="gather_plain",
        )(spot, *outs[4:])
        extra = lax.psum(own + trade(far), "dp")
        first, second = jnp.where(core == 0, mine, theirs), jnp.where(core == 0, theirs, mine)
        grads = pl.pallas_call(
            functools.partial(split_again, layout),
            out_shape=grads_out,
            in_specs=[VMEM, VMEM],
            out_specs=[VMEM] * 9,
            scratch_shapes=[whole],
            compiler_params=params(24),
            name="split_again",
        )(jnp.concatenate([first, second]), extra)
        return (latents_grad, *grads)

    flag = layout.bias + 3
    holder = flag // half
    flags = jnp.where(core == holder, mine[flag - holder * half, 0], theirs[flag - holder * half, 0])
    ends = lax.cond(flags.astype(F32) > 0.5, longer_end, usual_end, latents_grad)
    latents_grad, kernel_grad, first_bias, mix_grad, mix_bias, project_grad, project_bias, book, decode, decode_bias = ends
    return (
        decoded,
        latents_grad,
        kernel_grad,
        first_bias.reshape(HALF),
        mix_grad,
        mix_bias.reshape(HALF),
        project_grad.T,
        project_bias.reshape(embed),
        book.T,
        decode,
        decode_bias.reshape(HALF),
    )


def solution(mesh):
    tile = P("dp", None, None, "mp")
    placed = (
        tile,
        P("dp"),
        P("dp", None, None),
        P(None, None, "mp"),
        P("mp"),
        P("mp", None),
        P("mp"),
        P("mp", None),
        P(),
        P(),
        P(None, "mp"),
        P("mp"),
        tile,
    )
    outs = (
        tile,
        tile,
        P(None, None, "mp"),
        P("mp"),
        P("mp", None),
        P("mp"),
        P("mp", None),
        P(),
        P(),
        P(None, "mp"),
        P("mp"),
    )
    return jax.shard_map(local, mesh=mesh, in_specs=placed, out_specs=outs, check_vma=False)
```

```python
import functools

import jax
import jax.numpy as jnp
from jax import lax
from jax.experimental import pallas as pl
from jax.experimental.pallas import tpu as pltpu
from jax.sharding import PartitionSpec as P

SIDE = 16
HALF = 128
LEAD = 16
BLOCK = 32
TILE = 32
MARK = 1e9
GELU_SCALE = 0.7978845608028654
GELU_CUBE = 0.044715
COMMIT = 0.25
F32 = jnp.float32
BF16 = jnp.bfloat16
ANY = pl.BlockSpec(memory_space=pl.ANY)
SMEM = pl.BlockSpec(memory_space=pltpu.SMEM)
HBM = pl.BlockSpec(memory_space=pltpu.HBM)
VMEM = pl.BlockSpec(memory_space=pltpu.VMEM)
MIB = 1 << 20

NT = (((1,), (1,)), ((), ()))
TN = (((0,), (0,)), ((), ()))
NN = (((1,), (0,)), ((), ()))


def dot(a, b, dims=NN):
    return lax.dot_general(a, b, dims, preferred_element_type=F32)


def one_hot_columns(codes, code_of):
    return jnp.where(code_of == codes.astype(jnp.int16), jnp.bfloat16(1), jnp.bfloat16(0))


def numbers(count, width):
    return lax.broadcasted_iota(jnp.int32, (count, width), 0).astype(jnp.int16)


def shape(dims, kind):
    return jax.ShapeDtypeStruct(dims, kind)


def params(mib):
    return pltpu.CompilerParams(vmem_limit_bytes=mib * MIB)


def cost(flops, moved, slow=0):
    return pl.CostEstimate(flops=flops, bytes_accessed=moved, transcendentals=slow)


class Plan:
    def __init__(self, images):
        self.images = images
        longest = images * SIDE // 2 + SIDE // 2
        part = images // 8
        self.chunks = [19 * part, 28 * part]
        self.usual = len(self.chunks)
        rest = longest - sum(self.chunks)
        self.chunks.append(rest)
        self.starts = [sum(self.chunks[:k]) for k in range(len(self.chunks))]
        self.total = sum(self.chunks)
        self.packed = -(-(LEAD + longest + self.total + LEAD) // SIDE) * SIDE
        self.rows, self.block = [], []
        for k, c in enumerate(self.chunks):
            block = BLOCK if k < self.usual else SIDE
            most = 1 + c + 15 + c // 4 + 1
            self.rows.append(-(-most // block) * block)
            self.block.append(block)
        self.covered = sum(self.chunks[: self.usual])


def meta_size(plan):
    return plan.images + len(plan.chunks) + 1 + 5


def plan_rows(plan, heights, place, meta):
    images = plan.images
    base = images + len(plan.chunks) + 1

    def total_of(b, acc):
        return acc + heights[b]

    total = lax.fori_loop(0, images, total_of, jnp.int32(0))

    def split_of(b, state):
        acc, best, split, cut = state
        acc = acc + heights[b]
        worst = jnp.maximum(acc, total - acc)
        better = worst < best
        return (acc, jnp.where(better, worst, best), jnp.where(better, b + 1, split), jnp.where(better, acc, cut))

    _, _, split, cut = lax.fori_loop(0, images, split_of, (jnp.int32(0), jnp.int32(1 << 20), jnp.int32(0), jnp.int32(0)))
    mine = place[0]
    own_first = jnp.where(mine == 0, 0, split)
    own_last = jnp.where(mine == 0, split, images)
    own_row = jnp.where(mine == 0, 0, cut)
    send_row = jnp.where(mine == 0, cut, 0)
    for k in range(len(plan.chunks) + 1):
        meta[images + k] = own_first
    ends = [plan.starts[k] + plan.chunks[k] for k in range(len(plan.chunks))]

    def place_of(b, acc):
        meta[b] = acc - own_row
        acc = acc + heights[b]
        end = acc - own_row
        inside = jnp.logical_and(b >= own_first, b < own_last)
        step = jnp.int32(0)
        for k in range(len(plan.chunks) - 1):
            step = step + (end > ends[k]).astype(jnp.int32)

        @pl.when(inside)
        def _():
            meta[images + 1 + step] = b + 1

        return acc

    lax.fori_loop(0, images, place_of, jnp.int32(0))
    for k in range(len(plan.chunks)):
        meta[images + k + 1] = jnp.maximum(meta[images + k + 1], meta[images + k])
    meta[base] = own_row
    meta[base + 1] = send_row
    meta[base + 2] = own_first
    meta[base + 3] = own_last
    meta[base + 4] = jnp.maximum(cut, total - cut)


def pack_rows(plan, meta, source, packed, piece, count):
    base = plan.images + len(plan.chunks) + 1

    def one(i, carry):
        b = piece * count + i
        row = meta[b] + meta[base] + LEAD
        packed[pl.ds(row, SIDE)] = source[b]
        return carry

    lax.fori_loop(0, count, one, 0)


def pack_latents(plan, heights, place, x_hbm, _, meta, own, *rest):
    n = len(plan.chunks)
    sends, (x_in, packed, sem_in, sem_out) = rest[:n], rest[n:]
    pieces = 8
    count = plan.images // pieces
    fetch = []
    for p in range(pieces):
        part = pl.ds(p * count, count)
        fetch.append(pltpu.make_async_copy(x_hbm.at[part], x_in.at[part], sem_in.at[p]))
        fetch[-1].start()
    plan_rows(plan, heights, place, meta)
    base = plan.images + n + 1
    for p in range(pieces):
        fetch[p].wait()
        pack_rows(plan, meta, x_in, packed, p, count)
    copies = []
    for k in range(n):
        part = pl.ds(LEAD + meta[base + 1] + plan.starts[k], plan.chunks[k])
        copies.append(pltpu.make_async_copy(packed.at[part], sends[k], sem_out.at[k]))
        copies[-1].start()
    copies.append(pltpu.make_async_copy(packed.at[pl.ds(meta[base], LEAD + plan.total)], own, sem_out.at[n]))
    copies[-1].start()
    for copy in copies:
        copy.wait()


def pack_code_grads(plan, meta, og_hbm, *rest):
    n = len(plan.chunks)
    sources, (own, small), rest = rest[:5], rest[6:8], rest[8:]
    sends, rest = rest[:n], rest[n:]
    og_in, packed, sem_in, sem_small = rest[:4]
    held = rest[4:]
    small_fetch = []
    for i in range(5):
        small_fetch.append(pltpu.make_async_copy(sources[i], held[i], sem_small.at[i]))
        small_fetch[-1].start()
    decode_w, weight_mix, project_t, bias_first, bias_mix = held
    pieces = 8
    count = plan.images // pieces
    fetch = []
    for p in range(pieces):
        part = pl.ds(p * count, count)
        fetch.append(pltpu.make_async_copy(og_hbm.at[part], og_in.at[part], sem_in.at[p]))
        fetch[-1].start()
    base = plan.images + n + 1

    def clear(i, carry):
        packed[pl.ds(i * SIDE, SIDE)] = jnp.zeros((SIDE, SIDE, HALF), BF16)
        return carry

    lax.fori_loop(0, packed.shape[0] // SIDE, clear, 0)
    for copy in small_fetch:
        copy.wait()
    side = HALF // 2
    small[0:HALF] = weight_mix[:, :HALF]
    small[HALF : 2 * HALF] = weight_mix[:, HALF:]
    small[2 * HALF : 2 * HALF + side] = project_t[...]
    which = lax.broadcasted_iota(jnp.int32, (SIDE, HALF), 0)
    first, second = bias_first[...].astype(F32), bias_mix[...].astype(F32)
    first = jnp.where(which == 0, first, jnp.where(which == 1, second, 0.0))
    small[2 * HALF + side : 2 * HALF + side + SIDE] = first.astype(BF16)
    w = decode_w[...]
    blank = jnp.zeros_like(w)
    upper = jnp.concatenate([w, blank], axis=0)
    lower = jnp.concatenate([blank, w], axis=0)
    for p in range(pieces):
        fetch[p].wait()
        pack_rows(plan, meta, og_in, packed, p, count)
    for k in range(n):
        half = plan.chunks[k] // 2
        for which in range(2):
            row = LEAD + meta[base + 1 - which] + plan.starts[k]
            a = packed[pl.ds(row, half)].reshape(half * SIDE, HALF)
            b = packed[pl.ds(row + half, half)].reshape(half * SIDE, HALF)
            both = dot(a, upper, NT) + dot(b, lower, NT)
            both = both.reshape(half, SIDE, HALF)
            if which == 0:
                sends[k][...] = both.astype(BF16)
            else:
                own[pl.ds(plan.starts[k] // 2, half)] = both


def prepare_weights(place, own_hbm, far_hbm, far_other_hbm, small, far_small, bias_code, codebook_t, *refs):
    forward, backward, mix, project, bias, book, kernel, far_kernel, sems = refs
    copies = []
    halves = [pl.ds(pl.multiple_of(at * HALF, HALF), HALF) for at in (place[1], 1 - place[1])]
    pairs = [(own_hbm, kernel)]
    pairs += [(source, far_kernel.at[:, rows, :]) for source, rows in zip((far_hbm, far_other_hbm), halves)]
    for i, (source, target) in enumerate(pairs):
        copies.append(pltpu.make_async_copy(source, target, sems.at[i]))
        copies[-1].start()
    for copy in copies:
        copy.wait()
    first = pl.multiple_of(place[0] * HALF, HALF)
    order = (first, HALF - first)
    for tap in range(9):
        for d, source in enumerate((kernel, far_kernel)):
            for c in range(2):
                tile = source[tap, pl.ds(order[c], HALF), :]
                row = tap * 2 * HALF
                forward[row + c * HALF : row + (c + 1) * HALF, d * HALF : (d + 1) * HALF] = tile
                backward[row + d * HALF : row + (d + 1) * HALF, c * HALF : (c + 1) * HALF] = tile.T
    blank = jnp.zeros((HALF, HALF // 2), BF16)
    for d, source in enumerate((small, far_small)):
        rows = pl.ds(d * HALF, HALF)
        for c in range(2):
            mix[rows, c * HALF : (c + 1) * HALF] = source[pl.ds(order[c], HALF), :]
        part = source[2 * HALF : 2 * HALF + HALF // 2, :].T
        project[0, rows, :] = jnp.concatenate([part, blank], axis=1)
        project[1, rows, :] = jnp.concatenate([blank, part], axis=1)
        bias[0:8, d * HALF : (d + 1) * HALF] = source[2 * HALF + HALF // 2 : 2 * HALF + HALF // 2 + SIDE, :].astype(F32)[0:8]
    code = bias_code[...].astype(F32)
    code = jnp.concatenate([code, code], axis=1)
    bias[8:16, :] = jnp.broadcast_to(jnp.concatenate([code, code], axis=1), (8, 2 * HALF))
    book[...] = jnp.concatenate([codebook_t[...], codebook_t[...]], axis=0)


def sum_codes(first, group, heights, codes, og, codebook_t, _, __, grads, hot, cots, sums):
    step = pl.program_id(0)

    @pl.when(step == 0)
    def _():
        sums[...] = jnp.zeros_like(sums)

    spots = SIDE * SIDE
    code_of = numbers(codebook_t.shape[1], spots)
    spot = lax.broadcasted_iota(jnp.int32, (spots, 1), 0)
    for i in range(group):
        live = heights[(first + step) * group + i] * SIDE
        hot[:, i * spots : (i + 1) * spots] = one_hot_columns(codes[i : i + 1, :], code_of)
        cot = og[i].reshape(spots, HALF).astype(F32)
        cots[i * spots : (i + 1) * spots] = jnp.where(spot < live, cot, 0.0).astype(BF16)
    half = sums.shape[0] // 2
    for h in (0, half):
        sums[h : h + half] += dot(hot[h : h + half], cots[...])

    @pl.when(step == pl.num_programs(0) - 1)
    def _():
        total = sums[...]
        book = codebook_t[...].astype(F32)
        w = lax.dot_general(book, total, NN, precision=lax.Precision.HIGHEST, preferred_element_type=F32)
        bias = jnp.sum(total, axis=0, keepdims=True)
        embed = w.shape[0]
        grads[0:embed] = w
        grads[embed : embed + 8] = jnp.broadcast_to(bias, (8, HALF))


def decode_images(plan, steps, heights, codes, codebook_t, decode_w, decode_b, _, decoded, token, table):
    step = pl.program_id(0)
    token[...] = jnp.zeros_like(token)
    group = plan.images // steps

    @pl.when(step == 0)
    def _():
        full = dot(codebook_t[...], decode_w[...], TN) + decode_b[...].astype(F32)
        table[...] = full.T.astype(BF16)

    spots = SIDE * SIDE
    code_of = numbers(codebook_t.shape[1], spots)
    spot = lax.broadcasted_iota(jnp.int32, (spots, 1), 0)
    for i in range(group):
        live = heights[step * group + i] * SIDE
        out = dot(table[...], one_hot_columns(codes[i : i + 1, :], code_of)).T
        decoded[i] = jnp.where(spot < live, out, 0.0).astype(BF16).reshape(SIDE, SIDE, HALF)


def put_codes(code_rows, codes, b, height, dst):
    spot = lax.broadcasted_iota(jnp.int32, (1, SIDE * SIDE), 1)
    lane = lax.broadcasted_iota(jnp.int32, (1, HALF), 1)
    per_row = HALF // SIDE
    row = jnp.where(spot < height * SIDE, codes[pl.ds(b, 1), :], -1)
    turn = lax.rem(dst, per_row) * SIDE
    upper = pltpu.roll(row[:, :HALF], turn, 1)
    lower = pltpu.roll(row[:, HALF:], turn, 1)
    inside = lane >= turn
    pieces = (jnp.where(inside, upper, -1), jnp.where(inside, lower, upper), jnp.where(inside, -1, lower))
    for i, piece in enumerate(pieces):
        target = pl.ds(dst // per_row + i, 1)
        code_rows[target, :] = jnp.where(piece < 0, code_rows[target, :], piece)


def gelu_parts(v):
    square = v * v
    t = jnp.tanh(v * (GELU_SCALE + (GELU_SCALE * GELU_CUBE) * square))
    half = 0.5 + 0.5 * t
    slope = half + (0.5 * v) * (1.0 - t * t) * (GELU_SCALE + (3.0 * GELU_SCALE * GELU_CUBE) * square)
    return v * half, slope


def main_step(plan, layout, k, waits, *refs):
    first_step = k == 0
    fresh = k in (0, plan.usual)
    final = k == plan.usual - 1
    refs = list(refs[waits:])

    def take(count):
        got = refs[:count]
        del refs[:count]
        return got

    if final:
        place, decode_acc = take(2)
    meta, heights, x_own, x_far, q_own, q_far, codes = take(7)
    kernel_hbm, kernel_t_hbm, mix, project, bias, book = take(6)
    if not first_step:
        x_past, q_past, carry_own, carry_far = take(4)
    if not fresh:
        past_accs = take(5)
    win_own, win_far, next_own, next_far = take(4)
    if final:
        laid_out = take(3)
    if not final:
        sums_out = take(5)
    kernel_acc, mix_acc, project_acc, book_acc, bias_acc = take(5)
    kernel, kernel_t, weight_sems = take(3)
    xo, xf, qo, qf, qd, xc_o, xc_f, qc, code_rows, act3, slope_x, grad3, block_g = take(13)
    second_s, slope_s, low_s, mixed_s, code_s, hot_s, found_s, diff_s, sems = refs

    chunk, start = plan.chunks[k], plan.starts[k]
    images, rows, block = plan.images, plan.rows[k], plan.block[k]
    half = chunk // 2
    spots = block * SIDE
    low = meta[images + k]
    high = meta[images + k + 1]

    copies = [
        (x_own.at[pl.ds(start, LEAD + chunk)], xo.at[pl.ds(0, LEAD + chunk)]),
        (x_far, xf.at[pl.ds(LEAD, chunk)]),
        (q_own.at[pl.ds(start // 2, half)], qo.at[pl.ds(LEAD, half)]),
        (q_far, qf.at[pl.ds(LEAD, half)]),
    ]
    if not first_step:
        past = plan.chunks[k - 1]
        copies += [
            (x_past.at[pl.ds(past - LEAD, LEAD)], xf.at[pl.ds(0, LEAD)]),
            (q_own.at[pl.ds(start // 2 - LEAD, LEAD)], qo.at[pl.ds(0, LEAD)]),
            (q_past.at[pl.ds(past // 2 - LEAD, LEAD)], qf.at[pl.ds(0, LEAD)]),
        ]
    accs = (mix_acc, project_acc, book_acc, bias_acc, kernel_acc)
    early = len(copies)
    if not fresh:
        copies += list(zip(past_accs[1:] + past_accs[:1], accs))
    weight_copies = []
    for i, (source, target) in enumerate(((kernel_hbm, kernel), (kernel_t_hbm, kernel_t))):
        weight_copies.append(pltpu.make_async_copy(source, target, weight_sems.at[i]))
    started = []
    for i, (source, target) in enumerate(copies):
        started.append(pltpu.make_async_copy(source, target, sems.at[i]))
        started[-1].start()
    for copy in weight_copies:
        copy.start()
    started, later = started[:early], started[early:]

    if fresh:
        for acc in accs:
            acc[...] = jnp.zeros(acc.shape, F32)

    blank = jnp.zeros((SIDE, SIDE, HALF), BF16)
    no_row = jnp.full((SIDE, SIDE, HALF), MARK, F32)
    code_rows[...] = jnp.full(code_rows.shape, -1, jnp.int32)
    for r in range(0, rows + 2 * block, SIDE):
        part = pl.ds(r, SIDE)
        xc_o[part] = blank
        xc_f[part] = blank
        if r < rows:
            qc[part] = no_row
    for copy in started:
        copy.wait()

    lane3 = lax.broadcasted_iota(jnp.int32, (1, SIDE, HALF), 2) < HALF // 2

    def spread(r0, count):
        both = (qo[pl.ds(r0, count)] + qf[pl.ds(r0, count)].astype(F32)).reshape(count * SIDE, HALF)
        turned = pltpu.roll(both, HALF // 2, 1).reshape(count, SIDE, HALF)
        both = both.reshape(count, SIDE, HALF)
        return jnp.where(lane3, both, turned), jnp.where(lane3, turned, both)

    upper, lower = spread(LEAD, half)
    qd[pl.ds(LEAD, half)] = upper
    qd[pl.ds(LEAD + half, half)] = lower
    if not first_step:
        _, lower = spread(0, LEAD)
        qd[0:LEAD] = lower

    per_row = HALF // SIDE

    def put(b, dst):
        src = meta[b] - start + LEAD
        xc_o[pl.ds(dst, SIDE)] = xo[pl.ds(src, SIDE)]
        xc_f[pl.ds(dst, SIDE)] = xf[pl.ds(src, SIDE)]
        qc[pl.ds(dst, SIDE)] = qd[pl.ds(src, SIDE)]
        end = dst + heights[b]
        xc_o[pl.ds(end, SIDE)] = blank
        xc_f[pl.ds(end, SIDE)] = blank
        qc[pl.ds(end, SIDE)] = no_row
        put_codes(code_rows, codes, b, heights[b], dst)
        return end + 1

    used = lax.fori_loop(low, high, put, jnp.int32(1))
    blocks = jnp.where(high > low, (used + (block - 1)) // block, 0)

    column = lax.rem(lax.broadcasted_iota(jnp.int32, (TILE, 1), 0), SIDE)
    not_first = column != 0
    not_last = column != SIDE - 1

    def shifted(value):
        back = jnp.where(not_first, pltpu.roll(value, 1, 0), 0.0)
        ahead = jnp.where(not_last, pltpu.roll(value, TILE - 1, 0), 0.0)
        return back.astype(BF16), ahead.astype(BF16)

    edge = jnp.zeros((SIDE, 3 * 2 * HALF), BF16)
    act3[0:SIDE] = edge
    grad3[0:SIDE] = edge
    beyond = pl.multiple_of((blocks * block + 1) * SIDE, SIDE)
    grad3[pl.ds(beyond, SIDE)] = edge

    tiles = range(0, spots, TILE)

    def read_x(r0, t):
        part = pl.ds(r0 + t // SIDE, TILE // SIDE)
        o = xc_o[part].reshape(TILE, HALF)
        f = xc_f[part].reshape(TILE, HALF)
        return jnp.concatenate([o, f], axis=1).astype(F32)

    def at(row, count=block):
        return pl.ds(pl.multiple_of(row * SIDE, SIDE), count * SIDE)

    def tile_at(row, t):
        return pl.ds(pl.multiple_of(row * SIDE, SIDE) + t, TILE)

    def activate(j, carry):
        r0 = j * block
        for t in tiles:
            value, slope = gelu_parts(read_x(r0, t))
            slope_x[tile_at(r0, t), :] = slope
            back, ahead = shifted(value)
            act3[tile_at(r0 + 1, t), 0 : 2 * HALF] = back
            act3[tile_at(r0 + 1, t), 2 * HALF : 4 * HALF] = value.astype(BF16)
            act3[tile_at(r0 + 1, t), 4 * HALF : 6 * HALF] = ahead
        return carry

    fused = k < plan.usual
    lax.fori_loop(0, 2 if fused else blocks + 1, activate, 0)
    for copy in later:
        copy.wait()
    for copy in weight_copies:
        copy.wait()

    bias_first = bias[0:1, :]
    bias_mix = bias[1:2, :]
    bias_code = bias[8:9, 0:HALF]
    lane = lax.broadcasted_iota(jnp.int32, (1, HALF), 1) < HALF // 2
    hb = block // 2
    hs = hb * SIDE

    def add_rows(total, value):
        value = value.astype(F32)
        for i in range(0, value.shape[0], 8):
            part = value[i : i + 8]
            total = part if total is None else total + part
        return total

    half_tiles = range(0, hs, TILE)
    code_of = numbers(book_acc.shape[0], HALF)
    halves = (0, hs)

    def middle(j, carry):
        r0 = j * block
        for i in range(block // per_row):
            row = code_rows[pl.ds(j * (block // per_row) + i, 1), :]
            hot_s[:, i * HALF : (i + 1) * HALF] = one_hot_columns(row, code_of)
        for h in halves:
            found_s[h : h + hs] = dot(book[...], hot_s[:, h : h + hs]).astype(BF16).T
        pre = []
        for h in halves:
            window = jnp.concatenate([act3[at(r0 + i + h // SIDE, hb), :] for i in range(3)], axis=1)
            pre.append(dot(window, kernel[...]))
        for h, part in zip(halves, pre):
            for t in half_tiles:
                value, slope = gelu_parts(part[t : t + TILE] + bias_first)
                second_s[h + t : h + t + TILE] = value.astype(BF16)
                slope_s[h + t : h + t + TILE] = slope
        mixed = [dot(second_s[h : h + hs], mix[...]) for h in halves]
        for h, part in zip(halves, mixed):
            for t in half_tiles:
                low_s[h + t : h + t + TILE] = (read_x(r0, h + t) + part[t : t + TILE] + bias_mix).astype(BF16)
        latents = [dot(low_s[h : h + hs], project[i]) for i, h in enumerate(halves)]
        total = None
        for t in half_tiles:
            first = pl.ds(r0 + t // SIDE, TILE // SIDE)
            other = pl.ds(r0 + hb + t // SIDE, TILE // SIDE)
            ch = jnp.where(lane, found_s[t : t + TILE].astype(F32), found_s[hs + t : hs + t + TILE].astype(F32))
            q = jnp.where(lane3, qc[first], qc[other]).reshape(TILE, HALF)
            live = q < 0.5 * MARK
            latent = latents[0][t : t + TILE] + latents[1][t : t + TILE] + bias_code
            diff = jnp.where(live, latent - ch, 0.0)
            code_grad = jnp.where(live, q + (2.0 * COMMIT) * diff, 0.0).astype(BF16)
            code_s[t : t + TILE] = code_grad
            total = add_rows(total, code_grad)
            big = diff.astype(BF16).astype(F32)
            small = diff - big
            turned = pltpu.roll(small, HALF // 2, 1)
            diff_s[t : t + TILE] = jnp.where(lane, big, turned).astype(BF16)
            turned = pltpu.roll(big, HALF // 2, 1)
            diff_s[hs + t : hs + t + TILE] = jnp.where(lane, turned, small).astype(BF16)
        bias_acc[16:24, 0:HALF] += total
        total = None
        blocks_g = [dot(code_s[...], project[i], NT) for i in range(2)]
        for h, part in zip(halves, blocks_g):
            for t in half_tiles:
                block_g[tile_at(r0, h + t), :] = part[t : t + TILE]
                mixed_grad = part[t : t + TILE].astype(BF16)
                mixed_s[h + t : h + t + TILE] = mixed_grad
                total = add_rows(total, mixed_grad)
        bias_acc[8:16] += total
        second_grad = [dot(mixed_s[h : h + hs], mix[...], NT) for h in halves]
        total = None
        for h, part in zip(halves, second_grad):
            for t in half_tiles:
                first_grad = slope_s[h + t : h + t + TILE] * part[t : t + TILE]
                back, ahead = shifted(first_grad)
                first_low = first_grad.astype(BF16)
                grad3[tile_at(r0 + 1, h + t), 0 : 2 * HALF] = ahead
                grad3[tile_at(r0 + 1, h + t), 2 * HALF : 4 * HALF] = first_low
                grad3[tile_at(r0 + 1, h + t), 4 * HALF : 6 * HALF] = back
                total = add_rows(total, first_low)
        bias_acc[0:8] += total
        book_acc[...] += dot(hot_s[...], diff_s[...])
        mix_acc[...] += dot(second_s[...], mixed_s[...], TN)
        project_acc[...] += jnp.where(lane, dot(low_s[0:hs], code_s[...], TN), dot(low_s[hs:], code_s[...], TN))
        return carry

    def finish(j, carry):
        r0 = j * block
        active = act3[at(r0 + 1), 2 * HALF : 4 * HALF].T
        for i in range(3):
            kernel_acc[:, i * 6 * HALF : (i + 1) * 6 * HALF] += dot(active, grad3[at(r0 + 2 - i), :])
        grads = []
        for h in halves:
            window = jnp.concatenate([grad3[at(r0 + 2 - i + h // SIDE, hb), :] for i in range(3)], axis=1)
            grads.append(dot(window, kernel_t[...]))
        for h, grad in zip(halves, grads):
            for t in half_tiles:
                here = tile_at(r0, h + t)
                out = (block_g[here, :] + slope_x[here, :] * grad[t : t + TILE]).astype(BF16)
                part = pl.ds(r0 + (h + t) // SIDE, TILE // SIDE)
                xc_o[part] = out[:, :HALF].reshape(TILE // SIDE, SIDE, HALF)
                xc_f[part] = out[:, HALF:].reshape(TILE // SIDE, SIDE, HALF)
        return carry

    def opening(j, carry):
        middle(j, carry)
        return activate(j + 2, carry)

    def steady(j, carry):
        finish(j - 2, carry)
        middle(j, carry)
        return activate(j + 2, carry)

    if fused:
        lax.fori_loop(0, jnp.minimum(blocks, 2), opening, 0)
        lax.fori_loop(2, blocks, steady, 0)
        lax.fori_loop(jnp.maximum(blocks - 2, 0), blocks, finish, 0)
    else:
        lax.fori_loop(0, blocks, middle, 0)
        lax.fori_loop(0, blocks, finish, 0)
    leaving = []
    if not final:
        leaving += list(zip((kernel_acc, mix_acc, project_acc, book_acc, bias_acc), sums_out))
        for i, (source, target) in enumerate(leaving):
            leaving[i] = pltpu.make_async_copy(source, target, sems.at[i])
            leaving[i].start()

    out_o, out_f = xo, xf
    if first_step:
        out_o[0:LEAD] = blank
        out_f[0:LEAD] = blank
    else:
        out_o[0:LEAD] = carry_own[...]
        out_f[0:LEAD] = carry_far[...]

    def collect(b, src):
        dst = meta[b] - start + LEAD
        out_o[pl.ds(dst, SIDE)] = xc_o[pl.ds(src, SIDE)]
        out_f[pl.ds(dst, SIDE)] = xc_f[pl.ds(src, SIDE)]
        return src + heights[b] + 1

    lax.fori_loop(low, high, collect, jnp.int32(1))
    size = win_own.shape[0]
    windows = (
        (out_o.at[pl.ds(0, size)], win_own),
        (out_f.at[pl.ds(0, size)], win_far),
        (out_o.at[pl.ds(chunk, LEAD)], next_own),
        (out_f.at[pl.ds(chunk, LEAD)], next_far),
    )
    for i, (source, target) in enumerate(windows):
        leaving.append(pltpu.make_async_copy(source, target, sems.at[5 + i]))
        leaving[-1].start()
    if final:
        sums = (kernel_acc, mix_acc, project_acc, book_acc, bias_acc, decode_acc)
        laid_out += [slope_x.at[pl.ds(0, layout.rows), pl.ds(i * HALF, HALF)] for i in range(2)]
        leaving += gather_grads(plan, layout, place, meta, sums, *laid_out, sems)
    for copy in leaving:
        copy.wait()


class Layout:
    def __init__(self, devices, book_rows, embed):
        self.mix = 9 * 2 * HALF
        self.project = self.mix + 2 * HALF
        self.book = self.project + HALF // 2
        self.bias = self.book + book_rows // 2
        self.decode = self.bias + 8
        used = self.decode + embed + 8
        self.devices = devices
        self.piece = -(-used // (devices * SIDE)) * SIDE
        self.rows = self.piece * devices
        self.half = self.rows // 2
        self.used = used


def lay_out(layout, swap, kernel_acc, mix_acc, project_acc, book_acc, bias_acc, decode_acc, own, far):
    def lanes(value):
        return value[:, :HALF], value[:, HALF:]

    def order(first, second):
        return jnp.where(swap, second, first), jnp.where(swap, first, second)

    row = 0
    for tap in range(9):
        block = kernel_acc[:, tap * 2 * HALF : (tap + 1) * 2 * HALF]
        mine, theirs = lanes(block)
        a, b = order(mine[:HALF], mine[HALF:])
        own[row : row + HALF] = a
        own[row + HALF : row + 2 * HALF] = b
        a, b = order(theirs[:HALF], theirs[HALF:])
        far[row : row + HALF] = a
        far[row + HALF : row + 2 * HALF] = b
        row += 2 * HALF
    row = layout.mix
    for target, part in ((own, mix_acc[:HALF]), (far, mix_acc[HALF:])):
        a, b = order(*lanes(part))
        target[row : row + HALF] = a
        target[row + HALF : row + 2 * HALF] = b
    row = layout.project
    side = HALF // 2
    for target, part in ((own, project_acc[:HALF]), (far, project_acc[HALF:])):
        part = part + pltpu.roll(part, side, 1)
        target[row : row + side] = part.T[:side]
    row = layout.book
    book = book_acc[...]
    book = -2.0 * (book + pltpu.roll(book, side, 1))
    book = book.T[:side]
    for c in range(book.shape[1] // HALF):
        part = book[:, c * HALF : (c + 1) * HALF]
        own[row + c * side : row + (c + 1) * side] = part
        far[row + c * side : row + (c + 1) * side] = part
    row = layout.bias
    sums = [jnp.sum(bias_acc[8 * i : 8 * i + 8], axis=0, keepdims=True) for i in range(3)]
    code = sums[2][:, :HALF]
    code = code + pltpu.roll(code, side, 1)
    which = lax.broadcasted_iota(jnp.int32, (8, HALF), 0)
    for target, first in ((own, 0), (far, HALF)):
        part = jnp.where(which == 0, sums[0][:, first : first + HALF], sums[1][:, first : first + HALF])
        target[row : row + 8] = jnp.where(which == 2, code, jnp.where(which < 2, part, 0.0))
    row = layout.decode
    rest = layout.rows - row
    own[row:] = jnp.zeros((rest, HALF), F32)
    far[row:] = jnp.zeros((rest, HALF), F32)
    if decode_acc is not None:
        own[row : row + decode_acc.shape[0]] = decode_acc[...]


def gather_plain(layout, place, *refs):
    lay_out(layout, place[0] == 1, *refs[:5], None, *refs[5:])


def gather_grads(plan, layout, place, meta, accs, keep_own, keep_far, send, own, far, sems):
    lay_out(layout, place[0] == 1, *accs, own, far)
    base = plan.images + len(plan.chunks) + 1
    over = (meta[base + 4] > plan.covered).astype(F32)
    which = lax.broadcasted_iota(jnp.int32, (8, HALF), 0)
    row = layout.bias
    own[row : row + 8] = jnp.where(which == 3, over, own[row : row + 8])
    half = layout.half
    mine = pl.ds(pl.multiple_of(place[1] * half, SIDE), half)
    other = pl.ds(pl.multiple_of((1 - place[1]) * half, SIDE), half)
    kept = []
    for i, (source, target) in enumerate(((own, keep_own), (far, keep_far))):
        kept.append(pltpu.make_async_copy(source.at[mine, :], target, sems.at[9 + i]))
        kept[-1].start()
    send[0] = own[other, :].astype(BF16)
    send[1] = far[other, :].astype(BF16)
    return kept


def hold(*refs):
    pass


def add_far(keep_far, came, out):
    out[...] = (keep_far[...] + came[1].astype(F32)).astype(BF16)


def add_own(keep_own, came, came_far, out, token):
    token[...] = jnp.zeros_like(token)
    total = keep_own[...] + came[0].astype(F32) + came_far[...].astype(F32)
    out[...] = total.astype(BF16).reshape(out.shape)


def add_pieces(pieces, _, out, token):
    token[...] = jnp.zeros_like(token)
    total = pieces[0].astype(F32)
    for i in range(1, pieces.shape[0]):
        total = total + pieces[i].astype(F32)
    out[...] = jnp.broadcast_to(total.astype(BF16)[None], out.shape)


def write_grads(layout, place, mine, theirs, kernel, first_bias, mix, mix_bias, project, project_bias, book, decode, decode_bias, whole):
    half = layout.half
    whole[pl.ds(pl.multiple_of(place[1] * half, SIDE), half), :] = mine[...].astype(F32)
    whole[pl.ds(pl.multiple_of((1 - place[1]) * half, SIDE), half), :] = theirs[...].astype(F32)
    split_grads(layout, whole, kernel, first_bias, mix, mix_bias, project, project_bias, book, decode, decode_bias)


def split_grads(layout, whole, kernel, first_bias, mix, mix_bias, project, project_bias, book, decode, decode_bias):
    for tap in range(9):
        kernel[tap] = whole[tap * 2 * HALF : (tap + 1) * 2 * HALF]
    row = layout.mix
    mix[:, :HALF] = whole[row : row + HALF]
    mix[:, HALF:] = whole[row + HALF : row + 2 * HALF]
    side = HALF // 2
    for row, target in ((layout.project, project), (layout.book, book)):
        for c in range(target.shape[1] // HALF):
            target[:, c * HALF : (c + 1) * HALF] = whole[row + c * side : row + (c + 1) * side]
    row = layout.bias
    first_bias[...] = whole[row : row + 1]
    mix_bias[...] = whole[row + 1 : row + 2]
    project_bias[...] = whole[row + 2 : row + 3, :side]
    row = layout.decode
    n = decode.shape[0]
    decode[...] = whole[row : row + n]
    decode_bias[...] = whole[row + n : row + n + 1]


def split_again(layout, total, extra, *refs):
    whole = refs[-1]
    whole[...] = total[...].astype(F32) + extra[...]
    split_grads(layout, whole, *refs[:-1])


def restore_rows(plan, n, waits, *refs):
    meta, heights, *refs = refs[waits:]
    own, far, out, token = refs[:n], refs[n : 2 * n], refs[2 * n], refs[2 * n + 1]
    token[...] = jnp.zeros_like(token)
    stage_own, stage_far, sems = refs[2 * n + 2 :]
    copies = []
    for k in range(n):
        size = plan.chunks[k] + (LEAD if k == n - 1 else 0)
        for i, (source, target) in enumerate(((own[k], stage_own), (far[k], stage_far))):
            from_rows = source.at[pl.ds(0, size)]
            copies.append(pltpu.make_async_copy(from_rows, target.at[pl.ds(plan.starts[k], size)], sems.at[i, k]))
            copies[-1].start()
    for copy in copies:
        copy.wait()
    base = plan.images + len(plan.chunks) + 1
    own_row, send_row = meta[base], meta[base + 1]
    first, last = meta[base + 2], meta[base + 3]
    row_of = lax.broadcasted_iota(jnp.int32, (SIDE, 1, 1), 0)

    def own_image(b, carry):
        rows = stage_own[pl.ds(meta[b] + LEAD, SIDE)]
        out[b] = jnp.where(row_of < heights[b], rows, jnp.zeros_like(rows))
        return carry

    def far_image(b, carry):
        rows = stage_far[pl.ds(meta[b] + own_row - send_row + LEAD, SIDE)]
        out[b] = jnp.where(row_of < heights[b], rows, jnp.zeros_like(rows))
        return carry

    lax.fori_loop(first, last, own_image, 0)
    lax.fori_loop(0, first, far_image, 0)
    lax.fori_loop(last, plan.images, far_image, 0)


def trade(value):
    return lax.ppermute(value, "mp", [(0, 1), (1, 0)])


def held(value, *others):
    return pl.pallas_call(
        hold,
        out_shape=shape(value.shape, value.dtype),
        in_specs=[ANY] * (1 + len(others)),
        out_specs=ANY,
        input_output_aliases={0: 0},
        compiler_params=params(60),
        name="hold",
    )(value, *others)


def run_main(plan, layout, k, meta, heights, streams, weights, state, waits=(), ending=()):
    chunk, rows, block = plan.chunks[k], plan.rows[k], plan.block[k]
    last = k >= plan.usual - 1
    final = k == plan.usual - 1
    x_own, x_far, q_own, q_far, codes = streams
    book_rows = weights[-1].shape[1]
    args = [*waits, *ending, meta, heights, x_own, x_far[k], q_own, q_far[k], codes, *weights]
    specs = [ANY] * len(waits) + ([SMEM, VMEM] if final else [])
    specs += [SMEM, SMEM, ANY, ANY, ANY, ANY, VMEM, ANY, ANY] + [VMEM] * (len(weights) - 2)
    alias = {}
    if state is not None:
        args += [x_far[k - 1], q_far[k - 1], *state]
        specs += [ANY, ANY, VMEM, VMEM] + [ANY] * (len(state) - 2)
        if not final:
            for i in range(len(state) - 2):
                alias[len(args) - 5 + i] = 4 + i
    size = chunk + LEAD if last else chunk
    tile = (SIDE, HALF)
    outs = [shape((size,) + tile, BF16)] * 2 + [shape((LEAD,) + tile, BF16)] * 2
    sums = [(2 * HALF, 18 * HALF), (2 * HALF, 2 * HALF), (2 * HALF, HALF), (book_rows, HALF), (24, 2 * HALF)]
    scratch = [pltpu.VMEM(dims, F32) for dims in sums]
    out_specs = [ANY] * 4
    if final:
        outs += [shape((layout.half, HALF), F32)] * 2 + [shape((2, layout.half, HALF), BF16)]
        out_specs += [ANY, ANY, VMEM]
    else:
        outs += [shape(dims, F32) for dims in sums]
        out_specs += [ANY] * 5
    scratch += [pltpu.VMEM((18 * HALF, 2 * HALF), BF16)] * 2 + [pltpu.SemaphoreType.DMA((2,))]
    half = chunk // 2
    spots = block * SIDE
    scratch += [
        pltpu.VMEM((LEAD + chunk + 2 * SIDE,) + tile, BF16),
        pltpu.VMEM((LEAD + chunk + 2 * SIDE,) + tile, BF16),
        pltpu.VMEM((LEAD + half,) + tile, F32),
        pltpu.VMEM((LEAD + half,) + tile, BF16),
        pltpu.VMEM((LEAD + chunk + SIDE,) + tile, F32),
        pltpu.VMEM((rows + 2 * block + SIDE,) + tile, BF16),
        pltpu.VMEM((rows + 2 * block + SIDE,) + tile, BF16),
        pltpu.VMEM((rows + 2 * SIDE,) + tile, F32),
        pltpu.VMEM((-(-(rows * SIDE // HALF + 4) // 8) * 8, HALF), jnp.int32),
        pltpu.VMEM(((rows + 2 * block + 2) * SIDE, 6 * HALF), BF16),
        pltpu.VMEM(((rows + 2 * block) * SIDE, 2 * HALF), F32),
        pltpu.VMEM(((rows + 2) * SIDE, 6 * HALF), BF16),
        pltpu.VMEM((rows * SIDE, 2 * HALF), F32),
        pltpu.VMEM((spots, 2 * HALF), BF16),
        pltpu.VMEM((spots, 2 * HALF), F32),
        pltpu.VMEM((spots, 2 * HALF), BF16),
        pltpu.VMEM((spots, 2 * HALF), BF16),
        pltpu.VMEM((spots // 2, HALF), BF16),
        pltpu.VMEM((book_rows, spots), BF16),
        pltpu.VMEM((spots, HALF), BF16),
        pltpu.VMEM((spots, HALF), BF16),
        pltpu.SemaphoreType.DMA((13,)),
    ]
    spots = chunk * SIDE
    return pl.pallas_call(
        functools.partial(main_step, plan, layout, k, len(waits)),
        out_shape=outs,
        in_specs=specs,
        out_specs=out_specs,
        scratch_shapes=scratch,
        input_output_aliases=alias,
        compiler_params=params(58),
        cost_estimate=cost(60 * 65536 * spots, 8 * MIB, 2 * 256 * spots),
        name=f"main_{k}",
    )(*args)


def local(
    image_latents,
    image_heights,
    code_index,
    kernel_three,
    bias_three,
    weight_mix,
    bias_mix,
    weight_project,
    bias_project,
    codebook,
    weight_decode,
    bias_decode,
    out_grad,
):
    images = image_latents.shape[0]
    plan = Plan(images)
    n = len(plan.chunks)
    tile = (SIDE, HALF)
    where = lax.axis_index("mp").astype(jnp.int32)
    core = lax.rem(lax.axis_index("dp").astype(jnp.int32), 2)
    spot = place = jnp.stack([where, core])

    devices = lax.axis_size("dp")
    across = [(i, i ^ 1) for i in range(devices)]
    kernel_half = lax.dynamic_slice_in_dim(kernel_three, core * HALF, HALF, 1)
    far_kernel = trade(kernel_half)
    far_kernel_other = lax.ppermute(far_kernel, "dp", across)

    packed = pl.pallas_call(
        functools.partial(pack_latents, plan),
        out_shape=[
            shape((meta_size(plan),), jnp.int32),
            shape((LEAD + plan.total,) + tile, BF16),
        ]
        + [shape((c,) + tile, BF16) for c in plan.chunks],
        in_specs=[SMEM, SMEM, HBM, ANY],
        out_specs=[SMEM, ANY] + [ANY] * n,
        scratch_shapes=[
            pltpu.VMEM((images, SIDE) + tile, BF16),
            pltpu.VMEM((plan.packed + SIDE,) + tile, BF16),
            pltpu.SemaphoreType.DMA((8,)),
            pltpu.SemaphoreType.DMA((n + 1,)),
        ],
        compiler_params=params(60),
        cost_estimate=cost(0, 12 * MIB),
        name="pack_latents",
    )(image_heights, place, image_latents, kernel_half)
    meta, x_own, x_send = packed[0], packed[1], packed[2:]

    packed = pl.pallas_call(
        functools.partial(pack_code_grads, plan),
        out_shape=[shape((plan.total // 2,) + tile, F32), shape((2 * HALF + HALF // 2 + SIDE, HALF), BF16)]
        + [shape((c // 2,) + tile, BF16) for c in plan.chunks],
        in_specs=[SMEM] + [HBM] * 6 + [ANY],
        out_specs=[VMEM] * (n + 2),
        scratch_shapes=[
            pltpu.VMEM((images, SIDE) + tile, BF16),
            pltpu.VMEM((plan.packed + SIDE,) + tile, BF16),
            pltpu.SemaphoreType.DMA((8,)),
            pltpu.SemaphoreType.DMA((5,)),
            pltpu.VMEM(weight_decode.shape, BF16),
            pltpu.VMEM(weight_mix.shape, BF16),
            pltpu.VMEM(weight_project.shape[::-1], BF16),
            pltpu.VMEM((1, HALF), BF16),
            pltpu.VMEM((1, HALF), BF16),
        ],
        compiler_params=params(60),
        cost_estimate=cost(2 * 2 * plan.total * SIDE * 256 * 128, 10 * MIB),
        name="pack_code_grads",
    )(meta, out_grad, weight_decode, weight_mix, weight_project.T, bias_three.reshape(1, HALF), bias_mix.reshape(1, HALF), far_kernel)
    q_own, small, q_send = packed[0], packed[1], packed[2:]

    book_rows, embed = codebook.shape
    codebook_t = codebook.T
    far_small = trade(small)
    usual = plan.usual
    x_far, q_far = [], []
    x_far.append(trade(x_send[0]))
    q_far.append(trade(q_send[0]))

    weights = pl.pallas_call(
        prepare_weights,
        out_shape=[
            shape((18 * HALF, 2 * HALF), BF16),
            shape((18 * HALF, 2 * HALF), BF16),
            shape((2 * HALF, 2 * HALF), BF16),
            shape((2, 2 * HALF, HALF), BF16),
            shape((SIDE, 2 * HALF), F32),
            shape((HALF, book_rows), BF16),
        ],
        in_specs=[SMEM, HBM, HBM, HBM] + [VMEM] * 4,
        out_specs=[VMEM] * 6,
        scratch_shapes=[pltpu.VMEM(kernel_three.shape, BF16)] * 2 + [pltpu.SemaphoreType.DMA((3,))],
        compiler_params=params(20),
        cost_estimate=cost(0, 5 * MIB),
        name="prepare_weights",
    )(place, kernel_three, far_kernel, far_kernel_other, small, far_small, bias_project.reshape(1, -1), codebook_t)

    groups = 8
    group = images // groups
    codes = code_index.reshape(images, SIDE * SIDE)
    whole = lambda dims: pl.BlockSpec(dims, lambda g: (0,) * len(dims))
    four = pl.BlockSpec((group, SIDE) + tile, lambda g: (g, 0, 0, 0))
    row = pl.BlockSpec((group, SIDE * SIDE), lambda g: (g, 0))
    def code_sums(first, steps):
        return pl.pallas_call(
            functools.partial(sum_codes, first, group),
            grid=(steps,),
            out_shape=shape((embed + 8, HALF), F32),
            in_specs=[
                SMEM,
                pl.BlockSpec((group, SIDE * SIDE), lambda g: (g + first, 0)),
                pl.BlockSpec((group, SIDE) + tile, lambda g: (g + first, 0, 0, 0)),
                whole((embed, book_rows)),
                ANY,
                ANY,
            ],
            out_specs=whole((embed + 8, HALF)),
            scratch_shapes=[
                pltpu.VMEM((book_rows, group * SIDE * SIDE), BF16),
                pltpu.VMEM((group * SIDE * SIDE, HALF), BF16),
                pltpu.VMEM((book_rows, HALF), F32),
            ],
            compiler_params=params(60),
            cost_estimate=cost(steps * group * 256 * 512 * 256, steps * group * 65536),
            name=f"sum_codes_{first}",
        )(image_heights, codes, out_grad, codebook_t, small, far_kernel)

    def decode(after):
        return pl.pallas_call(
            functools.partial(decode_images, plan, groups),
            grid=(groups,),
            out_shape=[shape((images, SIDE) + tile, BF16), shape((8, HALF), F32)],
            in_specs=[SMEM, row, whole((embed, book_rows)), whole((embed, HALF)), whole((1, HALF)), ANY],
            out_specs=[four, whole((8, HALF))],
            scratch_shapes=[pltpu.VMEM((HALF, book_rows), BF16)],
            compiler_params=params(32),
            cost_estimate=cost(images * 256 * 512 * 256, 5 * MIB),
            name="decode_images",
        )(image_heights, codes, codebook_t, weight_decode, bias_decode.reshape(1, HALF), after)

    decode_acc = code_sums(0, groups)
    for k in range(1, usual):
        x_far.append(trade(held(x_send[k], decode_acc, far_small, x_far[0], q_far[0])))
        q_far.append(trade(held(q_send[k], decode_acc, far_small, x_far[0], q_far[0])))

    layout = Layout(devices, book_rows, embed)
    half, piece, chips = layout.half, layout.piece, devices // 2
    streams = (x_own, x_far, q_own, q_far, codes)
    state = None
    win_own, win_far = [], []
    for k in range(usual):
        waits = win_far[k - 2 : k - 1] if k > 1 else []
        ending = (spot, decode_acc) if k == usual - 1 else ()
        outs = run_main(plan, layout, k, meta, image_heights, streams, weights, state, waits, ending)
        win_own.append(outs[0])
        if k < usual - 1:
            win_far.append(trade(outs[1]))
        state = outs[2:]
    last_window = outs[1]
    carry, (keep_own, keep_far, send) = state[:2], state[2:]

    def restore(own, far, waits=()):
        count = len(own)
        return pl.pallas_call(
            functools.partial(restore_rows, plan, count, len(waits)),
            out_shape=[shape((images, SIDE) + tile, BF16), shape((8, HALF), F32)],
            in_specs=[ANY] * len(waits) + [SMEM, SMEM] + [ANY] * (2 * count),
            out_specs=[VMEM, VMEM],
            scratch_shapes=[
                pltpu.VMEM((plan.total + LEAD + SIDE,) + tile, BF16),
                pltpu.VMEM((plan.total + LEAD + SIDE,) + tile, BF16),
                pltpu.SemaphoreType.DMA((2, count)),
            ],
            compiler_params=params(60),
            cost_estimate=cost(0, 10 * MIB),
            name="restore_rows",
        )(*waits, meta, image_heights, *own, *far)


    def step(body, out, name, *args, waits=()):
        specs = [VMEM] * len(args) + [ANY] * len(waits)
        args = (*args, *waits)
        return pl.pallas_call(
            body,
            out_shape=out,
            in_specs=specs,
            out_specs=[VMEM] * len(out) if isinstance(out, list) else VMEM,
            compiler_params=params(24),
            cost_estimate=cost(0, 2 * MIB),
            name=name,
        )(*args)

    send = held(send, win_far[usual - 2])
    came = lax.ppermute(send, "dp", across)
    far_sums = step(add_far, shape((half, HALF), BF16), "add_far", keep_far, came)
    came_far = trade(far_sums)
    parts = [shape((chips, piece, HALF), BF16), shape((8, HALF), F32)]
    mine, token = step(add_own, parts, "add_own", keep_own, came, came_far)
    win_far.append(trade(held(last_window, token)))
    decoded, token = decode(token)
    cores = [[i for i in range(devices) if i % 2 == c] for c in range(2)]
    mine = lax.all_to_all(mine, "dp", 0, 0, axis_index_groups=cores, tiled=True)
    mine, token = step(add_pieces, parts, "add_pieces", mine, waits=[token])
    latents_grad, token = restore(win_own, win_far, [token])
    mine = lax.all_to_all(mine, "dp", 0, 0, axis_index_groups=cores, tiled=True)
    mine = held(mine, token).reshape(half, HALF)
    theirs = lax.ppermute(mine, "dp", across)

    grads_out = [
        shape((9, 2 * HALF, HALF), F32),
        shape((1, HALF), F32),
        shape((HALF, 2 * HALF), F32),
        shape((1, HALF), F32),
        shape((embed, HALF), F32),
        shape((1, embed), F32),
        shape((embed, book_rows), F32),
        shape((embed, HALF), F32),
        shape((1, HALF), F32),
    ]
    whole = pltpu.VMEM((layout.rows, HALF), F32)

    def usual_end(latents_grad):
        grads = pl.pallas_call(
            functools.partial(write_grads, layout),
            out_shape=grads_out,
            in_specs=[SMEM, VMEM, VMEM],
            out_specs=[VMEM] * 9,
            scratch_shapes=[whole],
            compiler_params=params(24),
            cost_estimate=cost(0, 4 * MIB),
            name="write_grads",
        )(spot, mine, theirs)
        return (latents_grad, *grads)

    def longer_end(latents_grad):
        last_x, last_q = trade(x_send[usual]), trade(q_send[usual])
        streams = (x_own, x_far + [last_x], q_own, q_far + [last_q], codes)
        outs = run_main(plan, layout, usual, meta, image_heights, streams, weights, carry)
        latents_grad, _ = restore(win_own + [outs[0]], win_far + [trade(outs[1])])
        own, far = pl.pallas_call(
            functools.partial(gather_plain, layout),
            out_shape=[shape((layout.rows, HALF), F32)] * 2,
            in_specs=[SMEM] + [VMEM] * 5,
            out_specs=[VMEM] * 2,
            compiler_params=params(40),
            name="gather_plain",
        )(spot, *outs[4:])
        extra = lax.psum(own + trade(far), "dp")
        first, second = jnp.where(core == 0, mine, theirs), jnp.where(core == 0, theirs, mine)
        grads = pl.pallas_call(
            functools.partial(split_again, layout),
            out_shape=grads_out,
            in_specs=[VMEM, VMEM],
            out_specs=[VMEM] * 9,
            scratch_shapes=[whole],
            compiler_params=params(24),
            name="split_again",
        )(jnp.concatenate([first, second]), extra)
        return (latents_grad, *grads)

    flag = layout.bias + 3
    holder = flag // half
    flags = jnp.where(core == holder, mine[flag - holder * half, 0], theirs[flag - holder * half, 0])
    ends = lax.cond(flags.astype(F32) > 0.5, longer_end, usual_end, latents_grad)
    latents_grad, kernel_grad, first_bias, mix_grad, mix_bias, project_grad, project_bias, book, decode, decode_bias = ends
    return (
        decoded,
        latents_grad,
        kernel_grad,
        first_bias.reshape(HALF),
        mix_grad,
        mix_bias.reshape(HALF),
        project_grad.T,
        project_bias.reshape(embed),
        book.T,
        decode,
        decode_bias.reshape(HALF),
    )


def solution(mesh):
    tile = P("dp", None, None, "mp")
    placed = (
        tile,
        P("dp"),
        P("dp", None, None),
        P(None, None, "mp"),
        P("mp"),
        P("mp", None),
        P("mp"),
        P("mp", None),
        P(),
        P(),
        P(None, "mp"),
        P("mp"),
        tile,
    )
    outs = (
        tile,
        tile,
        P(None, None, "mp"),
        P("mp"),
        P("mp", None),
        P("mp"),
        P("mp", None),
        P(),
        P(),
        P(None, "mp"),
        P("mp"),
    )
    return jax.shard_map(local, mesh=mesh, in_specs=placed, out_specs=outs, check_vma=False)
```

```python
import functools

import jax
import jax.numpy as jnp
from jax import lax
from jax.experimental import pallas as pl
from jax.experimental.pallas import tpu as pltpu
from jax.sharding import PartitionSpec as P

SIDE = 16
HALF = 128
LEAD = 16
BLOCK = 32
TILE = 32
MARK = 1e9
GELU_SCALE = 0.7978845608028654
GELU_CUBE = 0.044715
COMMIT = 0.25
F32 = jnp.float32
BF16 = jnp.bfloat16
ANY = pl.BlockSpec(memory_space=pl.ANY)
SMEM = pl.BlockSpec(memory_space=pltpu.SMEM)
HBM = pl.BlockSpec(memory_space=pltpu.HBM)
VMEM = pl.BlockSpec(memory_space=pltpu.VMEM)
MIB = 1 << 20

NT = (((1,), (1,)), ((), ()))
TN = (((0,), (0,)), ((), ()))
NN = (((1,), (0,)), ((), ()))


def dot(a, b, dims=NN):
    return lax.dot_general(a, b, dims, preferred_element_type=F32)


def one_hot_columns(codes, code_of):
    return jnp.where(code_of == codes.astype(jnp.int16), jnp.bfloat16(1), jnp.bfloat16(0))


def numbers(count, width):
    return lax.broadcasted_iota(jnp.int32, (count, width), 0).astype(jnp.int16)


def shape(dims, kind):
    return jax.ShapeDtypeStruct(dims, kind)


def params(mib):
    return pltpu.CompilerParams(vmem_limit_bytes=mib * MIB)


def cost(flops, moved, slow=0):
    return pl.CostEstimate(flops=flops, bytes_accessed=moved, transcendentals=slow)


class Plan:
    def __init__(self, images):
        self.images = images
        longest = images * SIDE // 2 + SIDE // 2
        part = images // 8
        self.chunks = [19 * part, 28 * part]
        self.usual = len(self.chunks)
        rest = longest - sum(self.chunks)
        self.chunks.append(rest)
        self.starts = [sum(self.chunks[:k]) for k in range(len(self.chunks))]
        self.total = sum(self.chunks)
        self.packed = -(-(LEAD + longest + self.total + LEAD) // SIDE) * SIDE
        self.rows, self.block = [], []
        for k, c in enumerate(self.chunks):
            block = BLOCK if k < self.usual else SIDE
            most = 1 + c + 15 + c // 4 + 1
            self.rows.append(-(-most // block) * block)
            self.block.append(block)
        self.covered = sum(self.chunks[: self.usual])


def meta_size(plan):
    return plan.images + len(plan.chunks) + 1 + 5


def plan_rows(plan, heights, place, meta):
    images = plan.images
    base = images + len(plan.chunks) + 1

    def total_of(b, acc):
        return acc + heights[b]

    total = lax.fori_loop(0, images, total_of, jnp.int32(0))

    def split_of(b, state):
        acc, best, split, cut = state
        acc = acc + heights[b]
        worst = jnp.maximum(acc, total - acc)
        better = worst < best
        return (acc, jnp.where(better, worst, best), jnp.where(better, b + 1, split), jnp.where(better, acc, cut))

    _, _, split, cut = lax.fori_loop(0, images, split_of, (jnp.int32(0), jnp.int32(1 << 20), jnp.int32(0), jnp.int32(0)))
    mine = place[0]
    own_first = jnp.where(mine == 0, 0, split)
    own_last = jnp.where(mine == 0, split, images)
    own_row = jnp.where(mine == 0, 0, cut)
    send_row = jnp.where(mine == 0, cut, 0)
    for k in range(len(plan.chunks) + 1):
        meta[images + k] = own_first
    ends = [plan.starts[k] + plan.chunks[k] for k in range(len(plan.chunks))]

    def place_of(b, acc):
        meta[b] = acc - own_row
        acc = acc + heights[b]
        end = acc - own_row
        inside = jnp.logical_and(b >= own_first, b < own_last)
        step = jnp.int32(0)
        for k in range(len(plan.chunks) - 1):
            step = step + (end > ends[k]).astype(jnp.int32)

        @pl.when(inside)
        def _():
            meta[images + 1 + step] = b + 1

        return acc

    lax.fori_loop(0, images, place_of, jnp.int32(0))
    for k in range(len(plan.chunks)):
        meta[images + k + 1] = jnp.maximum(meta[images + k + 1], meta[images + k])
    meta[base] = own_row
    meta[base + 1] = send_row
    meta[base + 2] = own_first
    meta[base + 3] = own_last
    meta[base + 4] = jnp.maximum(cut, total - cut)


def pack_rows(plan, meta, source, packed, piece, count):
    base = plan.images + len(plan.chunks) + 1

    def one(i, carry):
        b = piece * count + i
        row = meta[b] + meta[base] + LEAD
        packed[pl.ds(row, SIDE)] = source[b]
        return carry

    lax.fori_loop(0, count, one, 0)


def pack_latents(plan, heights, place, x_hbm, _, meta, own, *rest):
    n = len(plan.chunks)
    sends, (x_in, packed, sem_in, sem_out) = rest[:n], rest[n:]
    pieces = 8
    count = plan.images // pieces
    fetch = []
    for p in range(pieces):
        part = pl.ds(p * count, count)
        fetch.append(pltpu.make_async_copy(x_hbm.at[part], x_in.at[part], sem_in.at[p]))
        fetch[-1].start()
    plan_rows(plan, heights, place, meta)
    base = plan.images + n + 1
    for p in range(pieces):
        fetch[p].wait()
        pack_rows(plan, meta, x_in, packed, p, count)
    copies = []
    for k in range(n):
        part = pl.ds(LEAD + meta[base + 1] + plan.starts[k], plan.chunks[k])
        copies.append(pltpu.make_async_copy(packed.at[part], sends[k], sem_out.at[k]))
        copies[-1].start()
    copies.append(pltpu.make_async_copy(packed.at[pl.ds(meta[base], LEAD + plan.total)], own, sem_out.at[n]))
    copies[-1].start()
    for copy in copies:
        copy.wait()


def pack_code_grads(plan, meta, og_hbm, *rest):
    n = len(plan.chunks)
    sources, (own, small), rest = rest[:5], rest[6:8], rest[8:]
    sends, rest = rest[:n], rest[n:]
    og_in, packed, sem_in, sem_small = rest[:4]
    held = rest[4:]
    small_fetch = []
    for i in range(5):
        small_fetch.append(pltpu.make_async_copy(sources[i], held[i], sem_small.at[i]))
        small_fetch[-1].start()
    decode_w, weight_mix, project_t, bias_first, bias_mix = held
    pieces = 8
    count = plan.images // pieces
    fetch = []
    for p in range(pieces):
        part = pl.ds(p * count, count)
        fetch.append(pltpu.make_async_copy(og_hbm.at[part], og_in.at[part], sem_in.at[p]))
        fetch[-1].start()
    base = plan.images + n + 1

    def clear(i, carry):
        packed[pl.ds(i * SIDE, SIDE)] = jnp.zeros((SIDE, SIDE, HALF), BF16)
        return carry

    lax.fori_loop(0, packed.shape[0] // SIDE, clear, 0)
    for copy in small_fetch:
        copy.wait()
    side = HALF // 2
    small[0:HALF] = weight_mix[:, :HALF]
    small[HALF : 2 * HALF] = weight_mix[:, HALF:]
    small[2 * HALF : 2 * HALF + side] = project_t[...]
    which = lax.broadcasted_iota(jnp.int32, (SIDE, HALF), 0)
    first, second = bias_first[...].astype(F32), bias_mix[...].astype(F32)
    first = jnp.where(which == 0, first, jnp.where(which == 1, second, 0.0))
    small[2 * HALF + side : 2 * HALF + side + SIDE] = first.astype(BF16)
    w = decode_w[...]
    blank = jnp.zeros_like(w)
    upper = jnp.concatenate([w, blank], axis=0)
    lower = jnp.concatenate([blank, w], axis=0)
    for p in range(pieces):
        fetch[p].wait()
        pack_rows(plan, meta, og_in, packed, p, count)
    for k in range(n):
        half = plan.chunks[k] // 2
        for which in range(2):
            row = LEAD + meta[base + 1 - which] + plan.starts[k]
            a = packed[pl.ds(row, half)].reshape(half * SIDE, HALF)
            b = packed[pl.ds(row + half, half)].reshape(half * SIDE, HALF)
            both = dot(a, upper, NT) + dot(b, lower, NT)
            both = both.reshape(half, SIDE, HALF)
            if which == 0:
                sends[k][...] = both.astype(BF16)
            else:
                own[pl.ds(plan.starts[k] // 2, half)] = both


def prepare_weights(place, own_hbm, far_hbm, far_other_hbm, small, far_small, bias_code, codebook_t, *refs):
    forward, backward, mix, project, bias, book, kernel, far_kernel, sems = refs
    copies = []
    halves = [pl.ds(pl.multiple_of(at * HALF, HALF), HALF) for at in (place[1], 1 - place[1])]
    pairs = [(own_hbm, kernel)]
    pairs += [(source, far_kernel.at[:, rows, :]) for source, rows in zip((far_hbm, far_other_hbm), halves)]
    for i, (source, target) in enumerate(pairs):
        copies.append(pltpu.make_async_copy(source, target, sems.at[i]))
        copies[-1].start()
    for copy in copies:
        copy.wait()
    first = pl.multiple_of(place[0] * HALF, HALF)
    order = (first, HALF - first)
    for tap in range(9):
        for d, source in enumerate((kernel, far_kernel)):
            for c in range(2):
                tile = source[tap, pl.ds(order[c], HALF), :]
                row = tap * 2 * HALF
                forward[row + c * HALF : row + (c + 1) * HALF, d * HALF : (d + 1) * HALF] = tile
                backward[row + d * HALF : row + (d + 1) * HALF, c * HALF : (c + 1) * HALF] = tile.T
    blank = jnp.zeros((HALF, HALF // 2), BF16)
    for d, source in enumerate((small, far_small)):
        rows = pl.ds(d * HALF, HALF)
        for c in range(2):
            mix[rows, c * HALF : (c + 1) * HALF] = source[pl.ds(order[c], HALF), :]
        part = source[2 * HALF : 2 * HALF + HALF // 2, :].T
        project[0, rows, :] = jnp.concatenate([part, blank], axis=1)
        project[1, rows, :] = jnp.concatenate([blank, part], axis=1)
        bias[0:8, d * HALF : (d + 1) * HALF] = source[2 * HALF + HALF // 2 : 2 * HALF + HALF // 2 + SIDE, :].astype(F32)[0:8]
    code = bias_code[...].astype(F32)
    code = jnp.concatenate([code, code], axis=1)
    bias[8:16, :] = jnp.broadcast_to(jnp.concatenate([code, code], axis=1), (8, 2 * HALF))
    book[...] = jnp.concatenate([codebook_t[...], codebook_t[...]], axis=0)


def sum_codes(first, group, heights, codes, og, codebook_t, _, __, grads, hot, cots, sums):
    step = pl.program_id(0)

    @pl.when(step == 0)
    def _():
        sums[...] = jnp.zeros_like(sums)

    spots = SIDE * SIDE
    code_of = numbers(codebook_t.shape[1], spots)
    spot = lax.broadcasted_iota(jnp.int32, (spots, 1), 0)
    for i in range(group):
        live = heights[(first + step) * group + i] * SIDE
        hot[:, i * spots : (i + 1) * spots] = one_hot_columns(codes[i : i + 1, :], code_of)
        cot = og[i].reshape(spots, HALF).astype(F32)
        cots[i * spots : (i + 1) * spots] = jnp.where(spot < live, cot, 0.0).astype(BF16)
    half = sums.shape[0] // 2
    for h in (0, half):
        sums[h : h + half] += dot(hot[h : h + half], cots[...])

    @pl.when(step == pl.num_programs(0) - 1)
    def _():
        total = sums[...]
        book = codebook_t[...].astype(F32)
        w = lax.dot_general(book, total, NN, precision=lax.Precision.HIGHEST, preferred_element_type=F32)
        bias = jnp.sum(total, axis=0, keepdims=True)
        embed = w.shape[0]
        grads[0:embed] = w
        grads[embed : embed + 8] = jnp.broadcast_to(bias, (8, HALF))


def decode_images(plan, steps, heights, codes, codebook_t, decode_w, decode_b, _, decoded, token, table):
    step = pl.program_id(0)
    token[...] = jnp.zeros_like(token)
    group = plan.images // steps

    @pl.when(step == 0)
    def _():
        full = dot(codebook_t[...], decode_w[...], TN) + decode_b[...].astype(F32)
        table[...] = full.T.astype(BF16)

    spots = SIDE * SIDE
    code_of = numbers(codebook_t.shape[1], spots)
    spot = lax.broadcasted_iota(jnp.int32, (spots, 1), 0)
    for i in range(group):
        live = heights[step * group + i] * SIDE
        out = dot(table[...], one_hot_columns(codes[i : i + 1, :], code_of)).T
        decoded[i] = jnp.where(spot < live, out, 0.0).astype(BF16).reshape(SIDE, SIDE, HALF)


def put_codes(code_rows, codes, b, height, dst):
    spot = lax.broadcasted_iota(jnp.int32, (1, SIDE * SIDE), 1)
    lane = lax.broadcasted_iota(jnp.int32, (1, HALF), 1)
    per_row = HALF // SIDE
    row = jnp.where(spot < height * SIDE, codes[pl.ds(b, 1), :], -1)
    turn = lax.rem(dst, per_row) * SIDE
    upper = pltpu.roll(row[:, :HALF], turn, 1)
    lower = pltpu.roll(row[:, HALF:], turn, 1)
    inside = lane >= turn
    pieces = (jnp.where(inside, upper, -1), jnp.where(inside, lower, upper), jnp.where(inside, -1, lower))
    for i, piece in enumerate(pieces):
        target = pl.ds(dst // per_row + i, 1)
        code_rows[target, :] = jnp.where(piece < 0, code_rows[target, :], piece)


def gelu_parts(v):
    square = v * v
    t = jnp.tanh(v * (GELU_SCALE + (GELU_SCALE * GELU_CUBE) * square))
    half = 0.5 + 0.5 * t
    value = v * half
    slope = half + (value - value * half) * (2.0 * GELU_SCALE + (6.0 * GELU_SCALE * GELU_CUBE) * square)
    return value, slope


def main_step(plan, layout, k, waits, *refs):
    first_step = k == 0
    fresh = k in (0, plan.usual)
    final = k == plan.usual - 1
    refs = list(refs[waits:])

    def take(count):
        got = refs[:count]
        del refs[:count]
        return got

    if final:
        place, decode_acc = take(2)
    meta, heights, x_own, x_far, q_own, q_far, codes = take(7)
    kernel_hbm, kernel_t_hbm, mix, project, bias, book = take(6)
    if not first_step:
        x_past, q_past, carry_own, carry_far = take(4)
    if not fresh:
        past_accs = take(5)
    win_own, win_far, next_own, next_far = take(4)
    if final:
        laid_out = take(3)
    if not final:
        sums_out = take(5)
    kernel_acc, mix_acc, project_acc, book_acc, bias_acc = take(5)
    kernel, kernel_t, weight_sems = take(3)
    xo, xf, qo, qf, qd, xc_o, xc_f, qc, code_rows, act3, slope_x, grad3, block_g = take(13)
    second_s, slope_s, low_s, mixed_s, code_s, hot_s, found_s, diff_s, sems = refs

    chunk, start = plan.chunks[k], plan.starts[k]
    images, rows, block = plan.images, plan.rows[k], plan.block[k]
    half = chunk // 2
    spots = block * SIDE
    low = meta[images + k]
    high = meta[images + k + 1]

    copies = [
        (x_own.at[pl.ds(start, LEAD + chunk)], xo.at[pl.ds(0, LEAD + chunk)]),
        (x_far, xf.at[pl.ds(LEAD, chunk)]),
        (q_own.at[pl.ds(start // 2, half)], qo.at[pl.ds(LEAD, half)]),
        (q_far, qf.at[pl.ds(LEAD, half)]),
    ]
    if not first_step:
        past = plan.chunks[k - 1]
        copies += [
            (x_past.at[pl.ds(past - LEAD, LEAD)], xf.at[pl.ds(0, LEAD)]),
            (q_own.at[pl.ds(start // 2 - LEAD, LEAD)], qo.at[pl.ds(0, LEAD)]),
            (q_past.at[pl.ds(past // 2 - LEAD, LEAD)], qf.at[pl.ds(0, LEAD)]),
        ]
    accs = (mix_acc, project_acc, book_acc, bias_acc, kernel_acc)
    early = len(copies)
    if not fresh:
        copies += list(zip(past_accs[1:] + past_accs[:1], accs))
    weight_copies = []
    for i, (source, target) in enumerate(((kernel_hbm, kernel), (kernel_t_hbm, kernel_t))):
        weight_copies.append(pltpu.make_async_copy(source, target, weight_sems.at[i]))
    started = []
    for i, (source, target) in enumerate(copies):
        started.append(pltpu.make_async_copy(source, target, sems.at[i]))
        started[-1].start()
    for copy in weight_copies:
        copy.start()
    started, later = started[:early], started[early:]

    if fresh:
        for acc in accs:
            acc[...] = jnp.zeros(acc.shape, F32)

    blank = jnp.zeros((SIDE, SIDE, HALF), BF16)
    no_row = jnp.full((SIDE, SIDE, HALF), MARK, F32)
    code_rows[...] = jnp.full(code_rows.shape, -1, jnp.int32)
    for r in range(0, rows + 2 * block, SIDE):
        part = pl.ds(r, SIDE)
        xc_o[part] = blank
        xc_f[part] = blank
        if r < rows:
            qc[part] = no_row
    for copy in started:
        copy.wait()

    lane3 = lax.broadcasted_iota(jnp.int32, (1, SIDE, HALF), 2) < HALF // 2

    def spread(r0, count):
        both = (qo[pl.ds(r0, count)] + qf[pl.ds(r0, count)].astype(F32)).reshape(count * SIDE, HALF)
        turned = pltpu.roll(both, HALF // 2, 1).reshape(count, SIDE, HALF)
        both = both.reshape(count, SIDE, HALF)
        return jnp.where(lane3, both, turned), jnp.where(lane3, turned, both)

    upper, lower = spread(LEAD, half)
    qd[pl.ds(LEAD, half)] = upper
    qd[pl.ds(LEAD + half, half)] = lower
    if not first_step:
        _, lower = spread(0, LEAD)
        qd[0:LEAD] = lower

    per_row = HALF // SIDE

    def put(b, dst):
        src = meta[b] - start + LEAD
        xc_o[pl.ds(dst, SIDE)] = xo[pl.ds(src, SIDE)]
        xc_f[pl.ds(dst, SIDE)] = xf[pl.ds(src, SIDE)]
        qc[pl.ds(dst, SIDE)] = qd[pl.ds(src, SIDE)]
        end = dst + heights[b]
        xc_o[pl.ds(end, SIDE)] = blank
        xc_f[pl.ds(end, SIDE)] = blank
        qc[pl.ds(end, SIDE)] = no_row
        put_codes(code_rows, codes, b, heights[b], dst)
        return end + 1

    used = lax.fori_loop(low, high, put, jnp.int32(1))
    blocks = jnp.where(high > low, (used + (block - 1)) // block, 0)

    column = lax.rem(lax.broadcasted_iota(jnp.int32, (TILE, 1), 0), SIDE)
    not_first = column != 0
    not_last = column != SIDE - 1

    def shifted(value):
        back = jnp.where(not_first, pltpu.roll(value, 1, 0), 0.0)
        ahead = jnp.where(not_last, pltpu.roll(value, TILE - 1, 0), 0.0)
        return back.astype(BF16), ahead.astype(BF16)

    edge = jnp.zeros((SIDE, 3 * 2 * HALF), BF16)
    act3[0:SIDE] = edge
    grad3[0:SIDE] = edge
    beyond = pl.multiple_of((blocks * block + 1) * SIDE, SIDE)
    grad3[pl.ds(beyond, SIDE)] = edge

    tiles = range(0, spots, TILE)

    def read_x(r0, t):
        part = pl.ds(r0 + t // SIDE, TILE // SIDE)
        o = xc_o[part].reshape(TILE, HALF)
        f = xc_f[part].reshape(TILE, HALF)
        return jnp.concatenate([o, f], axis=1).astype(F32)

    def at(row, count=block):
        return pl.ds(pl.multiple_of(row * SIDE, SIDE), count * SIDE)

    def tile_at(row, t):
        return pl.ds(pl.multiple_of(row * SIDE, SIDE) + t, TILE)

    def activate(j, carry):
        r0 = j * block
        for t in tiles:
            value, slope = gelu_parts(read_x(r0, t))
            slope_x[tile_at(r0, t), :] = slope
            back, ahead = shifted(value)
            act3[tile_at(r0 + 1, t), 0 : 2 * HALF] = back
            act3[tile_at(r0 + 1, t), 2 * HALF : 4 * HALF] = value.astype(BF16)
            act3[tile_at(r0 + 1, t), 4 * HALF : 6 * HALF] = ahead
        return carry

    fused = k < plan.usual
    lax.fori_loop(0, 2 if fused else blocks + 1, activate, 0)
    for copy in later:
        copy.wait()
    for copy in weight_copies:
        copy.wait()

    bias_first = bias[0:1, :]
    bias_mix = bias[1:2, :]
    bias_code = bias[8:9, 0:HALF]
    lane = lax.broadcasted_iota(jnp.int32, (1, HALF), 1) < HALF // 2
    hb = block // 2
    hs = hb * SIDE

    def add_rows(total, value):
        for i in range(0, value.shape[0], 8):
            part = value[i : i + 8]
            total = part if total is None else total + part
        return total

    half_tiles = range(0, hs, TILE)
    code_of = numbers(book_acc.shape[0], HALF)
    halves = (0, hs)

    def middle(j, carry):
        r0 = j * block
        for i in range(block // per_row):
            row = code_rows[pl.ds(j * (block // per_row) + i, 1), :]
            hot_s[:, i * HALF : (i + 1) * HALF] = one_hot_columns(row, code_of)
        for h in halves:
            found_s[h : h + hs] = dot(book[...], hot_s[:, h : h + hs]).astype(BF16).T
        pre = []
        for h in halves:
            window = jnp.concatenate([act3[at(r0 + i + h // SIDE, hb), :] for i in range(3)], axis=1)
            pre.append(dot(window, kernel[...]))
        for h, part in zip(halves, pre):
            for t in half_tiles:
                value, slope = gelu_parts(part[t : t + TILE] + bias_first)
                second_s[h + t : h + t + TILE] = value.astype(BF16)
                slope_s[h + t : h + t + TILE] = slope
        mixed = [dot(second_s[h : h + hs], mix[...]) for h in halves]
        for h, part in zip(halves, mixed):
            for t in half_tiles:
                low_s[h + t : h + t + TILE] = (read_x(r0, h + t) + part[t : t + TILE] + bias_mix).astype(BF16)
        latents = [dot(low_s[h : h + hs], project[i]) for i, h in enumerate(halves)]
        total = None
        for t in half_tiles:
            first = pl.ds(r0 + t // SIDE, TILE // SIDE)
            other = pl.ds(r0 + hb + t // SIDE, TILE // SIDE)
            ch = jnp.where(lane, found_s[t : t + TILE].astype(F32), found_s[hs + t : hs + t + TILE].astype(F32))
            q = jnp.where(lane3, qc[first], qc[other]).reshape(TILE, HALF)
            live = q < 0.5 * MARK
            latent = latents[0][t : t + TILE] + latents[1][t : t + TILE] + bias_code
            diff = jnp.where(live, latent - ch, 0.0)
            code_grad = jnp.where(live, q + (2.0 * COMMIT) * diff, 0.0)
            code_s[t : t + TILE] = code_grad.astype(BF16)
            total = add_rows(total, code_grad)
            big = diff.astype(BF16).astype(F32)
            small = diff - big
            turned = pltpu.roll(small, HALF // 2, 1)
            diff_s[t : t + TILE] = jnp.where(lane, big, turned).astype(BF16)
            turned = pltpu.roll(big, HALF // 2, 1)
            diff_s[hs + t : hs + t + TILE] = jnp.where(lane, turned, small).astype(BF16)
        bias_acc[16:24, 0:HALF] += total
        total = None
        blocks_g = [dot(code_s[...], project[i], NT) for i in range(2)]
        for h, part in zip(halves, blocks_g):
            for t in half_tiles:
                block_g[tile_at(r0, h + t), :] = part[t : t + TILE]
                mixed_s[h + t : h + t + TILE] = part[t : t + TILE].astype(BF16)
                total = add_rows(total, part[t : t + TILE])
        bias_acc[8:16] += total
        second_grad = [dot(mixed_s[h : h + hs], mix[...], NT) for h in halves]
        total = None
        for h, part in zip(halves, second_grad):
            for t in half_tiles:
                first_grad = slope_s[h + t : h + t + TILE] * part[t : t + TILE]
                back, ahead = shifted(first_grad)
                grad3[tile_at(r0 + 1, h + t), 0 : 2 * HALF] = ahead
                grad3[tile_at(r0 + 1, h + t), 2 * HALF : 4 * HALF] = first_grad.astype(BF16)
                grad3[tile_at(r0 + 1, h + t), 4 * HALF : 6 * HALF] = back
                total = add_rows(total, first_grad)
        bias_acc[0:8] += total
        book_acc[...] += dot(hot_s[...], diff_s[...])
        mix_acc[...] += dot(second_s[...], mixed_s[...], TN)
        project_acc[...] += jnp.where(lane, dot(low_s[0:hs], code_s[...], TN), dot(low_s[hs:], code_s[...], TN))
        return carry

    def finish(j, carry):
        r0 = j * block
        active = act3[at(r0 + 1), 2 * HALF : 4 * HALF].T
        for i in range(3):
            kernel_acc[:, i * 6 * HALF : (i + 1) * 6 * HALF] += dot(active, grad3[at(r0 + 2 - i), :])
        grads = []
        for h in halves:
            window = jnp.concatenate([grad3[at(r0 + 2 - i + h // SIDE, hb), :] for i in range(3)], axis=1)
            grads.append(dot(window, kernel_t[...]))
        for h, grad in zip(halves, grads):
            for t in half_tiles:
                here = tile_at(r0, h + t)
                out = (block_g[here, :] + slope_x[here, :] * grad[t : t + TILE]).astype(BF16)
                part = pl.ds(r0 + (h + t) // SIDE, TILE // SIDE)
                xc_o[part] = out[:, :HALF].reshape(TILE // SIDE, SIDE, HALF)
                xc_f[part] = out[:, HALF:].reshape(TILE // SIDE, SIDE, HALF)
        return carry

    def opening(j, carry):
        middle(j, carry)
        return activate(j + 2, carry)

    def steady(j, carry):
        finish(j - 2, carry)
        middle(j, carry)
        return activate(j + 2, carry)

    if fused:
        lax.fori_loop(0, jnp.minimum(blocks, 2), opening, 0)
        lax.fori_loop(2, blocks, steady, 0)
        lax.fori_loop(jnp.maximum(blocks - 2, 0), blocks, finish, 0)
    else:
        lax.fori_loop(0, blocks, middle, 0)
        lax.fori_loop(0, blocks, finish, 0)
    leaving = []
    if not final:
        leaving += list(zip((kernel_acc, mix_acc, project_acc, book_acc, bias_acc), sums_out))
        for i, (source, target) in enumerate(leaving):
            leaving[i] = pltpu.make_async_copy(source, target, sems.at[i])
            leaving[i].start()

    out_o, out_f = xo, xf
    if first_step:
        out_o[0:LEAD] = blank
        out_f[0:LEAD] = blank
    else:
        out_o[0:LEAD] = carry_own[...]
        out_f[0:LEAD] = carry_far[...]

    def collect(b, src):
        dst = meta[b] - start + LEAD
        out_o[pl.ds(dst, SIDE)] = xc_o[pl.ds(src, SIDE)]
        out_f[pl.ds(dst, SIDE)] = xc_f[pl.ds(src, SIDE)]
        return src + heights[b] + 1

    lax.fori_loop(low, high, collect, jnp.int32(1))
    size = win_own.shape[0]
    windows = (
        (out_o.at[pl.ds(0, size)], win_own),
        (out_f.at[pl.ds(0, size)], win_far),
        (out_o.at[pl.ds(chunk, LEAD)], next_own),
        (out_f.at[pl.ds(chunk, LEAD)], next_far),
    )
    for i, (source, target) in enumerate(windows):
        leaving.append(pltpu.make_async_copy(source, target, sems.at[5 + i]))
        leaving[-1].start()
    if final:
        sums = (kernel_acc, mix_acc, project_acc, book_acc, bias_acc, decode_acc)
        laid_out += [slope_x.at[pl.ds(0, layout.rows), pl.ds(i * HALF, HALF)] for i in range(2)]
        leaving += gather_grads(plan, layout, place, meta, sums, *laid_out, sems)
    for copy in leaving:
        copy.wait()


class Layout:
    def __init__(self, devices, book_rows, embed):
        self.mix = 9 * 2 * HALF
        self.project = self.mix + 2 * HALF
        self.book = self.project + HALF // 2
        self.bias = self.book + book_rows // 2
        self.decode = self.bias + 8
        used = self.decode + embed + 8
        self.devices = devices
        self.piece = -(-used // (devices * SIDE)) * SIDE
        self.rows = self.piece * devices
        self.half = self.rows // 2
        self.used = used


def lay_out(layout, swap, kernel_acc, mix_acc, project_acc, book_acc, bias_acc, decode_acc, own, far):
    def lanes(value):
        return value[:, :HALF], value[:, HALF:]

    def order(first, second):
        return jnp.where(swap, second, first), jnp.where(swap, first, second)

    row = 0
    for tap in range(9):
        block = kernel_acc[:, tap * 2 * HALF : (tap + 1) * 2 * HALF]
        mine, theirs = lanes(block)
        a, b = order(mine[:HALF], mine[HALF:])
        own[row : row + HALF] = a
        own[row + HALF : row + 2 * HALF] = b
        a, b = order(theirs[:HALF], theirs[HALF:])
        far[row : row + HALF] = a
        far[row + HALF : row + 2 * HALF] = b
        row += 2 * HALF
    row = layout.mix
    for target, part in ((own, mix_acc[:HALF]), (far, mix_acc[HALF:])):
        a, b = order(*lanes(part))
        target[row : row + HALF] = a
        target[row + HALF : row + 2 * HALF] = b
    row = layout.project
    side = HALF // 2
    for target, part in ((own, project_acc[:HALF]), (far, project_acc[HALF:])):
        part = part + pltpu.roll(part, side, 1)
        target[row : row + side] = part.T[:side]
    row = layout.book
    book = book_acc[...]
    book = -2.0 * (book + pltpu.roll(book, side, 1))
    book = book.T[:side]
    for c in range(book.shape[1] // HALF):
        part = book[:, c * HALF : (c + 1) * HALF]
        own[row + c * side : row + (c + 1) * side] = part
        far[row + c * side : row + (c + 1) * side] = part
    row = layout.bias
    sums = [jnp.sum(bias_acc[8 * i : 8 * i + 8], axis=0, keepdims=True) for i in range(3)]
    code = sums[2][:, :HALF]
    code = code + pltpu.roll(code, side, 1)
    which = lax.broadcasted_iota(jnp.int32, (8, HALF), 0)
    for target, first in ((own, 0), (far, HALF)):
        part = jnp.where(which == 0, sums[0][:, first : first + HALF], sums[1][:, first : first + HALF])
        target[row : row + 8] = jnp.where(which == 2, code, jnp.where(which < 2, part, 0.0))
    row = layout.decode
    rest = layout.rows - row
    own[row:] = jnp.zeros((rest, HALF), F32)
    far[row:] = jnp.zeros((rest, HALF), F32)
    if decode_acc is not None:
        own[row : row + decode_acc.shape[0]] = decode_acc[...]


def gather_plain(layout, place, *refs):
    lay_out(layout, place[0] == 1, *refs[:5], None, *refs[5:])


def gather_grads(plan, layout, place, meta, accs, keep_own, keep_far, send, own, far, sems):
    lay_out(layout, place[0] == 1, *accs, own, far)
    base = plan.images + len(plan.chunks) + 1
    over = (meta[base + 4] > plan.covered).astype(F32)
    which = lax.broadcasted_iota(jnp.int32, (8, HALF), 0)
    row = layout.bias
    own[row : row + 8] = jnp.where(which == 3, over, own[row : row + 8])
    half = layout.half
    mine = pl.ds(pl.multiple_of(place[1] * half, SIDE), half)
    other = pl.ds(pl.multiple_of((1 - place[1]) * half, SIDE), half)
    kept = []
    for i, (source, target) in enumerate(((own, keep_own), (far, keep_far))):
        kept.append(pltpu.make_async_copy(source.at[mine, :], target, sems.at[9 + i]))
        kept[-1].start()
    send[0] = own[other, :].astype(BF16)
    send[1] = far[other, :].astype(BF16)
    return kept


def hold(*refs):
    pass


def add_far(keep_far, came, out):
    out[...] = (keep_far[...] + came[1].astype(F32)).astype(BF16)


def add_own(keep_own, came, came_far, out, token):
    token[...] = jnp.zeros_like(token)
    total = keep_own[...] + came[0].astype(F32) + came_far[...].astype(F32)
    out[...] = total.astype(BF16).reshape(out.shape)


def add_pieces(pieces, _, out, token):
    token[...] = jnp.zeros_like(token)
    total = pieces[0].astype(F32)
    for i in range(1, pieces.shape[0]):
        total = total + pieces[i].astype(F32)
    out[...] = jnp.broadcast_to(total.astype(BF16)[None], out.shape)


def write_grads(layout, place, mine, theirs, kernel, first_bias, mix, mix_bias, project, project_bias, book, decode, decode_bias, whole):
    half = layout.half
    whole[pl.ds(pl.multiple_of(place[1] * half, SIDE), half), :] = mine[...].astype(F32)
    whole[pl.ds(pl.multiple_of((1 - place[1]) * half, SIDE), half), :] = theirs[...].astype(F32)
    split_grads(layout, whole, kernel, first_bias, mix, mix_bias, project, project_bias, book, decode, decode_bias)


def split_grads(layout, whole, kernel, first_bias, mix, mix_bias, project, project_bias, book, decode, decode_bias):
    for tap in range(9):
        kernel[tap] = whole[tap * 2 * HALF : (tap + 1) * 2 * HALF]
    row = layout.mix
    mix[:, :HALF] = whole[row : row + HALF]
    mix[:, HALF:] = whole[row + HALF : row + 2 * HALF]
    side = HALF // 2
    for row, target in ((layout.project, project), (layout.book, book)):
        for c in range(target.shape[1] // HALF):
            target[:, c * HALF : (c + 1) * HALF] = whole[row + c * side : row + (c + 1) * side]
    row = layout.bias
    first_bias[...] = whole[row : row + 1]
    mix_bias[...] = whole[row + 1 : row + 2]
    project_bias[...] = whole[row + 2 : row + 3, :side]
    row = layout.decode
    n = decode.shape[0]
    decode[...] = whole[row : row + n]
    decode_bias[...] = whole[row + n : row + n + 1]


def split_again(layout, total, extra, *refs):
    whole = refs[-1]
    whole[...] = total[...].astype(F32) + extra[...]
    split_grads(layout, whole, *refs[:-1])


def restore_rows(plan, n, waits, *refs):
    meta, heights, *refs = refs[waits:]
    own, far, out, token = refs[:n], refs[n : 2 * n], refs[2 * n], refs[2 * n + 1]
    token[...] = jnp.zeros_like(token)
    stage_own, stage_far, sems = refs[2 * n + 2 :]
    copies = []
    for k in range(n):
        size = plan.chunks[k] + (LEAD if k == n - 1 else 0)
        for i, (source, target) in enumerate(((own[k], stage_own), (far[k], stage_far))):
            from_rows = source.at[pl.ds(0, size)]
            copies.append(pltpu.make_async_copy(from_rows, target.at[pl.ds(plan.starts[k], size)], sems.at[i, k]))
            copies[-1].start()
    for copy in copies:
        copy.wait()
    base = plan.images + len(plan.chunks) + 1
    own_row, send_row = meta[base], meta[base + 1]
    first, last = meta[base + 2], meta[base + 3]
    row_of = lax.broadcasted_iota(jnp.int32, (SIDE, 1, 1), 0)

    def own_image(b, carry):
        rows = stage_own[pl.ds(meta[b] + LEAD, SIDE)]
        out[b] = jnp.where(row_of < heights[b], rows, jnp.zeros_like(rows))
        return carry

    def far_image(b, carry):
        rows = stage_far[pl.ds(meta[b] + own_row - send_row + LEAD, SIDE)]
        out[b] = jnp.where(row_of < heights[b], rows, jnp.zeros_like(rows))
        return carry

    lax.fori_loop(first, last, own_image, 0)
    lax.fori_loop(0, first, far_image, 0)
    lax.fori_loop(last, plan.images, far_image, 0)


def trade(value):
    return lax.ppermute(value, "mp", [(0, 1), (1, 0)])


def held(value, *others):
    return pl.pallas_call(
        hold,
        out_shape=shape(value.shape, value.dtype),
        in_specs=[ANY] * (1 + len(others)),
        out_specs=ANY,
        input_output_aliases={0: 0},
        compiler_params=params(60),
        name="hold",
    )(value, *others)


def run_main(plan, layout, k, meta, heights, streams, weights, state, waits=(), ending=()):
    chunk, rows, block = plan.chunks[k], plan.rows[k], plan.block[k]
    last = k >= plan.usual - 1
    final = k == plan.usual - 1
    x_own, x_far, q_own, q_far, codes = streams
    book_rows = weights[-1].shape[1]
    args = [*waits, *ending, meta, heights, x_own, x_far[k], q_own, q_far[k], codes, *weights]
    specs = [ANY] * len(waits) + ([SMEM, VMEM] if final else [])
    specs += [SMEM, SMEM, ANY, ANY, ANY, ANY, VMEM, ANY, ANY] + [VMEM] * (len(weights) - 2)
    alias = {}
    if state is not None:
        args += [x_far[k - 1], q_far[k - 1], *state]
        specs += [ANY, ANY, VMEM, VMEM] + [ANY] * (len(state) - 2)
        if not final:
            for i in range(len(state) - 2):
                alias[len(args) - 5 + i] = 4 + i
    size = chunk + LEAD if last else chunk
    tile = (SIDE, HALF)
    outs = [shape((size,) + tile, BF16)] * 2 + [shape((LEAD,) + tile, BF16)] * 2
    sums = [(2 * HALF, 18 * HALF), (2 * HALF, 2 * HALF), (2 * HALF, HALF), (book_rows, HALF), (24, 2 * HALF)]
    scratch = [pltpu.VMEM(dims, F32) for dims in sums]
    out_specs = [ANY] * 4
    if final:
        outs += [shape((layout.half, HALF), F32)] * 2 + [shape((2, layout.half, HALF), BF16)]
        out_specs += [ANY, ANY, VMEM]
    else:
        outs += [shape(dims, F32) for dims in sums]
        out_specs += [ANY] * 5
    scratch += [pltpu.VMEM((18 * HALF, 2 * HALF), BF16)] * 2 + [pltpu.SemaphoreType.DMA((2,))]
    half = chunk // 2
    spots = block * SIDE
    scratch += [
        pltpu.VMEM((LEAD + chunk + 2 * SIDE,) + tile, BF16),
        pltpu.VMEM((LEAD + chunk + 2 * SIDE,) + tile, BF16),
        pltpu.VMEM((LEAD + half,) + tile, F32),
        pltpu.VMEM((LEAD + half,) + tile, BF16),
        pltpu.VMEM((LEAD + chunk + SIDE,) + tile, F32),
        pltpu.VMEM((rows + 2 * block + SIDE,) + tile, BF16),
        pltpu.VMEM((rows + 2 * block + SIDE,) + tile, BF16),
        pltpu.VMEM((rows + 2 * SIDE,) + tile, F32),
        pltpu.VMEM((-(-(rows * SIDE // HALF + 4) // 8) * 8, HALF), jnp.int32),
        pltpu.VMEM(((rows + 2 * block + 2) * SIDE, 6 * HALF), BF16),
        pltpu.VMEM(((rows + 2 * block) * SIDE, 2 * HALF), F32),
        pltpu.VMEM(((rows + 2) * SIDE, 6 * HALF), BF16),
        pltpu.VMEM((rows * SIDE, 2 * HALF), F32),
        pltpu.VMEM((spots, 2 * HALF), BF16),
        pltpu.VMEM((spots, 2 * HALF), F32),
        pltpu.VMEM((spots, 2 * HALF), BF16),
        pltpu.VMEM((spots, 2 * HALF), BF16),
        pltpu.VMEM((spots // 2, HALF), BF16),
        pltpu.VMEM((book_rows, spots), BF16),
        pltpu.VMEM((spots, HALF), BF16),
        pltpu.VMEM((spots, HALF), BF16),
        pltpu.SemaphoreType.DMA((13,)),
    ]
    spots = chunk * SIDE
    return pl.pallas_call(
        functools.partial(main_step, plan, layout, k, len(waits)),
        out_shape=outs,
        in_specs=specs,
        out_specs=out_specs,
        scratch_shapes=scratch,
        input_output_aliases=alias,
        compiler_params=params(58),
        cost_estimate=cost(60 * 65536 * spots, 8 * MIB, 2 * 256 * spots),
        name=f"main_{k}",
    )(*args)


def local(
    image_latents,
    image_heights,
    code_index,
    kernel_three,
    bias_three,
    weight_mix,
    bias_mix,
    weight_project,
    bias_project,
    codebook,
    weight_decode,
    bias_decode,
    out_grad,
):
    images = image_latents.shape[0]
    plan = Plan(images)
    n = len(plan.chunks)
    tile = (SIDE, HALF)
    where = lax.axis_index("mp").astype(jnp.int32)
    core = lax.rem(lax.axis_index("dp").astype(jnp.int32), 2)
    spot = place = jnp.stack([where, core])

    devices = lax.axis_size("dp")
    across = [(i, i ^ 1) for i in range(devices)]
    kernel_half = lax.dynamic_slice_in_dim(kernel_three, core * HALF, HALF, 1)
    far_kernel = trade(kernel_half)
    far_kernel_other = lax.ppermute(far_kernel, "dp", across)

    packed = pl.pallas_call(
        functools.partial(pack_latents, plan),
        out_shape=[
            shape((meta_size(plan),), jnp.int32),
            shape((LEAD + plan.total,) + tile, BF16),
        ]
        + [shape((c,) + tile, BF16) for c in plan.chunks],
        in_specs=[SMEM, SMEM, HBM, ANY],
        out_specs=[SMEM, ANY] + [ANY] * n,
        scratch_shapes=[
            pltpu.VMEM((images, SIDE) + tile, BF16),
            pltpu.VMEM((plan.packed + SIDE,) + tile, BF16),
            pltpu.SemaphoreType.DMA((8,)),
            pltpu.SemaphoreType.DMA((n + 1,)),
        ],
        compiler_params=params(60),
        cost_estimate=cost(0, 12 * MIB),
        name="pack_latents",
    )(image_heights, place, image_latents, kernel_half)
    meta, x_own, x_send = packed[0], packed[1], packed[2:]

    packed = pl.pallas_call(
        functools.partial(pack_code_grads, plan),
        out_shape=[shape((plan.total // 2,) + tile, F32), shape((2 * HALF + HALF // 2 + SIDE, HALF), BF16)]
        + [shape((c // 2,) + tile, BF16) for c in plan.chunks],
        in_specs=[SMEM] + [HBM] * 6 + [ANY],
        out_specs=[VMEM] * (n + 2),
        scratch_shapes=[
            pltpu.VMEM((images, SIDE) + tile, BF16),
            pltpu.VMEM((plan.packed + SIDE,) + tile, BF16),
            pltpu.SemaphoreType.DMA((8,)),
            pltpu.SemaphoreType.DMA((5,)),
            pltpu.VMEM(weight_decode.shape, BF16),
            pltpu.VMEM(weight_mix.shape, BF16),
            pltpu.VMEM(weight_project.shape[::-1], BF16),
            pltpu.VMEM((1, HALF), BF16),
            pltpu.VMEM((1, HALF), BF16),
        ],
        compiler_params=params(60),
        cost_estimate=cost(2 * 2 * plan.total * SIDE * 256 * 128, 10 * MIB),
        name="pack_code_grads",
    )(meta, out_grad, weight_decode, weight_mix, weight_project.T, bias_three.reshape(1, HALF), bias_mix.reshape(1, HALF), far_kernel)
    q_own, small, q_send = packed[0], packed[1], packed[2:]

    book_rows, embed = codebook.shape
    codebook_t = codebook.T
    far_small = trade(small)
    usual = plan.usual
    x_far, q_far = [], []
    x_far.append(trade(x_send[0]))
    q_far.append(trade(q_send[0]))

    weights = pl.pallas_call(
        prepare_weights,
        out_shape=[
            shape((18 * HALF, 2 * HALF), BF16),
            shape((18 * HALF, 2 * HALF), BF16),
            shape((2 * HALF, 2 * HALF), BF16),
            shape((2, 2 * HALF, HALF), BF16),
            shape((SIDE, 2 * HALF), F32),
            shape((HALF, book_rows), BF16),
        ],
        in_specs=[SMEM, HBM, HBM, HBM] + [VMEM] * 4,
        out_specs=[VMEM] * 6,
        scratch_shapes=[pltpu.VMEM(kernel_three.shape, BF16)] * 2 + [pltpu.SemaphoreType.DMA((3,))],
        compiler_params=params(20),
        cost_estimate=cost(0, 5 * MIB),
        name="prepare_weights",
    )(place, kernel_three, far_kernel, far_kernel_other, small, far_small, bias_project.reshape(1, -1), codebook_t)

    groups = 8
    group = images // groups
    codes = code_index.reshape(images, SIDE * SIDE)
    whole = lambda dims: pl.BlockSpec(dims, lambda g: (0,) * len(dims))
    four = pl.BlockSpec((group, SIDE) + tile, lambda g: (g, 0, 0, 0))
    row = pl.BlockSpec((group, SIDE * SIDE), lambda g: (g, 0))
    def code_sums(first, steps):
        return pl.pallas_call(
            functools.partial(sum_codes, first, group),
            grid=(steps,),
            out_shape=shape((embed + 8, HALF), F32),
            in_specs=[
                SMEM,
                pl.BlockSpec((group, SIDE * SIDE), lambda g: (g + first, 0)),
                pl.BlockSpec((group, SIDE) + tile, lambda g: (g + first, 0, 0, 0)),
                whole((embed, book_rows)),
                ANY,
                ANY,
            ],
            out_specs=whole((embed + 8, HALF)),
            scratch_shapes=[
                pltpu.VMEM((book_rows, group * SIDE * SIDE), BF16),
                pltpu.VMEM((group * SIDE * SIDE, HALF), BF16),
                pltpu.VMEM((book_rows, HALF), F32),
            ],
            compiler_params=params(60),
            cost_estimate=cost(steps * group * 256 * 512 * 256, steps * group * 65536),
            name=f"sum_codes_{first}",
        )(image_heights, codes, out_grad, codebook_t, small, far_kernel)

    def decode(after):
        return pl.pallas_call(
            functools.partial(decode_images, plan, groups),
            grid=(groups,),
            out_shape=[shape((images, SIDE) + tile, BF16), shape((8, HALF), F32)],
            in_specs=[SMEM, row, whole((embed, book_rows)), whole((embed, HALF)), whole((1, HALF)), ANY],
            out_specs=[four, whole((8, HALF))],
            scratch_shapes=[pltpu.VMEM((HALF, book_rows), BF16)],
            compiler_params=params(32),
            cost_estimate=cost(images * 256 * 512 * 256, 5 * MIB),
            name="decode_images",
        )(image_heights, codes, codebook_t, weight_decode, bias_decode.reshape(1, HALF), after)

    decode_acc = code_sums(0, groups)
    for k in range(1, usual):
        x_far.append(trade(held(x_send[k], decode_acc, far_small, x_far[0], q_far[0])))
        q_far.append(trade(held(q_send[k], decode_acc, far_small, x_far[0], q_far[0])))

    layout = Layout(devices, book_rows, embed)
    half, piece, chips = layout.half, layout.piece, devices // 2
    streams = (x_own, x_far, q_own, q_far, codes)
    state = None
    win_own, win_far = [], []
    for k in range(usual):
        waits = win_far[k - 2 : k - 1] if k > 1 else []
        ending = (spot, decode_acc) if k == usual - 1 else ()
        outs = run_main(plan, layout, k, meta, image_heights, streams, weights, state, waits, ending)
        win_own.append(outs[0])
        if k < usual - 1:
            win_far.append(trade(outs[1]))
        state = outs[2:]
    last_window = outs[1]
    carry, (keep_own, keep_far, send) = state[:2], state[2:]

    def restore(own, far, waits=()):
        count = len(own)
        return pl.pallas_call(
            functools.partial(restore_rows, plan, count, len(waits)),
            out_shape=[shape((images, SIDE) + tile, BF16), shape((8, HALF), F32)],
            in_specs=[ANY] * len(waits) + [SMEM, SMEM] + [ANY] * (2 * count),
            out_specs=[VMEM, VMEM],
            scratch_shapes=[
                pltpu.VMEM((plan.total + LEAD + SIDE,) + tile, BF16),
                pltpu.VMEM((plan.total + LEAD + SIDE,) + tile, BF16),
                pltpu.SemaphoreType.DMA((2, count)),
            ],
            compiler_params=params(60),
            cost_estimate=cost(0, 10 * MIB),
            name="restore_rows",
        )(*waits, meta, image_heights, *own, *far)


    def step(body, out, name, *args, waits=()):
        specs = [VMEM] * len(args) + [ANY] * len(waits)
        args = (*args, *waits)
        return pl.pallas_call(
            body,
            out_shape=out,
            in_specs=specs,
            out_specs=[VMEM] * len(out) if isinstance(out, list) else VMEM,
            compiler_params=params(24),
            cost_estimate=cost(0, 2 * MIB),
            name=name,
        )(*args)

    send = held(send, win_far[usual - 2])
    came = lax.ppermute(send, "dp", across)
    win_far.append(trade(last_window))
    far_sums = step(add_far, shape((half, HALF), BF16), "add_far", keep_far, came)
    came_far = trade(far_sums)
    parts = [shape((chips, piece, HALF), BF16), shape((8, HALF), F32)]
    mine, token = step(add_own, parts, "add_own", keep_own, came, came_far)
    decoded, token = decode(token)
    cores = [[i for i in range(devices) if i % 2 == c] for c in range(2)]
    mine = lax.all_to_all(mine, "dp", 0, 0, axis_index_groups=cores, tiled=True)
    mine, token = step(add_pieces, parts, "add_pieces", mine, waits=[token])
    latents_grad, token = restore(win_own, win_far, [token])
    mine = lax.all_to_all(mine, "dp", 0, 0, axis_index_groups=cores, tiled=True)
    mine = held(mine, token).reshape(half, HALF)
    theirs = lax.ppermute(mine, "dp", across)

    grads_out = [
        shape((9, 2 * HALF, HALF), F32),
        shape((1, HALF), F32),
        shape((HALF, 2 * HALF), F32),
        shape((1, HALF), F32),
        shape((embed, HALF), F32),
        shape((1, embed), F32),
        shape((embed, book_rows), F32),
        shape((embed, HALF), F32),
        shape((1, HALF), F32),
    ]
    whole = pltpu.VMEM((layout.rows, HALF), F32)

    def usual_end(latents_grad):
        grads = pl.pallas_call(
            functools.partial(write_grads, layout),
            out_shape=grads_out,
            in_specs=[SMEM, VMEM, VMEM],
            out_specs=[VMEM] * 9,
            scratch_shapes=[whole],
            compiler_params=params(24),
            cost_estimate=cost(0, 4 * MIB),
            name="write_grads",
        )(spot, mine, theirs)
        return (latents_grad, *grads)

    def longer_end(latents_grad):
        last_x, last_q = trade(x_send[usual]), trade(q_send[usual])
        streams = (x_own, x_far + [last_x], q_own, q_far + [last_q], codes)
        outs = run_main(plan, layout, usual, meta, image_heights, streams, weights, carry)
        latents_grad, _ = restore(win_own + [outs[0]], win_far + [trade(outs[1])])
        own, far = pl.pallas_call(
            functools.partial(gather_plain, layout),
            out_shape=[shape((layout.rows, HALF), F32)] * 2,
            in_specs=[SMEM] + [VMEM] * 5,
            out_specs=[VMEM] * 2,
            compiler_params=params(40),
            name="gather_plain",
        )(spot, *outs[4:])
        extra = lax.psum(own + trade(far), "dp")
        first, second = jnp.where(core == 0, mine, theirs), jnp.where(core == 0, theirs, mine)
        grads = pl.pallas_call(
            functools.partial(split_again, layout),
            out_shape=grads_out,
            in_specs=[VMEM, VMEM],
            out_specs=[VMEM] * 9,
            scratch_shapes=[whole],
            compiler_params=params(24),
            name="split_again",
        )(jnp.concatenate([first, second]), extra)
        return (latents_grad, *grads)

    flag = layout.bias + 3
    holder = flag // half
    flags = jnp.where(core == holder, mine[flag - holder * half, 0], theirs[flag - holder * half, 0])
    ends = lax.cond(flags.astype(F32) > 0.5, longer_end, usual_end, latents_grad)
    latents_grad, kernel_grad, first_bias, mix_grad, mix_bias, project_grad, project_bias, book, decode, decode_bias = ends
    return (
        decoded,
        latents_grad,
        kernel_grad,
        first_bias.reshape(HALF),
        mix_grad,
        mix_bias.reshape(HALF),
        project_grad.T,
        project_bias.reshape(embed),
        book.T,
        decode,
        decode_bias.reshape(HALF),
    )


def solution(mesh):
    tile = P("dp", None, None, "mp")
    placed = (
        tile,
        P("dp"),
        P("dp", None, None),
        P(None, None, "mp"),
        P("mp"),
        P("mp", None),
        P("mp"),
        P("mp", None),
        P(),
        P(),
        P(None, "mp"),
        P("mp"),
        tile,
    )
    outs = (
        tile,
        tile,
        P(None, None, "mp"),
        P("mp"),
        P("mp", None),
        P("mp"),
        P("mp", None),
        P(),
        P(),
        P(None, "mp"),
        P("mp"),
    )
    return jax.shard_map(local, mesh=mesh, in_specs=placed, out_specs=outs, check_vma=False)
```

```python
import functools

import jax
import jax.numpy as jnp
from jax import lax
from jax.experimental import pallas as pl
from jax.experimental.pallas import tpu as pltpu
from jax.sharding import PartitionSpec as P

SIDE = 16
HALF = 128
LEAD = 16
BLOCK = 32
TILE = 32
MARK = 1e9
GELU_SCALE = 0.7978845608028654
GELU_CUBE = 0.044715
COMMIT = 0.25
F32 = jnp.float32
BF16 = jnp.bfloat16
ANY = pl.BlockSpec(memory_space=pl.ANY)
SMEM = pl.BlockSpec(memory_space=pltpu.SMEM)
HBM = pl.BlockSpec(memory_space=pltpu.HBM)
VMEM = pl.BlockSpec(memory_space=pltpu.VMEM)
MIB = 1 << 20

NT = (((1,), (1,)), ((), ()))
TN = (((0,), (0,)), ((), ()))
NN = (((1,), (0,)), ((), ()))


def dot(a, b, dims=NN):
    return lax.dot_general(a, b, dims, preferred_element_type=F32)


def one_hot_columns(codes, code_of):
    return jnp.where(code_of == codes.astype(jnp.int16), jnp.bfloat16(1), jnp.bfloat16(0))


def numbers(count, width):
    return lax.broadcasted_iota(jnp.int32, (count, width), 0).astype(jnp.int16)


def shape(dims, kind):
    return jax.ShapeDtypeStruct(dims, kind)


def params(mib):
    return pltpu.CompilerParams(vmem_limit_bytes=mib * MIB)


def cost(flops, moved, slow=0):
    return pl.CostEstimate(flops=flops, bytes_accessed=moved, transcendentals=slow)


class Plan:
    def __init__(self, images):
        self.images = images
        longest = images * SIDE // 2 + SIDE // 2
        part = images // 8
        self.chunks = [18 * part, 29 * part]
        self.usual = len(self.chunks)
        rest = longest - sum(self.chunks)
        self.chunks.append(rest)
        self.starts = [sum(self.chunks[:k]) for k in range(len(self.chunks))]
        self.total = sum(self.chunks)
        self.packed = -(-(LEAD + longest + self.total + LEAD) // SIDE) * SIDE
        self.rows, self.block = [], []
        for k, c in enumerate(self.chunks):
            block = BLOCK if k < self.usual else SIDE
            most = 1 + c + 15 + c // 4 + 1
            self.rows.append(-(-most // block) * block)
            self.block.append(block)
        self.covered = sum(self.chunks[: self.usual])


def meta_size(plan):
    return plan.images + len(plan.chunks) + 1 + 5


def plan_rows(plan, heights, place, meta):
    images = plan.images
    base = images + len(plan.chunks) + 1

    def total_of(b, acc):
        return acc + heights[b]

    total = lax.fori_loop(0, images, total_of, jnp.int32(0))

    def split_of(b, state):
        acc, best, split, cut = state
        acc = acc + heights[b]
        worst = jnp.maximum(acc, total - acc)
        better = worst < best
        return (acc, jnp.where(better, worst, best), jnp.where(better, b + 1, split), jnp.where(better, acc, cut))

    _, _, split, cut = lax.fori_loop(0, images, split_of, (jnp.int32(0), jnp.int32(1 << 20), jnp.int32(0), jnp.int32(0)))
    mine = place[0]
    own_first = jnp.where(mine == 0, 0, split)
    own_last = jnp.where(mine == 0, split, images)
    own_row = jnp.where(mine == 0, 0, cut)
    send_row = jnp.where(mine == 0, cut, 0)
    for k in range(len(plan.chunks) + 1):
        meta[images + k] = own_first
    ends = [plan.starts[k] + plan.chunks[k] for k in range(len(plan.chunks))]

    def place_of(b, acc):
        meta[b] = acc - own_row
        acc = acc + heights[b]
        end = acc - own_row
        inside = jnp.logical_and(b >= own_first, b < own_last)
        step = jnp.int32(0)
        for k in range(len(plan.chunks) - 1):
            step = step + (end > ends[k]).astype(jnp.int32)

        @pl.when(inside)
        def _():
            meta[images + 1 + step] = b + 1

        return acc

    lax.fori_loop(0, images, place_of, jnp.int32(0))
    for k in range(len(plan.chunks)):
        meta[images + k + 1] = jnp.maximum(meta[images + k + 1], meta[images + k])
    meta[base] = own_row
    meta[base + 1] = send_row
    meta[base + 2] = own_first
    meta[base + 3] = own_last
    meta[base + 4] = jnp.maximum(cut, total - cut)


def pack_rows(plan, meta, source, packed, piece, count):
    base = plan.images + len(plan.chunks) + 1

    def one(i, carry):
        b = piece * count + i
        row = meta[b] + meta[base] + LEAD
        packed[pl.ds(row, SIDE)] = source[b]
        return carry

    lax.fori_loop(0, count, one, 0)


def pack_latents(plan, heights, place, x_hbm, _, meta, own, *rest):
    n = len(plan.chunks)
    sends, (x_in, packed, sem_in, sem_out) = rest[:n], rest[n:]
    pieces = 8
    count = plan.images // pieces
    fetch = []
    for p in range(pieces):
        part = pl.ds(p * count, count)
        fetch.append(pltpu.make_async_copy(x_hbm.at[part], x_in.at[part], sem_in.at[p]))
        fetch[-1].start()
    plan_rows(plan, heights, place, meta)
    base = plan.images + n + 1
    for p in range(pieces):
        fetch[p].wait()
        pack_rows(plan, meta, x_in, packed, p, count)
    copies = []
    for k in range(n):
        part = pl.ds(LEAD + meta[base + 1] + plan.starts[k], plan.chunks[k])
        copies.append(pltpu.make_async_copy(packed.at[part], sends[k], sem_out.at[k]))
        copies[-1].start()
    copies.append(pltpu.make_async_copy(packed.at[pl.ds(meta[base], LEAD + plan.total)], own, sem_out.at[n]))
    copies[-1].start()
    for copy in copies:
        copy.wait()


def pack_code_grads(plan, meta, og_hbm, *rest):
    n = len(plan.chunks)
    sources, (own, small), rest = rest[:5], rest[6:8], rest[8:]
    sends, rest = rest[:n], rest[n:]
    og_in, packed, sem_in, sem_small = rest[:4]
    held = rest[4:]
    small_fetch = []
    for i in range(5):
        small_fetch.append(pltpu.make_async_copy(sources[i], held[i], sem_small.at[i]))
        small_fetch[-1].start()
    decode_w, weight_mix, project_t, bias_first, bias_mix = held
    pieces = 8
    count = plan.images // pieces
    fetch = []
    for p in range(pieces):
        part = pl.ds(p * count, count)
        fetch.append(pltpu.make_async_copy(og_hbm.at[part], og_in.at[part], sem_in.at[p]))
        fetch[-1].start()
    base = plan.images + n + 1

    def clear(i, carry):
        packed[pl.ds(i * SIDE, SIDE)] = jnp.zeros((SIDE, SIDE, HALF), BF16)
        return carry

    lax.fori_loop(0, packed.shape[0] // SIDE, clear, 0)
    for copy in small_fetch:
        copy.wait()
    side = HALF // 2
    small[0:HALF] = weight_mix[:, :HALF]
    small[HALF : 2 * HALF] = weight_mix[:, HALF:]
    small[2 * HALF : 2 * HALF + side] = project_t[...]
    which = lax.broadcasted_iota(jnp.int32, (SIDE, HALF), 0)
    first, second = bias_first[...].astype(F32), bias_mix[...].astype(F32)
    first = jnp.where(which == 0, first, jnp.where(which == 1, second, 0.0))
    small[2 * HALF + side : 2 * HALF + side + SIDE] = first.astype(BF16)
    w = decode_w[...]
    blank = jnp.zeros_like(w)
    upper = jnp.concatenate([w, blank], axis=0)
    lower = jnp.concatenate([blank, w], axis=0)
    for p in range(pieces):
        fetch[p].wait()
        pack_rows(plan, meta, og_in, packed, p, count)
    for k in range(n):
        half = plan.chunks[k] // 2
        for which in range(2):
            row = LEAD + meta[base + 1 - which] + plan.starts[k]
            a = packed[pl.ds(row, half)].reshape(half * SIDE, HALF)
            b = packed[pl.ds(row + half, half)].reshape(half * SIDE, HALF)
            both = dot(a, upper, NT) + dot(b, lower, NT)
            both = both.reshape(half, SIDE, HALF)
            if which == 0:
                sends[k][...] = both.astype(BF16)
            else:
                own[pl.ds(plan.starts[k] // 2, half)] = both


def prepare_weights(place, own_hbm, far_hbm, far_other_hbm, small, far_small, bias_code, codebook_t, *refs):
    forward, backward, mix, project, bias, book, kernel, far_kernel, sems = refs
    copies = []
    halves = [pl.ds(pl.multiple_of(at * HALF, HALF), HALF) for at in (place[1], 1 - place[1])]
    pairs = [(own_hbm, kernel)]
    pairs += [(source, far_kernel.at[:, rows, :]) for source, rows in zip((far_hbm, far_other_hbm), halves)]
    for i, (source, target) in enumerate(pairs):
        copies.append(pltpu.make_async_copy(source, target, sems.at[i]))
        copies[-1].start()
    for copy in copies:
        copy.wait()
    first = pl.multiple_of(place[0] * HALF, HALF)
    order = (first, HALF - first)
    for tap in range(9):
        for d, source in enumerate((kernel, far_kernel)):
            for c in range(2):
                tile = source[tap, pl.ds(order[c], HALF), :]
                row = tap * 2 * HALF
                forward[row + c * HALF : row + (c + 1) * HALF, d * HALF : (d + 1) * HALF] = tile
                backward[row + d * HALF : row + (d + 1) * HALF, c * HALF : (c + 1) * HALF] = tile.T
    blank = jnp.zeros((HALF, HALF // 2), BF16)
    for d, source in enumerate((small, far_small)):
        rows = pl.ds(d * HALF, HALF)
        for c in range(2):
            mix[rows, c * HALF : (c + 1) * HALF] = source[pl.ds(order[c], HALF), :]
        part = source[2 * HALF : 2 * HALF + HALF // 2, :].T
        project[0, rows, :] = jnp.concatenate([part, blank], axis=1)
        project[1, rows, :] = jnp.concatenate([blank, part], axis=1)
        bias[0:8, d * HALF : (d + 1) * HALF] = source[2 * HALF + HALF // 2 : 2 * HALF + HALF // 2 + SIDE, :].astype(F32)[0:8]
    code = bias_code[...].astype(F32)
    code = jnp.concatenate([code, code], axis=1)
    bias[8:16, :] = jnp.broadcast_to(jnp.concatenate([code, code], axis=1), (8, 2 * HALF))
    book[...] = jnp.concatenate([codebook_t[...], codebook_t[...]], axis=0)


def sum_codes(first, group, heights, codes, og, codebook_t, _, __, grads, hot, cots, sums):
    step = pl.program_id(0)

    @pl.when(step == 0)
    def _():
        sums[...] = jnp.zeros_like(sums)

    spots = SIDE * SIDE
    code_of = numbers(codebook_t.shape[1], spots)
    spot = lax.broadcasted_iota(jnp.int32, (spots, 1), 0)
    for i in range(group):
        live = heights[(first + step) * group + i] * SIDE
        hot[:, i * spots : (i + 1) * spots] = one_hot_columns(codes[i : i + 1, :], code_of)
        cot = og[i].reshape(spots, HALF).astype(F32)
        cots[i * spots : (i + 1) * spots] = jnp.where(spot < live, cot, 0.0).astype(BF16)
    half = sums.shape[0] // 2
    for h in (0, half):
        sums[h : h + half] += dot(hot[h : h + half], cots[...])

    @pl.when(step == pl.num_programs(0) - 1)
    def _():
        total = sums[...]
        book = codebook_t[...].astype(F32)
        w = lax.dot_general(book, total, NN, precision=lax.Precision.HIGHEST, preferred_element_type=F32)
        bias = jnp.sum(total, axis=0, keepdims=True)
        embed = w.shape[0]
        grads[0:embed] = w
        grads[embed : embed + 8] = jnp.broadcast_to(bias, (8, HALF))


def decode_images(plan, steps, heights, codes, codebook_t, decode_w, decode_b, _, decoded, token, table):
    step = pl.program_id(0)
    token[...] = jnp.zeros_like(token)
    group = plan.images // steps

    @pl.when(step == 0)
    def _():
        full = dot(codebook_t[...], decode_w[...], TN) + decode_b[...].astype(F32)
        table[...] = full.T.astype(BF16)

    spots = SIDE * SIDE
    code_of = numbers(codebook_t.shape[1], spots)
    spot = lax.broadcasted_iota(jnp.int32, (spots, 1), 0)
    for i in range(group):
        live = heights[step * group + i] * SIDE
        out = dot(table[...], one_hot_columns(codes[i : i + 1, :], code_of)).T
        decoded[i] = jnp.where(spot < live, out, 0.0).astype(BF16).reshape(SIDE, SIDE, HALF)


def put_codes(code_rows, codes, b, height, dst):
    spot = lax.broadcasted_iota(jnp.int32, (1, SIDE * SIDE), 1)
    lane = lax.broadcasted_iota(jnp.int32, (1, HALF), 1)
    per_row = HALF // SIDE
    row = jnp.where(spot < height * SIDE, codes[pl.ds(b, 1), :], -1)
    turn = lax.rem(dst, per_row) * SIDE
    upper = pltpu.roll(row[:, :HALF], turn, 1)
    lower = pltpu.roll(row[:, HALF:], turn, 1)
    inside = lane >= turn
    pieces = (jnp.where(inside, upper, -1), jnp.where(inside, lower, upper), jnp.where(inside, -1, lower))
    for i, piece in enumerate(pieces):
        target = pl.ds(dst // per_row + i, 1)
        code_rows[target, :] = jnp.where(piece < 0, code_rows[target, :], piece)


def gelu_parts(v):
    square = v * v
    t = jnp.tanh(v * (GELU_SCALE + (GELU_SCALE * GELU_CUBE) * square))
    half = 0.5 + 0.5 * t
    value = v * half
    slope = half + (value - value * half) * (2.0 * GELU_SCALE + (6.0 * GELU_SCALE * GELU_CUBE) * square)
    return value, slope


def main_step(plan, layout, k, waits, *refs):
    first_step = k == 0
    fresh = k in (0, plan.usual)
    final = k == plan.usual - 1
    refs = list(refs[waits:])

    def take(count):
        got = refs[:count]
        del refs[:count]
        return got

    if final:
        place, decode_acc = take(2)
    meta, heights, x_own, x_far, q_own, q_far, codes = take(7)
    kernel_hbm, kernel_t_hbm, mix, project, bias, book = take(6)
    if not first_step:
        x_past, q_past, carry_own, carry_far = take(4)
    if not fresh:
        past_accs = take(5)
    win_own, win_far, next_own, next_far = take(4)
    if final:
        laid_out = take(3)
    if not final:
        sums_out = take(5)
    kernel_acc, mix_acc, project_acc, book_acc, bias_acc = take(5)
    kernel, kernel_t, weight_sems = take(3)
    xo, xf, qo, qf, qd, xc_o, xc_f, qc, code_rows, act3, slope_x, grad3, block_g = take(13)
    second_s, slope_s, low_s, mixed_s, code_s, hot_s, found_s, diff_s, sems = refs

    chunk, start = plan.chunks[k], plan.starts[k]
    images, rows, block = plan.images, plan.rows[k], plan.block[k]
    half = chunk // 2
    spots = block * SIDE
    low = meta[images + k]
    high = meta[images + k + 1]

    copies = [
        (x_own.at[pl.ds(start, LEAD + chunk)], xo.at[pl.ds(0, LEAD + chunk)]),
        (x_far, xf.at[pl.ds(LEAD, chunk)]),
        (q_own.at[pl.ds(start // 2, half)], qo.at[pl.ds(LEAD, half)]),
        (q_far, qf.at[pl.ds(LEAD, half)]),
    ]
    if not first_step:
        past = plan.chunks[k - 1]
        copies += [
            (x_past.at[pl.ds(past - LEAD, LEAD)], xf.at[pl.ds(0, LEAD)]),
            (q_own.at[pl.ds(start // 2 - LEAD, LEAD)], qo.at[pl.ds(0, LEAD)]),
            (q_past.at[pl.ds(past // 2 - LEAD, LEAD)], qf.at[pl.ds(0, LEAD)]),
        ]
    accs = (mix_acc, project_acc, book_acc, bias_acc, kernel_acc)
    early = len(copies)
    if not fresh:
        copies += list(zip(past_accs[1:] + past_accs[:1], accs))
    weight_copies = []
    for i, (source, target) in enumerate(((kernel_hbm, kernel), (kernel_t_hbm, kernel_t))):
        weight_copies.append(pltpu.make_async_copy(source, target, weight_sems.at[i]))
    started = []
    for i, (source, target) in enumerate(copies):
        started.append(pltpu.make_async_copy(source, target, sems.at[i]))
        started[-1].start()
    for copy in weight_copies:
        copy.start()
    started, later = started[:early], started[early:]

    if fresh:
        for acc in accs:
            acc[...] = jnp.zeros(acc.shape, F32)

    blank = jnp.zeros((SIDE, SIDE, HALF), BF16)
    no_row = jnp.full((SIDE, SIDE, HALF), MARK, F32)
    code_rows[...] = jnp.full(code_rows.shape, -1, jnp.int32)
    for r in range(0, rows + 2 * block, SIDE):
        part = pl.ds(r, SIDE)
        xc_o[part] = blank
        xc_f[part] = blank
        if r < rows:
            qc[part] = no_row
    for copy in started:
        copy.wait()

    lane3 = lax.broadcasted_iota(jnp.int32, (1, SIDE, HALF), 2) < HALF // 2

    def spread(r0, count):
        both = (qo[pl.ds(r0, count)] + qf[pl.ds(r0, count)].astype(F32)).reshape(count * SIDE, HALF)
        turned = pltpu.roll(both, HALF // 2, 1).reshape(count, SIDE, HALF)
        both = both.reshape(count, SIDE, HALF)
        return jnp.where(lane3, both, turned), jnp.where(lane3, turned, both)

    upper, lower = spread(LEAD, half)
    qd[pl.ds(LEAD, half)] = upper
    qd[pl.ds(LEAD + half, half)] = lower
    if not first_step:
        _, lower = spread(0, LEAD)
        qd[0:LEAD] = lower

    per_row = HALF // SIDE

    def put(b, dst):
        src = meta[b] - start + LEAD
        xc_o[pl.ds(dst, SIDE)] = xo[pl.ds(src, SIDE)]
        xc_f[pl.ds(dst, SIDE)] = xf[pl.ds(src, SIDE)]
        qc[pl.ds(dst, SIDE)] = qd[pl.ds(src, SIDE)]
        end = dst + heights[b]
        xc_o[pl.ds(end, SIDE)] = blank
        xc_f[pl.ds(end, SIDE)] = blank
        qc[pl.ds(end, SIDE)] = no_row
        put_codes(code_rows, codes, b, heights[b], dst)
        return end + 1

    used = lax.fori_loop(low, high, put, jnp.int32(1))
    blocks = jnp.where(high > low, (used + (block - 1)) // block, 0)

    column = lax.rem(lax.broadcasted_iota(jnp.int32, (TILE, 1), 0), SIDE)
    not_first = column != 0
    not_last = column != SIDE - 1

    def shifted(value):
        back = jnp.where(not_first, pltpu.roll(value, 1, 0), 0.0)
        ahead = jnp.where(not_last, pltpu.roll(value, TILE - 1, 0), 0.0)
        return back.astype(BF16), ahead.astype(BF16)

    edge = jnp.zeros((SIDE, 3 * 2 * HALF), BF16)
    act3[0:SIDE] = edge
    grad3[0:SIDE] = edge
    beyond = pl.multiple_of((blocks * block + 1) * SIDE, SIDE)
    grad3[pl.ds(beyond, SIDE)] = edge

    tiles = range(0, spots, TILE)

    def read_x(r0, t):
        part = pl.ds(r0 + t // SIDE, TILE // SIDE)
        o = xc_o[part].reshape(TILE, HALF)
        f = xc_f[part].reshape(TILE, HALF)
        return jnp.concatenate([o, f], axis=1).astype(F32)

    def at(row, count=block):
        return pl.ds(pl.multiple_of(row * SIDE, SIDE), count * SIDE)

    def tile_at(row, t):
        return pl.ds(pl.multiple_of(row * SIDE, SIDE) + t, TILE)

    def activate(j, carry):
        r0 = j * block
        for t in tiles:
            value, slope = gelu_parts(read_x(r0, t))
            slope_x[tile_at(r0, t), :] = slope
            back, ahead = shifted(value)
            act3[tile_at(r0 + 1, t), 0 : 2 * HALF] = back
            act3[tile_at(r0 + 1, t), 2 * HALF : 4 * HALF] = value.astype(BF16)
            act3[tile_at(r0 + 1, t), 4 * HALF : 6 * HALF] = ahead
        return carry

    fused = k < plan.usual
    lax.fori_loop(0, 2 if fused else blocks + 1, activate, 0)
    for copy in later:
        copy.wait()
    for copy in weight_copies:
        copy.wait()

    bias_first = bias[0:1, :]
    bias_mix = bias[1:2, :]
    bias_code = bias[8:9, 0:HALF]
    lane = lax.broadcasted_iota(jnp.int32, (1, HALF), 1) < HALF // 2
    hb = block // 2
    hs = hb * SIDE

    def add_rows(total, value):
        for i in range(0, value.shape[0], 8):
            part = value[i : i + 8]
            total = part if total is None else total + part
        return total

    half_tiles = range(0, hs, TILE)
    code_of = numbers(book_acc.shape[0], HALF)
    halves = (0, hs)

    def cut(value):
        return value[:hs], value[hs:]

    def middle(j, carry):
        r0 = j * block
        for i in range(block // per_row):
            row = code_rows[pl.ds(j * (block // per_row) + i, 1), :]
            hot_s[:, i * HALF : (i + 1) * HALF] = one_hot_columns(row, code_of)
        for h in halves:
            found_s[h : h + hs] = dot(book[...], hot_s[:, h : h + hs]).astype(BF16).T
        window = jnp.concatenate([act3[at(r0 + i), :] for i in range(3)], axis=1)
        pre = cut(dot(window, kernel[...]))
        for h, part in zip(halves, pre):
            for t in half_tiles:
                value, slope = gelu_parts(part[t : t + TILE] + bias_first)
                second_s[h + t : h + t + TILE] = value.astype(BF16)
                slope_s[h + t : h + t + TILE] = slope
        mixed = cut(dot(second_s[...], mix[...]))
        for h, part in zip(halves, mixed):
            for t in half_tiles:
                low_s[h + t : h + t + TILE] = (read_x(r0, h + t) + part[t : t + TILE] + bias_mix).astype(BF16)
        latents = [dot(low_s[h : h + hs], project[i]) for i, h in enumerate(halves)]
        total = None
        for t in half_tiles:
            first = pl.ds(r0 + t // SIDE, TILE // SIDE)
            other = pl.ds(r0 + hb + t // SIDE, TILE // SIDE)
            ch = jnp.where(lane, found_s[t : t + TILE].astype(F32), found_s[hs + t : hs + t + TILE].astype(F32))
            q = jnp.where(lane3, qc[first], qc[other]).reshape(TILE, HALF)
            live = q < 0.5 * MARK
            latent = latents[0][t : t + TILE] + latents[1][t : t + TILE] + bias_code
            diff = jnp.where(live, latent - ch, 0.0)
            code_grad = jnp.where(live, q + (2.0 * COMMIT) * diff, 0.0)
            code_s[t : t + TILE] = code_grad.astype(BF16)
            total = add_rows(total, code_grad)
            big = diff.astype(BF16).astype(F32)
            small = diff - big
            turned = pltpu.roll(small, HALF // 2, 1)
            diff_s[t : t + TILE] = jnp.where(lane, big, turned).astype(BF16)
            turned = pltpu.roll(big, HALF // 2, 1)
            diff_s[hs + t : hs + t + TILE] = jnp.where(lane, turned, small).astype(BF16)
        bias_acc[16:24, 0:HALF] += total
        total = None
        blocks_g = [dot(code_s[...], project[i], NT) for i in range(2)]
        for h, part in zip(halves, blocks_g):
            for t in half_tiles:
                block_g[tile_at(r0, h + t), :] = part[t : t + TILE]
                mixed_s[h + t : h + t + TILE] = part[t : t + TILE].astype(BF16)
                total = add_rows(total, part[t : t + TILE])
        bias_acc[8:16] += total
        second_grad = cut(dot(mixed_s[...], mix[...], NT))
        total = None
        for h, part in zip(halves, second_grad):
            for t in half_tiles:
                first_grad = slope_s[h + t : h + t + TILE] * part[t : t + TILE]
                back, ahead = shifted(first_grad)
                grad3[tile_at(r0 + 1, h + t), 0 : 2 * HALF] = ahead
                grad3[tile_at(r0 + 1, h + t), 2 * HALF : 4 * HALF] = first_grad.astype(BF16)
                grad3[tile_at(r0 + 1, h + t), 4 * HALF : 6 * HALF] = back
                total = add_rows(total, first_grad)
        bias_acc[0:8] += total
        book_acc[...] += dot(hot_s[...], diff_s[...])
        mix_acc[...] += dot(second_s[...], mixed_s[...], TN)
        project_acc[...] += jnp.where(lane, dot(low_s[0:hs], code_s[...], TN), dot(low_s[hs:], code_s[...], TN))
        return carry

    def finish(j, carry):
        r0 = j * block
        active = act3[at(r0 + 1), 2 * HALF : 4 * HALF].T
        for i in range(3):
            kernel_acc[:, i * 6 * HALF : (i + 1) * 6 * HALF] += dot(active, grad3[at(r0 + 2 - i), :])
        window = jnp.concatenate([grad3[at(r0 + 2 - i), :] for i in range(3)], axis=1)
        grads = cut(dot(window, kernel_t[...]))
        for h, grad in zip(halves, grads):
            for t in half_tiles:
                here = tile_at(r0, h + t)
                out = (block_g[here, :] + slope_x[here, :] * grad[t : t + TILE]).astype(BF16)
                part = pl.ds(r0 + (h + t) // SIDE, TILE // SIDE)
                xc_o[part] = out[:, :HALF].reshape(TILE // SIDE, SIDE, HALF)
                xc_f[part] = out[:, HALF:].reshape(TILE // SIDE, SIDE, HALF)
        return carry

    def opening(j, carry):
        middle(j, carry)
        return activate(j + 2, carry)

    def steady(j, carry):
        finish(j - 2, carry)
        middle(j, carry)
        return activate(j + 2, carry)

    if fused:
        lax.fori_loop(0, jnp.minimum(blocks, 2), opening, 0)
        lax.fori_loop(2, blocks, steady, 0)
        lax.fori_loop(jnp.maximum(blocks - 2, 0), blocks, finish, 0)
    else:
        lax.fori_loop(0, blocks, middle, 0)
        lax.fori_loop(0, blocks, finish, 0)
    leaving = []
    if not final:
        leaving += list(zip((kernel_acc, mix_acc, project_acc, book_acc, bias_acc), sums_out))
        for i, (source, target) in enumerate(leaving):
            leaving[i] = pltpu.make_async_copy(source, target, sems.at[i])
            leaving[i].start()

    out_o, out_f = xo, xf
    if first_step:
        out_o[0:LEAD] = blank
        out_f[0:LEAD] = blank
    else:
        out_o[0:LEAD] = carry_own[...]
        out_f[0:LEAD] = carry_far[...]

    def collect(b, src):
        dst = meta[b] - start + LEAD
        out_o[pl.ds(dst, SIDE)] = xc_o[pl.ds(src, SIDE)]
        out_f[pl.ds(dst, SIDE)] = xc_f[pl.ds(src, SIDE)]
        return src + heights[b] + 1

    lax.fori_loop(low, high, collect, jnp.int32(1))
    size = win_own.shape[0]
    windows = (
        (out_o.at[pl.ds(0, size)], win_own),
        (out_f.at[pl.ds(0, size)], win_far),
        (out_o.at[pl.ds(chunk, LEAD)], next_own),
        (out_f.at[pl.ds(chunk, LEAD)], next_far),
    )
    for i, (source, target) in enumerate(windows):
        leaving.append(pltpu.make_async_copy(source, target, sems.at[5 + i]))
        leaving[-1].start()
    if final:
        sums = (kernel_acc, mix_acc, project_acc, book_acc, bias_acc, decode_acc)
        laid_out += [slope_x.at[pl.ds(0, layout.rows), pl.ds(i * HALF, HALF)] for i in range(2)]
        leaving += gather_grads(plan, layout, place, meta, sums, *laid_out, sems)
    for copy in leaving:
        copy.wait()


class Layout:
    def __init__(self, devices, book_rows, embed):
        self.mix = 9 * 2 * HALF
        self.project = self.mix + 2 * HALF
        self.book = self.project + HALF // 2
        self.bias = self.book + book_rows // 2
        self.decode = self.bias + 8
        used = self.decode + embed + 8
        self.devices = devices
        self.piece = -(-used // (devices * SIDE)) * SIDE
        self.rows = self.piece * devices
        self.half = self.rows // 2
        self.used = used


def lay_out(layout, swap, kernel_acc, mix_acc, project_acc, book_acc, bias_acc, decode_acc, own, far):
    def lanes(value):
        return value[:, :HALF], value[:, HALF:]

    def order(first, second):
        return jnp.where(swap, second, first), jnp.where(swap, first, second)

    row = 0
    for tap in range(9):
        block = kernel_acc[:, tap * 2 * HALF : (tap + 1) * 2 * HALF]
        mine, theirs = lanes(block)
        a, b = order(mine[:HALF], mine[HALF:])
        own[row : row + HALF] = a
        own[row + HALF : row + 2 * HALF] = b
        a, b = order(theirs[:HALF], theirs[HALF:])
        far[row : row + HALF] = a
        far[row + HALF : row + 2 * HALF] = b
        row += 2 * HALF
    row = layout.mix
    for target, part in ((own, mix_acc[:HALF]), (far, mix_acc[HALF:])):
        a, b = order(*lanes(part))
        target[row : row + HALF] = a
        target[row + HALF : row + 2 * HALF] = b
    row = layout.project
    side = HALF // 2
    for target, part in ((own, project_acc[:HALF]), (far, project_acc[HALF:])):
        part = part + pltpu.roll(part, side, 1)
        target[row : row + side] = part.T[:side]
    row = layout.book
    book = book_acc[...]
    book = -2.0 * (book + pltpu.roll(book, side, 1))
    book = book.T[:side]
    for c in range(book.shape[1] // HALF):
        part = book[:, c * HALF : (c + 1) * HALF]
        own[row + c * side : row + (c + 1) * side] = part
        far[row + c * side : row + (c + 1) * side] = part
    row = layout.bias
    sums = [jnp.sum(bias_acc[8 * i : 8 * i + 8], axis=0, keepdims=True) for i in range(3)]
    code = sums[2][:, :HALF]
    code = code + pltpu.roll(code, side, 1)
    which = lax.broadcasted_iota(jnp.int32, (8, HALF), 0)
    for target, first in ((own, 0), (far, HALF)):
        part = jnp.where(which == 0, sums[0][:, first : first + HALF], sums[1][:, first : first + HALF])
        target[row : row + 8] = jnp.where(which == 2, code, jnp.where(which < 2, part, 0.0))
    row = layout.decode
    rest = layout.rows - row
    own[row:] = jnp.zeros((rest, HALF), F32)
    far[row:] = jnp.zeros((rest, HALF), F32)
    if decode_acc is not None:
        own[row : row + decode_acc.shape[0]] = decode_acc[...]


def gather_plain(layout, place, *refs):
    lay_out(layout, place[0] == 1, *refs[:5], None, *refs[5:])


def gather_grads(plan, layout, place, meta, accs, keep_own, keep_far, send, own, far, sems):
    lay_out(layout, place[0] == 1, *accs, own, far)
    base = plan.images + len(plan.chunks) + 1
    over = (meta[base + 4] > plan.covered).astype(F32)
    which = lax.broadcasted_iota(jnp.int32, (8, HALF), 0)
    row = layout.bias
    own[row : row + 8] = jnp.where(which == 3, over, own[row : row + 8])
    half = layout.half
    mine = pl.ds(pl.multiple_of(place[1] * half, SIDE), half)
    other = pl.ds(pl.multiple_of((1 - place[1]) * half, SIDE), half)
    kept = []
    for i, (source, target) in enumerate(((own, keep_own), (far, keep_far))):
        kept.append(pltpu.make_async_copy(source.at[mine, :], target, sems.at[9 + i]))
        kept[-1].start()
    send[0] = own[other, :].astype(BF16)
    send[1] = far[other, :].astype(BF16)
    return kept


def hold(*refs):
    pass


def add_far(keep_far, came, out):
    out[...] = (keep_far[...] + came[1].astype(F32)).astype(BF16)


def add_own(keep_own, came, came_far, out, token):
    token[...] = jnp.zeros_like(token)
    total = keep_own[...] + came[0].astype(F32) + came_far[...].astype(F32)
    out[...] = total.astype(BF16).reshape(out.shape)


def add_pieces(pieces, _, out, token):
    token[...] = jnp.zeros_like(token)
    total = pieces[0].astype(F32)
    for i in range(1, pieces.shape[0]):
        total = total + pieces[i].astype(F32)
    out[...] = jnp.broadcast_to(total.astype(BF16)[None], out.shape)


def write_grads(layout, place, mine, theirs, kernel, first_bias, mix, mix_bias, project, project_bias, book, decode, decode_bias, whole):
    half = layout.half
    whole[pl.ds(pl.multiple_of(place[1] * half, SIDE), half), :] = mine[...].astype(F32)
    whole[pl.ds(pl.multiple_of((1 - place[1]) * half, SIDE), half), :] = theirs[...].astype(F32)
    split_grads(layout, whole, kernel, first_bias, mix, mix_bias, project, project_bias, book, decode, decode_bias)


def split_grads(layout, whole, kernel, first_bias, mix, mix_bias, project, project_bias, book, decode, decode_bias):
    for tap in range(9):
        kernel[tap] = whole[tap * 2 * HALF : (tap + 1) * 2 * HALF]
    row = layout.mix
    mix[:, :HALF] = whole[row : row + HALF]
    mix[:, HALF:] = whole[row + HALF : row + 2 * HALF]
    side = HALF // 2
    for row, target in ((layout.project, project), (layout.book, book)):
        for c in range(target.shape[1] // HALF):
            target[:, c * HALF : (c + 1) * HALF] = whole[row + c * side : row + (c + 1) * side]
    row = layout.bias
    first_bias[...] = whole[row : row + 1]
    mix_bias[...] = whole[row + 1 : row + 2]
    project_bias[...] = whole[row + 2 : row + 3, :side]
    row = layout.decode
    n = decode.shape[0]
    decode[...] = whole[row : row + n]
    decode_bias[...] = whole[row + n : row + n + 1]


def split_again(layout, total, extra, *refs):
    whole = refs[-1]
    whole[...] = total[...].astype(F32) + extra[...]
    split_grads(layout, whole, *refs[:-1])


def restore_rows(plan, n, waits, *refs):
    meta, heights, *refs = refs[waits:]
    own, far, out, token = refs[:n], refs[n : 2 * n], refs[2 * n], refs[2 * n + 1]
    token[...] = jnp.zeros_like(token)
    stage_own, stage_far, sems = refs[2 * n + 2 :]
    copies = []
    for k in range(n):
        size = plan.chunks[k] + (LEAD if k == n - 1 else 0)
        for i, (source, target) in enumerate(((own[k], stage_own), (far[k], stage_far))):
            from_rows = source.at[pl.ds(0, size)]
            copies.append(pltpu.make_async_copy(from_rows, target.at[pl.ds(plan.starts[k], size)], sems.at[i, k]))
            copies[-1].start()
    for copy in copies:
        copy.wait()
    base = plan.images + len(plan.chunks) + 1
    own_row, send_row = meta[base], meta[base + 1]
    first, last = meta[base + 2], meta[base + 3]
    row_of = lax.broadcasted_iota(jnp.int32, (SIDE, 1, 1), 0)

    def own_image(b, carry):
        rows = stage_own[pl.ds(meta[b] + LEAD, SIDE)]
        out[b] = jnp.where(row_of < heights[b], rows, jnp.zeros_like(rows))
        return carry

    def far_image(b, carry):
        rows = stage_far[pl.ds(meta[b] + own_row - send_row + LEAD, SIDE)]
        out[b] = jnp.where(row_of < heights[b], rows, jnp.zeros_like(rows))
        return carry

    lax.fori_loop(first, last, own_image, 0)
    lax.fori_loop(0, first, far_image, 0)
    lax.fori_loop(last, plan.images, far_image, 0)


def trade(value):
    return lax.ppermute(value, "mp", [(0, 1), (1, 0)])


def held(value, *others):
    return pl.pallas_call(
        hold,
        out_shape=shape(value.shape, value.dtype),
        in_specs=[ANY] * (1 + len(others)),
        out_specs=ANY,
        input_output_aliases={0: 0},
        compiler_params=params(60),
        name="hold",
    )(value, *others)


def run_main(plan, layout, k, meta, heights, streams, weights, state, waits=(), ending=()):
    chunk, rows, block = plan.chunks[k], plan.rows[k], plan.block[k]
    last = k >= plan.usual - 1
    final = k == plan.usual - 1
    x_own, x_far, q_own, q_far, codes = streams
    book_rows = weights[-1].shape[1]
    args = [*waits, *ending, meta, heights, x_own, x_far[k], q_own, q_far[k], codes, *weights]
    specs = [ANY] * len(waits) + ([SMEM, VMEM] if final else [])
    specs += [SMEM, SMEM, ANY, ANY, ANY, ANY, VMEM, ANY, ANY] + [VMEM] * (len(weights) - 2)
    alias = {}
    if state is not None:
        args += [x_far[k - 1], q_far[k - 1], *state]
        specs += [ANY, ANY, VMEM, VMEM] + [ANY] * (len(state) - 2)
        if not final:
            for i in range(len(state) - 2):
                alias[len(args) - 5 + i] = 4 + i
    size = chunk + LEAD if last else chunk
    tile = (SIDE, HALF)
    outs = [shape((size,) + tile, BF16)] * 2 + [shape((LEAD,) + tile, BF16)] * 2
    sums = [(2 * HALF, 18 * HALF), (2 * HALF, 2 * HALF), (2 * HALF, HALF), (book_rows, HALF), (24, 2 * HALF)]
    scratch = [pltpu.VMEM(dims, F32) for dims in sums]
    out_specs = [ANY] * 4
    if final:
        outs += [shape((layout.half, HALF), F32)] * 2 + [shape((2, layout.half, HALF), BF16)]
        out_specs += [ANY, ANY, VMEM]
    else:
        outs += [shape(dims, F32) for dims in sums]
        out_specs += [ANY] * 5
    scratch += [pltpu.VMEM((18 * HALF, 2 * HALF), BF16)] * 2 + [pltpu.SemaphoreType.DMA((2,))]
    half = chunk // 2
    spots = block * SIDE
    scratch += [
        pltpu.VMEM((LEAD + chunk + 2 * SIDE,) + tile, BF16),
        pltpu.VMEM((LEAD + chunk + 2 * SIDE,) + tile, BF16),
        pltpu.VMEM((LEAD + half,) + tile, F32),
        pltpu.VMEM((LEAD + half,) + tile, BF16),
        pltpu.VMEM((LEAD + chunk + SIDE,) + tile, F32),
        pltpu.VMEM((rows + 2 * block + SIDE,) + tile, BF16),
        pltpu.VMEM((rows + 2 * block + SIDE,) + tile, BF16),
        pltpu.VMEM((rows + 2 * SIDE,) + tile, F32),
        pltpu.VMEM((-(-(rows * SIDE // HALF + 4) // 8) * 8, HALF), jnp.int32),
        pltpu.VMEM(((rows + 2 * block + 2) * SIDE, 6 * HALF), BF16),
        pltpu.VMEM(((rows + 2 * block) * SIDE, 2 * HALF), F32),
        pltpu.VMEM(((rows + 2) * SIDE, 6 * HALF), BF16),
        pltpu.VMEM((rows * SIDE, 2 * HALF), F32),
        pltpu.VMEM((spots, 2 * HALF), BF16),
        pltpu.VMEM((spots, 2 * HALF), F32),
        pltpu.VMEM((spots, 2 * HALF), BF16),
        pltpu.VMEM((spots, 2 * HALF), BF16),
        pltpu.VMEM((spots // 2, HALF), BF16),
        pltpu.VMEM((book_rows, spots), BF16),
        pltpu.VMEM((spots, HALF), BF16),
        pltpu.VMEM((spots, HALF), BF16),
        pltpu.SemaphoreType.DMA((13,)),
    ]
    spots = chunk * SIDE
    return pl.pallas_call(
        functools.partial(main_step, plan, layout, k, len(waits)),
        out_shape=outs,
        in_specs=specs,
        out_specs=out_specs,
        scratch_shapes=scratch,
        input_output_aliases=alias,
        compiler_params=params(58),
        cost_estimate=cost(60 * 65536 * spots, 8 * MIB, 2 * 256 * spots),
        name=f"main_{k}",
    )(*args)


def local(
    image_latents,
    image_heights,
    code_index,
    kernel_three,
    bias_three,
    weight_mix,
    bias_mix,
    weight_project,
    bias_project,
    codebook,
    weight_decode,
    bias_decode,
    out_grad,
):
    images = image_latents.shape[0]
    plan = Plan(images)
    n = len(plan.chunks)
    tile = (SIDE, HALF)
    where = lax.axis_index("mp").astype(jnp.int32)
    core = lax.rem(lax.axis_index("dp").astype(jnp.int32), 2)
    spot = place = jnp.stack([where, core])

    devices = lax.axis_size("dp")
    across = [(i, i ^ 1) for i in range(devices)]
    kernel_half = lax.dynamic_slice_in_dim(kernel_three, core * HALF, HALF, 1)
    far_kernel = trade(kernel_half)
    far_kernel_other = lax.ppermute(far_kernel, "dp", across)

    packed = pl.pallas_call(
        functools.partial(pack_latents, plan),
        out_shape=[
            shape((meta_size(plan),), jnp.int32),
            shape((LEAD + plan.total,) + tile, BF16),
        ]
        + [shape((c,) + tile, BF16) for c in plan.chunks],
        in_specs=[SMEM, SMEM, HBM, ANY],
        out_specs=[SMEM, ANY] + [ANY] * n,
        scratch_shapes=[
            pltpu.VMEM((images, SIDE) + tile, BF16),
            pltpu.VMEM((plan.packed + SIDE,) + tile, BF16),
            pltpu.SemaphoreType.DMA((8,)),
            pltpu.SemaphoreType.DMA((n + 1,)),
        ],
        compiler_params=params(60),
        cost_estimate=cost(0, 12 * MIB),
        name="pack_latents",
    )(image_heights, place, image_latents, kernel_half)
    meta, x_own, x_send = packed[0], packed[1], packed[2:]

    packed = pl.pallas_call(
        functools.partial(pack_code_grads, plan),
        out_shape=[shape((plan.total // 2,) + tile, F32), shape((2 * HALF + HALF // 2 + SIDE, HALF), BF16)]
        + [shape((c // 2,) + tile, BF16) for c in plan.chunks],
        in_specs=[SMEM] + [HBM] * 6 + [ANY],
        out_specs=[VMEM] * (n + 2),
        scratch_shapes=[
            pltpu.VMEM((images, SIDE) + tile, BF16),
            pltpu.VMEM((plan.packed + SIDE,) + tile, BF16),
            pltpu.SemaphoreType.DMA((8,)),
            pltpu.SemaphoreType.DMA((5,)),
            pltpu.VMEM(weight_decode.shape, BF16),
            pltpu.VMEM(weight_mix.shape, BF16),
            pltpu.VMEM(weight_project.shape[::-1], BF16),
            pltpu.VMEM((1, HALF), BF16),
            pltpu.VMEM((1, HALF), BF16),
        ],
        compiler_params=params(60),
        cost_estimate=cost(2 * 2 * plan.total * SIDE * 256 * 128, 10 * MIB),
        name="pack_code_grads",
    )(meta, out_grad, weight_decode, weight_mix, weight_project.T, bias_three.reshape(1, HALF), bias_mix.reshape(1, HALF), far_kernel)
    q_own, small, q_send = packed[0], packed[1], packed[2:]

    book_rows, embed = codebook.shape
    codebook_t = codebook.T
    far_small = trade(small)
    usual = plan.usual
    x_far, q_far = [], []
    x_far.append(trade(x_send[0]))
    q_far.append(trade(q_send[0]))

    weights = pl.pallas_call(
        prepare_weights,
        out_shape=[
            shape((18 * HALF, 2 * HALF), BF16),
            shape((18 * HALF, 2 * HALF), BF16),
            shape((2 * HALF, 2 * HALF), BF16),
            shape((2, 2 * HALF, HALF), BF16),
            shape((SIDE, 2 * HALF), F32),
            shape((HALF, book_rows), BF16),
        ],
        in_specs=[SMEM, HBM, HBM, HBM] + [VMEM] * 4,
        out_specs=[VMEM] * 6,
        scratch_shapes=[pltpu.VMEM(kernel_three.shape, BF16)] * 2 + [pltpu.SemaphoreType.DMA((3,))],
        compiler_params=params(20),
        cost_estimate=cost(0, 5 * MIB),
        name="prepare_weights",
    )(place, kernel_three, far_kernel, far_kernel_other, small, far_small, bias_project.reshape(1, -1), codebook_t)

    groups = 8
    group = images // groups
    codes = code_index.reshape(images, SIDE * SIDE)
    whole = lambda dims: pl.BlockSpec(dims, lambda g: (0,) * len(dims))
    four = pl.BlockSpec((group, SIDE) + tile, lambda g: (g, 0, 0, 0))
    row = pl.BlockSpec((group, SIDE * SIDE), lambda g: (g, 0))
    def code_sums(first, steps):
        return pl.pallas_call(
            functools.partial(sum_codes, first, group),
            grid=(steps,),
            out_shape=shape((embed + 8, HALF), F32),
            in_specs=[
                SMEM,
                pl.BlockSpec((group, SIDE * SIDE), lambda g: (g + first, 0)),
                pl.BlockSpec((group, SIDE) + tile, lambda g: (g + first, 0, 0, 0)),
                whole((embed, book_rows)),
                ANY,
                ANY,
            ],
            out_specs=whole((embed + 8, HALF)),
            scratch_shapes=[
                pltpu.VMEM((book_rows, group * SIDE * SIDE), BF16),
                pltpu.VMEM((group * SIDE * SIDE, HALF), BF16),
                pltpu.VMEM((book_rows, HALF), F32),
            ],
            compiler_params=params(60),
            cost_estimate=cost(steps * group * 256 * 512 * 256, steps * group * 65536),
            name=f"sum_codes_{first}",
        )(image_heights, codes, out_grad, codebook_t, small, far_kernel)

    def decode(after):
        return pl.pallas_call(
            functools.partial(decode_images, plan, groups),
            grid=(groups,),
            out_shape=[shape((images, SIDE) + tile, BF16), shape((8, HALF), F32)],
            in_specs=[SMEM, row, whole((embed, book_rows)), whole((embed, HALF)), whole((1, HALF)), ANY],
            out_specs=[four, whole((8, HALF))],
            scratch_shapes=[pltpu.VMEM((HALF, book_rows), BF16)],
            compiler_params=params(32),
            cost_estimate=cost(images * 256 * 512 * 256, 5 * MIB),
            name="decode_images",
        )(image_heights, codes, codebook_t, weight_decode, bias_decode.reshape(1, HALF), after)

    decode_acc = code_sums(0, groups)
    for k in range(1, usual):
        x_far.append(trade(held(x_send[k], decode_acc, far_small, x_far[0], q_far[0])))
        q_far.append(trade(held(q_send[k], decode_acc, far_small, x_far[0], q_far[0])))

    layout = Layout(devices, book_rows, embed)
    half, piece, chips = layout.half, layout.piece, devices // 2
    streams = (x_own, x_far, q_own, q_far, codes)
    state = None
    win_own, win_far = [], []
    for k in range(usual):
        waits = win_far[k - 2 : k - 1] if k > 1 else []
        ending = (spot, decode_acc) if k == usual - 1 else ()
        outs = run_main(plan, layout, k, meta, image_heights, streams, weights, state, waits, ending)
        win_own.append(outs[0])
        if k < usual - 1:
            win_far.append(trade(outs[1]))
        state = outs[2:]
    last_window = outs[1]
    carry, (keep_own, keep_far, send) = state[:2], state[2:]

    def restore(own, far, waits=()):
        count = len(own)
        return pl.pallas_call(
            functools.partial(restore_rows, plan, count, len(waits)),
            out_shape=[shape((images, SIDE) + tile, BF16), shape((8, HALF), F32)],
            in_specs=[ANY] * len(waits) + [SMEM, SMEM] + [ANY] * (2 * count),
            out_specs=[VMEM, VMEM],
            scratch_shapes=[
                pltpu.VMEM((plan.total + LEAD + SIDE,) + tile, BF16),
                pltpu.VMEM((plan.total + LEAD + SIDE,) + tile, BF16),
                pltpu.SemaphoreType.DMA((2, count)),
            ],
            compiler_params=params(60),
            cost_estimate=cost(0, 10 * MIB),
            name="restore_rows",
        )(*waits, meta, image_heights, *own, *far)


    def step(body, out, name, *args, waits=()):
        specs = [VMEM] * len(args) + [ANY] * len(waits)
        args = (*args, *waits)
        return pl.pallas_call(
            body,
            out_shape=out,
            in_specs=specs,
            out_specs=[VMEM] * len(out) if isinstance(out, list) else VMEM,
            compiler_params=params(24),
            cost_estimate=cost(0, 2 * MIB),
            name=name,
        )(*args)

    send = held(send, win_far[usual - 2])
    came = lax.ppermute(send, "dp", across)
    win_far.append(trade(last_window))
    far_sums = step(add_far, shape((half, HALF), BF16), "add_far", keep_far, came)
    came_far = trade(far_sums)
    parts = [shape((chips, piece, HALF), BF16), shape((8, HALF), F32)]
    mine, token = step(add_own, parts, "add_own", keep_own, came, came_far)
    decoded, token = decode(token)
    cores = [[i for i in range(devices) if i % 2 == c] for c in range(2)]
    mine = lax.all_to_all(mine, "dp", 0, 0, axis_index_groups=cores, tiled=True)
    mine, token = step(add_pieces, parts, "add_pieces", mine, waits=[token])
    latents_grad, token = restore(win_own, win_far, [token])
    mine = lax.all_to_all(mine, "dp", 0, 0, axis_index_groups=cores, tiled=True)
    mine = held(mine, token).reshape(half, HALF)
    theirs = lax.ppermute(mine, "dp", across)

    grads_out = [
        shape((9, 2 * HALF, HALF), F32),
        shape((1, HALF), F32),
        shape((HALF, 2 * HALF), F32),
        shape((1, HALF), F32),
        shape((embed, HALF), F32),
        shape((1, embed), F32),
        shape((embed, book_rows), F32),
        shape((embed, HALF), F32),
        shape((1, HALF), F32),
    ]
    whole = pltpu.VMEM((layout.rows, HALF), F32)

    def usual_end(latents_grad):
        grads = pl.pallas_call(
            functools.partial(write_grads, layout),
            out_shape=grads_out,
            in_specs=[SMEM, VMEM, VMEM],
            out_specs=[VMEM] * 9,
            scratch_shapes=[whole],
            compiler_params=params(24),
            cost_estimate=cost(0, 4 * MIB),
            name="write_grads",
        )(spot, mine, theirs)
        return (latents_grad, *grads)

    def longer_end(latents_grad):
        last_x, last_q = trade(x_send[usual]), trade(q_send[usual])
        streams = (x_own, x_far + [last_x], q_own, q_far + [last_q], codes)
        outs = run_main(plan, layout, usual, meta, image_heights, streams, weights, carry)
        latents_grad, _ = restore(win_own + [outs[0]], win_far + [trade(outs[1])])
        own, far = pl.pallas_call(
            functools.partial(gather_plain, layout),
            out_shape=[shape((layout.rows, HALF), F32)] * 2,
            in_specs=[SMEM] + [VMEM] * 5,
            out_specs=[VMEM] * 2,
            compiler_params=params(40),
            name="gather_plain",
        )(spot, *outs[4:])
        extra = lax.psum(own + trade(far), "dp")
        first, second = jnp.where(core == 0, mine, theirs), jnp.where(core == 0, theirs, mine)
        grads = pl.pallas_call(
            functools.partial(split_again, layout),
            out_shape=grads_out,
            in_specs=[VMEM, VMEM],
            out_specs=[VMEM] * 9,
            scratch_shapes=[whole],
            compiler_params=params(24),
            name="split_again",
        )(jnp.concatenate([first, second]), extra)
        return (latents_grad, *grads)

    flag = layout.bias + 3
    holder = flag // half
    flags = jnp.where(core == holder, mine[flag - holder * half, 0], theirs[flag - holder * half, 0])
    ends = lax.cond(flags.astype(F32) > 0.5, longer_end, usual_end, latents_grad)
    latents_grad, kernel_grad, first_bias, mix_grad, mix_bias, project_grad, project_bias, book, decode, decode_bias = ends
    return (
        decoded,
        latents_grad,
        kernel_grad,
        first_bias.reshape(HALF),
        mix_grad,
        mix_bias.reshape(HALF),
        project_grad.T,
        project_bias.reshape(embed),
        book.T,
        decode,
        decode_bias.reshape(HALF),
    )


def solution(mesh):
    tile = P("dp", None, None, "mp")
    placed = (
        tile,
        P("dp"),
        P("dp", None, None),
        P(None, None, "mp"),
        P("mp"),
        P("mp", None),
        P("mp"),
        P("mp", None),
        P(),
        P(),
        P(None, "mp"),
        P("mp"),
        tile,
    )
    outs = (
        tile,
        tile,
        P(None, None, "mp"),
        P("mp"),
        P("mp", None),
        P("mp"),
        P("mp", None),
        P(),
        P(),
        P(None, "mp"),
        P("mp"),
    )
    return jax.shard_map(local, mesh=mesh, in_specs=placed, out_specs=outs, check_vma=False)
```

```python
import functools

import jax
import jax.numpy as jnp
from jax import lax
from jax.experimental import pallas as pl
from jax.experimental.pallas import tpu as pltpu
from jax.sharding import PartitionSpec as P

SIDE = 16
HALF = 128
LEAD = 16
BLOCK = 32
TILE = 32
MARK = 1e9
GELU_SCALE = 0.7978845608028654
GELU_CUBE = 0.044715
COMMIT = 0.25
F32 = jnp.float32
BF16 = jnp.bfloat16
ANY = pl.BlockSpec(memory_space=pl.ANY)
SMEM = pl.BlockSpec(memory_space=pltpu.SMEM)
HBM = pl.BlockSpec(memory_space=pltpu.HBM)
VMEM = pl.BlockSpec(memory_space=pltpu.VMEM)
MIB = 1 << 20

NT = (((1,), (1,)), ((), ()))
TN = (((0,), (0,)), ((), ()))
NN = (((1,), (0,)), ((), ()))


def dot(a, b, dims=NN):
    return lax.dot_general(a, b, dims, preferred_element_type=F32)


def one_hot_columns(codes, code_of):
    return jnp.where(code_of == codes.astype(jnp.int16), jnp.bfloat16(1), jnp.bfloat16(0))


def numbers(count, width):
    return lax.broadcasted_iota(jnp.int32, (count, width), 0).astype(jnp.int16)


def shape(dims, kind):
    return jax.ShapeDtypeStruct(dims, kind)


def params(mib):
    return pltpu.CompilerParams(vmem_limit_bytes=mib * MIB)


def cost(flops, moved, slow=0):
    return pl.CostEstimate(flops=flops, bytes_accessed=moved, transcendentals=slow)


class Plan:
    def __init__(self, images):
        self.images = images
        longest = images * SIDE // 2 + SIDE // 2
        part = images // 8
        self.chunks = [18 * part, 29 * part]
        self.usual = len(self.chunks)
        rest = longest - sum(self.chunks)
        self.chunks.append(rest)
        self.starts = [sum(self.chunks[:k]) for k in range(len(self.chunks))]
        self.total = sum(self.chunks)
        self.packed = -(-(LEAD + longest + self.total + LEAD) // SIDE) * SIDE
        self.rows, self.block = [], []
        for k, c in enumerate(self.chunks):
            block = BLOCK if k < self.usual else SIDE
            most = 1 + c + 15 + c // 4 + 1
            self.rows.append(-(-most // block) * block)
            self.block.append(block)
        self.covered = sum(self.chunks[: self.usual])


def meta_size(plan):
    return plan.images + len(plan.chunks) + 1 + 5


def plan_rows(plan, heights, place, meta):
    images = plan.images
    base = images + len(plan.chunks) + 1

    def total_of(b, acc):
        return acc + heights[b]

    total = lax.fori_loop(0, images, total_of, jnp.int32(0))

    def split_of(b, state):
        acc, best, split, cut = state
        acc = acc + heights[b]
        worst = jnp.maximum(acc, total - acc)
        better = worst < best
        return (acc, jnp.where(better, worst, best), jnp.where(better, b + 1, split), jnp.where(better, acc, cut))

    _, _, split, cut = lax.fori_loop(0, images, split_of, (jnp.int32(0), jnp.int32(1 << 20), jnp.int32(0), jnp.int32(0)))
    mine = place[0]
    own_first = jnp.where(mine == 0, 0, split)
    own_last = jnp.where(mine == 0, split, images)
    own_row = jnp.where(mine == 0, 0, cut)
    send_row = jnp.where(mine == 0, cut, 0)
    for k in range(len(plan.chunks) + 1):
        meta[images + k] = own_first
    ends = [plan.starts[k] + plan.chunks[k] for k in range(len(plan.chunks))]

    def place_of(b, acc):
        meta[b] = acc - own_row
        acc = acc + heights[b]
        end = acc - own_row
        inside = jnp.logical_and(b >= own_first, b < own_last)
        step = jnp.int32(0)
        for k in range(len(plan.chunks) - 1):
            step = step + (end > ends[k]).astype(jnp.int32)

        @pl.when(inside)
        def _():
            meta[images + 1 + step] = b + 1

        return acc

    lax.fori_loop(0, images, place_of, jnp.int32(0))
    for k in range(len(plan.chunks)):
        meta[images + k + 1] = jnp.maximum(meta[images + k + 1], meta[images + k])
    meta[base] = own_row
    meta[base + 1] = send_row
    meta[base + 2] = own_first
    meta[base + 3] = own_last
    meta[base + 4] = jnp.maximum(cut, total - cut)


def pack_rows(plan, meta, source, packed, piece, count):
    base = plan.images + len(plan.chunks) + 1

    def one(i, carry):
        b = piece * count + i
        row = meta[b] + meta[base] + LEAD
        packed[pl.ds(row, SIDE)] = source[b]
        return carry

    lax.fori_loop(0, count, one, 0)


def pack_latents(plan, heights, place, x_hbm, _, meta, own, *rest):
    n = len(plan.chunks)
    sends, (x_in, packed, sem_in, sem_out) = rest[:n], rest[n:]
    pieces = 8
    count = plan.images // pieces
    fetch = []
    for p in range(pieces):
        part = pl.ds(p * count, count)
        fetch.append(pltpu.make_async_copy(x_hbm.at[part], x_in.at[part], sem_in.at[p]))
        fetch[-1].start()
    plan_rows(plan, heights, place, meta)
    base = plan.images + n + 1
    for p in range(pieces):
        fetch[p].wait()
        pack_rows(plan, meta, x_in, packed, p, count)
    copies = []
    for k in range(n):
        part = pl.ds(LEAD + meta[base + 1] + plan.starts[k], plan.chunks[k])
        copies.append(pltpu.make_async_copy(packed.at[part], sends[k], sem_out.at[k]))
        copies[-1].start()
    copies.append(pltpu.make_async_copy(packed.at[pl.ds(meta[base], LEAD + plan.total)], own, sem_out.at[n]))
    copies[-1].start()
    for copy in copies:
        copy.wait()


def pack_code_grads(plan, meta, og_hbm, *rest):
    n = len(plan.chunks)
    sources, (own, small), rest = rest[:5], rest[6:8], rest[8:]
    sends, rest = rest[:n], rest[n:]
    og_in, packed, sem_in, sem_small = rest[:4]
    held = rest[4:]
    small_fetch = []
    for i in range(5):
        small_fetch.append(pltpu.make_async_copy(sources[i], held[i], sem_small.at[i]))
        small_fetch[-1].start()
    decode_w, weight_mix, project_t, bias_first, bias_mix = held
    pieces = 8
    count = plan.images // pieces
    fetch = []
    for p in range(pieces):
        part = pl.ds(p * count, count)
        fetch.append(pltpu.make_async_copy(og_hbm.at[part], og_in.at[part], sem_in.at[p]))
        fetch[-1].start()
    base = plan.images + n + 1

    def clear(i, carry):
        packed[pl.ds(i * SIDE, SIDE)] = jnp.zeros((SIDE, SIDE, HALF), BF16)
        return carry

    lax.fori_loop(0, packed.shape[0] // SIDE, clear, 0)
    for copy in small_fetch:
        copy.wait()
    side = HALF // 2
    small[0:HALF] = weight_mix[:, :HALF]
    small[HALF : 2 * HALF] = weight_mix[:, HALF:]
    small[2 * HALF : 2 * HALF + side] = project_t[...]
    which = lax.broadcasted_iota(jnp.int32, (SIDE, HALF), 0)
    first, second = bias_first[...].astype(F32), bias_mix[...].astype(F32)
    first = jnp.where(which == 0, first, jnp.where(which == 1, second, 0.0))
    small[2 * HALF + side : 2 * HALF + side + SIDE] = first.astype(BF16)
    w = decode_w[...]
    blank = jnp.zeros_like(w)
    upper = jnp.concatenate([w, blank], axis=0)
    lower = jnp.concatenate([blank, w], axis=0)
    for p in range(pieces):
        fetch[p].wait()
        pack_rows(plan, meta, og_in, packed, p, count)
    for k in range(n):
        half = plan.chunks[k] // 2
        for which in range(2):
            row = LEAD + meta[base + 1 - which] + plan.starts[k]
            a = packed[pl.ds(row, half)].reshape(half * SIDE, HALF)
            b = packed[pl.ds(row + half, half)].reshape(half * SIDE, HALF)
            both = dot(a, upper, NT) + dot(b, lower, NT)
            both = both.reshape(half, SIDE, HALF)
            if which == 0:
                sends[k][...] = both.astype(BF16)
            else:
                own[pl.ds(plan.starts[k] // 2, half)] = both


def prepare_weights(place, own_hbm, far_hbm, far_other_hbm, small, far_small, bias_code, codebook_t, *refs):
    forward, backward, mix, project, bias, book, kernel, far_kernel, sems = refs
    copies = []
    halves = [pl.ds(pl.multiple_of(at * HALF, HALF), HALF) for at in (place[1], 1 - place[1])]
    pairs = [(own_hbm, kernel)]
    pairs += [(source, far_kernel.at[:, rows, :]) for source, rows in zip((far_hbm, far_other_hbm), halves)]
    for i, (source, target) in enumerate(pairs):
        copies.append(pltpu.make_async_copy(source, target, sems.at[i]))
        copies[-1].start()
    for copy in copies:
        copy.wait()
    first = pl.multiple_of(place[0] * HALF, HALF)
    order = (first, HALF - first)
    for tap in range(9):
        for d, source in enumerate((kernel, far_kernel)):
            for c in range(2):
                tile = source[tap, pl.ds(order[c], HALF), :]
                row = tap * 2 * HALF
                forward[row + c * HALF : row + (c + 1) * HALF, d * HALF : (d + 1) * HALF] = tile
                backward[row + d * HALF : row + (d + 1) * HALF, c * HALF : (c + 1) * HALF] = tile.T
    blank = jnp.zeros((HALF, HALF // 2), BF16)
    for d, source in enumerate((small, far_small)):
        rows = pl.ds(d * HALF, HALF)
        for c in range(2):
            mix[rows, c * HALF : (c + 1) * HALF] = source[pl.ds(order[c], HALF), :]
        part = source[2 * HALF : 2 * HALF + HALF // 2, :].T
        project[0, rows, :] = jnp.concatenate([part, blank], axis=1)
        project[1, rows, :] = jnp.concatenate([blank, part], axis=1)
        bias[0:8, d * HALF : (d + 1) * HALF] = source[2 * HALF + HALF // 2 : 2 * HALF + HALF // 2 + SIDE, :].astype(F32)[0:8]
    code = bias_code[...].astype(F32)
    code = jnp.concatenate([code, code], axis=1)
    bias[8:16, :] = jnp.broadcast_to(jnp.concatenate([code, code], axis=1), (8, 2 * HALF))
    book[...] = jnp.concatenate([codebook_t[...], codebook_t[...]], axis=0)


def sum_codes(first, group, heights, codes, og, codebook_t, _, __, grads, hot, cots, sums):
    step = pl.program_id(0)

    @pl.when(step == 0)
    def _():
        sums[...] = jnp.zeros_like(sums)

    spots = SIDE * SIDE
    code_of = numbers(codebook_t.shape[1], spots)
    spot = lax.broadcasted_iota(jnp.int32, (spots, 1), 0)
    for i in range(group):
        live = heights[(first + step) * group + i] * SIDE
        hot[:, i * spots : (i + 1) * spots] = one_hot_columns(codes[i : i + 1, :], code_of)
        cot = og[i].reshape(spots, HALF).astype(F32)
        cots[i * spots : (i + 1) * spots] = jnp.where(spot < live, cot, 0.0).astype(BF16)
    half = sums.shape[0] // 2
    for h in (0, half):
        sums[h : h + half] += dot(hot[h : h + half], cots[...])

    @pl.when(step == pl.num_programs(0) - 1)
    def _():
        total = sums[...]
        book = codebook_t[...].astype(F32)
        w = lax.dot_general(book, total, NN, precision=lax.Precision.HIGHEST, preferred_element_type=F32)
        bias = jnp.sum(total, axis=0, keepdims=True)
        embed = w.shape[0]
        grads[0:embed] = w
        grads[embed : embed + 8] = jnp.broadcast_to(bias, (8, HALF))


def decode_images(plan, steps, heights, codes, codebook_t, decode_w, decode_b, _, decoded, token, table):
    step = pl.program_id(0)
    token[...] = jnp.zeros_like(token)
    group = plan.images // steps

    @pl.when(step == 0)
    def _():
        full = dot(codebook_t[...], decode_w[...], TN) + decode_b[...].astype(F32)
        table[...] = full.T.astype(BF16)

    spots = SIDE * SIDE
    code_of = numbers(codebook_t.shape[1], spots)
    spot = lax.broadcasted_iota(jnp.int32, (spots, 1), 0)
    for i in range(group):
        live = heights[step * group + i] * SIDE
        out = dot(table[...], one_hot_columns(codes[i : i + 1, :], code_of)).T
        decoded[i] = jnp.where(spot < live, out, 0.0).astype(BF16).reshape(SIDE, SIDE, HALF)


def put_codes(code_rows, codes, b, height, dst):
    spot = lax.broadcasted_iota(jnp.int32, (1, SIDE * SIDE), 1)
    lane = lax.broadcasted_iota(jnp.int32, (1, HALF), 1)
    per_row = HALF // SIDE
    row = jnp.where(spot < height * SIDE, codes[pl.ds(b, 1), :], -1)
    turn = lax.rem(dst, per_row) * SIDE
    upper = pltpu.roll(row[:, :HALF], turn, 1)
    lower = pltpu.roll(row[:, HALF:], turn, 1)
    inside = lane >= turn
    pieces = (jnp.where(inside, upper, -1), jnp.where(inside, lower, upper), jnp.where(inside, -1, lower))
    for i, piece in enumerate(pieces):
        target = pl.ds(dst // per_row + i, 1)
        code_rows[target, :] = jnp.where(piece < 0, code_rows[target, :], piece)


def gelu_parts(v):
    square = v * v
    t = jnp.tanh(v * (GELU_SCALE + (GELU_SCALE * GELU_CUBE) * square))
    half = 0.5 + 0.5 * t
    value = v * half
    slope = half + (value - value * half) * (2.0 * GELU_SCALE + (6.0 * GELU_SCALE * GELU_CUBE) * square)
    return value, slope


def main_step(plan, layout, k, waits, *refs):
    first_step = k == 0
    fresh = k in (0, plan.usual)
    final = k == plan.usual - 1
    refs = list(refs[waits:])

    def take(count):
        got = refs[:count]
        del refs[:count]
        return got

    if final:
        place, decode_acc = take(2)
    meta, heights, x_own, x_far, q_own, q_far, codes = take(7)
    kernel_hbm, kernel_t_hbm, mix, project, bias, book = take(6)
    if not first_step:
        x_past, q_past, carry_own, carry_far = take(4)
    if not fresh:
        past_accs = take(5)
    win_own, win_far, next_own, next_far = take(4)
    if final:
        laid_out = take(3)
    if not final:
        sums_out = take(5)
    kernel_acc, mix_acc, project_acc, book_acc, bias_acc = take(5)
    kernel, kernel_t, weight_sems = take(3)
    xo, xf, qo, qf, qd, xc_o, xc_f, qc, code_rows, act3, slope_x, grad3, block_g = take(13)
    second_s, slope_s, low_s, mixed_s, code_s, hot_s, found_s, diff_s, sems = refs

    chunk, start = plan.chunks[k], plan.starts[k]
    images, rows, block = plan.images, plan.rows[k], plan.block[k]
    half = chunk // 2
    spots = block * SIDE
    low = meta[images + k]
    high = meta[images + k + 1]

    copies = [
        (x_own.at[pl.ds(start, LEAD + chunk)], xo.at[pl.ds(0, LEAD + chunk)]),
        (x_far, xf.at[pl.ds(LEAD, chunk)]),
        (q_own.at[pl.ds(start // 2, half)], qo.at[pl.ds(LEAD, half)]),
        (q_far, qf.at[pl.ds(LEAD, half)]),
    ]
    if not first_step:
        past = plan.chunks[k - 1]
        copies += [
            (x_past.at[pl.ds(past - LEAD, LEAD)], xf.at[pl.ds(0, LEAD)]),
            (q_own.at[pl.ds(start // 2 - LEAD, LEAD)], qo.at[pl.ds(0, LEAD)]),
            (q_past.at[pl.ds(past // 2 - LEAD, LEAD)], qf.at[pl.ds(0, LEAD)]),
        ]
    accs = (mix_acc, project_acc, book_acc, bias_acc, kernel_acc)
    early = len(copies)
    if not fresh:
        copies += list(zip(past_accs[1:] + past_accs[:1], accs))
    weight_copies = []
    for i, (source, target) in enumerate(((kernel_hbm, kernel), (kernel_t_hbm, kernel_t))):
        weight_copies.append(pltpu.make_async_copy(source, target, weight_sems.at[i]))
    started = []
    for i, (source, target) in enumerate(copies):
        started.append(pltpu.make_async_copy(source, target, sems.at[i]))
        started[-1].start()
    for copy in weight_copies:
        copy.start()
    started, later = started[:early], started[early:]

    if fresh:
        for acc in accs:
            acc[...] = jnp.zeros(acc.shape, F32)

    blank = jnp.zeros((SIDE, SIDE, HALF), BF16)
    no_row = jnp.full((SIDE, SIDE, HALF), MARK, F32)
    code_rows[...] = jnp.full(code_rows.shape, -1, jnp.int32)
    for r in range(0, rows + 2 * block, SIDE):
        part = pl.ds(r, SIDE)
        xc_o[part] = blank
        xc_f[part] = blank
        if r < rows:
            qc[part] = no_row
    for copy in started:
        copy.wait()

    lane3 = lax.broadcasted_iota(jnp.int32, (1, SIDE, HALF), 2) < HALF // 2

    def spread(r0, count):
        both = (qo[pl.ds(r0, count)] + qf[pl.ds(r0, count)].astype(F32)).reshape(count * SIDE, HALF)
        turned = pltpu.roll(both, HALF // 2, 1).reshape(count, SIDE, HALF)
        both = both.reshape(count, SIDE, HALF)
        return jnp.where(lane3, both, turned), jnp.where(lane3, turned, both)

    upper, lower = spread(LEAD, half)
    qd[pl.ds(LEAD, half)] = upper
    qd[pl.ds(LEAD + half, half)] = lower
    if not first_step:
        _, lower = spread(0, LEAD)
        qd[0:LEAD] = lower

    per_row = HALF // SIDE

    def put(b, dst):
        src = meta[b] - start + LEAD
        xc_o[pl.ds(dst, SIDE)] = xo[pl.ds(src, SIDE)]
        xc_f[pl.ds(dst, SIDE)] = xf[pl.ds(src, SIDE)]
        qc[pl.ds(dst, SIDE)] = qd[pl.ds(src, SIDE)]
        end = dst + heights[b]
        xc_o[pl.ds(end, SIDE)] = blank
        xc_f[pl.ds(end, SIDE)] = blank
        qc[pl.ds(end, SIDE)] = no_row
        put_codes(code_rows, codes, b, heights[b], dst)
        return end + 1

    used = lax.fori_loop(low, high, put, jnp.int32(1))
    blocks = jnp.where(high > low, (used + (block - 1)) // block, 0)

    column = lax.rem(lax.broadcasted_iota(jnp.int32, (TILE, 1), 0), SIDE)
    not_first = column != 0
    not_last = column != SIDE - 1

    def shifted(value):
        back = jnp.where(not_first, pltpu.roll(value, 1, 0), 0.0)
        ahead = jnp.where(not_last, pltpu.roll(value, TILE - 1, 0), 0.0)
        return back.astype(BF16), ahead.astype(BF16)

    edge = jnp.zeros((SIDE, 3 * 2 * HALF), BF16)
    act3[0:SIDE] = edge
    grad3[0:SIDE] = edge
    beyond = pl.multiple_of((blocks * block + 1) * SIDE, SIDE)
    grad3[pl.ds(beyond, SIDE)] = edge

    tiles = range(0, spots, TILE)

    def read_x(r0, t):
        part = pl.ds(r0 + t // SIDE, TILE // SIDE)
        o = xc_o[part].reshape(TILE, HALF)
        f = xc_f[part].reshape(TILE, HALF)
        return jnp.concatenate([o, f], axis=1).astype(F32)

    def at(row, count=block):
        return pl.ds(pl.multiple_of(row * SIDE, SIDE), count * SIDE)

    def tile_at(row, t):
        return pl.ds(pl.multiple_of(row * SIDE, SIDE) + t, TILE)

    def activate(j, carry):
        r0 = j * block
        for t in tiles:
            value, slope = gelu_parts(read_x(r0, t))
            slope_x[tile_at(r0, t), :] = slope
            back, ahead = shifted(value)
            act3[tile_at(r0 + 1, t), 0 : 2 * HALF] = back
            act3[tile_at(r0 + 1, t), 2 * HALF : 4 * HALF] = value.astype(BF16)
            act3[tile_at(r0 + 1, t), 4 * HALF : 6 * HALF] = ahead
        return carry

    fused = k < plan.usual
    lax.fori_loop(0, 2 if fused else blocks + 1, activate, 0)
    for copy in later:
        copy.wait()
    for copy in weight_copies:
        copy.wait()

    bias_first = bias[0:1, :]
    bias_mix = bias[1:2, :]
    bias_code = bias[8:9, 0:HALF]
    lane = lax.broadcasted_iota(jnp.int32, (1, HALF), 1) < HALF // 2
    hb = block // 2
    hs = hb * SIDE

    def add_rows(total, value):
        for i in range(0, value.shape[0], 8):
            part = value[i : i + 8]
            total = part if total is None else total + part
        return total

    half_tiles = range(0, hs, TILE)
    code_of = numbers(book_acc.shape[0], HALF)
    halves = (0, hs)

    def middle(j, carry):
        r0 = j * block
        for i in range(block // per_row):
            row = code_rows[pl.ds(j * (block // per_row) + i, 1), :]
            hot_s[:, i * HALF : (i + 1) * HALF] = one_hot_columns(row, code_of)
        for h in halves:
            found_s[h : h + hs] = dot(book[...], hot_s[:, h : h + hs]).astype(BF16).T
        pre = []
        for h in halves:
            window = jnp.concatenate([act3[at(r0 + i + h // SIDE, hb), :] for i in range(3)], axis=1)
            pre.append(dot(window, kernel[...]))
        for h, part in zip(halves, pre):
            for t in half_tiles:
                value, slope = gelu_parts(part[t : t + TILE] + bias_first)
                second_s[h + t : h + t + TILE] = value.astype(BF16)
                slope_s[h + t : h + t + TILE] = slope
        mixed = [dot(second_s[h : h + hs], mix[...]) for h in halves]
        for h, part in zip(halves, mixed):
            for t in half_tiles:
                low_s[h + t : h + t + TILE] = (read_x(r0, h + t) + part[t : t + TILE] + bias_mix).astype(BF16)
        latents = [dot(low_s[h : h + hs], project[i]) for i, h in enumerate(halves)]
        total = None
        for t in half_tiles:
            first = pl.ds(r0 + t // SIDE, TILE // SIDE)
            other = pl.ds(r0 + hb + t // SIDE, TILE // SIDE)
            ch = jnp.where(lane, found_s[t : t + TILE].astype(F32), found_s[hs + t : hs + t + TILE].astype(F32))
            q = jnp.where(lane3, qc[first], qc[other]).reshape(TILE, HALF)
            live = q < 0.5 * MARK
            latent = latents[0][t : t + TILE] + latents[1][t : t + TILE] + bias_code
            diff = jnp.where(live, latent - ch, 0.0)
            code_grad = jnp.where(live, q + (2.0 * COMMIT) * diff, 0.0)
            code_s[t : t + TILE] = code_grad.astype(BF16)
            total = add_rows(total, code_grad)
            big = diff.astype(BF16).astype(F32)
            small = diff - big
            turned = pltpu.roll(small, HALF // 2, 1)
            diff_s[t : t + TILE] = jnp.where(lane, big, turned).astype(BF16)
            turned = pltpu.roll(big, HALF // 2, 1)
            diff_s[hs + t : hs + t + TILE] = jnp.where(lane, turned, small).astype(BF16)
        bias_acc[16:24, 0:HALF] += total
        total = None
        blocks_g = [dot(code_s[...], project[i], NT) for i in range(2)]
        for h, part in zip(halves, blocks_g):
            for t in half_tiles:
                block_g[tile_at(r0, h + t), :] = part[t : t + TILE]
                mixed_s[h + t : h + t + TILE] = part[t : t + TILE].astype(BF16)
                total = add_rows(total, part[t : t + TILE])
        bias_acc[8:16] += total
        second_grad = [dot(mixed_s[h : h + hs], mix[...], NT) for h in halves]
        total = None
        for h, part in zip(halves, second_grad):
            for t in half_tiles:
                first_grad = slope_s[h + t : h + t + TILE] * part[t : t + TILE]
                back, ahead = shifted(first_grad)
                grad3[tile_at(r0 + 1, h + t), 0 : 2 * HALF] = ahead
                grad3[tile_at(r0 + 1, h + t), 2 * HALF : 4 * HALF] = first_grad.astype(BF16)
                grad3[tile_at(r0 + 1, h + t), 4 * HALF : 6 * HALF] = back
                total = add_rows(total, first_grad)
        bias_acc[0:8] += total
        book_acc[...] += dot(hot_s[...], diff_s[...])
        mix_acc[...] += dot(second_s[...], mixed_s[...], TN)
        project_acc[...] += jnp.where(lane, dot(low_s[0:hs], code_s[...], TN), dot(low_s[hs:], code_s[...], TN))
        return carry

    def finish(j, carry):
        r0 = j * block
        active = act3[at(r0 + 1), 2 * HALF : 4 * HALF].T
        for i in range(3):
            kernel_acc[:, i * 6 * HALF : (i + 1) * 6 * HALF] += dot(active, grad3[at(r0 + 2 - i), :])
        grads = []
        for h in halves:
            window = jnp.concatenate([grad3[at(r0 + 2 - i + h // SIDE, hb), :] for i in range(3)], axis=1)
            grads.append(dot(window, kernel_t[...]))
        for h, grad in zip(halves, grads):
            for t in half_tiles:
                here = tile_at(r0, h + t)
                out = (block_g[here, :] + slope_x[here, :] * grad[t : t + TILE]).astype(BF16)
                part = pl.ds(r0 + (h + t) // SIDE, TILE // SIDE)
                xc_o[part] = out[:, :HALF].reshape(TILE // SIDE, SIDE, HALF)
                xc_f[part] = out[:, HALF:].reshape(TILE // SIDE, SIDE, HALF)
        return carry

    def opening(j, carry):
        middle(j, carry)
        return activate(j + 2, carry)

    def steady(j, carry):
        finish(j - 2, carry)
        middle(j, carry)
        return activate(j + 2, carry)

    if fused:
        lax.fori_loop(0, jnp.minimum(blocks, 2), opening, 0)
        lax.fori_loop(2, blocks, steady, 0)
        lax.fori_loop(jnp.maximum(blocks - 2, 0), blocks, finish, 0)
    else:
        lax.fori_loop(0, blocks, middle, 0)
        lax.fori_loop(0, blocks, finish, 0)
    leaving = []
    if not final:
        leaving += list(zip((kernel_acc, mix_acc, project_acc, book_acc, bias_acc), sums_out))
        for i, (source, target) in enumerate(leaving):
            leaving[i] = pltpu.make_async_copy(source, target, sems.at[i])
            leaving[i].start()

    out_o, out_f = xo, xf
    if first_step:
        out_o[0:LEAD] = blank
        out_f[0:LEAD] = blank
    else:
        out_o[0:LEAD] = carry_own[...]
        out_f[0:LEAD] = carry_far[...]

    def collect(b, src):
        dst = meta[b] - start + LEAD
        out_o[pl.ds(dst, SIDE)] = xc_o[pl.ds(src, SIDE)]
        out_f[pl.ds(dst, SIDE)] = xc_f[pl.ds(src, SIDE)]
        return src + heights[b] + 1

    lax.fori_loop(low, high, collect, jnp.int32(1))
    size = win_own.shape[0]
    windows = (
        (out_o.at[pl.ds(0, size)], win_own),
        (out_f.at[pl.ds(0, size)], win_far),
        (out_o.at[pl.ds(chunk, LEAD)], next_own),
        (out_f.at[pl.ds(chunk, LEAD)], next_far),
    )
    for i, (source, target) in enumerate(windows):
        leaving.append(pltpu.make_async_copy(source, target, sems.at[5 + i]))
        leaving[-1].start()
    if final:
        sums = (kernel_acc, mix_acc, project_acc, book_acc, bias_acc, decode_acc)
        laid_out += [slope_x.at[pl.ds(0, layout.rows), pl.ds(i * HALF, HALF)] for i in range(2)]
        leaving += gather_grads(plan, layout, place, meta, sums, *laid_out, sems)
    for copy in leaving:
        copy.wait()


class Layout:
    def __init__(self, devices, book_rows, embed):
        self.mix = 9 * 2 * HALF
        self.project = self.mix + 2 * HALF
        self.book = self.project + HALF // 2
        self.bias = self.book + book_rows // 2
        self.decode = self.bias + 8
        used = self.decode + embed + 8
        self.devices = devices
        self.piece = -(-used // (devices * SIDE)) * SIDE
        self.rows = self.piece * devices
        self.half = self.rows // 2
        self.used = used


def lay_out(layout, swap, kernel_acc, mix_acc, project_acc, book_acc, bias_acc, decode_acc, own, far):
    def lanes(value):
        return value[:, :HALF], value[:, HALF:]

    def order(first, second):
        return jnp.where(swap, second, first), jnp.where(swap, first, second)

    row = 0
    for tap in range(9):
        block = kernel_acc[:, tap * 2 * HALF : (tap + 1) * 2 * HALF]
        mine, theirs = lanes(block)
        a, b = order(mine[:HALF], mine[HALF:])
        own[row : row + HALF] = a
        own[row + HALF : row + 2 * HALF] = b
        a, b = order(theirs[:HALF], theirs[HALF:])
        far[row : row + HALF] = a
        far[row + HALF : row + 2 * HALF] = b
        row += 2 * HALF
    row = layout.mix
    for target, part in ((own, mix_acc[:HALF]), (far, mix_acc[HALF:])):
        a, b = order(*lanes(part))
        target[row : row + HALF] = a
        target[row + HALF : row + 2 * HALF] = b
    row = layout.project
    side = HALF // 2
    for target, part in ((own, project_acc[:HALF]), (far, project_acc[HALF:])):
        part = part + pltpu.roll(part, side, 1)
        target[row : row + side] = part.T[:side]
    row = layout.book
    book = book_acc[...]
    book = -2.0 * (book + pltpu.roll(book, side, 1))
    book = book.T[:side]
    for c in range(book.shape[1] // HALF):
        part = book[:, c * HALF : (c + 1) * HALF]
        own[row + c * side : row + (c + 1) * side] = part
        far[row + c * side : row + (c + 1) * side] = part
    row = layout.bias
    sums = [jnp.sum(bias_acc[8 * i : 8 * i + 8], axis=0, keepdims=True) for i in range(3)]
    code = sums[2][:, :HALF]
    code = code + pltpu.roll(code, side, 1)
    which = lax.broadcasted_iota(jnp.int32, (8, HALF), 0)
    for target, first in ((own, 0), (far, HALF)):
        part = jnp.where(which == 0, sums[0][:, first : first + HALF], sums[1][:, first : first + HALF])
        target[row : row + 8] = jnp.where(which == 2, code, jnp.where(which < 2, part, 0.0))
    row = layout.decode
    rest = layout.rows - row
    own[row:] = jnp.zeros((rest, HALF), F32)
    far[row:] = jnp.zeros((rest, HALF), F32)
    if decode_acc is not None:
        own[row : row + decode_acc.shape[0]] = decode_acc[...]


def gather_plain(layout, place, *refs):
    lay_out(layout, place[0] == 1, *refs[:5], None, *refs[5:])


def gather_grads(plan, layout, place, meta, accs, keep_own, keep_far, send, own, far, sems):
    lay_out(layout, place[0] == 1, *accs, own, far)
    base = plan.images + len(plan.chunks) + 1
    over = (meta[base + 4] > plan.covered).astype(F32)
    which = lax.broadcasted_iota(jnp.int32, (8, HALF), 0)
    row = layout.bias
    own[row : row + 8] = jnp.where(which == 3, over, own[row : row + 8])
    half = layout.half
    mine = pl.ds(pl.multiple_of(place[1] * half, SIDE), half)
    other = pl.ds(pl.multiple_of((1 - place[1]) * half, SIDE), half)
    kept = []
    for i, (source, target) in enumerate(((own, keep_own), (far, keep_far))):
        kept.append(pltpu.make_async_copy(source.at[mine, :], target, sems.at[9 + i]))
        kept[-1].start()
    send[0] = own[other, :].astype(BF16)
    send[1] = far[other, :].astype(BF16)
    return kept


def hold(*refs):
    pass


def add_far(keep_far, came, out):
    out[...] = (keep_far[...] + came[1].astype(F32)).astype(BF16)


def add_own(keep_own, came, came_far, out, token):
    token[...] = jnp.zeros_like(token)
    total = keep_own[...] + came[0].astype(F32) + came_far[...].astype(F32)
    out[...] = total.astype(BF16).reshape(out.shape)


def add_pieces(pieces, _, out, token):
    token[...] = jnp.zeros_like(token)
    total = pieces[0].astype(F32)
    for i in range(1, pieces.shape[0]):
        total = total + pieces[i].astype(F32)
    out[...] = jnp.broadcast_to(total.astype(BF16)[None], out.shape)


def write_grads(layout, place, mine, theirs, kernel, first_bias, mix, mix_bias, project, project_bias, book, decode, decode_bias, whole):
    half = layout.half
    whole[pl.ds(pl.multiple_of(place[1] * half, SIDE), half), :] = mine[...].astype(F32)
    whole[pl.ds(pl.multiple_of((1 - place[1]) * half, SIDE), half), :] = theirs[...].astype(F32)
    split_grads(layout, whole, kernel, first_bias, mix, mix_bias, project, project_bias, book, decode, decode_bias)


def split_grads(layout, whole, kernel, first_bias, mix, mix_bias, project, project_bias, book, decode, decode_bias):
    for tap in range(9):
        kernel[tap] = whole[tap * 2 * HALF : (tap + 1) * 2 * HALF]
    row = layout.mix
    mix[:, :HALF] = whole[row : row + HALF]
    mix[:, HALF:] = whole[row + HALF : row + 2 * HALF]
    side = HALF // 2
    for row, target in ((layout.project, project), (layout.book, book)):
        for c in range(target.shape[1] // HALF):
            target[:, c * HALF : (c + 1) * HALF] = whole[row + c * side : row + (c + 1) * side]
    row = layout.bias
    first_bias[...] = whole[row : row + 1]
    mix_bias[...] = whole[row + 1 : row + 2]
    project_bias[...] = whole[row + 2 : row + 3, :side]
    row = layout.decode
    n = decode.shape[0]
    decode[...] = whole[row : row + n]
    decode_bias[...] = whole[row + n : row + n + 1]


def split_again(layout, total, extra, *refs):
    whole = refs[-1]
    whole[...] = total[...].astype(F32) + extra[...]
    split_grads(layout, whole, *refs[:-1])


def restore_rows(plan, n, waits, *refs):
    meta, heights, *refs = refs[waits:]
    own, far, out, token = refs[:n], refs[n : 2 * n], refs[2 * n], refs[2 * n + 1]
    token[...] = jnp.zeros_like(token)
    stage_own, stage_far, sems = refs[2 * n + 2 :]
    copies = []
    for k in range(n):
        size = plan.chunks[k] + (LEAD if k == n - 1 else 0)
        for i, (source, target) in enumerate(((own[k], stage_own), (far[k], stage_far))):
            from_rows = source.at[pl.ds(0, size)]
            copies.append(pltpu.make_async_copy(from_rows, target.at[pl.ds(plan.starts[k], size)], sems.at[i, k]))
            copies[-1].start()
    for copy in copies:
        copy.wait()
    base = plan.images + len(plan.chunks) + 1
    own_row, send_row = meta[base], meta[base + 1]
    first, last = meta[base + 2], meta[base + 3]
    row_of = lax.broadcasted_iota(jnp.int32, (SIDE, 1, 1), 0)

    def own_image(b, carry):
        rows = stage_own[pl.ds(meta[b] + LEAD, SIDE)]
        out[b] = jnp.where(row_of < heights[b], rows, jnp.zeros_like(rows))
        return carry

    def far_image(b, carry):
        rows = stage_far[pl.ds(meta[b] + own_row - send_row + LEAD, SIDE)]
        out[b] = jnp.where(row_of < heights[b], rows, jnp.zeros_like(rows))
        return carry

    lax.fori_loop(first, last, own_image, 0)
    lax.fori_loop(0, first, far_image, 0)
    lax.fori_loop(last, plan.images, far_image, 0)


def trade(value):
    return lax.ppermute(value, "mp", [(0, 1), (1, 0)])


def held(value, *others):
    return pl.pallas_call(
        hold,
        out_shape=shape(value.shape, value.dtype),
        in_specs=[ANY] + [VMEM if other.size <= 1 << 14 else ANY for other in others],
        out_specs=ANY,
        input_output_aliases={0: 0},
        compiler_params=params(60),
        name="hold",
    )(value, *others)


def run_main(plan, layout, k, meta, heights, streams, weights, state, waits=(), ending=()):
    chunk, rows, block = plan.chunks[k], plan.rows[k], plan.block[k]
    last = k >= plan.usual - 1
    final = k == plan.usual - 1
    x_own, x_far, q_own, q_far, codes = streams
    book_rows = weights[-1].shape[1]
    args = [*waits, *ending, meta, heights, x_own, x_far[k], q_own, q_far[k], codes, *weights]
    specs = [ANY] * len(waits) + ([SMEM, VMEM] if final else [])
    specs += [SMEM, SMEM, ANY, ANY, ANY, ANY, VMEM, ANY, ANY] + [VMEM] * (len(weights) - 2)
    alias = {}
    if state is not None:
        args += [x_far[k - 1], q_far[k - 1], *state]
        specs += [ANY, ANY, VMEM, VMEM] + [ANY] * (len(state) - 2)
        if not final:
            for i in range(len(state) - 2):
                alias[len(args) - 5 + i] = 4 + i
    size = chunk + LEAD if last else chunk
    tile = (SIDE, HALF)
    outs = [shape((size,) + tile, BF16)] * 2 + [shape((LEAD,) + tile, BF16)] * 2
    sums = [(2 * HALF, 18 * HALF), (2 * HALF, 2 * HALF), (2 * HALF, HALF), (book_rows, HALF), (24, 2 * HALF)]
    scratch = [pltpu.VMEM(dims, F32) for dims in sums]
    out_specs = [ANY] * 4
    if final:
        outs += [shape((layout.half, HALF), F32)] * 2 + [shape((2, layout.half, HALF), BF16)]
        out_specs += [ANY, ANY, VMEM]
    else:
        outs += [shape(dims, F32) for dims in sums]
        out_specs += [ANY] * 5
    scratch += [pltpu.VMEM((18 * HALF, 2 * HALF), BF16)] * 2 + [pltpu.SemaphoreType.DMA((2,))]
    half = chunk // 2
    spots = block * SIDE
    scratch += [
        pltpu.VMEM((LEAD + chunk + 2 * SIDE,) + tile, BF16),
        pltpu.VMEM((LEAD + chunk + 2 * SIDE,) + tile, BF16),
        pltpu.VMEM((LEAD + half,) + tile, F32),
        pltpu.VMEM((LEAD + half,) + tile, BF16),
        pltpu.VMEM((LEAD + chunk + SIDE,) + tile, F32),
        pltpu.VMEM((rows + 2 * block + SIDE,) + tile, BF16),
        pltpu.VMEM((rows + 2 * block + SIDE,) + tile, BF16),
        pltpu.VMEM((rows + 2 * SIDE,) + tile, F32),
        pltpu.VMEM((-(-(rows * SIDE // HALF + 4) // 8) * 8, HALF), jnp.int32),
        pltpu.VMEM(((rows + 2 * block + 2) * SIDE, 6 * HALF), BF16),
        pltpu.VMEM(((rows + 2 * block) * SIDE, 2 * HALF), F32),
        pltpu.VMEM(((rows + 2) * SIDE, 6 * HALF), BF16),
        pltpu.VMEM((rows * SIDE, 2 * HALF), F32),
        pltpu.VMEM((spots, 2 * HALF), BF16),
        pltpu.VMEM((spots, 2 * HALF), F32),
        pltpu.VMEM((spots, 2 * HALF), BF16),
        pltpu.VMEM((spots, 2 * HALF), BF16),
        pltpu.VMEM((spots // 2, HALF), BF16),
        pltpu.VMEM((book_rows, spots), BF16),
        pltpu.VMEM((spots, HALF), BF16),
        pltpu.VMEM((spots, HALF), BF16),
        pltpu.SemaphoreType.DMA((13,)),
    ]
    spots = chunk * SIDE
    return pl.pallas_call(
        functools.partial(main_step, plan, layout, k, len(waits)),
        out_shape=outs,
        in_specs=specs,
        out_specs=out_specs,
        scratch_shapes=scratch,
        input_output_aliases=alias,
        compiler_params=params(58),
        cost_estimate=cost(60 * 65536 * spots, 8 * MIB, 2 * 256 * spots),
        name=f"main_{k}",
    )(*args)


def local(
    image_latents,
    image_heights,
    code_index,
    kernel_three,
    bias_three,
    weight_mix,
    bias_mix,
    weight_project,
    bias_project,
    codebook,
    weight_decode,
    bias_decode,
    out_grad,
):
    images = image_latents.shape[0]
    plan = Plan(images)
    n = len(plan.chunks)
    tile = (SIDE, HALF)
    where = lax.axis_index("mp").astype(jnp.int32)
    core = lax.rem(lax.axis_index("dp").astype(jnp.int32), 2)
    spot = place = jnp.stack([where, core])

    devices = lax.axis_size("dp")
    across = [(i, i ^ 1) for i in range(devices)]
    kernel_half = lax.dynamic_slice_in_dim(kernel_three, core * HALF, HALF, 1)
    far_kernel = trade(kernel_half)
    far_kernel_other = lax.ppermute(far_kernel, "dp", across)

    packed = pl.pallas_call(
        functools.partial(pack_latents, plan),
        out_shape=[
            shape((meta_size(plan),), jnp.int32),
            shape((LEAD + plan.total,) + tile, BF16),
        ]
        + [shape((c,) + tile, BF16) for c in plan.chunks],
        in_specs=[SMEM, SMEM, HBM, ANY],
        out_specs=[SMEM, ANY] + [ANY] * n,
        scratch_shapes=[
            pltpu.VMEM((images, SIDE) + tile, BF16),
            pltpu.VMEM((plan.packed + SIDE,) + tile, BF16),
            pltpu.SemaphoreType.DMA((8,)),
            pltpu.SemaphoreType.DMA((n + 1,)),
        ],
        compiler_params=params(60),
        cost_estimate=cost(0, 12 * MIB),
        name="pack_latents",
    )(image_heights, place, image_latents, kernel_half)
    meta, x_own, x_send = packed[0], packed[1], packed[2:]

    packed = pl.pallas_call(
        functools.partial(pack_code_grads, plan),
        out_shape=[shape((plan.total // 2,) + tile, F32), shape((2 * HALF + HALF // 2 + SIDE, HALF), BF16)]
        + [shape((c // 2,) + tile, BF16) for c in plan.chunks],
        in_specs=[SMEM] + [HBM] * 6 + [ANY],
        out_specs=[VMEM] * (n + 2),
        scratch_shapes=[
            pltpu.VMEM((images, SIDE) + tile, BF16),
            pltpu.VMEM((plan.packed + SIDE,) + tile, BF16),
            pltpu.SemaphoreType.DMA((8,)),
            pltpu.SemaphoreType.DMA((5,)),
            pltpu.VMEM(weight_decode.shape, BF16),
            pltpu.VMEM(weight_mix.shape, BF16),
            pltpu.VMEM(weight_project.shape[::-1], BF16),
            pltpu.VMEM((1, HALF), BF16),
            pltpu.VMEM((1, HALF), BF16),
        ],
        compiler_params=params(60),
        cost_estimate=cost(2 * 2 * plan.total * SIDE * 256 * 128, 10 * MIB),
        name="pack_code_grads",
    )(meta, out_grad, weight_decode, weight_mix, weight_project.T, bias_three.reshape(1, HALF), bias_mix.reshape(1, HALF), far_kernel)
    q_own, small, q_send = packed[0], packed[1], packed[2:]

    book_rows, embed = codebook.shape
    codebook_t = codebook.T
    far_small = trade(small)
    usual = plan.usual
    x_far, q_far = [], []
    x_far.append(trade(x_send[0]))
    q_far.append(trade(q_send[0]))

    weights = pl.pallas_call(
        prepare_weights,
        out_shape=[
            shape((18 * HALF, 2 * HALF), BF16),
            shape((18 * HALF, 2 * HALF), BF16),
            shape((2 * HALF, 2 * HALF), BF16),
            shape((2, 2 * HALF, HALF), BF16),
            shape((SIDE, 2 * HALF), F32),
            shape((HALF, book_rows), BF16),
        ],
        in_specs=[SMEM, HBM, HBM, HBM] + [VMEM] * 4,
        out_specs=[VMEM] * 6,
        scratch_shapes=[pltpu.VMEM(kernel_three.shape, BF16)] * 2 + [pltpu.SemaphoreType.DMA((3,))],
        compiler_params=params(20),
        cost_estimate=cost(0, 5 * MIB),
        name="prepare_weights",
    )(place, kernel_three, far_kernel, far_kernel_other, small, far_small, bias_project.reshape(1, -1), codebook_t)

    groups = 8
    group = images // groups
    codes = code_index.reshape(images, SIDE * SIDE)
    whole = lambda dims: pl.BlockSpec(dims, lambda g: (0,) * len(dims))
    four = pl.BlockSpec((group, SIDE) + tile, lambda g: (g, 0, 0, 0))
    row = pl.BlockSpec((group, SIDE * SIDE), lambda g: (g, 0))
    def code_sums(first, steps):
        return pl.pallas_call(
            functools.partial(sum_codes, first, group),
            grid=(steps,),
            out_shape=shape((embed + 8, HALF), F32),
            in_specs=[
                SMEM,
                pl.BlockSpec((group, SIDE * SIDE), lambda g: (g + first, 0)),
                pl.BlockSpec((group, SIDE) + tile, lambda g: (g + first, 0, 0, 0)),
                whole((embed, book_rows)),
                ANY,
                ANY,
            ],
            out_specs=whole((embed + 8, HALF)),
            scratch_shapes=[
                pltpu.VMEM((book_rows, group * SIDE * SIDE), BF16),
                pltpu.VMEM((group * SIDE * SIDE, HALF), BF16),
                pltpu.VMEM((book_rows, HALF), F32),
            ],
            compiler_params=params(60),
            cost_estimate=cost(steps * group * 256 * 512 * 256, steps * group * 65536),
            name=f"sum_codes_{first}",
        )(image_heights, codes, out_grad, codebook_t, small, far_kernel)

    def decode(after):
        return pl.pallas_call(
            functools.partial(decode_images, plan, groups),
            grid=(groups,),
            out_shape=[shape((images, SIDE) + tile, BF16), shape((8, HALF), F32)],
            in_specs=[SMEM, row, whole((embed, book_rows)), whole((embed, HALF)), whole((1, HALF)), whole((8, HALF))],
            out_specs=[four, whole((8, HALF))],
            scratch_shapes=[pltpu.VMEM((HALF, book_rows), BF16)],
            compiler_params=params(32),
            cost_estimate=cost(images * 256 * 512 * 256, 5 * MIB),
            name="decode_images",
        )(image_heights, codes, codebook_t, weight_decode, bias_decode.reshape(1, HALF), after)

    decode_acc = code_sums(0, groups)
    for k in range(1, usual):
        x_far.append(trade(held(x_send[k], decode_acc, far_small, x_far[0], q_far[0])))
        q_far.append(trade(held(q_send[k], decode_acc, far_small, x_far[0], q_far[0])))

    layout = Layout(devices, book_rows, embed)
    half, piece, chips = layout.half, layout.piece, devices // 2
    streams = (x_own, x_far, q_own, q_far, codes)
    state = None
    win_own, win_far = [], []
    for k in range(usual):
        waits = win_far[k - 2 : k - 1] if k > 1 else []
        ending = (spot, decode_acc) if k == usual - 1 else ()
        outs = run_main(plan, layout, k, meta, image_heights, streams, weights, state, waits, ending)
        win_own.append(outs[0])
        if k < usual - 1:
            win_far.append(trade(outs[1]))
        state = outs[2:]
    last_window = outs[1]
    carry, (keep_own, keep_far, send) = state[:2], state[2:]

    def restore(own, far, waits=()):
        count = len(own)
        return pl.pallas_call(
            functools.partial(restore_rows, plan, count, len(waits)),
            out_shape=[shape((images, SIDE) + tile, BF16), shape((8, HALF), F32)],
            in_specs=[VMEM] * len(waits) + [SMEM, SMEM] + [ANY] * (2 * count),
            out_specs=[VMEM, VMEM],
            scratch_shapes=[
                pltpu.VMEM((plan.total + LEAD + SIDE,) + tile, BF16),
                pltpu.VMEM((plan.total + LEAD + SIDE,) + tile, BF16),
                pltpu.SemaphoreType.DMA((2, count)),
            ],
            compiler_params=params(60),
            cost_estimate=cost(0, 10 * MIB),
            name="restore_rows",
        )(*waits, meta, image_heights, *own, *far)


    def step(body, out, name, *args, waits=()):
        specs = [VMEM] * (len(args) + len(waits))
        args = (*args, *waits)
        return pl.pallas_call(
            body,
            out_shape=out,
            in_specs=specs,
            out_specs=[VMEM] * len(out) if isinstance(out, list) else VMEM,
            compiler_params=params(24),
            cost_estimate=cost(0, 2 * MIB),
            name=name,
        )(*args)

    send = held(send, win_far[usual - 2])
    came = lax.ppermute(send, "dp", across)
    win_far.append(trade(last_window))
    far_sums = step(add_far, shape((half, HALF), BF16), "add_far", keep_far, came)
    came_far = trade(far_sums)
    parts = [shape((chips, piece, HALF), BF16), shape((8, HALF), F32)]
    mine, token = step(add_own, parts, "add_own", keep_own, came, came_far)
    decoded, token = decode(token)
    cores = [[i for i in range(devices) if i % 2 == c] for c in range(2)]
    mine = lax.all_to_all(mine, "dp", 0, 0, axis_index_groups=cores, tiled=True)
    mine, token = step(add_pieces, parts, "add_pieces", mine, waits=[token])
    latents_grad, token = restore(win_own, win_far, [token])
    mine = lax.all_to_all(mine, "dp", 0, 0, axis_index_groups=cores, tiled=True)
    mine = held(mine, token).reshape(half, HALF)
    theirs = lax.ppermute(mine, "dp", across)

    grads_out = [
        shape((9, 2 * HALF, HALF), F32),
        shape((1, HALF), F32),
        shape((HALF, 2 * HALF), F32),
        shape((1, HALF), F32),
        shape((embed, HALF), F32),
        shape((1, embed), F32),
        shape((embed, book_rows), F32),
        shape((embed, HALF), F32),
        shape((1, HALF), F32),
    ]
    whole = pltpu.VMEM((layout.rows, HALF), F32)

    def usual_end(latents_grad):
        grads = pl.pallas_call(
            functools.partial(write_grads, layout),
            out_shape=grads_out,
            in_specs=[SMEM, VMEM, VMEM],
            out_specs=[VMEM] * 9,
            scratch_shapes=[whole],
            compiler_params=params(24),
            cost_estimate=cost(0, 4 * MIB),
            name="write_grads",
        )(spot, mine, theirs)
        return (latents_grad, *grads)

    def longer_end(latents_grad):
        last_x, last_q = trade(x_send[usual]), trade(q_send[usual])
        streams = (x_own, x_far + [last_x], q_own, q_far + [last_q], codes)
        outs = run_main(plan, layout, usual, meta, image_heights, streams, weights, carry)
        latents_grad, _ = restore(win_own + [outs[0]], win_far + [trade(outs[1])])
        own, far = pl.pallas_call(
            functools.partial(gather_plain, layout),
            out_shape=[shape((layout.rows, HALF), F32)] * 2,
            in_specs=[SMEM] + [VMEM] * 5,
            out_specs=[VMEM] * 2,
            compiler_params=params(40),
            name="gather_plain",
        )(spot, *outs[4:])
        extra = lax.psum(own + trade(far), "dp")
        first, second = jnp.where(core == 0, mine, theirs), jnp.where(core == 0, theirs, mine)
        grads = pl.pallas_call(
            functools.partial(split_again, layout),
            out_shape=grads_out,
            in_specs=[VMEM, VMEM],
            out_specs=[VMEM] * 9,
            scratch_shapes=[whole],
            compiler_params=params(24),
            name="split_again",
        )(jnp.concatenate([first, second]), extra)
        return (latents_grad, *grads)

    flag = layout.bias + 3
    holder = flag // half
    flags = jnp.where(core == holder, mine[flag - holder * half, 0], theirs[flag - holder * half, 0])
    ends = lax.cond(flags.astype(F32) > 0.5, longer_end, usual_end, latents_grad)
    latents_grad, kernel_grad, first_bias, mix_grad, mix_bias, project_grad, project_bias, book, decode, decode_bias = ends
    return (
        decoded,
        latents_grad,
        kernel_grad,
        first_bias.reshape(HALF),
        mix_grad,
        mix_bias.reshape(HALF),
        project_grad.T,
        project_bias.reshape(embed),
        book.T,
        decode,
        decode_bias.reshape(HALF),
    )


def solution(mesh):
    tile = P("dp", None, None, "mp")
    placed = (
        tile,
        P("dp"),
        P("dp", None, None),
        P(None, None, "mp"),
        P("mp"),
        P("mp", None),
        P("mp"),
        P("mp", None),
        P(),
        P(),
        P(None, "mp"),
        P("mp"),
        tile,
    )
    outs = (
        tile,
        tile,
        P(None, None, "mp"),
        P("mp"),
        P("mp", None),
        P("mp"),
        P("mp", None),
        P(),
        P(),
        P(None, "mp"),
        P("mp"),
    )
    return jax.shard_map(local, mesh=mesh, in_specs=placed, out_specs=outs, check_vma=False)
```

```python
import functools

import jax
import jax.numpy as jnp
from jax import lax
from jax.experimental import pallas as pl
from jax.experimental.pallas import tpu as pltpu
from jax.sharding import PartitionSpec as P

SIDE = 16
HALF = 128
LEAD = 16
BLOCK = 32
TILE = 32
MARK = 1e9
GELU_SCALE = 0.7978845608028654
GELU_CUBE = 0.044715
COMMIT = 0.25
F32 = jnp.float32
BF16 = jnp.bfloat16
ANY = pl.BlockSpec(memory_space=pl.ANY)
SMEM = pl.BlockSpec(memory_space=pltpu.SMEM)
HBM = pl.BlockSpec(memory_space=pltpu.HBM)
VMEM = pl.BlockSpec(memory_space=pltpu.VMEM)
MIB = 1 << 20

NT = (((1,), (1,)), ((), ()))
TN = (((0,), (0,)), ((), ()))
NN = (((1,), (0,)), ((), ()))


def dot(a, b, dims=NN):
    return lax.dot_general(a, b, dims, preferred_element_type=F32)


def one_hot_columns(codes, code_of):
    return jnp.where(code_of == codes.astype(jnp.int16), jnp.bfloat16(1), jnp.bfloat16(0))


def numbers(count, width):
    return lax.broadcasted_iota(jnp.int32, (count, width), 0).astype(jnp.int16)


def shape(dims, kind):
    return jax.ShapeDtypeStruct(dims, kind)


def params(mib):
    return pltpu.CompilerParams(vmem_limit_bytes=mib * MIB)


def cost(flops, moved, slow=0):
    return pl.CostEstimate(flops=flops, bytes_accessed=moved, transcendentals=slow)


class Plan:
    def __init__(self, images):
        self.images = images
        longest = images * SIDE // 2 + SIDE // 2
        part = images // 8
        self.chunks = [18 * part, 29 * part]
        self.usual = len(self.chunks)
        rest = longest - sum(self.chunks)
        self.chunks.append(rest)
        self.starts = [sum(self.chunks[:k]) for k in range(len(self.chunks))]
        self.total = sum(self.chunks)
        self.packed = -(-(LEAD + longest + self.total + LEAD) // SIDE) * SIDE
        self.rows, self.block = [], []
        for k, c in enumerate(self.chunks):
            block = BLOCK if k < self.usual else SIDE
            most = 1 + c + 15 + c // 4 + 1
            self.rows.append(-(-most // block) * block)
            self.block.append(block)
        self.covered = sum(self.chunks[: self.usual])


def meta_size(plan):
    return plan.images + len(plan.chunks) + 1 + 5


def plan_rows(plan, heights, place, meta):
    images = plan.images
    base = images + len(plan.chunks) + 1

    def total_of(b, acc):
        return acc + heights[b]

    total = lax.fori_loop(0, images, total_of, jnp.int32(0))

    def split_of(b, state):
        acc, best, split, cut = state
        acc = acc + heights[b]
        worst = jnp.maximum(acc, total - acc)
        better = worst < best
        return (acc, jnp.where(better, worst, best), jnp.where(better, b + 1, split), jnp.where(better, acc, cut))

    _, _, split, cut = lax.fori_loop(0, images, split_of, (jnp.int32(0), jnp.int32(1 << 20), jnp.int32(0), jnp.int32(0)))
    mine = place[0]
    own_first = jnp.where(mine == 0, 0, split)
    own_last = jnp.where(mine == 0, split, images)
    own_row = jnp.where(mine == 0, 0, cut)
    send_row = jnp.where(mine == 0, cut, 0)
    for k in range(len(plan.chunks) + 1):
        meta[images + k] = own_first
    ends = [plan.starts[k] + plan.chunks[k] for k in range(len(plan.chunks))]

    def place_of(b, acc):
        meta[b] = acc - own_row
        acc = acc + heights[b]
        end = acc - own_row
        inside = jnp.logical_and(b >= own_first, b < own_last)
        step = jnp.int32(0)
        for k in range(len(plan.chunks) - 1):
            step = step + (end > ends[k]).astype(jnp.int32)

        @pl.when(inside)
        def _():
            meta[images + 1 + step] = b + 1

        return acc

    lax.fori_loop(0, images, place_of, jnp.int32(0))
    for k in range(len(plan.chunks)):
        meta[images + k + 1] = jnp.maximum(meta[images + k + 1], meta[images + k])
    meta[base] = own_row
    meta[base + 1] = send_row
    meta[base + 2] = own_first
    meta[base + 3] = own_last
    meta[base + 4] = jnp.maximum(cut, total - cut)


def pack_rows(plan, meta, source, packed, piece, count):
    base = plan.images + len(plan.chunks) + 1

    def one(i, carry):
        b = piece * count + i
        row = meta[b] + meta[base] + LEAD
        packed[pl.ds(row, SIDE)] = source[b]
        return carry

    lax.fori_loop(0, count, one, 0)


def pack_latents(plan, heights, place, x_hbm, _, meta, own, *rest):
    n = len(plan.chunks)
    sends, (x_in, packed, sem_in, sem_out) = rest[:n], rest[n:]
    pieces = 8
    count = plan.images // pieces
    fetch = []
    for p in range(pieces):
        part = pl.ds(p * count, count)
        fetch.append(pltpu.make_async_copy(x_hbm.at[part], x_in.at[part], sem_in.at[p]))
        fetch[-1].start()
    plan_rows(plan, heights, place, meta)
    base = plan.images + n + 1
    for p in range(pieces):
        fetch[p].wait()
        pack_rows(plan, meta, x_in, packed, p, count)
    copies = []
    for k in range(n):
        part = pl.ds(LEAD + meta[base + 1] + plan.starts[k], plan.chunks[k])
        copies.append(pltpu.make_async_copy(packed.at[part], sends[k], sem_out.at[k]))
        copies[-1].start()
    copies.append(pltpu.make_async_copy(packed.at[pl.ds(meta[base], LEAD + plan.total)], own, sem_out.at[n]))
    copies[-1].start()
    for copy in copies:
        copy.wait()


def pack_code_grads(plan, meta, og_hbm, *rest):
    n = len(plan.chunks)
    sources, (own, small), rest = rest[:5], rest[6:8], rest[8:]
    sends, rest = rest[:n], rest[n:]
    og_in, packed, sem_in, sem_small = rest[:4]
    held = rest[4:]
    small_fetch = []
    for i in range(5):
        small_fetch.append(pltpu.make_async_copy(sources[i], held[i], sem_small.at[i]))
        small_fetch[-1].start()
    decode_w, weight_mix, project_t, bias_first, bias_mix = held
    pieces = 8
    count = plan.images // pieces
    fetch = []
    for p in range(pieces):
        part = pl.ds(p * count, count)
        fetch.append(pltpu.make_async_copy(og_hbm.at[part], og_in.at[part], sem_in.at[p]))
        fetch[-1].start()
    base = plan.images + n + 1

    def clear(i, carry):
        packed[pl.ds(i * SIDE, SIDE)] = jnp.zeros((SIDE, SIDE, HALF), BF16)
        return carry

    lax.fori_loop(0, packed.shape[0] // SIDE, clear, 0)
    for copy in small_fetch:
        copy.wait()
    side = HALF // 2
    small[0:HALF] = weight_mix[:, :HALF]
    small[HALF : 2 * HALF] = weight_mix[:, HALF:]
    small[2 * HALF : 2 * HALF + side] = project_t[...]
    which = lax.broadcasted_iota(jnp.int32, (SIDE, HALF), 0)
    first, second = bias_first[...].astype(F32), bias_mix[...].astype(F32)
    first = jnp.where(which == 0, first, jnp.where(which == 1, second, 0.0))
    small[2 * HALF + side : 2 * HALF + side + SIDE] = first.astype(BF16)
    w = decode_w[...]
    blank = jnp.zeros_like(w)
    upper = jnp.concatenate([w, blank], axis=0)
    lower = jnp.concatenate([blank, w], axis=0)
    for p in range(pieces):
        fetch[p].wait()
        pack_rows(plan, meta, og_in, packed, p, count)
    for k in range(n):
        half = plan.chunks[k] // 2
        for which in range(2):
            row = LEAD + meta[base + 1 - which] + plan.starts[k]
            a = packed[pl.ds(row, half)].reshape(half * SIDE, HALF)
            b = packed[pl.ds(row + half, half)].reshape(half * SIDE, HALF)
            both = dot(a, upper, NT) + dot(b, lower, NT)
            both = both.reshape(half, SIDE, HALF)
            if which == 0:
                sends[k][...] = both.astype(BF16)
            else:
                own[pl.ds(plan.starts[k] // 2, half)] = both


def prepare_weights(place, own_hbm, far_hbm, far_other_hbm, small, far_small, bias_code, codebook_t, *refs):
    forward, backward, mix, project, bias, book, kernel, far_kernel, sems = refs
    copies = []
    halves = [pl.ds(pl.multiple_of(at * HALF, HALF), HALF) for at in (place[1], 1 - place[1])]
    pairs = [(own_hbm, kernel)]
    pairs += [(source, far_kernel.at[:, rows, :]) for source, rows in zip((far_hbm, far_other_hbm), halves)]
    for i, (source, target) in enumerate(pairs):
        copies.append(pltpu.make_async_copy(source, target, sems.at[i]))
        copies[-1].start()
    for copy in copies:
        copy.wait()
    first = pl.multiple_of(place[0] * HALF, HALF)
    order = (first, HALF - first)
    for tap in range(9):
        for d, source in enumerate((kernel, far_kernel)):
            for c in range(2):
                tile = source[tap, pl.ds(order[c], HALF), :]
                row = tap * 2 * HALF
                forward[row + c * HALF : row + (c + 1) * HALF, d * HALF : (d + 1) * HALF] = tile
                backward[row + d * HALF : row + (d + 1) * HALF, c * HALF : (c + 1) * HALF] = tile.T
    blank = jnp.zeros((HALF, HALF // 2), BF16)
    for d, source in enumerate((small, far_small)):
        rows = pl.ds(d * HALF, HALF)
        for c in range(2):
            mix[rows, c * HALF : (c + 1) * HALF] = source[pl.ds(order[c], HALF), :]
        part = source[2 * HALF : 2 * HALF + HALF // 2, :].T
        project[0, rows, :] = jnp.concatenate([part, blank], axis=1)
        project[1, rows, :] = jnp.concatenate([blank, part], axis=1)
        bias[0:8, d * HALF : (d + 1) * HALF] = source[2 * HALF + HALF // 2 : 2 * HALF + HALF // 2 + SIDE, :].astype(F32)[0:8]
    code = bias_code[...].astype(F32)
    code = jnp.concatenate([code, code], axis=1)
    bias[8:16, :] = jnp.broadcast_to(jnp.concatenate([code, code], axis=1), (8, 2 * HALF))
    book[...] = jnp.concatenate([codebook_t[...], codebook_t[...]], axis=0)


def sum_codes(first, group, heights, codes, og, codebook_t, _, __, grads, hot, cots, sums):
    step = pl.program_id(0)

    @pl.when(step == 0)
    def _():
        sums[...] = jnp.zeros_like(sums)

    spots = SIDE * SIDE
    code_of = numbers(codebook_t.shape[1], spots)
    spot = lax.broadcasted_iota(jnp.int32, (spots, 1), 0)
    for i in range(group):
        live = heights[(first + step) * group + i] * SIDE
        hot[:, i * spots : (i + 1) * spots] = one_hot_columns(codes[i : i + 1, :], code_of)
        cot = og[i].reshape(spots, HALF).astype(F32)
        cots[i * spots : (i + 1) * spots] = jnp.where(spot < live, cot, 0.0).astype(BF16)
    half = sums.shape[0] // 2
    for h in (0, half):
        sums[h : h + half] += dot(hot[h : h + half], cots[...])

    @pl.when(step == pl.num_programs(0) - 1)
    def _():
        total = sums[...]
        book = codebook_t[...].astype(F32)
        w = lax.dot_general(book, total, NN, precision=lax.Precision.HIGHEST, preferred_element_type=F32)
        bias = jnp.sum(total, axis=0, keepdims=True)
        embed = w.shape[0]
        grads[0:embed] = w
        grads[embed : embed + 8] = jnp.broadcast_to(bias, (8, HALF))


def decode_images(plan, steps, heights, codes, codebook_t, decode_w, decode_b, _, decoded, token, table):
    step = pl.program_id(0)
    token[...] = jnp.zeros_like(token)
    group = plan.images // steps

    @pl.when(step == 0)
    def _():
        full = dot(codebook_t[...], decode_w[...], TN) + decode_b[...].astype(F32)
        table[...] = full.T.astype(BF16)

    spots = SIDE * SIDE
    code_of = numbers(codebook_t.shape[1], spots)
    spot = lax.broadcasted_iota(jnp.int32, (spots, 1), 0)
    for i in range(group):
        live = heights[step * group + i] * SIDE
        out = dot(table[...], one_hot_columns(codes[i : i + 1, :], code_of)).T
        decoded[i] = jnp.where(spot < live, out, 0.0).astype(BF16).reshape(SIDE, SIDE, HALF)


def put_codes(code_rows, codes, b, height, dst):
    spot = lax.broadcasted_iota(jnp.int32, (1, SIDE * SIDE), 1)
    lane = lax.broadcasted_iota(jnp.int32, (1, HALF), 1)
    per_row = HALF // SIDE
    row = jnp.where(spot < height * SIDE, codes[pl.ds(b, 1), :], -1)
    turn = lax.rem(dst, per_row) * SIDE
    upper = pltpu.roll(row[:, :HALF], turn, 1)
    lower = pltpu.roll(row[:, HALF:], turn, 1)
    inside = lane >= turn
    pieces = (jnp.where(inside, upper, -1), jnp.where(inside, lower, upper), jnp.where(inside, -1, lower))
    for i, piece in enumerate(pieces):
        target = pl.ds(dst // per_row + i, 1)
        code_rows[target, :] = jnp.where(piece < 0, code_rows[target, :], piece)


def gelu_parts(v):
    square = v * v
    t = jnp.tanh(v * (GELU_SCALE + (GELU_SCALE * GELU_CUBE) * square))
    half = 0.5 + 0.5 * t
    value = v * half
    slope = half + (value - value * half) * (2.0 * GELU_SCALE + (6.0 * GELU_SCALE * GELU_CUBE) * square)
    return value, slope


def main_step(plan, layout, k, waits, *refs):
    first_step = k == 0
    fresh = k in (0, plan.usual)
    final = k == plan.usual - 1
    refs = list(refs[waits:])

    def take(count):
        got = refs[:count]
        del refs[:count]
        return got

    if final:
        place, decode_acc = take(2)
    meta, heights, x_own, x_far, q_own, q_far, codes = take(7)
    kernel_hbm, kernel_t_hbm, mix, project, bias, book = take(6)
    if not first_step:
        x_past, q_past, carry_own, carry_far = take(4)
    if not fresh:
        past_accs = take(5)
    win_own, win_far, next_own, next_far = take(4)
    if final:
        laid_out = take(3)
    if not final:
        sums_out = take(5)
    kernel_acc, mix_acc, project_acc, book_acc, bias_acc = take(5)
    kernel, kernel_t, weight_sems = take(3)
    xo, xf, qo, qf, qd, xc_o, xc_f, qc, code_rows, act3, slope_x, grad3, block_g = take(13)
    second_s, slope_s, low_s, mixed_s, code_s, hot_s, found_s, diff_s, sems = refs

    chunk, start = plan.chunks[k], plan.starts[k]
    images, rows, block = plan.images, plan.rows[k], plan.block[k]
    half = chunk // 2
    spots = block * SIDE
    low = meta[images + k]
    high = meta[images + k + 1]

    copies = [
        (x_own.at[pl.ds(start, LEAD + chunk)], xo.at[pl.ds(0, LEAD + chunk)]),
        (x_far, xf.at[pl.ds(LEAD, chunk)]),
        (q_own.at[pl.ds(start // 2, half)], qo.at[pl.ds(LEAD, half)]),
        (q_far, qf.at[pl.ds(LEAD, half)]),
    ]
    if not first_step:
        past = plan.chunks[k - 1]
        copies += [
            (x_past.at[pl.ds(past - LEAD, LEAD)], xf.at[pl.ds(0, LEAD)]),
            (q_own.at[pl.ds(start // 2 - LEAD, LEAD)], qo.at[pl.ds(0, LEAD)]),
            (q_past.at[pl.ds(past // 2 - LEAD, LEAD)], qf.at[pl.ds(0, LEAD)]),
        ]
    accs = (mix_acc, project_acc, book_acc, bias_acc, kernel_acc)
    early = len(copies)
    if not fresh:
        copies += list(zip(past_accs[1:] + past_accs[:1], accs))
    weight_copies = []
    for i, (source, target) in enumerate(((kernel_hbm, kernel), (kernel_t_hbm, kernel_t))):
        weight_copies.append(pltpu.make_async_copy(source, target, weight_sems.at[i]))
    started = []
    for i, (source, target) in enumerate(copies):
        started.append(pltpu.make_async_copy(source, target, sems.at[i]))
        started[-1].start()
    for copy in weight_copies:
        copy.start()
    started, later = started[:early], started[early:]

    if fresh:
        for acc in accs:
            acc[...] = jnp.zeros(acc.shape, F32)

    blank = jnp.zeros((SIDE, SIDE, HALF), BF16)
    no_row = jnp.full((SIDE, SIDE, HALF), MARK, F32)
    code_rows[...] = jnp.full(code_rows.shape, -1, jnp.int32)
    for r in range(0, rows + 2 * block, SIDE):
        part = pl.ds(r, SIDE)
        xc_o[part] = blank
        xc_f[part] = blank
        if r < rows:
            qc[part] = no_row
    for copy in started:
        copy.wait()

    lane3 = lax.broadcasted_iota(jnp.int32, (1, SIDE, HALF), 2) < HALF // 2

    def spread(r0, count):
        both = (qo[pl.ds(r0, count)] + qf[pl.ds(r0, count)].astype(F32)).reshape(count * SIDE, HALF)
        turned = pltpu.roll(both, HALF // 2, 1).reshape(count, SIDE, HALF)
        both = both.reshape(count, SIDE, HALF)
        return jnp.where(lane3, both, turned), jnp.where(lane3, turned, both)

    upper, lower = spread(LEAD, half)
    qd[pl.ds(LEAD, half)] = upper
    qd[pl.ds(LEAD + half, half)] = lower
    if not first_step:
        _, lower = spread(0, LEAD)
        qd[0:LEAD] = lower

    per_row = HALF // SIDE

    def put(b, dst):
        src = meta[b] - start + LEAD
        xc_o[pl.ds(dst, SIDE)] = xo[pl.ds(src, SIDE)]
        xc_f[pl.ds(dst, SIDE)] = xf[pl.ds(src, SIDE)]
        qc[pl.ds(dst, SIDE)] = qd[pl.ds(src, SIDE)]
        end = dst + heights[b]
        xc_o[pl.ds(end, SIDE)] = blank
        xc_f[pl.ds(end, SIDE)] = blank
        qc[pl.ds(end, SIDE)] = no_row
        put_codes(code_rows, codes, b, heights[b], dst)
        return end + 1

    used = lax.fori_loop(low, high, put, jnp.int32(1))
    blocks = jnp.where(high > low, (used + (block - 1)) // block, 0)

    column = lax.rem(lax.broadcasted_iota(jnp.int32, (TILE, 1), 0), SIDE)
    not_first = column != 0
    not_last = column != SIDE - 1

    def shifted(value):
        back = jnp.where(not_first, pltpu.roll(value, 1, 0), 0.0)
        ahead = jnp.where(not_last, pltpu.roll(value, TILE - 1, 0), 0.0)
        return back.astype(BF16), ahead.astype(BF16)

    edge = jnp.zeros((SIDE, 3 * 2 * HALF), BF16)
    act3[0:SIDE] = edge
    grad3[0:SIDE] = edge
    beyond = pl.multiple_of((blocks * block + 1) * SIDE, SIDE)
    grad3[pl.ds(beyond, SIDE)] = edge

    tiles = range(0, spots, TILE)

    def read_x(r0, t):
        part = pl.ds(r0 + t // SIDE, TILE // SIDE)
        o = xc_o[part].reshape(TILE, HALF)
        f = xc_f[part].reshape(TILE, HALF)
        return jnp.concatenate([o, f], axis=1).astype(F32)

    def at(row, count=block):
        return pl.ds(pl.multiple_of(row * SIDE, SIDE), count * SIDE)

    def tile_at(row, t):
        return pl.ds(pl.multiple_of(row * SIDE, SIDE) + t, TILE)

    def activate(j, carry):
        r0 = j * block
        for t in tiles:
            value, slope = gelu_parts(read_x(r0, t))
            slope_x[tile_at(r0, t), :] = slope
            back, ahead = shifted(value)
            act3[tile_at(r0 + 1, t), 0 : 2 * HALF] = back
            act3[tile_at(r0 + 1, t), 2 * HALF : 4 * HALF] = value.astype(BF16)
            act3[tile_at(r0 + 1, t), 4 * HALF : 6 * HALF] = ahead
        return carry

    fused = k < plan.usual
    lax.fori_loop(0, 2 if fused else blocks + 1, activate, 0)
    for copy in later:
        copy.wait()
    for copy in weight_copies:
        copy.wait()

    bias_first = bias[0:1, :]
    bias_mix = bias[1:2, :]
    bias_code = bias[8:9, 0:HALF]
    lane = lax.broadcasted_iota(jnp.int32, (1, HALF), 1) < HALF // 2
    hb = block // 2
    hs = hb * SIDE

    def add_rows(total, value):
        for i in range(0, value.shape[0], 8):
            part = value[i : i + 8]
            total = part if total is None else total + part
        return total

    half_tiles = range(0, hs, TILE)
    code_of = numbers(book_acc.shape[0], HALF)
    halves = (0, hs)

    def middle(j, carry):
        r0 = j * block
        for i in range(block // per_row):
            row = code_rows[pl.ds(j * (block // per_row) + i, 1), :]
            hot_s[:, i * HALF : (i + 1) * HALF] = one_hot_columns(row, code_of)
        for h in halves:
            found_s[h : h + hs] = dot(book[...], hot_s[:, h : h + hs]).astype(BF16).T
        pre = []
        for h in halves:
            window = jnp.concatenate([act3[at(r0 + i + h // SIDE, hb), :] for i in range(3)], axis=1)
            pre.append(dot(window, kernel[...]))
        for h, part in zip(halves, pre):
            for t in half_tiles:
                value, slope = gelu_parts(part[t : t + TILE] + bias_first)
                second_s[h + t : h + t + TILE] = value.astype(BF16)
                slope_s[h + t : h + t + TILE] = slope
        mixed = [dot(second_s[h : h + hs], mix[...]) for h in halves]
        for h, part in zip(halves, mixed):
            for t in half_tiles:
                low_s[h + t : h + t + TILE] = (read_x(r0, h + t) + part[t : t + TILE] + bias_mix).astype(BF16)
        latents = [dot(low_s[h : h + hs], project[i]) for i, h in enumerate(halves)]
        total = None
        for t in half_tiles:
            first = pl.ds(r0 + t // SIDE, TILE // SIDE)
            other = pl.ds(r0 + hb + t // SIDE, TILE // SIDE)
            ch = jnp.where(lane, found_s[t : t + TILE].astype(F32), found_s[hs + t : hs + t + TILE].astype(F32))
            q = jnp.where(lane3, qc[first], qc[other]).reshape(TILE, HALF)
            live = q < 0.5 * MARK
            latent = latents[0][t : t + TILE] + latents[1][t : t + TILE] + bias_code
            diff = jnp.where(live, latent - ch, 0.0)
            code_grad = jnp.where(live, q + (2.0 * COMMIT) * diff, 0.0)
            code_s[t : t + TILE] = code_grad.astype(BF16)
            total = add_rows(total, code_grad)
            big = diff.astype(BF16).astype(F32)
            small = diff - big
            turned = pltpu.roll(small, HALF // 2, 1)
            diff_s[t : t + TILE] = jnp.where(lane, big, turned).astype(BF16)
            turned = pltpu.roll(big, HALF // 2, 1)
            diff_s[hs + t : hs + t + TILE] = jnp.where(lane, turned, small).astype(BF16)
        bias_acc[16:24, 0:HALF] += total
        total = None
        blocks_g = [dot(code_s[...], project[i], NT) for i in range(2)]
        for h, part in zip(halves, blocks_g):
            for t in half_tiles:
                block_g[tile_at(r0, h + t), :] = part[t : t + TILE]
                mixed_s[h + t : h + t + TILE] = part[t : t + TILE].astype(BF16)
                total = add_rows(total, part[t : t + TILE])
        bias_acc[8:16] += total
        second_grad = [dot(mixed_s[h : h + hs], mix[...], NT) for h in halves]
        total = None
        for h, part in zip(halves, second_grad):
            for t in half_tiles:
                first_grad = slope_s[h + t : h + t + TILE] * part[t : t + TILE]
                back, ahead = shifted(first_grad)
                grad3[tile_at(r0 + 1, h + t), 0 : 2 * HALF] = ahead
                grad3[tile_at(r0 + 1, h + t), 2 * HALF : 4 * HALF] = first_grad.astype(BF16)
                grad3[tile_at(r0 + 1, h + t), 4 * HALF : 6 * HALF] = back
                total = add_rows(total, first_grad)
        bias_acc[0:8] += total
        book_acc[...] += dot(hot_s[...], diff_s[...])
        mix_acc[...] += dot(second_s[...], mixed_s[...], TN)
        project_acc[...] += jnp.where(lane, dot(low_s[0:hs], code_s[...], TN), dot(low_s[hs:], code_s[...], TN))
        return carry

    def finish(j, carry):
        r0 = j * block
        active = act3[at(r0 + 1), 2 * HALF : 4 * HALF].T
        for i in range(3):
            kernel_acc[:, i * 6 * HALF : (i + 1) * 6 * HALF] += dot(active, grad3[at(r0 + 2 - i), :])
        grads = []
        for h in halves:
            window = jnp.concatenate([grad3[at(r0 + 2 - i + h // SIDE, hb), :] for i in range(3)], axis=1)
            grads.append(dot(window, kernel_t[...]))
        for h, grad in zip(halves, grads):
            for t in half_tiles:
                here = tile_at(r0, h + t)
                out = (block_g[here, :] + slope_x[here, :] * grad[t : t + TILE]).astype(BF16)
                part = pl.ds(r0 + (h + t) // SIDE, TILE // SIDE)
                xc_o[part] = out[:, :HALF].reshape(TILE // SIDE, SIDE, HALF)
                xc_f[part] = out[:, HALF:].reshape(TILE // SIDE, SIDE, HALF)
        return carry

    def opening(j, carry):
        middle(j, carry)
        return activate(j + 2, carry)

    def steady(j, carry):
        finish(j - 2, carry)
        middle(j, carry)
        return activate(j + 2, carry)

    if fused:
        lax.fori_loop(0, jnp.minimum(blocks, 2), opening, 0)
        lax.fori_loop(2, blocks, steady, 0)
        lax.fori_loop(jnp.maximum(blocks - 2, 0), blocks, finish, 0)
    else:
        lax.fori_loop(0, blocks, middle, 0)
        lax.fori_loop(0, blocks, finish, 0)
    leaving = []
    if not final:
        leaving += list(zip((kernel_acc, mix_acc, project_acc, book_acc, bias_acc), sums_out))
        for i, (source, target) in enumerate(leaving):
            leaving[i] = pltpu.make_async_copy(source, target, sems.at[i])
            leaving[i].start()

    out_o, out_f = xo, xf
    if first_step:
        out_o[0:LEAD] = blank
        out_f[0:LEAD] = blank
    else:
        out_o[0:LEAD] = carry_own[...]
        out_f[0:LEAD] = carry_far[...]

    def collect(b, src):
        dst = meta[b] - start + LEAD
        out_o[pl.ds(dst, SIDE)] = xc_o[pl.ds(src, SIDE)]
        out_f[pl.ds(dst, SIDE)] = xc_f[pl.ds(src, SIDE)]
        return src + heights[b] + 1

    lax.fori_loop(low, high, collect, jnp.int32(1))
    size = win_own.shape[0]
    windows = (
        (out_o.at[pl.ds(0, size)], win_own),
        (out_f.at[pl.ds(0, size)], win_far),
        (out_o.at[pl.ds(chunk, LEAD)], next_own),
        (out_f.at[pl.ds(chunk, LEAD)], next_far),
    )
    for i, (source, target) in enumerate(windows):
        leaving.append(pltpu.make_async_copy(source, target, sems.at[5 + i]))
        leaving[-1].start()
    if final:
        sums = (kernel_acc, mix_acc, project_acc, book_acc, bias_acc, decode_acc)
        laid_out += [slope_x.at[pl.ds(0, layout.rows), pl.ds(i * HALF, HALF)] for i in range(2)]
        leaving += gather_grads(plan, layout, place, meta, sums, *laid_out, sems)
    for copy in leaving:
        copy.wait()


class Layout:
    def __init__(self, devices, book_rows, embed):
        self.mix = 9 * 2 * HALF
        self.project = self.mix + 2 * HALF
        self.book = self.project + HALF // 2
        self.bias = self.book + book_rows // 2
        self.decode = self.bias + 8
        used = self.decode + embed + 8
        self.devices = devices
        self.piece = -(-used // (devices * SIDE)) * SIDE
        self.rows = self.piece * devices
        self.half = self.rows // 2
        self.used = used


def lay_out(layout, swap, kernel_acc, mix_acc, project_acc, book_acc, bias_acc, decode_acc, own, far):
    def lanes(value):
        return value[:, :HALF], value[:, HALF:]

    def order(first, second):
        return jnp.where(swap, second, first), jnp.where(swap, first, second)

    row = 0
    for tap in range(9):
        block = kernel_acc[:, tap * 2 * HALF : (tap + 1) * 2 * HALF]
        mine, theirs = lanes(block)
        a, b = order(mine[:HALF], mine[HALF:])
        own[row : row + HALF] = a
        own[row + HALF : row + 2 * HALF] = b
        a, b = order(theirs[:HALF], theirs[HALF:])
        far[row : row + HALF] = a
        far[row + HALF : row + 2 * HALF] = b
        row += 2 * HALF
    row = layout.mix
    for target, part in ((own, mix_acc[:HALF]), (far, mix_acc[HALF:])):
        a, b = order(*lanes(part))
        target[row : row + HALF] = a
        target[row + HALF : row + 2 * HALF] = b
    row = layout.project
    side = HALF // 2
    for target, part in ((own, project_acc[:HALF]), (far, project_acc[HALF:])):
        part = part + pltpu.roll(part, side, 1)
        target[row : row + side] = part.T[:side]
    row = layout.book
    book = book_acc[...]
    book = -2.0 * (book + pltpu.roll(book, side, 1))
    book = book.T[:side]
    for c in range(book.shape[1] // HALF):
        part = book[:, c * HALF : (c + 1) * HALF]
        own[row + c * side : row + (c + 1) * side] = part
        far[row + c * side : row + (c + 1) * side] = part
    row = layout.bias
    sums = [jnp.sum(bias_acc[8 * i : 8 * i + 8], axis=0, keepdims=True) for i in range(3)]
    code = sums[2][:, :HALF]
    code = code + pltpu.roll(code, side, 1)
    which = lax.broadcasted_iota(jnp.int32, (8, HALF), 0)
    for target, first in ((own, 0), (far, HALF)):
        part = jnp.where(which == 0, sums[0][:, first : first + HALF], sums[1][:, first : first + HALF])
        target[row : row + 8] = jnp.where(which == 2, code, jnp.where(which < 2, part, 0.0))
    row = layout.decode
    rest = layout.rows - row
    own[row:] = jnp.zeros((rest, HALF), F32)
    far[row:] = jnp.zeros((rest, HALF), F32)
    if decode_acc is not None:
        own[row : row + decode_acc.shape[0]] = decode_acc[...]


def gather_plain(layout, place, *refs):
    lay_out(layout, place[0] == 1, *refs[:5], None, *refs[5:])


def gather_grads(plan, layout, place, meta, accs, keep_own, keep_far, send, own, far, sems):
    lay_out(layout, place[0] == 1, *accs, own, far)
    base = plan.images + len(plan.chunks) + 1
    over = (meta[base + 4] > plan.covered).astype(F32)
    which = lax.broadcasted_iota(jnp.int32, (8, HALF), 0)
    row = layout.bias
    own[row : row + 8] = jnp.where(which == 3, over, own[row : row + 8])
    half = layout.half
    mine = pl.ds(pl.multiple_of(place[1] * half, SIDE), half)
    other = pl.ds(pl.multiple_of((1 - place[1]) * half, SIDE), half)
    kept = []
    for i, (source, target) in enumerate(((own, keep_own), (far, keep_far))):
        kept.append(pltpu.make_async_copy(source.at[mine, :], target, sems.at[9 + i]))
        kept[-1].start()
    send[0] = own[other, :].astype(BF16)
    send[1] = far[other, :].astype(BF16)
    return kept


def hold(*refs):
    pass


def add_far(keep_far, came, out):
    out[...] = (keep_far[...] + came[1].astype(F32)).astype(BF16)


def add_own(keep_own, came, came_far, out, token):
    token[...] = jnp.zeros_like(token)
    total = keep_own[...] + came[0].astype(F32) + came_far[...].astype(F32)
    out[...] = total.astype(BF16).reshape(out.shape)


def add_pieces(pieces, *rest):
    out, token = rest[-2:]
    token[...] = jnp.zeros_like(token)
    total = pieces[0].astype(F32)
    for i in range(1, pieces.shape[0]):
        total = total + pieces[i].astype(F32)
    out[...] = jnp.broadcast_to(total.astype(BF16)[None], out.shape)


def write_grads(layout, place, mine, theirs, kernel, first_bias, mix, mix_bias, project, project_bias, book, decode, decode_bias, whole):
    half = layout.half
    whole[pl.ds(pl.multiple_of(place[1] * half, SIDE), half), :] = mine[...].astype(F32)
    whole[pl.ds(pl.multiple_of((1 - place[1]) * half, SIDE), half), :] = theirs[...].astype(F32)
    split_grads(layout, whole, kernel, first_bias, mix, mix_bias, project, project_bias, book, decode, decode_bias)


def split_grads(layout, whole, kernel, first_bias, mix, mix_bias, project, project_bias, book, decode, decode_bias):
    for tap in range(9):
        kernel[tap] = whole[tap * 2 * HALF : (tap + 1) * 2 * HALF]
    row = layout.mix
    mix[:, :HALF] = whole[row : row + HALF]
    mix[:, HALF:] = whole[row + HALF : row + 2 * HALF]
    side = HALF // 2
    for row, target in ((layout.project, project), (layout.book, book)):
        for c in range(target.shape[1] // HALF):
            target[:, c * HALF : (c + 1) * HALF] = whole[row + c * side : row + (c + 1) * side]
    row = layout.bias
    first_bias[...] = whole[row : row + 1]
    mix_bias[...] = whole[row + 1 : row + 2]
    project_bias[...] = whole[row + 2 : row + 3, :side]
    row = layout.decode
    n = decode.shape[0]
    decode[...] = whole[row : row + n]
    decode_bias[...] = whole[row + n : row + n + 1]


def split_again(layout, total, extra, *refs):
    whole = refs[-1]
    whole[...] = total[...].astype(F32) + extra[...]
    split_grads(layout, whole, *refs[:-1])


def restore_rows(plan, n, waits, *refs):
    meta, heights, *refs = refs[waits:]
    own, far, out, token = refs[:n], refs[n : 2 * n], refs[2 * n], refs[2 * n + 1]
    token[...] = jnp.zeros_like(token)
    stage_own, stage_far, sems = refs[2 * n + 2 :]
    copies = []
    for k in range(n):
        size = plan.chunks[k] + (LEAD if k == n - 1 else 0)
        for i, (source, target) in enumerate(((own[k], stage_own), (far[k], stage_far))):
            from_rows = source.at[pl.ds(0, size)]
            copies.append(pltpu.make_async_copy(from_rows, target.at[pl.ds(plan.starts[k], size)], sems.at[i, k]))
            copies[-1].start()
    for copy in copies:
        copy.wait()
    base = plan.images + len(plan.chunks) + 1
    own_row, send_row = meta[base], meta[base + 1]
    first, last = meta[base + 2], meta[base + 3]
    row_of = lax.broadcasted_iota(jnp.int32, (SIDE, 1, 1), 0)

    def own_image(b, carry):
        rows = stage_own[pl.ds(meta[b] + LEAD, SIDE)]
        out[b] = jnp.where(row_of < heights[b], rows, jnp.zeros_like(rows))
        return carry

    def far_image(b, carry):
        rows = stage_far[pl.ds(meta[b] + own_row - send_row + LEAD, SIDE)]
        out[b] = jnp.where(row_of < heights[b], rows, jnp.zeros_like(rows))
        return carry

    lax.fori_loop(first, last, own_image, 0)
    lax.fori_loop(0, first, far_image, 0)
    lax.fori_loop(last, plan.images, far_image, 0)


def trade(value):
    return lax.ppermute(value, "mp", [(0, 1), (1, 0)])


def held(value, *others):
    return pl.pallas_call(
        hold,
        out_shape=shape(value.shape, value.dtype),
        in_specs=[ANY] * (1 + len(others)),
        out_specs=ANY,
        input_output_aliases={0: 0},
        compiler_params=params(60),
        name="hold",
    )(value, *others)


def run_main(plan, layout, k, meta, heights, streams, weights, state, waits=(), ending=()):
    chunk, rows, block = plan.chunks[k], plan.rows[k], plan.block[k]
    last = k >= plan.usual - 1
    final = k == plan.usual - 1
    x_own, x_far, q_own, q_far, codes = streams
    book_rows = weights[-1].shape[1]
    args = [*waits, *ending, meta, heights, x_own, x_far[k], q_own, q_far[k], codes, *weights]
    specs = [ANY] * len(waits) + ([SMEM, VMEM] if final else [])
    specs += [SMEM, SMEM, ANY, ANY, ANY, ANY, VMEM, ANY, ANY] + [VMEM] * (len(weights) - 2)
    alias = {}
    if state is not None:
        args += [x_far[k - 1], q_far[k - 1], *state]
        specs += [ANY, ANY, VMEM, VMEM] + [ANY] * (len(state) - 2)
        if not final:
            for i in range(len(state) - 2):
                alias[len(args) - 5 + i] = 4 + i
    size = chunk + LEAD if last else chunk
    tile = (SIDE, HALF)
    outs = [shape((size,) + tile, BF16)] * 2 + [shape((LEAD,) + tile, BF16)] * 2
    sums = [(2 * HALF, 18 * HALF), (2 * HALF, 2 * HALF), (2 * HALF, HALF), (book_rows, HALF), (24, 2 * HALF)]
    scratch = [pltpu.VMEM(dims, F32) for dims in sums]
    out_specs = [ANY] * 4
    if final:
        outs += [shape((layout.half, HALF), F32)] * 2 + [shape((2, layout.half, HALF), BF16)]
        out_specs += [ANY, ANY, VMEM]
    else:
        outs += [shape(dims, F32) for dims in sums]
        out_specs += [ANY] * 5
    scratch += [pltpu.VMEM((18 * HALF, 2 * HALF), BF16)] * 2 + [pltpu.SemaphoreType.DMA((2,))]
    half = chunk // 2
    spots = block * SIDE
    scratch += [
        pltpu.VMEM((LEAD + chunk + 2 * SIDE,) + tile, BF16),
        pltpu.VMEM((LEAD + chunk + 2 * SIDE,) + tile, BF16),
        pltpu.VMEM((LEAD + half,) + tile, F32),
        pltpu.VMEM((LEAD + half,) + tile, BF16),
        pltpu.VMEM((LEAD + chunk + SIDE,) + tile, F32),
        pltpu.VMEM((rows + 2 * block + SIDE,) + tile, BF16),
        pltpu.VMEM((rows + 2 * block + SIDE,) + tile, BF16),
        pltpu.VMEM((rows + 2 * SIDE,) + tile, F32),
        pltpu.VMEM((-(-(rows * SIDE // HALF + 4) // 8) * 8, HALF), jnp.int32),
        pltpu.VMEM(((rows + 2 * block + 2) * SIDE, 6 * HALF), BF16),
        pltpu.VMEM(((rows + 2 * block) * SIDE, 2 * HALF), F32),
        pltpu.VMEM(((rows + 2) * SIDE, 6 * HALF), BF16),
        pltpu.VMEM((rows * SIDE, 2 * HALF), F32),
        pltpu.VMEM((spots, 2 * HALF), BF16),
        pltpu.VMEM((spots, 2 * HALF), F32),
        pltpu.VMEM((spots, 2 * HALF), BF16),
        pltpu.VMEM((spots, 2 * HALF), BF16),
        pltpu.VMEM((spots // 2, HALF), BF16),
        pltpu.VMEM((book_rows, spots), BF16),
        pltpu.VMEM((spots, HALF), BF16),
        pltpu.VMEM((spots, HALF), BF16),
        pltpu.SemaphoreType.DMA((13,)),
    ]
    spots = chunk * SIDE
    return pl.pallas_call(
        functools.partial(main_step, plan, layout, k, len(waits)),
        out_shape=outs,
        in_specs=specs,
        out_specs=out_specs,
        scratch_shapes=scratch,
        input_output_aliases=alias,
        compiler_params=params(58),
        cost_estimate=cost(60 * 65536 * spots, 8 * MIB, 2 * 256 * spots),
        name=f"main_{k}",
    )(*args)


def local(
    image_latents,
    image_heights,
    code_index,
    kernel_three,
    bias_three,
    weight_mix,
    bias_mix,
    weight_project,
    bias_project,
    codebook,
    weight_decode,
    bias_decode,
    out_grad,
):
    images = image_latents.shape[0]
    plan = Plan(images)
    n = len(plan.chunks)
    tile = (SIDE, HALF)
    where = lax.axis_index("mp").astype(jnp.int32)
    core = lax.rem(lax.axis_index("dp").astype(jnp.int32), 2)
    spot = place = jnp.stack([where, core])

    devices = lax.axis_size("dp")
    across = [(i, i ^ 1) for i in range(devices)]
    kernel_half = lax.dynamic_slice_in_dim(kernel_three, core * HALF, HALF, 1)
    far_kernel = trade(kernel_half)
    far_kernel_other = lax.ppermute(far_kernel, "dp", across)

    packed = pl.pallas_call(
        functools.partial(pack_latents, plan),
        out_shape=[
            shape((meta_size(plan),), jnp.int32),
            shape((LEAD + plan.total,) + tile, BF16),
        ]
        + [shape((c,) + tile, BF16) for c in plan.chunks],
        in_specs=[SMEM, SMEM, HBM, ANY],
        out_specs=[SMEM, ANY] + [ANY] * n,
        scratch_shapes=[
            pltpu.VMEM((images, SIDE) + tile, BF16),
            pltpu.VMEM((plan.packed + SIDE,) + tile, BF16),
            pltpu.SemaphoreType.DMA((8,)),
            pltpu.SemaphoreType.DMA((n + 1,)),
        ],
        compiler_params=params(60),
        cost_estimate=cost(0, 12 * MIB),
        name="pack_latents",
    )(image_heights, place, image_latents, kernel_half)
    meta, x_own, x_send = packed[0], packed[1], packed[2:]

    packed = pl.pallas_call(
        functools.partial(pack_code_grads, plan),
        out_shape=[shape((plan.total // 2,) + tile, F32), shape((2 * HALF + HALF // 2 + SIDE, HALF), BF16)]
        + [shape((c // 2,) + tile, BF16) for c in plan.chunks],
        in_specs=[SMEM] + [HBM] * 6 + [ANY],
        out_specs=[VMEM] * (n + 2),
        scratch_shapes=[
            pltpu.VMEM((images, SIDE) + tile, BF16),
            pltpu.VMEM((plan.packed + SIDE,) + tile, BF16),
            pltpu.SemaphoreType.DMA((8,)),
            pltpu.SemaphoreType.DMA((5,)),
            pltpu.VMEM(weight_decode.shape, BF16),
            pltpu.VMEM(weight_mix.shape, BF16),
            pltpu.VMEM(weight_project.shape[::-1], BF16),
            pltpu.VMEM((1, HALF), BF16),
            pltpu.VMEM((1, HALF), BF16),
        ],
        compiler_params=params(60),
        cost_estimate=cost(2 * 2 * plan.total * SIDE * 256 * 128, 10 * MIB),
        name="pack_code_grads",
    )(meta, out_grad, weight_decode, weight_mix, weight_project.T, bias_three.reshape(1, HALF), bias_mix.reshape(1, HALF), far_kernel)
    q_own, small, q_send = packed[0], packed[1], packed[2:]

    book_rows, embed = codebook.shape
    codebook_t = codebook.T
    far_small = trade(small)
    usual = plan.usual
    x_far, q_far = [], []
    x_far.append(trade(x_send[0]))
    q_far.append(trade(q_send[0]))

    weights = pl.pallas_call(
        prepare_weights,
        out_shape=[
            shape((18 * HALF, 2 * HALF), BF16),
            shape((18 * HALF, 2 * HALF), BF16),
            shape((2 * HALF, 2 * HALF), BF16),
            shape((2, 2 * HALF, HALF), BF16),
            shape((SIDE, 2 * HALF), F32),
            shape((HALF, book_rows), BF16),
        ],
        in_specs=[SMEM, HBM, HBM, HBM] + [VMEM] * 4,
        out_specs=[VMEM] * 6,
        scratch_shapes=[pltpu.VMEM(kernel_three.shape, BF16)] * 2 + [pltpu.SemaphoreType.DMA((3,))],
        compiler_params=params(20),
        cost_estimate=cost(0, 5 * MIB),
        name="prepare_weights",
    )(place, kernel_three, far_kernel, far_kernel_other, small, far_small, bias_project.reshape(1, -1), codebook_t)

    groups = 8
    group = images // groups
    codes = code_index.reshape(images, SIDE * SIDE)
    whole = lambda dims: pl.BlockSpec(dims, lambda g: (0,) * len(dims))
    four = pl.BlockSpec((group, SIDE) + tile, lambda g: (g, 0, 0, 0))
    row = pl.BlockSpec((group, SIDE * SIDE), lambda g: (g, 0))
    def code_sums(first, steps):
        return pl.pallas_call(
            functools.partial(sum_codes, first, group),
            grid=(steps,),
            out_shape=shape((embed + 8, HALF), F32),
            in_specs=[
                SMEM,
                pl.BlockSpec((group, SIDE * SIDE), lambda g: (g + first, 0)),
                pl.BlockSpec((group, SIDE) + tile, lambda g: (g + first, 0, 0, 0)),
                whole((embed, book_rows)),
                ANY,
                ANY,
            ],
            out_specs=whole((embed + 8, HALF)),
            scratch_shapes=[
                pltpu.VMEM((book_rows, group * SIDE * SIDE), BF16),
                pltpu.VMEM((group * SIDE * SIDE, HALF), BF16),
                pltpu.VMEM((book_rows, HALF), F32),
            ],
            compiler_params=params(60),
            cost_estimate=cost(steps * group * 256 * 512 * 256, steps * group * 65536),
            name=f"sum_codes_{first}",
        )(image_heights, codes, out_grad, codebook_t, small, far_kernel)

    def decode(after):
        return pl.pallas_call(
            functools.partial(decode_images, plan, groups),
            grid=(groups,),
            out_shape=[shape((images, SIDE) + tile, BF16), shape((8, HALF), F32)],
            in_specs=[SMEM, row, whole((embed, book_rows)), whole((embed, HALF)), whole((1, HALF)), whole((8, HALF))],
            out_specs=[four, whole((8, HALF))],
            scratch_shapes=[pltpu.VMEM((HALF, book_rows), BF16)],
            compiler_params=params(32),
            cost_estimate=cost(images * 256 * 512 * 256, 5 * MIB),
            name="decode_images",
        )(image_heights, codes, codebook_t, weight_decode, bias_decode.reshape(1, HALF), after)

    decode_acc = code_sums(0, groups)
    for k in range(1, usual):
        x_far.append(trade(held(x_send[k], decode_acc, far_small, x_far[0], q_far[0])))
        q_far.append(trade(held(q_send[k], decode_acc, far_small, x_far[0], q_far[0])))

    layout = Layout(devices, book_rows, embed)
    half, piece, chips = layout.half, layout.piece, devices // 2
    streams = (x_own, x_far, q_own, q_far, codes)
    state = None
    win_own, win_far = [], []
    for k in range(usual):
        waits = win_far[k - 2 : k - 1] if k > 1 else []
        ending = (spot, decode_acc) if k == usual - 1 else ()
        outs = run_main(plan, layout, k, meta, image_heights, streams, weights, state, waits, ending)
        win_own.append(outs[0])
        if k < usual - 1:
            win_far.append(trade(outs[1]))
        state = outs[2:]
    last_window = outs[1]
    carry, (keep_own, keep_far, send) = state[:2], state[2:]

    def restore(own, far, waits=()):
        count = len(own)
        return pl.pallas_call(
            functools.partial(restore_rows, plan, count, len(waits)),
            out_shape=[shape((images, SIDE) + tile, BF16), shape((8, HALF), F32)],
            in_specs=[VMEM] * len(waits) + [SMEM, SMEM] + [ANY] * (2 * count),
            out_specs=[VMEM, VMEM],
            scratch_shapes=[
                pltpu.VMEM((plan.total + LEAD + SIDE,) + tile, BF16),
                pltpu.VMEM((plan.total + LEAD + SIDE,) + tile, BF16),
                pltpu.SemaphoreType.DMA((2, count)),
            ],
            compiler_params=params(60),
            cost_estimate=cost(0, 10 * MIB),
            name="restore_rows",
        )(*waits, meta, image_heights, *own, *far)


    def step(body, out, name, *args, waits=()):
        specs = [VMEM] * len(args) + [VMEM if wait.size <= 1 << 14 else ANY for wait in waits]
        args = (*args, *waits)
        return pl.pallas_call(
            body,
            out_shape=out,
            in_specs=specs,
            out_specs=[VMEM] * len(out) if isinstance(out, list) else VMEM,
            compiler_params=params(24),
            cost_estimate=cost(0, 2 * MIB),
            name=name,
        )(*args)

    send = held(send, win_far[usual - 2])
    came = lax.ppermute(send, "dp", across)
    win_far.append(trade(last_window))
    far_sums = step(add_far, shape((half, HALF), BF16), "add_far", keep_far, came)
    came_far = trade(far_sums)
    parts = [shape((chips, piece, HALF), BF16), shape((8, HALF), F32)]
    mine, token = step(add_own, parts, "add_own", keep_own, came, came_far)
    decoded, token = decode(token)
    cores = [[i for i in range(devices) if i % 2 == c] for c in range(2)]
    mine = lax.all_to_all(mine, "dp", 0, 0, axis_index_groups=cores, tiled=True)
    mine, token = step(add_pieces, parts, "add_pieces", mine, waits=[token, win_far[usual - 1]])
    latents_grad, token = restore(win_own, win_far, [token])
    mine = lax.all_to_all(mine, "dp", 0, 0, axis_index_groups=cores, tiled=True)
    mine = held(mine, token).reshape(half, HALF)
    theirs = lax.ppermute(mine, "dp", across)

    grads_out = [
        shape((9, 2 * HALF, HALF), F32),
        shape((1, HALF), F32),
        shape((HALF, 2 * HALF), F32),
        shape((1, HALF), F32),
        shape((embed, HALF), F32),
        shape((1, embed), F32),
        shape((embed, book_rows), F32),
        shape((embed, HALF), F32),
        shape((1, HALF), F32),
    ]
    whole = pltpu.VMEM((layout.rows, HALF), F32)

    def usual_end(latents_grad):
        grads = pl.pallas_call(
            functools.partial(write_grads, layout),
            out_shape=grads_out,
            in_specs=[SMEM, VMEM, VMEM],
            out_specs=[VMEM] * 9,
            scratch_shapes=[whole],
            compiler_params=params(24),
            cost_estimate=cost(0, 4 * MIB),
            name="write_grads",
        )(spot, mine, theirs)
        return (latents_grad, *grads)

    def longer_end(latents_grad):
        last_x, last_q = trade(x_send[usual]), trade(q_send[usual])
        streams = (x_own, x_far + [last_x], q_own, q_far + [last_q], codes)
        outs = run_main(plan, layout, usual, meta, image_heights, streams, weights, carry)
        latents_grad, _ = restore(win_own + [outs[0]], win_far + [trade(outs[1])])
        own, far = pl.pallas_call(
            functools.partial(gather_plain, layout),
            out_shape=[shape((layout.rows, HALF), F32)] * 2,
            in_specs=[SMEM] + [VMEM] * 5,
            out_specs=[VMEM] * 2,
            compiler_params=params(40),
            name="gather_plain",
        )(spot, *outs[4:])
        extra = lax.psum(own + trade(far), "dp")
        first, second = jnp.where(core == 0, mine, theirs), jnp.where(core == 0, theirs, mine)
        grads = pl.pallas_call(
            functools.partial(split_again, layout),
            out_shape=grads_out,
            in_specs=[VMEM, VMEM],
            out_specs=[VMEM] * 9,
            scratch_shapes=[whole],
            compiler_params=params(24),
            name="split_again",
        )(jnp.concatenate([first, second]), extra)
        return (latents_grad, *grads)

    flag = layout.bias + 3
    holder = flag // half
    flags = jnp.where(core == holder, mine[flag - holder * half, 0], theirs[flag - holder * half, 0])
    ends = lax.cond(flags.astype(F32) > 0.5, longer_end, usual_end, latents_grad)
    latents_grad, kernel_grad, first_bias, mix_grad, mix_bias, project_grad, project_bias, book, decode, decode_bias = ends
    return (
        decoded,
        latents_grad,
        kernel_grad,
        first_bias.reshape(HALF),
        mix_grad,
        mix_bias.reshape(HALF),
        project_grad.T,
        project_bias.reshape(embed),
        book.T,
        decode,
        decode_bias.reshape(HALF),
    )


def solution(mesh):
    tile = P("dp", None, None, "mp")
    placed = (
        tile,
        P("dp"),
        P("dp", None, None),
        P(None, None, "mp"),
        P("mp"),
        P("mp", None),
        P("mp"),
        P("mp", None),
        P(),
        P(),
        P(None, "mp"),
        P("mp"),
        tile,
    )
    outs = (
        tile,
        tile,
        P(None, None, "mp"),
        P("mp"),
        P("mp", None),
        P("mp"),
        P("mp", None),
        P(),
        P(),
        P(None, "mp"),
        P("mp"),
    )
    return jax.shard_map(local, mesh=mesh, in_specs=placed, out_specs=outs, check_vma=False)
```

```python
import functools

import jax
import jax.numpy as jnp
from jax import lax
from jax.experimental import pallas as pl
from jax.experimental.pallas import tpu as pltpu
from jax.sharding import PartitionSpec as P

SIDE = 16
HALF = 128
LEAD = 16
BLOCK = 32
TILE = 32
MARK = 1e9
GELU_SCALE = 0.7978845608028654
GELU_CUBE = 0.044715
COMMIT = 0.25
F32 = jnp.float32
BF16 = jnp.bfloat16
ANY = pl.BlockSpec(memory_space=pl.ANY)
SMEM = pl.BlockSpec(memory_space=pltpu.SMEM)
HBM = pl.BlockSpec(memory_space=pltpu.HBM)
VMEM = pl.BlockSpec(memory_space=pltpu.VMEM)
MIB = 1 << 20

NT = (((1,), (1,)), ((), ()))
TN = (((0,), (0,)), ((), ()))
NN = (((1,), (0,)), ((), ()))


def dot(a, b, dims=NN):
    return lax.dot_general(a, b, dims, preferred_element_type=F32)


def one_hot_columns(codes, code_of):
    return jnp.where(code_of == codes.astype(jnp.int16), jnp.bfloat16(1), jnp.bfloat16(0))


def numbers(count, width):
    return lax.broadcasted_iota(jnp.int32, (count, width), 0).astype(jnp.int16)


def shape(dims, kind):
    return jax.ShapeDtypeStruct(dims, kind)


def params(mib):
    return pltpu.CompilerParams(vmem_limit_bytes=mib * MIB)


def cost(flops, moved, slow=0):
    return pl.CostEstimate(flops=flops, bytes_accessed=moved, transcendentals=slow)


class Plan:
    def __init__(self, images):
        self.images = images
        longest = images * SIDE // 2 + SIDE // 2
        part = images // 8
        self.chunks = [18 * part, 29 * part]
        self.usual = len(self.chunks)
        rest = longest - sum(self.chunks)
        self.chunks.append(rest)
        self.starts = [sum(self.chunks[:k]) for k in range(len(self.chunks))]
        self.total = sum(self.chunks)
        self.packed = -(-(LEAD + longest + self.total + LEAD) // SIDE) * SIDE
        self.rows, self.block = [], []
        for k, c in enumerate(self.chunks):
            block = BLOCK if k < self.usual else SIDE
            most = 1 + c + 15 + c // 4 + 1
            self.rows.append(-(-most // block) * block)
            self.block.append(block)
        self.covered = sum(self.chunks[: self.usual])


def meta_size(plan):
    return plan.images + len(plan.chunks) + 1 + 5


def plan_rows(plan, heights, place, meta):
    images = plan.images
    base = images + len(plan.chunks) + 1

    def total_of(b, acc):
        return acc + heights[b]

    total = lax.fori_loop(0, images, total_of, jnp.int32(0))

    def split_of(b, state):
        acc, best, split, cut = state
        acc = acc + heights[b]
        worst = jnp.maximum(acc, total - acc)
        better = worst < best
        return (acc, jnp.where(better, worst, best), jnp.where(better, b + 1, split), jnp.where(better, acc, cut))

    _, _, split, cut = lax.fori_loop(0, images, split_of, (jnp.int32(0), jnp.int32(1 << 20), jnp.int32(0), jnp.int32(0)))
    mine = place[0]
    own_first = jnp.where(mine == 0, 0, split)
    own_last = jnp.where(mine == 0, split, images)
    own_row = jnp.where(mine == 0, 0, cut)
    send_row = jnp.where(mine == 0, cut, 0)
    for k in range(len(plan.chunks) + 1):
        meta[images + k] = own_first
    ends = [plan.starts[k] + plan.chunks[k] for k in range(len(plan.chunks))]

    def place_of(b, acc):
        meta[b] = acc - own_row
        acc = acc + heights[b]
        end = acc - own_row
        inside = jnp.logical_and(b >= own_first, b < own_last)
        step = jnp.int32(0)
        for k in range(len(plan.chunks) - 1):
            step = step + (end > ends[k]).astype(jnp.int32)

        @pl.when(inside)
        def _():
            meta[images + 1 + step] = b + 1

        return acc

    lax.fori_loop(0, images, place_of, jnp.int32(0))
    for k in range(len(plan.chunks)):
        meta[images + k + 1] = jnp.maximum(meta[images + k + 1], meta[images + k])
    meta[base] = own_row
    meta[base + 1] = send_row
    meta[base + 2] = own_first
    meta[base + 3] = own_last
    meta[base + 4] = jnp.maximum(cut, total - cut)


def pack_rows(plan, meta, source, packed, piece, count):
    base = plan.images + len(plan.chunks) + 1

    def one(i, carry):
        b = piece * count + i
        row = meta[b] + meta[base] + LEAD
        packed[pl.ds(row, SIDE)] = source[b]
        return carry

    lax.fori_loop(0, count, one, 0)


def pack_latents(plan, heights, place, x_hbm, _, meta, own, *rest):
    n = len(plan.chunks)
    sends, (x_in, packed, sem_in, sem_out) = rest[:n], rest[n:]
    pieces = 8
    count = plan.images // pieces
    fetch = []
    for p in range(pieces):
        part = pl.ds(p * count, count)
        fetch.append(pltpu.make_async_copy(x_hbm.at[part], x_in.at[part], sem_in.at[p]))
        fetch[-1].start()
    plan_rows(plan, heights, place, meta)
    base = plan.images + n + 1
    for p in range(pieces):
        fetch[p].wait()
        pack_rows(plan, meta, x_in, packed, p, count)
    copies = []
    for k in range(n):
        part = pl.ds(LEAD + meta[base + 1] + plan.starts[k], plan.chunks[k])
        copies.append(pltpu.make_async_copy(packed.at[part], sends[k], sem_out.at[k]))
        copies[-1].start()
    copies.append(pltpu.make_async_copy(packed.at[pl.ds(meta[base], LEAD + plan.total)], own, sem_out.at[n]))
    copies[-1].start()
    for copy in copies:
        copy.wait()


def pack_code_grads(plan, meta, og_hbm, *rest):
    n = len(plan.chunks)
    sources, (own, small), rest = rest[:5], rest[6:8], rest[8:]
    sends, rest = rest[:n], rest[n:]
    og_in, packed, sem_in, sem_small = rest[:4]
    held = rest[4:]
    small_fetch = []
    for i in range(5):
        small_fetch.append(pltpu.make_async_copy(sources[i], held[i], sem_small.at[i]))
        small_fetch[-1].start()
    decode_w, weight_mix, project_t, bias_first, bias_mix = held
    pieces = 8
    count = plan.images // pieces
    fetch = []
    for p in range(pieces):
        part = pl.ds(p * count, count)
        fetch.append(pltpu.make_async_copy(og_hbm.at[part], og_in.at[part], sem_in.at[p]))
        fetch[-1].start()
    base = plan.images + n + 1

    def clear(i, carry):
        packed[pl.ds(i * SIDE, SIDE)] = jnp.zeros((SIDE, SIDE, HALF), BF16)
        return carry

    lax.fori_loop(0, packed.shape[0] // SIDE, clear, 0)
    for copy in small_fetch:
        copy.wait()
    side = HALF // 2
    small[0:HALF] = weight_mix[:, :HALF]
    small[HALF : 2 * HALF] = weight_mix[:, HALF:]
    small[2 * HALF : 2 * HALF + side] = project_t[...]
    which = lax.broadcasted_iota(jnp.int32, (SIDE, HALF), 0)
    first, second = bias_first[...].astype(F32), bias_mix[...].astype(F32)
    first = jnp.where(which == 0, first, jnp.where(which == 1, second, 0.0))
    small[2 * HALF + side : 2 * HALF + side + SIDE] = first.astype(BF16)
    w = decode_w[...]
    blank = jnp.zeros_like(w)
    upper = jnp.concatenate([w, blank], axis=0)
    lower = jnp.concatenate([blank, w], axis=0)
    for p in range(pieces):
        fetch[p].wait()
        pack_rows(plan, meta, og_in, packed, p, count)
    for k in range(n):
        half = plan.chunks[k] // 2
        for which in range(2):
            row = LEAD + meta[base + 1 - which] + plan.starts[k]
            a = packed[pl.ds(row, half)].reshape(half * SIDE, HALF)
            b = packed[pl.ds(row + half, half)].reshape(half * SIDE, HALF)
            both = dot(a, upper, NT) + dot(b, lower, NT)
            both = both.reshape(half, SIDE, HALF)
            if which == 0:
                sends[k][...] = both.astype(BF16)
            else:
                own[pl.ds(plan.starts[k] // 2, half)] = both


def prepare_weights(place, own_hbm, far_hbm, far_other_hbm, small, far_small, bias_code, codebook_t, *refs):
    forward, backward, mix, project, bias, book, kernel, far_kernel, sems = refs
    copies = []
    halves = [pl.ds(pl.multiple_of(at * HALF, HALF), HALF) for at in (place[1], 1 - place[1])]
    pairs = [(own_hbm, kernel)]
    pairs += [(source, far_kernel.at[:, rows, :]) for source, rows in zip((far_hbm, far_other_hbm), halves)]
    for i, (source, target) in enumerate(pairs):
        copies.append(pltpu.make_async_copy(source, target, sems.at[i]))
        copies[-1].start()
    for copy in copies:
        copy.wait()
    first = pl.multiple_of(place[0] * HALF, HALF)
    order = (first, HALF - first)
    for tap in range(9):
        for d, source in enumerate((kernel, far_kernel)):
            for c in range(2):
                tile = source[tap, pl.ds(order[c], HALF), :]
                row = tap * 2 * HALF
                forward[row + c * HALF : row + (c + 1) * HALF, d * HALF : (d + 1) * HALF] = tile
                backward[row + d * HALF : row + (d + 1) * HALF, c * HALF : (c + 1) * HALF] = tile.T
    blank = jnp.zeros((HALF, HALF // 2), BF16)
    for d, source in enumerate((small, far_small)):
        rows = pl.ds(d * HALF, HALF)
        for c in range(2):
            mix[rows, c * HALF : (c + 1) * HALF] = source[pl.ds(order[c], HALF), :]
        part = source[2 * HALF : 2 * HALF + HALF // 2, :].T
        project[0, rows, :] = jnp.concatenate([part, blank], axis=1)
        project[1, rows, :] = jnp.concatenate([blank, part], axis=1)
        bias[0:8, d * HALF : (d + 1) * HALF] = source[2 * HALF + HALF // 2 : 2 * HALF + HALF // 2 + SIDE, :].astype(F32)[0:8]
    code = bias_code[...].astype(F32)
    code = jnp.concatenate([code, code], axis=1)
    bias[8:16, :] = jnp.broadcast_to(jnp.concatenate([code, code], axis=1), (8, 2 * HALF))
    book[...] = jnp.concatenate([codebook_t[...], codebook_t[...]], axis=0)


def sum_codes(first, group, heights, codes, og, codebook_t, _, __, grads, hot, cots, sums):
    step = pl.program_id(0)

    @pl.when(step == 0)
    def _():
        sums[...] = jnp.zeros_like(sums)

    spots = SIDE * SIDE
    code_of = numbers(codebook_t.shape[1], spots)
    spot = lax.broadcasted_iota(jnp.int32, (spots, 1), 0)
    for i in range(group):
        live = heights[(first + step) * group + i] * SIDE
        hot[:, i * spots : (i + 1) * spots] = one_hot_columns(codes[i : i + 1, :], code_of)
        cot = og[i].reshape(spots, HALF).astype(F32)
        cots[i * spots : (i + 1) * spots] = jnp.where(spot < live, cot, 0.0).astype(BF16)
    half = sums.shape[0] // 2
    for h in (0, half):
        sums[h : h + half] += dot(hot[h : h + half], cots[...])

    @pl.when(step == pl.num_programs(0) - 1)
    def _():
        total = sums[...]
        book = codebook_t[...].astype(F32)
        w = lax.dot_general(book, total, NN, precision=lax.Precision.HIGHEST, preferred_element_type=F32)
        bias = jnp.sum(total, axis=0, keepdims=True)
        embed = w.shape[0]
        grads[0:embed] = w
        grads[embed : embed + 8] = jnp.broadcast_to(bias, (8, HALF))


def decode_images(plan, steps, heights, codes, codebook_t, decode_w, decode_b, _, decoded, token, table):
    step = pl.program_id(0)
    token[...] = jnp.zeros_like(token)
    group = plan.images // steps

    @pl.when(step == 0)
    def _():
        full = dot(codebook_t[...], decode_w[...], TN) + decode_b[...].astype(F32)
        table[...] = full.T.astype(BF16)

    spots = SIDE * SIDE
    code_of = numbers(codebook_t.shape[1], spots)
    spot = lax.broadcasted_iota(jnp.int32, (spots, 1), 0)
    for i in range(group):
        live = heights[step * group + i] * SIDE
        out = dot(table[...], one_hot_columns(codes[i : i + 1, :], code_of)).T
        decoded[i] = jnp.where(spot < live, out, 0.0).astype(BF16).reshape(SIDE, SIDE, HALF)


def put_codes(code_rows, codes, b, height, dst):
    spot = lax.broadcasted_iota(jnp.int32, (1, SIDE * SIDE), 1)
    lane = lax.broadcasted_iota(jnp.int32, (1, HALF), 1)
    per_row = HALF // SIDE
    row = jnp.where(spot < height * SIDE, codes[pl.ds(b, 1), :], -1)
    turn = lax.rem(dst, per_row) * SIDE
    upper = pltpu.roll(row[:, :HALF], turn, 1)
    lower = pltpu.roll(row[:, HALF:], turn, 1)
    inside = lane >= turn
    pieces = (jnp.where(inside, upper, -1), jnp.where(inside, lower, upper), jnp.where(inside, -1, lower))
    for i, piece in enumerate(pieces):
        target = pl.ds(dst // per_row + i, 1)
        code_rows[target, :] = jnp.where(piece < 0, code_rows[target, :], piece)


def gelu_parts(v):
    square = v * v
    t = jnp.tanh(v * (GELU_SCALE + (GELU_SCALE * GELU_CUBE) * square))
    half = 0.5 + 0.5 * t
    value = v * half
    slope = half + (value - value * half) * (2.0 * GELU_SCALE + (6.0 * GELU_SCALE * GELU_CUBE) * square)
    return value, slope


def main_step(plan, layout, k, waits, *refs):
    first_step = k == 0
    fresh = k in (0, plan.usual)
    final = k == plan.usual - 1
    refs = list(refs[waits:])

    def take(count):
        got = refs[:count]
        del refs[:count]
        return got

    if final:
        place, decode_acc = take(2)
    meta, heights, x_own, x_far, q_own, q_far, codes = take(7)
    kernel_hbm, kernel_t_hbm, mix, project, bias, book = take(6)
    if not first_step:
        x_past, q_past, carry_own, carry_far = take(4)
    if not fresh:
        past_accs = take(5)
    win_own, win_far, next_own, next_far = take(4)
    if final:
        laid_out = take(3)
    if not final:
        sums_out = take(5)
    kernel_acc, mix_acc, project_acc, book_acc, bias_acc = take(5)
    kernel, kernel_t, weight_sems = take(3)
    xo, xf, qo, qf, qd, xc_o, xc_f, qc, code_rows, act3, slope_x, grad3, block_g = take(13)
    second_s, slope_s, low_s, mixed_s, code_s, hot_s, found_s, diff_s, sems = refs

    chunk, start = plan.chunks[k], plan.starts[k]
    images, rows, block = plan.images, plan.rows[k], plan.block[k]
    half = chunk // 2
    spots = block * SIDE
    low = meta[images + k]
    high = meta[images + k + 1]

    copies = [
        (x_own.at[pl.ds(start, LEAD + chunk)], xo.at[pl.ds(0, LEAD + chunk)]),
        (x_far, xf.at[pl.ds(LEAD, chunk)]),
        (q_own.at[pl.ds(start // 2, half)], qo.at[pl.ds(LEAD, half)]),
        (q_far, qf.at[pl.ds(LEAD, half)]),
    ]
    if not first_step:
        past = plan.chunks[k - 1]
        copies += [
            (x_past.at[pl.ds(past - LEAD, LEAD)], xf.at[pl.ds(0, LEAD)]),
            (q_own.at[pl.ds(start // 2 - LEAD, LEAD)], qo.at[pl.ds(0, LEAD)]),
            (q_past.at[pl.ds(past // 2 - LEAD, LEAD)], qf.at[pl.ds(0, LEAD)]),
        ]
    accs = (mix_acc, project_acc, book_acc, bias_acc, kernel_acc)
    early = len(copies)
    if not fresh:
        copies += list(zip(past_accs[1:] + past_accs[:1], accs))
    weight_copies = []
    for i, (source, target) in enumerate(((kernel_hbm, kernel), (kernel_t_hbm, kernel_t))):
        weight_copies.append(pltpu.make_async_copy(source, target, weight_sems.at[i]))
    started = []
    for i, (source, target) in enumerate(copies):
        started.append(pltpu.make_async_copy(source, target, sems.at[i]))
        started[-1].start()
    for copy in weight_copies:
        copy.start()
    started, later = started[:early], started[early:]

    if fresh:
        for acc in accs:
            acc[...] = jnp.zeros(acc.shape, F32)

    blank = jnp.zeros((SIDE, SIDE, HALF), BF16)
    no_row = jnp.full((SIDE, SIDE, HALF), MARK, F32)
    code_rows[...] = jnp.full(code_rows.shape, -1, jnp.int32)
    for r in range(0, rows + 2 * block, SIDE):
        part = pl.ds(r, SIDE)
        xc_o[part] = blank
        xc_f[part] = blank
        if r < rows:
            qc[part] = no_row
    for copy in started:
        copy.wait()

    lane3 = lax.broadcasted_iota(jnp.int32, (1, SIDE, HALF), 2) < HALF // 2

    def spread(r0, count):
        both = (qo[pl.ds(r0, count)] + qf[pl.ds(r0, count)].astype(F32)).reshape(count * SIDE, HALF)
        turned = pltpu.roll(both, HALF // 2, 1).reshape(count, SIDE, HALF)
        both = both.reshape(count, SIDE, HALF)
        return jnp.where(lane3, both, turned), jnp.where(lane3, turned, both)

    upper, lower = spread(LEAD, half)
    qd[pl.ds(LEAD, half)] = upper
    qd[pl.ds(LEAD + half, half)] = lower
    if not first_step:
        _, lower = spread(0, LEAD)
        qd[0:LEAD] = lower

    per_row = HALF // SIDE

    def put(b, dst):
        src = meta[b] - start + LEAD
        xc_o[pl.ds(dst, SIDE)] = xo[pl.ds(src, SIDE)]
        xc_f[pl.ds(dst, SIDE)] = xf[pl.ds(src, SIDE)]
        qc[pl.ds(dst, SIDE)] = qd[pl.ds(src, SIDE)]
        end = dst + heights[b]
        xc_o[pl.ds(end, SIDE)] = blank
        xc_f[pl.ds(end, SIDE)] = blank
        qc[pl.ds(end, SIDE)] = no_row
        put_codes(code_rows, codes, b, heights[b], dst)
        return end + 1

    used = lax.fori_loop(low, high, put, jnp.int32(1))
    blocks = jnp.where(high > low, (used + (block - 1)) // block, 0)

    column = lax.rem(lax.broadcasted_iota(jnp.int32, (TILE, 1), 0), SIDE)
    not_first = column != 0
    not_last = column != SIDE - 1

    def shifted(value):
        back = jnp.where(not_first, pltpu.roll(value, 1, 0), 0.0)
        ahead = jnp.where(not_last, pltpu.roll(value, TILE - 1, 0), 0.0)
        return back.astype(BF16), ahead.astype(BF16)

    edge = jnp.zeros((SIDE, 3 * 2 * HALF), BF16)
    act3[0:SIDE] = edge
    grad3[0:SIDE] = edge
    beyond = pl.multiple_of((blocks * block + 1) * SIDE, SIDE)
    grad3[pl.ds(beyond, SIDE)] = edge

    tiles = range(0, spots, TILE)

    def read_x(r0, t):
        part = pl.ds(r0 + t // SIDE, TILE // SIDE)
        o = xc_o[part].reshape(TILE, HALF)
        f = xc_f[part].reshape(TILE, HALF)
        return jnp.concatenate([o, f], axis=1).astype(F32)

    def at(row, count=block):
        return pl.ds(pl.multiple_of(row * SIDE, SIDE), count * SIDE)

    def tile_at(row, t):
        return pl.ds(pl.multiple_of(row * SIDE, SIDE) + t, TILE)

    def activate(j, carry):
        r0 = j * block
        for t in tiles:
            value, slope = gelu_parts(read_x(r0, t))
            slope_x[tile_at(r0, t), :] = slope
            back, ahead = shifted(value)
            act3[tile_at(r0 + 1, t), 0 : 2 * HALF] = back
            act3[tile_at(r0 + 1, t), 2 * HALF : 4 * HALF] = value.astype(BF16)
            act3[tile_at(r0 + 1, t), 4 * HALF : 6 * HALF] = ahead
        return carry

    fused = k < plan.usual
    lax.fori_loop(0, 2 if fused else blocks + 1, activate, 0)
    for copy in later:
        copy.wait()
    for copy in weight_copies:
        copy.wait()

    bias_first = bias[0:1, :]
    bias_mix = bias[1:2, :]
    bias_code = bias[8:9, 0:HALF]
    lane = lax.broadcasted_iota(jnp.int32, (1, HALF), 1) < HALF // 2
    hb = block // 2
    hs = hb * SIDE

    def add_rows(total, value):
        for i in range(0, value.shape[0], 8):
            part = value[i : i + 8]
            total = part if total is None else total + part
        return total

    half_tiles = range(0, hs, TILE)
    code_of = numbers(book_acc.shape[0], HALF)
    halves = (0, hs)

    def middle(j, carry):
        r0 = j * block
        for i in range(block // per_row):
            row = code_rows[pl.ds(j * (block // per_row) + i, 1), :]
            hot_s[:, i * HALF : (i + 1) * HALF] = one_hot_columns(row, code_of)
        for h in halves:
            found_s[h : h + hs] = dot(book[...], hot_s[:, h : h + hs]).astype(BF16).T
        pre = []
        for h in halves:
            window = jnp.concatenate([act3[at(r0 + i + h // SIDE, hb), :] for i in range(3)], axis=1)
            pre.append(dot(window, kernel[...]))
        for h, part in zip(halves, pre):
            for t in half_tiles:
                value, slope = gelu_parts(part[t : t + TILE] + bias_first)
                second_s[h + t : h + t + TILE] = value.astype(BF16)
                slope_s[h + t : h + t + TILE] = slope
        mixed = [dot(second_s[h : h + hs], mix[...]) for h in halves]
        for h, part in zip(halves, mixed):
            for t in half_tiles:
                low_s[h + t : h + t + TILE] = (read_x(r0, h + t) + part[t : t + TILE] + bias_mix).astype(BF16)
        latents = [dot(low_s[h : h + hs], project[i]) for i, h in enumerate(halves)]
        total = None
        for t in half_tiles:
            first = pl.ds(r0 + t // SIDE, TILE // SIDE)
            other = pl.ds(r0 + hb + t // SIDE, TILE // SIDE)
            ch = jnp.where(lane, found_s[t : t + TILE].astype(F32), found_s[hs + t : hs + t + TILE].astype(F32))
            q = jnp.where(lane3, qc[first], qc[other]).reshape(TILE, HALF)
            live = q < 0.5 * MARK
            latent = latents[0][t : t + TILE] + latents[1][t : t + TILE] + bias_code
            diff = jnp.where(live, latent - ch, 0.0)
            code_grad = jnp.where(live, q + (2.0 * COMMIT) * diff, 0.0)
            code_s[t : t + TILE] = code_grad.astype(BF16)
            total = add_rows(total, code_grad)
            big = diff.astype(BF16).astype(F32)
            small = diff - big
            turned = pltpu.roll(small, HALF // 2, 1)
            diff_s[t : t + TILE] = jnp.where(lane, big, turned).astype(BF16)
            turned = pltpu.roll(big, HALF // 2, 1)
            diff_s[hs + t : hs + t + TILE] = jnp.where(lane, turned, small).astype(BF16)
        bias_acc[16:24, 0:HALF] += total
        total = None
        blocks_g = [dot(code_s[...], project[i], NT) for i in range(2)]
        for h, part in zip(halves, blocks_g):
            for t in half_tiles:
                block_g[tile_at(r0, h + t), :] = part[t : t + TILE]
                mixed_s[h + t : h + t + TILE] = part[t : t + TILE].astype(BF16)
                total = add_rows(total, part[t : t + TILE])
        bias_acc[8:16] += total
        second_grad = [dot(mixed_s[h : h + hs], mix[...], NT) for h in halves]
        total = None
        for h, part in zip(halves, second_grad):
            for t in half_tiles:
                first_grad = slope_s[h + t : h + t + TILE] * part[t : t + TILE]
                back, ahead = shifted(first_grad)
                grad3[tile_at(r0 + 1, h + t), 0 : 2 * HALF] = ahead
                grad3[tile_at(r0 + 1, h + t), 2 * HALF : 4 * HALF] = first_grad.astype(BF16)
                grad3[tile_at(r0 + 1, h + t), 4 * HALF : 6 * HALF] = back
                total = add_rows(total, first_grad)
        bias_acc[0:8] += total
        book_acc[...] += dot(hot_s[...], diff_s[...])
        mix_acc[...] += dot(second_s[...], mixed_s[...], TN)
        project_acc[...] += jnp.where(lane, dot(low_s[0:hs], code_s[...], TN), dot(low_s[hs:], code_s[...], TN))
        return carry

    def finish(j, carry):
        r0 = j * block
        active = act3[at(r0 + 1), 2 * HALF : 4 * HALF].T
        for i in range(3):
            kernel_acc[:, i * 6 * HALF : (i + 1) * 6 * HALF] += dot(active, grad3[at(r0 + 2 - i), :])
        grads = []
        for h in halves:
            window = jnp.concatenate([grad3[at(r0 + 2 - i + h // SIDE, hb), :] for i in range(3)], axis=1)
            grads.append(dot(window, kernel_t[...]))
        for h, grad in zip(halves, grads):
            for t in half_tiles:
                here = tile_at(r0, h + t)
                out = (block_g[here, :] + slope_x[here, :] * grad[t : t + TILE]).astype(BF16)
                part = pl.ds(r0 + (h + t) // SIDE, TILE // SIDE)
                xc_o[part] = out[:, :HALF].reshape(TILE // SIDE, SIDE, HALF)
                xc_f[part] = out[:, HALF:].reshape(TILE // SIDE, SIDE, HALF)
        return carry

    def opening(j, carry):
        middle(j, carry)
        return activate(j + 2, carry)

    def steady(j, carry):
        finish(j - 2, carry)
        middle(j, carry)
        return activate(j + 2, carry)

    if fused:
        lax.fori_loop(0, jnp.minimum(blocks, 2), opening, 0)
        lax.fori_loop(2, blocks, steady, 0)
        lax.fori_loop(jnp.maximum(blocks - 2, 0), blocks, finish, 0)
    else:
        lax.fori_loop(0, blocks, middle, 0)
        lax.fori_loop(0, blocks, finish, 0)
    leaving = []
    if not final:
        leaving += list(zip((kernel_acc, mix_acc, project_acc, book_acc, bias_acc), sums_out))
        for i, (source, target) in enumerate(leaving):
            leaving[i] = pltpu.make_async_copy(source, target, sems.at[i])
            leaving[i].start()

    out_o, out_f = xo, xf
    if first_step:
        out_o[0:LEAD] = blank
        out_f[0:LEAD] = blank
    else:
        out_o[0:LEAD] = carry_own[...]
        out_f[0:LEAD] = carry_far[...]

    def collect(b, src):
        dst = meta[b] - start + LEAD
        out_o[pl.ds(dst, SIDE)] = xc_o[pl.ds(src, SIDE)]
        out_f[pl.ds(dst, SIDE)] = xc_f[pl.ds(src, SIDE)]
        return src + heights[b] + 1

    lax.fori_loop(low, high, collect, jnp.int32(1))
    size = win_own.shape[0]
    windows = (
        (out_o.at[pl.ds(0, size)], win_own),
        (out_f.at[pl.ds(0, size)], win_far),
        (out_o.at[pl.ds(chunk, LEAD)], next_own),
        (out_f.at[pl.ds(chunk, LEAD)], next_far),
    )
    for i, (source, target) in enumerate(windows):
        leaving.append(pltpu.make_async_copy(source, target, sems.at[5 + i]))
        leaving[-1].start()
    if final:
        sums = (kernel_acc, mix_acc, project_acc, book_acc, bias_acc, decode_acc)
        laid_out += [slope_x.at[pl.ds(0, layout.rows), pl.ds(i * HALF, HALF)] for i in range(2)]
        leaving += gather_grads(plan, layout, place, meta, sums, *laid_out, sems)
    for copy in leaving:
        copy.wait()


class Layout:
    def __init__(self, devices, book_rows, embed):
        self.mix = 9 * 2 * HALF
        self.project = self.mix + 2 * HALF
        self.book = self.project + HALF // 2
        self.bias = self.book + book_rows // 2
        self.decode = self.bias + 8
        used = self.decode + embed + 8
        self.devices = devices
        self.piece = -(-used // (devices * SIDE)) * SIDE
        self.rows = self.piece * devices
        self.half = self.rows // 2
        self.used = used


def lay_out(layout, swap, kernel_acc, mix_acc, project_acc, book_acc, bias_acc, decode_acc, own, far):
    def lanes(value):
        return value[:, :HALF], value[:, HALF:]

    def order(first, second):
        return jnp.where(swap, second, first), jnp.where(swap, first, second)

    row = 0
    for tap in range(9):
        block = kernel_acc[:, tap * 2 * HALF : (tap + 1) * 2 * HALF]
        mine, theirs = lanes(block)
        a, b = order(mine[:HALF], mine[HALF:])
        own[row : row + HALF] = a
        own[row + HALF : row + 2 * HALF] = b
        a, b = order(theirs[:HALF], theirs[HALF:])
        far[row : row + HALF] = a
        far[row + HALF : row + 2 * HALF] = b
        row += 2 * HALF
    row = layout.mix
    for target, part in ((own, mix_acc[:HALF]), (far, mix_acc[HALF:])):
        a, b = order(*lanes(part))
        target[row : row + HALF] = a
        target[row + HALF : row + 2 * HALF] = b
    row = layout.project
    side = HALF // 2
    for target, part in ((own, project_acc[:HALF]), (far, project_acc[HALF:])):
        part = part + pltpu.roll(part, side, 1)
        target[row : row + side] = part.T[:side]
    row = layout.book
    book = book_acc[...]
    book = -2.0 * (book + pltpu.roll(book, side, 1))
    book = book.T[:side]
    for c in range(book.shape[1] // HALF):
        part = book[:, c * HALF : (c + 1) * HALF]
        own[row + c * side : row + (c + 1) * side] = part
        far[row + c * side : row + (c + 1) * side] = part
    row = layout.bias
    sums = [jnp.sum(bias_acc[8 * i : 8 * i + 8], axis=0, keepdims=True) for i in range(3)]
    code = sums[2][:, :HALF]
    code = code + pltpu.roll(code, side, 1)
    which = lax.broadcasted_iota(jnp.int32, (8, HALF), 0)
    for target, first in ((own, 0), (far, HALF)):
        part = jnp.where(which == 0, sums[0][:, first : first + HALF], sums[1][:, first : first + HALF])
        target[row : row + 8] = jnp.where(which == 2, code, jnp.where(which < 2, part, 0.0))
    row = layout.decode
    rest = layout.rows - row
    own[row:] = jnp.zeros((rest, HALF), F32)
    far[row:] = jnp.zeros((rest, HALF), F32)
    if decode_acc is not None:
        own[row : row + decode_acc.shape[0]] = decode_acc[...]


def gather_plain(layout, place, *refs):
    lay_out(layout, place[0] == 1, *refs[:5], None, *refs[5:])


def gather_grads(plan, layout, place, meta, accs, keep_own, keep_far, send, own, far, sems):
    lay_out(layout, place[0] == 1, *accs, own, far)
    base = plan.images + len(plan.chunks) + 1
    over = (meta[base + 4] > plan.covered).astype(F32)
    which = lax.broadcasted_iota(jnp.int32, (8, HALF), 0)
    row = layout.bias
    own[row : row + 8] = jnp.where(which == 3, over, own[row : row + 8])
    half = layout.half
    mine = pl.ds(pl.multiple_of(place[1] * half, SIDE), half)
    other = pl.ds(pl.multiple_of((1 - place[1]) * half, SIDE), half)
    kept = []
    for i, (source, target) in enumerate(((own, keep_own), (far, keep_far))):
        kept.append(pltpu.make_async_copy(source.at[mine, :], target, sems.at[9 + i]))
        kept[-1].start()
    send[0] = own[other, :].astype(BF16)
    send[1] = far[other, :].astype(BF16)
    return kept


def hold(*refs):
    pass


def add_far(keep_far, came, out):
    out[...] = (keep_far[...] + came[1].astype(F32)).astype(BF16)


def add_own(keep_own, came, came_far, out, token):
    token[...] = jnp.zeros_like(token)
    total = keep_own[...] + came[0].astype(F32) + came_far[...].astype(F32)
    out[...] = total.astype(BF16).reshape(out.shape)


def add_pieces(pieces, _, out, token):
    token[...] = jnp.zeros_like(token)
    total = pieces[0].astype(F32)
    for i in range(1, pieces.shape[0]):
        total = total + pieces[i].astype(F32)
    out[...] = jnp.broadcast_to(total.astype(BF16)[None], out.shape)


def write_grads(layout, place, mine, theirs, kernel, first_bias, mix, mix_bias, project, project_bias, book, decode, decode_bias, whole):
    half = layout.half
    whole[pl.ds(pl.multiple_of(place[1] * half, SIDE), half), :] = mine[...].astype(F32)
    whole[pl.ds(pl.multiple_of((1 - place[1]) * half, SIDE), half), :] = theirs[...].astype(F32)
    split_grads(layout, whole, kernel, first_bias, mix, mix_bias, project, project_bias, book, decode, decode_bias)


def split_grads(layout, whole, kernel, first_bias, mix, mix_bias, project, project_bias, book, decode, decode_bias):
    for tap in range(9):
        kernel[tap] = whole[tap * 2 * HALF : (tap + 1) * 2 * HALF]
    row = layout.mix
    mix[:, :HALF] = whole[row : row + HALF]
    mix[:, HALF:] = whole[row + HALF : row + 2 * HALF]
    side = HALF // 2
    for row, target in ((layout.project, project), (layout.book, book)):
        for c in range(target.shape[1] // HALF):
            target[:, c * HALF : (c + 1) * HALF] = whole[row + c * side : row + (c + 1) * side]
    row = layout.bias
    first_bias[...] = whole[row : row + 1]
    mix_bias[...] = whole[row + 1 : row + 2]
    project_bias[...] = whole[row + 2 : row + 3, :side]
    row = layout.decode
    n = decode.shape[0]
    decode[...] = whole[row : row + n]
    decode_bias[...] = whole[row + n : row + n + 1]


def split_again(layout, total, extra, *refs):
    whole = refs[-1]
    whole[...] = total[...].astype(F32) + extra[...]
    split_grads(layout, whole, *refs[:-1])


def restore_rows(plan, n, waits, *refs):
    meta, heights, *refs = refs[waits:]
    own, far, out, token = refs[:n], refs[n : 2 * n], refs[2 * n], refs[2 * n + 1]
    token[...] = jnp.zeros_like(token)
    stage_own, stage_far, sems = refs[2 * n + 2 :]
    copies = []
    for k in range(n):
        size = plan.chunks[k] + (LEAD if k == n - 1 else 0)
        for i, (source, target) in enumerate(((own[k], stage_own), (far[k], stage_far))):
            from_rows = source.at[pl.ds(0, size)]
            copies.append(pltpu.make_async_copy(from_rows, target.at[pl.ds(plan.starts[k], size)], sems.at[i, k]))
            copies[-1].start()
    for copy in copies:
        copy.wait()
    base = plan.images + len(plan.chunks) + 1
    own_row, send_row = meta[base], meta[base + 1]
    first, last = meta[base + 2], meta[base + 3]
    row_of = lax.broadcasted_iota(jnp.int32, (SIDE, 1, 1), 0)

    def own_image(b, carry):
        rows = stage_own[pl.ds(meta[b] + LEAD, SIDE)]
        out[b] = jnp.where(row_of < heights[b], rows, jnp.zeros_like(rows))
        return carry

    def far_image(b, carry):
        rows = stage_far[pl.ds(meta[b] + own_row - send_row + LEAD, SIDE)]
        out[b] = jnp.where(row_of < heights[b], rows, jnp.zeros_like(rows))
        return carry

    lax.fori_loop(first, last, own_image, 0)
    lax.fori_loop(0, first, far_image, 0)
    lax.fori_loop(last, plan.images, far_image, 0)


def trade(value):
    return lax.ppermute(value, "mp", [(0, 1), (1, 0)])


def held(value, *others):
    return pl.pallas_call(
        hold,
        out_shape=shape(value.shape, value.dtype),
        in_specs=[ANY] * (1 + len(others)),
        out_specs=ANY,
        input_output_aliases={0: 0},
        compiler_params=params(60),
        name="hold",
    )(value, *others)


def run_main(plan, layout, k, meta, heights, streams, weights, state, waits=(), ending=()):
    chunk, rows, block = plan.chunks[k], plan.rows[k], plan.block[k]
    last = k >= plan.usual - 1
    final = k == plan.usual - 1
    x_own, x_far, q_own, q_far, codes = streams
    book_rows = weights[-1].shape[1]
    args = [*waits, *ending, meta, heights, x_own, x_far[k], q_own, q_far[k], codes, *weights]
    specs = [ANY] * len(waits) + ([SMEM, VMEM] if final else [])
    specs += [SMEM, SMEM, ANY, ANY, ANY, ANY, VMEM, ANY, ANY] + [VMEM] * (len(weights) - 2)
    alias = {}
    if state is not None:
        args += [x_far[k - 1], q_far[k - 1], *state]
        specs += [ANY, ANY, VMEM, VMEM] + [ANY] * (len(state) - 2)
        if not final:
            for i in range(len(state) - 2):
                alias[len(args) - 5 + i] = 4 + i
    size = chunk + LEAD if last else chunk
    tile = (SIDE, HALF)
    outs = [shape((size,) + tile, BF16)] * 2 + [shape((LEAD,) + tile, BF16)] * 2
    sums = [(2 * HALF, 18 * HALF), (2 * HALF, 2 * HALF), (2 * HALF, HALF), (book_rows, HALF), (24, 2 * HALF)]
    scratch = [pltpu.VMEM(dims, F32) for dims in sums]
    out_specs = [ANY] * 4
    if final:
        outs += [shape((layout.half, HALF), F32)] * 2 + [shape((2, layout.half, HALF), BF16)]
        out_specs += [ANY, ANY, VMEM]
    else:
        outs += [shape(dims, F32) for dims in sums]
        out_specs += [ANY] * 5
    scratch += [pltpu.VMEM((18 * HALF, 2 * HALF), BF16)] * 2 + [pltpu.SemaphoreType.DMA((2,))]
    half = chunk // 2
    spots = block * SIDE
    scratch += [
        pltpu.VMEM((LEAD + chunk + 2 * SIDE,) + tile, BF16),
        pltpu.VMEM((LEAD + chunk + 2 * SIDE,) + tile, BF16),
        pltpu.VMEM((LEAD + half,) + tile, F32),
        pltpu.VMEM((LEAD + half,) + tile, BF16),
        pltpu.VMEM((LEAD + chunk + SIDE,) + tile, F32),
        pltpu.VMEM((rows + 2 * block + SIDE,) + tile, BF16),
        pltpu.VMEM((rows + 2 * block + SIDE,) + tile, BF16),
        pltpu.VMEM((rows + 2 * SIDE,) + tile, F32),
        pltpu.VMEM((-(-(rows * SIDE // HALF + 4) // 8) * 8, HALF), jnp.int32),
        pltpu.VMEM(((rows + 2 * block + 2) * SIDE, 6 * HALF), BF16),
        pltpu.VMEM(((rows + 2 * block) * SIDE, 2 * HALF), F32),
        pltpu.VMEM(((rows + 2) * SIDE, 6 * HALF), BF16),
        pltpu.VMEM((rows * SIDE, 2 * HALF), F32),
        pltpu.VMEM((spots, 2 * HALF), BF16),
        pltpu.VMEM((spots, 2 * HALF), F32),
        pltpu.VMEM((spots, 2 * HALF), BF16),
        pltpu.VMEM((spots, 2 * HALF), BF16),
        pltpu.VMEM((spots // 2, HALF), BF16),
        pltpu.VMEM((book_rows, spots), BF16),
        pltpu.VMEM((spots, HALF), BF16),
        pltpu.VMEM((spots, HALF), BF16),
        pltpu.SemaphoreType.DMA((13,)),
    ]
    spots = chunk * SIDE
    return pl.pallas_call(
        functools.partial(main_step, plan, layout, k, len(waits)),
        out_shape=outs,
        in_specs=specs,
        out_specs=out_specs,
        scratch_shapes=scratch,
        input_output_aliases=alias,
        compiler_params=params(58),
        cost_estimate=cost(60 * 65536 * spots, 8 * MIB, 2 * 256 * spots),
        name=f"main_{k}",
    )(*args)


def local(
    image_latents,
    image_heights,
    code_index,
    kernel_three,
    bias_three,
    weight_mix,
    bias_mix,
    weight_project,
    bias_project,
    codebook,
    weight_decode,
    bias_decode,
    out_grad,
):
    images = image_latents.shape[0]
    plan = Plan(images)
    n = len(plan.chunks)
    tile = (SIDE, HALF)
    where = lax.axis_index("mp").astype(jnp.int32)
    core = lax.rem(lax.axis_index("dp").astype(jnp.int32), 2)
    spot = place = jnp.stack([where, core])

    devices = lax.axis_size("dp")
    across = [(i, i ^ 1) for i in range(devices)]
    kernel_half = lax.dynamic_slice_in_dim(kernel_three, core * HALF, HALF, 1)
    far_kernel = trade(kernel_half)
    far_kernel_other = lax.ppermute(far_kernel, "dp", across)

    packed = pl.pallas_call(
        functools.partial(pack_latents, plan),
        out_shape=[
            shape((meta_size(plan),), jnp.int32),
            shape((LEAD + plan.total,) + tile, BF16),
        ]
        + [shape((c,) + tile, BF16) for c in plan.chunks],
        in_specs=[SMEM, SMEM, HBM, ANY],
        out_specs=[SMEM, ANY] + [ANY] * n,
        scratch_shapes=[
            pltpu.VMEM((images, SIDE) + tile, BF16),
            pltpu.VMEM((plan.packed + SIDE,) + tile, BF16),
            pltpu.SemaphoreType.DMA((8,)),
            pltpu.SemaphoreType.DMA((n + 1,)),
        ],
        compiler_params=params(60),
        cost_estimate=cost(0, 12 * MIB),
        name="pack_latents",
    )(image_heights, place, image_latents, kernel_half)
    meta, x_own, x_send = packed[0], packed[1], packed[2:]

    packed = pl.pallas_call(
        functools.partial(pack_code_grads, plan),
        out_shape=[shape((plan.total // 2,) + tile, F32), shape((2 * HALF + HALF // 2 + SIDE, HALF), BF16)]
        + [shape((c // 2,) + tile, BF16) for c in plan.chunks],
        in_specs=[SMEM] + [HBM] * 6 + [ANY],
        out_specs=[VMEM] * (n + 2),
        scratch_shapes=[
            pltpu.VMEM((images, SIDE) + tile, BF16),
            pltpu.VMEM((plan.packed + SIDE,) + tile, BF16),
            pltpu.SemaphoreType.DMA((8,)),
            pltpu.SemaphoreType.DMA((5,)),
            pltpu.VMEM(weight_decode.shape, BF16),
            pltpu.VMEM(weight_mix.shape, BF16),
            pltpu.VMEM(weight_project.shape[::-1], BF16),
            pltpu.VMEM((1, HALF), BF16),
            pltpu.VMEM((1, HALF), BF16),
        ],
        compiler_params=params(60),
        cost_estimate=cost(2 * 2 * plan.total * SIDE * 256 * 128, 10 * MIB),
        name="pack_code_grads",
    )(meta, out_grad, weight_decode, weight_mix, weight_project.T, bias_three.reshape(1, HALF), bias_mix.reshape(1, HALF), far_kernel)
    q_own, small, q_send = packed[0], packed[1], packed[2:]

    book_rows, embed = codebook.shape
    codebook_t = codebook.T
    far_small = trade(small)
    usual = plan.usual
    x_far, q_far = [], []
    x_far.append(trade(x_send[0]))
    q_far.append(trade(q_send[0]))

    weights = pl.pallas_call(
        prepare_weights,
        out_shape=[
            shape((18 * HALF, 2 * HALF), BF16),
            shape((18 * HALF, 2 * HALF), BF16),
            shape((2 * HALF, 2 * HALF), BF16),
            shape((2, 2 * HALF, HALF), BF16),
            shape((SIDE, 2 * HALF), F32),
            shape((HALF, book_rows), BF16),
        ],
        in_specs=[SMEM, HBM, HBM, HBM] + [VMEM] * 4,
        out_specs=[VMEM] * 6,
        scratch_shapes=[pltpu.VMEM(kernel_three.shape, BF16)] * 2 + [pltpu.SemaphoreType.DMA((3,))],
        compiler_params=params(20),
        cost_estimate=cost(0, 5 * MIB),
        name="prepare_weights",
    )(place, kernel_three, far_kernel, far_kernel_other, small, far_small, bias_project.reshape(1, -1), codebook_t)

    groups = 8
    group = images // groups
    codes = code_index.reshape(images, SIDE * SIDE)
    whole = lambda dims: pl.BlockSpec(dims, lambda g: (0,) * len(dims))
    four = pl.BlockSpec((group, SIDE) + tile, lambda g: (g, 0, 0, 0))
    row = pl.BlockSpec((group, SIDE * SIDE), lambda g: (g, 0))
    def code_sums(first, steps):
        return pl.pallas_call(
            functools.partial(sum_codes, first, group),
            grid=(steps,),
            out_shape=shape((embed + 8, HALF), F32),
            in_specs=[
                SMEM,
                pl.BlockSpec((group, SIDE * SIDE), lambda g: (g + first, 0)),
                pl.BlockSpec((group, SIDE) + tile, lambda g: (g + first, 0, 0, 0)),
                whole((embed, book_rows)),
                ANY,
                ANY,
            ],
            out_specs=whole((embed + 8, HALF)),
            scratch_shapes=[
                pltpu.VMEM((book_rows, group * SIDE * SIDE), BF16),
                pltpu.VMEM((group * SIDE * SIDE, HALF), BF16),
                pltpu.VMEM((book_rows, HALF), F32),
            ],
            compiler_params=params(60),
            cost_estimate=cost(steps * group * 256 * 512 * 256, steps * group * 65536),
            name=f"sum_codes_{first}",
        )(image_heights, codes, out_grad, codebook_t, small, far_kernel)

    def decode(after):
        return pl.pallas_call(
            functools.partial(decode_images, plan, groups),
            grid=(groups,),
            out_shape=[shape((images, SIDE) + tile, BF16), shape((8, HALF), F32)],
            in_specs=[SMEM, row, whole((embed, book_rows)), whole((embed, HALF)), whole((1, HALF)), ANY],
            out_specs=[four, whole((8, HALF))],
            scratch_shapes=[pltpu.VMEM((HALF, book_rows), BF16)],
            compiler_params=params(32),
            cost_estimate=cost(images * 256 * 512 * 256, 5 * MIB),
            name="decode_images",
        )(image_heights, codes, codebook_t, weight_decode, bias_decode.reshape(1, HALF), after)

    decode_acc = code_sums(0, groups)
    for k in range(1, usual):
        x_far.append(trade(held(x_send[k], decode_acc, far_small, x_far[0], q_far[0])))
        q_far.append(trade(held(q_send[k], decode_acc, far_small, x_far[0], q_far[0])))

    layout = Layout(devices, book_rows, embed)
    half, piece, chips = layout.half, layout.piece, devices // 2
    streams = (x_own, x_far, q_own, q_far, codes)
    state = None
    win_own, win_far = [], []
    for k in range(usual):
        waits = win_far[k - 2 : k - 1] if k > 1 else []
        ending = (spot, decode_acc) if k == usual - 1 else ()
        outs = run_main(plan, layout, k, meta, image_heights, streams, weights, state, waits, ending)
        win_own.append(outs[0])
        if k < usual - 1:
            win_far.append(trade(outs[1]))
        state = outs[2:]
    last_window = outs[1]
    carry, (keep_own, keep_far, send) = state[:2], state[2:]

    def restore(own, far, waits=()):
        count = len(own)
        return pl.pallas_call(
            functools.partial(restore_rows, plan, count, len(waits)),
            out_shape=[shape((images, SIDE) + tile, BF16), shape((8, HALF), F32)],
            in_specs=[ANY] * len(waits) + [SMEM, SMEM] + [ANY] * (2 * count),
            out_specs=[VMEM, VMEM],
            scratch_shapes=[
                pltpu.VMEM((plan.total + LEAD + SIDE,) + tile, BF16),
                pltpu.VMEM((plan.total + LEAD + SIDE,) + tile, BF16),
                pltpu.SemaphoreType.DMA((2, count)),
            ],
            compiler_params=params(60),
            cost_estimate=cost(0, 10 * MIB),
            name="restore_rows",
        )(*waits, meta, image_heights, *own, *far)


    def step(body, out, name, *args, waits=()):
        specs = [VMEM] * len(args) + [ANY] * len(waits)
        args = (*args, *waits)
        return pl.pallas_call(
            body,
            out_shape=out,
            in_specs=specs,
            out_specs=[VMEM] * len(out) if isinstance(out, list) else VMEM,
            compiler_params=params(24),
            cost_estimate=cost(0, 2 * MIB),
            name=name,
        )(*args)

    send = held(send, win_far[usual - 2])
    came = lax.ppermute(send, "dp", across)
    win_far.append(trade(last_window))
    far_sums = step(add_far, shape((half, HALF), BF16), "add_far", keep_far, came)
    came_far = trade(far_sums)
    parts = [shape((chips, piece, HALF), BF16), shape((8, HALF), F32)]
    mine, token = step(add_own, parts, "add_own", keep_own, came, came_far)
    decoded, token = decode(token)
    cores = [[i for i in range(devices) if i % 2 == c] for c in range(2)]
    mine = lax.all_to_all(mine, "dp", 0, 0, axis_index_groups=cores, tiled=True)
    mine, token = step(add_pieces, parts, "add_pieces", mine, waits=[token])
    latents_grad, token = restore(win_own, win_far, [token])
    mine = lax.all_to_all(mine, "dp", 0, 0, axis_index_groups=cores, tiled=True)
    mine = held(mine, token).reshape(half, HALF)
    theirs = lax.ppermute(mine, "dp", across)

    grads_out = [
        shape((9, 2 * HALF, HALF), F32),
        shape((1, HALF), F32),
        shape((HALF, 2 * HALF), F32),
        shape((1, HALF), F32),
        shape((embed, HALF), F32),
        shape((1, embed), F32),
        shape((embed, book_rows), F32),
        shape((embed, HALF), F32),
        shape((1, HALF), F32),
    ]
    whole = pltpu.VMEM((layout.rows, HALF), F32)

    def usual_end(latents_grad):
        grads = pl.pallas_call(
            functools.partial(write_grads, layout),
            out_shape=grads_out,
            in_specs=[SMEM, VMEM, VMEM],
            out_specs=[VMEM] * 9,
            scratch_shapes=[whole],
            compiler_params=params(24),
            cost_estimate=cost(0, 4 * MIB),
            name="write_grads",
        )(spot, mine, theirs)
        return (latents_grad, *grads)

    def longer_end(latents_grad):
        last_x, last_q = trade(x_send[usual]), trade(q_send[usual])
        streams = (x_own, x_far + [last_x], q_own, q_far + [last_q], codes)
        outs = run_main(plan, layout, usual, meta, image_heights, streams, weights, carry)
        latents_grad, _ = restore(win_own + [outs[0]], win_far + [trade(outs[1])])
        own, far = pl.pallas_call(
            functools.partial(gather_plain, layout),
            out_shape=[shape((layout.rows, HALF), F32)] * 2,
            in_specs=[SMEM] + [VMEM] * 5,
            out_specs=[VMEM] * 2,
            compiler_params=params(40),
            name="gather_plain",
        )(spot, *outs[4:])
        extra = lax.psum(own + trade(far), "dp")
        first, second = jnp.where(core == 0, mine, theirs), jnp.where(core == 0, theirs, mine)
        grads = pl.pallas_call(
            functools.partial(split_again, layout),
            out_shape=grads_out,
            in_specs=[VMEM, VMEM],
            out_specs=[VMEM] * 9,
            scratch_shapes=[whole],
            compiler_params=params(24),
            name="split_again",
        )(jnp.concatenate([first, second]), extra)
        return (latents_grad, *grads)

    flag = layout.bias + 3
    holder = flag // half
    flags = jnp.where(core == holder, mine[flag - holder * half, 0], theirs[flag - holder * half, 0])
    ends = lax.cond(flags.astype(F32) > 0.5, longer_end, usual_end, latents_grad)
    latents_grad, kernel_grad, first_bias, mix_grad, mix_bias, project_grad, project_bias, book, decode, decode_bias = ends
    return (
        decoded,
        latents_grad,
        kernel_grad,
        first_bias.reshape(HALF),
        mix_grad,
        mix_bias.reshape(HALF),
        project_grad.T,
        project_bias.reshape(embed),
        book.T,
        decode,
        decode_bias.reshape(HALF),
    )


def solution(mesh):
    tile = P("dp", None, None, "mp")
    placed = (
        tile,
        P("dp"),
        P("dp", None, None),
        P(None, None, "mp"),
        P("mp"),
        P("mp", None),
        P("mp"),
        P("mp", None),
        P(),
        P(),
        P(None, "mp"),
        P("mp"),
        tile,
    )
    outs = (
        tile,
        tile,
        P(None, None, "mp"),
        P("mp"),
        P("mp", None),
        P("mp"),
        P("mp", None),
        P(),
        P(),
        P(None, "mp"),
        P("mp"),
    )
    return jax.shard_map(local, mesh=mesh, in_specs=placed, out_specs=outs, check_vma=False)
```
